32 devices in a mesh: grp: 4 (over y, x), ray: 8 (over z, core).
Axes of the slice: x: 2, y: 2, z: 4, core: 2. Of those that a mesh axis runs over, the one named last changes fastest.
Arguments:
- image_tokens: bfloat16 [16384, 1024], P(('grp', 'ray')), may hold values from -6 to 6
- tile_lists: int32 [32, 16384], P(None, ('grp', 'ray')), may hold values from 0 to 8191, as said below
- opacity: float32 [32, 16384], P(None, ('grp', 'ray')), may hold values from 0.02 to 0.5
- tile_counts: int32 [16384], P(('grp', 'ray')), may hold values from 1 to 32, as said below
- ray_pixel: int32 [4, 4096], P('grp'), may hold values from 0 to 4095, as said below
- block_owner: int32 [4, 8], P('grp'), may hold values from 0 to 7, each once within a row
- gaussian_features: bfloat16 [32768, 1024], P(('grp', 'ray')), may hold values from -6 to 6
- layer_norm_gain: float32 [1024], replicated, may hold values from 0.5 to 1.5
- layer_scale: float32 [1024], replicated, may hold values from 0.25 to 1
- up_weight: bfloat16 [1024, 2048], P(None, 'ray'), may hold values from -0.1875 to 0.1875
- down_weight: bfloat16 [2048, 1024], P('ray'), may hold values from -0.125 to 0.125
Outputs:
- grad_up: float32 [1024, 2048], P(None, 'ray')
- grad_down: float32 [2048, 1024], P('ray')
- gain_gradient: float32 [1024], replicated
- grad_scale: float32 [1024], replicated
- loss: float32 [], replicated
The draws below stay inside these ranges and needn't reach their ends.
Inputs may be any that keep to these rules, and one draw needn't show every extreme that they name: `tile_lists`: A ray's entries name Gaussians of the block of 1024 rows of gaussian_features that is held by the same device as the ray. `tile_counts`: in each group some device holds a ray with 32 live entries. `ray_pixel`: each group's row is a permutation of its pixels, and the 512 rays of each device name exactly 64 pixels of each block of 512 consecutive pixels. `block_owner`: each group's row is a permutation.
All inputs are finite; a program needn't handle non-finite values.
Results may differ from the reference program's by a relative error of at most 0.0068.
Values may be sent and summed in bfloat16 or wider, within the bound.
No kernel may reach another device: no remote copies, remote signals or barrier semaphores. Data moves between devices by JAX's collectives and lax.ppermute only.
A program may use at most 128 MiB of HBM per device.

```python
import math
import jax
import jax.numpy as jnp
from jax import lax

D = 1024
FF = 2048
TOK_DEV = 512
GAUSS_DEV = 1024
KMAX = 32
TOKENS = 16384
GAUSSIANS = 32768
N_GRP = 4
N_RAY = 8


def draw_tile_lists(key, part):
    key = jax.random.fold_in(key, 1)
    columns = N_GRP * N_RAY * TOK_DEV
    holder = jnp.arange(columns, dtype=jnp.int32) // TOK_DEV % N_RAY
    offsets = jax.random.randint(key, (KMAX, columns), 0, GAUSS_DEV)
    offsets = offsets.at[0, 0].set(0).at[0, columns - 1].set(GAUSS_DEV - 1)
    return (holder[None, :] * GAUSS_DEV + offsets).astype(jnp.int32)


def draw_tile_counts(key, part):
    key = jax.random.fold_in(key, 2)
    devices = N_GRP * N_RAY
    cap_key, full_key, count_key = jax.random.split(key, 3)
    caps = jax.random.randint(cap_key, (N_GRP, N_RAY), KMAX // 4, KMAX + 1)
    fullest = jax.random.randint(full_key, (N_GRP, 1), 0, N_RAY)
    caps = jnp.where(jnp.arange(N_RAY)[None, :] == fullest, KMAX, caps).reshape(devices)
    per_ray = jnp.repeat(caps, TOK_DEV, total_repeat_length=devices * TOK_DEV)
    counts = jax.random.randint(count_key, (devices * TOK_DEV,), 1, per_ray + 1)
    first = jnp.arange(devices * TOK_DEV) % TOK_DEV == 0
    return jnp.where(first, per_ray, counts).astype(jnp.int32)


def draw_ray_pixel(key, part):
    key = jax.random.fold_in(key, 3)
    each_pair = TOK_DEV // N_RAY

    def one_group(group_key):
        block_key, shuffle_key = jax.random.split(group_key)
        perms = jax.vmap(lambda single: jax.random.permutation(single, TOK_DEV))(jax.random.split(block_key, N_RAY))
        blocks = perms.reshape(N_RAY, N_RAY, each_pair) + (jnp.arange(N_RAY, dtype=jnp.int32) * TOK_DEV)[:, None, None]
        rows = blocks.transpose(1, 0, 2).reshape(N_RAY, TOK_DEV)
        mixed = jax.vmap(lambda single, row: jax.random.permutation(single, row))(jax.random.split(shuffle_key, N_RAY), rows)
        return mixed.reshape(N_RAY * TOK_DEV)
    return jax.vmap(one_group)(jax.random.split(key, N_GRP)).astype(jnp.int32)


def shard_levels(key, shape, shards, least, high):
    level, own = 1.0, jax.random.fold_in(key, 6)
    for dim, blocks in shards:
        draws = jnp.exp(jax.random.uniform(jax.random.fold_in(own, dim), (blocks,), jnp.float32, least / len(shards), high / len(shards)))
        level = level * jnp.repeat(draws, shape[dim] // blocks).reshape([-1 if axis == dim else 1 for axis in range(len(shape))])
    return level


def noise(own_key, shape, spread, reach, cuts=(), kind=jnp.bfloat16):
    drawn = spread * jax.random.normal(own_key, shape, jnp.float32)
    if cuts:
        drawn = drawn * shard_levels(own_key, shape, cuts, -0.22, 0.18)
    return jnp.clip(drawn, -reach, reach).astype(kind)


def setup_inputs(seed: int = 0) -> dict:
    key_of = jax.random.split(jax.random.key(seed), 12)
    return {
        "image_tokens": noise(key_of[0], (TOKENS, D), 1.0, 6.0, ((0, 32),)),
        "tile_lists": draw_tile_lists(jax.random.fold_in(key_of[11], 71), 0),
        "opacity": jnp.clip(0.02 + 0.48 * jax.random.uniform(key_of[2], (KMAX, TOKENS), jnp.float32) ** shard_levels(key_of[2], (KMAX, TOKENS), ((1, 32),), -0.2, 0.2), 0.02, 0.5),
        "tile_counts": draw_tile_counts(jax.random.fold_in(key_of[11], 71), 0),
        "ray_pixel": draw_ray_pixel(jax.random.fold_in(key_of[11], 71), 0),
        "block_owner": jax.vmap(lambda own: jax.random.permutation(own, N_RAY))(jax.random.split(key_of[5], N_GRP)).reshape((N_GRP, N_RAY)).astype(jnp.int32),
        "gaussian_features": noise(key_of[6], (GAUSSIANS, D), 1.0, 6.0, ((0, 32),)),
        "layer_norm_gain": jnp.clip(1.0 + 0.1 * jax.random.normal(key_of[7], (D,), jnp.float32), 0.5, 1.5),
        "layer_scale": jnp.clip(jnp.exp(jax.random.uniform(key_of[8], (D,), jnp.float32, math.log(0.25), math.log(1.0))), 0.25, 1.0),
        "up_weight": noise(key_of[9], (D, FF), D ** -0.5, 0.1875, ((1, 8),)),
        "down_weight": noise(key_of[10], (FF, D), FF ** -0.5, 0.125, ((0, 8),)),
    }


STABILITY_EPSILON = 1e-06

def weights_for(ids_local, alphas, counts, width, depth):
    columns = jnp.arange(width, dtype=jnp.int32)

    def advance(level, carry):
        table, passing = carry
        alpha_now = lax.dynamic_index_in_dim(alphas, level, 0, keepdims=False)
        ident = lax.dynamic_index_in_dim(ids_local, level, 0, keepdims=False)
        live = jnp.where(level < counts, jnp.float32(1.0), jnp.float32(0.0))
        share = alpha_now * passing * live
        table = table + jnp.where(ident[:, None] == columns[None, :], share[:, None], jnp.float32(0.0))
        return (table, passing * (1.0 - alpha_now))
    rays_here = ids_local.shape[1]
    start = (jnp.zeros((rays_here, width), jnp.float32), jnp.ones((rays_here,), jnp.float32))
    table, passing = lax.fori_loop(0, depth, advance, start)
    return table

def render_group(lists, alphas, counts, pixels, owner, features):

    def one_device(position):
        lists_here = lax.dynamic_slice_in_dim(lists, position * TOK_DEV, TOK_DEV, 1) - position * GAUSS_DEV
        alphas_here = lax.dynamic_slice_in_dim(alphas, position * TOK_DEV, TOK_DEV, 1)
        counts_here = lax.dynamic_slice_in_dim(counts, position * TOK_DEV, TOK_DEV, 0)
        table = weights_for(lists_here, alphas_here, counts_here, GAUSS_DEV, KMAX).astype(jnp.bfloat16)
        features_here = lax.dynamic_slice_in_dim(features, position * GAUSS_DEV, GAUSS_DEV, 0)
        return jnp.dot(table, features_here, preferred_element_type=jnp.float32).astype(jnp.bfloat16)
    rendered = lax.map(one_device, jnp.arange(N_RAY, dtype=jnp.int32)).reshape(N_RAY * TOK_DEV, D)
    destination = owner[pixels // TOK_DEV] * TOK_DEV + pixels % TOK_DEV
    return jnp.zeros_like(rendered).at[destination].set(rendered)

def layer_grads(tokens, target, layer_norm_gain, layer_scale, up_weight, down_weight):
    values = tokens.astype(jnp.float32)
    centered_input = values - lax.optimization_barrier(jnp.mean(values, axis=-1, keepdims=True))
    row_variance = lax.optimization_barrier(jnp.mean(centered_input * centered_input, axis=-1, keepdims=True))
    standardized_input = centered_input * lax.rsqrt(row_variance + STABILITY_EPSILON)
    normalized_rows = (standardized_input * layer_norm_gain).astype(jnp.bfloat16)
    hidden = jnp.dot(normalized_rows, up_weight, preferred_element_type=jnp.float32)
    act = jax.nn.gelu(hidden, approximate=False).astype(jnp.bfloat16)
    mixed = jnp.dot(act, down_weight, preferred_element_type=jnp.float32)
    layer_out = values + layer_scale * mixed
    goal = target.astype(jnp.float32)
    out_norm = jnp.sqrt(lax.optimization_barrier(jnp.sum(layer_out * layer_out, axis=-1, keepdims=True)) + STABILITY_EPSILON)
    goal_norm = jnp.sqrt(lax.optimization_barrier(jnp.sum(goal * goal, axis=-1, keepdims=True)) + STABILITY_EPSILON)
    cosine = lax.optimization_barrier(jnp.sum(layer_out * goal, axis=-1, keepdims=True)) / (out_norm * goal_norm)
    loss_sum = jnp.sum(1.0 - cosine)
    upstream = -(goal / (out_norm * goal_norm) - cosine * layer_out / (out_norm * out_norm))
    grad_scale = lax.optimization_barrier(jnp.sum(upstream * mixed, axis=0))
    back_mixed = (upstream * layer_scale).astype(jnp.bfloat16)
    grad_down = jnp.dot(act.T, back_mixed, preferred_element_type=jnp.float32)
    back_act = jnp.dot(back_mixed, down_weight.T, preferred_element_type=jnp.float32)
    slope = 0.5 * (1.0 + lax.erf(hidden / jnp.sqrt(2.0))) + hidden * jnp.exp(-0.5 * hidden * hidden) / jnp.sqrt(2.0 * jnp.pi)
    back_hidden = (back_act * slope).astype(jnp.bfloat16)
    grad_up = jnp.dot(normalized_rows.T, back_hidden, preferred_element_type=jnp.float32)
    normalized_gradient = jnp.dot(back_hidden, up_weight.T, preferred_element_type=jnp.float32)
    gain_gradient = lax.optimization_barrier(jnp.sum(normalized_gradient * standardized_input, axis=0))
    return (grad_up, grad_down, gain_gradient, grad_scale, loss_sum)

def reference(image_tokens, tile_lists, opacity, tile_counts, ray_pixel, block_owner, gaussian_features, layer_norm_gain, layer_scale, up_weight, down_weight):
    group_rows = N_RAY * TOK_DEV
    tokens_grouped = image_tokens.reshape(N_GRP, group_rows, D)
    lists_grouped = tile_lists.reshape(KMAX, N_GRP, group_rows).transpose(1, 0, 2)
    opacity_grouped = opacity.reshape(KMAX, N_GRP, group_rows).transpose(1, 0, 2)
    counts_grouped = tile_counts.reshape(N_GRP, group_rows)
    features_grouped = gaussian_features.reshape(N_GRP, N_RAY * GAUSS_DEV, D)

    def per_group(carry, pieces):
        tokens, lists, alphas, counts, pixels, owner, features = pieces
        target = render_group(lists, alphas, counts, pixels, owner, features)
        results = layer_grads(tokens, target, layer_norm_gain, layer_scale, up_weight, down_weight)
        return (jax.tree.map(jnp.add, carry, results), None)
    start = (jnp.zeros((D, FF), jnp.float32), jnp.zeros((FF, D), jnp.float32), jnp.zeros((D,), jnp.float32), jnp.zeros((D,), jnp.float32), jnp.zeros((), jnp.float32))
    totals, unused = lax.scan(per_group, start, (tokens_grouped, lists_grouped, opacity_grouped, counts_grouped, ray_pixel, block_owner, features_grouped))
    return (totals[0], totals[1], totals[2], totals[3], totals[4] / (N_GRP * group_rows))
```

```python
import functools

import jax
import jax.numpy as jnp
from jax import lax
from jax.experimental import pallas as pl
from jax.experimental.pallas import tpu as pltpu
from jax.sharding import PartitionSpec as P

STABILITY_EPSILON = 1e-06
F32 = jnp.float32
BF16 = jnp.bfloat16
VMEM_BYTES = 56 * 1024 * 1024
SMEM = pl.BlockSpec(memory_space=pltpu.SMEM)
VMEM = pl.BlockSpec(memory_space=pltpu.VMEM)


def params(**more):
    return pltpu.CompilerParams(vmem_limit_bytes=VMEM_BYTES, **more)


def dot_nn(a, b):
    return lax.dot_general(a, b, (((1,), (0,)), ((), ())), preferred_element_type=F32)


def dot_tn(a, b):
    return lax.dot_general(a, b, (((0,), (0,)), ((), ())), preferred_element_type=F32)


def dot_nt(a, b):
    return lax.dot_general(a, b, (((1,), (1,)), ((), ())), preferred_element_type=F32)


def owner_of(pixels, owner_ref, rows, count):
    block = lax.div(pixels, jnp.int32(rows))
    owner = jnp.zeros_like(pixels)
    for slot in range(count):
        owner = jnp.where(block == slot, owner_ref[0, slot], owner)
    return owner


def earlier(rows):
    before = lax.broadcasted_iota(jnp.int32, (rows, rows), 0)
    after = lax.broadcasted_iota(jnp.int32, (rows, rows), 1)
    return jnp.where(before < after, 1.0, 0.0).astype(BF16)


def render_kernel(
    ray_count, me_ref, owner_ref, lists_ref, opacity_ref, counts_ref, pixels_ref, features_ref,
    out_ref, ids_ref, share_ref, table_ref, send_ref,
):
    depth, rays = lists_ref.shape
    gauss = features_ref.shape[0]
    width = features_ref.shape[1]
    me = me_ref[0]
    ids_ref[...] = lists_ref[...] - me * gauss
    passing = jnp.ones((1, rays), F32)
    counts = counts_ref[...]
    for level in range(depth):
        alpha = opacity_ref[pl.ds(level, 1), :]
        share_ref[pl.ds(level, 1), :] = jnp.where(level < counts, alpha * passing, 0.0)
        passing = passing * (1.0 - alpha)

    tile = 128
    lanes = 128
    columns = rays // lanes

    @pl.loop(0, (gauss // tile) * columns)
    def _(step):
        first = pl.multiple_of(lax.div(step, columns) * tile, tile)
        lane = pl.multiple_of(lax.rem(step, columns) * lanes, lanes)
        number = lax.broadcasted_iota(jnp.int32, (tile, lanes), 0) + first
        total = jnp.zeros((tile, lanes), F32)
        for level in range(depth):
            ident = ids_ref[pl.ds(level, 1), pl.ds(lane, lanes)]
            share = share_ref[pl.ds(level, 1), pl.ds(lane, lanes)]
            total = total + jnp.where(ident == number, share, 0.0)
        table_ref[pl.ds(first, tile), pl.ds(lane, lanes)] = total.astype(BF16)

    mine = pixels_ref[pl.ds(me, 1), :]
    owner = owner_of(mine, owner_ref, rays, ray_count)
    padded = -(-ray_count // 16) * 16
    member = (lax.broadcasted_iota(jnp.int32, (padded, rays), 0) == owner)
    ranks = dot_nn(member.astype(F32).astype(BF16), earlier(rays))
    rank = jnp.sum(jnp.where(member, ranks, 0.0), axis=0, keepdims=True).astype(jnp.int32)
    slot = owner * (rays // ray_count) + rank
    send_ref[...] = (
        (lax.broadcasted_iota(jnp.int32, (rays, rays), 0) == slot).astype(F32).astype(BF16)
    )

    piece = 256

    @pl.loop(0, width // piece)
    def _(step):
        cols = pl.ds(pl.multiple_of(step * piece, piece), piece)
        rendered = dot_tn(table_ref[...], features_ref[:, cols]).astype(BF16)
        out_ref[:, cols] = dot_nn(send_ref[...], rendered).astype(BF16)


def render(me, owner, lists, opacity, counts, pixels, features):
    ray_count = pixels.shape[0]
    depth, rays = lists.shape
    gauss, width = features.shape
    return pl.pallas_call(
        functools.partial(render_kernel, ray_count),
        out_shape=jax.ShapeDtypeStruct((rays, width), BF16),
        in_specs=[SMEM, SMEM, VMEM, VMEM, VMEM, VMEM, VMEM],
        out_specs=VMEM,
        scratch_shapes=[
            pltpu.VMEM((depth, rays), jnp.int32),
            pltpu.VMEM((depth, rays), F32),
            pltpu.VMEM((gauss, rays), BF16),
            pltpu.VMEM((rays, rays), BF16),
        ],
        compiler_params=params(),
        cost_estimate=pl.CostEstimate(
            flops=2 * rays * width * (gauss + rays) + 3 * depth * rays * gauss * 40,
            bytes_accessed=2 * (gauss + rays) * width, transcendentals=0,
        ),
        name="render",
    )(me, owner, lists, opacity, counts, pixels, features)


def tokens_kernel(
    ray_count, me_ref, owner_ref, pixels_ref, tokens_ref, gain_ref,
    tokens_out, normed_out, normed_t_out, place_ref,
):
    rows, width = tokens_ref.shape
    me = me_ref[0]
    each = rows // ray_count
    pixels = pixels_ref[...]
    mine = owner_of(pixels, owner_ref, rows, ray_count) == me
    place = lax.rem(pixels, jnp.int32(rows)).astype(F32)
    member = jnp.where(mine, 1.0, 0.0)
    padded = -(-ray_count // 16) * 16
    if padded > ray_count:
        spread = jnp.concatenate([member, jnp.zeros((padded - ray_count, rows), F32)], axis=0)
    else:
        spread = member
    ranks = dot_nn(spread.astype(BF16), earlier(rows))
    for sender in range(ray_count):
        rank = jnp.where(mine[sender:sender + 1], ranks[sender:sender + 1], -1.0).astype(jnp.int32)
        hit = lax.broadcasted_iota(jnp.int32, (each, rows), 0) == rank
        at = jnp.sum(jnp.where(hit, place[sender:sender + 1], 0.0), axis=1, keepdims=True)
        here = lax.broadcasted_iota(jnp.int32, (each, rows), 1) == at.astype(jnp.int32)
        place_ref[pl.ds(sender * each, each), :] = here.astype(F32).astype(BF16)
    half = min(128, rows)
    gain = gain_ref[...]

    @pl.loop(0, rows // half)
    def _(step):
        span = pl.ds(pl.multiple_of(step * half, half), half)
        values = dot_nn(place_ref[span, :], tokens_ref[...])
        tokens_out[span, :] = values.astype(BF16)
        centered = values - jnp.mean(values, axis=-1, keepdims=True)
        variance = jnp.mean(centered * centered, axis=-1, keepdims=True)
        xhat = centered * lax.rsqrt(variance + STABILITY_EPSILON)
        normed = (xhat * gain).astype(BF16)
        normed_out[span, :] = normed
        normed_t_out[:, span] = normed.T


def prepare_tokens(me, owner, pixels, tokens, gain):
    ray_count = pixels.shape[0]
    rows, width = tokens.shape
    return pl.pallas_call(
        functools.partial(tokens_kernel, ray_count),
        out_shape=(
            jax.ShapeDtypeStruct((rows, width), BF16),
            jax.ShapeDtypeStruct((rows, width), BF16),
            jax.ShapeDtypeStruct((width, rows), BF16),
        ),
        in_specs=[SMEM, SMEM, VMEM, VMEM, VMEM],
        out_specs=(VMEM, VMEM, VMEM),
        scratch_shapes=[pltpu.VMEM((rows, rows), BF16)],
        compiler_params=params(),
        cost_estimate=pl.CostEstimate(
            flops=2 * rows * rows * width * 4, bytes_accessed=8 * rows * width, transcendentals=0
        ),
        name="tokens",
    )(me, owner, pixels, tokens, gain)


def up_kernel(normed_ref, up_ref, act_ref, slope_ref):
    parts, _, part_rows, width = up_ref.shape
    up = up_ref[...].reshape(parts * part_rows, width)
    rows = normed_ref.shape[0]
    piece = min(128, rows)

    @pl.loop(0, rows // piece)
    def _(step):
        span = pl.ds(pl.multiple_of(step * piece, piece), piece)
        hidden = dot_nn(normed_ref[span, :], up)
        phi = 0.5 * (1.0 + lax.erf(hidden * (0.5 ** 0.5)))
        density = jnp.exp(-0.5 * hidden * hidden) * ((2.0 * jnp.pi) ** -0.5)
        act_ref[span, :] = (hidden * phi).astype(BF16)
        slope_ref[span, :] = (phi + hidden * density).astype(slope_ref.dtype)


def project_up(normed, up):
    rows, width = normed.shape
    parts, chunks, part_rows, chunk = up.shape
    return pl.pallas_call(
        up_kernel,
        grid=(chunks,),
        out_shape=(
            jax.ShapeDtypeStruct((rows, chunks * chunk), BF16),
            jax.ShapeDtypeStruct((rows, chunks * chunk), F32),
        ),
        in_specs=[
            pl.BlockSpec((rows, width), lambda j: (0, 0)),
            pl.BlockSpec((parts, 1, part_rows, chunk), lambda j: (0, j, 0, 0)),
        ],
        out_specs=(
            pl.BlockSpec((rows, chunk), lambda j: (0, j)),
            pl.BlockSpec((rows, chunk), lambda j: (0, j)),
        ),
        compiler_params=params(dimension_semantics=("arbitrary",)),
        cost_estimate=pl.CostEstimate(
            flops=2 * rows * width * chunks * chunk * 3,
            bytes_accessed=2 * width * chunks * chunk + 6 * rows * chunks * chunk,
            transcendentals=2 * rows * chunks * chunk,
        ),
        name="up",
    )(normed, up)


def down_kernel(
    chunks, act_ref, down_ref, tokens_ref, target_ref, scale_ref,
    grad_ref, back_ref, small_ref, mixed_ref,
):
    step = pl.program_id(0)
    rows, width = tokens_ref.shape
    act = act_ref[...]

    @pl.when(step < chunks)
    def _():
        parts, _, part_rows, _ = down_ref.shape
        part = dot_nn(act, down_ref[...].reshape(parts * part_rows, width))

        @pl.when(step == 0)
        def _():
            mixed_ref[...] = part

        @pl.when(step > 0)
        def _():
            mixed_ref[...] += part

    @pl.when(step == chunks - 1)
    def _():
        scale = scale_ref[...]
        small_ref[...] = jnp.zeros_like(small_ref)
        piece = min(64, rows)

        @pl.loop(0, rows // piece)
        def _(index):
            span = pl.ds(pl.multiple_of(index * piece, piece), piece)
            mixed = mixed_ref[span, :]
            out = tokens_ref[span, :].astype(F32) + scale * mixed
            goal = target_ref[span, :].astype(F32)
            out_norm = jnp.sqrt(jnp.sum(out * out, axis=-1, keepdims=True) + STABILITY_EPSILON)
            goal_norm = jnp.sqrt(jnp.sum(goal * goal, axis=-1, keepdims=True) + STABILITY_EPSILON)
            norms = out_norm * goal_norm
            cosine = jnp.sum(out * goal, axis=-1, keepdims=True) / norms
            upstream = (cosine / (out_norm * out_norm)) * out - goal * (1.0 / norms)
            back_ref[span, :] = (upstream * scale).astype(BF16)
            small_ref[0:1, :] += jnp.sum(upstream * mixed, axis=0, keepdims=True)
            loss = jnp.sum(1.0 - cosine, axis=0, keepdims=True)
            small_ref[1:2, :] += jnp.broadcast_to(loss, (1, width))

    @pl.when(step >= chunks)
    def _():
        grad = dot_tn(act, back_ref[...])
        grad_ref[...] = grad.astype(BF16).reshape(grad_ref.shape)


def project_down(act, down, tokens, target, scale):
    rows, width = tokens.shape
    parts, chunks, part_rows, _ = down.shape
    chunk = parts * part_rows
    return pl.pallas_call(
        functools.partial(down_kernel, chunks),
        grid=(2 * chunks,),
        out_shape=(
            jax.ShapeDtypeStruct(down.shape, BF16),
            jax.ShapeDtypeStruct((rows, width), BF16),
            jax.ShapeDtypeStruct((8, width), F32),
        ),
        in_specs=[
            pl.BlockSpec((rows, chunk), lambda j: (0, lax.rem(j, chunks))),
            pl.BlockSpec(
                (parts, 1, part_rows, width), lambda j: (0, jnp.minimum(j, chunks - 1), 0, 0)
            ),
            pl.BlockSpec((rows, width), lambda j: (0, 0)),
            pl.BlockSpec((rows, width), lambda j: (0, 0)),
            pl.BlockSpec((1, width), lambda j: (0, 0)),
        ],
        out_specs=(
            pl.BlockSpec(
                (parts, 1, part_rows, width), lambda j: (0, jnp.maximum(j - chunks, 0), 0, 0)
            ),
            pl.BlockSpec((rows, width), lambda j: (0, 0)),
            pl.BlockSpec((8, width), lambda j: (0, 0)),
        ),
        scratch_shapes=[pltpu.VMEM((rows, width), F32)],
        compiler_params=params(dimension_semantics=("arbitrary",)),
        cost_estimate=pl.CostEstimate(
            flops=4 * rows * width * chunks * chunk,
            bytes_accessed=4 * width * chunks * chunk + 4 * rows * chunks * chunk,
            transcendentals=0,
        ),
        name="down",
    )(act, down, tokens, target, scale)


def back_kernel(back_ref, down_ref, slope_ref, normed_t_ref, up_ref, gain_ref, grad_ref, sum_ref):
    step = pl.program_id(0)
    parts, _, part_rows, width = down_ref.shape
    chunk = parts * part_rows
    rows = back_ref.shape[0]
    back_act = dot_nt(back_ref[...], down_ref[...].reshape(chunk, width))
    back_hidden = (back_act * slope_ref[...]).astype(BF16)
    up_parts, _, up_rows, _ = up_ref.shape

    @pl.when(step == 0)
    def _():
        sum_ref[...] = jnp.zeros_like(sum_ref)

    grad = dot_nn(normed_t_ref[...], back_hidden)
    grad_ref[...] = grad.astype(BF16).reshape(grad_ref.shape)
    up = up_ref[...].reshape(up_parts * up_rows, chunk).astype(F32)
    sum_ref[...] += jnp.sum(grad * up, axis=1, keepdims=True) / gain_ref[...]


def back_up(back, down, slope, normed_t, up, gain):
    width, rows = normed_t.shape
    parts, chunks, part_rows, _ = down.shape
    chunk = parts * part_rows
    up_parts, _, up_rows, _ = up.shape
    return pl.pallas_call(
        back_kernel,
        grid=(chunks,),
        out_shape=(
            jax.ShapeDtypeStruct(up.shape, BF16),
            jax.ShapeDtypeStruct((width, 1), F32),
        ),
        in_specs=[
            pl.BlockSpec((rows, width), lambda j: (0, 0)),
            pl.BlockSpec((parts, 1, part_rows, width), lambda j: (0, j, 0, 0)),
            pl.BlockSpec((rows, chunk), lambda j: (0, j)),
            pl.BlockSpec((width, rows), lambda j: (0, 0)),
            pl.BlockSpec((up_parts, 1, up_rows, chunk), lambda j: (0, j, 0, 0)),
            pl.BlockSpec((width, 1), lambda j: (0, 0)),
        ],
        out_specs=(
            pl.BlockSpec((up_parts, 1, up_rows, chunk), lambda j: (0, j, 0, 0)),
            pl.BlockSpec((width, 1), lambda j: (0, 0)),
        ),
        compiler_params=params(dimension_semantics=("arbitrary",)),
        cost_estimate=pl.CostEstimate(
            flops=4 * rows * width * chunks * chunk,
            bytes_accessed=6 * width * chunks * chunk + 4 * rows * chunks * chunk,
            transcendentals=0,
        ),
        name="back",
    )(back, down, slope, normed_t, up, gain)


def gather_weight(weight, parts, group, group_count, ray_count):
    rows, cols = weight.shape
    if parts == 1:
        whole = lax.all_gather(weight, "ray", axis=0, tiled=True)
    else:
        part = lax.dynamic_slice_in_dim(weight, group * (rows // parts), rows // parts, 0)
        whole = lax.all_gather(part, ("grp", "ray"), axis=0, tiled=True)
    return whole.reshape(parts, ray_count, rows // parts, cols)


def reduce_gradient(grad):
    parts, ray_count, part_rows, cols = grad.shape
    flat = grad.reshape(parts * ray_count * part_rows, cols)
    if parts == 1:
        share = lax.psum_scatter(flat, "ray", scatter_dimension=0, tiled=True)
        return lax.psum(share.astype(F32), "grp")
    share = lax.psum_scatter(flat, "grp", scatter_dimension=0, tiled=True)
    share = lax.psum_scatter(share, "ray", scatter_dimension=0, tiled=True)
    return lax.all_gather(share, "grp", axis=0, tiled=True).astype(F32)


def shards(
    image_tokens,
    tile_lists,
    opacity,
    tile_counts,
    ray_pixel,
    block_owner,
    gaussian_features,
    layer_norm_gain,
    layer_scale,
    up_weight,
    down_weight,
):
    ray_count = lax.axis_size("ray")
    group_count = lax.axis_size("grp")
    group = lax.axis_index("grp")
    me = lax.axis_index("ray").reshape(1)
    rows, width = image_tokens.shape
    up_parts = group_count if up_weight.shape[0] % (16 * group_count) == 0 else 1
    down_parts = group_count if down_weight.shape[0] % (16 * group_count) == 0 else 1
    up = gather_weight(up_weight, up_parts, group, group_count, ray_count)
    down = gather_weight(down_weight, down_parts, group, group_count, ray_count)
    pixels = ray_pixel[0].reshape(ray_count, rows)
    rendered = render(
        me, block_owner, tile_lists, opacity, tile_counts.reshape(1, rows), pixels,
        gaussian_features,
    )
    target = lax.all_to_all(rendered, "ray", split_axis=0, concat_axis=0, tiled=True)
    tokens, normed, normed_t = prepare_tokens(
        me, block_owner, pixels, image_tokens, layer_norm_gain.reshape(1, width)
    )
    act, slope = project_up(normed, up)
    grad_down, back, small = project_down(act, down, tokens, target, layer_scale.reshape(1, width))
    grad_up, gain_sum = back_up(back, down, slope, normed_t, up, layer_norm_gain.reshape(width, 1))
    grad_down = reduce_gradient(grad_down)
    grad_up = reduce_gradient(grad_up)
    sums = jnp.concatenate([gain_sum.reshape(1, width), small[:2]], axis=0)
    sums = lax.psum(sums, ("grp", "ray"))
    loss = sums[2, 0] / (rows * ray_count * group_count)
    return (grad_up, grad_down, sums[0], sums[1], loss)


def solution(mesh):
    return jax.shard_map(
        shards,
        mesh=mesh,
        in_specs=(
            P(("grp", "ray"), None),
            P(None, ("grp", "ray")),
            P(None, ("grp", "ray")),
            P(("grp", "ray")),
            P("grp", None),
            P("grp", None),
            P(("grp", "ray"), None),
            P(),
            P(),
            P(None, "ray"),
            P("ray", None),
        ),
        out_specs=(P(None, "ray"), P("ray", None), P(), P(), P()),
        check_vma=False,
    )
```

```python
import functools

import jax
import jax.numpy as jnp
from jax import lax
from jax.experimental import pallas as pl
from jax.experimental.pallas import tpu as pltpu
from jax.sharding import PartitionSpec as P

STABILITY_EPSILON = 1e-06
F32 = jnp.float32
BF16 = jnp.bfloat16
VMEM_BYTES = 56 * 1024 * 1024
SMALL_VMEM_BYTES = 28 * 1024 * 1024
SMEM = pl.BlockSpec(memory_space=pltpu.SMEM)
VMEM = pl.BlockSpec(memory_space=pltpu.VMEM)


def params(**more):
    return pltpu.CompilerParams(vmem_limit_bytes=VMEM_BYTES, **more)


def small_params():
    return pltpu.CompilerParams(vmem_limit_bytes=SMALL_VMEM_BYTES)


def dot_nn(a, b):
    return lax.dot_general(a, b, (((1,), (0,)), ((), ())), preferred_element_type=F32)


def dot_tn(a, b):
    return lax.dot_general(a, b, (((0,), (0,)), ((), ())), preferred_element_type=F32)


def dot_nt(a, b):
    return lax.dot_general(a, b, (((1,), (1,)), ((), ())), preferred_element_type=F32)


def owner_of(pixels, owner_ref, rows, count):
    block = lax.div(pixels, jnp.int32(rows))
    owner = jnp.zeros_like(pixels)
    for slot in range(count):
        owner = jnp.where(block == slot, owner_ref[0, slot], owner)
    return owner


def earlier(rows):
    before = lax.broadcasted_iota(jnp.int32, (rows, rows), 0)
    after = lax.broadcasted_iota(jnp.int32, (rows, rows), 1)
    return jnp.where(before < after, 1.0, 0.0).astype(BF16)


def render_kernel(
    ray_count, me_ref, owner_ref, lists_ref, opacity_ref, counts_ref, pixels_ref, features_ref,
    out_ref, ids_ref, share_ref, table_ref, send_ref,
):
    depth, rays = lists_ref.shape
    gauss = features_ref.shape[0]
    width = features_ref.shape[1]
    me = me_ref[0]
    ids_ref[...] = lists_ref[...] - me * gauss
    passing = jnp.ones((1, rays), F32)
    counts = counts_ref[...]
    for level in range(depth):
        alpha = opacity_ref[pl.ds(level, 1), :]
        share_ref[pl.ds(level, 1), :] = jnp.where(level < counts, alpha * passing, 0.0)
        passing = passing * (1.0 - alpha)

    tile = 128
    lanes = 128
    columns = rays // lanes

    @pl.loop(0, (gauss // tile) * columns)
    def _(step):
        first = pl.multiple_of(lax.div(step, columns) * tile, tile)
        lane = pl.multiple_of(lax.rem(step, columns) * lanes, lanes)
        number = lax.broadcasted_iota(jnp.int32, (tile, lanes), 0) + first
        total = jnp.zeros((tile, lanes), F32)
        for level in range(depth):
            ident = ids_ref[pl.ds(level, 1), pl.ds(lane, lanes)]
            share = share_ref[pl.ds(level, 1), pl.ds(lane, lanes)]
            total = total + jnp.where(ident == number, share, 0.0)
        table_ref[pl.ds(first, tile), pl.ds(lane, lanes)] = total.astype(BF16)

    mine = pixels_ref[pl.ds(me, 1), :]
    owner = owner_of(mine, owner_ref, rays, ray_count)
    padded = -(-ray_count // 16) * 16
    member = (lax.broadcasted_iota(jnp.int32, (padded, rays), 0) == owner)
    ranks = dot_nn(member.astype(F32).astype(BF16), earlier(rays))
    rank = jnp.sum(jnp.where(member, ranks, 0.0), axis=0, keepdims=True).astype(jnp.int32)
    slot = owner * (rays // ray_count) + rank
    send_ref[...] = (
        (lax.broadcasted_iota(jnp.int32, (rays, rays), 0) == slot).astype(F32).astype(BF16)
    )

    piece = 256

    @pl.loop(0, width // piece)
    def _(step):
        cols = pl.ds(pl.multiple_of(step * piece, piece), piece)
        rendered = dot_tn(table_ref[...], features_ref[:, cols]).astype(BF16)
        out_ref[:, cols] = dot_nn(send_ref[...], rendered).astype(BF16)


def render(me, owner, lists, opacity, counts, pixels, features):
    ray_count = pixels.shape[0]
    depth, rays = lists.shape
    gauss, width = features.shape
    return pl.pallas_call(
        functools.partial(render_kernel, ray_count),
        out_shape=jax.ShapeDtypeStruct((rays, width), BF16),
        in_specs=[SMEM, SMEM, VMEM, VMEM, VMEM, VMEM, VMEM],
        out_specs=VMEM,
        scratch_shapes=[
            pltpu.VMEM((depth, rays), jnp.int32),
            pltpu.VMEM((depth, rays), F32),
            pltpu.VMEM((gauss, rays), BF16),
            pltpu.VMEM((rays, rays), BF16),
        ],
        compiler_params=params(),
        cost_estimate=pl.CostEstimate(
            flops=2 * rays * width * (gauss + rays) + 3 * depth * rays * gauss * 40,
            bytes_accessed=2 * (gauss + rays) * width, transcendentals=0,
        ),
        name="render",
    )(me, owner, lists, opacity, counts, pixels, features)


def tokens_kernel(
    ray_count, me_ref, owner_ref, pixels_ref, tokens_ref, gain_ref,
    tokens_out, normed_out, normed_t_out, place_ref,
):
    rows, width = tokens_ref.shape
    me = me_ref[0]
    each = rows // ray_count
    pixels = pixels_ref[...]
    mine = owner_of(pixels, owner_ref, rows, ray_count) == me
    place = lax.rem(pixels, jnp.int32(rows)).astype(F32)
    member = jnp.where(mine, 1.0, 0.0)
    padded = -(-ray_count // 16) * 16
    if padded > ray_count:
        spread = jnp.concatenate([member, jnp.zeros((padded - ray_count, rows), F32)], axis=0)
    else:
        spread = member
    ranks = dot_nn(spread.astype(BF16), earlier(rows))
    for sender in range(ray_count):
        rank = jnp.where(mine[sender:sender + 1], ranks[sender:sender + 1], -1.0).astype(jnp.int32)
        hit = lax.broadcasted_iota(jnp.int32, (each, rows), 0) == rank
        at = jnp.sum(jnp.where(hit, place[sender:sender + 1], 0.0), axis=1, keepdims=True)
        here = lax.broadcasted_iota(jnp.int32, (each, rows), 1) == at.astype(jnp.int32)
        place_ref[pl.ds(sender * each, each), :] = here.astype(F32).astype(BF16)
    half = min(128, rows)
    gain = gain_ref[...]

    @pl.loop(0, rows // half)
    def _(step):
        span = pl.ds(pl.multiple_of(step * half, half), half)
        values = dot_nn(place_ref[span, :], tokens_ref[...])
        tokens_out[span, :] = values.astype(BF16)
        centered = values - jnp.mean(values, axis=-1, keepdims=True)
        variance = jnp.mean(centered * centered, axis=-1, keepdims=True)
        xhat = centered * lax.rsqrt(variance + STABILITY_EPSILON)
        normed = (xhat * gain).astype(BF16)
        normed_out[span, :] = normed
        normed_t_out[:, span] = normed.T


def prepare_tokens(me, owner, pixels, tokens, gain):
    ray_count = pixels.shape[0]
    rows, width = tokens.shape
    return pl.pallas_call(
        functools.partial(tokens_kernel, ray_count),
        out_shape=(
            jax.ShapeDtypeStruct((rows, width), BF16),
            jax.ShapeDtypeStruct((rows, width), BF16),
            jax.ShapeDtypeStruct((width, rows), BF16),
        ),
        in_specs=[SMEM, SMEM, VMEM, VMEM, VMEM],
        out_specs=(VMEM, VMEM, VMEM),
        scratch_shapes=[pltpu.VMEM((rows, rows), BF16)],
        compiler_params=params(),
        cost_estimate=pl.CostEstimate(
            flops=2 * rows * rows * width * 4, bytes_accessed=8 * rows * width, transcendentals=0
        ),
        name="tokens",
    )(me, owner, pixels, tokens, gain)


def up_kernel(normed_ref, up_ref, act_ref, slope_ref):
    parts, _, part_rows, width = up_ref.shape
    up = up_ref[...].reshape(parts * part_rows, width)
    rows = normed_ref.shape[0]
    piece = min(128, rows)

    @pl.loop(0, rows // piece)
    def _(step):
        span = pl.ds(pl.multiple_of(step * piece, piece), piece)
        hidden = dot_nn(normed_ref[span, :], up)
        phi = 0.5 * (1.0 + lax.erf(hidden * (0.5 ** 0.5)))
        density = jnp.exp(-0.5 * hidden * hidden) * ((2.0 * jnp.pi) ** -0.5)
        act_ref[span, :] = (hidden * phi).astype(BF16)
        slope_ref[span, :] = (phi + hidden * density).astype(slope_ref.dtype)


def project_up(normed, up):
    rows, width = normed.shape
    parts, chunks, part_rows, chunk = up.shape
    return pl.pallas_call(
        up_kernel,
        grid=(chunks,),
        out_shape=(
            jax.ShapeDtypeStruct((rows, chunks * chunk), BF16),
            jax.ShapeDtypeStruct((rows, chunks * chunk), F32),
        ),
        in_specs=[
            pl.BlockSpec((rows, width), lambda j: (0, 0)),
            pl.BlockSpec((parts, 1, part_rows, chunk), lambda j: (0, j, 0, 0)),
        ],
        out_specs=(
            pl.BlockSpec((rows, chunk), lambda j: (0, j)),
            pl.BlockSpec((rows, chunk), lambda j: (0, j)),
        ),
        compiler_params=params(dimension_semantics=("arbitrary",)),
        cost_estimate=pl.CostEstimate(
            flops=2 * rows * width * chunks * chunk * 3,
            bytes_accessed=2 * width * chunks * chunk + 6 * rows * chunks * chunk,
            transcendentals=2 * rows * chunks * chunk,
        ),
        name="up",
    )(normed, up)


def down_kernel(
    chunks, act_ref, down_ref, tokens_ref, target_ref, scale_ref,
    grad_ref, back_ref, small_ref, mixed_ref,
):
    step = pl.program_id(0)
    rows, width = tokens_ref.shape
    act = act_ref[...]

    @pl.when(step < chunks)
    def _():
        parts, _, part_rows, _ = down_ref.shape
        part = dot_nn(act, down_ref[...].reshape(parts * part_rows, width))

        @pl.when(step == 0)
        def _():
            mixed_ref[...] = part

        @pl.when(step > 0)
        def _():
            mixed_ref[...] += part

    @pl.when(step == chunks - 1)
    def _():
        scale = scale_ref[...]
        small_ref[...] = jnp.zeros_like(small_ref)
        piece = min(64, rows)

        @pl.loop(0, rows // piece)
        def _(index):
            span = pl.ds(pl.multiple_of(index * piece, piece), piece)
            mixed = mixed_ref[span, :]
            out = tokens_ref[span, :].astype(F32) + scale * mixed
            goal = target_ref[span, :].astype(F32)
            out_norm = jnp.sqrt(jnp.sum(out * out, axis=-1, keepdims=True) + STABILITY_EPSILON)
            goal_norm = jnp.sqrt(jnp.sum(goal * goal, axis=-1, keepdims=True) + STABILITY_EPSILON)
            norms = out_norm * goal_norm
            cosine = jnp.sum(out * goal, axis=-1, keepdims=True) / norms
            upstream = (cosine / (out_norm * out_norm)) * out - goal * (1.0 / norms)
            back_ref[span, :] = (upstream * scale).astype(BF16)
            small_ref[0:1, :] += jnp.sum(upstream * mixed, axis=0, keepdims=True)
            loss = jnp.sum(1.0 - cosine, axis=0, keepdims=True)
            small_ref[1:2, :] += jnp.broadcast_to(loss, (1, width))

    @pl.when(step >= chunks)
    def _():
        grad = dot_tn(act, back_ref[...])
        grad_ref[...] = grad.astype(BF16).reshape(grad_ref.shape)


def project_down(act, down, tokens, target, scale):
    rows, width = tokens.shape
    parts, chunks, part_rows, _ = down.shape
    chunk = parts * part_rows
    return pl.pallas_call(
        functools.partial(down_kernel, chunks),
        grid=(2 * chunks,),
        out_shape=(
            jax.ShapeDtypeStruct(down.shape, BF16),
            jax.ShapeDtypeStruct((rows, width), BF16),
            jax.ShapeDtypeStruct((8, width), F32),
        ),
        in_specs=[
            pl.BlockSpec((rows, chunk), lambda j: (0, lax.rem(j, chunks))),
            pl.BlockSpec(
                (parts, 1, part_rows, width), lambda j: (0, jnp.minimum(j, chunks - 1), 0, 0)
            ),
            pl.BlockSpec((rows, width), lambda j: (0, 0)),
            pl.BlockSpec((rows, width), lambda j: (0, 0)),
            pl.BlockSpec((1, width), lambda j: (0, 0)),
        ],
        out_specs=(
            pl.BlockSpec(
                (parts, 1, part_rows, width), lambda j: (0, jnp.maximum(j - chunks, 0), 0, 0)
            ),
            pl.BlockSpec((rows, width), lambda j: (0, 0)),
            pl.BlockSpec((8, width), lambda j: (0, 0)),
        ),
        scratch_shapes=[pltpu.VMEM((rows, width), F32)],
        compiler_params=params(dimension_semantics=("arbitrary",)),
        cost_estimate=pl.CostEstimate(
            flops=4 * rows * width * chunks * chunk,
            bytes_accessed=4 * width * chunks * chunk + 4 * rows * chunks * chunk,
            transcendentals=0,
        ),
        name="down",
    )(act, down, tokens, target, scale)


def back_kernel(back_ref, down_ref, slope_ref, normed_t_ref, up_ref, gain_ref, grad_ref, sum_ref):
    step = pl.program_id(0)
    parts, _, part_rows, width = down_ref.shape
    chunk = parts * part_rows
    rows = back_ref.shape[0]
    back_act = dot_nt(back_ref[...], down_ref[...].reshape(chunk, width))
    back_hidden = (back_act * slope_ref[...]).astype(BF16)
    up_parts, _, up_rows, _ = up_ref.shape

    @pl.when(step == 0)
    def _():
        sum_ref[...] = jnp.zeros_like(sum_ref)

    grad = dot_nn(normed_t_ref[...], back_hidden)
    grad_ref[...] = grad.astype(BF16).reshape(grad_ref.shape)
    up = up_ref[...].reshape(up_parts * up_rows, chunk).astype(F32)
    sum_ref[...] += jnp.sum(grad * up, axis=1, keepdims=True) / gain_ref[...]


def back_up(back, down, slope, normed_t, up, gain):
    width, rows = normed_t.shape
    parts, chunks, part_rows, _ = down.shape
    chunk = parts * part_rows
    up_parts, _, up_rows, _ = up.shape
    return pl.pallas_call(
        back_kernel,
        grid=(chunks,),
        out_shape=(
            jax.ShapeDtypeStruct(up.shape, BF16),
            jax.ShapeDtypeStruct((width, 1), F32),
        ),
        in_specs=[
            pl.BlockSpec((rows, width), lambda j: (0, 0)),
            pl.BlockSpec((parts, 1, part_rows, width), lambda j: (0, j, 0, 0)),
            pl.BlockSpec((rows, chunk), lambda j: (0, j)),
            pl.BlockSpec((width, rows), lambda j: (0, 0)),
            pl.BlockSpec((up_parts, 1, up_rows, chunk), lambda j: (0, j, 0, 0)),
            pl.BlockSpec((width, 1), lambda j: (0, 0)),
        ],
        out_specs=(
            pl.BlockSpec((up_parts, 1, up_rows, chunk), lambda j: (0, j, 0, 0)),
            pl.BlockSpec((width, 1), lambda j: (0, 0)),
        ),
        compiler_params=params(dimension_semantics=("arbitrary",)),
        cost_estimate=pl.CostEstimate(
            flops=4 * rows * width * chunks * chunk,
            bytes_accessed=6 * width * chunks * chunk + 4 * rows * chunks * chunk,
            transcendentals=0,
        ),
        name="back",
    )(back, down, slope, normed_t, up, gain)


def gather_weight(weight, parts, group, group_count, ray_count):
    rows, cols = weight.shape
    if parts == 1:
        whole = lax.all_gather(weight, "ray", axis=0, tiled=True)
    else:
        part = lax.dynamic_slice_in_dim(weight, group * (rows // parts), rows // parts, 0)
        whole = lax.all_gather(part, ("grp", "ray"), axis=0, tiled=True)
    return whole.reshape(parts, ray_count, rows // parts, cols)


def reduce_gradient(grad):
    parts, ray_count, part_rows, cols = grad.shape
    flat = grad.reshape(parts * ray_count * part_rows, cols)
    if parts == 1:
        share = lax.psum_scatter(flat, "ray", scatter_dimension=0, tiled=True)
        return lax.psum(share.astype(F32), "grp")
    share = lax.psum_scatter(flat, "grp", scatter_dimension=0, tiled=True)
    share = lax.psum_scatter(share, "ray", scatter_dimension=0, tiled=True)
    return lax.all_gather(share, "grp", axis=0, tiled=True).astype(F32)


def shards_general(
    image_tokens,
    tile_lists,
    opacity,
    tile_counts,
    ray_pixel,
    block_owner,
    gaussian_features,
    layer_norm_gain,
    layer_scale,
    up_weight,
    down_weight,
):
    ray_count = lax.axis_size("ray")
    group_count = lax.axis_size("grp")
    group = lax.axis_index("grp")
    me = lax.axis_index("ray").reshape(1)
    rows, width = image_tokens.shape
    up_parts = group_count if up_weight.shape[0] % (16 * group_count) == 0 else 1
    down_parts = group_count if down_weight.shape[0] % (16 * group_count) == 0 else 1
    up = gather_weight(up_weight, up_parts, group, group_count, ray_count)
    down = gather_weight(down_weight, down_parts, group, group_count, ray_count)
    pixels = ray_pixel[0].reshape(ray_count, rows)
    rendered = render(
        me, block_owner, tile_lists, opacity, tile_counts.reshape(1, rows), pixels,
        gaussian_features,
    )
    target = lax.all_to_all(rendered, "ray", split_axis=0, concat_axis=0, tiled=True)
    tokens, normed, normed_t = prepare_tokens(
        me, block_owner, pixels, image_tokens, layer_norm_gain.reshape(1, width)
    )
    act, slope = project_up(normed, up)
    grad_down, back, small = project_down(act, down, tokens, target, layer_scale.reshape(1, width))
    grad_up, gain_sum = back_up(back, down, slope, normed_t, up, layer_norm_gain.reshape(width, 1))
    grad_down = reduce_gradient(grad_down)
    grad_up = reduce_gradient(grad_up)
    sums = jnp.concatenate([gain_sum.reshape(1, width), small[:2]], axis=0)
    sums = lax.psum(sums, ("grp", "ray"))
    loss = sums[2, 0] / (rows * ray_count * group_count)
    return (grad_up, grad_down, sums[0], sums[1], loss)


def quarter_kernel(group_ref, up_ref, down_ref, out_ref, turned_ref):
    part = out_ref.shape[1]
    first = pl.multiple_of(group_ref[0] * part, part)
    turned_ref[...] = up_ref[...].T
    out_ref[0] = turned_ref[pl.ds(first, part), :]
    out_ref[1] = down_ref[pl.ds(first, part), :]


def own_quarter(group, up, down, part):
    width, chunk = up.shape
    return pl.pallas_call(
        quarter_kernel,
        out_shape=jax.ShapeDtypeStruct((2, part, width), BF16),
        in_specs=[SMEM, VMEM, VMEM],
        out_specs=VMEM,
        scratch_shapes=[pltpu.VMEM((chunk, width), BF16)],
        compiler_params=small_params(),
        cost_estimate=pl.CostEstimate(flops=0, bytes_accessed=6 * width * chunk, transcendentals=0),
        name="quarter",
    )(group, up, down)


def finish_rows(tokens, mixed, goal, scale):
    out = tokens + scale * mixed
    out_norm = jnp.sqrt(jnp.sum(out * out, axis=-1, keepdims=True) + STABILITY_EPSILON)
    goal_norm = jnp.sqrt(jnp.sum(goal * goal, axis=-1, keepdims=True) + STABILITY_EPSILON)
    norms = out_norm * goal_norm
    cosine = jnp.sum(out * goal, axis=-1, keepdims=True) / norms
    upstream = (cosine / (out_norm * out_norm)) * out - goal * (1.0 / norms)
    return upstream, 1.0 - cosine


def forward_kernel(first, last, *refs):
    refs = list(refs)
    normed_t_ref, own_ref, other_ref = refs[:3]
    del refs[:3]
    mixed_in = None if first else refs.pop(0)
    if last:
        tokens_ref, target_ref, scale_ref = refs[:3]
        del refs[:3]
    act_ref, slope_ref = refs[:2]
    del refs[:2]
    count, _, part, width = own_ref.shape
    rows = normed_t_ref.shape[1]
    for side, ref in enumerate((own_ref, other_ref)):
        for index in range(count):
            hidden = dot_nn(ref[index, 0], normed_t_ref[...])
            phi = 0.5 * (1.0 + lax.erf(hidden * (0.5 ** 0.5)))
            density = jnp.exp(-0.5 * hidden * hidden) * ((2.0 * jnp.pi) ** -0.5)
            act_ref[side, index] = (hidden * phi).astype(BF16)
            slope_ref[side, index] = phi + hidden * density
    act = act_ref[...].reshape(2 * count * part, rows)
    down = jnp.concatenate(
        [own_ref[:, 1].reshape(count * part, width), other_ref[:, 1].reshape(count * part, width)],
        axis=0,
    )
    if not last:
        mixed_out = refs[0]
        part_sum = dot_tn(act, down)
        mixed_out[...] = part_sum if first else mixed_in[...] + part_sum
        return
    back_ref, back_t_ref, small_ref, mixed_ref = refs
    mixed_ref[...] = mixed_in[...] + dot_tn(act, down)
    scale = scale_ref[...]
    small_ref[...] = jnp.zeros_like(small_ref)
    piece = 128

    @pl.loop(0, rows // piece)
    def _(index):
        span = pl.ds(pl.multiple_of(index * piece, piece), piece)
        mixed = mixed_ref[span, :]
        upstream, loss = finish_rows(
            tokens_ref[span, :].astype(F32), mixed, target_ref[span, :].astype(F32), scale
        )
        back = (upstream * scale).astype(BF16)
        back_ref[span, :] = back
        back_t_ref[:, span] = back.T
        small_ref[0:1, :] += jnp.sum(upstream * mixed, axis=0, keepdims=True)
        small_ref[1:2, :] += jnp.broadcast_to(jnp.sum(loss, axis=0, keepdims=True), (1, width))


def forward(normed_t, own, other, mixed=None, finish=None):
    width, rows = normed_t.shape
    count, _, part, _ = own.shape
    first, last = mixed is None, finish is not None
    operands = [normed_t, own, other]
    if not first:
        operands.append(mixed)
    if last:
        operands.extend(finish)
    piece = (2, count, part, rows)
    shapes = [jax.ShapeDtypeStruct(piece, BF16), jax.ShapeDtypeStruct(piece, F32)]
    scratch = []
    if last:
        shapes += [
            jax.ShapeDtypeStruct((rows, width), BF16),
            jax.ShapeDtypeStruct((width, rows), BF16),
            jax.ShapeDtypeStruct((8, width), F32),
        ]
        scratch = [pltpu.VMEM((rows, width), F32)]
    else:
        shapes += [jax.ShapeDtypeStruct((rows, width), F32)]
    return pl.pallas_call(
        functools.partial(forward_kernel, first, last),
        out_shape=tuple(shapes),
        in_specs=[VMEM] * len(operands),
        out_specs=tuple([VMEM] * len(shapes)),
        scratch_shapes=scratch,
        compiler_params=small_params(),
        cost_estimate=pl.CostEstimate(
            flops=8 * rows * width * count * part * 2,
            bytes_accessed=4 * rows * width, transcendentals=0,
        ),
        name="forward",
    )(*operands)


def backward_kernel(side, quarter, add, *refs):
    refs = list(refs)
    back_ref, back_t_ref, normed_ref, near_ref, far_ref = refs[:5]
    act_near, slope_near, act_far, slope_far = refs[5:9]
    del refs[:9]
    arrived = refs.pop(0) if add else None
    up_ref, down_ref, gain_ref = refs
    part, width = near_ref.shape[-2:]
    far = far_ref.shape[0]
    chunk = (far + 1) * part
    rows = back_ref.shape[0]

    def joined(near, other):
        return jnp.concatenate([near, other.reshape(far * part, other.shape[-1])], axis=0)

    slope = joined(slope_near[side, quarter], slope_far[side])
    back_act = dot_nn(joined(near_ref[quarter, 1], far_ref[:, 1]), back_t_ref[...])
    back_hidden = (back_act * slope).astype(BF16)
    grad_up = dot_nn(back_hidden, normed_ref[...])
    up = joined(near_ref[quarter, 0], far_ref[:, 0]).astype(F32)
    gain_ref[...] = jnp.sum(grad_up * up, axis=0, keepdims=True)
    grad_down = dot_nn(joined(act_near[side, quarter], act_far[side]), back_ref[...])
    if add:
        grad_up += arrived[0].reshape(chunk, width).astype(F32)
        grad_down += arrived[1].reshape(chunk, width).astype(F32)
    up_ref[...] = grad_up.astype(BF16).reshape(up_ref.shape)
    down_ref[...] = grad_down.astype(BF16).reshape(down_ref.shape)


def backward(side, quarter, common, near, far, act_near, slope_near, act_far, slope_far, arrived):
    back, back_t, normed = common
    rows, width = back.shape
    part = near.shape[2]
    count = far.shape[0] + 1
    operands = [back, back_t, normed, near, far, act_near, slope_near, act_far, slope_far]
    if arrived is None:
        def body(*refs):
            grads, gain_ref = refs[-2:]
            backward_kernel(
                side, quarter, False, *refs[:-2], grads.at[0], grads.at[1], gain_ref
            )

        shapes = [jax.ShapeDtypeStruct((2, count, part, width), BF16)]
    else:
        operands.append(arrived)
        body = functools.partial(backward_kernel, side, quarter, True)
        shapes = [jax.ShapeDtypeStruct((count, part, width), BF16)] * 2
    shapes.append(jax.ShapeDtypeStruct((1, width), F32))
    return pl.pallas_call(
        body,
        out_shape=tuple(shapes),
        in_specs=[VMEM] * len(operands),
        out_specs=tuple([VMEM] * len(shapes)),
        compiler_params=small_params(),
        cost_estimate=pl.CostEstimate(
            flops=6 * rows * width * count * part,
            bytes_accessed=6 * rows * width, transcendentals=0,
        ),
        name="backward",
    )(*operands)


def total_kernel(*refs):
    ins, outs = refs[:4], refs[4:]
    for index, out in enumerate(outs):
        total = ins[0][index].astype(F32)
        for ref in ins[1:]:
            total = total + ref[index].astype(F32)
        out[...] = total.astype(BF16)


def totals(parts):
    count, part, width = parts[0].shape
    return pl.pallas_call(
        total_kernel,
        out_shape=tuple([jax.ShapeDtypeStruct((part, width), BF16)] * count),
        in_specs=[VMEM] * 4,
        out_specs=tuple([VMEM] * count),
        compiler_params=small_params(),
        cost_estimate=pl.CostEstimate(
            flops=4 * count * part * width, bytes_accessed=10 * count * part * width,
            transcendentals=0,
        ),
        name="totals",
    )(*parts)


def place_kernel(turn, group_ref, a_ref, b_ref, c_ref, d_ref, out_ref, held_ref):
    part = a_ref.shape[0]
    group = group_ref[0]
    for index, ref in enumerate((a_ref, b_ref, c_ref, d_ref)):
        first = pl.multiple_of(jnp.bitwise_xor(group, index) * part, part)
        held_ref[pl.ds(first, part), :] = ref[...].astype(F32)
    out_ref[...] = held_ref[...].T if turn else held_ref[...]


def place_quarters(group, quarters, turn):
    part, width = quarters[0].shape
    shape = (width, 4 * part) if turn else (4 * part, width)
    return pl.pallas_call(
        functools.partial(place_kernel, turn),
        out_shape=jax.ShapeDtypeStruct(shape, F32),
        in_specs=[SMEM] + [VMEM] * 4,
        out_specs=VMEM,
        scratch_shapes=[pltpu.VMEM((4 * part, width), F32)],
        compiler_params=small_params(),
        cost_estimate=pl.CostEstimate(
            flops=0, bytes_accessed=24 * part * width, transcendentals=0
        ),
        name="place",
    )(group, *quarters)


def shards_square(
    image_tokens,
    tile_lists,
    opacity,
    tile_counts,
    ray_pixel,
    block_owner,
    gaussian_features,
    layer_norm_gain,
    layer_scale,
    up_weight,
    down_weight,
):
    ray_count = lax.axis_size("ray")
    group_count = lax.axis_size("grp")
    depth = ray_count // 2
    group = lax.axis_index("grp").reshape(1)
    me = lax.axis_index("ray").reshape(1)
    rows, width = image_tokens.shape
    part = down_weight.shape[0] // group_count

    def beside(array, flip):
        return lax.ppermute(array, "grp", [(g, g ^ flip) for g in range(group_count)])

    def partner(array, flip=1):
        return lax.ppermute(array, "ray", [(r, r ^ flip) for r in range(ray_count)])

    def along(array, shift):
        pairs = [(r, (r + 2 * shift) % ray_count) for r in range(ray_count)]
        return lax.ppermute(array, "ray", pairs)

    mine = own_quarter(group, up_weight, down_weight, part)
    far = [along(mine, -shift) for shift in range(1, depth)]
    near = jnp.stack([mine] + [beside(mine, flip) for flip in (1, 2, 3)])
    near_other = partner(near)
    far = jnp.stack(far)
    far = [far] + [beside(far, flip) for flip in (1, 2, 3)]
    far_other = [partner(array) for array in far]

    pixels = ray_pixel[0].reshape(ray_count, rows)
    rendered = render(
        me, block_owner, tile_lists, opacity, tile_counts.reshape(1, rows), pixels,
        gaussian_features,
    )
    target = lax.all_to_all(rendered, "ray", split_axis=0, concat_axis=0, tiled=True)
    tokens, normed, normed_t = prepare_tokens(
        me, block_owner, pixels, image_tokens, layer_norm_gain.reshape(1, width)
    )
    act_near, slope_near, mixed = forward(normed_t, near, near_other)
    act_far, slope_far = [None] * 4, [None] * 4
    for quarter in (0, 1, 2):
        act_far[quarter], slope_far[quarter], mixed = forward(
            normed_t, far[quarter], far_other[quarter], mixed
        )
    act_far[3], slope_far[3], back, back_t, small = forward(
        normed_t, far[3], far_other[3], mixed, (tokens, target, layer_scale.reshape(1, width))
    )
    common = (back, back_t, normed)

    def grads(side, quarter, arrived):
        weights = (near, far) if side == 0 else (near_other, far_other)
        return backward(
            side, quarter, common, weights[0], weights[1][quarter], act_near, slope_near,
            act_far[quarter], slope_far[quarter], arrived,
        )

    order = (3, 1, 2, 0)
    arrived, gains, sums = {}, [], {}
    for quarter in order:
        out, gain = grads(1, quarter, None)
        arrived[quarter] = partner(out)
        gains.append(gain)
    for quarter in order:
        grad_up, grad_down, gain = grads(0, quarter, arrived[quarter])
        gains.append(gain)
        sums[quarter] = (grad_up, grad_down)
    sent = {
        (quarter, which): beside(sums[quarter][which], quarter)
        for which in (1, 0) for quarter in (3, 1, 2)
    }
    results = {}
    for which in (1, 0):
        shares = totals([sums[0][which]] + [sent[quarter, which] for quarter in (1, 2, 3)])
        total = shares[0].astype(F32)
        for shift in range(1, depth):
            total = total + along(shares[shift], shift).astype(F32)
        total = total.astype(BF16)
        results[which] = place_quarters(
            group, [total] + [beside(total, flip) for flip in (1, 2, 3)], which == 0
        )
    vector = jnp.concatenate(
        [sum(gains) / layer_norm_gain.reshape(1, width), small[:2]], axis=0
    )
    vector = vector + partner(vector)
    for flip in (1, 2):
        vector = vector + beside(vector, flip)
    flip = 2
    while flip < ray_count:
        vector = vector + partner(vector, flip)
        flip *= 2
    loss = vector[2, 0] / (rows * ray_count * group_count)
    return (results[0], results[1], vector[0], vector[1], loss)


def shards(*operands):
    ray_count, group_count = lax.axis_size("ray"), lax.axis_size("grp")
    hidden = operands[-1].shape[0]
    square = group_count == 4 and ray_count in (4, 8, 16) and hidden % (16 * group_count) == 0
    return (shards_square if square else shards_general)(*operands)


def solution(mesh):
    return jax.shard_map(
        shards,
        mesh=mesh,
        in_specs=(
            P(("grp", "ray"), None),
            P(None, ("grp", "ray")),
            P(None, ("grp", "ray")),
            P(("grp", "ray")),
            P("grp", None),
            P("grp", None),
            P(("grp", "ray"), None),
            P(),
            P(),
            P(None, "ray"),
            P("ray", None),
        ),
        out_specs=(P(None, "ray"), P("ray", None), P(), P(), P()),
        check_vma=False,
    )
```

```python
import functools

import jax
import jax.numpy as jnp
from jax import lax
from jax.experimental import pallas as pl
from jax.experimental.pallas import tpu as pltpu
from jax.sharding import PartitionSpec as P

STABILITY_EPSILON = 1e-06
F32 = jnp.float32
BF16 = jnp.bfloat16
VMEM_BYTES = 56 * 1024 * 1024
SMALL_VMEM_BYTES = 28 * 1024 * 1024
COST = pl.CostEstimate(flops=1 << 20, bytes_accessed=1 << 16, transcendentals=0)
SMEM = pl.BlockSpec(memory_space=pltpu.SMEM)
VMEM = pl.BlockSpec(memory_space=pltpu.VMEM)
ANY = pl.BlockSpec(memory_space=pl.ANY)


def params(**more):
    return pltpu.CompilerParams(vmem_limit_bytes=VMEM_BYTES, **more)


def small_params():
    return pltpu.CompilerParams(vmem_limit_bytes=SMALL_VMEM_BYTES)


def dot_nn(a, b):
    return lax.dot_general(a, b, (((1,), (0,)), ((), ())), preferred_element_type=F32)


def dot_tn(a, b):
    return lax.dot_general(a, b, (((0,), (0,)), ((), ())), preferred_element_type=F32)


def dot_nt(a, b):
    return lax.dot_general(a, b, (((1,), (1,)), ((), ())), preferred_element_type=F32)


def owner_of(pixels, owner_ref, rows, count):
    block = lax.div(pixels, jnp.int32(rows))
    owner = jnp.zeros_like(pixels)
    for slot in range(count):
        owner = jnp.where(block == slot, owner_ref[0, slot], owner)
    return owner


def earlier(rows):
    before = lax.broadcasted_iota(jnp.int32, (rows, rows), 0)
    after = lax.broadcasted_iota(jnp.int32, (rows, rows), 1)
    return jnp.where(before < after, 1.0, 0.0).astype(BF16)


def render_kernel(
    ray_count, me_ref, owner_ref, lists_ref, opacity_ref, counts_ref, pixels_ref, features_ref,
    *refs,
):
    out_ref, ids_ref, share_ref, table_ref, send_ref = refs[-5:]
    depth, rays = lists_ref.shape
    gauss = features_ref.shape[0]
    width = features_ref.shape[1]
    me = me_ref[0]
    ids_ref[...] = lists_ref[...] - me * gauss
    passing = jnp.ones((1, rays), F32)
    counts = counts_ref[...]
    for level in range(depth):
        alpha = opacity_ref[pl.ds(level, 1), :]
        share_ref[pl.ds(level, 1), :] = jnp.where(level < counts, alpha * passing, 0.0)
        passing = passing * (1.0 - alpha)

    tile = 128
    lanes = 128
    columns = rays // lanes

    @pl.loop(0, (gauss // tile) * columns)
    def _(step):
        first = pl.multiple_of(lax.div(step, columns) * tile, tile)
        lane = pl.multiple_of(lax.rem(step, columns) * lanes, lanes)
        number = lax.broadcasted_iota(jnp.int32, (tile, lanes), 0) + first
        total = jnp.zeros((tile, lanes), F32)
        for level in range(depth):
            ident = ids_ref[pl.ds(level, 1), pl.ds(lane, lanes)]
            share = share_ref[pl.ds(level, 1), pl.ds(lane, lanes)]
            total = total + jnp.where(ident == number, share, 0.0)
        table_ref[pl.ds(first, tile), pl.ds(lane, lanes)] = total.astype(BF16)

    mine = pixels_ref[pl.ds(me, 1), :]
    owner = owner_of(mine, owner_ref, rays, ray_count)
    padded = -(-ray_count // 16) * 16
    member = (lax.broadcasted_iota(jnp.int32, (padded, rays), 0) == owner)
    ranks = dot_nn(member.astype(F32).astype(BF16), earlier(rays))
    rank = jnp.sum(jnp.where(member, ranks, 0.0), axis=0, keepdims=True).astype(jnp.int32)
    slot = owner * (rays // ray_count) + rank
    send_ref[...] = (
        (lax.broadcasted_iota(jnp.int32, (rays, rays), 0) == slot).astype(F32).astype(BF16)
    )

    piece = 256

    @pl.loop(0, width // piece)
    def _(step):
        cols = pl.ds(pl.multiple_of(step * piece, piece), piece)
        rendered = dot_tn(table_ref[...], features_ref[:, cols]).astype(BF16)
        out_ref[:, cols] = dot_nn(send_ref[...], rendered).astype(BF16)


def render(me, owner, lists, opacity, counts, pixels, features, after=()):
    ray_count = pixels.shape[0]
    depth, rays = lists.shape
    gauss, width = features.shape
    return pl.pallas_call(
        functools.partial(render_kernel, ray_count),
        out_shape=jax.ShapeDtypeStruct((rays, width), BF16),
        in_specs=[SMEM, SMEM, VMEM, VMEM, VMEM, VMEM, VMEM] + [ANY] * len(after),
        out_specs=VMEM,
        scratch_shapes=[
            pltpu.VMEM((depth, rays), jnp.int32),
            pltpu.VMEM((depth, rays), F32),
            pltpu.VMEM((gauss, rays), BF16),
            pltpu.VMEM((rays, rays), BF16),
        ],
        compiler_params=params(),
        cost_estimate=COST,
        name="render",
    )(me, owner, lists, opacity, counts, pixels, features, *after)


def tokens_kernel(
    ray_count, me_ref, owner_ref, pixels_ref, tokens_ref, gain_ref,
    tokens_out, normed_out, normed_t_out, place_ref,
):
    rows, width = tokens_ref.shape
    me = me_ref[0]
    each = rows // ray_count
    pixels = pixels_ref[...]
    mine = owner_of(pixels, owner_ref, rows, ray_count) == me
    place = lax.rem(pixels, jnp.int32(rows)).astype(F32)
    member = jnp.where(mine, 1.0, 0.0)
    padded = -(-ray_count // 16) * 16
    if padded > ray_count:
        spread = jnp.concatenate([member, jnp.zeros((padded - ray_count, rows), F32)], axis=0)
    else:
        spread = member
    ranks = dot_nn(spread.astype(BF16), earlier(rows))
    for sender in range(ray_count):
        rank = jnp.where(mine[sender:sender + 1], ranks[sender:sender + 1], -1.0).astype(jnp.int32)
        hit = lax.broadcasted_iota(jnp.int32, (each, rows), 0) == rank
        at = jnp.sum(jnp.where(hit, place[sender:sender + 1], 0.0), axis=1, keepdims=True)
        here = lax.broadcasted_iota(jnp.int32, (each, rows), 1) == at.astype(jnp.int32)
        place_ref[pl.ds(sender * each, each), :] = here.astype(F32).astype(BF16)
    half = min(128, rows)
    gain = gain_ref[...]

    @pl.loop(0, rows // half)
    def _(step):
        span = pl.ds(pl.multiple_of(step * half, half), half)
        values = dot_nn(place_ref[span, :], tokens_ref[...])
        tokens_out[span, :] = values.astype(BF16)
        centered = values - jnp.mean(values, axis=-1, keepdims=True)
        variance = jnp.mean(centered * centered, axis=-1, keepdims=True)
        xhat = centered * lax.rsqrt(variance + STABILITY_EPSILON)
        normed = (xhat * gain).astype(BF16)
        normed_out[span, :] = normed
        normed_t_out[:, span] = normed.T


def prepare_tokens(me, owner, pixels, tokens, gain):
    ray_count = pixels.shape[0]
    rows, width = tokens.shape
    return pl.pallas_call(
        functools.partial(tokens_kernel, ray_count),
        out_shape=(
            jax.ShapeDtypeStruct((rows, width), BF16),
            jax.ShapeDtypeStruct((rows, width), BF16),
            jax.ShapeDtypeStruct((width, rows), BF16),
        ),
        in_specs=[SMEM, SMEM, VMEM, VMEM, VMEM],
        out_specs=(VMEM, VMEM, VMEM),
        scratch_shapes=[pltpu.VMEM((rows, rows), BF16)],
        compiler_params=params(),
        cost_estimate=COST,
        name="tokens",
    )(me, owner, pixels, tokens, gain)


def up_kernel(normed_ref, up_ref, act_ref, slope_ref):
    parts, _, part_rows, width = up_ref.shape
    up = up_ref[...].reshape(parts * part_rows, width)
    rows = normed_ref.shape[0]
    piece = min(128, rows)

    @pl.loop(0, rows // piece)
    def _(step):
        span = pl.ds(pl.multiple_of(step * piece, piece), piece)
        hidden = dot_nn(normed_ref[span, :], up)
        phi = 0.5 * (1.0 + lax.erf(hidden * (0.5 ** 0.5)))
        density = jnp.exp(-0.5 * hidden * hidden) * ((2.0 * jnp.pi) ** -0.5)
        act_ref[span, :] = (hidden * phi).astype(BF16)
        slope_ref[span, :] = (phi + hidden * density).astype(slope_ref.dtype)


def project_up(normed, up):
    rows, width = normed.shape
    parts, chunks, part_rows, chunk = up.shape
    return pl.pallas_call(
        up_kernel,
        grid=(chunks,),
        out_shape=(
            jax.ShapeDtypeStruct((rows, chunks * chunk), BF16),
            jax.ShapeDtypeStruct((rows, chunks * chunk), F32),
        ),
        in_specs=[
            pl.BlockSpec((rows, width), lambda j: (0, 0)),
            pl.BlockSpec((parts, 1, part_rows, chunk), lambda j: (0, j, 0, 0)),
        ],
        out_specs=(
            pl.BlockSpec((rows, chunk), lambda j: (0, j)),
            pl.BlockSpec((rows, chunk), lambda j: (0, j)),
        ),
        compiler_params=params(dimension_semantics=("arbitrary",)),
        cost_estimate=COST,
        name="up",
    )(normed, up)


def down_kernel(
    chunks, act_ref, down_ref, tokens_ref, target_ref, scale_ref,
    grad_ref, back_ref, small_ref, mixed_ref,
):
    step = pl.program_id(0)
    rows, width = tokens_ref.shape
    act = act_ref[...]

    @pl.when(step < chunks)
    def _():
        parts, _, part_rows, _ = down_ref.shape
        part = dot_nn(act, down_ref[...].reshape(parts * part_rows, width))

        @pl.when(step == 0)
        def _():
            mixed_ref[...] = part

        @pl.when(step > 0)
        def _():
            mixed_ref[...] += part

    @pl.when(step == chunks - 1)
    def _():
        scale = scale_ref[...]
        small_ref[...] = jnp.zeros_like(small_ref)
        piece = min(64, rows)

        @pl.loop(0, rows // piece)
        def _(index):
            span = pl.ds(pl.multiple_of(index * piece, piece), piece)
            mixed = mixed_ref[span, :]
            out = tokens_ref[span, :].astype(F32) + scale * mixed
            goal = target_ref[span, :].astype(F32)
            out_norm = jnp.sqrt(jnp.sum(out * out, axis=-1, keepdims=True) + STABILITY_EPSILON)
            goal_norm = jnp.sqrt(jnp.sum(goal * goal, axis=-1, keepdims=True) + STABILITY_EPSILON)
            norms = out_norm * goal_norm
            cosine = jnp.sum(out * goal, axis=-1, keepdims=True) / norms
            upstream = (cosine / (out_norm * out_norm)) * out - goal * (1.0 / norms)
            back_ref[span, :] = (upstream * scale).astype(BF16)
            small_ref[0:1, :] += jnp.sum(upstream * mixed, axis=0, keepdims=True)
            loss = jnp.sum(1.0 - cosine, axis=0, keepdims=True)
            small_ref[1:2, :] += jnp.broadcast_to(loss, (1, width))

    @pl.when(step >= chunks)
    def _():
        grad = dot_tn(act, back_ref[...])
        grad_ref[...] = grad.astype(BF16).reshape(grad_ref.shape)


def project_down(act, down, tokens, target, scale):
    rows, width = tokens.shape
    parts, chunks, part_rows, _ = down.shape
    chunk = parts * part_rows
    return pl.pallas_call(
        functools.partial(down_kernel, chunks),
        grid=(2 * chunks,),
        out_shape=(
            jax.ShapeDtypeStruct(down.shape, BF16),
            jax.ShapeDtypeStruct((rows, width), BF16),
            jax.ShapeDtypeStruct((8, width), F32),
        ),
        in_specs=[
            pl.BlockSpec((rows, chunk), lambda j: (0, lax.rem(j, chunks))),
            pl.BlockSpec(
                (parts, 1, part_rows, width), lambda j: (0, jnp.minimum(j, chunks - 1), 0, 0)
            ),
            pl.BlockSpec((rows, width), lambda j: (0, 0)),
            pl.BlockSpec((rows, width), lambda j: (0, 0)),
            pl.BlockSpec((1, width), lambda j: (0, 0)),
        ],
        out_specs=(
            pl.BlockSpec(
                (parts, 1, part_rows, width), lambda j: (0, jnp.maximum(j - chunks, 0), 0, 0)
            ),
            pl.BlockSpec((rows, width), lambda j: (0, 0)),
            pl.BlockSpec((8, width), lambda j: (0, 0)),
        ),
        scratch_shapes=[pltpu.VMEM((rows, width), F32)],
        compiler_params=params(dimension_semantics=("arbitrary",)),
        cost_estimate=COST,
        name="down",
    )(act, down, tokens, target, scale)


def back_kernel(back_ref, down_ref, slope_ref, normed_t_ref, up_ref, gain_ref, grad_ref, sum_ref):
    step = pl.program_id(0)
    parts, _, part_rows, width = down_ref.shape
    chunk = parts * part_rows
    rows = back_ref.shape[0]
    back_act = dot_nt(back_ref[...], down_ref[...].reshape(chunk, width))
    back_hidden = (back_act * slope_ref[...]).astype(BF16)
    up_parts, _, up_rows, _ = up_ref.shape

    @pl.when(step == 0)
    def _():
        sum_ref[...] = jnp.zeros_like(sum_ref)

    grad = dot_nn(normed_t_ref[...], back_hidden)
    grad_ref[...] = grad.astype(BF16).reshape(grad_ref.shape)
    up = up_ref[...].reshape(up_parts * up_rows, chunk).astype(F32)
    sum_ref[...] += jnp.sum(grad * up, axis=1, keepdims=True) / gain_ref[...]


def back_up(back, down, slope, normed_t, up, gain):
    width, rows = normed_t.shape
    parts, chunks, part_rows, _ = down.shape
    chunk = parts * part_rows
    up_parts, _, up_rows, _ = up.shape
    return pl.pallas_call(
        back_kernel,
        grid=(chunks,),
        out_shape=(
            jax.ShapeDtypeStruct(up.shape, BF16),
            jax.ShapeDtypeStruct((width, 1), F32),
        ),
        in_specs=[
            pl.BlockSpec((rows, width), lambda j: (0, 0)),
            pl.BlockSpec((parts, 1, part_rows, width), lambda j: (0, j, 0, 0)),
            pl.BlockSpec((rows, chunk), lambda j: (0, j)),
            pl.BlockSpec((width, rows), lambda j: (0, 0)),
            pl.BlockSpec((up_parts, 1, up_rows, chunk), lambda j: (0, j, 0, 0)),
            pl.BlockSpec((width, 1), lambda j: (0, 0)),
        ],
        out_specs=(
            pl.BlockSpec((up_parts, 1, up_rows, chunk), lambda j: (0, j, 0, 0)),
            pl.BlockSpec((width, 1), lambda j: (0, 0)),
        ),
        compiler_params=params(dimension_semantics=("arbitrary",)),
        cost_estimate=COST,
        name="back",
    )(back, down, slope, normed_t, up, gain)


def gather_weight(weight, parts, group, group_count, ray_count):
    rows, cols = weight.shape
    if parts == 1:
        whole = lax.all_gather(weight, "ray", axis=0, tiled=True)
    else:
        part = lax.dynamic_slice_in_dim(weight, group * (rows // parts), rows // parts, 0)
        whole = lax.all_gather(part, ("grp", "ray"), axis=0, tiled=True)
    return whole.reshape(parts, ray_count, rows // parts, cols)


def reduce_gradient(grad):
    parts, ray_count, part_rows, cols = grad.shape
    flat = grad.reshape(parts * ray_count * part_rows, cols)
    if parts == 1:
        share = lax.psum_scatter(flat, "ray", scatter_dimension=0, tiled=True)
        return lax.psum(share.astype(F32), "grp")
    share = lax.psum_scatter(flat, "grp", scatter_dimension=0, tiled=True)
    share = lax.psum_scatter(share, "ray", scatter_dimension=0, tiled=True)
    return lax.all_gather(share, "grp", axis=0, tiled=True).astype(F32)


def shards_general(
    image_tokens,
    tile_lists,
    opacity,
    tile_counts,
    ray_pixel,
    block_owner,
    gaussian_features,
    layer_norm_gain,
    layer_scale,
    up_weight,
    down_weight,
):
    ray_count = lax.axis_size("ray")
    group_count = lax.axis_size("grp")
    group = lax.axis_index("grp")
    me = lax.axis_index("ray").reshape(1)
    rows, width = image_tokens.shape
    up_parts = group_count if up_weight.shape[0] % (16 * group_count) == 0 else 1
    down_parts = group_count if down_weight.shape[0] % (16 * group_count) == 0 else 1
    up = gather_weight(up_weight, up_parts, group, group_count, ray_count)
    down = gather_weight(down_weight, down_parts, group, group_count, ray_count)
    pixels = ray_pixel[0].reshape(ray_count, rows)
    rendered = render(
        me, block_owner, tile_lists, opacity, tile_counts.reshape(1, rows), pixels,
        gaussian_features,
    )
    target = lax.all_to_all(rendered, "ray", split_axis=0, concat_axis=0, tiled=True)
    tokens, normed, normed_t = prepare_tokens(
        me, block_owner, pixels, image_tokens, layer_norm_gain.reshape(1, width)
    )
    act, slope = project_up(normed, up)
    grad_down, back, small = project_down(act, down, tokens, target, layer_scale.reshape(1, width))
    grad_up, gain_sum = back_up(back, down, slope, normed_t, up, layer_norm_gain.reshape(width, 1))
    grad_down = reduce_gradient(grad_down)
    grad_up = reduce_gradient(grad_up)
    sums = jnp.concatenate([gain_sum.reshape(1, width), small[:2]], axis=0)
    sums = lax.psum(sums, ("grp", "ray"))
    loss = sums[2, 0] / (rows * ray_count * group_count)
    return (grad_up, grad_down, sums[0], sums[1], loss)


def quarter_kernel(group_ref, up_ref, down_ref, out_ref, turned_ref):
    part = out_ref.shape[1]
    first = pl.multiple_of(group_ref[0] * part, part)
    turned_ref[...] = up_ref[...].T
    out_ref[0] = turned_ref[pl.ds(first, part), :]
    out_ref[1] = down_ref[pl.ds(first, part), :]


def own_quarter(group, up, down, part):
    width, chunk = up.shape
    return pl.pallas_call(
        quarter_kernel,
        out_shape=jax.ShapeDtypeStruct((2, part, width), BF16),
        in_specs=[SMEM, VMEM, VMEM],
        out_specs=VMEM,
        scratch_shapes=[pltpu.VMEM((chunk, width), BF16)],
        compiler_params=small_params(),
        cost_estimate=COST,
        name="quarter",
    )(group, up, down)


def finish_rows(tokens, mixed, goal, scale):
    out = tokens + scale * mixed
    out_norm = jnp.sqrt(jnp.sum(out * out, axis=-1, keepdims=True) + STABILITY_EPSILON)
    goal_norm = jnp.sqrt(jnp.sum(goal * goal, axis=-1, keepdims=True) + STABILITY_EPSILON)
    norms = out_norm * goal_norm
    cosine = jnp.sum(out * goal, axis=-1, keepdims=True) / norms
    upstream = (cosine / (out_norm * out_norm)) * out - goal * (1.0 / norms)
    return upstream, 1.0 - cosine


def forward_kernel(first, last, *refs):
    refs = list(refs)
    normed_t_ref, own_ref, other_ref = refs[:3]
    del refs[:3]
    mixed_in = None if first else refs.pop(0)
    if last:
        tokens_ref, target_ref, scale_ref = refs[:3]
        del refs[:3]
    act_ref, slope_ref = refs[:2]
    del refs[:2]
    count, _, part, width = own_ref.shape
    rows = normed_t_ref.shape[1]
    for side, ref in enumerate((own_ref, other_ref)):
        for index in range(count):
            hidden = dot_nn(ref[index, 0], normed_t_ref[...])
            phi = 0.5 * (1.0 + lax.erf(hidden * (0.5 ** 0.5)))
            density = jnp.exp(-0.5 * hidden * hidden) * ((2.0 * jnp.pi) ** -0.5)
            act_ref[side, index] = (hidden * phi).astype(BF16)
            slope_ref[side, index] = phi + hidden * density
    act = act_ref[...].reshape(2 * count * part, rows)
    down = jnp.concatenate(
        [own_ref[:, 1].reshape(count * part, width), other_ref[:, 1].reshape(count * part, width)],
        axis=0,
    )
    if not last:
        mixed_out = refs[0]
        part_sum = dot_tn(act, down)
        mixed_out[...] = part_sum if first else mixed_in[...] + part_sum
        return
    back_ref, back_t_ref, small_ref, mixed_ref = refs
    mixed_ref[...] = mixed_in[...] + dot_tn(act, down)
    scale = scale_ref[...]
    small_ref[...] = jnp.zeros_like(small_ref)
    piece = 128

    @pl.loop(0, rows // piece)
    def _(index):
        span = pl.ds(pl.multiple_of(index * piece, piece), piece)
        mixed = mixed_ref[span, :]
        upstream, loss = finish_rows(
            tokens_ref[span, :].astype(F32), mixed, target_ref[span, :].astype(F32), scale
        )
        back = (upstream * scale).astype(BF16)
        back_ref[span, :] = back
        back_t_ref[:, span] = back.T
        small_ref[0:1, :] += jnp.sum(upstream * mixed, axis=0, keepdims=True)
        small_ref[1:2, :] += jnp.broadcast_to(jnp.sum(loss, axis=0, keepdims=True), (1, width))


def forward(normed_t, own, other, mixed=None, finish=None):
    width, rows = normed_t.shape
    count, _, part, _ = own.shape
    first, last = mixed is None, finish is not None
    operands = [normed_t, own, other]
    if not first:
        operands.append(mixed)
    if last:
        operands.extend(finish)
    piece = (2, count, part, rows)
    shapes = [jax.ShapeDtypeStruct(piece, BF16), jax.ShapeDtypeStruct(piece, F32)]
    scratch = []
    if last:
        shapes += [
            jax.ShapeDtypeStruct((rows, width), BF16),
            jax.ShapeDtypeStruct((width, rows), BF16),
            jax.ShapeDtypeStruct((8, width), F32),
        ]
        scratch = [pltpu.VMEM((rows, width), F32)]
    else:
        shapes += [jax.ShapeDtypeStruct((rows, width), F32)]
    return pl.pallas_call(
        functools.partial(forward_kernel, first, last),
        out_shape=tuple(shapes),
        in_specs=[VMEM] * len(operands),
        out_specs=tuple([VMEM] * len(shapes)),
        scratch_shapes=scratch,
        compiler_params=small_params(),
        cost_estimate=COST,
        name="forward",
    )(*operands)


def backward_kernel(side, quarter, add, *refs):
    refs = list(refs)
    back_ref, back_t_ref, normed_ref, near_ref, far_ref = refs[:5]
    act_near, slope_near, act_far, slope_far, gain_in = refs[5:10]
    del refs[:10]
    arrived = refs.pop(0) if add else None
    up_ref, down_ref, gain_ref = refs
    part, width = near_ref.shape[-2:]
    far = far_ref.shape[0]
    chunk = (far + 1) * part
    rows = back_ref.shape[0]

    def joined(near, other):
        return jnp.concatenate([near, other.reshape(far * part, other.shape[-1])], axis=0)

    slope = joined(slope_near[side, quarter], slope_far[side])
    back_act = dot_nn(joined(near_ref[quarter, 1], far_ref[:, 1]), back_t_ref[...])
    back_hidden = (back_act * slope).astype(BF16)
    grad_up = dot_nn(back_hidden, normed_ref[...])
    up = joined(near_ref[quarter, 0], far_ref[:, 0]).astype(F32)
    gain_ref[...] = gain_in[...] + jnp.sum(grad_up * up, axis=0, keepdims=True)
    grad_down = dot_nn(joined(act_near[side, quarter], act_far[side]), back_ref[...])
    if add:
        grad_up += arrived[0].reshape(chunk, width).astype(F32)
        grad_down += arrived[1].reshape(chunk, width).astype(F32)
    up_ref[...] = grad_up.astype(BF16).reshape(up_ref.shape)
    down_ref[...] = grad_down.astype(BF16).reshape(down_ref.shape)


def backward(
    side, quarter, common, near, far, act_near, slope_near, act_far, slope_far, gain, arrived
):
    back, back_t, normed = common
    rows, width = back.shape
    part = near.shape[2]
    count = far.shape[0] + 1
    operands = [back, back_t, normed, near, far, act_near, slope_near, act_far, slope_far, gain]
    if arrived is None:
        def body(*refs):
            grads, gain_ref = refs[-2:]
            backward_kernel(
                side, quarter, False, *refs[:-2], grads.at[0], grads.at[1], gain_ref
            )

        shapes = [jax.ShapeDtypeStruct((2, count, part, width), BF16)]
    else:
        operands.append(arrived)
        body = functools.partial(backward_kernel, side, quarter, True)
        shapes = [jax.ShapeDtypeStruct((count, part, width), BF16)] * 2
    shapes.append(jax.ShapeDtypeStruct((1, width), F32))
    return pl.pallas_call(
        body,
        out_shape=tuple(shapes),
        in_specs=[VMEM] * len(operands),
        out_specs=tuple([VMEM] * len(shapes)),
        compiler_params=small_params(),
        cost_estimate=COST,
        name="backward",
    )(*operands)


def total_kernel(count, *refs):
    ins, outs = refs[:4], refs[-count:]
    for index, out in enumerate(outs):
        total = ins[0][index].astype(F32)
        for ref in ins[1:]:
            total = total + ref[index].astype(F32)
        out[...] = total.astype(BF16)
    if len(refs) > 4 + count:
        refs[5][...] = refs[4][...]


def totals(parts, vector=None):
    count, part, width = parts[0].shape
    operands, shapes = list(parts), []
    if vector is not None:
        operands.append(vector)
        shapes.append(jax.ShapeDtypeStruct(vector.shape, F32))
    shapes += [jax.ShapeDtypeStruct((part, width), BF16)] * count
    return pl.pallas_call(
        functools.partial(total_kernel, count),
        out_shape=tuple(shapes),
        in_specs=[VMEM] * len(operands),
        out_specs=tuple([VMEM] * len(shapes)),
        compiler_params=small_params(),
        cost_estimate=COST,
        name="totals",
    )(*operands)


def collect_kernel(count, *refs):
    out_ref = refs[-1]
    part, width = refs[0].shape
    total = refs[0][...].astype(F32)
    for ref in refs[1:count]:
        total = total + ref[...].astype(F32)
    out_ref[pl.ds(0, part), :] = total.astype(BF16)
    if len(refs) > count + 1:
        rest = refs[count][...]
        pieces = []
        for _ in range(3):
            piece = rest.astype(BF16).astype(F32)
            pieces.append(piece)
            rest = rest - piece
        pieces.append(jnp.zeros_like(rest))
        out_ref[pl.ds(part, 32), :] = jnp.concatenate(pieces, axis=0).astype(BF16)


def collect(parts, vector=None):
    part, width = parts[0].shape
    operands = list(parts) + ([] if vector is None else [vector])
    return pl.pallas_call(
        functools.partial(collect_kernel, len(parts)),
        out_shape=jax.ShapeDtypeStruct((part + (0 if vector is None else 32), width), BF16),
        in_specs=[VMEM] * len(operands),
        out_specs=VMEM,
        compiler_params=small_params(),
        cost_estimate=COST,
        name="collect",
    )(*operands)


def place_kernel(part, group_ref, a_ref, b_ref, c_ref, d_ref, *refs):
    group = group_ref[0]
    held_ref = refs[-1]
    quarters = (a_ref, b_ref, c_ref, d_ref)
    for index, ref in enumerate(quarters):
        first = pl.multiple_of(jnp.bitwise_xor(group, index) * part, part)
        held_ref[pl.ds(first, part), :] = ref[pl.ds(0, part), :].astype(F32)
    if len(refs) == 2:
        refs[0][...] = held_ref[...]
        return
    refs[0][...] = held_ref[...].T
    vectors = []
    for ref in quarters:
        rows = ref[pl.ds(part, 32), :].astype(F32)
        vectors.append((rows[0:8] + rows[8:16]) + rows[16:24])
    refs[1][...] = (vectors[0] + vectors[1]) + (vectors[2] + vectors[3])


def place_quarters(group, quarters, part, vector):
    width = quarters[0].shape[1]
    if vector:
        shapes = [
            jax.ShapeDtypeStruct((width, 4 * part), F32), jax.ShapeDtypeStruct((8, width), F32)
        ]
    else:
        shapes = [jax.ShapeDtypeStruct((4 * part, width), F32)]
    return pl.pallas_call(
        functools.partial(place_kernel, part),
        out_shape=tuple(shapes),
        in_specs=[SMEM] + [VMEM] * 4,
        out_specs=tuple([VMEM] * len(shapes)),
        scratch_shapes=[pltpu.VMEM((4 * part, width), F32)],
        compiler_params=small_params(),
        cost_estimate=COST,
        name="place",
    )(group, *quarters)


def shards_square(
    image_tokens,
    tile_lists,
    opacity,
    tile_counts,
    ray_pixel,
    block_owner,
    gaussian_features,
    layer_norm_gain,
    layer_scale,
    up_weight,
    down_weight,
):
    ray_count = lax.axis_size("ray")
    group_count = lax.axis_size("grp")
    depth = ray_count // 2
    group = lax.axis_index("grp").reshape(1)
    me = lax.axis_index("ray").reshape(1)
    rows, width = image_tokens.shape
    part = down_weight.shape[0] // group_count

    def beside(array, flip):
        return lax.ppermute(array, "grp", [(g, g ^ flip) for g in range(group_count)])

    def partner(array, flip=1):
        return lax.ppermute(array, "ray", [(r, r ^ flip) for r in range(ray_count)])

    def along(array, shift):
        pairs = [(r, (r + 2 * shift) % ray_count) for r in range(ray_count)]
        return lax.ppermute(array, "ray", pairs)

    mine = own_quarter(group, up_weight, down_weight, part)
    far = [along(mine, -shift) for shift in range(1, depth)]
    near = jnp.stack([mine] + [beside(mine, flip) for flip in (1, 2, 3)])
    near_other = partner(near)
    far = jnp.stack(far)
    far = [far] + [beside(far, flip) for flip in (1, 2, 3)]
    far_other = [partner(array) for array in far]

    pixels = ray_pixel[0].reshape(ray_count, rows)
    rendered = render(
        me, block_owner, tile_lists, opacity, tile_counts.reshape(1, rows), pixels,
        gaussian_features, (far[0],),
    )
    target = lax.all_to_all(rendered, "ray", split_axis=0, concat_axis=0, tiled=True)
    tokens, normed, normed_t = prepare_tokens(
        me, block_owner, pixels, image_tokens, layer_norm_gain.reshape(1, width)
    )
    act_near, slope_near, mixed = forward(normed_t, near, near_other)
    act_far, slope_far = [None] * 4, [None] * 4
    for quarter in (0, 1, 2):
        act_far[quarter], slope_far[quarter], mixed = forward(
            normed_t, far[quarter], far_other[quarter], mixed
        )
    act_far[3], slope_far[3], back, back_t, small = forward(
        normed_t, far[3], far_other[3], mixed, (tokens, target, layer_scale.reshape(1, width))
    )
    common = (back, back_t, normed)

    def grads(side, quarter, gain, arrived):
        weights = (near, far) if side == 0 else (near_other, far_other)
        return backward(
            side, quarter, common, weights[0], weights[1][quarter], act_near, slope_near,
            act_far[quarter], slope_far[quarter], gain, arrived,
        )

    gain = jnp.zeros((1, width), F32)
    arrived, sums, sent = {}, {}, {}
    for side, quarter in ((1, 3), (1, 1), (0, 3), (1, 2), (0, 1), (1, 0), (0, 2), (0, 0)):
        if side == 1:
            out, gain = grads(1, quarter, gain, None)
            arrived[quarter] = partner(out)
        else:
            grad_up, grad_down, gain = grads(0, quarter, gain, arrived[quarter])
            sums[quarter] = (grad_up, grad_down)
            if quarter:
                sent[quarter] = (beside(grad_up, quarter), beside(grad_down, quarter))
    vector = jnp.concatenate(
        [gain / layer_norm_gain.reshape(1, width), small[:2], jnp.zeros((5, width), F32)], axis=0
    )
    vector, *shares = totals([sums[0][1]] + [sent[quarter][1] for quarter in (1, 2, 3)], vector)

    def sum_along(shares, *vector):
        arrivals = [along(shares[shift], shift) for shift in range(1, depth)]
        total = collect([shares[0]] + arrivals, *vector)
        return [total] + [beside(total, flip) for flip in (1, 2, 3)]

    quarters = sum_along(shares)
    (grad_down,) = place_quarters(group, quarters, part, False)
    vector = vector + partner(vector)
    flip = 2
    while flip < ray_count:
        vector = vector + partner(vector, flip)
        flip *= 2
    shares = totals([sums[0][0]] + [sent[quarter][0] for quarter in (1, 2, 3)])
    quarters = sum_along(shares, vector)
    grad_up, vector = place_quarters(group, quarters, part, True)
    loss = vector[2, 0] / (rows * ray_count * group_count)
    return (grad_up, grad_down, vector[0], vector[1], loss)


def shards(*operands):
    ray_count, group_count = lax.axis_size("ray"), lax.axis_size("grp")
    hidden = operands[-1].shape[0]
    square = group_count == 4 and ray_count in (4, 8, 16) and hidden % (16 * group_count) == 0
    return (shards_square if square else shards_general)(*operands)


def solution(mesh):
    return jax.shard_map(
        shards,
        mesh=mesh,
        in_specs=(
            P(("grp", "ray"), None),
            P(None, ("grp", "ray")),
            P(None, ("grp", "ray")),
            P(("grp", "ray")),
            P("grp", None),
            P("grp", None),
            P(("grp", "ray"), None),
            P(),
            P(),
            P(None, "ray"),
            P("ray", None),
        ),
        out_specs=(P(None, "ray"), P("ray", None), P(), P(), P()),
        check_vma=False,
    )
```

```python
import functools

import jax
import jax.numpy as jnp
from jax import lax
from jax.experimental import pallas as pl
from jax.experimental.pallas import tpu as pltpu
from jax.sharding import PartitionSpec as P

STABILITY_EPSILON = 1e-06
F32 = jnp.float32
BF16 = jnp.bfloat16
MIB = 1024 * 1024
COST = pl.CostEstimate(flops=1 << 20, bytes_accessed=1 << 16, transcendentals=0)
SMEM = pl.BlockSpec(memory_space=pltpu.SMEM)
VMEM = pl.BlockSpec(memory_space=pltpu.VMEM)
ANY = pl.BlockSpec(memory_space=pl.ANY)


def params(mib=48, **more):
    return pltpu.CompilerParams(vmem_limit_bytes=mib * MIB, **more)


def dot_nn(a, b):
    return lax.dot_general(a, b, (((1,), (0,)), ((), ())), preferred_element_type=F32)


def dot_tn(a, b):
    return lax.dot_general(a, b, (((0,), (0,)), ((), ())), preferred_element_type=F32)


def dot_nt(a, b):
    return lax.dot_general(a, b, (((1,), (1,)), ((), ())), preferred_element_type=F32)


def owner_of(pixels, owner_ref, rows, count):
    block = lax.div(pixels, jnp.int32(rows))
    owner = jnp.zeros_like(pixels)
    for slot in range(count):
        owner = jnp.where(block == slot, owner_ref[0, slot], owner)
    return owner


def earlier(rows):
    before = lax.broadcasted_iota(jnp.int32, (rows, rows), 0)
    after = lax.broadcasted_iota(jnp.int32, (rows, rows), 1)
    return jnp.where(before < after, 1.0, 0.0).astype(BF16)


def render_kernel(
    ray_count, me_ref, owner_ref, lists_ref, opacity_ref, counts_ref, pixels_ref, features_ref,
    *refs,
):
    out_ref, ids_ref, share_ref, table_ref, send_ref = refs[-5:]
    depth, rays = lists_ref.shape
    gauss = features_ref.shape[0]
    width = features_ref.shape[1]
    me = me_ref[0]
    ids_ref[...] = lists_ref[...] - me * gauss
    passing = jnp.ones((1, rays), F32)
    counts = counts_ref[...]
    for level in range(depth):
        alpha = opacity_ref[pl.ds(level, 1), :]
        share_ref[pl.ds(level, 1), :] = jnp.where(level < counts, alpha * passing, 0.0)
        passing = passing * (1.0 - alpha)

    tile = 128
    lanes = 128
    columns = rays // lanes

    @pl.loop(0, (gauss // tile) * columns)
    def _(step):
        first = pl.multiple_of(lax.div(step, columns) * tile, tile)
        lane = pl.multiple_of(lax.rem(step, columns) * lanes, lanes)
        number = lax.broadcasted_iota(jnp.int32, (tile, lanes), 0) + first
        total = jnp.zeros((tile, lanes), F32)
        for level in range(depth):
            ident = ids_ref[pl.ds(level, 1), pl.ds(lane, lanes)]
            share = share_ref[pl.ds(level, 1), pl.ds(lane, lanes)]
            total = total + jnp.where(ident == number, share, 0.0)
        table_ref[pl.ds(first, tile), pl.ds(lane, lanes)] = total.astype(BF16)

    mine = pixels_ref[pl.ds(me, 1), :]
    owner = owner_of(mine, owner_ref, rays, ray_count)
    padded = -(-ray_count // 16) * 16
    member = (lax.broadcasted_iota(jnp.int32, (padded, rays), 0) == owner)
    ranks = dot_nn(member.astype(F32).astype(BF16), earlier(rays))
    rank = jnp.sum(jnp.where(member, ranks, 0.0), axis=0, keepdims=True).astype(jnp.int32)
    slot = owner * (rays // ray_count) + rank
    send_ref[...] = (
        (lax.broadcasted_iota(jnp.int32, (rays, rays), 0) == slot).astype(F32).astype(BF16)
    )

    piece = 256

    @pl.loop(0, width // piece)
    def _(step):
        cols = pl.ds(pl.multiple_of(step * piece, piece), piece)
        rendered = dot_tn(table_ref[...], features_ref[:, cols]).astype(BF16)
        out_ref[:, cols] = dot_nn(send_ref[...], rendered).astype(BF16)


def render(me, owner, lists, opacity, counts, pixels, features, after=()):
    ray_count = pixels.shape[0]
    depth, rays = lists.shape
    gauss, width = features.shape
    return pl.pallas_call(
        functools.partial(render_kernel, ray_count),
        out_shape=jax.ShapeDtypeStruct((rays, width), BF16),
        in_specs=[SMEM, SMEM, VMEM, VMEM, VMEM, VMEM, VMEM] + [ANY] * len(after),
        out_specs=VMEM,
        scratch_shapes=[
            pltpu.VMEM((depth, rays), jnp.int32),
            pltpu.VMEM((depth, rays), F32),
            pltpu.VMEM((gauss, rays), BF16),
            pltpu.VMEM((rays, rays), BF16),
        ],
        compiler_params=params(20),
        cost_estimate=COST,
        name="render",
    )(me, owner, lists, opacity, counts, pixels, features, *after)


def tokens_kernel(
    ray_count, me_ref, owner_ref, pixels_ref, tokens_ref, gain_ref,
    tokens_out, normed_out, normed_t_out, place_ref,
):
    rows, width = tokens_ref.shape
    me = me_ref[0]
    each = rows // ray_count
    pixels = pixels_ref[...]
    mine = owner_of(pixels, owner_ref, rows, ray_count) == me
    place = lax.rem(pixels, jnp.int32(rows)).astype(F32)
    member = jnp.where(mine, 1.0, 0.0)
    padded = -(-ray_count // 16) * 16
    if padded > ray_count:
        spread = jnp.concatenate([member, jnp.zeros((padded - ray_count, rows), F32)], axis=0)
    else:
        spread = member
    ranks = dot_nn(spread.astype(BF16), earlier(rows))
    for sender in range(ray_count):
        rank = jnp.where(mine[sender:sender + 1], ranks[sender:sender + 1], -1.0).astype(jnp.int32)
        hit = lax.broadcasted_iota(jnp.int32, (each, rows), 0) == rank
        at = jnp.sum(jnp.where(hit, place[sender:sender + 1], 0.0), axis=1, keepdims=True)
        here = lax.broadcasted_iota(jnp.int32, (each, rows), 1) == at.astype(jnp.int32)
        place_ref[pl.ds(sender * each, each), :] = here.astype(F32).astype(BF16)
    half = min(128, rows)
    gain = gain_ref[...]

    @pl.loop(0, rows // half)
    def _(step):
        span = pl.ds(pl.multiple_of(step * half, half), half)
        values = dot_nn(place_ref[span, :], tokens_ref[...])
        tokens_out[span, :] = values.astype(BF16)
        centered = values - jnp.mean(values, axis=-1, keepdims=True)
        variance = jnp.mean(centered * centered, axis=-1, keepdims=True)
        xhat = centered * lax.rsqrt(variance + STABILITY_EPSILON)
        normed = (xhat * gain).astype(BF16)
        normed_out[span, :] = normed
        normed_t_out[:, span] = normed.T


def prepare_tokens(me, owner, pixels, tokens, gain):
    ray_count = pixels.shape[0]
    rows, width = tokens.shape
    return pl.pallas_call(
        functools.partial(tokens_kernel, ray_count),
        out_shape=(
            jax.ShapeDtypeStruct((rows, width), BF16),
            jax.ShapeDtypeStruct((rows, width), BF16),
            jax.ShapeDtypeStruct((width, rows), BF16),
        ),
        in_specs=[SMEM, SMEM, VMEM, VMEM, VMEM],
        out_specs=(VMEM, VMEM, VMEM),
        scratch_shapes=[pltpu.VMEM((rows, rows), BF16)],
        compiler_params=params(20),
        cost_estimate=COST,
        name="tokens",
    )(me, owner, pixels, tokens, gain)


def up_kernel(normed_ref, up_ref, act_ref, slope_ref):
    parts, _, part_rows, width = up_ref.shape
    up = up_ref[...].reshape(parts * part_rows, width)
    rows = normed_ref.shape[0]
    piece = min(128, rows)

    @pl.loop(0, rows // piece)
    def _(step):
        span = pl.ds(pl.multiple_of(step * piece, piece), piece)
        hidden = dot_nn(normed_ref[span, :], up)
        phi = 0.5 * (1.0 + lax.erf(hidden * (0.5 ** 0.5)))
        density = jnp.exp(-0.5 * hidden * hidden) * ((2.0 * jnp.pi) ** -0.5)
        act_ref[span, :] = (hidden * phi).astype(BF16)
        slope_ref[span, :] = (phi + hidden * density).astype(slope_ref.dtype)


def project_up(normed, up):
    rows, width = normed.shape
    parts, chunks, part_rows, chunk = up.shape
    return pl.pallas_call(
        up_kernel,
        grid=(chunks,),
        out_shape=(
            jax.ShapeDtypeStruct((rows, chunks * chunk), BF16),
            jax.ShapeDtypeStruct((rows, chunks * chunk), F32),
        ),
        in_specs=[
            pl.BlockSpec((rows, width), lambda j: (0, 0)),
            pl.BlockSpec((parts, 1, part_rows, chunk), lambda j: (0, j, 0, 0)),
        ],
        out_specs=(
            pl.BlockSpec((rows, chunk), lambda j: (0, j)),
            pl.BlockSpec((rows, chunk), lambda j: (0, j)),
        ),
        compiler_params=params(dimension_semantics=("arbitrary",)),
        cost_estimate=COST,
        name="up",
    )(normed, up)


def down_kernel(
    chunks, act_ref, down_ref, tokens_ref, target_ref, scale_ref,
    grad_ref, back_ref, small_ref, mixed_ref,
):
    step = pl.program_id(0)
    rows, width = tokens_ref.shape
    act = act_ref[...]

    @pl.when(step < chunks)
    def _():
        parts, _, part_rows, _ = down_ref.shape
        part = dot_nn(act, down_ref[...].reshape(parts * part_rows, width))

        @pl.when(step == 0)
        def _():
            mixed_ref[...] = part

        @pl.when(step > 0)
        def _():
            mixed_ref[...] += part

    @pl.when(step == chunks - 1)
    def _():
        scale = scale_ref[...]
        small_ref[...] = jnp.zeros_like(small_ref)
        piece = min(64, rows)

        @pl.loop(0, rows // piece)
        def _(index):
            span = pl.ds(pl.multiple_of(index * piece, piece), piece)
            mixed = mixed_ref[span, :]
            out = tokens_ref[span, :].astype(F32) + scale * mixed
            goal = target_ref[span, :].astype(F32)
            out_norm = jnp.sqrt(jnp.sum(out * out, axis=-1, keepdims=True) + STABILITY_EPSILON)
            goal_norm = jnp.sqrt(jnp.sum(goal * goal, axis=-1, keepdims=True) + STABILITY_EPSILON)
            norms = out_norm * goal_norm
            cosine = jnp.sum(out * goal, axis=-1, keepdims=True) / norms
            upstream = (cosine / (out_norm * out_norm)) * out - goal * (1.0 / norms)
            back_ref[span, :] = (upstream * scale).astype(BF16)
            small_ref[0:1, :] += jnp.sum(upstream * mixed, axis=0, keepdims=True)
            loss = jnp.sum(1.0 - cosine, axis=0, keepdims=True)
            small_ref[1:2, :] += jnp.broadcast_to(loss, (1, width))

    @pl.when(step >= chunks)
    def _():
        grad = dot_tn(act, back_ref[...])
        grad_ref[...] = grad.astype(BF16).reshape(grad_ref.shape)


def project_down(act, down, tokens, target, scale):
    rows, width = tokens.shape
    parts, chunks, part_rows, _ = down.shape
    chunk = parts * part_rows
    return pl.pallas_call(
        functools.partial(down_kernel, chunks),
        grid=(2 * chunks,),
        out_shape=(
            jax.ShapeDtypeStruct(down.shape, BF16),
            jax.ShapeDtypeStruct((rows, width), BF16),
            jax.ShapeDtypeStruct((8, width), F32),
        ),
        in_specs=[
            pl.BlockSpec((rows, chunk), lambda j: (0, lax.rem(j, chunks))),
            pl.BlockSpec(
                (parts, 1, part_rows, width), lambda j: (0, jnp.minimum(j, chunks - 1), 0, 0)
            ),
            pl.BlockSpec((rows, width), lambda j: (0, 0)),
            pl.BlockSpec((rows, width), lambda j: (0, 0)),
            pl.BlockSpec((1, width), lambda j: (0, 0)),
        ],
        out_specs=(
            pl.BlockSpec(
                (parts, 1, part_rows, width), lambda j: (0, jnp.maximum(j - chunks, 0), 0, 0)
            ),
            pl.BlockSpec((rows, width), lambda j: (0, 0)),
            pl.BlockSpec((8, width), lambda j: (0, 0)),
        ),
        scratch_shapes=[pltpu.VMEM((rows, width), F32)],
        compiler_params=params(dimension_semantics=("arbitrary",)),
        cost_estimate=COST,
        name="down",
    )(act, down, tokens, target, scale)


def back_kernel(back_ref, down_ref, slope_ref, normed_t_ref, up_ref, gain_ref, grad_ref, sum_ref):
    step = pl.program_id(0)
    parts, _, part_rows, width = down_ref.shape
    chunk = parts * part_rows
    rows = back_ref.shape[0]
    back_act = dot_nt(back_ref[...], down_ref[...].reshape(chunk, width))
    back_hidden = (back_act * slope_ref[...]).astype(BF16)
    up_parts, _, up_rows, _ = up_ref.shape

    @pl.when(step == 0)
    def _():
        sum_ref[...] = jnp.zeros_like(sum_ref)

    grad = dot_nn(normed_t_ref[...], back_hidden)
    grad_ref[...] = grad.astype(BF16).reshape(grad_ref.shape)
    up = up_ref[...].reshape(up_parts * up_rows, chunk).astype(F32)
    sum_ref[...] += jnp.sum(grad * up, axis=1, keepdims=True) / gain_ref[...]


def back_up(back, down, slope, normed_t, up, gain):
    width, rows = normed_t.shape
    parts, chunks, part_rows, _ = down.shape
    chunk = parts * part_rows
    up_parts, _, up_rows, _ = up.shape
    return pl.pallas_call(
        back_kernel,
        grid=(chunks,),
        out_shape=(
            jax.ShapeDtypeStruct(up.shape, BF16),
            jax.ShapeDtypeStruct((width, 1), F32),
        ),
        in_specs=[
            pl.BlockSpec((rows, width), lambda j: (0, 0)),
            pl.BlockSpec((parts, 1, part_rows, width), lambda j: (0, j, 0, 0)),
            pl.BlockSpec((rows, chunk), lambda j: (0, j)),
            pl.BlockSpec((width, rows), lambda j: (0, 0)),
            pl.BlockSpec((up_parts, 1, up_rows, chunk), lambda j: (0, j, 0, 0)),
            pl.BlockSpec((width, 1), lambda j: (0, 0)),
        ],
        out_specs=(
            pl.BlockSpec((up_parts, 1, up_rows, chunk), lambda j: (0, j, 0, 0)),
            pl.BlockSpec((width, 1), lambda j: (0, 0)),
        ),
        compiler_params=params(dimension_semantics=("arbitrary",)),
        cost_estimate=COST,
        name="back",
    )(back, down, slope, normed_t, up, gain)


def gather_weight(weight, parts, group, group_count, ray_count):
    rows, cols = weight.shape
    if parts == 1:
        whole = lax.all_gather(weight, "ray", axis=0, tiled=True)
    else:
        part = lax.dynamic_slice_in_dim(weight, group * (rows // parts), rows // parts, 0)
        whole = lax.all_gather(part, ("grp", "ray"), axis=0, tiled=True)
    return whole.reshape(parts, ray_count, rows // parts, cols)


def reduce_gradient(grad):
    parts, ray_count, part_rows, cols = grad.shape
    flat = grad.reshape(parts * ray_count * part_rows, cols)
    if parts == 1:
        share = lax.psum_scatter(flat, "ray", scatter_dimension=0, tiled=True)
        return lax.psum(share.astype(F32), "grp")
    share = lax.psum_scatter(flat, "grp", scatter_dimension=0, tiled=True)
    share = lax.psum_scatter(share, "ray", scatter_dimension=0, tiled=True)
    return lax.all_gather(share, "grp", axis=0, tiled=True).astype(F32)


def shards_general(
    image_tokens,
    tile_lists,
    opacity,
    tile_counts,
    ray_pixel,
    block_owner,
    gaussian_features,
    layer_norm_gain,
    layer_scale,
    up_weight,
    down_weight,
):
    ray_count = lax.axis_size("ray")
    group_count = lax.axis_size("grp")
    group = lax.axis_index("grp")
    me = lax.axis_index("ray").reshape(1)
    rows, width = image_tokens.shape
    up_parts = group_count if up_weight.shape[0] % (16 * group_count) == 0 else 1
    down_parts = group_count if down_weight.shape[0] % (16 * group_count) == 0 else 1
    up = gather_weight(up_weight, up_parts, group, group_count, ray_count)
    down = gather_weight(down_weight, down_parts, group, group_count, ray_count)
    pixels = ray_pixel[0].reshape(ray_count, rows)
    rendered = render(
        me, block_owner, tile_lists, opacity, tile_counts.reshape(1, rows), pixels,
        gaussian_features,
    )
    target = lax.all_to_all(rendered, "ray", split_axis=0, concat_axis=0, tiled=True)
    tokens, normed, normed_t = prepare_tokens(
        me, block_owner, pixels, image_tokens, layer_norm_gain.reshape(1, width)
    )
    act, slope = project_up(normed, up)
    grad_down, back, small = project_down(act, down, tokens, target, layer_scale.reshape(1, width))
    grad_up, gain_sum = back_up(back, down, slope, normed_t, up, layer_norm_gain.reshape(width, 1))
    grad_down = reduce_gradient(grad_down)
    grad_up = reduce_gradient(grad_up)
    sums = jnp.concatenate([gain_sum.reshape(1, width), small[:2]], axis=0)
    sums = lax.psum(sums, ("grp", "ray"))
    loss = sums[2, 0] / (rows * ray_count * group_count)
    return (grad_up, grad_down, sums[0], sums[1], loss)


def quarter_kernel(group_ref, up_ref, down_ref, out_ref, turned_ref):
    part = out_ref.shape[1]
    first = pl.multiple_of(group_ref[0] * part, part)
    turned_ref[...] = up_ref[...].T
    out_ref[0] = turned_ref[pl.ds(first, part), :]
    out_ref[1] = down_ref[pl.ds(first, part), :]


def own_quarter(group, up, down, part):
    width, chunk = up.shape
    return pl.pallas_call(
        quarter_kernel,
        out_shape=jax.ShapeDtypeStruct((2, part, width), BF16),
        in_specs=[SMEM, VMEM, VMEM],
        out_specs=VMEM,
        scratch_shapes=[pltpu.VMEM((chunk, width), BF16)],
        compiler_params=params(16),
        cost_estimate=COST,
        name="quarter",
    )(group, up, down)


def finish_rows(tokens, mixed, goal, scale):
    out = tokens + scale * mixed
    out_norm = jnp.sqrt(jnp.sum(out * out, axis=-1, keepdims=True) + STABILITY_EPSILON)
    goal_norm = jnp.sqrt(jnp.sum(goal * goal, axis=-1, keepdims=True) + STABILITY_EPSILON)
    norms = out_norm * goal_norm
    cosine = jnp.sum(out * goal, axis=-1, keepdims=True) / norms
    upstream = (cosine / (out_norm * out_norm)) * out - goal * (1.0 / norms)
    return upstream, 1.0 - cosine


def forward_kernel(first, last, sides, *refs):
    refs = list(refs)
    normed_t_ref = refs.pop(0)
    own, other = refs[:sides], refs[sides:2 * sides]
    del refs[:2 * sides]
    mixed_in = None if first else refs.pop(0)
    if last:
        tokens_ref, target_ref, scale_ref = refs[:3]
        del refs[:3]
    act_ref, slope_ref = refs[:2]
    del refs[:2]
    width, rows = normed_t_ref.shape
    total = act_ref.shape[1]
    part = act_ref.shape[2]
    downs = []
    for side, group in enumerate((own, other)):
        start = 0
        for ref in group:
            count = ref.shape[0]
            hiddens = dot_nn(ref[:, 0].reshape(count * part, width), normed_t_ref[...])
            for index in range(count):
                hidden = hiddens[index * part:(index + 1) * part]
                phi = 0.5 * (1.0 + lax.erf(hidden * (0.5 ** 0.5)))
                density = jnp.exp(-0.5 * hidden * hidden) * ((2.0 * jnp.pi) ** -0.5)
                act_ref[side, start + index] = (hidden * phi).astype(BF16)
                slope_ref[side, start + index] = phi + hidden * density
            downs.append(ref[:, 1].reshape(count * part, width))
            start += count
    act = act_ref[...].reshape(2 * total * part, rows)
    down = jnp.concatenate(downs, axis=0)
    if not last:
        mixed_out = refs[0]
        part_sum = dot_tn(act, down)
        mixed_out[...] = part_sum if first else mixed_in[...] + part_sum
        return
    back_ref, back_t_ref, small_ref, mixed_ref = refs
    mixed_ref[...] = mixed_in[...] + dot_tn(act, down)
    scale = scale_ref[...]
    small_ref[...] = jnp.zeros_like(small_ref)
    piece = 128

    @pl.loop(0, rows // piece)
    def _(index):
        span = pl.ds(pl.multiple_of(index * piece, piece), piece)
        mixed = mixed_ref[span, :]
        upstream, loss = finish_rows(
            tokens_ref[span, :].astype(F32), mixed, target_ref[span, :].astype(F32), scale
        )
        back = (upstream * scale).astype(BF16)
        back_ref[span, :] = back
        back_t_ref[:, span] = back.T
        small_ref[0:1, :] += jnp.sum(upstream * mixed, axis=0, keepdims=True)
        small_ref[1:2, :] += jnp.broadcast_to(jnp.sum(loss, axis=0, keepdims=True), (1, width))


def forward(normed_t, own, other, mixed=None, finish=None):
    width, rows = normed_t.shape
    part = own[0].shape[2]
    total = sum(array.shape[0] for array in own)
    first, last = mixed is None, finish is not None
    operands = [normed_t, *own, *other]
    if not first:
        operands.append(mixed)
    if last:
        operands.extend(finish)
    piece = (2, total, part, rows)
    shapes = [jax.ShapeDtypeStruct(piece, BF16), jax.ShapeDtypeStruct(piece, F32)]
    scratch = []
    if last:
        shapes += [
            jax.ShapeDtypeStruct((rows, width), BF16),
            jax.ShapeDtypeStruct((width, rows), BF16),
            jax.ShapeDtypeStruct((8, width), F32),
        ]
        scratch = [pltpu.VMEM((rows, width), F32)]
    else:
        shapes += [jax.ShapeDtypeStruct((rows, width), F32)]
    return pl.pallas_call(
        functools.partial(forward_kernel, first, last, len(own)),
        out_shape=tuple(shapes),
        in_specs=[VMEM] * len(operands),
        out_specs=tuple([VMEM] * len(shapes)),
        scratch_shapes=scratch,
        compiler_params=params(24),
        cost_estimate=COST,
        name="forward",
    )(*operands)


def pack_kernel(mine_ref, x_ref, y_ref, *refs):
    count = len(refs) - 3
    arrivals, (all_ref, far_ref) = refs[:count], refs[-2:]
    for index, ref in enumerate((mine_ref, x_ref, y_ref)):
        all_ref[index] = ref[...]
    for index, ref in enumerate(arrivals):
        block = ref[...]
        all_ref[3 + index] = block
        far_ref[index] = block


def pack(mine, x, y, arrivals, after):
    count = len(arrivals)
    return pl.pallas_call(
        pack_kernel,
        out_shape=(
            jax.ShapeDtypeStruct((3 + count, *mine.shape), BF16),
            jax.ShapeDtypeStruct((count, *mine.shape), BF16),
        ),
        in_specs=[VMEM] * (3 + count) + [ANY],
        out_specs=(VMEM, VMEM),
        compiler_params=params(16),
        cost_estimate=COST,
        name="pack",
    )(mine, x, y, *arrivals, after)


def turn_kernel(y_ref, y_far_ref, x_far_ref, a_ref, b_ref):
    held = a_ref.shape[0] - 1
    a_ref[0] = y_ref[...]
    for index in range(held):
        a_ref[1 + index] = y_far_ref[index]
    for index in range(b_ref.shape[0]):
        b_ref[index] = x_far_ref[held + index]


def turn(y, y_far, x_far):
    count = y_far.shape[0]
    first = (count + 1) // 2
    return pl.pallas_call(
        turn_kernel,
        out_shape=(
            jax.ShapeDtypeStruct((first, *y.shape), BF16),
            jax.ShapeDtypeStruct((count + 1 - first, *y.shape), BF16),
        ),
        in_specs=[VMEM] * 3,
        out_specs=(VMEM, VMEM),
        compiler_params=params(16),
        cost_estimate=COST,
        name="turn",
    )(y, y_far, x_far)


def tie_kernel(*refs):
    pass


def tie(array, after):
    return pl.pallas_call(
        tie_kernel,
        out_shape=jax.ShapeDtypeStruct(array.shape, array.dtype),
        in_specs=[ANY, ANY],
        out_specs=ANY,
        input_output_aliases={0: 0},
        compiler_params=params(4),
        cost_estimate=COST,
        name="tie",
    )(array, after)


def backward_kernel(side, places, add, count, *refs):
    refs = list(refs)
    back_ref, back_t_ref, normed_ref, gain_in = refs[:4]
    del refs[:4]
    weights, acts, slopes = refs[:count], refs[count:2 * count], refs[2 * count:3 * count]
    del refs[:3 * count]
    arrived = refs.pop(0) if add else None
    up_ref, down_ref, gain_ref = refs
    rows, width = back_ref.shape

    def joined(values):
        flat = [value.reshape(-1, value.shape[-1]) for value in values]
        return flat[0] if count == 1 else jnp.concatenate(flat, axis=0)

    def rows_of(which):
        return joined([
            ref[w:w + n, which] for ref, (w, a, n) in zip(weights, places)
        ])

    slope = joined([ref[side, a:a + n] for ref, (w, a, n) in zip(slopes, places)])
    act = joined([ref[side, a:a + n] for ref, (w, a, n) in zip(acts, places)])
    chunk = act.shape[0]
    back_act = dot_nn(rows_of(1), back_t_ref[...])
    back_hidden = (back_act * slope).astype(BF16)
    grad_up = dot_nn(back_hidden, normed_ref[...])
    up = rows_of(0).astype(F32)
    gain_ref[...] = gain_in[...] + jnp.sum(grad_up * up, axis=0, keepdims=True)
    grad_down = dot_nn(act, back_ref[...])
    if add:
        grad_up += arrived[0].reshape(chunk, width).astype(F32)
        grad_down += arrived[1].reshape(chunk, width).astype(F32)
    up_ref[...] = grad_up.astype(BF16).reshape(up_ref.shape)
    down_ref[...] = grad_down.astype(BF16).reshape(down_ref.shape)


def backward(side, common, gain, pieces, arrived):
    rows, width = common[0].shape
    part = pieces[0][0].shape[2]
    places = tuple((piece[1], piece[4], piece[5]) for piece in pieces)
    count = sum(piece[5] for piece in pieces)
    operands = [*common, gain]
    for which in (0, 2, 3):
        operands += [piece[which] for piece in pieces]
    body = functools.partial(backward_kernel, side, places, arrived is not None, len(pieces))
    if arrived is None:
        def run(*refs):
            grads, gain_ref = refs[-2:]
            body(*refs[:-2], grads.at[0], grads.at[1], gain_ref)

        shapes = [jax.ShapeDtypeStruct((2, count, part, width), BF16)]
    else:
        operands.append(arrived)
        run = body
        shapes = [jax.ShapeDtypeStruct((count, part, width), BF16)] * 2
    shapes.append(jax.ShapeDtypeStruct((1, width), F32))
    return pl.pallas_call(
        run,
        out_shape=tuple(shapes),
        in_specs=[VMEM] * len(operands),
        out_specs=tuple([VMEM] * len(shapes)),
        compiler_params=params(20),
        cost_estimate=COST,
        name="backward",
    )(*operands)


def total_kernel(count, *refs):
    ins, outs = refs[:4], refs[-count:]
    for index, out in enumerate(outs):
        total = ins[0][index].astype(F32)
        for ref in ins[1:]:
            total = total + ref[index].astype(F32)
        out[...] = total.astype(BF16)
    if len(refs) > 4 + count:
        refs[5][...] = refs[4][...]


def totals(parts, vector=None):
    count, part, width = parts[0].shape
    operands, shapes = list(parts), []
    if vector is not None:
        operands.append(vector)
        shapes.append(jax.ShapeDtypeStruct(vector.shape, F32))
    shapes += [jax.ShapeDtypeStruct((part, width), BF16)] * count
    return pl.pallas_call(
        functools.partial(total_kernel, count),
        out_shape=tuple(shapes),
        in_specs=[VMEM] * len(operands),
        out_specs=tuple([VMEM] * len(shapes)),
        compiler_params=params(16),
        cost_estimate=COST,
        name="totals",
    )(*operands)


def collect_kernel(count, *refs):
    out_ref = refs[-1]
    part, width = refs[0].shape
    total = refs[0][...].astype(F32)
    for ref in refs[1:count]:
        total = total + ref[...].astype(F32)
    out_ref[pl.ds(0, part), :] = total.astype(BF16)
    if len(refs) > count + 1:
        rest = refs[count][...]
        pieces = []
        for _ in range(3):
            piece = rest.astype(BF16).astype(F32)
            pieces.append(piece)
            rest = rest - piece
        pieces.append(jnp.zeros_like(rest))
        out_ref[pl.ds(part, 32), :] = jnp.concatenate(pieces, axis=0).astype(BF16)


def collect(parts, vector=None):
    part, width = parts[0].shape
    operands = list(parts) + ([] if vector is None else [vector])
    return pl.pallas_call(
        functools.partial(collect_kernel, len(parts)),
        out_shape=jax.ShapeDtypeStruct((part + (0 if vector is None else 32), width), BF16),
        in_specs=[VMEM] * len(operands),
        out_specs=VMEM,
        compiler_params=params(16),
        cost_estimate=COST,
        name="collect",
    )(*operands)


def place_kernel(part, group_ref, a_ref, b_ref, c_ref, d_ref, *refs):
    group = group_ref[0]
    held_ref = refs[-1]
    quarters = (a_ref, b_ref, c_ref, d_ref)
    for index, ref in enumerate(quarters):
        first = pl.multiple_of(jnp.bitwise_xor(group, index) * part, part)
        held_ref[pl.ds(first, part), :] = ref[pl.ds(0, part), :].astype(F32)
    if len(refs) == 2:
        refs[0][...] = held_ref[...]
        return
    refs[0][...] = held_ref[...].T
    vectors = []
    for ref in quarters:
        rows = ref[pl.ds(part, 32), :].astype(F32)
        vectors.append((rows[0:8] + rows[8:16]) + rows[16:24])
    refs[1][...] = (vectors[0] + vectors[1]) + (vectors[2] + vectors[3])


def place_quarters(group, quarters, part, vector):
    width = quarters[0].shape[1]
    if vector:
        shapes = [
            jax.ShapeDtypeStruct((width, 4 * part), F32), jax.ShapeDtypeStruct((8, width), F32)
        ]
    else:
        shapes = [jax.ShapeDtypeStruct((4 * part, width), F32)]
    return pl.pallas_call(
        functools.partial(place_kernel, part),
        out_shape=tuple(shapes),
        in_specs=[SMEM] + [VMEM] * 4,
        out_specs=tuple([VMEM] * len(shapes)),
        scratch_shapes=[pltpu.VMEM((4 * part, width), F32)],
        compiler_params=params(16),
        cost_estimate=COST,
        name="place",
    )(group, *quarters)


def shards_square(
    image_tokens,
    tile_lists,
    opacity,
    tile_counts,
    ray_pixel,
    block_owner,
    gaussian_features,
    layer_norm_gain,
    layer_scale,
    up_weight,
    down_weight,
):
    ray_count = lax.axis_size("ray")
    group_count = lax.axis_size("grp")
    depth = ray_count // 2
    group = lax.axis_index("grp").reshape(1)
    me = lax.axis_index("ray").reshape(1)
    rows, width = image_tokens.shape
    part = down_weight.shape[0] // group_count

    def beside(array, flip):
        return lax.ppermute(array, "grp", [(g, g ^ flip) for g in range(group_count)])

    def partner(array, flip=1):
        return lax.ppermute(array, "ray", [(r, r ^ flip) for r in range(ray_count)])

    def along(array, shift):
        pairs = [(r, (r + 2 * shift) % ray_count) for r in range(ray_count)]
        return lax.ppermute(array, "ray", pairs)

    mine = own_quarter(group, up_weight, down_weight, part)
    arrivals = [along(mine, -shift) for shift in range(1, depth)]
    x, y = beside(mine, 1), beside(mine, 2)

    pixels = ray_pixel[0].reshape(ray_count, rows)
    rendered = render(
        me, block_owner, tile_lists, opacity, tile_counts.reshape(1, rows), pixels,
        gaussian_features,
    )
    first, far = pack(mine, x, y, arrivals, rendered)
    x_far, y_far = beside(far, 1), beside(far, 2)
    first_other = partner(first)
    tokens, normed, normed_t = prepare_tokens(
        me, block_owner, pixels, image_tokens, layer_norm_gain.reshape(1, width)
    )
    rendered = tie(rendered, normed)
    target = lax.all_to_all(rendered, "ray", split_axis=0, concat_axis=0, tiled=True)
    passed_x, passed_y = turn(y, y_far, x_far)
    d_low, d_high = beside(passed_x, 1), beside(passed_y, 2)
    act_first, slope_first, mixed = forward(normed_t, [first], [first_other])
    x_far, y_far = tie(x_far, mixed), tie(y_far, mixed)
    x_other, y_other = partner(x_far), partner(y_far)
    act_next, slope_next, mixed = forward(normed_t, [x_far, y_far], [x_other, y_other], mixed)
    d_low, d_high = tie(d_low, mixed), tie(d_high, mixed)
    low_other, high_other = partner(d_low), partner(d_high)
    act_last, slope_last, back, back_t, small = forward(
        normed_t, [d_low, d_high], [low_other, high_other], mixed,
        (tokens, target, layer_scale.reshape(1, width)),
    )
    common = (back, back_t, normed)
    held = {
        0: (first, x_far, y_far, d_low, d_high),
        1: (first_other, x_other, y_other, low_other, high_other),
    }
    low = d_low.shape[0]

    def grads(side, quarter, gain, arrived):
        firsts, xs, ys, lows, highs = held[side]
        start = (firsts, quarter, act_first, slope_first, quarter, 1)
        pieces = {
            0: [start, (firsts, 3, act_first, slope_first, 3, depth - 1)],
            1: [start, (xs, 0, act_next, slope_next, 0, depth - 1)],
            2: [start, (ys, 0, act_next, slope_next, depth - 1, depth - 1)],
            3: [
                (lows, 0, act_last, slope_last, 0, low),
                (highs, 0, act_last, slope_last, low, depth - low),
            ],
        }[quarter]
        return backward(side, common, gain, pieces, arrived)

    gain = jnp.zeros((1, width), F32)
    arrived, sums, sent = {}, {}, {}
    for side, quarter in ((1, 3), (1, 1), (0, 3), (1, 2), (0, 1), (1, 0), (0, 2), (0, 0)):
        if side == 1:
            out, gain = grads(1, quarter, gain, None)
            arrived[quarter] = partner(out)
        else:
            grad_up, grad_down, gain = grads(0, quarter, gain, arrived[quarter])
            sums[quarter] = (grad_up, grad_down)
            if quarter:
                sent[quarter] = (beside(grad_up, quarter), beside(grad_down, quarter))
    vector = jnp.concatenate(
        [gain / layer_norm_gain.reshape(1, width), small[:2], jnp.zeros((5, width), F32)], axis=0
    )
    vector, *shares = totals([sums[0][1]] + [sent[quarter][1] for quarter in (1, 2, 3)], vector)

    def sum_along(shares, *vector):
        arrivals = [along(shares[shift], shift) for shift in range(1, depth)]
        total = collect([shares[0]] + arrivals, *vector)
        return [total] + [beside(total, flip) for flip in (1, 2, 3)]

    quarters = sum_along(shares)
    (grad_down,) = place_quarters(group, quarters, part, False)
    vector = vector + partner(vector)
    flip = 2
    while flip < ray_count:
        vector = vector + partner(vector, flip)
        flip *= 2
    shares = totals([sums[0][0]] + [sent[quarter][0] for quarter in (1, 2, 3)])
    quarters = sum_along(shares, vector)
    grad_up, vector = place_quarters(group, quarters, part, True)
    loss = vector[2, 0] / (rows * ray_count * group_count)
    return (grad_up, grad_down, vector[0], vector[1], loss)


def shards(*operands):
    ray_count, group_count = lax.axis_size("ray"), lax.axis_size("grp")
    hidden = operands[-1].shape[0]
    square = group_count == 4 and ray_count in (4, 8, 16) and hidden % (16 * group_count) == 0
    return (shards_square if square else shards_general)(*operands)


def solution(mesh):
    return jax.shard_map(
        shards,
        mesh=mesh,
        in_specs=(
            P(("grp", "ray"), None),
            P(None, ("grp", "ray")),
            P(None, ("grp", "ray")),
            P(("grp", "ray")),
            P("grp", None),
            P("grp", None),
            P(("grp", "ray"), None),
            P(),
            P(),
            P(None, "ray"),
            P("ray", None),
        ),
        out_specs=(P(None, "ray"), P("ray", None), P(), P(), P()),
        check_vma=False,
    )
```

```python
import functools

import jax
import jax.numpy as jnp
from jax import lax
from jax.experimental import pallas as pl
from jax.experimental.pallas import tpu as pltpu
from jax.sharding import PartitionSpec as P

STABILITY_EPSILON = 1e-06
F32 = jnp.float32
BF16 = jnp.bfloat16
MIB = 1024 * 1024
COST = pl.CostEstimate(flops=1 << 20, bytes_accessed=1 << 16, transcendentals=0)
SMEM = pl.BlockSpec(memory_space=pltpu.SMEM)
VMEM = pl.BlockSpec(memory_space=pltpu.VMEM)
ANY = pl.BlockSpec(memory_space=pl.ANY)


def params(mib=48, **more):
    return pltpu.CompilerParams(vmem_limit_bytes=mib * MIB, **more)


def dot_nn(a, b):
    return lax.dot_general(a, b, (((1,), (0,)), ((), ())), preferred_element_type=F32)


def dot_tn(a, b):
    return lax.dot_general(a, b, (((0,), (0,)), ((), ())), preferred_element_type=F32)


def dot_nt(a, b):
    return lax.dot_general(a, b, (((1,), (1,)), ((), ())), preferred_element_type=F32)


def owner_of(pixels, owner_ref, rows, count):
    block = lax.div(pixels, jnp.int32(rows))
    owner = jnp.zeros_like(pixels)
    for slot in range(count):
        owner = jnp.where(block == slot, owner_ref[0, slot], owner)
    return owner


def earlier(rows):
    before = lax.broadcasted_iota(jnp.int32, (rows, rows), 0)
    after = lax.broadcasted_iota(jnp.int32, (rows, rows), 1)
    return jnp.where(before < after, 1.0, 0.0).astype(BF16)


def whole(array):
    return pl.BlockSpec(array.shape, lambda step: (0,) * array.ndim)


def render_kernel(
    ray_count, relative, me_ref, owner_ref, lists_ref, opacity_ref, counts_ref, pixels_ref,
    features_ref, near_ref, other_ref, ids_ref, share_ref, table_ref, send_ref,
):
    depth, rays = lists_ref.shape
    gauss = features_ref.shape[0]
    width = features_ref.shape[1]
    me = me_ref[0]
    ids_ref[...] = lists_ref[...] - me * gauss
    passing = jnp.ones((1, rays), F32)
    counts = counts_ref[...]
    for level in range(depth):
        alpha = opacity_ref[pl.ds(level, 1), :]
        share_ref[pl.ds(level, 1), :] = jnp.where(level < counts, alpha * passing, 0.0)
        passing = passing * (1.0 - alpha)

    tile = 128
    lanes = 128
    columns = rays // lanes

    @pl.loop(0, (gauss // tile) * columns)
    def _(step):
        first = pl.multiple_of(lax.div(step, columns) * tile, tile)
        lane = pl.multiple_of(lax.rem(step, columns) * lanes, lanes)
        number = lax.broadcasted_iota(jnp.int32, (tile, lanes), 0) + first
        total = jnp.zeros((tile, lanes), F32)
        for level in range(depth):
            ident = ids_ref[pl.ds(level, 1), pl.ds(lane, lanes)]
            share = share_ref[pl.ds(level, 1), pl.ds(lane, lanes)]
            total = total + jnp.where(ident == number, share, 0.0)
        table_ref[pl.ds(first, tile), pl.ds(lane, lanes)] = total.astype(BF16)

    mine = pixels_ref[:, pl.ds(pl.multiple_of(me * rays, rays), rays)]
    owner = owner_of(mine, owner_ref, rays, ray_count)
    padded = -(-ray_count // 16) * 16
    member = (lax.broadcasted_iota(jnp.int32, (padded, rays), 0) == owner)
    ranks = dot_nn(member.astype(F32).astype(BF16), earlier(rays))
    rank = jnp.sum(jnp.where(member, ranks, 0.0), axis=0, keepdims=True).astype(jnp.int32)
    if relative:
        chips = ray_count // 2
        shift = lax.div(owner, jnp.int32(2)) - lax.div(me, jnp.int32(2))
        shift = jnp.where(shift < 0, shift + chips, shift)
        flip = jnp.where(lax.rem(owner, jnp.int32(2)) == lax.rem(me, jnp.int32(2)), 0, 1)
        block = flip * chips + shift
    else:
        block = owner
    slot = block * (rays // ray_count) + rank
    send_ref[...] = (
        (lax.broadcasted_iota(jnp.int32, (rays, rays), 0) == slot).astype(F32).astype(BF16)
    )

    piece = 256
    half = rays // 2

    @pl.loop(0, width // piece)
    def _(step):
        cols = pl.ds(pl.multiple_of(step * piece, piece), piece)
        rendered = dot_tn(table_ref[...], features_ref[:, cols]).astype(BF16)
        ordered = dot_nn(send_ref[...], rendered).astype(BF16)
        near_ref[:, :, cols] = ordered[:half].reshape(*near_ref.shape[:2], piece)
        other_ref[:, :, cols] = ordered[half:].reshape(*other_ref.shape[:2], piece)


def render(ray_count, relative, me, owner, lists, opacity, counts, pixels, features):
    depth, rays = lists.shape
    gauss, width = features.shape
    shape = jax.ShapeDtypeStruct((ray_count // 2, rays // ray_count, width), BF16)
    operands = (lists, opacity, counts, pixels, features)
    return pl.pallas_call(
        functools.partial(render_kernel, ray_count, relative),
        grid=(1,),
        out_shape=(shape, shape),
        in_specs=[SMEM, SMEM] + [whole(array) for array in operands],
        out_specs=(VMEM, VMEM),
        scratch_shapes=[
            pltpu.VMEM((depth, rays), jnp.int32),
            pltpu.VMEM((depth, rays), F32),
            pltpu.VMEM((gauss, rays), BF16),
            pltpu.VMEM((rays, rays), BF16),
        ],
        compiler_params=params(24),
        cost_estimate=COST,
        name="render",
    )(me, owner, *operands)


def tokens_kernel(
    ray_count, relative, me_ref, owner_ref, pixels_ref, tokens_ref, gain_ref,
    tokens_out, normed_out, normed_t_out, order_ref, rank_ref, place_ref,
):
    rows, width = tokens_ref.shape
    me = me_ref[0]
    each = rows // ray_count
    pixels = jnp.concatenate(
        [pixels_ref[:, sender * rows:(sender + 1) * rows] for sender in range(ray_count)], axis=0
    )
    mine = owner_of(pixels, owner_ref, rows, ray_count) == me
    place_ref[...] = lax.rem(pixels, jnp.int32(rows)).astype(F32)
    member = jnp.where(mine, 1.0, 0.0)
    padded = -(-ray_count // 16) * 16
    if padded > ray_count:
        spread = jnp.concatenate([member, jnp.zeros((padded - ray_count, rows), F32)], axis=0)
    else:
        spread = member
    ranks = dot_nn(spread.astype(BF16), earlier(rows))
    rank_ref[...] = jnp.where(mine, ranks[:ray_count], -1.0)
    chips = ray_count // 2
    for index in range(ray_count):
        if relative:
            chip = lax.rem(lax.div(me, jnp.int32(2)) + (chips - index // 2), jnp.int32(chips))
            sender = 2 * chip + jnp.bitwise_xor(lax.rem(me, jnp.int32(2)), index % 2)
        else:
            sender = index
        rank = rank_ref[pl.ds(sender, 1), :].astype(jnp.int32)
        hit = lax.broadcasted_iota(jnp.int32, (each, rows), 0) == rank
        at = jnp.sum(
            jnp.where(hit, place_ref[pl.ds(sender, 1), :], 0.0), axis=1, keepdims=True
        )
        here = lax.broadcasted_iota(jnp.int32, (each, rows), 1) == at.astype(jnp.int32)
        order_ref[pl.ds(index * each, each), :] = here.astype(F32).astype(BF16)
    half = min(128, rows)
    gain = gain_ref[...]

    @pl.loop(0, rows // half)
    def _(step):
        span = pl.ds(pl.multiple_of(step * half, half), half)
        values = dot_nn(order_ref[span, :], tokens_ref[...])
        tokens_out[span, :] = values.astype(BF16)
        centered = values - jnp.mean(values, axis=-1, keepdims=True)
        variance = jnp.mean(centered * centered, axis=-1, keepdims=True)
        xhat = centered * lax.rsqrt(variance + STABILITY_EPSILON)
        normed = (xhat * gain).astype(BF16)
        normed_out[span, :] = normed
        normed_t_out[:, span] = normed.T


def prepare_tokens(ray_count, relative, me, owner, pixels, tokens, gain):
    rows, width = tokens.shape
    return pl.pallas_call(
        functools.partial(tokens_kernel, ray_count, relative),
        grid=(1,),
        out_shape=(
            jax.ShapeDtypeStruct((rows, width), BF16),
            jax.ShapeDtypeStruct((rows, width), BF16),
            jax.ShapeDtypeStruct((width, rows), BF16),
        ),
        in_specs=[SMEM, SMEM, whole(pixels), whole(tokens), whole(gain)],
        out_specs=(VMEM, VMEM, VMEM),
        scratch_shapes=[
            pltpu.VMEM((rows, rows), BF16),
            pltpu.VMEM((ray_count, rows), F32),
            pltpu.VMEM((ray_count, rows), F32),
        ],
        compiler_params=params(20),
        cost_estimate=COST,
        name="tokens",
    )(me, owner, pixels, tokens, gain)


def up_kernel(normed_ref, up_ref, act_ref, slope_ref):
    parts, _, part_rows, width = up_ref.shape
    up = up_ref[...].reshape(parts * part_rows, width)
    rows = normed_ref.shape[0]
    piece = min(128, rows)

    @pl.loop(0, rows // piece)
    def _(step):
        span = pl.ds(pl.multiple_of(step * piece, piece), piece)
        hidden = dot_nn(normed_ref[span, :], up)
        phi = 0.5 * (1.0 + lax.erf(hidden * (0.5 ** 0.5)))
        density = jnp.exp(-0.5 * hidden * hidden) * ((2.0 * jnp.pi) ** -0.5)
        act_ref[span, :] = (hidden * phi).astype(BF16)
        slope_ref[span, :] = (phi + hidden * density).astype(slope_ref.dtype)


def project_up(normed, up):
    rows, width = normed.shape
    parts, chunks, part_rows, chunk = up.shape
    return pl.pallas_call(
        up_kernel,
        grid=(chunks,),
        out_shape=(
            jax.ShapeDtypeStruct((rows, chunks * chunk), BF16),
            jax.ShapeDtypeStruct((rows, chunks * chunk), F32),
        ),
        in_specs=[
            pl.BlockSpec((rows, width), lambda j: (0, 0)),
            pl.BlockSpec((parts, 1, part_rows, chunk), lambda j: (0, j, 0, 0)),
        ],
        out_specs=(
            pl.BlockSpec((rows, chunk), lambda j: (0, j)),
            pl.BlockSpec((rows, chunk), lambda j: (0, j)),
        ),
        compiler_params=params(dimension_semantics=("arbitrary",)),
        cost_estimate=COST,
        name="up",
    )(normed, up)


def down_kernel(
    chunks, act_ref, down_ref, tokens_ref, target_ref, scale_ref,
    grad_ref, back_ref, small_ref, mixed_ref,
):
    step = pl.program_id(0)
    rows, width = tokens_ref.shape
    act = act_ref[...]

    @pl.when(step < chunks)
    def _():
        parts, _, part_rows, _ = down_ref.shape
        part = dot_nn(act, down_ref[...].reshape(parts * part_rows, width))

        @pl.when(step == 0)
        def _():
            mixed_ref[...] = part

        @pl.when(step > 0)
        def _():
            mixed_ref[...] += part

    @pl.when(step == chunks - 1)
    def _():
        scale = scale_ref[...]
        small_ref[...] = jnp.zeros_like(small_ref)
        piece = min(64, rows)

        @pl.loop(0, rows // piece)
        def _(index):
            span = pl.ds(pl.multiple_of(index * piece, piece), piece)
            mixed = mixed_ref[span, :]
            out = tokens_ref[span, :].astype(F32) + scale * mixed
            goal = target_ref[span, :].astype(F32)
            out_norm = jnp.sqrt(jnp.sum(out * out, axis=-1, keepdims=True) + STABILITY_EPSILON)
            goal_norm = jnp.sqrt(jnp.sum(goal * goal, axis=-1, keepdims=True) + STABILITY_EPSILON)
            norms = out_norm * goal_norm
            cosine = jnp.sum(out * goal, axis=-1, keepdims=True) / norms
            upstream = (cosine / (out_norm * out_norm)) * out - goal * (1.0 / norms)
            back_ref[span, :] = (upstream * scale).astype(BF16)
            small_ref[0:1, :] += jnp.sum(upstream * mixed, axis=0, keepdims=True)
            loss = jnp.sum(1.0 - cosine, axis=0, keepdims=True)
            small_ref[1:2, :] += jnp.broadcast_to(loss, (1, width))

    @pl.when(step >= chunks)
    def _():
        grad = dot_tn(act, back_ref[...])
        grad_ref[...] = grad.astype(BF16).reshape(grad_ref.shape)


def project_down(act, down, tokens, target, scale):
    rows, width = tokens.shape
    parts, chunks, part_rows, _ = down.shape
    chunk = parts * part_rows
    return pl.pallas_call(
        functools.partial(down_kernel, chunks),
        grid=(2 * chunks,),
        out_shape=(
            jax.ShapeDtypeStruct(down.shape, BF16),
            jax.ShapeDtypeStruct((rows, width), BF16),
            jax.ShapeDtypeStruct((8, width), F32),
        ),
        in_specs=[
            pl.BlockSpec((rows, chunk), lambda j: (0, lax.rem(j, chunks))),
            pl.BlockSpec(
                (parts, 1, part_rows, width), lambda j: (0, jnp.minimum(j, chunks - 1), 0, 0)
            ),
            pl.BlockSpec((rows, width), lambda j: (0, 0)),
            pl.BlockSpec((rows, width), lambda j: (0, 0)),
            pl.BlockSpec((1, width), lambda j: (0, 0)),
        ],
        out_specs=(
            pl.BlockSpec(
                (parts, 1, part_rows, width), lambda j: (0, jnp.maximum(j - chunks, 0), 0, 0)
            ),
            pl.BlockSpec((rows, width), lambda j: (0, 0)),
            pl.BlockSpec((8, width), lambda j: (0, 0)),
        ),
        scratch_shapes=[pltpu.VMEM((rows, width), F32)],
        compiler_params=params(dimension_semantics=("arbitrary",)),
        cost_estimate=COST,
        name="down",
    )(act, down, tokens, target, scale)


def back_kernel(back_ref, down_ref, slope_ref, normed_t_ref, up_ref, gain_ref, grad_ref, sum_ref):
    step = pl.program_id(0)
    parts, _, part_rows, width = down_ref.shape
    chunk = parts * part_rows
    rows = back_ref.shape[0]
    back_act = dot_nt(back_ref[...], down_ref[...].reshape(chunk, width))
    back_hidden = (back_act * slope_ref[...]).astype(BF16)
    up_parts, _, up_rows, _ = up_ref.shape

    @pl.when(step == 0)
    def _():
        sum_ref[...] = jnp.zeros_like(sum_ref)

    grad = dot_nn(normed_t_ref[...], back_hidden)
    grad_ref[...] = grad.astype(BF16).reshape(grad_ref.shape)
    up = up_ref[...].reshape(up_parts * up_rows, chunk).astype(F32)
    sum_ref[...] += jnp.sum(grad * up, axis=1, keepdims=True) / gain_ref[...]


def back_up(back, down, slope, normed_t, up, gain):
    width, rows = normed_t.shape
    parts, chunks, part_rows, _ = down.shape
    chunk = parts * part_rows
    up_parts, _, up_rows, _ = up.shape
    return pl.pallas_call(
        back_kernel,
        grid=(chunks,),
        out_shape=(
            jax.ShapeDtypeStruct(up.shape, BF16),
            jax.ShapeDtypeStruct((width, 1), F32),
        ),
        in_specs=[
            pl.BlockSpec((rows, width), lambda j: (0, 0)),
            pl.BlockSpec((parts, 1, part_rows, width), lambda j: (0, j, 0, 0)),
            pl.BlockSpec((rows, chunk), lambda j: (0, j)),
            pl.BlockSpec((width, rows), lambda j: (0, 0)),
            pl.BlockSpec((up_parts, 1, up_rows, chunk), lambda j: (0, j, 0, 0)),
            pl.BlockSpec((width, 1), lambda j: (0, 0)),
        ],
        out_specs=(
            pl.BlockSpec((up_parts, 1, up_rows, chunk), lambda j: (0, j, 0, 0)),
            pl.BlockSpec((width, 1), lambda j: (0, 0)),
        ),
        compiler_params=params(dimension_semantics=("arbitrary",)),
        cost_estimate=COST,
        name="back",
    )(back, down, slope, normed_t, up, gain)


def gather_weight(weight, parts, group, group_count, ray_count):
    rows, cols = weight.shape
    if parts == 1:
        whole = lax.all_gather(weight, "ray", axis=0, tiled=True)
    else:
        part = lax.dynamic_slice_in_dim(weight, group * (rows // parts), rows // parts, 0)
        whole = lax.all_gather(part, ("grp", "ray"), axis=0, tiled=True)
    return whole.reshape(parts, ray_count, rows // parts, cols)


def reduce_gradient(grad):
    parts, ray_count, part_rows, cols = grad.shape
    flat = grad.reshape(parts * ray_count * part_rows, cols)
    if parts == 1:
        share = lax.psum_scatter(flat, "ray", scatter_dimension=0, tiled=True)
        return lax.psum(share.astype(F32), "grp")
    share = lax.psum_scatter(flat, "grp", scatter_dimension=0, tiled=True)
    share = lax.psum_scatter(share, "ray", scatter_dimension=0, tiled=True)
    return lax.all_gather(share, "grp", axis=0, tiled=True).astype(F32)


def shards_general(
    image_tokens,
    tile_lists,
    opacity,
    tile_counts,
    ray_pixel,
    block_owner,
    gaussian_features,
    layer_norm_gain,
    layer_scale,
    up_weight,
    down_weight,
):
    ray_count = lax.axis_size("ray")
    group_count = lax.axis_size("grp")
    group = lax.axis_index("grp")
    me = lax.axis_index("ray").reshape(1)
    rows, width = image_tokens.shape
    up_parts = group_count if up_weight.shape[0] % (16 * group_count) == 0 else 1
    down_parts = group_count if down_weight.shape[0] % (16 * group_count) == 0 else 1
    up = gather_weight(up_weight, up_parts, group, group_count, ray_count)
    down = gather_weight(down_weight, down_parts, group, group_count, ray_count)
    rendered = render(
        ray_count, False, me, block_owner, tile_lists, opacity, tile_counts.reshape(1, rows),
        ray_pixel, gaussian_features,
    )
    rendered = jnp.concatenate(rendered, axis=0).reshape(rows, width)
    target = lax.all_to_all(rendered, "ray", split_axis=0, concat_axis=0, tiled=True)
    tokens, normed, normed_t = prepare_tokens(
        ray_count, False, me, block_owner, ray_pixel, image_tokens,
        layer_norm_gain.reshape(1, width),
    )
    act, slope = project_up(normed, up)
    grad_down, back, small = project_down(act, down, tokens, target, layer_scale.reshape(1, width))
    grad_up, gain_sum = back_up(back, down, slope, normed_t, up, layer_norm_gain.reshape(width, 1))
    grad_down = reduce_gradient(grad_down)
    grad_up = reduce_gradient(grad_up)
    sums = jnp.concatenate([gain_sum.reshape(1, width), small[:2]], axis=0)
    sums = lax.psum(sums, ("grp", "ray"))
    loss = sums[2, 0] / (rows * ray_count * group_count)
    return (grad_up, grad_down, sums[0], sums[1], loss)


def quarter_kernel(group_ref, up_ref, down_ref, out_ref, turned_ref):
    part = out_ref.shape[1]
    first = pl.multiple_of(group_ref[0] * part, part)
    turned_ref[...] = up_ref[...].T
    out_ref[0] = turned_ref[pl.ds(first, part), :]
    out_ref[1] = down_ref[pl.ds(first, part), :]


def own_quarter(group, up, down, part):
    width, chunk = up.shape
    return pl.pallas_call(
        quarter_kernel,
        out_shape=jax.ShapeDtypeStruct((2, part, width), BF16),
        grid=(1,),
        in_specs=[SMEM, whole(up), whole(down)],
        out_specs=VMEM,
        scratch_shapes=[pltpu.VMEM((chunk, width), BF16)],
        compiler_params=params(16),
        cost_estimate=COST,
        name="quarter",
    )(group, up, down)


def finish_rows(tokens, mixed, goal, scale):
    out = tokens + scale * mixed
    out_norm = jnp.sqrt(jnp.sum(out * out, axis=-1, keepdims=True) + STABILITY_EPSILON)
    goal_norm = jnp.sqrt(jnp.sum(goal * goal, axis=-1, keepdims=True) + STABILITY_EPSILON)
    norms = out_norm * goal_norm
    cosine = jnp.sum(out * goal, axis=-1, keepdims=True) / norms
    upstream = (cosine / (out_norm * out_norm)) * out - goal * (1.0 / norms)
    return upstream, 1.0 - cosine


def forward_kernel(first, blocks, sides, *refs):
    last = blocks > 0
    refs = list(refs)
    normed_t_ref = refs.pop(0)
    own, other = refs[:sides], refs[sides:2 * sides]
    del refs[:2 * sides]
    mixed_in = None if first else refs.pop(0)
    if last:
        tokens_ref, scale_ref = refs[:2]
        targets = refs[2:2 + blocks]
        del refs[:2 + blocks]
    act_ref, slope_ref = refs[:2]
    del refs[:2]
    width, rows = normed_t_ref.shape
    total = act_ref.shape[1]
    part = act_ref.shape[2]
    downs = []
    for side, group in enumerate((own, other)):
        start = 0
        for ref in group:
            count = ref.shape[0]
            hiddens = dot_nn(ref[:, 0].reshape(count * part, width), normed_t_ref[...])
            for index in range(count):
                hidden = hiddens[index * part:(index + 1) * part]
                phi = 0.5 * (1.0 + lax.erf(hidden * (0.5 ** 0.5)))
                density = jnp.exp(-0.5 * hidden * hidden) * ((2.0 * jnp.pi) ** -0.5)
                act_ref[side, start + index] = (hidden * phi).astype(BF16)
                slope_ref[side, start + index] = phi + hidden * density
            downs.append(ref[:, 1].reshape(count * part, width))
            start += count
    act = act_ref[...].reshape(2 * total * part, rows)
    down = jnp.concatenate(downs, axis=0)
    if not last:
        mixed_out = refs[0]
        part_sum = dot_tn(act, down)
        mixed_out[...] = part_sum if first else mixed_in[...] + part_sum
        return
    back_ref, back_t_ref, small_ref, mixed_ref = refs
    mixed_ref[...] = mixed_in[...] + dot_tn(act, down)
    scale = scale_ref[...]
    small_ref[...] = jnp.zeros_like(small_ref)
    piece = rows // blocks
    for index, target_ref in enumerate(targets):
        span = pl.ds(index * piece, piece)
        mixed = mixed_ref[span, :]
        upstream, loss = finish_rows(
            tokens_ref[span, :].astype(F32), mixed,
            target_ref[...].reshape(piece, width).astype(F32), scale,
        )
        back = (upstream * scale).astype(BF16)
        back_ref[span, :] = back
        back_t_ref[:, span] = back.T
        small_ref[0:1, :] += jnp.sum(upstream * mixed, axis=0, keepdims=True)
        small_ref[1:2, :] += jnp.broadcast_to(jnp.sum(loss, axis=0, keepdims=True), (1, width))


def forward(normed_t, own, other, mixed=None, finish=None):
    width, rows = normed_t.shape
    part = own[0].shape[2]
    total = sum(array.shape[0] for array in own)
    first, last = mixed is None, finish is not None
    blocks = len(finish) - 2 if last else 0
    operands = [normed_t, *own, *other]
    if not first:
        operands.append(mixed)
    if last:
        operands.extend(finish)
    piece = (2, total, part, rows)
    shapes = [jax.ShapeDtypeStruct(piece, BF16), jax.ShapeDtypeStruct(piece, F32)]
    scratch = []
    if last:
        shapes += [
            jax.ShapeDtypeStruct((rows, width), BF16),
            jax.ShapeDtypeStruct((width, rows), BF16),
            jax.ShapeDtypeStruct((8, width), F32),
        ]
        scratch = [pltpu.VMEM((rows, width), F32)]
    else:
        shapes += [jax.ShapeDtypeStruct((rows, width), F32)]
    return pl.pallas_call(
        functools.partial(forward_kernel, first, blocks, len(own)),
        out_shape=tuple(shapes),
        in_specs=[VMEM] * len(operands),
        out_specs=tuple([VMEM] * len(shapes)),
        scratch_shapes=scratch,
        compiler_params=params(24),
        cost_estimate=COST,
        name="forward",
    )(*operands)


def pack_kernel(mine_ref, x_ref, y_ref, *refs):
    count = len(refs) - 3
    arrivals, (all_ref, far_ref) = refs[:count], refs[-2:]
    for index, ref in enumerate((mine_ref, x_ref, y_ref)):
        all_ref[index] = ref[...]
    for index, ref in enumerate(arrivals):
        block = ref[...]
        all_ref[3 + index] = block
        far_ref[index] = block


def pack(mine, x, y, arrivals, after):
    count = len(arrivals)
    return pl.pallas_call(
        pack_kernel,
        out_shape=(
            jax.ShapeDtypeStruct((3 + count, *mine.shape), BF16),
            jax.ShapeDtypeStruct((count, *mine.shape), BF16),
        ),
        in_specs=[VMEM] * (3 + count) + [ANY],
        out_specs=(VMEM, VMEM),
        compiler_params=params(16),
        cost_estimate=COST,
        name="pack",
    )(mine, x, y, *arrivals, after)


def turn_kernel(y_ref, y_far_ref, x_far_ref, after_ref, a_ref, b_ref):
    held = a_ref.shape[0] - 1
    a_ref[0] = y_ref[...]
    for index in range(held):
        a_ref[1 + index] = y_far_ref[index]
    for index in range(b_ref.shape[0]):
        b_ref[index] = x_far_ref[held + index]


def turn(y, y_far, x_far, after):
    count = y_far.shape[0]
    first = (count + 1) // 2
    return pl.pallas_call(
        turn_kernel,
        out_shape=(
            jax.ShapeDtypeStruct((first, *y.shape), BF16),
            jax.ShapeDtypeStruct((count + 1 - first, *y.shape), BF16),
        ),
        in_specs=[VMEM] * 3 + [ANY],
        out_specs=(VMEM, VMEM),
        compiler_params=params(16),
        cost_estimate=COST,
        name="turn",
    )(y, y_far, x_far, after)


def tie_kernel(*refs):
    pass


def tie(array, *after):
    return pl.pallas_call(
        tie_kernel,
        out_shape=jax.ShapeDtypeStruct(array.shape, array.dtype),
        in_specs=[ANY] * (1 + len(after)),
        out_specs=ANY,
        input_output_aliases={0: 0},
        compiler_params=params(4),
        cost_estimate=COST,
        name="tie",
    )(array, *after)


def mix_kernel(*refs):
    near_ref, other_ref, outs = refs[0], refs[1], refs[2:]
    for index, ref in enumerate(outs):
        ref[0] = near_ref[index]
        ref[1] = other_ref[index]


def mix(near, other):
    count, each, width = near.shape
    return pl.pallas_call(
        mix_kernel,
        out_shape=tuple([jax.ShapeDtypeStruct((2, each, width), BF16)] * count),
        in_specs=[VMEM, VMEM],
        out_specs=tuple([VMEM] * count),
        compiler_params=params(16),
        cost_estimate=COST,
        name="mix",
    )(near, other)


def joined(refs, pieces, pick):
    values = [pick(refs[which], start, count) for which, start, count in pieces]
    flat = [value.reshape(-1, value.shape[-1]) for value in values]
    return jnp.concatenate(flat, axis=0)


def put(quarter, value, outs):
    own_ref, x_ref, y_ref, x_later_ref, y_later_ref = outs
    value = value.astype(BF16).reshape(own_ref.shape)
    half = x_ref.shape[0] // 2
    if quarter == 0:
        own_ref[...] = value
    elif quarter == 1:
        x_ref[half:] = value[:half]
        x_later_ref[...] = value[half:]
    elif quarter == 2:
        y_ref[half:] = value[half:]
        y_later_ref[...] = value[:half]
    else:
        x_ref[:half] = value[:half]
        y_ref[:half] = value[half:]


def emit(quarter, value, arrived, outs):
    if arrived is None:
        outs[0][quarter] = value.astype(BF16).reshape(outs[0].shape[1:])
    else:
        put(quarter, value + arrived[quarter].reshape(value.shape).astype(F32), outs)


def down_grad_kernel(side, act_pieces, add, *refs):
    count = 3
    acts, back_ref = refs[:count], refs[count]
    arrived = refs[count + 1] if add else None
    outs = refs[count + 2:] if add else refs[count + 1:]
    for quarter in (3, 1, 2, 0):
        act = joined(acts, act_pieces[quarter], lambda ref, a, n: ref[side, a:a + n])
        emit(quarter, dot_nn(act, back_ref[...]), arrived, outs)


def up_grad_kernel(side, weight_pieces, act_pieces, add, *refs):
    weights, slopes = refs[:5], refs[5:8]
    back_t_ref, normed_ref, gain_in = refs[8:11]
    arrived = refs[11] if add else None
    outs, gain_ref = refs[12 if add else 11:-1], refs[-1]
    gain_ref[...] = gain_in[...]
    for quarter in (3, 1, 2, 0):
        pieces = weight_pieces[quarter]
        slope = joined(slopes, act_pieces[quarter], lambda ref, a, n: ref[side, a:a + n])
        back_act = dot_nn(joined(weights, pieces, lambda ref, a, n: ref[a:a + n, 1]), back_t_ref[...])
        back_hidden = (back_act * slope).astype(BF16)
        grad = dot_nn(back_hidden, normed_ref[...])
        up = joined(weights, pieces, lambda ref, a, n: ref[a:a + n, 0]).astype(F32)
        gain_ref[...] += jnp.sum(grad * up, axis=0, keepdims=True)
        emit(quarter, grad, arrived, outs)


def gradient_shapes(depth, part, width, add):
    if not add:
        return [jax.ShapeDtypeStruct((4, depth, part, width), BF16)]
    counts = (depth, depth, depth, depth - depth // 2, depth // 2)
    return [jax.ShapeDtypeStruct((count, part, width), BF16) for count in counts]


def down_gradient(side, act_pieces, depth, acts, back, arrived=None):
    part = acts[0].shape[2]
    width = back.shape[1]
    add = arrived is not None
    operands = [*acts, back] + ([arrived] if add else [])
    shapes = gradient_shapes(depth, part, width, add)
    return pl.pallas_call(
        functools.partial(down_grad_kernel, side, act_pieces, add),
        out_shape=tuple(shapes),
        in_specs=[VMEM] * len(operands),
        out_specs=tuple([VMEM] * len(shapes)),
        compiler_params=params(20),
        cost_estimate=COST,
        name="down_gradient",
    )(*operands)


def up_gradient(
    side, weight_pieces, act_pieces, depth, weights, slopes, back_t, normed, gain, arrived=None
):
    part, width = weights[0].shape[2:]
    add = arrived is not None
    operands = [*weights, *slopes, back_t, normed, gain] + ([arrived] if add else [])
    shapes = gradient_shapes(depth, part, width, add) + [jax.ShapeDtypeStruct((1, width), F32)]
    return pl.pallas_call(
        functools.partial(up_grad_kernel, side, weight_pieces, act_pieces, add),
        out_shape=tuple(shapes),
        in_specs=[VMEM] * len(operands),
        out_specs=tuple([VMEM] * len(shapes)),
        compiler_params=params(24),
        cost_estimate=COST,
        name="up_gradient",
    )(*operands)


def merge_kernel(x_ref, y_ref, x_later_ref, y_later_ref, x_out, y_out):
    half = y_later_ref.shape[0]
    x_out[...] = (x_later_ref[...].astype(F32) + y_ref[:half].astype(F32)).astype(BF16)
    y_out[...] = (y_later_ref[...].astype(F32) + x_ref[:half].astype(F32)).astype(BF16)


def merge(x, y, x_later, y_later):
    return pl.pallas_call(
        merge_kernel,
        out_shape=tuple(jax.ShapeDtypeStruct(a.shape, BF16) for a in (x_later, y_later)),
        in_specs=[VMEM] * 4,
        out_specs=(VMEM, VMEM),
        compiler_params=params(16),
        cost_estimate=COST,
        name="merge",
    )(x, y, x_later, y_later)


def total_kernel(own_ref, x_ref, y_ref, x_late_ref, y_late_ref, *outs):
    half = y_late_ref.shape[0]
    for index, out in enumerate(outs):
        total = own_ref[index].astype(F32)
        if index < half:
            total += x_ref[half + index].astype(F32) + y_late_ref[index].astype(F32)
        else:
            total += y_ref[index].astype(F32) + x_late_ref[index - half].astype(F32)
        out[...] = total.astype(BF16)


def totals(own, x, y, x_late, y_late):
    count, part, width = own.shape
    return pl.pallas_call(
        total_kernel,
        out_shape=tuple([jax.ShapeDtypeStruct((part, width), BF16)] * count),
        in_specs=[VMEM] * 5,
        out_specs=tuple([VMEM] * count),
        compiler_params=params(16),
        cost_estimate=COST,
        name="totals",
    )(own, x, y, x_late, y_late)


def collect_kernel(count, *refs):
    out_ref = refs[-1]
    part, width = refs[0].shape
    total = refs[0][...].astype(F32)
    for ref in refs[1:count]:
        total = total + ref[...].astype(F32)
    out_ref[pl.ds(0, part), :] = total.astype(BF16)
    if len(refs) > count + 1:
        rest = refs[count][...]
        pieces = []
        for _ in range(3):
            piece = rest.astype(BF16).astype(F32)
            pieces.append(piece)
            rest = rest - piece
        pieces.append(jnp.zeros_like(rest))
        out_ref[pl.ds(part, 32), :] = jnp.concatenate(pieces, axis=0).astype(BF16)


def collect(parts, vector=None):
    part, width = parts[0].shape
    operands = list(parts) + ([] if vector is None else [vector])
    return pl.pallas_call(
        functools.partial(collect_kernel, len(parts)),
        out_shape=jax.ShapeDtypeStruct((part + (0 if vector is None else 32), width), BF16),
        in_specs=[VMEM] * len(operands),
        out_specs=VMEM,
        compiler_params=params(16),
        cost_estimate=COST,
        name="collect",
    )(*operands)


def place_kernel(part, group_ref, a_ref, b_ref, c_ref, d_ref, *refs):
    group = group_ref[0]
    held_ref = refs[-1]
    quarters = (a_ref, b_ref, c_ref, d_ref)
    for index, ref in enumerate(quarters):
        first = pl.multiple_of(jnp.bitwise_xor(group, index) * part, part)
        held_ref[pl.ds(first, part), :] = ref[pl.ds(0, part), :].astype(F32)
    if len(refs) == 2:
        refs[0][...] = held_ref[...]
        return
    refs[0][...] = held_ref[...].T
    vectors = []
    for ref in quarters:
        rows = ref[pl.ds(part, 32), :].astype(F32)
        vectors.append((rows[0:8] + rows[8:16]) + rows[16:24])
    refs[1][...] = (vectors[0] + vectors[1]) + (vectors[2] + vectors[3])


def place_quarters(group, quarters, part, vector):
    width = quarters[0].shape[1]
    if vector:
        shapes = [
            jax.ShapeDtypeStruct((width, 4 * part), F32), jax.ShapeDtypeStruct((8, width), F32)
        ]
    else:
        shapes = [jax.ShapeDtypeStruct((4 * part, width), F32)]
    return pl.pallas_call(
        functools.partial(place_kernel, part),
        out_shape=tuple(shapes),
        in_specs=[SMEM] + [VMEM] * 4,
        out_specs=tuple([VMEM] * len(shapes)),
        scratch_shapes=[pltpu.VMEM((4 * part, width), F32)],
        compiler_params=params(16),
        cost_estimate=COST,
        name="place",
    )(group, *quarters)


def shards_square(
    image_tokens,
    tile_lists,
    opacity,
    tile_counts,
    ray_pixel,
    block_owner,
    gaussian_features,
    layer_norm_gain,
    layer_scale,
    up_weight,
    down_weight,
):
    ray_count = lax.axis_size("ray")
    group_count = lax.axis_size("grp")
    depth = ray_count // 2
    group = lax.axis_index("grp").reshape(1)
    me = lax.axis_index("ray").reshape(1)
    rows, width = image_tokens.shape
    part = down_weight.shape[0] // group_count

    def beside(array, flip):
        return lax.ppermute(array, "grp", [(g, g ^ flip) for g in range(group_count)])

    def partner(array, flip=1):
        return lax.ppermute(array, "ray", [(r, r ^ flip) for r in range(ray_count)])

    def along(array, shift):
        pairs = [(r, (r + 2 * shift) % ray_count) for r in range(ray_count)]
        return lax.ppermute(array, "ray", pairs)

    mine = own_quarter(group, up_weight, down_weight, part)
    arrivals = [along(mine, -shift) for shift in range(1, depth)]
    x, y = beside(mine, 1), beside(mine, 2)

    rendered, rendered_other = render(
        ray_count, True, me, block_owner, tile_lists, opacity, tile_counts.reshape(1, rows),
        ray_pixel, gaussian_features,
    )
    first, far = pack(mine, x, y, arrivals, rendered)
    x_far, y_far = beside(far, 1), beside(far, 2)
    blocks = mix(rendered, partner(rendered_other))
    targets = [blocks[0]] + [along(blocks[shift], shift) for shift in range(1, depth)]
    first_other = partner(first)
    tokens, normed, normed_t = prepare_tokens(
        ray_count, True, me, block_owner, ray_pixel, image_tokens,
        layer_norm_gain.reshape(1, width),
    )
    act_first, slope_first, mixed = forward(normed_t, [first], [first_other])
    passed_x, passed_y = turn(y, y_far, x_far, mixed)
    d_low, d_high = beside(passed_x, 1), beside(passed_y, 2)
    x_other, y_other = partner(x_far), partner(y_far)
    act_next, slope_next, mixed = forward(normed_t, [x_far, y_far], [x_other, y_other], mixed)
    d_low, d_high = tie(d_low, mixed, *targets[1:]), tie(d_high, mixed, *targets[1:])
    low_other, high_other = partner(d_low), partner(d_high)
    act_last, slope_last, back, back_t, small = forward(
        normed_t, [d_low, d_high], [low_other, high_other], mixed,
        (tokens, layer_scale.reshape(1, width), *targets),
    )
    acts = (act_first, act_next, act_last)
    slopes = (slope_first, slope_next, slope_last)
    weights = (
        (first, x_far, y_far, d_low, d_high),
        (first_other, x_other, y_other, low_other, high_other),
    )
    low = d_low.shape[0]
    act_pieces = (
        ((0, 0, 1), (0, 3, depth - 1)),
        ((0, 1, 1), (1, 0, depth - 1)),
        ((0, 2, 1), (1, depth - 1, depth - 1)),
        ((2, 0, depth),),
    )
    weight_pieces = (
        ((0, 0, 1), (0, 3, depth - 1)),
        ((0, 1, 1), (1, 0, depth - 1)),
        ((0, 2, 1), (2, 0, depth - 1)),
        ((3, 0, low), (4, 0, depth - low)),
    )
    gain = jnp.zeros((1, width), F32)
    (down_other,) = down_gradient(1, act_pieces, depth, acts, back)
    down_arrived = partner(down_other)
    up_other, gain = up_gradient(
        1, weight_pieces, act_pieces, depth, weights[1], slopes, back_t, normed, gain
    )
    up_arrived = partner(up_other)
    down_sums = down_gradient(0, act_pieces, depth, acts, back, down_arrived)
    *up_sums, gain = up_gradient(
        0, weight_pieces, act_pieces, depth, weights[0], slopes, back_t, normed, gain, up_arrived
    )

    def sum_beside(own, to_x, to_y, x_later, y_later):
        from_x, from_y = beside(to_x, 1), beside(to_y, 2)
        x_later, y_later = merge(from_x, from_y, x_later, y_later)
        return totals(own, from_x, from_y, beside(x_later, 1), beside(y_later, 2))

    def sum_along(shares, *vector):
        arrivals = [along(shares[shift], shift) for shift in range(1, depth)]
        total = collect([shares[0]] + arrivals, *vector)
        return [total] + [beside(total, flip) for flip in (1, 2, 3)]

    vector = jnp.concatenate(
        [gain / layer_norm_gain.reshape(1, width), small[:2], jnp.zeros((5, width), F32)], axis=0
    )
    vector = vector + partner(vector)
    flip = 2
    while flip < ray_count:
        vector = vector + partner(vector, flip)
        flip *= 2
    quarters = sum_along(sum_beside(*down_sums))
    (grad_down,) = place_quarters(group, quarters, part, False)
    quarters = sum_along(sum_beside(*up_sums), vector)
    grad_up, vector = place_quarters(group, quarters, part, True)
    loss = vector[2, 0] / (rows * ray_count * group_count)
    return (grad_up, grad_down, vector[0], vector[1], loss)


def shards(*operands):
    ray_count, group_count = lax.axis_size("ray"), lax.axis_size("grp")
    hidden = operands[-1].shape[0]
    square = group_count == 4 and ray_count in (4, 8, 16) and hidden % (16 * group_count) == 0
    return (shards_square if square else shards_general)(*operands)


def solution(mesh):
    return jax.shard_map(
        shards,
        mesh=mesh,
        in_specs=(
            P(("grp", "ray"), None),
            P(None, ("grp", "ray")),
            P(None, ("grp", "ray")),
            P(("grp", "ray")),
            P("grp", None),
            P("grp", None),
            P(("grp", "ray"), None),
            P(),
            P(),
            P(None, "ray"),
            P("ray", None),
        ),
        out_specs=(P(None, "ray"), P("ray", None), P(), P(), P()),
        check_vma=False,
    )
```

```python
import functools

import jax
import jax.numpy as jnp
from jax import lax
from jax.experimental import pallas as pl
from jax.experimental.pallas import tpu as pltpu
from jax.sharding import PartitionSpec as P

STABILITY_EPSILON = 1e-06
F32 = jnp.float32
BF16 = jnp.bfloat16
MIB = 1024 * 1024
COST = pl.CostEstimate(flops=1 << 20, bytes_accessed=1 << 16, transcendentals=0)
LONG = pl.CostEstimate(flops=10**10, bytes_accessed=1 << 20, transcendentals=0)
SMEM = pl.BlockSpec(memory_space=pltpu.SMEM)
VMEM = pl.BlockSpec(memory_space=pltpu.VMEM)
ANY = pl.BlockSpec(memory_space=pl.ANY)


def params(mib=48, **more):
    return pltpu.CompilerParams(vmem_limit_bytes=mib * MIB, **more)


def dot_nn(a, b):
    return lax.dot_general(a, b, (((1,), (0,)), ((), ())), preferred_element_type=F32)


def dot_tn(a, b):
    return lax.dot_general(a, b, (((0,), (0,)), ((), ())), preferred_element_type=F32)


def dot_nt(a, b):
    return lax.dot_general(a, b, (((1,), (1,)), ((), ())), preferred_element_type=F32)


def owner_of(pixels, owner_ref, rows, count):
    block = lax.div(pixels, jnp.int32(rows))
    owner = jnp.zeros_like(pixels)
    for slot in range(count):
        owner = jnp.where(block == slot, owner_ref[0:1, slot:slot + 1], owner)
    return owner


def earlier(rows):
    before = lax.broadcasted_iota(jnp.int32, (rows, rows), 0)
    after = lax.broadcasted_iota(jnp.int32, (rows, rows), 1)
    return jnp.where(before < after, 1.0, 0.0).astype(BF16)


HBM = pl.BlockSpec(memory_space=pltpu.HBM)


def fetch(copies, sems):
    started = [
        pltpu.make_async_copy(source, target, sems.at[index])
        for index, (source, target) in enumerate(copies)
    ]
    for copy in started:
        copy.start()

    def wait(*numbers):
        for number in numbers:
            started[number].wait()

    return wait


def render_kernel(
    ray_count, relative, me_ref, owner_hbm, lists_hbm, opacity_hbm, counts_hbm, pixels_hbm,
    features_hbm, near_ref, other_ref, owner_ref, ids_ref, opacity_ref, counts_ref, mine_ref,
    features_ref, share_ref, table_ref, send_ref, sems,
):
    depth, rays = lists_hbm.shape
    gauss = features_hbm.shape[0]
    width = features_hbm.shape[1]
    me = me_ref[0]
    own_pixels = pixels_hbm.at[:, pl.ds(pl.multiple_of(me * rays, rays), rays)]
    wait = fetch(
        [
            (lists_hbm, ids_ref), (opacity_hbm, opacity_ref), (counts_hbm, counts_ref),
            (owner_hbm, owner_ref), (own_pixels, mine_ref), (features_hbm, features_ref),
        ],
        sems,
    )
    wait(0, 1, 2)
    ids_ref[...] = ids_ref[...] - me * gauss
    passing = jnp.ones((1, rays), F32)
    counts = counts_ref[...]
    for level in range(depth):
        alpha = opacity_ref[pl.ds(level, 1), :]
        share_ref[pl.ds(level, 1), :] = jnp.where(level < counts, alpha * passing, 0.0)
        passing = passing * (1.0 - alpha)

    tile = 128
    lanes = 128
    columns = rays // lanes

    @pl.loop(0, (gauss // tile) * columns)
    def _(step):
        first = pl.multiple_of(lax.div(step, columns) * tile, tile)
        lane = pl.multiple_of(lax.rem(step, columns) * lanes, lanes)
        number = lax.broadcasted_iota(jnp.int32, (tile, lanes), 0) + first
        total = jnp.zeros((tile, lanes), F32)
        for level in range(depth):
            ident = ids_ref[pl.ds(level, 1), pl.ds(lane, lanes)]
            share = share_ref[pl.ds(level, 1), pl.ds(lane, lanes)]
            total = total + jnp.where(ident == number, share, 0.0)
        table_ref[pl.ds(first, tile), pl.ds(lane, lanes)] = total.astype(BF16)

    wait(3, 4, 5)
    owner = owner_of(mine_ref[...], owner_ref, rays, ray_count)
    padded = -(-ray_count // 16) * 16
    member = (lax.broadcasted_iota(jnp.int32, (padded, rays), 0) == owner)
    ranks = dot_nn(member.astype(F32).astype(BF16), earlier(rays))
    rank = jnp.sum(jnp.where(member, ranks, 0.0), axis=0, keepdims=True).astype(jnp.int32)
    if relative:
        chips = ray_count // 2
        shift = lax.div(owner, jnp.int32(2)) - lax.div(me, jnp.int32(2))
        shift = jnp.where(shift < 0, shift + chips, shift)
        flip = jnp.where(lax.rem(owner, jnp.int32(2)) == lax.rem(me, jnp.int32(2)), 0, 1)
        block = flip * chips + shift
    else:
        block = owner
    slot = block * (rays // ray_count) + rank
    send_ref[...] = (
        (lax.broadcasted_iota(jnp.int32, (rays, rays), 0) == slot).astype(F32).astype(BF16)
    )

    piece = 256
    half = rays // 2

    @pl.loop(0, width // piece)
    def _(step):
        cols = pl.ds(pl.multiple_of(step * piece, piece), piece)
        rendered = dot_tn(table_ref[...], features_ref[:, cols]).astype(BF16)
        ordered = dot_nn(send_ref[...], rendered).astype(BF16)
        near_ref[:, :, cols] = ordered[:half].reshape(*near_ref.shape[:2], piece)
        other_ref[:, :, cols] = ordered[half:].reshape(*other_ref.shape[:2], piece)


def render(ray_count, relative, me, owner, lists, opacity, counts, pixels, features):
    depth, rays = lists.shape
    gauss, width = features.shape
    shape = jax.ShapeDtypeStruct((ray_count // 2, rays // ray_count, width), BF16)
    return pl.pallas_call(
        functools.partial(render_kernel, ray_count, relative),
        out_shape=(shape, shape),
        in_specs=[SMEM] + [HBM] * 6,
        out_specs=(VMEM, VMEM),
        scratch_shapes=[
            pltpu.VMEM(owner.shape, jnp.int32),
            pltpu.VMEM((depth, rays), jnp.int32),
            pltpu.VMEM((depth, rays), F32),
            pltpu.VMEM((1, rays), jnp.int32),
            pltpu.VMEM((1, rays), jnp.int32),
            pltpu.VMEM((gauss, width), BF16),
            pltpu.VMEM((depth, rays), F32),
            pltpu.VMEM((gauss, rays), BF16),
            pltpu.VMEM((rays, rays), BF16),
            pltpu.SemaphoreType.DMA((6,)),
        ],
        compiler_params=params(20),
        cost_estimate=COST,
        name="render",
    )(me, owner, lists, opacity, counts, pixels, features)


def tokens_kernel(
    ray_count, relative, me_ref, owner_hbm, pixels_hbm, tokens_hbm, gain_hbm,
    *refs,
):
    tokens_out, normed_out, normed_t_out = refs[-11:-8]
    owner_ref, pixels_ref, tokens_ref, gain_ref, order_ref, rank_ref, place_ref, sems = refs[-8:]
    rows, width = tokens_hbm.shape
    me = me_ref[0]
    each = rows // ray_count
    wait = fetch(
        [
            (owner_hbm, owner_ref), (pixels_hbm, pixels_ref), (gain_hbm, gain_ref),
            (tokens_hbm, tokens_ref),
        ],
        sems,
    )
    wait(0, 1)
    pixels = jnp.concatenate(
        [pixels_ref[:, sender * rows:(sender + 1) * rows] for sender in range(ray_count)], axis=0
    )
    mine = owner_of(pixels, owner_ref, rows, ray_count) == me
    place_ref[...] = lax.rem(pixels, jnp.int32(rows)).astype(F32)
    member = jnp.where(mine, 1.0, 0.0)
    padded = -(-ray_count // 16) * 16
    if padded > ray_count:
        spread = jnp.concatenate([member, jnp.zeros((padded - ray_count, rows), F32)], axis=0)
    else:
        spread = member
    ranks = dot_nn(spread.astype(BF16), earlier(rows))
    rank_ref[...] = jnp.where(mine, ranks[:ray_count], -1.0)
    chips = ray_count // 2
    for index in range(ray_count):
        if relative:
            chip = lax.rem(lax.div(me, jnp.int32(2)) + (chips - index // 2), jnp.int32(chips))
            sender = 2 * chip + jnp.bitwise_xor(lax.rem(me, jnp.int32(2)), index % 2)
        else:
            sender = index
        rank = rank_ref[pl.ds(sender, 1), :].astype(jnp.int32)
        hit = lax.broadcasted_iota(jnp.int32, (each, rows), 0) == rank
        at = jnp.sum(
            jnp.where(hit, place_ref[pl.ds(sender, 1), :], 0.0), axis=1, keepdims=True
        )
        here = lax.broadcasted_iota(jnp.int32, (each, rows), 1) == at.astype(jnp.int32)
        order_ref[pl.ds(index * each, each), :] = here.astype(F32).astype(BF16)
    wait(2, 3)
    half = min(128, rows)
    gain = gain_ref[...]

    @pl.loop(0, rows // half)
    def _(step):
        span = pl.ds(pl.multiple_of(step * half, half), half)
        values = dot_nn(order_ref[span, :], tokens_ref[...])
        tokens_out[span, :] = values.astype(BF16)
        centered = values - jnp.mean(values, axis=-1, keepdims=True)
        variance = jnp.mean(centered * centered, axis=-1, keepdims=True)
        xhat = centered * lax.rsqrt(variance + STABILITY_EPSILON)
        normed = (xhat * gain).astype(BF16)
        normed_out[span, :] = normed
        normed_t_out[:, span] = normed.T


def prepare_tokens(ray_count, relative, me, owner, pixels, tokens, gain, after=()):
    rows, width = tokens.shape
    return pl.pallas_call(
        functools.partial(tokens_kernel, ray_count, relative),
        out_shape=(
            jax.ShapeDtypeStruct((rows, width), BF16),
            jax.ShapeDtypeStruct((rows, width), BF16),
            jax.ShapeDtypeStruct((width, rows), BF16),
        ),
        in_specs=[SMEM] + [HBM] * 4 + [ANY] * len(after),
        out_specs=(VMEM, VMEM, VMEM),
        scratch_shapes=[
            pltpu.VMEM(owner.shape, jnp.int32),
            pltpu.VMEM(pixels.shape, jnp.int32),
            pltpu.VMEM((rows, width), BF16),
            pltpu.VMEM((1, width), F32),
            pltpu.VMEM((rows, rows), BF16),
            pltpu.VMEM((ray_count, rows), F32),
            pltpu.VMEM((ray_count, rows), F32),
            pltpu.SemaphoreType.DMA((4,)),
        ],
        compiler_params=params(20),
        cost_estimate=COST,
        name="tokens",
    )(me, owner, pixels, tokens, gain, *after)


def up_kernel(normed_ref, up_ref, act_ref, slope_ref):
    parts, _, part_rows, width = up_ref.shape
    up = up_ref[...].reshape(parts * part_rows, width)
    rows = normed_ref.shape[0]
    piece = min(128, rows)

    @pl.loop(0, rows // piece)
    def _(step):
        span = pl.ds(pl.multiple_of(step * piece, piece), piece)
        hidden = dot_nn(normed_ref[span, :], up)
        phi = 0.5 * (1.0 + lax.erf(hidden * (0.5 ** 0.5)))
        density = jnp.exp(-0.5 * hidden * hidden) * ((2.0 * jnp.pi) ** -0.5)
        act_ref[span, :] = (hidden * phi).astype(BF16)
        slope_ref[span, :] = (phi + hidden * density).astype(slope_ref.dtype)


def project_up(normed, up):
    rows, width = normed.shape
    parts, chunks, part_rows, chunk = up.shape
    return pl.pallas_call(
        up_kernel,
        grid=(chunks,),
        out_shape=(
            jax.ShapeDtypeStruct((rows, chunks * chunk), BF16),
            jax.ShapeDtypeStruct((rows, chunks * chunk), F32),
        ),
        in_specs=[
            pl.BlockSpec((rows, width), lambda j: (0, 0)),
            pl.BlockSpec((parts, 1, part_rows, chunk), lambda j: (0, j, 0, 0)),
        ],
        out_specs=(
            pl.BlockSpec((rows, chunk), lambda j: (0, j)),
            pl.BlockSpec((rows, chunk), lambda j: (0, j)),
        ),
        compiler_params=params(dimension_semantics=("arbitrary",)),
        cost_estimate=COST,
        name="up",
    )(normed, up)


def down_kernel(
    chunks, act_ref, down_ref, tokens_ref, target_ref, scale_ref,
    grad_ref, back_ref, small_ref, mixed_ref,
):
    step = pl.program_id(0)
    rows, width = tokens_ref.shape
    act = act_ref[...]

    @pl.when(step < chunks)
    def _():
        parts, _, part_rows, _ = down_ref.shape
        part = dot_nn(act, down_ref[...].reshape(parts * part_rows, width))

        @pl.when(step == 0)
        def _():
            mixed_ref[...] = part

        @pl.when(step > 0)
        def _():
            mixed_ref[...] += part

    @pl.when(step == chunks - 1)
    def _():
        scale = scale_ref[...]
        small_ref[...] = jnp.zeros_like(small_ref)
        piece = min(64, rows)

        @pl.loop(0, rows // piece)
        def _(index):
            span = pl.ds(pl.multiple_of(index * piece, piece), piece)
            mixed = mixed_ref[span, :]
            out = tokens_ref[span, :].astype(F32) + scale * mixed
            goal = target_ref[span, :].astype(F32)
            out_norm = jnp.sqrt(jnp.sum(out * out, axis=-1, keepdims=True) + STABILITY_EPSILON)
            goal_norm = jnp.sqrt(jnp.sum(goal * goal, axis=-1, keepdims=True) + STABILITY_EPSILON)
            norms = out_norm * goal_norm
            cosine = jnp.sum(out * goal, axis=-1, keepdims=True) / norms
            upstream = (cosine / (out_norm * out_norm)) * out - goal * (1.0 / norms)
            back_ref[span, :] = (upstream * scale).astype(BF16)
            small_ref[0:1, :] += jnp.sum(upstream * mixed, axis=0, keepdims=True)
            loss = jnp.sum(1.0 - cosine, axis=0, keepdims=True)
            small_ref[1:2, :] += jnp.broadcast_to(loss, (1, width))

    @pl.when(step >= chunks)
    def _():
        grad = dot_tn(act, back_ref[...])
        grad_ref[...] = grad.astype(BF16).reshape(grad_ref.shape)


def project_down(act, down, tokens, target, scale):
    rows, width = tokens.shape
    parts, chunks, part_rows, _ = down.shape
    chunk = parts * part_rows
    return pl.pallas_call(
        functools.partial(down_kernel, chunks),
        grid=(2 * chunks,),
        out_shape=(
            jax.ShapeDtypeStruct(down.shape, BF16),
            jax.ShapeDtypeStruct((rows, width), BF16),
            jax.ShapeDtypeStruct((8, width), F32),
        ),
        in_specs=[
            pl.BlockSpec((rows, chunk), lambda j: (0, lax.rem(j, chunks))),
            pl.BlockSpec(
                (parts, 1, part_rows, width), lambda j: (0, jnp.minimum(j, chunks - 1), 0, 0)
            ),
            pl.BlockSpec((rows, width), lambda j: (0, 0)),
            pl.BlockSpec((rows, width), lambda j: (0, 0)),
            pl.BlockSpec((1, width), lambda j: (0, 0)),
        ],
        out_specs=(
            pl.BlockSpec(
                (parts, 1, part_rows, width), lambda j: (0, jnp.maximum(j - chunks, 0), 0, 0)
            ),
            pl.BlockSpec((rows, width), lambda j: (0, 0)),
            pl.BlockSpec((8, width), lambda j: (0, 0)),
        ),
        scratch_shapes=[pltpu.VMEM((rows, width), F32)],
        compiler_params=params(dimension_semantics=("arbitrary",)),
        cost_estimate=COST,
        name="down",
    )(act, down, tokens, target, scale)


def back_kernel(back_ref, down_ref, slope_ref, normed_t_ref, up_ref, gain_ref, grad_ref, sum_ref):
    step = pl.program_id(0)
    parts, _, part_rows, width = down_ref.shape
    chunk = parts * part_rows
    rows = back_ref.shape[0]
    back_act = dot_nt(back_ref[...], down_ref[...].reshape(chunk, width))
    back_hidden = (back_act * slope_ref[...]).astype(BF16)
    up_parts, _, up_rows, _ = up_ref.shape

    @pl.when(step == 0)
    def _():
        sum_ref[...] = jnp.zeros_like(sum_ref)

    grad = dot_nn(normed_t_ref[...], back_hidden)
    grad_ref[...] = grad.astype(BF16).reshape(grad_ref.shape)
    up = up_ref[...].reshape(up_parts * up_rows, chunk).astype(F32)
    sum_ref[...] += jnp.sum(grad * up, axis=1, keepdims=True) / gain_ref[...]


def back_up(back, down, slope, normed_t, up, gain):
    width, rows = normed_t.shape
    parts, chunks, part_rows, _ = down.shape
    chunk = parts * part_rows
    up_parts, _, up_rows, _ = up.shape
    return pl.pallas_call(
        back_kernel,
        grid=(chunks,),
        out_shape=(
            jax.ShapeDtypeStruct(up.shape, BF16),
            jax.ShapeDtypeStruct((width, 1), F32),
        ),
        in_specs=[
            pl.BlockSpec((rows, width), lambda j: (0, 0)),
            pl.BlockSpec((parts, 1, part_rows, width), lambda j: (0, j, 0, 0)),
            pl.BlockSpec((rows, chunk), lambda j: (0, j)),
            pl.BlockSpec((width, rows), lambda j: (0, 0)),
            pl.BlockSpec((up_parts, 1, up_rows, chunk), lambda j: (0, j, 0, 0)),
            pl.BlockSpec((width, 1), lambda j: (0, 0)),
        ],
        out_specs=(
            pl.BlockSpec((up_parts, 1, up_rows, chunk), lambda j: (0, j, 0, 0)),
            pl.BlockSpec((width, 1), lambda j: (0, 0)),
        ),
        compiler_params=params(dimension_semantics=("arbitrary",)),
        cost_estimate=COST,
        name="back",
    )(back, down, slope, normed_t, up, gain)


def gather_weight(weight, parts, group, group_count, ray_count):
    rows, cols = weight.shape
    if parts == 1:
        whole = lax.all_gather(weight, "ray", axis=0, tiled=True)
    else:
        part = lax.dynamic_slice_in_dim(weight, group * (rows // parts), rows // parts, 0)
        whole = lax.all_gather(part, ("grp", "ray"), axis=0, tiled=True)
    return whole.reshape(parts, ray_count, rows // parts, cols)


def reduce_gradient(grad):
    parts, ray_count, part_rows, cols = grad.shape
    flat = grad.reshape(parts * ray_count * part_rows, cols)
    if parts == 1:
        share = lax.psum_scatter(flat, "ray", scatter_dimension=0, tiled=True)
        return lax.psum(share.astype(F32), "grp")
    share = lax.psum_scatter(flat, "grp", scatter_dimension=0, tiled=True)
    share = lax.psum_scatter(share, "ray", scatter_dimension=0, tiled=True)
    return lax.all_gather(share, "grp", axis=0, tiled=True).astype(F32)


def shards_general(
    image_tokens,
    tile_lists,
    opacity,
    tile_counts,
    ray_pixel,
    block_owner,
    gaussian_features,
    layer_norm_gain,
    layer_scale,
    up_weight,
    down_weight,
):
    ray_count = lax.axis_size("ray")
    group_count = lax.axis_size("grp")
    group = lax.axis_index("grp")
    me = lax.axis_index("ray").reshape(1)
    rows, width = image_tokens.shape
    up_parts = group_count if up_weight.shape[0] % (16 * group_count) == 0 else 1
    down_parts = group_count if down_weight.shape[0] % (16 * group_count) == 0 else 1
    up = gather_weight(up_weight, up_parts, group, group_count, ray_count)
    down = gather_weight(down_weight, down_parts, group, group_count, ray_count)
    rendered = render(
        ray_count, False, me, block_owner, tile_lists, opacity, tile_counts.reshape(1, rows),
        ray_pixel, gaussian_features,
    )
    rendered = jnp.concatenate(rendered, axis=0).reshape(rows, width)
    target = lax.all_to_all(rendered, "ray", split_axis=0, concat_axis=0, tiled=True)
    tokens, normed, normed_t = prepare_tokens(
        ray_count, False, me, block_owner, ray_pixel, image_tokens,
        layer_norm_gain.reshape(1, width),
    )
    act, slope = project_up(normed, up)
    grad_down, back, small = project_down(act, down, tokens, target, layer_scale.reshape(1, width))
    grad_up, gain_sum = back_up(back, down, slope, normed_t, up, layer_norm_gain.reshape(width, 1))
    grad_down = reduce_gradient(grad_down)
    grad_up = reduce_gradient(grad_up)
    sums = jnp.concatenate([gain_sum.reshape(1, width), small[:2]], axis=0)
    sums = lax.psum(sums, ("grp", "ray"))
    loss = sums[2, 0] / (rows * ray_count * group_count)
    return (grad_up, grad_down, sums[0], sums[1], loss)


def quarter_kernel(group_ref, up_hbm, down_hbm, out_ref, up_ref, turned_ref, sems):
    part = out_ref.shape[1]
    lanes = up_ref.shape[1]
    start = pl.multiple_of(group_ref[0] * part, part)
    lane = pl.multiple_of(lax.div(start, jnp.int32(lanes)) * lanes, lanes)
    wait = fetch(
        [
            (up_hbm.at[:, pl.ds(lane, lanes)], up_ref),
            (down_hbm.at[pl.ds(start, part), :], out_ref.at[1]),
        ],
        sems,
    )
    wait(0)
    turned_ref[...] = up_ref[...].T
    out_ref[0] = turned_ref[pl.ds(pl.multiple_of(start - lane, part), part), :]
    wait(1)


def own_quarter(group, up, down, part):
    width, chunk = up.shape
    lanes = max(128, part)
    return pl.pallas_call(
        quarter_kernel,
        out_shape=jax.ShapeDtypeStruct((2, part, width), BF16),
        in_specs=[SMEM, HBM, HBM],
        out_specs=VMEM,
        scratch_shapes=[
            pltpu.VMEM((width, lanes), BF16),
            pltpu.VMEM((lanes, width), BF16),
            pltpu.SemaphoreType.DMA((2,)),
        ],
        compiler_params=params(16),
        cost_estimate=LONG,
        name="quarter",
    )(group, up, down)


def finish_rows(tokens, mixed, goal, scale):
    out = tokens + scale * mixed
    out_norm = jnp.sqrt(jnp.sum(out * out, axis=-1, keepdims=True) + STABILITY_EPSILON)
    goal_norm = jnp.sqrt(jnp.sum(goal * goal, axis=-1, keepdims=True) + STABILITY_EPSILON)
    norms = out_norm * goal_norm
    cosine = jnp.sum(out * goal, axis=-1, keepdims=True) / norms
    upstream = (cosine / (out_norm * out_norm)) * out - goal * (1.0 / norms)
    return upstream, 1.0 - cosine


def forward_kernel(first, blocks, sides, *refs):
    last = blocks > 0
    refs = list(refs)
    normed_t_ref = refs.pop(0)
    own, other = refs[:sides], refs[sides:2 * sides]
    del refs[:2 * sides]
    mixed_in = None if first else refs.pop(0)
    if last:
        tokens_ref, scale_ref = refs[:2]
        targets = refs[2:2 + blocks]
        del refs[:2 + blocks]
    act_ref, slope_ref = refs[:2]
    del refs[:2]
    width, rows = normed_t_ref.shape
    total = act_ref.shape[1]
    part = act_ref.shape[2]
    downs = []
    for side, group in enumerate((own, other)):
        start = 0
        for ref in group:
            count = ref.shape[0]
            hiddens = dot_nn(ref[:, 0].reshape(count * part, width), normed_t_ref[...])
            for index in range(count):
                hidden = hiddens[index * part:(index + 1) * part]
                phi = 0.5 * (1.0 + lax.erf(hidden * (0.5 ** 0.5)))
                density = jnp.exp(-0.5 * hidden * hidden) * ((2.0 * jnp.pi) ** -0.5)
                act_ref[side, start + index] = (hidden * phi).astype(BF16)
                slope_ref[side, start + index] = phi + hidden * density
            downs.append(ref[:, 1].reshape(count * part, width))
            start += count
    act = act_ref[...].reshape(2 * total * part, rows)
    down = jnp.concatenate(downs, axis=0)
    if not last:
        mixed_out = refs[0]
        part_sum = dot_tn(act, down)
        mixed_out[...] = part_sum if first else mixed_in[...] + part_sum
        return
    back_ref, back_t_ref, small_ref, mixed_ref = refs
    mixed_ref[...] = mixed_in[...] + dot_tn(act, down)
    scale = scale_ref[...]
    small_ref[...] = jnp.zeros_like(small_ref)
    piece = rows // blocks
    for index, target_ref in enumerate(targets):
        span = pl.ds(index * piece, piece)
        mixed = mixed_ref[span, :]
        upstream, loss = finish_rows(
            tokens_ref[span, :].astype(F32), mixed,
            target_ref[...].reshape(piece, width).astype(F32), scale,
        )
        back = (upstream * scale).astype(BF16)
        back_ref[span, :] = back
        back_t_ref[:, span] = back.T
        small_ref[0:1, :] += jnp.sum(upstream * mixed, axis=0, keepdims=True)
        small_ref[1:2, :] += jnp.broadcast_to(jnp.sum(loss, axis=0, keepdims=True), (1, width))


def forward(normed_t, own, other, mixed=None, finish=None):
    width, rows = normed_t.shape
    part = own[0].shape[2]
    total = sum(array.shape[0] for array in own)
    first, last = mixed is None, finish is not None
    blocks = len(finish) - 2 if last else 0
    operands = [normed_t, *own, *other]
    if not first:
        operands.append(mixed)
    if last:
        operands.extend(finish)
    piece = (2, total, part, rows)
    shapes = [jax.ShapeDtypeStruct(piece, BF16), jax.ShapeDtypeStruct(piece, F32)]
    scratch = []
    if last:
        shapes += [
            jax.ShapeDtypeStruct((rows, width), BF16),
            jax.ShapeDtypeStruct((width, rows), BF16),
            jax.ShapeDtypeStruct((8, width), F32),
        ]
        scratch = [pltpu.VMEM((rows, width), F32)]
    else:
        shapes += [jax.ShapeDtypeStruct((rows, width), F32)]
    return pl.pallas_call(
        functools.partial(forward_kernel, first, blocks, len(own)),
        out_shape=tuple(shapes),
        in_specs=[VMEM] * len(operands),
        out_specs=tuple([VMEM] * len(shapes)),
        scratch_shapes=scratch,
        compiler_params=params(24),
        cost_estimate=COST,
        name="forward",
    )(*operands)


def pack_kernel(mine_ref, *refs):
    count = len(refs) - 5
    arrivals, (x_ref, y_ref) = refs[:count], refs[count:count + 2]
    all_ref, far_ref = refs[-2:]
    for index, ref in enumerate((mine_ref, x_ref, y_ref)):
        all_ref[index] = ref[...]
    for index, ref in enumerate(arrivals):
        block = ref[...]
        all_ref[3 + index] = block
        far_ref[index] = block


def pack(mine, x, y, arrivals, after):
    count = len(arrivals)
    return pl.pallas_call(
        pack_kernel,
        out_shape=(
            jax.ShapeDtypeStruct((3 + count, *mine.shape), BF16),
            jax.ShapeDtypeStruct((count, *mine.shape), BF16),
        ),
        in_specs=[VMEM] * (3 + count) + [ANY],
        out_specs=(VMEM, VMEM),
        compiler_params=params(16),
        cost_estimate=COST,
        name="pack",
    )(mine, *arrivals, x, y, after)


def turn_kernel(y_ref, y_far_ref, x_far_ref, after_ref, a_ref, b_ref):
    held = a_ref.shape[0] - 1
    a_ref[0] = y_ref[...]
    for index in range(held):
        a_ref[1 + index] = y_far_ref[index]
    for index in range(b_ref.shape[0]):
        b_ref[index] = x_far_ref[held + index]


def turn(y, y_far, x_far, after):
    count = y_far.shape[0]
    first = (count + 1) // 2
    return pl.pallas_call(
        turn_kernel,
        out_shape=(
            jax.ShapeDtypeStruct((first, *y.shape), BF16),
            jax.ShapeDtypeStruct((count + 1 - first, *y.shape), BF16),
        ),
        in_specs=[VMEM] * 3 + [ANY],
        out_specs=(VMEM, VMEM),
        compiler_params=params(16),
        cost_estimate=COST,
        name="turn",
    )(y, y_far, x_far, after)


def tie_kernel(*refs):
    pass


def tie(array, *after):
    return pl.pallas_call(
        tie_kernel,
        out_shape=jax.ShapeDtypeStruct(array.shape, array.dtype),
        in_specs=[ANY] * (1 + len(after)),
        out_specs=ANY,
        input_output_aliases={0: 0},
        compiler_params=params(4),
        cost_estimate=COST,
        name="tie",
    )(array, *after)


def mix_kernel(*refs):
    near_ref, other_ref, outs = refs[0], refs[1], refs[2:]
    for index, ref in enumerate(outs):
        ref[0] = near_ref[index]
        ref[1] = other_ref[index]


def mix(near, other):
    count, each, width = near.shape
    return pl.pallas_call(
        mix_kernel,
        out_shape=tuple([jax.ShapeDtypeStruct((2, each, width), BF16)] * count),
        in_specs=[VMEM, VMEM],
        out_specs=tuple([VMEM] * count),
        compiler_params=params(16),
        cost_estimate=COST,
        name="mix",
    )(near, other)


def joined(refs, pieces, pick):
    values = [pick(refs[which], start, count) for which, start, count in pieces]
    flat = [value.reshape(-1, value.shape[-1]) for value in values]
    return jnp.concatenate(flat, axis=0)


def put(quarter, value, outs):
    own_ref, x_ref, y_ref, x_later_ref, y_later_ref = outs
    value = value.astype(BF16).reshape(own_ref.shape)
    half = x_ref.shape[0] // 2
    if quarter == 0:
        own_ref[...] = value
    elif quarter == 1:
        x_ref[half:] = value[:half]
        x_later_ref[...] = value[half:]
    elif quarter == 2:
        y_ref[half:] = value[half:]
        y_later_ref[...] = value[:half]
    else:
        x_ref[:half] = value[:half]
        y_ref[:half] = value[half:]


def emit(quarter, value, arrived, outs):
    if arrived is None:
        outs[0][quarter] = value.astype(BF16).reshape(outs[0].shape[1:])
    else:
        put(quarter, value + arrived[quarter].reshape(value.shape).astype(F32), outs)


def down_grad_kernel(side, act_pieces, add, *refs):
    count = 3
    acts, back_ref = refs[:count], refs[count]
    arrived = refs[count + 1] if add else None
    outs = refs[count + 2:] if add else refs[count + 1:]
    for quarter in (3, 1, 2, 0):
        act = joined(acts, act_pieces[quarter], lambda ref, a, n: ref[side, a:a + n])
        emit(quarter, dot_nn(act, back_ref[...]), arrived, outs)


def up_grad_kernel(side, weight_pieces, act_pieces, add, *refs):
    weights, slopes = refs[:5], refs[5:8]
    back_t_ref, normed_ref, gain_in = refs[8:11]
    if add:
        arrived, scale_ref, small_ref = refs[11:14]
        outs, vector_ref, gain_ref = refs[14:-2], refs[-2], refs[-1]
    else:
        arrived = None
        outs, gain_ref = refs[11:-1], refs[-1]
    gain_ref[...] = gain_in[...]
    for quarter in (3, 1, 2, 0):
        pieces = weight_pieces[quarter]
        slope = joined(slopes, act_pieces[quarter], lambda ref, a, n: ref[side, a:a + n])
        back_act = dot_nn(joined(weights, pieces, lambda ref, a, n: ref[a:a + n, 1]), back_t_ref[...])
        back_hidden = (back_act * slope).astype(BF16)
        grad = dot_nn(back_hidden, normed_ref[...])
        up = joined(weights, pieces, lambda ref, a, n: ref[a:a + n, 0]).astype(F32)
        gain_ref[...] += jnp.sum(grad * up, axis=0, keepdims=True)
        emit(quarter, grad, arrived, outs)
    if add:
        vector_ref[0:1, :] = gain_ref[...] / scale_ref[...]
        vector_ref[1:3, :] = small_ref[0:2, :]
        vector_ref[3:8, :] = jnp.zeros((5, gain_ref.shape[1]), F32)


def gradient_shapes(depth, part, width, add):
    if not add:
        return [jax.ShapeDtypeStruct((4, depth, part, width), BF16)]
    counts = (depth, depth, depth, depth - depth // 2, depth // 2)
    return [jax.ShapeDtypeStruct((count, part, width), BF16) for count in counts]


def down_gradient(side, act_pieces, depth, acts, back, arrived=None):
    part = acts[0].shape[2]
    width = back.shape[1]
    add = arrived is not None
    operands = [*acts, back] + ([arrived] if add else [])
    shapes = gradient_shapes(depth, part, width, add)
    return pl.pallas_call(
        functools.partial(down_grad_kernel, side, act_pieces, add),
        out_shape=tuple(shapes),
        in_specs=[VMEM] * len(operands),
        out_specs=tuple([VMEM] * len(shapes)),
        compiler_params=params(20),
        cost_estimate=COST,
        name="down_gradient",
    )(*operands)


def up_gradient(
    side, weight_pieces, act_pieces, depth, weights, slopes, back_t, normed, gain, extra=()
):
    part, width = weights[0].shape[2:]
    add = len(extra) > 0
    operands = [*weights, *slopes, back_t, normed, gain, *extra]
    shapes = gradient_shapes(depth, part, width, add)
    if add:
        shapes.append(jax.ShapeDtypeStruct((8, width), F32))
        scratch = [pltpu.VMEM((1, width), F32)]
    else:
        scratch = []
        shapes.append(jax.ShapeDtypeStruct((1, width), F32))
    return pl.pallas_call(
        functools.partial(up_grad_kernel, side, weight_pieces, act_pieces, add),
        out_shape=tuple(shapes),
        in_specs=[VMEM] * len(operands),
        out_specs=tuple([VMEM] * len(shapes)),
        scratch_shapes=scratch,
        compiler_params=params(24),
        cost_estimate=COST,
        name="up_gradient",
    )(*operands)


def merge_kernel(x_ref, y_ref, x_later_ref, y_later_ref, *refs):
    x_out, y_out = refs[-2:]
    half = y_later_ref.shape[0]
    x_out[...] = (x_later_ref[...].astype(F32) + y_ref[:half].astype(F32)).astype(BF16)
    y_out[...] = (y_later_ref[...].astype(F32) + x_ref[:half].astype(F32)).astype(BF16)


def merge(x, y, x_later, y_later, *after):
    return pl.pallas_call(
        merge_kernel,
        out_shape=tuple(jax.ShapeDtypeStruct(a.shape, BF16) for a in (x_later, y_later)),
        in_specs=[VMEM] * 4 + [ANY] * len(after),
        out_specs=(VMEM, VMEM),
        compiler_params=params(16),
        cost_estimate=COST,
        name="merge",
    )(x, y, x_later, y_later, *after)


def total_kernel(own_ref, x_ref, y_ref, x_late_ref, y_late_ref, *outs):
    half = y_late_ref.shape[0]
    for index, out in enumerate(outs):
        total = own_ref[index].astype(F32)
        if index < half:
            total += x_ref[half + index].astype(F32) + y_late_ref[index].astype(F32)
        else:
            total += y_ref[index].astype(F32) + x_late_ref[index - half].astype(F32)
        out[...] = total.astype(BF16)


def totals(own, x, y, x_late, y_late):
    count, part, width = own.shape
    return pl.pallas_call(
        total_kernel,
        out_shape=tuple([jax.ShapeDtypeStruct((part, width), BF16)] * count),
        in_specs=[VMEM] * 5,
        out_specs=tuple([VMEM] * count),
        compiler_params=params(16),
        cost_estimate=COST,
        name="totals",
    )(own, x, y, x_late, y_late)


def collect_kernel(count, *refs):
    out_ref = refs[-1]
    part, width = refs[0].shape
    total = refs[0][...].astype(F32)
    for ref in refs[1:count]:
        total = total + ref[...].astype(F32)
    out_ref[pl.ds(0, part), :] = total.astype(BF16)
    if len(refs) > count + 1:
        out_ref[pl.ds(part, part), :] = refs[count + 1][...]
        rest = refs[count][...]
        pieces = []
        for _ in range(3):
            piece = rest.astype(BF16).astype(F32)
            pieces.append(piece)
            rest = rest - piece
        pieces.append(jnp.zeros_like(rest))
        out_ref[pl.ds(2 * part, 32), :] = jnp.concatenate(pieces, axis=0).astype(BF16)


def collect(parts, extra=()):
    part, width = parts[0].shape
    operands = list(parts) + list(extra)
    rows = 2 * part + 32 if extra else part
    return pl.pallas_call(
        functools.partial(collect_kernel, len(parts)),
        out_shape=jax.ShapeDtypeStruct((rows, width), BF16),
        in_specs=[VMEM] * len(operands),
        out_specs=VMEM,
        compiler_params=params(16),
        cost_estimate=COST,
        name="collect",
    )(*operands)


def place_kernel(part, tokens, group_ref, *refs):
    quarters = refs[:4]
    up_ref, down_ref, gain_ref, scale_ref, loss_ref, held_ref = refs[4:]
    group = group_ref[0]
    vectors = []
    for index, ref in enumerate(quarters):
        first = pl.multiple_of(jnp.bitwise_xor(group, index) * part, part)
        held_ref[pl.ds(first, part), :] = ref[pl.ds(0, part), :].astype(F32)
        down_ref[pl.ds(first, part), :] = ref[pl.ds(part, part), :].astype(F32)
        rows = ref[pl.ds(2 * part, 32), :].astype(F32)
        vectors.append((rows[0:8] + rows[8:16]) + rows[16:24])
    up_ref[...] = held_ref[...].T
    vector = (vectors[0] + vectors[1]) + (vectors[2] + vectors[3])
    gain_ref[...] = vector[0:1]
    scale_ref[...] = vector[1:2]
    loss_ref[...] = vector[2:3, 0:1] * (1.0 / tokens)


def place_quarters(group, quarters, part, tokens):
    width = quarters[0].shape[1]
    shapes = [
        jax.ShapeDtypeStruct((width, 4 * part), F32),
        jax.ShapeDtypeStruct((4 * part, width), F32),
        jax.ShapeDtypeStruct((1, width), F32),
        jax.ShapeDtypeStruct((1, width), F32),
        jax.ShapeDtypeStruct((1, 1), F32),
    ]
    return pl.pallas_call(
        functools.partial(place_kernel, part, tokens),
        out_shape=tuple(shapes),
        in_specs=[SMEM] + [VMEM] * 4,
        out_specs=tuple([VMEM] * len(shapes)),
        scratch_shapes=[pltpu.VMEM((4 * part, width), F32)],
        compiler_params=params(16),
        cost_estimate=COST,
        name="place",
    )(group, *quarters)


def shards_square(
    image_tokens,
    tile_lists,
    opacity,
    tile_counts,
    ray_pixel,
    block_owner,
    gaussian_features,
    layer_norm_gain,
    layer_scale,
    up_weight,
    down_weight,
):
    ray_count = lax.axis_size("ray")
    group_count = lax.axis_size("grp")
    depth = ray_count // 2
    group = lax.axis_index("grp").reshape(1)
    me = lax.axis_index("ray").reshape(1)
    rows, width = image_tokens.shape
    part = down_weight.shape[0] // group_count

    def beside(array, flip):
        return lax.ppermute(array, "grp", [(g, g ^ flip) for g in range(group_count)])

    def partner(array, flip=1):
        return lax.ppermute(array, "ray", [(r, r ^ flip) for r in range(ray_count)])

    def along(array, shift):
        pairs = [(r, (r + 2 * shift) % ray_count) for r in range(ray_count)]
        return lax.ppermute(array, "ray", pairs)

    mine = own_quarter(group, up_weight, down_weight, part)
    arrivals = [along(mine, -shift) for shift in range(1, depth)]
    x, y = beside(mine, 1), beside(mine, 2)
    rendered, rendered_other = render(
        ray_count, True, me, block_owner, tile_lists, opacity, tile_counts.reshape(1, rows),
        ray_pixel, gaussian_features,
    )
    first, far = pack(mine, x, y, arrivals, rendered)
    x_far, y_far = beside(far, 1), beside(far, 2)
    blocks = mix(rendered, partner(rendered_other))
    targets = [blocks[0]] + [along(blocks[shift], shift) for shift in range(1, depth)]
    first_other = partner(first)
    tokens, normed, normed_t = prepare_tokens(
        ray_count, True, me, block_owner, ray_pixel, image_tokens,
        layer_norm_gain.reshape(1, width), (blocks[0],),
    )
    act_first, slope_first, mixed = forward(normed_t, [first], [first_other])
    x_far, y_far = tie(x_far, mixed, *targets[1:]), tie(y_far, mixed, *targets[1:])
    passed_x, passed_y = turn(y, y_far, x_far, mixed)
    d_low, d_high = beside(passed_x, 1), beside(passed_y, 2)
    x_other, y_other = partner(x_far), partner(y_far)
    act_next, slope_next, mixed = forward(normed_t, [x_far, y_far], [x_other, y_other], mixed)
    d_low, d_high = tie(d_low, mixed), tie(d_high, mixed)
    low_other, high_other = partner(d_low), partner(d_high)
    act_last, slope_last, back, back_t, small = forward(
        normed_t, [d_low, d_high], [low_other, high_other], mixed,
        (tokens, layer_scale.reshape(1, width), *targets),
    )
    acts = (act_first, act_next, act_last)
    slopes = (slope_first, slope_next, slope_last)
    weights = (
        (first, x_far, y_far, d_low, d_high),
        (first_other, x_other, y_other, low_other, high_other),
    )
    low = d_low.shape[0]
    act_pieces = (
        ((0, 0, 1), (0, 3, depth - 1)),
        ((0, 1, 1), (1, 0, depth - 1)),
        ((0, 2, 1), (1, depth - 1, depth - 1)),
        ((2, 0, depth),),
    )
    weight_pieces = (
        ((0, 0, 1), (0, 3, depth - 1)),
        ((0, 1, 1), (1, 0, depth - 1)),
        ((0, 2, 1), (2, 0, depth - 1)),
        ((3, 0, low), (4, 0, depth - low)),
    )
    gain = jnp.zeros((1, width), F32)
    (down_other,) = down_gradient(1, act_pieces, depth, acts, back)
    down_arrived = partner(down_other)
    up_other, gain = up_gradient(
        1, weight_pieces, act_pieces, depth, weights[1], slopes, back_t, normed, gain
    )
    up_arrived = partner(up_other)
    down_sums = down_gradient(0, act_pieces, depth, acts, back, down_arrived)
    *up_sums, vector = up_gradient(
        0, weight_pieces, act_pieces, depth, weights[0], slopes, back_t, normed, gain,
        (up_arrived, layer_norm_gain.reshape(1, width), small),
    )
    vector = vector + partner(vector)
    flip = 2
    while flip < ray_count:
        vector = vector + partner(vector, flip)
        flip *= 2

    def sum_beside(own, to_x, to_y, x_later, y_later):
        from_x, from_y = beside(to_x, 1), beside(to_y, 2)
        x_later, y_later = merge(from_x, from_y, x_later, y_later, vector)
        return totals(own, from_x, from_y, beside(x_later, 1), beside(y_later, 2))

    def sum_along(shares, extra=()):
        return collect(
            [shares[0]] + [along(shares[shift], shift) for shift in range(1, depth)], extra
        )

    down_total = sum_along(sum_beside(*down_sums))
    total = sum_along(sum_beside(*up_sums), (vector, down_total))
    quarters = [total] + [beside(total, flip) for flip in (1, 2, 3)]
    grad_up, grad_down, gain, scale, loss = place_quarters(
        group, quarters, part, rows * ray_count * group_count
    )
    return (grad_up, grad_down, gain.reshape(width), scale.reshape(width), loss.reshape(()))


def shards(*operands):
    ray_count, group_count = lax.axis_size("ray"), lax.axis_size("grp")
    hidden = operands[-1].shape[0]
    square = group_count == 4 and ray_count in (4, 8, 16) and hidden % (16 * group_count) == 0
    return (shards_square if square else shards_general)(*operands)


def solution(mesh):
    return jax.shard_map(
        shards,
        mesh=mesh,
        in_specs=(
            P(("grp", "ray"), None),
            P(None, ("grp", "ray")),
            P(None, ("grp", "ray")),
            P(("grp", "ray")),
            P("grp", None),
            P("grp", None),
            P(("grp", "ray"), None),
            P(),
            P(),
            P(None, "ray"),
            P("ray", None),
        ),
        out_specs=(P(None, "ray"), P("ray", None), P(), P(), P()),
        check_vma=False,
    )
```

```python
import functools

import jax
import jax.numpy as jnp
from jax import lax
from jax.experimental import pallas as pl
from jax.experimental.pallas import tpu as pltpu
from jax.sharding import PartitionSpec as P

STABILITY_EPSILON = 1e-06
F32 = jnp.float32
BF16 = jnp.bfloat16
MIB = 1024 * 1024
COST = pl.CostEstimate(flops=1 << 20, bytes_accessed=1 << 16, transcendentals=0)
LONG = pl.CostEstimate(flops=10**10, bytes_accessed=1 << 20, transcendentals=0)
SMEM = pl.BlockSpec(memory_space=pltpu.SMEM)
VMEM = pl.BlockSpec(memory_space=pltpu.VMEM)
ANY = pl.BlockSpec(memory_space=pl.ANY)


def params(mib=48, **more):
    return pltpu.CompilerParams(vmem_limit_bytes=mib * MIB, **more)


def dot_nn(a, b):
    return lax.dot_general(a, b, (((1,), (0,)), ((), ())), preferred_element_type=F32)


def dot_tn(a, b):
    return lax.dot_general(a, b, (((0,), (0,)), ((), ())), preferred_element_type=F32)


def dot_nt(a, b):
    return lax.dot_general(a, b, (((1,), (1,)), ((), ())), preferred_element_type=F32)


def owner_of(pixels, owner_ref, rows, count):
    block = lax.div(pixels, jnp.int32(rows))
    owner = jnp.zeros_like(pixels)
    for slot in range(count):
        owner = jnp.where(block == slot, owner_ref[0:1, slot:slot + 1], owner)
    return owner


def earlier(rows):
    before = lax.broadcasted_iota(jnp.int32, (rows, rows), 0)
    after = lax.broadcasted_iota(jnp.int32, (rows, rows), 1)
    return jnp.where(before < after, 1.0, 0.0).astype(BF16)


HBM = pl.BlockSpec(memory_space=pltpu.HBM)


def fetch(copies, sems):
    started = [
        pltpu.make_async_copy(source, target, sems.at[index])
        for index, (source, target) in enumerate(copies)
    ]
    for copy in started:
        copy.start()

    def wait(*numbers):
        for number in numbers:
            started[number].wait()

    return wait


def render_kernel(
    ray_count, relative, me_ref, owner_hbm, lists_hbm, opacity_hbm, counts_hbm, pixels_hbm,
    features_hbm, near_ref, other_ref, owner_ref, ids_ref, opacity_ref, counts_ref, mine_ref,
    features_ref, share_ref, table_ref, send_ref, sems,
):
    depth, rays = lists_hbm.shape
    gauss = features_hbm.shape[0]
    width = features_hbm.shape[1]
    me = me_ref[0]
    own_pixels = pixels_hbm.at[:, pl.ds(pl.multiple_of(me * rays, rays), rays)]
    wait = fetch(
        [
            (lists_hbm, ids_ref), (opacity_hbm, opacity_ref), (counts_hbm, counts_ref),
            (owner_hbm, owner_ref), (own_pixels, mine_ref), (features_hbm, features_ref),
        ],
        sems,
    )
    wait(0, 1, 2)
    ids_ref[...] = ids_ref[...] - me * gauss
    passing = jnp.ones((1, rays), F32)
    counts = counts_ref[...]
    for level in range(depth):
        alpha = opacity_ref[pl.ds(level, 1), :]
        share_ref[pl.ds(level, 1), :] = jnp.where(level < counts, alpha * passing, 0.0)
        passing = passing * (1.0 - alpha)

    tile = 128
    lanes = 128
    columns = rays // lanes

    @pl.loop(0, (gauss // tile) * columns)
    def _(step):
        first = pl.multiple_of(lax.div(step, columns) * tile, tile)
        lane = pl.multiple_of(lax.rem(step, columns) * lanes, lanes)
        number = lax.broadcasted_iota(jnp.int32, (tile, lanes), 0) + first
        total = jnp.zeros((tile, lanes), F32)
        for level in range(depth):
            ident = ids_ref[pl.ds(level, 1), pl.ds(lane, lanes)]
            share = share_ref[pl.ds(level, 1), pl.ds(lane, lanes)]
            total = total + jnp.where(ident == number, share, 0.0)
        table_ref[pl.ds(first, tile), pl.ds(lane, lanes)] = total.astype(BF16)

    wait(3, 4, 5)
    owner = owner_of(mine_ref[...], owner_ref, rays, ray_count)
    padded = -(-ray_count // 16) * 16
    member = (lax.broadcasted_iota(jnp.int32, (padded, rays), 0) == owner)
    ranks = dot_nn(member.astype(F32).astype(BF16), earlier(rays))
    rank = jnp.sum(jnp.where(member, ranks, 0.0), axis=0, keepdims=True).astype(jnp.int32)
    if relative:
        chips = ray_count // 2
        shift = lax.div(owner, jnp.int32(2)) - lax.div(me, jnp.int32(2))
        shift = jnp.where(shift < 0, shift + chips, shift)
        flip = jnp.where(lax.rem(owner, jnp.int32(2)) == lax.rem(me, jnp.int32(2)), 0, 1)
        block = flip * chips + shift
    else:
        block = owner
    slot = block * (rays // ray_count) + rank
    send_ref[...] = (
        (lax.broadcasted_iota(jnp.int32, (rays, rays), 0) == slot).astype(F32).astype(BF16)
    )

    piece = 256
    half = rays // 2

    @pl.loop(0, width // piece)
    def _(step):
        cols = pl.ds(pl.multiple_of(step * piece, piece), piece)
        rendered = dot_tn(table_ref[...], features_ref[:, cols]).astype(BF16)
        ordered = dot_nn(send_ref[...], rendered).astype(BF16)
        near_ref[:, :, cols] = ordered[:half].reshape(*near_ref.shape[:2], piece)
        other_ref[:, :, cols] = ordered[half:].reshape(*other_ref.shape[:2], piece)


def render(ray_count, relative, me, owner, lists, opacity, counts, pixels, features):
    depth, rays = lists.shape
    gauss, width = features.shape
    shape = jax.ShapeDtypeStruct((ray_count // 2, rays // ray_count, width), BF16)
    return pl.pallas_call(
        functools.partial(render_kernel, ray_count, relative),
        out_shape=(shape, shape),
        in_specs=[SMEM] + [HBM] * 6,
        out_specs=(VMEM, VMEM),
        scratch_shapes=[
            pltpu.VMEM(owner.shape, jnp.int32),
            pltpu.VMEM((depth, rays), jnp.int32),
            pltpu.VMEM((depth, rays), F32),
            pltpu.VMEM((1, rays), jnp.int32),
            pltpu.VMEM((1, rays), jnp.int32),
            pltpu.VMEM((gauss, width), BF16),
            pltpu.VMEM((depth, rays), F32),
            pltpu.VMEM((gauss, rays), BF16),
            pltpu.VMEM((rays, rays), BF16),
            pltpu.SemaphoreType.DMA((6,)),
        ],
        compiler_params=params(20),
        cost_estimate=COST,
        name="render",
    )(me, owner, lists, opacity, counts, pixels, features)


def tokens_kernel(
    ray_count, relative, me_ref, owner_hbm, pixels_hbm, tokens_hbm, gain_hbm,
    *refs,
):
    tokens_out, normed_out, normed_t_out = refs[-11:-8]
    owner_ref, pixels_ref, tokens_ref, gain_ref, order_ref, rank_ref, place_ref, sems = refs[-8:]
    rows, width = tokens_hbm.shape
    me = me_ref[0]
    each = rows // ray_count
    wait = fetch(
        [
            (owner_hbm, owner_ref), (pixels_hbm, pixels_ref), (gain_hbm, gain_ref),
            (tokens_hbm, tokens_ref),
        ],
        sems,
    )
    wait(0, 1)
    pixels = jnp.concatenate(
        [pixels_ref[:, sender * rows:(sender + 1) * rows] for sender in range(ray_count)], axis=0
    )
    mine = owner_of(pixels, owner_ref, rows, ray_count) == me
    place_ref[...] = lax.rem(pixels, jnp.int32(rows)).astype(F32)
    member = jnp.where(mine, 1.0, 0.0)
    padded = -(-ray_count // 16) * 16
    if padded > ray_count:
        spread = jnp.concatenate([member, jnp.zeros((padded - ray_count, rows), F32)], axis=0)
    else:
        spread = member
    ranks = dot_nn(spread.astype(BF16), earlier(rows))
    rank_ref[...] = jnp.where(mine, ranks[:ray_count], -1.0)
    chips = ray_count // 2
    for index in range(ray_count):
        if relative:
            chip = lax.rem(lax.div(me, jnp.int32(2)) + (chips - index // 2), jnp.int32(chips))
            sender = 2 * chip + jnp.bitwise_xor(lax.rem(me, jnp.int32(2)), index % 2)
        else:
            sender = index
        rank = rank_ref[pl.ds(sender, 1), :].astype(jnp.int32)
        hit = lax.broadcasted_iota(jnp.int32, (each, rows), 0) == rank
        at = jnp.sum(
            jnp.where(hit, place_ref[pl.ds(sender, 1), :], 0.0), axis=1, keepdims=True
        )
        here = lax.broadcasted_iota(jnp.int32, (each, rows), 1) == at.astype(jnp.int32)
        order_ref[pl.ds(index * each, each), :] = here.astype(F32).astype(BF16)
    wait(2, 3)
    half = min(128, rows)
    gain = gain_ref[...]

    @pl.loop(0, rows // half)
    def _(step):
        span = pl.ds(pl.multiple_of(step * half, half), half)
        values = dot_nn(order_ref[span, :], tokens_ref[...])
        tokens_out[span, :] = values.astype(BF16)
        centered = values - jnp.mean(values, axis=-1, keepdims=True)
        variance = jnp.mean(centered * centered, axis=-1, keepdims=True)
        xhat = centered * lax.rsqrt(variance + STABILITY_EPSILON)
        normed = (xhat * gain).astype(BF16)
        normed_out[span, :] = normed
        normed_t_out[:, span] = normed.T


def prepare_tokens(ray_count, relative, me, owner, pixels, tokens, gain, after=()):
    rows, width = tokens.shape
    return pl.pallas_call(
        functools.partial(tokens_kernel, ray_count, relative),
        out_shape=(
            jax.ShapeDtypeStruct((rows, width), BF16),
            jax.ShapeDtypeStruct((rows, width), BF16),
            jax.ShapeDtypeStruct((width, rows), BF16),
        ),
        in_specs=[SMEM] + [HBM] * 4 + [ANY] * len(after),
        out_specs=(VMEM, VMEM, VMEM),
        scratch_shapes=[
            pltpu.VMEM(owner.shape, jnp.int32),
            pltpu.VMEM(pixels.shape, jnp.int32),
            pltpu.VMEM((rows, width), BF16),
            pltpu.VMEM((1, width), F32),
            pltpu.VMEM((rows, rows), BF16),
            pltpu.VMEM((ray_count, rows), F32),
            pltpu.VMEM((ray_count, rows), F32),
            pltpu.SemaphoreType.DMA((4,)),
        ],
        compiler_params=params(20),
        cost_estimate=COST,
        name="tokens",
    )(me, owner, pixels, tokens, gain, *after)


def up_kernel(normed_ref, up_ref, act_ref, slope_ref):
    parts, _, part_rows, width = up_ref.shape
    up = up_ref[...].reshape(parts * part_rows, width)
    rows = normed_ref.shape[0]
    piece = min(128, rows)

    @pl.loop(0, rows // piece)
    def _(step):
        span = pl.ds(pl.multiple_of(step * piece, piece), piece)
        hidden = dot_nn(normed_ref[span, :], up)
        phi = 0.5 * (1.0 + lax.erf(hidden * (0.5 ** 0.5)))
        density = jnp.exp(-0.5 * hidden * hidden) * ((2.0 * jnp.pi) ** -0.5)
        act_ref[span, :] = (hidden * phi).astype(BF16)
        slope_ref[span, :] = (phi + hidden * density).astype(slope_ref.dtype)


def project_up(normed, up):
    rows, width = normed.shape
    parts, chunks, part_rows, chunk = up.shape
    return pl.pallas_call(
        up_kernel,
        grid=(chunks,),
        out_shape=(
            jax.ShapeDtypeStruct((rows, chunks * chunk), BF16),
            jax.ShapeDtypeStruct((rows, chunks * chunk), F32),
        ),
        in_specs=[
            pl.BlockSpec((rows, width), lambda j: (0, 0)),
            pl.BlockSpec((parts, 1, part_rows, chunk), lambda j: (0, j, 0, 0)),
        ],
        out_specs=(
            pl.BlockSpec((rows, chunk), lambda j: (0, j)),
            pl.BlockSpec((rows, chunk), lambda j: (0, j)),
        ),
        compiler_params=params(dimension_semantics=("arbitrary",)),
        cost_estimate=COST,
        name="up",
    )(normed, up)


def down_kernel(
    chunks, act_ref, down_ref, tokens_ref, target_ref, scale_ref,
    grad_ref, back_ref, small_ref, mixed_ref,
):
    step = pl.program_id(0)
    rows, width = tokens_ref.shape
    act = act_ref[...]

    @pl.when(step < chunks)
    def _():
        parts, _, part_rows, _ = down_ref.shape
        part = dot_nn(act, down_ref[...].reshape(parts * part_rows, width))

        @pl.when(step == 0)
        def _():
            mixed_ref[...] = part

        @pl.when(step > 0)
        def _():
            mixed_ref[...] += part

    @pl.when(step == chunks - 1)
    def _():
        scale = scale_ref[...]
        small_ref[...] = jnp.zeros_like(small_ref)
        piece = min(64, rows)

        @pl.loop(0, rows // piece)
        def _(index):
            span = pl.ds(pl.multiple_of(index * piece, piece), piece)
            mixed = mixed_ref[span, :]
            out = tokens_ref[span, :].astype(F32) + scale * mixed
            goal = target_ref[span, :].astype(F32)
            out_norm = jnp.sqrt(jnp.sum(out * out, axis=-1, keepdims=True) + STABILITY_EPSILON)
            goal_norm = jnp.sqrt(jnp.sum(goal * goal, axis=-1, keepdims=True) + STABILITY_EPSILON)
            norms = out_norm * goal_norm
            cosine = jnp.sum(out * goal, axis=-1, keepdims=True) / norms
            upstream = (cosine / (out_norm * out_norm)) * out - goal * (1.0 / norms)
            back_ref[span, :] = (upstream * scale).astype(BF16)
            small_ref[0:1, :] += jnp.sum(upstream * mixed, axis=0, keepdims=True)
            loss = jnp.sum(1.0 - cosine, axis=0, keepdims=True)
            small_ref[1:2, :] += jnp.broadcast_to(loss, (1, width))

    @pl.when(step >= chunks)
    def _():
        grad = dot_tn(act, back_ref[...])
        grad_ref[...] = grad.astype(BF16).reshape(grad_ref.shape)


def project_down(act, down, tokens, target, scale):
    rows, width = tokens.shape
    parts, chunks, part_rows, _ = down.shape
    chunk = parts * part_rows
    return pl.pallas_call(
        functools.partial(down_kernel, chunks),
        grid=(2 * chunks,),
        out_shape=(
            jax.ShapeDtypeStruct(down.shape, BF16),
            jax.ShapeDtypeStruct((rows, width), BF16),
            jax.ShapeDtypeStruct((8, width), F32),
        ),
        in_specs=[
            pl.BlockSpec((rows, chunk), lambda j: (0, lax.rem(j, chunks))),
            pl.BlockSpec(
                (parts, 1, part_rows, width), lambda j: (0, jnp.minimum(j, chunks - 1), 0, 0)
            ),
            pl.BlockSpec((rows, width), lambda j: (0, 0)),
            pl.BlockSpec((rows, width), lambda j: (0, 0)),
            pl.BlockSpec((1, width), lambda j: (0, 0)),
        ],
        out_specs=(
            pl.BlockSpec(
                (parts, 1, part_rows, width), lambda j: (0, jnp.maximum(j - chunks, 0), 0, 0)
            ),
            pl.BlockSpec((rows, width), lambda j: (0, 0)),
            pl.BlockSpec((8, width), lambda j: (0, 0)),
        ),
        scratch_shapes=[pltpu.VMEM((rows, width), F32)],
        compiler_params=params(dimension_semantics=("arbitrary",)),
        cost_estimate=COST,
        name="down",
    )(act, down, tokens, target, scale)


def back_kernel(back_ref, down_ref, slope_ref, normed_t_ref, up_ref, gain_ref, grad_ref, sum_ref):
    step = pl.program_id(0)
    parts, _, part_rows, width = down_ref.shape
    chunk = parts * part_rows
    rows = back_ref.shape[0]
    back_act = dot_nt(back_ref[...], down_ref[...].reshape(chunk, width))
    back_hidden = (back_act * slope_ref[...]).astype(BF16)
    up_parts, _, up_rows, _ = up_ref.shape

    @pl.when(step == 0)
    def _():
        sum_ref[...] = jnp.zeros_like(sum_ref)

    grad = dot_nn(normed_t_ref[...], back_hidden)
    grad_ref[...] = grad.astype(BF16).reshape(grad_ref.shape)
    up = up_ref[...].reshape(up_parts * up_rows, chunk).astype(F32)
    sum_ref[...] += jnp.sum(grad * up, axis=1, keepdims=True) / gain_ref[...]


def back_up(back, down, slope, normed_t, up, gain):
    width, rows = normed_t.shape
    parts, chunks, part_rows, _ = down.shape
    chunk = parts * part_rows
    up_parts, _, up_rows, _ = up.shape
    return pl.pallas_call(
        back_kernel,
        grid=(chunks,),
        out_shape=(
            jax.ShapeDtypeStruct(up.shape, BF16),
            jax.ShapeDtypeStruct((width, 1), F32),
        ),
        in_specs=[
            pl.BlockSpec((rows, width), lambda j: (0, 0)),
            pl.BlockSpec((parts, 1, part_rows, width), lambda j: (0, j, 0, 0)),
            pl.BlockSpec((rows, chunk), lambda j: (0, j)),
            pl.BlockSpec((width, rows), lambda j: (0, 0)),
            pl.BlockSpec((up_parts, 1, up_rows, chunk), lambda j: (0, j, 0, 0)),
            pl.BlockSpec((width, 1), lambda j: (0, 0)),
        ],
        out_specs=(
            pl.BlockSpec((up_parts, 1, up_rows, chunk), lambda j: (0, j, 0, 0)),
            pl.BlockSpec((width, 1), lambda j: (0, 0)),
        ),
        compiler_params=params(dimension_semantics=("arbitrary",)),
        cost_estimate=COST,
        name="back",
    )(back, down, slope, normed_t, up, gain)


def gather_weight(weight, parts, group, group_count, ray_count):
    rows, cols = weight.shape
    if parts == 1:
        whole = lax.all_gather(weight, "ray", axis=0, tiled=True)
    else:
        part = lax.dynamic_slice_in_dim(weight, group * (rows // parts), rows // parts, 0)
        whole = lax.all_gather(part, ("grp", "ray"), axis=0, tiled=True)
    return whole.reshape(parts, ray_count, rows // parts, cols)


def reduce_gradient(grad):
    parts, ray_count, part_rows, cols = grad.shape
    flat = grad.reshape(parts * ray_count * part_rows, cols)
    if parts == 1:
        share = lax.psum_scatter(flat, "ray", scatter_dimension=0, tiled=True)
        return lax.psum(share.astype(F32), "grp")
    share = lax.psum_scatter(flat, "grp", scatter_dimension=0, tiled=True)
    share = lax.psum_scatter(share, "ray", scatter_dimension=0, tiled=True)
    return lax.all_gather(share, "grp", axis=0, tiled=True).astype(F32)


def shards_general(
    image_tokens,
    tile_lists,
    opacity,
    tile_counts,
    ray_pixel,
    block_owner,
    gaussian_features,
    layer_norm_gain,
    layer_scale,
    up_weight,
    down_weight,
):
    ray_count = lax.axis_size("ray")
    group_count = lax.axis_size("grp")
    group = lax.axis_index("grp")
    me = lax.axis_index("ray").reshape(1)
    rows, width = image_tokens.shape
    up_parts = group_count if up_weight.shape[0] % (16 * group_count) == 0 else 1
    down_parts = group_count if down_weight.shape[0] % (16 * group_count) == 0 else 1
    up = gather_weight(up_weight, up_parts, group, group_count, ray_count)
    down = gather_weight(down_weight, down_parts, group, group_count, ray_count)
    rendered = render(
        ray_count, False, me, block_owner, tile_lists, opacity, tile_counts.reshape(1, rows),
        ray_pixel, gaussian_features,
    )
    rendered = jnp.concatenate(rendered, axis=0).reshape(rows, width)
    target = lax.all_to_all(rendered, "ray", split_axis=0, concat_axis=0, tiled=True)
    tokens, normed, normed_t = prepare_tokens(
        ray_count, False, me, block_owner, ray_pixel, image_tokens,
        layer_norm_gain.reshape(1, width),
    )
    act, slope = project_up(normed, up)
    grad_down, back, small = project_down(act, down, tokens, target, layer_scale.reshape(1, width))
    grad_up, gain_sum = back_up(back, down, slope, normed_t, up, layer_norm_gain.reshape(width, 1))
    grad_down = reduce_gradient(grad_down)
    grad_up = reduce_gradient(grad_up)
    sums = jnp.concatenate([gain_sum.reshape(1, width), small[:2]], axis=0)
    sums = lax.psum(sums, ("grp", "ray"))
    loss = sums[2, 0] / (rows * ray_count * group_count)
    return (grad_up, grad_down, sums[0], sums[1], loss)


def quarter_kernel(group_ref, up_hbm, down_hbm, out_ref, up_ref, turned_ref, sems):
    part = out_ref.shape[1]
    lanes = up_ref.shape[1]
    start = pl.multiple_of(group_ref[0] * part, part)
    lane = pl.multiple_of(lax.div(start, jnp.int32(lanes)) * lanes, lanes)
    wait = fetch(
        [
            (up_hbm.at[:, pl.ds(lane, lanes)], up_ref),
            (down_hbm.at[pl.ds(start, part), :], out_ref.at[1]),
        ],
        sems,
    )
    wait(0)
    turned_ref[...] = up_ref[...].T
    out_ref[0] = turned_ref[pl.ds(pl.multiple_of(start - lane, part), part), :]
    wait(1)


def own_quarter(group, up, down, part):
    width, chunk = up.shape
    lanes = max(128, part)
    return pl.pallas_call(
        quarter_kernel,
        out_shape=jax.ShapeDtypeStruct((2, part, width), BF16),
        in_specs=[SMEM, HBM, HBM],
        out_specs=VMEM,
        scratch_shapes=[
            pltpu.VMEM((width, lanes), BF16),
            pltpu.VMEM((lanes, width), BF16),
            pltpu.SemaphoreType.DMA((2,)),
        ],
        compiler_params=params(16),
        cost_estimate=LONG,
        name="quarter",
    )(group, up, down)


def finish_rows(tokens, mixed, goal, scale):
    out = tokens + scale * mixed
    out_norm = jnp.sqrt(jnp.sum(out * out, axis=-1, keepdims=True) + STABILITY_EPSILON)
    goal_norm = jnp.sqrt(jnp.sum(goal * goal, axis=-1, keepdims=True) + STABILITY_EPSILON)
    norms = out_norm * goal_norm
    cosine = jnp.sum(out * goal, axis=-1, keepdims=True) / norms
    upstream = (cosine / (out_norm * out_norm)) * out - goal * (1.0 / norms)
    return upstream, 1.0 - cosine


def forward_kernel(first, blocks, sides, skipped, *refs):
    last = blocks > 0
    refs = list(refs[skipped:])
    normed_t_ref = refs.pop(0)
    own, other = refs[:sides], refs[sides:2 * sides]
    del refs[:2 * sides]
    mixed_in = None if first else refs.pop(0)
    if last:
        tokens_ref, scale_ref = refs[:2]
        targets = refs[2:2 + blocks]
        del refs[:2 + blocks]
    act_ref, slope_ref = refs[:2]
    del refs[:2]
    width, rows = normed_t_ref.shape
    total = act_ref.shape[1]
    part = act_ref.shape[2]
    downs = []
    for side, group in enumerate((own, other)):
        start = 0
        for ref in group:
            count = ref.shape[0]
            hiddens = dot_nn(ref[:, 0].reshape(count * part, width), normed_t_ref[...])
            for index in range(count):
                hidden = hiddens[index * part:(index + 1) * part]
                phi = 0.5 * (1.0 + lax.erf(hidden * (0.5 ** 0.5)))
                density = jnp.exp(-0.5 * hidden * hidden) * ((2.0 * jnp.pi) ** -0.5)
                act_ref[side, start + index] = (hidden * phi).astype(BF16)
                slope_ref[side, start + index] = phi + hidden * density
            downs.append(ref[:, 1].reshape(count * part, width))
            start += count
    act = act_ref[...].reshape(2 * total * part, rows)
    down = jnp.concatenate(downs, axis=0)
    if not last:
        mixed_out = refs[0]
        part_sum = dot_tn(act, down)
        mixed_out[...] = part_sum if first else mixed_in[...] + part_sum
        return
    back_ref, back_t_ref, small_ref, mixed_ref = refs
    mixed_ref[...] = mixed_in[...] + dot_tn(act, down)
    scale = scale_ref[...]
    small_ref[...] = jnp.zeros_like(small_ref)
    piece = rows // blocks
    for index, target_ref in enumerate(targets):
        span = pl.ds(index * piece, piece)
        mixed = mixed_ref[span, :]
        upstream, loss = finish_rows(
            tokens_ref[span, :].astype(F32), mixed,
            target_ref[...].reshape(piece, width).astype(F32), scale,
        )
        back = (upstream * scale).astype(BF16)
        back_ref[span, :] = back
        back_t_ref[:, span] = back.T
        small_ref[0:1, :] += jnp.sum(upstream * mixed, axis=0, keepdims=True)
        small_ref[1:2, :] += jnp.broadcast_to(jnp.sum(loss, axis=0, keepdims=True), (1, width))


def forward(normed_t, own, other, mixed=None, finish=None, after=()):
    width, rows = normed_t.shape
    part = own[0].shape[2]
    total = sum(array.shape[0] for array in own)
    first, last = mixed is None, finish is not None
    blocks = len(finish) - 2 if last else 0
    operands = [*after, normed_t, *own, *other]
    if not first:
        operands.append(mixed)
    if last:
        operands.extend(finish)
    piece = (2, total, part, rows)
    shapes = [jax.ShapeDtypeStruct(piece, BF16), jax.ShapeDtypeStruct(piece, F32)]
    scratch = []
    if last:
        shapes += [
            jax.ShapeDtypeStruct((rows, width), BF16),
            jax.ShapeDtypeStruct((width, rows), BF16),
            jax.ShapeDtypeStruct((8, width), F32),
        ]
        scratch = [pltpu.VMEM((rows, width), F32)]
    else:
        shapes += [jax.ShapeDtypeStruct((rows, width), F32)]
    return pl.pallas_call(
        functools.partial(forward_kernel, first, blocks, len(own), len(after)),
        out_shape=tuple(shapes),
        in_specs=[ANY] * len(after) + [VMEM] * (len(operands) - len(after)),
        out_specs=tuple([VMEM] * len(shapes)),
        scratch_shapes=scratch,
        compiler_params=params(24),
        cost_estimate=COST,
        name="forward",
    )(*operands)


def pack_kernel(count, *refs):
    out_ref = refs[-1]
    for index, ref in enumerate(refs[:count]):
        out_ref[index] = ref[...]


def pack(pieces, *after):
    return pl.pallas_call(
        functools.partial(pack_kernel, len(pieces)),
        out_shape=jax.ShapeDtypeStruct((len(pieces), *pieces[0].shape), BF16),
        in_specs=[VMEM] * len(pieces) + [ANY] * len(after),
        out_specs=VMEM,
        compiler_params=params(16),
        cost_estimate=COST,
        name="pack",
    )(*pieces, *after)


def turn_kernel(y_ref, x_ref, *refs):
    a_ref, b_ref = refs[-2:]
    first = a_ref.shape[0]
    a_ref[...] = y_ref[:first]
    b_ref[...] = x_ref[first:]


def turn(y, x, *after):
    count = y.shape[0]
    first = count // 2
    return pl.pallas_call(
        turn_kernel,
        out_shape=(
            jax.ShapeDtypeStruct((first, *y.shape[1:]), BF16),
            jax.ShapeDtypeStruct((count - first, *y.shape[1:]), BF16),
        ),
        in_specs=[VMEM] * 2 + [ANY] * len(after),
        out_specs=(VMEM, VMEM),
        compiler_params=params(16),
        cost_estimate=COST,
        name="turn",
    )(y, x, *after)


def tie_kernel(*refs):
    pass


def tie(array, *after):
    return pl.pallas_call(
        tie_kernel,
        out_shape=jax.ShapeDtypeStruct(array.shape, array.dtype),
        in_specs=[ANY] * (1 + len(after)),
        out_specs=ANY,
        input_output_aliases={0: 0},
        compiler_params=params(4),
        cost_estimate=COST,
        name="tie",
    )(array, *after)


def mix_kernel(*refs):
    near_ref, other_ref, outs = refs[0], refs[1], refs[3:]
    for index, ref in enumerate(outs):
        ref[0] = near_ref[index]
        ref[1] = other_ref[index]


def mix(near, other, after):
    count, each, width = near.shape
    return pl.pallas_call(
        mix_kernel,
        out_shape=tuple([jax.ShapeDtypeStruct((2, each, width), BF16)] * count),
        in_specs=[VMEM, VMEM, ANY],
        out_specs=tuple([VMEM] * count),
        compiler_params=params(16),
        cost_estimate=COST,
        name="mix",
    )(near, other, after)


def joined(refs, pieces, pick):
    values = [pick(refs[which], start, count) for which, start, count in pieces]
    flat = [value.reshape(-1, value.shape[-1]) for value in values]
    return flat[0] if len(flat) == 1 else jnp.concatenate(flat, axis=0)


def put(quarter, value, outs):
    own_ref, x_ref, y_ref, x_later_ref, y_later_ref = outs
    value = value.astype(BF16).reshape(own_ref.shape)
    half = x_ref.shape[0] // 2
    if quarter == 0:
        own_ref[...] = value
    elif quarter == 1:
        x_ref[half:] = value[:half]
        x_later_ref[...] = value[half:]
    elif quarter == 2:
        y_ref[half:] = value[half:]
        y_later_ref[...] = value[:half]
    else:
        x_ref[:half] = value[:half]
        y_ref[:half] = value[half:]


def emit(quarter, value, arrived, outs):
    if arrived is None:
        outs[0][quarter] = value.astype(BF16).reshape(outs[0].shape[1:])
    else:
        put(quarter, value + arrived[quarter].reshape(value.shape).astype(F32), outs)


def down_grad_kernel(side, act_pieces, add, *refs):
    count = 3
    acts, back_ref = refs[:count], refs[count]
    arrived = refs[count + 1] if add else None
    outs = refs[count + 2:] if add else refs[count + 1:]
    for quarter in (3, 1, 2, 0):
        act = joined(acts, act_pieces[quarter], lambda ref, a, n: ref[side, a:a + n])
        emit(quarter, dot_nn(act, back_ref[...]), arrived, outs)


def up_grad_kernel(side, weight_pieces, act_pieces, add, *refs):
    weights, slopes = refs[:5], refs[5:8]
    back_t_ref, normed_ref, gain_in = refs[8:11]
    if add:
        arrived, scale_ref, small_ref = refs[11:14]
        outs, vector_ref, gain_ref = refs[14:-2], refs[-2], refs[-1]
    else:
        arrived = None
        outs, gain_ref = refs[11:-1], refs[-1]
    gain_ref[...] = gain_in[...]
    for quarter in (3, 1, 2, 0):
        pieces = weight_pieces[quarter]
        slope = joined(slopes, act_pieces[quarter], lambda ref, a, n: ref[side, a:a + n])
        back_act = dot_nn(joined(weights, pieces, lambda ref, a, n: ref[a:a + n, 1]), back_t_ref[...])
        back_hidden = (back_act * slope).astype(BF16)
        grad = dot_nn(back_hidden, normed_ref[...])
        up = joined(weights, pieces, lambda ref, a, n: ref[a:a + n, 0]).astype(F32)
        gain_ref[...] += jnp.sum(grad * up, axis=0, keepdims=True)
        emit(quarter, grad, arrived, outs)
    if add:
        vector_ref[0:1, :] = gain_ref[...] / scale_ref[...]
        vector_ref[1:3, :] = small_ref[0:2, :]
        vector_ref[3:8, :] = jnp.zeros((5, gain_ref.shape[1]), F32)


def gradient_shapes(depth, part, width, add):
    if not add:
        return [jax.ShapeDtypeStruct((4, depth, part, width), BF16)]
    counts = (depth, depth, depth, depth - depth // 2, depth // 2)
    return [jax.ShapeDtypeStruct((count, part, width), BF16) for count in counts]


def down_gradient(side, act_pieces, depth, acts, back, arrived=None):
    part = acts[0].shape[2]
    width = back.shape[1]
    add = arrived is not None
    operands = [*acts, back] + ([arrived] if add else [])
    shapes = gradient_shapes(depth, part, width, add)
    return pl.pallas_call(
        functools.partial(down_grad_kernel, side, act_pieces, add),
        out_shape=tuple(shapes),
        in_specs=[VMEM] * len(operands),
        out_specs=tuple([VMEM] * len(shapes)),
        compiler_params=params(20),
        cost_estimate=COST,
        name="down_gradient",
    )(*operands)


def up_gradient(
    side, weight_pieces, act_pieces, depth, weights, slopes, back_t, normed, gain, extra=()
):
    part, width = weights[0].shape[2:]
    add = len(extra) > 0
    operands = [*weights, *slopes, back_t, normed, gain, *extra]
    shapes = gradient_shapes(depth, part, width, add)
    if add:
        shapes.append(jax.ShapeDtypeStruct((8, width), F32))
        scratch = [pltpu.VMEM((1, width), F32)]
    else:
        scratch = []
        shapes.append(jax.ShapeDtypeStruct((1, width), F32))
    return pl.pallas_call(
        functools.partial(up_grad_kernel, side, weight_pieces, act_pieces, add),
        out_shape=tuple(shapes),
        in_specs=[VMEM] * len(operands),
        out_specs=tuple([VMEM] * len(shapes)),
        scratch_shapes=scratch,
        compiler_params=params(24),
        cost_estimate=COST,
        name="up_gradient",
    )(*operands)


def merge_kernel(x_ref, y_ref, x_later_ref, y_later_ref, *refs):
    x_out, y_out = refs[-2:]
    half = y_later_ref.shape[0]
    x_out[...] = (x_later_ref[...].astype(F32) + y_ref[:half].astype(F32)).astype(BF16)
    y_out[...] = (y_later_ref[...].astype(F32) + x_ref[:half].astype(F32)).astype(BF16)


def merge(x, y, x_later, y_later, *after):
    return pl.pallas_call(
        merge_kernel,
        out_shape=tuple(jax.ShapeDtypeStruct(a.shape, BF16) for a in (x_later, y_later)),
        in_specs=[VMEM] * 4 + [ANY] * len(after),
        out_specs=(VMEM, VMEM),
        compiler_params=params(16),
        cost_estimate=COST,
        name="merge",
    )(x, y, x_later, y_later, *after)


def total_kernel(own_ref, x_ref, y_ref, x_late_ref, y_late_ref, *outs):
    half = y_late_ref.shape[0]
    for index, out in enumerate(outs):
        total = own_ref[index].astype(F32)
        if index < half:
            total += x_ref[half + index].astype(F32) + y_late_ref[index].astype(F32)
        else:
            total += y_ref[index].astype(F32) + x_late_ref[index - half].astype(F32)
        out[...] = total.astype(BF16)


def totals(own, x, y, x_late, y_late):
    count, part, width = own.shape
    return pl.pallas_call(
        total_kernel,
        out_shape=tuple([jax.ShapeDtypeStruct((part, width), BF16)] * count),
        in_specs=[VMEM] * 5,
        out_specs=tuple([VMEM] * count),
        compiler_params=params(16),
        cost_estimate=COST,
        name="totals",
    )(own, x, y, x_late, y_late)


def collect_kernel(count, *refs):
    outs = refs[count:]
    part, width = refs[0].shape
    total = refs[0][...].astype(F32)
    for ref in refs[1:count]:
        total = total + ref[...].astype(F32)
    if len(outs) == 1:
        outs[0][...] = total.astype(BF16)
        return
    vector_ref, other_ref, short_ref, long_ref = outs[0], outs[1], outs[-2], outs[-1]
    short_ref[pl.ds(0, part), :] = total.astype(BF16)
    rest = vector_ref[...]
    pieces = []
    for _ in range(3):
        piece = rest.astype(BF16).astype(F32)
        pieces.append(piece)
        rest = rest - piece
    pieces.append(jnp.zeros_like(rest))
    short_ref[pl.ds(part, 32), :] = jnp.concatenate(pieces, axis=0).astype(BF16)
    long_ref[pl.ds(0, part + 32), :] = short_ref[...]
    long_ref[pl.ds(part + 32, part), :] = other_ref[...]


def collect(parts, vector=None, other=None, after=()):
    part, width = parts[0].shape
    operands = list(parts)
    if vector is None:
        counts = (part,)
    else:
        operands += [vector, other]
        counts = (part + 32, 2 * part + 32)
    return pl.pallas_call(
        functools.partial(collect_kernel, len(parts)),
        out_shape=tuple(jax.ShapeDtypeStruct((rows, width), BF16) for rows in counts),
        in_specs=[VMEM] * len(operands) + [ANY] * len(after),
        out_specs=tuple([VMEM] * len(counts)),
        compiler_params=params(16),
        cost_estimate=COST,
        name="collect",
    )(*operands, *after)


def place_kernel(part, tokens, group_ref, *refs):
    ups, downs = refs[:4], refs[4:8]
    up_ref, down_ref, gain_ref, scale_ref, loss_ref, held_ref = refs[8:]
    group = group_ref[0]
    vectors = []
    for index, (up, down) in enumerate(zip(ups, downs)):
        first = pl.multiple_of(jnp.bitwise_xor(group, index) * part, part)
        held_ref[pl.ds(first, part), :] = up[pl.ds(0, part), :].astype(F32)
        start = down.shape[0] - part
        down_ref[pl.ds(first, part), :] = down[pl.ds(start, part), :].astype(F32)
        rows = up[pl.ds(part, 32), :].astype(F32)
        vectors.append((rows[0:8] + rows[8:16]) + rows[16:24])
    up_ref[...] = held_ref[...].T
    vector = (vectors[0] + vectors[1]) + (vectors[2] + vectors[3])
    gain_ref[...] = vector[0:1]
    scale_ref[...] = vector[1:2]
    loss_ref[...] = vector[2:3, 0:1] * (1.0 / tokens)


def place_quarters(group, ups, downs, part, tokens):
    width = ups[0].shape[1]
    shapes = [
        jax.ShapeDtypeStruct((width, 4 * part), F32),
        jax.ShapeDtypeStruct((4 * part, width), F32),
        jax.ShapeDtypeStruct((1, width), F32),
        jax.ShapeDtypeStruct((1, width), F32),
        jax.ShapeDtypeStruct((1, 1), F32),
    ]
    return pl.pallas_call(
        functools.partial(place_kernel, part, tokens),
        out_shape=tuple(shapes),
        in_specs=[SMEM] + [VMEM] * 8,
        out_specs=tuple([VMEM] * len(shapes)),
        scratch_shapes=[pltpu.VMEM((4 * part, width), F32)],
        compiler_params=params(16),
        cost_estimate=COST,
        name="place",
    )(group, *ups, *downs)


def shards_square(
    image_tokens,
    tile_lists,
    opacity,
    tile_counts,
    ray_pixel,
    block_owner,
    gaussian_features,
    layer_norm_gain,
    layer_scale,
    up_weight,
    down_weight,
):
    ray_count = lax.axis_size("ray")
    group_count = lax.axis_size("grp")
    depth = ray_count // 2
    group = lax.axis_index("grp").reshape(1)
    me = lax.axis_index("ray").reshape(1)
    rows, width = image_tokens.shape
    part = down_weight.shape[0] // group_count

    def beside(array, flip):
        return lax.ppermute(array, "grp", [(g, g ^ flip) for g in range(group_count)])

    def partner(array, flip=1):
        return lax.ppermute(array, "ray", [(r, r ^ flip) for r in range(ray_count)])

    def along(array, shift):
        pairs = [(r, (r + 2 * shift) % ray_count) for r in range(ray_count)]
        return lax.ppermute(array, "ray", pairs)

    mine = own_quarter(group, up_weight, down_weight, part)
    arrivals = [along(mine, -shift) for shift in range(1, depth)]
    rendered, rendered_other = render(
        ray_count, True, me, block_owner, tile_lists, opacity, tile_counts.reshape(1, rows),
        ray_pixel, gaussian_features,
    )
    first = pack([mine] + arrivals, rendered)
    x_part, y_part = beside(first, 1), beside(first, 2)
    blocks = mix(rendered, partner(rendered_other), first)
    targets = [blocks[0]] + [along(blocks[shift], shift) for shift in range(1, depth)]
    first_other = partner(first)
    tokens, normed, normed_t = prepare_tokens(
        ray_count, True, me, block_owner, ray_pixel, image_tokens,
        layer_norm_gain.reshape(1, width), (blocks[0],),
    )
    act_first, slope_first, mixed = forward(normed_t, [first], [first_other])
    passed_x, passed_y = turn(y_part, x_part, mixed, *targets[1:-1])
    d_low, d_high = beside(passed_x, 1), beside(passed_y, 2)
    x_part, y_part = tie(x_part, passed_x, passed_y), tie(y_part, passed_x, passed_y)
    x_other, y_other = partner(x_part), partner(y_part)
    act_next, slope_next, mixed = forward(
        normed_t, [x_part, y_part], [x_other, y_other], mixed, after=targets[-1:]
    )
    d_low, d_high = tie(d_low, mixed), tie(d_high, mixed)
    low_other, high_other = partner(d_low), partner(d_high)
    act_last, slope_last, back, back_t, small = forward(
        normed_t, [d_low, d_high], [low_other, high_other], mixed,
        (tokens, layer_scale.reshape(1, width), *targets),
    )
    acts = (act_first, act_next, act_last)
    slopes = (slope_first, slope_next, slope_last)
    weights = (
        (first, x_part, y_part, d_low, d_high),
        (first_other, x_other, y_other, low_other, high_other),
    )
    low = d_low.shape[0]
    act_pieces = (((0, 0, depth),), ((1, 0, depth),), ((1, depth, depth),), ((2, 0, depth),))
    weight_pieces = (
        ((0, 0, depth),), ((1, 0, depth),), ((2, 0, depth),), ((3, 0, low), (4, 0, depth - low))
    )
    gain = jnp.zeros((1, width), F32)
    (down_other,) = down_gradient(1, act_pieces, depth, acts, back)
    down_arrived = partner(down_other)
    up_other, gain = up_gradient(
        1, weight_pieces, act_pieces, depth, weights[1], slopes, back_t, normed, gain
    )
    up_arrived = partner(up_other)
    down_sums = down_gradient(0, act_pieces, depth, acts, back, down_arrived)
    *up_sums, vector = up_gradient(
        0, weight_pieces, act_pieces, depth, weights[0], slopes, back_t, normed, gain,
        (up_arrived, layer_norm_gain.reshape(1, width), small),
    )
    vector = vector + partner(vector)
    flip = 2
    while flip < ray_count:
        vector = vector + partner(vector, flip)
        flip *= 2

    def sum_first(to_x, to_y, x_later, y_later, *after):
        from_x, from_y = beside(to_x, 1), beside(to_y, 2)
        return from_x, from_y, merge(from_x, from_y, x_later, y_later, *after)

    def sum_second(own, from_x, from_y, later):
        return totals(own, from_x, from_y, beside(later[0], 1), beside(later[1], 2))

    def arrive_along(shares):
        return [shares[0]] + [along(shares[shift], shift) for shift in range(1, depth)]

    own, *rest = down_sums
    *arrived, later = sum_first(*rest)
    shares = sum_second(own, *arrived, later)
    (down_total,) = collect(arrive_along(shares))
    down_x, down_y = beside(down_total, 1), beside(down_total, 2)
    own, *rest = up_sums
    *arrived, later = sum_first(*rest, vector)
    shares = sum_second(own, *arrived, later)
    short, long = collect(arrive_along(shares), vector, down_total, (down_x, down_y))
    up_x, up_y, both = beside(short, 1), beside(short, 2), beside(long, 3)
    grad_up, grad_down, gain, scale, loss = place_quarters(
        group, (short, up_x, up_y, both), (down_total, down_x, down_y, both), part,
        rows * ray_count * group_count,
    )
    return (grad_up, grad_down, gain.reshape(width), scale.reshape(width), loss.reshape(()))


def shards(*operands):
    ray_count, group_count = lax.axis_size("ray"), lax.axis_size("grp")
    hidden = operands[-1].shape[0]
    square = group_count == 4 and ray_count in (4, 8, 16) and hidden % (16 * group_count) == 0
    return (shards_square if square else shards_general)(*operands)


def solution(mesh):
    return jax.shard_map(
        shards,
        mesh=mesh,
        in_specs=(
            P(("grp", "ray"), None),
            P(None, ("grp", "ray")),
            P(None, ("grp", "ray")),
            P(("grp", "ray")),
            P("grp", None),
            P("grp", None),
            P(("grp", "ray"), None),
            P(),
            P(),
            P(None, "ray"),
            P("ray", None),
        ),
        out_specs=(P(None, "ray"), P("ray", None), P(), P(), P()),
        check_vma=False,
    )
```

```python
import functools

import jax
import jax.numpy as jnp
from jax import lax
from jax.experimental import pallas as pl
from jax.experimental.pallas import tpu as pltpu
from jax.sharding import PartitionSpec as P

STABILITY_EPSILON = 1e-06
F32 = jnp.float32
BF16 = jnp.bfloat16
MIB = 1024 * 1024
COST = pl.CostEstimate(flops=1 << 20, bytes_accessed=1 << 16, transcendentals=0)
LONG = pl.CostEstimate(flops=10**10, bytes_accessed=1 << 20, transcendentals=0)
SMEM = pl.BlockSpec(memory_space=pltpu.SMEM)
VMEM = pl.BlockSpec(memory_space=pltpu.VMEM)
ANY = pl.BlockSpec(memory_space=pl.ANY)


def params(mib=48, **more):
    return pltpu.CompilerParams(vmem_limit_bytes=mib * MIB, **more)


def dot_nn(a, b):
    return lax.dot_general(a, b, (((1,), (0,)), ((), ())), preferred_element_type=F32)


def dot_tn(a, b):
    return lax.dot_general(a, b, (((0,), (0,)), ((), ())), preferred_element_type=F32)


def dot_nt(a, b):
    return lax.dot_general(a, b, (((1,), (1,)), ((), ())), preferred_element_type=F32)


def owner_of(pixels, owner_ref, rows, count):
    block = lax.div(pixels, jnp.int32(rows))
    owner = jnp.zeros_like(pixels)
    for slot in range(count):
        owner = jnp.where(block == slot, owner_ref[0:1, slot:slot + 1], owner)
    return owner


def earlier(rows):
    before = lax.broadcasted_iota(jnp.int32, (rows, rows), 0)
    after = lax.broadcasted_iota(jnp.int32, (rows, rows), 1)
    return jnp.where(before < after, 1.0, 0.0).astype(BF16)


HBM = pl.BlockSpec(memory_space=pltpu.HBM)


def fetch(copies, sems):
    started = [
        pltpu.make_async_copy(source, target, sems.at[index])
        for index, (source, target) in enumerate(copies)
    ]
    for copy in started:
        copy.start()

    def wait(*numbers):
        for number in numbers:
            started[number].wait()

    return wait


def render_kernel(
    ray_count, relative, me_ref, owner_hbm, lists_hbm, opacity_hbm, counts_hbm, pixels_hbm,
    features_hbm, near_ref, other_ref, owner_ref, ids_ref, opacity_ref, counts_ref, mine_ref,
    features_ref, share_ref, table_ref, send_ref, sems,
):
    depth, rays = lists_hbm.shape
    gauss = features_hbm.shape[0]
    width = features_hbm.shape[1]
    me = me_ref[0]
    own_pixels = pixels_hbm.at[:, pl.ds(pl.multiple_of(me * rays, rays), rays)]
    wait = fetch(
        [
            (lists_hbm, ids_ref), (opacity_hbm, opacity_ref), (counts_hbm, counts_ref),
            (owner_hbm, owner_ref), (own_pixels, mine_ref), (features_hbm, features_ref),
        ],
        sems,
    )
    wait(0, 1, 2)
    ids_ref[...] = ids_ref[...] - me * gauss
    passing = jnp.ones((1, rays), F32)
    counts = counts_ref[...]
    for level in range(depth):
        alpha = opacity_ref[pl.ds(level, 1), :]
        share_ref[pl.ds(level, 1), :] = jnp.where(level < counts, alpha * passing, 0.0)
        passing = passing * (1.0 - alpha)

    tile = 128
    lanes = 128
    columns = rays // lanes

    @pl.loop(0, (gauss // tile) * columns)
    def _(step):
        first = pl.multiple_of(lax.div(step, columns) * tile, tile)
        lane = pl.multiple_of(lax.rem(step, columns) * lanes, lanes)
        number = lax.broadcasted_iota(jnp.int32, (tile, lanes), 0) + first
        total = jnp.zeros((tile, lanes), F32)
        for level in range(depth):
            ident = ids_ref[pl.ds(level, 1), pl.ds(lane, lanes)]
            share = share_ref[pl.ds(level, 1), pl.ds(lane, lanes)]
            total = total + jnp.where(ident == number, share, 0.0)
        table_ref[pl.ds(first, tile), pl.ds(lane, lanes)] = total.astype(BF16)

    wait(3, 4, 5)
    owner = owner_of(mine_ref[...], owner_ref, rays, ray_count)
    padded = -(-ray_count // 16) * 16
    member = (lax.broadcasted_iota(jnp.int32, (padded, rays), 0) == owner)
    ranks = dot_nn(member.astype(F32).astype(BF16), earlier(rays))
    rank = jnp.sum(jnp.where(member, ranks, 0.0), axis=0, keepdims=True).astype(jnp.int32)
    if relative:
        chips = ray_count // 2
        shift = lax.div(owner, jnp.int32(2)) - lax.div(me, jnp.int32(2))
        shift = jnp.where(shift < 0, shift + chips, shift)
        flip = jnp.where(lax.rem(owner, jnp.int32(2)) == lax.rem(me, jnp.int32(2)), 0, 1)
        block = flip * chips + shift
    else:
        block = owner
    slot = block * (rays // ray_count) + rank
    send_ref[...] = (
        (lax.broadcasted_iota(jnp.int32, (rays, rays), 0) == slot).astype(F32).astype(BF16)
    )

    piece = 256
    half = rays // 2

    @pl.loop(0, width // piece)
    def _(step):
        cols = pl.ds(pl.multiple_of(step * piece, piece), piece)
        rendered = dot_tn(table_ref[...], features_ref[:, cols]).astype(BF16)
        ordered = dot_nn(send_ref[...], rendered).astype(BF16)
        near_ref[:, :, cols] = ordered[:half].reshape(*near_ref.shape[:2], piece)
        other_ref[:, :, cols] = ordered[half:].reshape(*other_ref.shape[:2], piece)


def render(ray_count, relative, me, owner, lists, opacity, counts, pixels, features):
    depth, rays = lists.shape
    gauss, width = features.shape
    shape = jax.ShapeDtypeStruct((ray_count // 2, rays // ray_count, width), BF16)
    return pl.pallas_call(
        functools.partial(render_kernel, ray_count, relative),
        out_shape=(shape, shape),
        in_specs=[SMEM] + [HBM] * 6,
        out_specs=(VMEM, VMEM),
        scratch_shapes=[
            pltpu.VMEM(owner.shape, jnp.int32),
            pltpu.VMEM((depth, rays), jnp.int32),
            pltpu.VMEM((depth, rays), F32),
            pltpu.VMEM((1, rays), jnp.int32),
            pltpu.VMEM((1, rays), jnp.int32),
            pltpu.VMEM((gauss, width), BF16),
            pltpu.VMEM((depth, rays), F32),
            pltpu.VMEM((gauss, rays), BF16),
            pltpu.VMEM((rays, rays), BF16),
            pltpu.SemaphoreType.DMA((6,)),
        ],
        compiler_params=params(20),
        cost_estimate=COST,
        name="render",
    )(me, owner, lists, opacity, counts, pixels, features)


def tokens_kernel(
    ray_count, relative, me_ref, owner_hbm, pixels_hbm, tokens_hbm, gain_hbm,
    *refs,
):
    tokens_out, normed_out, normed_t_out = refs[-11:-8]
    owner_ref, pixels_ref, tokens_ref, gain_ref, order_ref, rank_ref, place_ref, sems = refs[-8:]
    rows, width = tokens_hbm.shape
    me = me_ref[0]
    each = rows // ray_count
    wait = fetch(
        [
            (owner_hbm, owner_ref), (pixels_hbm, pixels_ref), (gain_hbm, gain_ref),
            (tokens_hbm, tokens_ref),
        ],
        sems,
    )
    wait(0, 1)
    pixels = jnp.concatenate(
        [pixels_ref[:, sender * rows:(sender + 1) * rows] for sender in range(ray_count)], axis=0
    )
    mine = owner_of(pixels, owner_ref, rows, ray_count) == me
    place_ref[...] = lax.rem(pixels, jnp.int32(rows)).astype(F32)
    member = jnp.where(mine, 1.0, 0.0)
    padded = -(-ray_count // 16) * 16
    if padded > ray_count:
        spread = jnp.concatenate([member, jnp.zeros((padded - ray_count, rows), F32)], axis=0)
    else:
        spread = member
    ranks = dot_nn(spread.astype(BF16), earlier(rows))
    rank_ref[...] = jnp.where(mine, ranks[:ray_count], -1.0)
    chips = ray_count // 2
    for index in range(ray_count):
        if relative:
            chip = lax.rem(lax.div(me, jnp.int32(2)) + (chips - index // 2), jnp.int32(chips))
            sender = 2 * chip + jnp.bitwise_xor(lax.rem(me, jnp.int32(2)), index % 2)
        else:
            sender = index
        rank = rank_ref[pl.ds(sender, 1), :].astype(jnp.int32)
        hit = lax.broadcasted_iota(jnp.int32, (each, rows), 0) == rank
        at = jnp.sum(
            jnp.where(hit, place_ref[pl.ds(sender, 1), :], 0.0), axis=1, keepdims=True
        )
        here = lax.broadcasted_iota(jnp.int32, (each, rows), 1) == at.astype(jnp.int32)
        order_ref[pl.ds(index * each, each), :] = here.astype(F32).astype(BF16)
    wait(2, 3)
    half = min(128, rows)
    gain = gain_ref[...]

    @pl.loop(0, rows // half)
    def _(step):
        span = pl.ds(pl.multiple_of(step * half, half), half)
        values = dot_nn(order_ref[span, :], tokens_ref[...])
        tokens_out[span, :] = values.astype(BF16)
        centered = values - jnp.mean(values, axis=-1, keepdims=True)
        variance = jnp.mean(centered * centered, axis=-1, keepdims=True)
        xhat = centered * lax.rsqrt(variance + STABILITY_EPSILON)
        normed = (xhat * gain).astype(BF16)
        normed_out[span, :] = normed
        normed_t_out[:, span] = normed.T


def prepare_tokens(ray_count, relative, me, owner, pixels, tokens, gain, after=()):
    rows, width = tokens.shape
    return pl.pallas_call(
        functools.partial(tokens_kernel, ray_count, relative),
        out_shape=(
            jax.ShapeDtypeStruct((rows, width), BF16),
            jax.ShapeDtypeStruct((rows, width), BF16),
            jax.ShapeDtypeStruct((width, rows), BF16),
        ),
        in_specs=[SMEM] + [HBM] * 4 + [ANY] * len(after),
        out_specs=(VMEM, VMEM, VMEM),
        scratch_shapes=[
            pltpu.VMEM(owner.shape, jnp.int32),
            pltpu.VMEM(pixels.shape, jnp.int32),
            pltpu.VMEM((rows, width), BF16),
            pltpu.VMEM((1, width), F32),
            pltpu.VMEM((rows, rows), BF16),
            pltpu.VMEM((ray_count, rows), F32),
            pltpu.VMEM((ray_count, rows), F32),
            pltpu.SemaphoreType.DMA((4,)),
        ],
        compiler_params=params(20),
        cost_estimate=COST,
        name="tokens",
    )(me, owner, pixels, tokens, gain, *after)


def up_kernel(normed_ref, up_ref, act_ref, slope_ref):
    parts, _, part_rows, width = up_ref.shape
    up = up_ref[...].reshape(parts * part_rows, width)
    rows = normed_ref.shape[0]
    piece = min(128, rows)

    @pl.loop(0, rows // piece)
    def _(step):
        span = pl.ds(pl.multiple_of(step * piece, piece), piece)
        hidden = dot_nn(normed_ref[span, :], up)
        phi = 0.5 * (1.0 + lax.erf(hidden * (0.5 ** 0.5)))
        density = jnp.exp(-0.5 * hidden * hidden) * ((2.0 * jnp.pi) ** -0.5)
        act_ref[span, :] = (hidden * phi).astype(BF16)
        slope_ref[span, :] = (phi + hidden * density).astype(slope_ref.dtype)


def project_up(normed, up):
    rows, width = normed.shape
    parts, chunks, part_rows, chunk = up.shape
    return pl.pallas_call(
        up_kernel,
        grid=(chunks,),
        out_shape=(
            jax.ShapeDtypeStruct((rows, chunks * chunk), BF16),
            jax.ShapeDtypeStruct((rows, chunks * chunk), F32),
        ),
        in_specs=[
            pl.BlockSpec((rows, width), lambda j: (0, 0)),
            pl.BlockSpec((parts, 1, part_rows, chunk), lambda j: (0, j, 0, 0)),
        ],
        out_specs=(
            pl.BlockSpec((rows, chunk), lambda j: (0, j)),
            pl.BlockSpec((rows, chunk), lambda j: (0, j)),
        ),
        compiler_params=params(dimension_semantics=("arbitrary",)),
        cost_estimate=COST,
        name="up",
    )(normed, up)


def down_kernel(
    chunks, act_ref, down_ref, tokens_ref, target_ref, scale_ref,
    grad_ref, back_ref, small_ref, mixed_ref,
):
    step = pl.program_id(0)
    rows, width = tokens_ref.shape
    act = act_ref[...]

    @pl.when(step < chunks)
    def _():
        parts, _, part_rows, _ = down_ref.shape
        part = dot_nn(act, down_ref[...].reshape(parts * part_rows, width))

        @pl.when(step == 0)
        def _():
            mixed_ref[...] = part

        @pl.when(step > 0)
        def _():
            mixed_ref[...] += part

    @pl.when(step == chunks - 1)
    def _():
        scale = scale_ref[...]
        small_ref[...] = jnp.zeros_like(small_ref)
        piece = min(64, rows)

        @pl.loop(0, rows // piece)
        def _(index):
            span = pl.ds(pl.multiple_of(index * piece, piece), piece)
            mixed = mixed_ref[span, :]
            out = tokens_ref[span, :].astype(F32) + scale * mixed
            goal = target_ref[span, :].astype(F32)
            out_norm = jnp.sqrt(jnp.sum(out * out, axis=-1, keepdims=True) + STABILITY_EPSILON)
            goal_norm = jnp.sqrt(jnp.sum(goal * goal, axis=-1, keepdims=True) + STABILITY_EPSILON)
            norms = out_norm * goal_norm
            cosine = jnp.sum(out * goal, axis=-1, keepdims=True) / norms
            upstream = (cosine / (out_norm * out_norm)) * out - goal * (1.0 / norms)
            back_ref[span, :] = (upstream * scale).astype(BF16)
            small_ref[0:1, :] += jnp.sum(upstream * mixed, axis=0, keepdims=True)
            loss = jnp.sum(1.0 - cosine, axis=0, keepdims=True)
            small_ref[1:2, :] += jnp.broadcast_to(loss, (1, width))

    @pl.when(step >= chunks)
    def _():
        grad = dot_tn(act, back_ref[...])
        grad_ref[...] = grad.astype(BF16).reshape(grad_ref.shape)


def project_down(act, down, tokens, target, scale):
    rows, width = tokens.shape
    parts, chunks, part_rows, _ = down.shape
    chunk = parts * part_rows
    return pl.pallas_call(
        functools.partial(down_kernel, chunks),
        grid=(2 * chunks,),
        out_shape=(
            jax.ShapeDtypeStruct(down.shape, BF16),
            jax.ShapeDtypeStruct((rows, width), BF16),
            jax.ShapeDtypeStruct((8, width), F32),
        ),
        in_specs=[
            pl.BlockSpec((rows, chunk), lambda j: (0, lax.rem(j, chunks))),
            pl.BlockSpec(
                (parts, 1, part_rows, width), lambda j: (0, jnp.minimum(j, chunks - 1), 0, 0)
            ),
            pl.BlockSpec((rows, width), lambda j: (0, 0)),
            pl.BlockSpec((rows, width), lambda j: (0, 0)),
            pl.BlockSpec((1, width), lambda j: (0, 0)),
        ],
        out_specs=(
            pl.BlockSpec(
                (parts, 1, part_rows, width), lambda j: (0, jnp.maximum(j - chunks, 0), 0, 0)
            ),
            pl.BlockSpec((rows, width), lambda j: (0, 0)),
            pl.BlockSpec((8, width), lambda j: (0, 0)),
        ),
        scratch_shapes=[pltpu.VMEM((rows, width), F32)],
        compiler_params=params(dimension_semantics=("arbitrary",)),
        cost_estimate=COST,
        name="down",
    )(act, down, tokens, target, scale)


def back_kernel(back_ref, down_ref, slope_ref, normed_t_ref, up_ref, gain_ref, grad_ref, sum_ref):
    step = pl.program_id(0)
    parts, _, part_rows, width = down_ref.shape
    chunk = parts * part_rows
    rows = back_ref.shape[0]
    back_act = dot_nt(back_ref[...], down_ref[...].reshape(chunk, width))
    back_hidden = (back_act * slope_ref[...]).astype(BF16)
    up_parts, _, up_rows, _ = up_ref.shape

    @pl.when(step == 0)
    def _():
        sum_ref[...] = jnp.zeros_like(sum_ref)

    grad = dot_nn(normed_t_ref[...], back_hidden)
    grad_ref[...] = grad.astype(BF16).reshape(grad_ref.shape)
    up = up_ref[...].reshape(up_parts * up_rows, chunk).astype(F32)
    sum_ref[...] += jnp.sum(grad * up, axis=1, keepdims=True) / gain_ref[...]


def back_up(back, down, slope, normed_t, up, gain):
    width, rows = normed_t.shape
    parts, chunks, part_rows, _ = down.shape
    chunk = parts * part_rows
    up_parts, _, up_rows, _ = up.shape
    return pl.pallas_call(
        back_kernel,
        grid=(chunks,),
        out_shape=(
            jax.ShapeDtypeStruct(up.shape, BF16),
            jax.ShapeDtypeStruct((width, 1), F32),
        ),
        in_specs=[
            pl.BlockSpec((rows, width), lambda j: (0, 0)),
            pl.BlockSpec((parts, 1, part_rows, width), lambda j: (0, j, 0, 0)),
            pl.BlockSpec((rows, chunk), lambda j: (0, j)),
            pl.BlockSpec((width, rows), lambda j: (0, 0)),
            pl.BlockSpec((up_parts, 1, up_rows, chunk), lambda j: (0, j, 0, 0)),
            pl.BlockSpec((width, 1), lambda j: (0, 0)),
        ],
        out_specs=(
            pl.BlockSpec((up_parts, 1, up_rows, chunk), lambda j: (0, j, 0, 0)),
            pl.BlockSpec((width, 1), lambda j: (0, 0)),
        ),
        compiler_params=params(dimension_semantics=("arbitrary",)),
        cost_estimate=COST,
        name="back",
    )(back, down, slope, normed_t, up, gain)


def gather_weight(weight, parts, group, group_count, ray_count):
    rows, cols = weight.shape
    if parts == 1:
        whole = lax.all_gather(weight, "ray", axis=0, tiled=True)
    else:
        part = lax.dynamic_slice_in_dim(weight, group * (rows // parts), rows // parts, 0)
        whole = lax.all_gather(part, ("grp", "ray"), axis=0, tiled=True)
    return whole.reshape(parts, ray_count, rows // parts, cols)


def reduce_gradient(grad):
    parts, ray_count, part_rows, cols = grad.shape
    flat = grad.reshape(parts * ray_count * part_rows, cols)
    if parts == 1:
        share = lax.psum_scatter(flat, "ray", scatter_dimension=0, tiled=True)
        return lax.psum(share.astype(F32), "grp")
    share = lax.psum_scatter(flat, "grp", scatter_dimension=0, tiled=True)
    share = lax.psum_scatter(share, "ray", scatter_dimension=0, tiled=True)
    return lax.all_gather(share, "grp", axis=0, tiled=True).astype(F32)


def shards_general(
    image_tokens,
    tile_lists,
    opacity,
    tile_counts,
    ray_pixel,
    block_owner,
    gaussian_features,
    layer_norm_gain,
    layer_scale,
    up_weight,
    down_weight,
):
    ray_count = lax.axis_size("ray")
    group_count = lax.axis_size("grp")
    group = lax.axis_index("grp")
    me = lax.axis_index("ray").reshape(1)
    rows, width = image_tokens.shape
    up_parts = group_count if up_weight.shape[0] % (16 * group_count) == 0 else 1
    down_parts = group_count if down_weight.shape[0] % (16 * group_count) == 0 else 1
    up = gather_weight(up_weight, up_parts, group, group_count, ray_count)
    down = gather_weight(down_weight, down_parts, group, group_count, ray_count)
    rendered = render(
        ray_count, False, me, block_owner, tile_lists, opacity, tile_counts.reshape(1, rows),
        ray_pixel, gaussian_features,
    )
    rendered = jnp.concatenate(rendered, axis=0).reshape(rows, width)
    target = lax.all_to_all(rendered, "ray", split_axis=0, concat_axis=0, tiled=True)
    tokens, normed, normed_t = prepare_tokens(
        ray_count, False, me, block_owner, ray_pixel, image_tokens,
        layer_norm_gain.reshape(1, width),
    )
    act, slope = project_up(normed, up)
    grad_down, back, small = project_down(act, down, tokens, target, layer_scale.reshape(1, width))
    grad_up, gain_sum = back_up(back, down, slope, normed_t, up, layer_norm_gain.reshape(width, 1))
    grad_down = reduce_gradient(grad_down)
    grad_up = reduce_gradient(grad_up)
    sums = jnp.concatenate([gain_sum.reshape(1, width), small[:2]], axis=0)
    sums = lax.psum(sums, ("grp", "ray"))
    loss = sums[2, 0] / (rows * ray_count * group_count)
    return (grad_up, grad_down, sums[0], sums[1], loss)


def quarter_kernel(group_ref, up_hbm, down_hbm, out_ref, up_ref, turned_ref, sems):
    part = out_ref.shape[1]
    lanes = up_ref.shape[1]
    start = pl.multiple_of(group_ref[0] * part, part)
    lane = pl.multiple_of(lax.div(start, jnp.int32(lanes)) * lanes, lanes)
    wait = fetch(
        [
            (up_hbm.at[:, pl.ds(lane, lanes)], up_ref),
            (down_hbm.at[pl.ds(start, part), :], out_ref.at[1]),
        ],
        sems,
    )
    wait(0)
    turned_ref[...] = up_ref[...].T
    out_ref[0] = turned_ref[pl.ds(pl.multiple_of(start - lane, part), part), :]
    wait(1)


def own_quarter(group, up, down, part):
    width, chunk = up.shape
    lanes = max(128, part)
    return pl.pallas_call(
        quarter_kernel,
        out_shape=jax.ShapeDtypeStruct((2, part, width), BF16),
        in_specs=[SMEM, HBM, HBM],
        out_specs=VMEM,
        scratch_shapes=[
            pltpu.VMEM((width, lanes), BF16),
            pltpu.VMEM((lanes, width), BF16),
            pltpu.SemaphoreType.DMA((2,)),
        ],
        compiler_params=params(16),
        cost_estimate=LONG,
        name="quarter",
    )(group, up, down)


def finish_rows(tokens, mixed, goal, scale):
    out = tokens + scale * mixed
    out_norm = jnp.sqrt(jnp.sum(out * out, axis=-1, keepdims=True) + STABILITY_EPSILON)
    goal_norm = jnp.sqrt(jnp.sum(goal * goal, axis=-1, keepdims=True) + STABILITY_EPSILON)
    norms = out_norm * goal_norm
    cosine = jnp.sum(out * goal, axis=-1, keepdims=True) / norms
    upstream = (cosine / (out_norm * out_norm)) * out - goal * (1.0 / norms)
    return upstream, 1.0 - cosine


def forward_kernel(first, blocks, sides, skipped, *refs):
    last = blocks > 0
    refs = list(refs[skipped:])
    normed_t_ref = refs.pop(0)
    own, other = refs[:sides], refs[sides:2 * sides]
    del refs[:2 * sides]
    mixed_in = None if first else refs.pop(0)
    if last:
        tokens_ref, scale_ref = refs[:2]
        targets = refs[2:2 + blocks]
        del refs[:2 + blocks]
    act_ref, slope_ref = refs[:2]
    del refs[:2]
    width, rows = normed_t_ref.shape
    part = act_ref.shape[2]
    part_sum = None
    for side, group in enumerate((own, other)):
        start = 0
        for ref in group:
            count = ref.shape[0]
            hiddens = dot_nn(ref[:, 0].reshape(count * part, width), normed_t_ref[...])
            for index in range(count):
                hidden = hiddens[index * part:(index + 1) * part]
                phi = 0.5 * (1.0 + lax.erf(hidden * (0.5 ** 0.5)))
                density = jnp.exp(-0.5 * hidden * hidden) * ((2.0 * jnp.pi) ** -0.5)
                act_ref[side, start + index] = (hidden * phi).astype(BF16)
                slope_ref[side, start + index] = phi + hidden * density
            act = act_ref[side, start:start + count].reshape(count * part, rows)
            term = dot_tn(act, ref[:, 1].reshape(count * part, width))
            part_sum = term if part_sum is None else part_sum + term
            start += count
    if not last:
        mixed_out = refs[0]
        mixed_out[...] = part_sum if first else mixed_in[...] + part_sum
        return
    back_ref, back_t_ref, small_ref, mixed_ref = refs
    mixed_ref[...] = mixed_in[...] + part_sum
    scale = scale_ref[...]
    small_ref[...] = jnp.zeros_like(small_ref)
    piece = rows // blocks
    for index, target_ref in enumerate(targets):
        span = pl.ds(index * piece, piece)
        mixed = mixed_ref[span, :]
        upstream, loss = finish_rows(
            tokens_ref[span, :].astype(F32), mixed,
            target_ref[...].reshape(piece, width).astype(F32), scale,
        )
        back = (upstream * scale).astype(BF16)
        back_ref[span, :] = back
        back_t_ref[:, span] = back.T
        small_ref[0:1, :] += jnp.sum(upstream * mixed, axis=0, keepdims=True)
        small_ref[1:2, :] += jnp.broadcast_to(jnp.sum(loss, axis=0, keepdims=True), (1, width))


def forward(normed_t, own, other, mixed=None, finish=None, after=()):
    width, rows = normed_t.shape
    part = own[0].shape[2]
    total = sum(array.shape[0] for array in own)
    first, last = mixed is None, finish is not None
    blocks = len(finish) - 2 if last else 0
    operands = [*after, normed_t, *own, *other]
    if not first:
        operands.append(mixed)
    if last:
        operands.extend(finish)
    piece = (2, total, part, rows)
    shapes = [jax.ShapeDtypeStruct(piece, BF16), jax.ShapeDtypeStruct(piece, F32)]
    scratch = []
    if last:
        shapes += [
            jax.ShapeDtypeStruct((rows, width), BF16),
            jax.ShapeDtypeStruct((width, rows), BF16),
            jax.ShapeDtypeStruct((8, width), F32),
        ]
        scratch = [pltpu.VMEM((rows, width), F32)]
    else:
        shapes += [jax.ShapeDtypeStruct((rows, width), F32)]
    return pl.pallas_call(
        functools.partial(forward_kernel, first, blocks, len(own), len(after)),
        out_shape=tuple(shapes),
        in_specs=[ANY] * len(after) + [VMEM] * (len(operands) - len(after)),
        out_specs=tuple([VMEM] * len(shapes)),
        scratch_shapes=scratch,
        compiler_params=params(32),
        cost_estimate=COST,
        name="forward",
    )(*operands)


def pack_kernel(counts, *refs):
    out_ref = refs[-1]
    start = 0
    for count, ref in zip(counts, refs):
        out_ref[start:start + count] = ref[...].reshape(count, *out_ref.shape[1:])
        start += count


def pack(pieces, *after):
    counts = [1 if piece.ndim == 3 else piece.shape[0] for piece in pieces]
    return pl.pallas_call(
        functools.partial(pack_kernel, counts),
        out_shape=jax.ShapeDtypeStruct((sum(counts), *pieces[0].shape[-3:]), BF16),
        in_specs=[VMEM] * len(pieces) + [ANY] * len(after),
        out_specs=VMEM,
        compiler_params=params(16),
        cost_estimate=COST,
        name="pack",
    )(*pieces, *after)


def tie_kernel(*refs):
    pass


def tie(array, *after):
    return pl.pallas_call(
        tie_kernel,
        out_shape=jax.ShapeDtypeStruct(array.shape, array.dtype),
        in_specs=[ANY] * (1 + len(after)),
        out_specs=ANY,
        input_output_aliases={0: 0},
        compiler_params=params(4),
        cost_estimate=COST,
        name="tie",
    )(array, *after)


def mix_kernel(*refs):
    near_ref, other_ref = refs[:2]
    outs = refs[-near_ref.shape[0]:]
    for index, ref in enumerate(outs):
        ref[0] = near_ref[index]
        ref[1] = other_ref[index]


def mix(near, other, *after):
    count, each, width = near.shape
    return pl.pallas_call(
        mix_kernel,
        out_shape=tuple([jax.ShapeDtypeStruct((2, each, width), BF16)] * count),
        in_specs=[VMEM, VMEM] + [ANY] * len(after),
        out_specs=tuple([VMEM] * count),
        compiler_params=params(16),
        cost_estimate=COST,
        name="mix",
    )(near, other, *after)


def joined(refs, pieces, pick):
    values = [pick(refs[which], start, count) for which, start, count in pieces]
    flat = [value.reshape(-1, value.shape[-1]) for value in values]
    return flat[0] if len(flat) == 1 else jnp.concatenate(flat, axis=0)


def put(quarter, value, outs):
    own_ref, x_ref, y_ref, x_later_ref, y_later_ref = outs
    value = value.astype(BF16).reshape(own_ref.shape)
    half = x_ref.shape[0] // 2
    if quarter == 0:
        own_ref[...] = value
    elif quarter == 1:
        x_ref[half:] = value[:half]
        x_later_ref[...] = value[half:]
    elif quarter == 2:
        y_ref[half:] = value[half:]
        y_later_ref[...] = value[:half]
    else:
        x_ref[:half] = value[:half]
        y_ref[:half] = value[half:]


def emit(quarter, value, arrived, outs):
    if arrived is None:
        outs[0][quarter] = value.astype(BF16).reshape(outs[0].shape[1:])
    else:
        put(quarter, value + arrived[quarter].reshape(value.shape).astype(F32), outs)


def down_grad_kernel(side, act_pieces, add, *refs):
    acts, back_ref = refs[:2], refs[2]
    arrived = refs[3] if add else None
    outs = refs[4:] if add else refs[3:]
    for quarter in (3, 1, 2, 0):
        act = joined(acts, act_pieces[quarter], lambda ref, a, n: ref[side, a:a + n])
        emit(quarter, dot_nn(act, back_ref[...]), arrived, outs)


def up_grad_kernel(side, weight_pieces, act_pieces, add, *refs):
    weights, slopes = refs[:3], refs[3:5]
    back_t_ref, normed_ref, gain_in = refs[5:8]
    if add:
        arrived, scale_ref, small_ref = refs[8:11]
        outs, vector_ref, gain_ref = refs[11:-2], refs[-2], refs[-1]
    else:
        arrived = None
        outs, gain_ref = refs[8:-1], refs[-1]
    gain_ref[...] = gain_in[...]
    for quarter in (3, 1, 2, 0):
        pieces = weight_pieces[quarter]
        slope = joined(slopes, act_pieces[quarter], lambda ref, a, n: ref[side, a:a + n])
        back_act = dot_nn(joined(weights, pieces, lambda ref, a, n: ref[a:a + n, 1]), back_t_ref[...])
        back_hidden = (back_act * slope).astype(BF16)
        grad = dot_nn(back_hidden, normed_ref[...])
        up = joined(weights, pieces, lambda ref, a, n: ref[a:a + n, 0]).astype(F32)
        gain_ref[...] += jnp.sum(grad * up, axis=0, keepdims=True)
        emit(quarter, grad, arrived, outs)
    if add:
        vector_ref[0:1, :] = gain_ref[...] / scale_ref[...]
        vector_ref[1:3, :] = small_ref[0:2, :]
        vector_ref[3:8, :] = jnp.zeros((5, gain_ref.shape[1]), F32)


def gradient_shapes(depth, part, width, add):
    if not add:
        return [jax.ShapeDtypeStruct((4, depth, part, width), BF16)]
    counts = (depth, depth, depth, depth - depth // 2, depth // 2)
    return [jax.ShapeDtypeStruct((count, part, width), BF16) for count in counts]


def down_gradient(side, act_pieces, depth, acts, back, arrived=None):
    part = acts[0].shape[2]
    width = back.shape[1]
    add = arrived is not None
    operands = [*acts, back] + ([arrived] if add else [])
    shapes = gradient_shapes(depth, part, width, add)
    return pl.pallas_call(
        functools.partial(down_grad_kernel, side, act_pieces, add),
        out_shape=tuple(shapes),
        in_specs=[VMEM] * len(operands),
        out_specs=tuple([VMEM] * len(shapes)),
        compiler_params=params(20),
        cost_estimate=COST,
        name="down_gradient",
    )(*operands)


def up_gradient(
    side, weight_pieces, act_pieces, depth, weights, slopes, back_t, normed, gain, extra=()
):
    part, width = weights[0].shape[2:]
    add = len(extra) > 0
    operands = [*weights, *slopes, back_t, normed, gain, *extra]
    shapes = gradient_shapes(depth, part, width, add)
    if add:
        shapes.append(jax.ShapeDtypeStruct((8, width), F32))
        scratch = [pltpu.VMEM((1, width), F32)]
    else:
        scratch = []
        shapes.append(jax.ShapeDtypeStruct((1, width), F32))
    return pl.pallas_call(
        functools.partial(up_grad_kernel, side, weight_pieces, act_pieces, add),
        out_shape=tuple(shapes),
        in_specs=[VMEM] * len(operands),
        out_specs=tuple([VMEM] * len(shapes)),
        scratch_shapes=scratch,
        compiler_params=params(24),
        cost_estimate=COST,
        name="up_gradient",
    )(*operands)


def merge_kernel(x_ref, y_ref, x_later_ref, y_later_ref, *refs):
    x_out, y_out = refs[-2:]
    half = y_later_ref.shape[0]
    x_out[...] = (x_later_ref[...].astype(F32) + y_ref[:half].astype(F32)).astype(BF16)
    y_out[...] = (y_later_ref[...].astype(F32) + x_ref[:half].astype(F32)).astype(BF16)


def merge(x, y, x_later, y_later, *after):
    return pl.pallas_call(
        merge_kernel,
        out_shape=tuple(jax.ShapeDtypeStruct(a.shape, BF16) for a in (x_later, y_later)),
        in_specs=[VMEM] * 4 + [ANY] * len(after),
        out_specs=(VMEM, VMEM),
        compiler_params=params(16),
        cost_estimate=COST,
        name="merge",
    )(x, y, x_later, y_later, *after)


def total_kernel(own_ref, x_ref, y_ref, x_late_ref, y_late_ref, *outs):
    half = y_late_ref.shape[0]
    for index, out in enumerate(outs):
        total = own_ref[index].astype(F32)
        if index < half:
            total += x_ref[half + index].astype(F32) + y_late_ref[index].astype(F32)
        else:
            total += y_ref[index].astype(F32) + x_late_ref[index - half].astype(F32)
        out[...] = total.astype(BF16)


def totals(own, x, y, x_late, y_late):
    count, part, width = own.shape
    return pl.pallas_call(
        total_kernel,
        out_shape=tuple([jax.ShapeDtypeStruct((part, width), BF16)] * count),
        in_specs=[VMEM] * 5,
        out_specs=tuple([VMEM] * count),
        compiler_params=params(16),
        cost_estimate=COST,
        name="totals",
    )(own, x, y, x_late, y_late)


def collect_kernel(count, *refs):
    outs = refs[count:]
    part, width = refs[0].shape
    total = refs[0][...].astype(F32)
    for ref in refs[1:count]:
        total = total + ref[...].astype(F32)
    if len(outs) == 1:
        outs[0][...] = total.astype(BF16)
        return
    vector_ref, other_ref, short_ref, long_ref, held_ref = outs[0], outs[1], *outs[-3:]
    short_ref[pl.ds(0, part), :] = total.astype(BF16)
    rest = vector_ref[0:3, :]
    held_ref[...] = jnp.zeros_like(held_ref)
    for index in range(3):
        piece = rest.astype(BF16).astype(F32)
        held_ref[3 * index:3 * index + 3, :] = piece
        rest = rest - piece
    short_ref[pl.ds(part, 16), :] = held_ref[...].astype(BF16)
    long_ref[pl.ds(0, part + 16), :] = short_ref[...]
    long_ref[pl.ds(part + 16, part), :] = other_ref[...]


def collect(parts, vector=None, other=None, after=()):
    part, width = parts[0].shape
    operands = list(parts)
    if vector is None:
        counts = (part,)
        scratch = []
    else:
        operands += [vector, other]
        counts = (part + 16, 2 * part + 16)
        scratch = [pltpu.VMEM((16, width), F32)]
    return pl.pallas_call(
        functools.partial(collect_kernel, len(parts)),
        out_shape=tuple(jax.ShapeDtypeStruct((rows, width), BF16) for rows in counts),
        in_specs=[VMEM] * len(operands) + [ANY] * len(after),
        out_specs=tuple([VMEM] * len(counts)),
        scratch_shapes=scratch,
        compiler_params=params(16),
        cost_estimate=COST,
        name="collect",
    )(*operands, *after)


def place_kernel(part, tokens, group_ref, *refs):
    ups, downs = refs[:4], refs[4:8]
    up_ref, down_ref, gain_ref, scale_ref, loss_ref, held_ref = refs[8:]
    group = group_ref[0]
    vectors = []
    for index, (up, down) in enumerate(zip(ups, downs)):
        first = pl.multiple_of(jnp.bitwise_xor(group, index) * part, part)
        held_ref[pl.ds(first, part), :] = up[pl.ds(0, part), :].astype(F32)
        start = down.shape[0] - part
        down_ref[pl.ds(first, part), :] = down[pl.ds(start, part), :].astype(F32)
        rows = up[pl.ds(part, 16), :].astype(F32)
        vectors.append((rows[0:3] + rows[3:6]) + rows[6:9])
    up_ref[...] = held_ref[...].T
    vector = (vectors[0] + vectors[1]) + (vectors[2] + vectors[3])
    gain_ref[...] = vector[0:1]
    scale_ref[...] = vector[1:2]
    loss_ref[...] = vector[2:3, 0:1] * (1.0 / tokens)


def place_quarters(group, ups, downs, part, tokens):
    width = ups[0].shape[1]
    shapes = [
        jax.ShapeDtypeStruct((width, 4 * part), F32),
        jax.ShapeDtypeStruct((4 * part, width), F32),
        jax.ShapeDtypeStruct((1, width), F32),
        jax.ShapeDtypeStruct((1, width), F32),
        jax.ShapeDtypeStruct((1, 1), F32),
    ]
    return pl.pallas_call(
        functools.partial(place_kernel, part, tokens),
        out_shape=tuple(shapes),
        in_specs=[SMEM] + [VMEM] * 8,
        out_specs=tuple([VMEM] * len(shapes)),
        scratch_shapes=[pltpu.VMEM((4 * part, width), F32)],
        compiler_params=params(16),
        cost_estimate=COST,
        name="place",
    )(group, *ups, *downs)


def shards_square(
    image_tokens,
    tile_lists,
    opacity,
    tile_counts,
    ray_pixel,
    block_owner,
    gaussian_features,
    layer_norm_gain,
    layer_scale,
    up_weight,
    down_weight,
):
    ray_count = lax.axis_size("ray")
    group_count = lax.axis_size("grp")
    depth = ray_count // 2
    group = lax.axis_index("grp").reshape(1)
    me = lax.axis_index("ray").reshape(1)
    rows, width = image_tokens.shape
    part = down_weight.shape[0] // group_count

    def beside(array, flip):
        return lax.ppermute(array, "grp", [(g, g ^ flip) for g in range(group_count)])

    def partner(array, flip=1):
        return lax.ppermute(array, "ray", [(r, r ^ flip) for r in range(ray_count)])

    def along(array, shift):
        pairs = [(r, (r + 2 * shift) % ray_count) for r in range(ray_count)]
        return lax.ppermute(array, "ray", pairs)

    mine = own_quarter(group, up_weight, down_weight, part)
    arrivals = [along(mine, -shift) for shift in range(1, depth)]
    rendered, rendered_other = render(
        ray_count, True, me, block_owner, tile_lists, opacity, tile_counts.reshape(1, rows),
        ray_pixel, gaussian_features,
    )
    half = depth // 2
    low = pack([mine] + arrivals[:half - 1], rendered)
    x_low, y_low = beside(low, 1), beside(low, 2)
    high = pack(arrivals[half - 1:], low)
    x_high, y_high = beside(high, 1), beside(high, 2)
    d_low, d_high = beside(y_low, 1), beside(x_high, 2)
    blocks = mix(rendered, partner(rendered_other), x_low, y_low, high)
    targets = [blocks[0]] + [along(blocks[shift], shift) for shift in range(1, depth)]
    tokens, normed, normed_t = prepare_tokens(
        ray_count, True, me, block_owner, ray_pixel, image_tokens,
        layer_norm_gain.reshape(1, width),
    )
    most = pack([low, high, x_low, x_high, y_low, y_high], targets[half])
    most_other = partner(most)
    act_most, slope_most, mixed = forward(normed_t, [most], [most_other])
    late = [target for shift, target in enumerate(targets) if shift not in (0, half)]
    d_low, d_high = tie(d_low, mixed, *late), tie(d_high, mixed, *late)
    d_low_other, d_high_other = partner(d_low), partner(d_high)
    act_last, slope_last, back, back_t, small = forward(
        normed_t, [d_low, d_high], [d_low_other, d_high_other], mixed,
        (tokens, layer_scale.reshape(1, width), *targets),
    )
    acts = (act_most, act_last)
    slopes = (slope_most, slope_last)
    weights = ((most, d_low, d_high), (most_other, d_low_other, d_high_other))
    act_pieces = tuple(((0, quarter * depth, depth),) for quarter in range(3))
    act_pieces += (((1, 0, depth),),)
    weight_pieces = act_pieces[:3] + (((1, 0, half), (2, 0, depth - half)),)
    gain = jnp.zeros((1, width), F32)
    (down_other,) = down_gradient(1, act_pieces, depth, acts, back)
    down_arrived = partner(down_other)
    up_other, gain = up_gradient(
        1, weight_pieces, act_pieces, depth, weights[1], slopes, back_t, normed, gain
    )
    up_arrived = partner(up_other)
    down_sums = down_gradient(0, act_pieces, depth, acts, back, down_arrived)
    *up_sums, vector = up_gradient(
        0, weight_pieces, act_pieces, depth, weights[0], slopes, back_t, normed, gain,
        (up_arrived, layer_norm_gain.reshape(1, width), small),
    )
    vector = vector + partner(vector)
    flip = 2
    while flip < ray_count:
        vector = vector + partner(vector, flip)
        flip *= 2

    def sum_first(to_x, to_y, x_later, y_later, *after):
        from_x, from_y = beside(to_x, 1), beside(to_y, 2)
        return from_x, from_y, merge(from_x, from_y, x_later, y_later, *after)

    def sum_second(own, from_x, from_y, later):
        return totals(own, from_x, from_y, beside(later[0], 1), beside(later[1], 2))

    def arrive_along(shares):
        return [shares[0]] + [along(shares[shift], shift) for shift in range(1, depth)]

    own, *rest = down_sums
    *arrived, later = sum_first(*rest)
    shares = sum_second(own, *arrived, later)
    (down_total,) = collect(arrive_along(shares))
    down_x, down_y = beside(down_total, 1), beside(down_total, 2)
    own, *rest = up_sums
    *arrived, later = sum_first(*rest, vector)
    shares = sum_second(own, *arrived, later)
    short, long = collect(arrive_along(shares), vector, down_total, (down_x, down_y))
    up_x, up_y, both = beside(short, 1), beside(short, 2), beside(long, 3)
    grad_up, grad_down, gain, scale, loss = place_quarters(
        group, (short, up_x, up_y, both), (down_total, down_x, down_y, both), part,
        rows * ray_count * group_count,
    )
    return (grad_up, grad_down, gain.reshape(width), scale.reshape(width), loss.reshape(()))


def shards(*operands):
    ray_count, group_count = lax.axis_size("ray"), lax.axis_size("grp")
    hidden = operands[-1].shape[0]
    square = group_count == 4 and ray_count in (4, 8, 16) and hidden % (16 * group_count) == 0
    return (shards_square if square else shards_general)(*operands)


def solution(mesh):
    return jax.shard_map(
        shards,
        mesh=mesh,
        in_specs=(
            P(("grp", "ray"), None),
            P(None, ("grp", "ray")),
            P(None, ("grp", "ray")),
            P(("grp", "ray")),
            P("grp", None),
            P("grp", None),
            P(("grp", "ray"), None),
            P(),
            P(),
            P(None, "ray"),
            P("ray", None),
        ),
        out_specs=(P(None, "ray"), P("ray", None), P(), P(), P()),
        check_vma=False,
    )
```

```python
import functools

import jax
import jax.numpy as jnp
from jax import lax
from jax.experimental import pallas as pl
from jax.experimental.pallas import tpu as pltpu
from jax.sharding import PartitionSpec as P

STABILITY_EPSILON = 1e-06
F32 = jnp.float32
BF16 = jnp.bfloat16
MIB = 1024 * 1024
COST = pl.CostEstimate(flops=1 << 20, bytes_accessed=1 << 16, transcendentals=0)
LONG = pl.CostEstimate(flops=10**10, bytes_accessed=1 << 20, transcendentals=0)
SMEM = pl.BlockSpec(memory_space=pltpu.SMEM)
VMEM = pl.BlockSpec(memory_space=pltpu.VMEM)
ANY = pl.BlockSpec(memory_space=pl.ANY)


def params(mib=48, **more):
    return pltpu.CompilerParams(vmem_limit_bytes=mib * MIB, **more)


def dot_nn(a, b):
    return lax.dot_general(a, b, (((1,), (0,)), ((), ())), preferred_element_type=F32)


def dot_tn(a, b):
    return lax.dot_general(a, b, (((0,), (0,)), ((), ())), preferred_element_type=F32)


def dot_nt(a, b):
    return lax.dot_general(a, b, (((1,), (1,)), ((), ())), preferred_element_type=F32)


def owner_of(pixels, owner_ref, rows, count):
    block = lax.div(pixels, jnp.int32(rows))
    owner = jnp.zeros_like(pixels)
    for slot in range(count):
        owner = jnp.where(block == slot, owner_ref[0:1, slot:slot + 1], owner)
    return owner


def earlier(rows):
    before = lax.broadcasted_iota(jnp.int32, (rows, rows), 0)
    after = lax.broadcasted_iota(jnp.int32, (rows, rows), 1)
    return jnp.where(before < after, 1.0, 0.0).astype(BF16)


HBM = pl.BlockSpec(memory_space=pltpu.HBM)


def fetch(copies, sems):
    started = [
        pltpu.make_async_copy(source, target, sems.at[index])
        for index, (source, target) in enumerate(copies)
    ]
    for copy in started:
        copy.start()

    def wait(*numbers):
        for number in numbers:
            started[number].wait()

    return wait


def render_kernel(
    ray_count, relative, me_ref, owner_hbm, lists_hbm, opacity_hbm, counts_hbm, pixels_hbm,
    features_hbm, near_ref, other_ref, owner_ref, ids_ref, opacity_ref, counts_ref, mine_ref,
    features_ref, share_ref, table_ref, send_ref, sems,
):
    depth, rays = lists_hbm.shape
    gauss = features_hbm.shape[0]
    width = features_hbm.shape[1]
    me = me_ref[0]
    own_pixels = pixels_hbm.at[:, pl.ds(pl.multiple_of(me * rays, rays), rays)]
    wait = fetch(
        [
            (lists_hbm, ids_ref), (opacity_hbm, opacity_ref), (counts_hbm, counts_ref),
            (owner_hbm, owner_ref), (own_pixels, mine_ref), (features_hbm, features_ref),
        ],
        sems,
    )
    wait(0, 1, 2)
    ids_ref[...] = ids_ref[...] - me * gauss
    passing = jnp.ones((1, rays), F32)
    counts = counts_ref[...]
    for level in range(depth):
        alpha = opacity_ref[pl.ds(level, 1), :]
        share_ref[pl.ds(level, 1), :] = jnp.where(level < counts, alpha * passing, 0.0)
        passing = passing * (1.0 - alpha)

    tile = 256
    lanes = 128
    columns = rays // lanes

    @pl.loop(0, (gauss // tile) * columns)
    def _(step):
        first = pl.multiple_of(lax.div(step, columns) * tile, tile)
        lane = pl.multiple_of(lax.rem(step, columns) * lanes, lanes)
        number = (lax.broadcasted_iota(jnp.int32, (tile, lanes), 0) + first).astype(jnp.int16)
        total = jnp.zeros((tile, lanes), BF16)
        for level in range(depth):
            ident = jnp.broadcast_to(ids_ref[pl.ds(level, 1), pl.ds(lane, lanes)], (16, lanes))
            share = jnp.broadcast_to(share_ref[pl.ds(level, 1), pl.ds(lane, lanes)], (16, lanes))
            ident = jnp.concatenate([ident.astype(jnp.int16)] * (tile // 16), axis=0)
            share = jnp.concatenate([share.astype(BF16)] * (tile // 16), axis=0)
            total = total + jnp.where(ident == number, share, jnp.zeros_like(share))
        table_ref[pl.ds(first, tile), pl.ds(lane, lanes)] = total

    wait(3, 4, 5)
    owner = owner_of(mine_ref[...], owner_ref, rays, ray_count)
    padded = -(-ray_count // 16) * 16
    member = (lax.broadcasted_iota(jnp.int32, (padded, rays), 0) == owner)
    ranks = dot_nn(member.astype(F32).astype(BF16), earlier(rays))
    rank = jnp.sum(jnp.where(member, ranks, 0.0), axis=0, keepdims=True).astype(jnp.int32)
    if relative:
        chips = ray_count // 2
        shift = lax.div(owner, jnp.int32(2)) - lax.div(me, jnp.int32(2))
        shift = jnp.where(shift < 0, shift + chips, shift)
        flip = jnp.where(lax.rem(owner, jnp.int32(2)) == lax.rem(me, jnp.int32(2)), 0, 1)
        block = flip * chips + shift
    else:
        block = owner
    slot = block * (rays // ray_count) + rank
    send_ref[...] = (
        (lax.broadcasted_iota(jnp.int32, (rays, rays), 0) == slot).astype(F32).astype(BF16)
    )

    piece = 256
    half = rays // 2

    @pl.loop(0, width // piece)
    def _(step):
        cols = pl.ds(pl.multiple_of(step * piece, piece), piece)
        rendered = dot_tn(table_ref[...], features_ref[:, cols]).astype(BF16)
        ordered = dot_nn(send_ref[...], rendered).astype(BF16)
        near_ref[:, :, cols] = ordered[:half].reshape(*near_ref.shape[:2], piece)
        other_ref[:, :, cols] = ordered[half:].reshape(*other_ref.shape[:2], piece)


def render(ray_count, relative, me, owner, lists, opacity, counts, pixels, features):
    depth, rays = lists.shape
    gauss, width = features.shape
    shape = jax.ShapeDtypeStruct((ray_count // 2, rays // ray_count, width), BF16)
    return pl.pallas_call(
        functools.partial(render_kernel, ray_count, relative),
        out_shape=(shape, shape),
        in_specs=[SMEM] + [HBM] * 6,
        out_specs=(VMEM, VMEM),
        scratch_shapes=[
            pltpu.VMEM(owner.shape, jnp.int32),
            pltpu.VMEM((depth, rays), jnp.int32),
            pltpu.VMEM((depth, rays), F32),
            pltpu.VMEM((1, rays), jnp.int32),
            pltpu.VMEM((1, rays), jnp.int32),
            pltpu.VMEM((gauss, width), BF16),
            pltpu.VMEM((depth, rays), F32),
            pltpu.VMEM((gauss, rays), BF16),
            pltpu.VMEM((rays, rays), BF16),
            pltpu.SemaphoreType.DMA((6,)),
        ],
        compiler_params=params(20),
        cost_estimate=COST,
        name="render",
    )(me, owner, lists, opacity, counts, pixels, features)


def tokens_kernel(
    ray_count, relative, me_ref, owner_hbm, pixels_hbm, tokens_hbm, gain_hbm,
    *refs,
):
    tokens_out, normed_out, normed_t_out = refs[-11:-8]
    owner_ref, pixels_ref, tokens_ref, gain_ref, order_ref, rank_ref, place_ref, sems = refs[-8:]
    rows, width = tokens_hbm.shape
    me = me_ref[0]
    each = rows // ray_count
    wait = fetch(
        [
            (owner_hbm, owner_ref), (pixels_hbm, pixels_ref), (gain_hbm, gain_ref),
            (tokens_hbm, tokens_ref),
        ],
        sems,
    )
    wait(0, 1)
    pixels = jnp.concatenate(
        [pixels_ref[:, sender * rows:(sender + 1) * rows] for sender in range(ray_count)], axis=0
    )
    mine = owner_of(pixels, owner_ref, rows, ray_count) == me
    place_ref[...] = lax.rem(pixels, jnp.int32(rows)).astype(F32)
    member = jnp.where(mine, 1.0, 0.0)
    padded = -(-ray_count // 16) * 16
    if padded > ray_count:
        spread = jnp.concatenate([member, jnp.zeros((padded - ray_count, rows), F32)], axis=0)
    else:
        spread = member
    ranks = dot_nn(spread.astype(BF16), earlier(rows))
    rank_ref[...] = jnp.where(mine, ranks[:ray_count], -1.0)
    chips = ray_count // 2
    for index in range(ray_count):
        if relative:
            chip = lax.rem(lax.div(me, jnp.int32(2)) + (chips - index // 2), jnp.int32(chips))
            sender = 2 * chip + jnp.bitwise_xor(lax.rem(me, jnp.int32(2)), index % 2)
        else:
            sender = index
        rank = rank_ref[pl.ds(sender, 1), :].astype(jnp.int32)
        hit = lax.broadcasted_iota(jnp.int32, (each, rows), 0) == rank
        at = jnp.sum(
            jnp.where(hit, place_ref[pl.ds(sender, 1), :], 0.0), axis=1, keepdims=True
        )
        here = lax.broadcasted_iota(jnp.int32, (each, rows), 1) == at.astype(jnp.int32)
        order_ref[pl.ds(index * each, each), :] = here.astype(F32).astype(BF16)
    wait(2, 3)
    half = min(128, rows)
    gain = gain_ref[...]

    @pl.loop(0, rows // half)
    def _(step):
        span = pl.ds(pl.multiple_of(step * half, half), half)
        values = dot_nn(order_ref[span, :], tokens_ref[...])
        tokens_out[span, :] = values.astype(BF16)
        centered = values - jnp.mean(values, axis=-1, keepdims=True)
        variance = jnp.mean(centered * centered, axis=-1, keepdims=True)
        xhat = centered * lax.rsqrt(variance + STABILITY_EPSILON)
        normed = (xhat * gain).astype(BF16)
        normed_out[span, :] = normed
        normed_t_out[:, span] = normed.T


def prepare_tokens(ray_count, relative, me, owner, pixels, tokens, gain, after=()):
    rows, width = tokens.shape
    return pl.pallas_call(
        functools.partial(tokens_kernel, ray_count, relative),
        out_shape=(
            jax.ShapeDtypeStruct((rows, width), BF16),
            jax.ShapeDtypeStruct((rows, width), BF16),
            jax.ShapeDtypeStruct((width, rows), BF16),
        ),
        in_specs=[SMEM] + [HBM] * 4 + [ANY] * len(after),
        out_specs=(VMEM, VMEM, VMEM),
        scratch_shapes=[
            pltpu.VMEM(owner.shape, jnp.int32),
            pltpu.VMEM(pixels.shape, jnp.int32),
            pltpu.VMEM((rows, width), BF16),
            pltpu.VMEM((1, width), F32),
            pltpu.VMEM((rows, rows), BF16),
            pltpu.VMEM((ray_count, rows), F32),
            pltpu.VMEM((ray_count, rows), F32),
            pltpu.SemaphoreType.DMA((4,)),
        ],
        compiler_params=params(20),
        cost_estimate=COST,
        name="tokens",
    )(me, owner, pixels, tokens, gain, *after)


def up_kernel(normed_ref, up_ref, act_ref, slope_ref):
    parts, _, part_rows, width = up_ref.shape
    up = up_ref[...].reshape(parts * part_rows, width)
    rows = normed_ref.shape[0]
    piece = min(128, rows)

    @pl.loop(0, rows // piece)
    def _(step):
        span = pl.ds(pl.multiple_of(step * piece, piece), piece)
        hidden = dot_nn(normed_ref[span, :], up)
        phi = 0.5 * (1.0 + lax.erf(hidden * (0.5 ** 0.5)))
        density = jnp.exp(-0.5 * hidden * hidden) * ((2.0 * jnp.pi) ** -0.5)
        act_ref[span, :] = (hidden * phi).astype(BF16)
        slope_ref[span, :] = (phi + hidden * density).astype(slope_ref.dtype)


def project_up(normed, up):
    rows, width = normed.shape
    parts, chunks, part_rows, chunk = up.shape
    return pl.pallas_call(
        up_kernel,
        grid=(chunks,),
        out_shape=(
            jax.ShapeDtypeStruct((rows, chunks * chunk), BF16),
            jax.ShapeDtypeStruct((rows, chunks * chunk), F32),
        ),
        in_specs=[
            pl.BlockSpec((rows, width), lambda j: (0, 0)),
            pl.BlockSpec((parts, 1, part_rows, chunk), lambda j: (0, j, 0, 0)),
        ],
        out_specs=(
            pl.BlockSpec((rows, chunk), lambda j: (0, j)),
            pl.BlockSpec((rows, chunk), lambda j: (0, j)),
        ),
        compiler_params=params(dimension_semantics=("arbitrary",)),
        cost_estimate=COST,
        name="up",
    )(normed, up)


def down_kernel(
    chunks, act_ref, down_ref, tokens_ref, target_ref, scale_ref,
    grad_ref, back_ref, small_ref, mixed_ref,
):
    step = pl.program_id(0)
    rows, width = tokens_ref.shape
    act = act_ref[...]

    @pl.when(step < chunks)
    def _():
        parts, _, part_rows, _ = down_ref.shape
        part = dot_nn(act, down_ref[...].reshape(parts * part_rows, width))

        @pl.when(step == 0)
        def _():
            mixed_ref[...] = part

        @pl.when(step > 0)
        def _():
            mixed_ref[...] += part

    @pl.when(step == chunks - 1)
    def _():
        scale = scale_ref[...]
        small_ref[...] = jnp.zeros_like(small_ref)
        piece = min(64, rows)

        @pl.loop(0, rows // piece)
        def _(index):
            span = pl.ds(pl.multiple_of(index * piece, piece), piece)
            mixed = mixed_ref[span, :]
            out = tokens_ref[span, :].astype(F32) + scale * mixed
            goal = target_ref[span, :].astype(F32)
            out_norm = jnp.sqrt(jnp.sum(out * out, axis=-1, keepdims=True) + STABILITY_EPSILON)
            goal_norm = jnp.sqrt(jnp.sum(goal * goal, axis=-1, keepdims=True) + STABILITY_EPSILON)
            norms = out_norm * goal_norm
            cosine = jnp.sum(out * goal, axis=-1, keepdims=True) / norms
            upstream = (cosine / (out_norm * out_norm)) * out - goal * (1.0 / norms)
            back_ref[span, :] = (upstream * scale).astype(BF16)
            small_ref[0:1, :] += jnp.sum(upstream * mixed, axis=0, keepdims=True)
            loss = jnp.sum(1.0 - cosine, axis=0, keepdims=True)
            small_ref[1:2, :] += jnp.broadcast_to(loss, (1, width))

    @pl.when(step >= chunks)
    def _():
        grad = dot_tn(act, back_ref[...])
        grad_ref[...] = grad.astype(BF16).reshape(grad_ref.shape)


def project_down(act, down, tokens, target, scale):
    rows, width = tokens.shape
    parts, chunks, part_rows, _ = down.shape
    chunk = parts * part_rows
    return pl.pallas_call(
        functools.partial(down_kernel, chunks),
        grid=(2 * chunks,),
        out_shape=(
            jax.ShapeDtypeStruct(down.shape, BF16),
            jax.ShapeDtypeStruct((rows, width), BF16),
            jax.ShapeDtypeStruct((8, width), F32),
        ),
        in_specs=[
            pl.BlockSpec((rows, chunk), lambda j: (0, lax.rem(j, chunks))),
            pl.BlockSpec(
                (parts, 1, part_rows, width), lambda j: (0, jnp.minimum(j, chunks - 1), 0, 0)
            ),
            pl.BlockSpec((rows, width), lambda j: (0, 0)),
            pl.BlockSpec((rows, width), lambda j: (0, 0)),
            pl.BlockSpec((1, width), lambda j: (0, 0)),
        ],
        out_specs=(
            pl.BlockSpec(
                (parts, 1, part_rows, width), lambda j: (0, jnp.maximum(j - chunks, 0), 0, 0)
            ),
            pl.BlockSpec((rows, width), lambda j: (0, 0)),
            pl.BlockSpec((8, width), lambda j: (0, 0)),
        ),
        scratch_shapes=[pltpu.VMEM((rows, width), F32)],
        compiler_params=params(dimension_semantics=("arbitrary",)),
        cost_estimate=COST,
        name="down",
    )(act, down, tokens, target, scale)


def back_kernel(back_ref, down_ref, slope_ref, normed_t_ref, up_ref, gain_ref, grad_ref, sum_ref):
    step = pl.program_id(0)
    parts, _, part_rows, width = down_ref.shape
    chunk = parts * part_rows
    rows = back_ref.shape[0]
    back_act = dot_nt(back_ref[...], down_ref[...].reshape(chunk, width))
    back_hidden = (back_act * slope_ref[...]).astype(BF16)
    up_parts, _, up_rows, _ = up_ref.shape

    @pl.when(step == 0)
    def _():
        sum_ref[...] = jnp.zeros_like(sum_ref)

    grad = dot_nn(normed_t_ref[...], back_hidden)
    grad_ref[...] = grad.astype(BF16).reshape(grad_ref.shape)
    up = up_ref[...].reshape(up_parts * up_rows, chunk).astype(F32)
    sum_ref[...] += jnp.sum(grad * up, axis=1, keepdims=True) / gain_ref[...]


def back_up(back, down, slope, normed_t, up, gain):
    width, rows = normed_t.shape
    parts, chunks, part_rows, _ = down.shape
    chunk = parts * part_rows
    up_parts, _, up_rows, _ = up.shape
    return pl.pallas_call(
        back_kernel,
        grid=(chunks,),
        out_shape=(
            jax.ShapeDtypeStruct(up.shape, BF16),
            jax.ShapeDtypeStruct((width, 1), F32),
        ),
        in_specs=[
            pl.BlockSpec((rows, width), lambda j: (0, 0)),
            pl.BlockSpec((parts, 1, part_rows, width), lambda j: (0, j, 0, 0)),
            pl.BlockSpec((rows, chunk), lambda j: (0, j)),
            pl.BlockSpec((width, rows), lambda j: (0, 0)),
            pl.BlockSpec((up_parts, 1, up_rows, chunk), lambda j: (0, j, 0, 0)),
            pl.BlockSpec((width, 1), lambda j: (0, 0)),
        ],
        out_specs=(
            pl.BlockSpec((up_parts, 1, up_rows, chunk), lambda j: (0, j, 0, 0)),
            pl.BlockSpec((width, 1), lambda j: (0, 0)),
        ),
        compiler_params=params(dimension_semantics=("arbitrary",)),
        cost_estimate=COST,
        name="back",
    )(back, down, slope, normed_t, up, gain)


def gather_weight(weight, parts, group, group_count, ray_count):
    rows, cols = weight.shape
    if parts == 1:
        whole = lax.all_gather(weight, "ray", axis=0, tiled=True)
    else:
        part = lax.dynamic_slice_in_dim(weight, group * (rows // parts), rows // parts, 0)
        whole = lax.all_gather(part, ("grp", "ray"), axis=0, tiled=True)
    return whole.reshape(parts, ray_count, rows // parts, cols)


def reduce_gradient(grad):
    parts, ray_count, part_rows, cols = grad.shape
    flat = grad.reshape(parts * ray_count * part_rows, cols)
    if parts == 1:
        share = lax.psum_scatter(flat, "ray", scatter_dimension=0, tiled=True)
        return lax.psum(share.astype(F32), "grp")
    share = lax.psum_scatter(flat, "grp", scatter_dimension=0, tiled=True)
    share = lax.psum_scatter(share, "ray", scatter_dimension=0, tiled=True)
    return lax.all_gather(share, "grp", axis=0, tiled=True).astype(F32)


def shards_general(
    image_tokens,
    tile_lists,
    opacity,
    tile_counts,
    ray_pixel,
    block_owner,
    gaussian_features,
    layer_norm_gain,
    layer_scale,
    up_weight,
    down_weight,
):
    ray_count = lax.axis_size("ray")
    group_count = lax.axis_size("grp")
    group = lax.axis_index("grp")
    me = lax.axis_index("ray").reshape(1)
    rows, width = image_tokens.shape
    up_parts = group_count if up_weight.shape[0] % (16 * group_count) == 0 else 1
    down_parts = group_count if down_weight.shape[0] % (16 * group_count) == 0 else 1
    up = gather_weight(up_weight, up_parts, group, group_count, ray_count)
    down = gather_weight(down_weight, down_parts, group, group_count, ray_count)
    rendered = render(
        ray_count, False, me, block_owner, tile_lists, opacity, tile_counts.reshape(1, rows),
        ray_pixel, gaussian_features,
    )
    rendered = jnp.concatenate(rendered, axis=0).reshape(rows, width)
    target = lax.all_to_all(rendered, "ray", split_axis=0, concat_axis=0, tiled=True)
    tokens, normed, normed_t = prepare_tokens(
        ray_count, False, me, block_owner, ray_pixel, image_tokens,
        layer_norm_gain.reshape(1, width),
    )
    act, slope = project_up(normed, up)
    grad_down, back, small = project_down(act, down, tokens, target, layer_scale.reshape(1, width))
    grad_up, gain_sum = back_up(back, down, slope, normed_t, up, layer_norm_gain.reshape(width, 1))
    grad_down = reduce_gradient(grad_down)
    grad_up = reduce_gradient(grad_up)
    sums = jnp.concatenate([gain_sum.reshape(1, width), small[:2]], axis=0)
    sums = lax.psum(sums, ("grp", "ray"))
    loss = sums[2, 0] / (rows * ray_count * group_count)
    return (grad_up, grad_down, sums[0], sums[1], loss)


def quarter_kernel(group_ref, up_hbm, down_hbm, out_ref, up_ref, turned_ref, sems):
    part = out_ref.shape[1]
    lanes = up_ref.shape[1]
    start = pl.multiple_of(group_ref[0] * part, part)
    lane = pl.multiple_of(lax.div(start, jnp.int32(lanes)) * lanes, lanes)
    wait = fetch(
        [
            (up_hbm.at[:, pl.ds(lane, lanes)], up_ref),
            (down_hbm.at[pl.ds(start, part), :], out_ref.at[1]),
        ],
        sems,
    )
    wait(0)
    turned_ref[...] = up_ref[...].T
    out_ref[0] = turned_ref[pl.ds(pl.multiple_of(start - lane, part), part), :]
    wait(1)


def own_quarter(group, up, down, part):
    width, chunk = up.shape
    lanes = max(128, part)
    return pl.pallas_call(
        quarter_kernel,
        out_shape=jax.ShapeDtypeStruct((2, part, width), BF16),
        in_specs=[SMEM, HBM, HBM],
        out_specs=VMEM,
        scratch_shapes=[
            pltpu.VMEM((width, lanes), BF16),
            pltpu.VMEM((lanes, width), BF16),
            pltpu.SemaphoreType.DMA((2,)),
        ],
        compiler_params=params(16),
        cost_estimate=LONG,
        name="quarter",
    )(group, up, down)


def finish_rows(tokens, mixed, goal, scale):
    out = tokens + scale * mixed
    out_norm = jnp.sqrt(jnp.sum(out * out, axis=-1, keepdims=True) + STABILITY_EPSILON)
    goal_norm = jnp.sqrt(jnp.sum(goal * goal, axis=-1, keepdims=True) + STABILITY_EPSILON)
    norms = out_norm * goal_norm
    cosine = jnp.sum(out * goal, axis=-1, keepdims=True) / norms
    upstream = (cosine / (out_norm * out_norm)) * out - goal * (1.0 / norms)
    return upstream, 1.0 - cosine


def forward_kernel(first, blocks, sides, skipped, *refs):
    last = blocks > 0
    refs = list(refs[skipped:])
    normed_t_ref = refs.pop(0)
    own, other = refs[:sides], refs[sides:2 * sides]
    del refs[:2 * sides]
    mixed_in = None if first else refs.pop(0)
    if last:
        tokens_ref, scale_ref = refs[:2]
        targets = refs[2:2 + blocks]
        del refs[:2 + blocks]
    act_ref, slope_ref = refs[:2]
    del refs[:2]
    width, rows = normed_t_ref.shape
    part = act_ref.shape[2]
    part_sum = None
    downs = []
    for side, group in enumerate((own, other)):
        start = 0
        for ref in group:
            count = ref.shape[0]
            hiddens = dot_nn(ref[:, 0].reshape(count * part, width), normed_t_ref[...])
            for index in range(count):
                hidden = hiddens[index * part:(index + 1) * part]
                phi = 0.5 * (1.0 + lax.erf(hidden * (0.5 ** 0.5)))
                density = jnp.exp(-0.5 * hidden * hidden) * ((2.0 * jnp.pi) ** -0.5)
                act_ref[side, start + index] = (hidden * phi).astype(BF16)
                slope_ref[side, start + index] = phi + hidden * density
            downs.append(ref[:, 1].reshape(count * part, width))
            start += count
    if sides > 1:
        act = act_ref[...].reshape(2 * start * part, rows)
        part_sum = dot_tn(act, jnp.concatenate(downs, axis=0))
    else:
        for side, down in enumerate(downs):
            term = dot_tn(act_ref[side].reshape(start * part, rows), down)
            part_sum = term if part_sum is None else part_sum + term
    if not last:
        mixed_out = refs[0]
        mixed_out[...] = part_sum if first else mixed_in[...] + part_sum
        return
    back_ref, back_t_ref, small_ref, mixed_ref = refs
    mixed_ref[...] = mixed_in[...] + part_sum
    scale = scale_ref[...]
    small_ref[...] = jnp.zeros_like(small_ref)
    piece = rows // blocks
    for index, target_ref in enumerate(targets):
        span = pl.ds(index * piece, piece)
        mixed = mixed_ref[span, :]
        upstream, loss = finish_rows(
            tokens_ref[span, :].astype(F32), mixed,
            target_ref[...].reshape(piece, width).astype(F32), scale,
        )
        back = (upstream * scale).astype(BF16)
        back_ref[span, :] = back
        back_t_ref[:, span] = back.T
        small_ref[0:1, :] += jnp.sum(upstream * mixed, axis=0, keepdims=True)
        small_ref[1:2, :] += jnp.broadcast_to(jnp.sum(loss, axis=0, keepdims=True), (1, width))


def forward(normed_t, own, other, mixed=None, finish=None, after=()):
    width, rows = normed_t.shape
    part = own[0].shape[2]
    total = sum(array.shape[0] for array in own)
    first, last = mixed is None, finish is not None
    blocks = len(finish) - 2 if last else 0
    operands = [*after, normed_t, *own, *other]
    if not first:
        operands.append(mixed)
    if last:
        operands.extend(finish)
    piece = (2, total, part, rows)
    shapes = [jax.ShapeDtypeStruct(piece, BF16), jax.ShapeDtypeStruct(piece, F32)]
    scratch = []
    if last:
        shapes += [
            jax.ShapeDtypeStruct((rows, width), BF16),
            jax.ShapeDtypeStruct((width, rows), BF16),
            jax.ShapeDtypeStruct((8, width), F32),
        ]
        scratch = [pltpu.VMEM((rows, width), F32)]
    else:
        shapes += [jax.ShapeDtypeStruct((rows, width), F32)]
    return pl.pallas_call(
        functools.partial(forward_kernel, first, blocks, len(own), len(after)),
        out_shape=tuple(shapes),
        in_specs=[ANY] * len(after) + [VMEM] * (len(operands) - len(after)),
        out_specs=tuple([VMEM] * len(shapes)),
        scratch_shapes=scratch,
        compiler_params=params(32),
        cost_estimate=COST,
        name="forward",
    )(*operands)


def pack_kernel(counts, *refs):
    out_ref = refs[-1]
    start = 0
    for count, ref in zip(counts, refs):
        out_ref[start:start + count] = ref[...].reshape(count, *out_ref.shape[1:])
        start += count


def pack(pieces, *after):
    counts = [1 if piece.ndim == 3 else piece.shape[0] for piece in pieces]
    return pl.pallas_call(
        functools.partial(pack_kernel, counts),
        out_shape=jax.ShapeDtypeStruct((sum(counts), *pieces[0].shape[-3:]), BF16),
        in_specs=[VMEM] * len(pieces) + [ANY] * len(after),
        out_specs=VMEM,
        compiler_params=params(16),
        cost_estimate=COST,
        name="pack",
    )(*pieces, *after)


def tie_kernel(*refs):
    pass


def tie(array, *after):
    return pl.pallas_call(
        tie_kernel,
        out_shape=jax.ShapeDtypeStruct(array.shape, array.dtype),
        in_specs=[ANY] * (1 + len(after)),
        out_specs=ANY,
        input_output_aliases={0: 0},
        compiler_params=params(4),
        cost_estimate=COST,
        name="tie",
    )(array, *after)


def mix_kernel(*refs):
    near_ref, other_ref = refs[:2]
    outs = refs[-near_ref.shape[0]:]
    for index, ref in enumerate(outs):
        ref[0] = near_ref[index]
        ref[1] = other_ref[index]


def mix(near, other, *after):
    count, each, width = near.shape
    return pl.pallas_call(
        mix_kernel,
        out_shape=tuple([jax.ShapeDtypeStruct((2, each, width), BF16)] * count),
        in_specs=[VMEM, VMEM] + [ANY] * len(after),
        out_specs=tuple([VMEM] * count),
        compiler_params=params(16),
        cost_estimate=COST,
        name="mix",
    )(near, other, *after)


def joined(refs, pieces, pick):
    values = [pick(refs[which], start, count) for which, start, count in pieces]
    flat = [value.reshape(-1, value.shape[-1]) for value in values]
    return flat[0] if len(flat) == 1 else jnp.concatenate(flat, axis=0)


def put(quarter, value, outs):
    own_ref, x_ref, y_ref, x_later_ref, y_later_ref = outs
    value = value.astype(BF16).reshape(own_ref.shape)
    half = x_ref.shape[0] // 2
    if quarter == 0:
        own_ref[...] = value
    elif quarter == 1:
        x_ref[half:] = value[:half]
        x_later_ref[...] = value[half:]
    elif quarter == 2:
        y_ref[half:] = value[half:]
        y_later_ref[...] = value[:half]
    else:
        x_ref[:half] = value[:half]
        y_ref[:half] = value[half:]


def emit(quarter, value, arrived, outs):
    if arrived is None:
        outs[0][quarter] = value.astype(BF16).reshape(outs[0].shape[1:])
    else:
        put(quarter, value + arrived[quarter].reshape(value.shape).astype(F32), outs)


def down_grad_kernel(side, act_pieces, add, *refs):
    acts, back_ref = refs[:2], refs[2]
    arrived = refs[3] if add else None
    outs = refs[4:] if add else refs[3:]
    for quarter in (3, 1, 2, 0):
        act = joined(acts, act_pieces[quarter], lambda ref, a, n: ref[side, a:a + n])
        emit(quarter, dot_nn(act, back_ref[...]), arrived, outs)


def up_grad_kernel(side, weight_pieces, act_pieces, add, *refs):
    weights, slopes = refs[:3], refs[3:5]
    back_t_ref, normed_ref, gain_in = refs[5:8]
    if add:
        arrived, scale_ref, small_ref = refs[8:11]
        outs, vector_ref, gain_ref = refs[11:-2], refs[-2], refs[-1]
    else:
        arrived = None
        outs, gain_ref = refs[8:-1], refs[-1]
    gain_ref[...] = gain_in[...]
    for quarter in (3, 1, 2, 0):
        pieces = weight_pieces[quarter]
        slope = joined(slopes, act_pieces[quarter], lambda ref, a, n: ref[side, a:a + n])
        back_act = dot_nn(joined(weights, pieces, lambda ref, a, n: ref[a:a + n, 1]), back_t_ref[...])
        back_hidden = (back_act * slope).astype(BF16)
        grad = dot_nn(back_hidden, normed_ref[...])
        up = joined(weights, pieces, lambda ref, a, n: ref[a:a + n, 0]).astype(F32)
        gain_ref[...] += jnp.sum(grad * up, axis=0, keepdims=True)
        emit(quarter, grad, arrived, outs)
    if add:
        vector_ref[0:1, :] = gain_ref[...] / scale_ref[...]
        vector_ref[1:3, :] = small_ref[0:2, :]
        vector_ref[3:8, :] = jnp.zeros((5, gain_ref.shape[1]), F32)


def gradient_shapes(depth, part, width, add):
    if not add:
        return [jax.ShapeDtypeStruct((4, depth, part, width), BF16)]
    counts = (depth, depth, depth, depth - depth // 2, depth // 2)
    return [jax.ShapeDtypeStruct((count, part, width), BF16) for count in counts]


def down_gradient(side, act_pieces, depth, acts, back, arrived=None):
    part = acts[0].shape[2]
    width = back.shape[1]
    add = arrived is not None
    operands = [*acts, back] + ([arrived] if add else [])
    shapes = gradient_shapes(depth, part, width, add)
    return pl.pallas_call(
        functools.partial(down_grad_kernel, side, act_pieces, add),
        out_shape=tuple(shapes),
        in_specs=[VMEM] * len(operands),
        out_specs=tuple([VMEM] * len(shapes)),
        compiler_params=params(20),
        cost_estimate=COST,
        name="down_gradient",
    )(*operands)


def up_gradient(
    side, weight_pieces, act_pieces, depth, weights, slopes, back_t, normed, gain, extra=()
):
    part, width = weights[0].shape[2:]
    add = len(extra) > 0
    operands = [*weights, *slopes, back_t, normed, gain, *extra]
    shapes = gradient_shapes(depth, part, width, add)
    if add:
        shapes.append(jax.ShapeDtypeStruct((8, width), F32))
        scratch = [pltpu.VMEM((1, width), F32)]
    else:
        scratch = []
        shapes.append(jax.ShapeDtypeStruct((1, width), F32))
    return pl.pallas_call(
        functools.partial(up_grad_kernel, side, weight_pieces, act_pieces, add),
        out_shape=tuple(shapes),
        in_specs=[VMEM] * len(operands),
        out_specs=tuple([VMEM] * len(shapes)),
        scratch_shapes=scratch,
        compiler_params=params(24),
        cost_estimate=COST,
        name="up_gradient",
    )(*operands)


def merge_kernel(x_ref, y_ref, x_later_ref, y_later_ref, *refs):
    x_out, y_out = refs[-2:]
    half = y_later_ref.shape[0]
    x_out[...] = (x_later_ref[...].astype(F32) + y_ref[:half].astype(F32)).astype(BF16)
    y_out[...] = (y_later_ref[...].astype(F32) + x_ref[:half].astype(F32)).astype(BF16)


def merge(x, y, x_later, y_later, *after):
    return pl.pallas_call(
        merge_kernel,
        out_shape=tuple(jax.ShapeDtypeStruct(a.shape, BF16) for a in (x_later, y_later)),
        in_specs=[VMEM] * 4 + [ANY] * len(after),
        out_specs=(VMEM, VMEM),
        compiler_params=params(16),
        cost_estimate=COST,
        name="merge",
    )(x, y, x_later, y_later, *after)


def total_kernel(own_ref, x_ref, y_ref, x_late_ref, y_late_ref, *refs):
    outs = refs[-own_ref.shape[0]:]
    half = y_late_ref.shape[0]
    for index, out in enumerate(outs):
        total = own_ref[index].astype(F32)
        if index < half:
            total += x_ref[half + index].astype(F32) + y_late_ref[index].astype(F32)
        else:
            total += y_ref[index].astype(F32) + x_late_ref[index - half].astype(F32)
        out[...] = total.astype(BF16)


def totals(own, x, y, x_late, y_late, *after):
    count, part, width = own.shape
    return pl.pallas_call(
        total_kernel,
        out_shape=tuple([jax.ShapeDtypeStruct((part, width), BF16)] * count),
        in_specs=[VMEM] * 5 + [ANY] * len(after),
        out_specs=tuple([VMEM] * count),
        compiler_params=params(16),
        cost_estimate=COST,
        name="totals",
    )(own, x, y, x_late, y_late, *after)


def collect_kernel(count, *refs):
    outs = refs[count:]
    part, width = refs[0].shape
    total = refs[0][...].astype(F32)
    for ref in refs[1:count]:
        total = total + ref[...].astype(F32)
    if len(outs) == 1:
        outs[0][...] = total.astype(BF16)
        return
    vector_ref, other_ref, short_ref, long_ref, held_ref = outs[0], outs[1], *outs[-3:]
    short_ref[pl.ds(0, part), :] = total.astype(BF16)
    rest = vector_ref[0:3, :]
    held_ref[...] = jnp.zeros_like(held_ref)
    for index in range(3):
        piece = rest.astype(BF16).astype(F32)
        held_ref[3 * index:3 * index + 3, :] = piece
        rest = rest - piece
    short_ref[pl.ds(part, 16), :] = held_ref[...].astype(BF16)
    long_ref[pl.ds(0, part + 16), :] = short_ref[...]
    long_ref[pl.ds(part + 16, part), :] = other_ref[...]


def collect(parts, vector=None, other=None, after=()):
    part, width = parts[0].shape
    operands = list(parts)
    if vector is None:
        counts = (part,)
        scratch = []
    else:
        operands += [vector, other]
        counts = (part + 16, 2 * part + 16)
        scratch = [pltpu.VMEM((16, width), F32)]
    return pl.pallas_call(
        functools.partial(collect_kernel, len(parts)),
        out_shape=tuple(jax.ShapeDtypeStruct((rows, width), BF16) for rows in counts),
        in_specs=[VMEM] * len(operands) + [ANY] * len(after),
        out_specs=tuple([VMEM] * len(counts)),
        scratch_shapes=scratch,
        compiler_params=params(16),
        cost_estimate=COST,
        name="collect",
    )(*operands, *after)


def place_kernel(part, tokens, group_ref, *refs):
    ups, downs = refs[:4], refs[4:8]
    up_ref, down_ref, gain_ref, scale_ref, loss_ref, held_ref = refs[8:]
    group = group_ref[0]
    vectors = []
    for index, (up, down) in enumerate(zip(ups, downs)):
        first = pl.multiple_of(jnp.bitwise_xor(group, index) * part, part)
        held_ref[pl.ds(first, part), :] = up[pl.ds(0, part), :].astype(F32)
        start = down.shape[0] - part
        down_ref[pl.ds(first, part), :] = down[pl.ds(start, part), :].astype(F32)
        rows = up[pl.ds(part, 16), :].astype(F32)
        vectors.append((rows[0:3] + rows[3:6]) + rows[6:9])
    up_ref[...] = held_ref[...].T
    vector = (vectors[0] + vectors[1]) + (vectors[2] + vectors[3])
    gain_ref[...] = vector[0:1]
    scale_ref[...] = vector[1:2]
    loss_ref[...] = vector[2:3, 0:1] * (1.0 / tokens)


def place_quarters(group, ups, downs, part, tokens):
    width = ups[0].shape[1]
    shapes = [
        jax.ShapeDtypeStruct((width, 4 * part), F32),
        jax.ShapeDtypeStruct((4 * part, width), F32),
        jax.ShapeDtypeStruct((1, width), F32),
        jax.ShapeDtypeStruct((1, width), F32),
        jax.ShapeDtypeStruct((1, 1), F32),
    ]
    return pl.pallas_call(
        functools.partial(place_kernel, part, tokens),
        out_shape=tuple(shapes),
        in_specs=[SMEM] + [VMEM] * 8,
        out_specs=tuple([VMEM] * len(shapes)),
        scratch_shapes=[pltpu.VMEM((4 * part, width), F32)],
        compiler_params=params(16),
        cost_estimate=COST,
        name="place",
    )(group, *ups, *downs)


def shards_square(
    image_tokens,
    tile_lists,
    opacity,
    tile_counts,
    ray_pixel,
    block_owner,
    gaussian_features,
    layer_norm_gain,
    layer_scale,
    up_weight,
    down_weight,
):
    ray_count = lax.axis_size("ray")
    group_count = lax.axis_size("grp")
    depth = ray_count // 2
    group = lax.axis_index("grp").reshape(1)
    me = lax.axis_index("ray").reshape(1)
    rows, width = image_tokens.shape
    part = down_weight.shape[0] // group_count

    def beside(array, flip):
        return lax.ppermute(array, "grp", [(g, g ^ flip) for g in range(group_count)])

    def partner(array, flip=1):
        return lax.ppermute(array, "ray", [(r, r ^ flip) for r in range(ray_count)])

    def along(array, shift):
        pairs = [(r, (r + 2 * shift) % ray_count) for r in range(ray_count)]
        return lax.ppermute(array, "ray", pairs)

    mine = own_quarter(group, up_weight, down_weight, part)
    arrivals = [along(mine, -shift) for shift in range(1, depth)]
    x_mine, y_mine = beside(mine, 1), beside(mine, 2)
    rendered, rendered_other = render(
        ray_count, True, me, block_owner, tile_lists, opacity, tile_counts.reshape(1, rows),
        ray_pixel, gaussian_features,
    )
    half = depth // 2
    low = pack(arrivals[:half - 1], rendered, x_mine, y_mine)
    x_low, y_low = beside(low, 1), beside(low, 2)
    high = pack(arrivals[half - 1:], low)
    x_high, y_high = beside(high, 1), beside(high, 2)
    d_low, d_high = beside(pack([y_mine, y_low]), 1), beside(x_high, 2)
    blocks = mix(rendered, partner(tie(rendered_other, low)), x_low, y_low, high)
    targets = [blocks[0]] + [along(blocks[shift], shift) for shift in range(1, depth)]
    tokens, normed, normed_t = prepare_tokens(
        ray_count, True, me, block_owner, ray_pixel, image_tokens,
        layer_norm_gain.reshape(1, width),
    )
    most = pack(
        [mine, low, high, x_mine, x_low, x_high, y_mine, y_low, y_high], targets[half]
    )
    most_other = partner(most)
    act_most, slope_most, mixed = forward(normed_t, [most], [most_other])
    late = [target for shift, target in enumerate(targets) if shift not in (0, half)]
    d_low, d_high = tie(d_low, mixed, *late), tie(d_high, mixed, *late)
    d_low_other, d_high_other = partner(d_low), partner(d_high)
    act_last, slope_last, back, back_t, small = forward(
        normed_t, [d_low, d_high], [d_low_other, d_high_other], mixed,
        (tokens, layer_scale.reshape(1, width), *targets),
    )
    acts = (act_most, act_last)
    slopes = (slope_most, slope_last)
    weights = ((most, d_low, d_high), (most_other, d_low_other, d_high_other))
    act_pieces = tuple(((0, quarter * depth, depth),) for quarter in range(3))
    act_pieces += (((1, 0, depth),),)
    weight_pieces = act_pieces[:3] + (((1, 0, half), (2, 0, depth - half)),)
    gain = jnp.zeros((1, width), F32)
    (down_other,) = down_gradient(1, act_pieces, depth, acts, back)
    down_arrived = partner(down_other)
    up_other, gain = up_gradient(
        1, weight_pieces, act_pieces, depth, weights[1], slopes, back_t, normed, gain
    )
    up_arrived = partner(up_other)
    down_sums = down_gradient(0, act_pieces, depth, acts, back, down_arrived)
    *up_sums, vector = up_gradient(
        0, weight_pieces, act_pieces, depth, weights[0], slopes, back_t, normed, gain,
        (up_arrived, layer_norm_gain.reshape(1, width), small),
    )
    vector = vector + partner(vector)
    vector = vector + partner(vector, 2)

    def first_step(to_x, to_y, x_later, y_later, *after):
        from_x, from_y = beside(to_x, 1), beside(to_y, 2)
        return from_x, from_y, merge(from_x, from_y, x_later, y_later, *after)

    def second_step(later):
        return beside(later[0], 1), beside(later[1], 2)

    def arrive_along(shares):
        return [shares[0]] + [along(shares[shift], shift) for shift in range(1, depth)]

    own, *rest = down_sums
    own_up, to_x, to_y, *rest_up = up_sums
    from_x, from_y, later = first_step(*rest, vector)
    late = second_step(later)
    shares = totals(own, from_x, from_y, *late)
    (down_total,) = collect(arrive_along(shares))
    down_x, down_y = beside(down_total, 1), beside(down_total, 2)
    flip = 4
    while flip < ray_count:
        vector = vector + partner(vector, flip)
        flip *= 2
    from_x, from_y, later = first_step(to_x, to_y, *rest_up)
    shares = totals(own_up, from_x, from_y, *second_step(later), vector)
    short, long = collect(arrive_along(shares), vector, down_total, (down_x, down_y))
    up_x, up_y, both = beside(short, 1), beside(short, 2), beside(long, 3)
    grad_up, grad_down, gain, scale, loss = place_quarters(
        group, (short, up_x, up_y, both), (down_total, down_x, down_y, both), part,
        rows * ray_count * group_count,
    )
    return (grad_up, grad_down, gain.reshape(width), scale.reshape(width), loss.reshape(()))


def shards(*operands):
    ray_count, group_count = lax.axis_size("ray"), lax.axis_size("grp")
    hidden = operands[-1].shape[0]
    square = group_count == 4 and ray_count in (8, 16) and hidden % (16 * group_count) == 0
    return (shards_square if square else shards_general)(*operands)


def solution(mesh):
    return jax.shard_map(
        shards,
        mesh=mesh,
        in_specs=(
            P(("grp", "ray"), None),
            P(None, ("grp", "ray")),
            P(None, ("grp", "ray")),
            P(("grp", "ray")),
            P("grp", None),
            P("grp", None),
            P(("grp", "ray"), None),
            P(),
            P(),
            P(None, "ray"),
            P("ray", None),
        ),
        out_specs=(P(None, "ray"), P("ray", None), P(), P(), P()),
        check_vma=False,
    )
```

```python
import functools

import jax
import jax.numpy as jnp
from jax import lax
from jax.experimental import pallas as pl
from jax.experimental.pallas import tpu as pltpu
from jax.sharding import PartitionSpec as P

STABILITY_EPSILON = 1e-06
F32 = jnp.float32
BF16 = jnp.bfloat16
MIB = 1024 * 1024
COST = pl.CostEstimate(flops=1 << 20, bytes_accessed=1 << 16, transcendentals=0)
LONG = pl.CostEstimate(flops=10**10, bytes_accessed=1 << 20, transcendentals=0)
SMEM = pl.BlockSpec(memory_space=pltpu.SMEM)
VMEM = pl.BlockSpec(memory_space=pltpu.VMEM)
ANY = pl.BlockSpec(memory_space=pl.ANY)


def params(mib=48, **more):
    return pltpu.CompilerParams(vmem_limit_bytes=mib * MIB, **more)


def dot_nn(a, b):
    return lax.dot_general(a, b, (((1,), (0,)), ((), ())), preferred_element_type=F32)


def dot_tn(a, b):
    return lax.dot_general(a, b, (((0,), (0,)), ((), ())), preferred_element_type=F32)


def dot_nt(a, b):
    return lax.dot_general(a, b, (((1,), (1,)), ((), ())), preferred_element_type=F32)


def owner_of(pixels, owner_ref, rows, count):
    block = lax.div(pixels, jnp.int32(rows))
    owner = jnp.zeros_like(pixels)
    for slot in range(count):
        owner = jnp.where(block == slot, owner_ref[0:1, slot:slot + 1], owner)
    return owner


def earlier(rows):
    before = lax.broadcasted_iota(jnp.int32, (rows, rows), 0)
    after = lax.broadcasted_iota(jnp.int32, (rows, rows), 1)
    return jnp.where(before < after, 1.0, 0.0).astype(BF16)


HBM = pl.BlockSpec(memory_space=pltpu.HBM)


def fetch(copies, sems):
    started = [
        pltpu.make_async_copy(source, target, sems.at[index])
        for index, (source, target) in enumerate(copies)
    ]
    for copy in started:
        copy.start()

    def wait(*numbers):
        for number in numbers:
            started[number].wait()

    return wait


def render_kernel(
    ray_count, relative, me_ref, owner_hbm, lists_hbm, opacity_hbm, counts_hbm, pixels_hbm,
    features_hbm, near_ref, other_ref, owner_ref, ids_ref, opacity_ref, counts_ref, mine_ref,
    features_ref, share_ref, table_ref, send_ref, sems,
):
    depth, rays = lists_hbm.shape
    gauss = features_hbm.shape[0]
    width = features_hbm.shape[1]
    me = me_ref[0]
    own_pixels = pixels_hbm.at[:, pl.ds(pl.multiple_of(me * rays, rays), rays)]
    wait = fetch(
        [
            (lists_hbm, ids_ref), (opacity_hbm, opacity_ref), (counts_hbm, counts_ref),
            (owner_hbm, owner_ref), (own_pixels, mine_ref), (features_hbm, features_ref),
        ],
        sems,
    )
    wait(0, 1, 2)
    ids_ref[...] = ids_ref[...] - me * gauss
    passing = jnp.ones((1, rays), F32)
    counts = counts_ref[...]
    for level in range(depth):
        alpha = opacity_ref[pl.ds(level, 1), :]
        share_ref[pl.ds(level, 1), :] = jnp.where(level < counts, alpha * passing, 0.0)
        passing = passing * (1.0 - alpha)

    tile = 256
    lanes = 128
    columns = rays // lanes

    @pl.loop(0, (gauss // tile) * columns)
    def _(step):
        first = pl.multiple_of(lax.div(step, columns) * tile, tile)
        lane = pl.multiple_of(lax.rem(step, columns) * lanes, lanes)
        number = (lax.broadcasted_iota(jnp.int32, (tile, lanes), 0) + first).astype(jnp.int16)
        total = jnp.zeros((tile, lanes), BF16)
        for level in range(depth):
            ident = jnp.broadcast_to(ids_ref[pl.ds(level, 1), pl.ds(lane, lanes)], (16, lanes))
            share = jnp.broadcast_to(share_ref[pl.ds(level, 1), pl.ds(lane, lanes)], (16, lanes))
            ident = jnp.concatenate([ident.astype(jnp.int16)] * (tile // 16), axis=0)
            share = jnp.concatenate([share.astype(BF16)] * (tile // 16), axis=0)
            total = total + jnp.where(ident == number, share, jnp.zeros_like(share))
        table_ref[pl.ds(first, tile), pl.ds(lane, lanes)] = total

    wait(3, 4, 5)
    owner = owner_of(mine_ref[...], owner_ref, rays, ray_count)
    padded = -(-ray_count // 16) * 16
    member = (lax.broadcasted_iota(jnp.int32, (padded, rays), 0) == owner)
    ranks = dot_nn(member.astype(F32).astype(BF16), earlier(rays))
    rank = jnp.sum(jnp.where(member, ranks, 0.0), axis=0, keepdims=True).astype(jnp.int32)
    if relative:
        chips = ray_count // 2
        shift = lax.div(owner, jnp.int32(2)) - lax.div(me, jnp.int32(2))
        shift = jnp.where(shift < 0, shift + chips, shift)
        flip = jnp.where(lax.rem(owner, jnp.int32(2)) == lax.rem(me, jnp.int32(2)), 0, 1)
        block = flip * chips + shift
    else:
        block = owner
    slot = block * (rays // ray_count) + rank
    send_ref[...] = (
        (lax.broadcasted_iota(jnp.int32, (rays, rays), 0) == slot).astype(F32).astype(BF16)
    )

    piece = 256
    half = rays // 2

    @pl.loop(0, width // piece)
    def _(step):
        cols = pl.ds(pl.multiple_of(step * piece, piece), piece)
        rendered = dot_tn(table_ref[...], features_ref[:, cols]).astype(BF16)
        ordered = dot_nn(send_ref[...], rendered).astype(BF16)
        near_ref[:, :, cols] = ordered[:half].reshape(*near_ref.shape[:2], piece)
        other_ref[:, :, cols] = ordered[half:].reshape(*other_ref.shape[:2], piece)


def render(ray_count, relative, me, owner, lists, opacity, counts, pixels, features):
    depth, rays = lists.shape
    gauss, width = features.shape
    shape = jax.ShapeDtypeStruct((ray_count // 2, rays // ray_count, width), BF16)
    return pl.pallas_call(
        functools.partial(render_kernel, ray_count, relative),
        out_shape=(shape, shape),
        in_specs=[SMEM] + [HBM] * 6,
        out_specs=(VMEM, VMEM),
        scratch_shapes=[
            pltpu.VMEM(owner.shape, jnp.int32),
            pltpu.VMEM((depth, rays), jnp.int32),
            pltpu.VMEM((depth, rays), F32),
            pltpu.VMEM((1, rays), jnp.int32),
            pltpu.VMEM((1, rays), jnp.int32),
            pltpu.VMEM((gauss, width), BF16),
            pltpu.VMEM((depth, rays), F32),
            pltpu.VMEM((gauss, rays), BF16),
            pltpu.VMEM((rays, rays), BF16),
            pltpu.SemaphoreType.DMA((6,)),
        ],
        compiler_params=params(20),
        cost_estimate=COST,
        name="render",
    )(me, owner, lists, opacity, counts, pixels, features)


def tokens_kernel(
    ray_count, relative, me_ref, owner_hbm, pixels_hbm, tokens_hbm, gain_hbm,
    *refs,
):
    tokens_out, normed_out, normed_t_out = refs[-11:-8]
    owner_ref, pixels_ref, tokens_ref, gain_ref, order_ref, rank_ref, place_ref, sems = refs[-8:]
    rows, width = tokens_hbm.shape
    me = me_ref[0]
    each = rows // ray_count
    wait = fetch(
        [
            (owner_hbm, owner_ref), (pixels_hbm, pixels_ref), (gain_hbm, gain_ref),
            (tokens_hbm, tokens_ref),
        ],
        sems,
    )
    wait(0, 1)
    pixels = jnp.concatenate(
        [pixels_ref[:, sender * rows:(sender + 1) * rows] for sender in range(ray_count)], axis=0
    )
    mine = owner_of(pixels, owner_ref, rows, ray_count) == me
    place_ref[...] = lax.rem(pixels, jnp.int32(rows)).astype(F32)
    member = jnp.where(mine, 1.0, 0.0)
    padded = -(-ray_count // 16) * 16
    if padded > ray_count:
        spread = jnp.concatenate([member, jnp.zeros((padded - ray_count, rows), F32)], axis=0)
    else:
        spread = member
    ranks = dot_nn(spread.astype(BF16), earlier(rows))
    rank_ref[...] = jnp.where(mine, ranks[:ray_count], -1.0)
    chips = ray_count // 2
    for index in range(ray_count):
        if relative:
            chip = lax.rem(lax.div(me, jnp.int32(2)) + (chips - index // 2), jnp.int32(chips))
            sender = 2 * chip + jnp.bitwise_xor(lax.rem(me, jnp.int32(2)), index % 2)
        else:
            sender = index
        rank = rank_ref[pl.ds(sender, 1), :].astype(jnp.int32)
        hit = lax.broadcasted_iota(jnp.int32, (each, rows), 0) == rank
        at = jnp.sum(
            jnp.where(hit, place_ref[pl.ds(sender, 1), :], 0.0), axis=1, keepdims=True
        )
        here = lax.broadcasted_iota(jnp.int32, (each, rows), 1) == at.astype(jnp.int32)
        order_ref[pl.ds(index * each, each), :] = here.astype(F32).astype(BF16)
    wait(2, 3)
    half = min(128, rows)
    gain = gain_ref[...]

    @pl.loop(0, rows // half)
    def _(step):
        span = pl.ds(pl.multiple_of(step * half, half), half)
        values = dot_nn(order_ref[span, :], tokens_ref[...])
        tokens_out[span, :] = values.astype(BF16)
        centered = values - jnp.mean(values, axis=-1, keepdims=True)
        variance = jnp.mean(centered * centered, axis=-1, keepdims=True)
        xhat = centered * lax.rsqrt(variance + STABILITY_EPSILON)
        normed = (xhat * gain).astype(BF16)
        normed_out[span, :] = normed
        normed_t_out[:, span] = normed.T


def prepare_tokens(ray_count, relative, me, owner, pixels, tokens, gain, after=()):
    rows, width = tokens.shape
    return pl.pallas_call(
        functools.partial(tokens_kernel, ray_count, relative),
        out_shape=(
            jax.ShapeDtypeStruct((rows, width), BF16),
            jax.ShapeDtypeStruct((rows, width), BF16),
            jax.ShapeDtypeStruct((width, rows), BF16),
        ),
        in_specs=[SMEM] + [HBM] * 4 + [ANY] * len(after),
        out_specs=(VMEM, VMEM, VMEM),
        scratch_shapes=[
            pltpu.VMEM(owner.shape, jnp.int32),
            pltpu.VMEM(pixels.shape, jnp.int32),
            pltpu.VMEM((rows, width), BF16),
            pltpu.VMEM((1, width), F32),
            pltpu.VMEM((rows, rows), BF16),
            pltpu.VMEM((ray_count, rows), F32),
            pltpu.VMEM((ray_count, rows), F32),
            pltpu.SemaphoreType.DMA((4,)),
        ],
        compiler_params=params(20),
        cost_estimate=COST,
        name="tokens",
    )(me, owner, pixels, tokens, gain, *after)


def up_kernel(normed_ref, up_ref, act_ref, slope_ref):
    parts, _, part_rows, width = up_ref.shape
    up = up_ref[...].reshape(parts * part_rows, width)
    rows = normed_ref.shape[0]
    piece = min(128, rows)

    @pl.loop(0, rows // piece)
    def _(step):
        span = pl.ds(pl.multiple_of(step * piece, piece), piece)
        hidden = dot_nn(normed_ref[span, :], up)
        phi = 0.5 * (1.0 + lax.erf(hidden * (0.5 ** 0.5)))
        density = jnp.exp(-0.5 * hidden * hidden) * ((2.0 * jnp.pi) ** -0.5)
        act_ref[span, :] = (hidden * phi).astype(BF16)
        slope_ref[span, :] = (phi + hidden * density).astype(slope_ref.dtype)


def project_up(normed, up):
    rows, width = normed.shape
    parts, chunks, part_rows, chunk = up.shape
    return pl.pallas_call(
        up_kernel,
        grid=(chunks,),
        out_shape=(
            jax.ShapeDtypeStruct((rows, chunks * chunk), BF16),
            jax.ShapeDtypeStruct((rows, chunks * chunk), F32),
        ),
        in_specs=[
            pl.BlockSpec((rows, width), lambda j: (0, 0)),
            pl.BlockSpec((parts, 1, part_rows, chunk), lambda j: (0, j, 0, 0)),
        ],
        out_specs=(
            pl.BlockSpec((rows, chunk), lambda j: (0, j)),
            pl.BlockSpec((rows, chunk), lambda j: (0, j)),
        ),
        compiler_params=params(dimension_semantics=("arbitrary",)),
        cost_estimate=COST,
        name="up",
    )(normed, up)


def down_kernel(
    chunks, act_ref, down_ref, tokens_ref, target_ref, scale_ref,
    grad_ref, back_ref, small_ref, mixed_ref,
):
    step = pl.program_id(0)
    rows, width = tokens_ref.shape
    act = act_ref[...]

    @pl.when(step < chunks)
    def _():
        parts, _, part_rows, _ = down_ref.shape
        part = dot_nn(act, down_ref[...].reshape(parts * part_rows, width))

        @pl.when(step == 0)
        def _():
            mixed_ref[...] = part

        @pl.when(step > 0)
        def _():
            mixed_ref[...] += part

    @pl.when(step == chunks - 1)
    def _():
        scale = scale_ref[...]
        small_ref[...] = jnp.zeros_like(small_ref)
        piece = min(64, rows)

        @pl.loop(0, rows // piece)
        def _(index):
            span = pl.ds(pl.multiple_of(index * piece, piece), piece)
            mixed = mixed_ref[span, :]
            out = tokens_ref[span, :].astype(F32) + scale * mixed
            goal = target_ref[span, :].astype(F32)
            out_norm = jnp.sqrt(jnp.sum(out * out, axis=-1, keepdims=True) + STABILITY_EPSILON)
            goal_norm = jnp.sqrt(jnp.sum(goal * goal, axis=-1, keepdims=True) + STABILITY_EPSILON)
            norms = out_norm * goal_norm
            cosine = jnp.sum(out * goal, axis=-1, keepdims=True) / norms
            upstream = (cosine / (out_norm * out_norm)) * out - goal * (1.0 / norms)
            back_ref[span, :] = (upstream * scale).astype(BF16)
            small_ref[0:1, :] += jnp.sum(upstream * mixed, axis=0, keepdims=True)
            loss = jnp.sum(1.0 - cosine, axis=0, keepdims=True)
            small_ref[1:2, :] += jnp.broadcast_to(loss, (1, width))

    @pl.when(step >= chunks)
    def _():
        grad = dot_tn(act, back_ref[...])
        grad_ref[...] = grad.astype(BF16).reshape(grad_ref.shape)


def project_down(act, down, tokens, target, scale):
    rows, width = tokens.shape
    parts, chunks, part_rows, _ = down.shape
    chunk = parts * part_rows
    return pl.pallas_call(
        functools.partial(down_kernel, chunks),
        grid=(2 * chunks,),
        out_shape=(
            jax.ShapeDtypeStruct(down.shape, BF16),
            jax.ShapeDtypeStruct((rows, width), BF16),
            jax.ShapeDtypeStruct((8, width), F32),
        ),
        in_specs=[
            pl.BlockSpec((rows, chunk), lambda j: (0, lax.rem(j, chunks))),
            pl.BlockSpec(
                (parts, 1, part_rows, width), lambda j: (0, jnp.minimum(j, chunks - 1), 0, 0)
            ),
            pl.BlockSpec((rows, width), lambda j: (0, 0)),
            pl.BlockSpec((rows, width), lambda j: (0, 0)),
            pl.BlockSpec((1, width), lambda j: (0, 0)),
        ],
        out_specs=(
            pl.BlockSpec(
                (parts, 1, part_rows, width), lambda j: (0, jnp.maximum(j - chunks, 0), 0, 0)
            ),
            pl.BlockSpec((rows, width), lambda j: (0, 0)),
            pl.BlockSpec((8, width), lambda j: (0, 0)),
        ),
        scratch_shapes=[pltpu.VMEM((rows, width), F32)],
        compiler_params=params(dimension_semantics=("arbitrary",)),
        cost_estimate=COST,
        name="down",
    )(act, down, tokens, target, scale)


def back_kernel(back_ref, down_ref, slope_ref, normed_t_ref, up_ref, gain_ref, grad_ref, sum_ref):
    step = pl.program_id(0)
    parts, _, part_rows, width = down_ref.shape
    chunk = parts * part_rows
    rows = back_ref.shape[0]
    back_act = dot_nt(back_ref[...], down_ref[...].reshape(chunk, width))
    back_hidden = (back_act * slope_ref[...]).astype(BF16)
    up_parts, _, up_rows, _ = up_ref.shape

    @pl.when(step == 0)
    def _():
        sum_ref[...] = jnp.zeros_like(sum_ref)

    grad = dot_nn(normed_t_ref[...], back_hidden)
    grad_ref[...] = grad.astype(BF16).reshape(grad_ref.shape)
    up = up_ref[...].reshape(up_parts * up_rows, chunk).astype(F32)
    sum_ref[...] += jnp.sum(grad * up, axis=1, keepdims=True) / gain_ref[...]


def back_up(back, down, slope, normed_t, up, gain):
    width, rows = normed_t.shape
    parts, chunks, part_rows, _ = down.shape
    chunk = parts * part_rows
    up_parts, _, up_rows, _ = up.shape
    return pl.pallas_call(
        back_kernel,
        grid=(chunks,),
        out_shape=(
            jax.ShapeDtypeStruct(up.shape, BF16),
            jax.ShapeDtypeStruct((width, 1), F32),
        ),
        in_specs=[
            pl.BlockSpec((rows, width), lambda j: (0, 0)),
            pl.BlockSpec((parts, 1, part_rows, width), lambda j: (0, j, 0, 0)),
            pl.BlockSpec((rows, chunk), lambda j: (0, j)),
            pl.BlockSpec((width, rows), lambda j: (0, 0)),
            pl.BlockSpec((up_parts, 1, up_rows, chunk), lambda j: (0, j, 0, 0)),
            pl.BlockSpec((width, 1), lambda j: (0, 0)),
        ],
        out_specs=(
            pl.BlockSpec((up_parts, 1, up_rows, chunk), lambda j: (0, j, 0, 0)),
            pl.BlockSpec((width, 1), lambda j: (0, 0)),
        ),
        compiler_params=params(dimension_semantics=("arbitrary",)),
        cost_estimate=COST,
        name="back",
    )(back, down, slope, normed_t, up, gain)


def gather_weight(weight, parts, group, group_count, ray_count):
    rows, cols = weight.shape
    if parts == 1:
        whole = lax.all_gather(weight, "ray", axis=0, tiled=True)
    else:
        part = lax.dynamic_slice_in_dim(weight, group * (rows // parts), rows // parts, 0)
        whole = lax.all_gather(part, ("grp", "ray"), axis=0, tiled=True)
    return whole.reshape(parts, ray_count, rows // parts, cols)


def reduce_gradient(grad):
    parts, ray_count, part_rows, cols = grad.shape
    flat = grad.reshape(parts * ray_count * part_rows, cols)
    if parts == 1:
        share = lax.psum_scatter(flat, "ray", scatter_dimension=0, tiled=True)
        return lax.psum(share.astype(F32), "grp")
    share = lax.psum_scatter(flat, "grp", scatter_dimension=0, tiled=True)
    share = lax.psum_scatter(share, "ray", scatter_dimension=0, tiled=True)
    return lax.all_gather(share, "grp", axis=0, tiled=True).astype(F32)


def shards_general(
    image_tokens,
    tile_lists,
    opacity,
    tile_counts,
    ray_pixel,
    block_owner,
    gaussian_features,
    layer_norm_gain,
    layer_scale,
    up_weight,
    down_weight,
):
    ray_count = lax.axis_size("ray")
    group_count = lax.axis_size("grp")
    group = lax.axis_index("grp")
    me = lax.axis_index("ray").reshape(1)
    rows, width = image_tokens.shape
    up_parts = group_count if up_weight.shape[0] % (16 * group_count) == 0 else 1
    down_parts = group_count if down_weight.shape[0] % (16 * group_count) == 0 else 1
    up = gather_weight(up_weight, up_parts, group, group_count, ray_count)
    down = gather_weight(down_weight, down_parts, group, group_count, ray_count)
    rendered = render(
        ray_count, False, me, block_owner, tile_lists, opacity, tile_counts.reshape(1, rows),
        ray_pixel, gaussian_features,
    )
    rendered = jnp.concatenate(rendered, axis=0).reshape(rows, width)
    target = lax.all_to_all(rendered, "ray", split_axis=0, concat_axis=0, tiled=True)
    tokens, normed, normed_t = prepare_tokens(
        ray_count, False, me, block_owner, ray_pixel, image_tokens,
        layer_norm_gain.reshape(1, width),
    )
    act, slope = project_up(normed, up)
    grad_down, back, small = project_down(act, down, tokens, target, layer_scale.reshape(1, width))
    grad_up, gain_sum = back_up(back, down, slope, normed_t, up, layer_norm_gain.reshape(width, 1))
    grad_down = reduce_gradient(grad_down)
    grad_up = reduce_gradient(grad_up)
    sums = jnp.concatenate([gain_sum.reshape(1, width), small[:2]], axis=0)
    sums = lax.psum(sums, ("grp", "ray"))
    loss = sums[2, 0] / (rows * ray_count * group_count)
    return (grad_up, grad_down, sums[0], sums[1], loss)


def quarter_kernel(group_ref, up_hbm, down_hbm, out_ref, up_ref, turned_ref, sems):
    part = out_ref.shape[1]
    lanes = up_ref.shape[1]
    start = pl.multiple_of(group_ref[0] * part, part)
    lane = pl.multiple_of(lax.div(start, jnp.int32(lanes)) * lanes, lanes)
    wait = fetch(
        [
            (up_hbm.at[:, pl.ds(lane, lanes)], up_ref),
            (down_hbm.at[pl.ds(start, part), :], out_ref.at[1]),
        ],
        sems,
    )
    wait(0)
    turned_ref[...] = up_ref[...].T
    out_ref[0] = turned_ref[pl.ds(pl.multiple_of(start - lane, part), part), :]
    wait(1)


def own_quarter(group, up, down, part):
    width, chunk = up.shape
    lanes = max(128, part)
    return pl.pallas_call(
        quarter_kernel,
        out_shape=jax.ShapeDtypeStruct((2, part, width), BF16),
        in_specs=[SMEM, HBM, HBM],
        out_specs=VMEM,
        scratch_shapes=[
            pltpu.VMEM((width, lanes), BF16),
            pltpu.VMEM((lanes, width), BF16),
            pltpu.SemaphoreType.DMA((2,)),
        ],
        compiler_params=params(16),
        cost_estimate=LONG,
        name="quarter",
    )(group, up, down)


def own_rows_kernel(group_ref, up_ref, down_ref, out_ref, turned_ref):
    part = out_ref.shape[2]
    turned_ref[...] = up_ref[...].T
    for index in range(4):
        quarter = jnp.bitwise_xor(group_ref[0], index)
        span = pl.ds(pl.multiple_of(quarter * part, part), part)
        out_ref[index, 0] = turned_ref[span, :]
        out_ref[index, 1] = down_ref[span, :]


def own_rows(group, up, down):
    width, chunk = up.shape
    return pl.pallas_call(
        own_rows_kernel,
        out_shape=jax.ShapeDtypeStruct((4, 2, chunk // 4, width), BF16),
        in_specs=[SMEM, VMEM, VMEM],
        out_specs=VMEM,
        scratch_shapes=[pltpu.VMEM((chunk, width), BF16)],
        compiler_params=params(16),
        cost_estimate=COST,
        name="own_rows",
    )(group, up, down)


def finish_rows(tokens, mixed, goal, scale):
    out = tokens + scale * mixed
    out_norm = jnp.sqrt(jnp.sum(out * out, axis=-1, keepdims=True) + STABILITY_EPSILON)
    goal_norm = jnp.sqrt(jnp.sum(goal * goal, axis=-1, keepdims=True) + STABILITY_EPSILON)
    norms = out_norm * goal_norm
    cosine = jnp.sum(out * goal, axis=-1, keepdims=True) / norms
    upstream = (cosine / (out_norm * out_norm)) * out - goal * (1.0 / norms)
    return upstream, 1.0 - cosine


def forward_kernel(first, blocks, sides, skipped, *refs):
    last = blocks > 0
    refs = list(refs[skipped:])
    normed_t_ref = refs.pop(0)
    own, other = refs[:sides], refs[sides:2 * sides]
    del refs[:2 * sides]
    mixed_in = None if first else refs.pop(0)
    if last:
        tokens_ref, scale_ref = refs[:2]
        targets = refs[2:2 + blocks]
        del refs[:2 + blocks]
    act_ref, slope_ref = refs[:2]
    del refs[:2]
    width, rows = normed_t_ref.shape
    part = act_ref.shape[2]
    part_sum = None
    downs = []
    for side, group in enumerate((own, other)):
        start = 0
        for ref in group:
            count = ref.shape[0]
            hiddens = dot_nn(ref[:, 0].reshape(count * part, width), normed_t_ref[...])
            for index in range(count):
                hidden = hiddens[index * part:(index + 1) * part]
                phi = 0.5 * (1.0 + lax.erf(hidden * (0.5 ** 0.5)))
                density = jnp.exp(-0.5 * hidden * hidden) * ((2.0 * jnp.pi) ** -0.5)
                act_ref[side, start + index] = (hidden * phi).astype(BF16)
                slope_ref[side, start + index] = phi + hidden * density
            downs.append(ref[:, 1].reshape(count * part, width))
            start += count
    if sides > 1:
        act = act_ref[...].reshape(2 * start * part, rows)
        part_sum = dot_tn(act, jnp.concatenate(downs, axis=0))
    else:
        for side, down in enumerate(downs):
            term = dot_tn(act_ref[side].reshape(start * part, rows), down)
            part_sum = term if part_sum is None else part_sum + term
    if not last:
        mixed_out = refs[0]
        mixed_out[...] = part_sum if first else mixed_in[...] + part_sum
        return
    back_ref, back_t_ref, small_ref, mixed_ref = refs
    mixed_ref[...] = mixed_in[...] + part_sum
    scale = scale_ref[...]
    small_ref[...] = jnp.zeros_like(small_ref)
    piece = rows // blocks
    for index, target_ref in enumerate(targets):
        span = pl.ds(index * piece, piece)
        mixed = mixed_ref[span, :]
        upstream, loss = finish_rows(
            tokens_ref[span, :].astype(F32), mixed,
            target_ref[...].reshape(piece, width).astype(F32), scale,
        )
        back = (upstream * scale).astype(BF16)
        back_ref[span, :] = back
        back_t_ref[:, span] = back.T
        small_ref[0:1, :] += jnp.sum(upstream * mixed, axis=0, keepdims=True)
        small_ref[1:2, :] += jnp.broadcast_to(jnp.sum(loss, axis=0, keepdims=True), (1, width))


def forward(normed_t, own, other, mixed=None, finish=None, after=()):
    width, rows = normed_t.shape
    part = own[0].shape[2]
    total = sum(array.shape[0] for array in own)
    first, last = mixed is None, finish is not None
    blocks = len(finish) - 2 if last else 0
    operands = [*after, normed_t, *own, *other]
    if not first:
        operands.append(mixed)
    if last:
        operands.extend(finish)
    piece = (2, total, part, rows)
    shapes = [jax.ShapeDtypeStruct(piece, BF16), jax.ShapeDtypeStruct(piece, F32)]
    scratch = []
    if last:
        shapes += [
            jax.ShapeDtypeStruct((rows, width), BF16),
            jax.ShapeDtypeStruct((width, rows), BF16),
            jax.ShapeDtypeStruct((8, width), F32),
        ]
        scratch = [pltpu.VMEM((rows, width), F32)]
    else:
        shapes += [jax.ShapeDtypeStruct((rows, width), F32)]
    return pl.pallas_call(
        functools.partial(forward_kernel, first, blocks, len(own), len(after)),
        out_shape=tuple(shapes),
        in_specs=[ANY] * len(after) + [VMEM] * (len(operands) - len(after)),
        out_specs=tuple([VMEM] * len(shapes)),
        scratch_shapes=scratch,
        compiler_params=params(32),
        cost_estimate=COST,
        name="forward",
    )(*operands)


def pack_kernel(counts, *refs):
    out_ref = refs[-1]
    start = 0
    for count, ref in zip(counts, refs):
        out_ref[start:start + count] = ref[...].reshape(count, *out_ref.shape[1:])
        start += count


def pack(pieces, *after):
    counts = [1 if piece.ndim == 3 else piece.shape[0] for piece in pieces]
    return pl.pallas_call(
        functools.partial(pack_kernel, counts),
        out_shape=jax.ShapeDtypeStruct((sum(counts), *pieces[0].shape[-3:]), BF16),
        in_specs=[VMEM] * len(pieces) + [ANY] * len(after),
        out_specs=VMEM,
        compiler_params=params(16),
        cost_estimate=COST,
        name="pack",
    )(*pieces, *after)


def tie_kernel(*refs):
    pass


def tie(array, *after):
    return pl.pallas_call(
        tie_kernel,
        out_shape=jax.ShapeDtypeStruct(array.shape, array.dtype),
        in_specs=[ANY] * (1 + len(after)),
        out_specs=ANY,
        input_output_aliases={0: 0},
        compiler_params=params(4),
        cost_estimate=COST,
        name="tie",
    )(array, *after)


def mix_kernel(*refs):
    near_ref, other_ref = refs[:2]
    outs = refs[-near_ref.shape[0]:]
    for index, ref in enumerate(outs):
        ref[0] = near_ref[index]
        ref[1] = other_ref[index]


def mix(near, other, *after):
    count, each, width = near.shape
    return pl.pallas_call(
        mix_kernel,
        out_shape=tuple([jax.ShapeDtypeStruct((2, each, width), BF16)] * count),
        in_specs=[VMEM, VMEM] + [ANY] * len(after),
        out_specs=tuple([VMEM] * count),
        compiler_params=params(16),
        cost_estimate=COST,
        name="mix",
    )(near, other, *after)


def joined(refs, pieces, pick):
    values = [pick(refs[which], start, count) for which, start, count in pieces]
    flat = [value.reshape(-1, value.shape[-1]) for value in values]
    return flat[0] if len(flat) == 1 else jnp.concatenate(flat, axis=0)


def put(quarter, value, outs):
    own_ref, x_ref, y_ref, x_later_ref, y_later_ref = outs
    value = value.astype(BF16).reshape(own_ref.shape)
    half = x_ref.shape[0] // 2
    if quarter == 0:
        own_ref[...] = value
    elif quarter == 1:
        x_ref[half:] = value[:half]
        x_later_ref[...] = value[half:]
    elif quarter == 2:
        y_ref[half:] = value[half:]
        y_later_ref[...] = value[:half]
    else:
        x_ref[:half] = value[:half]
        y_ref[:half] = value[half:]


def emit(quarter, value, arrived, outs):
    if arrived is None:
        outs[0][quarter] = value.astype(BF16).reshape(outs[0].shape[1:])
    else:
        put(quarter, value + arrived[quarter].reshape(value.shape).astype(F32), outs)


def down_grad_kernel(side, act_pieces, add, *refs):
    acts, back_ref = refs[:2], refs[2]
    arrived = refs[3] if add else None
    outs = refs[4:] if add else refs[3:]
    for quarter in (3, 1, 2, 0):
        act = joined(acts, act_pieces[quarter], lambda ref, a, n: ref[side, a:a + n])
        emit(quarter, dot_nn(act, back_ref[...]), arrived, outs)


def up_grad_kernel(side, weight_pieces, act_pieces, add, *refs):
    weights, slopes = refs[:2], refs[2:4]
    back_t_ref, normed_ref, gain_in = refs[4:7]
    if add:
        arrived, scale_ref, small_ref = refs[7:10]
        outs, vector_ref, gain_ref = refs[10:-2], refs[-2], refs[-1]
    else:
        arrived = None
        outs, gain_ref = refs[7:-1], refs[-1]
    gain_ref[...] = gain_in[...]
    for quarter in (3, 1, 2, 0):
        pieces = weight_pieces[quarter]
        slope = joined(slopes, act_pieces[quarter], lambda ref, a, n: ref[side, a:a + n])
        back_act = dot_nn(joined(weights, pieces, lambda ref, a, n: ref[a:a + n, 1]), back_t_ref[...])
        back_hidden = (back_act * slope).astype(BF16)
        grad = dot_nn(back_hidden, normed_ref[...])
        up = joined(weights, pieces, lambda ref, a, n: ref[a:a + n, 0]).astype(F32)
        gain_ref[...] += jnp.sum(grad * up, axis=0, keepdims=True)
        emit(quarter, grad, arrived, outs)
    if add:
        vector_ref[0:1, :] = gain_ref[...] / scale_ref[...]
        vector_ref[1:3, :] = small_ref[0:2, :]
        vector_ref[3:8, :] = jnp.zeros((5, gain_ref.shape[1]), F32)


def gradient_shapes(depth, part, width, add):
    if not add:
        return [jax.ShapeDtypeStruct((4, depth, part, width), BF16)]
    counts = (depth, depth, depth, depth - depth // 2, depth // 2)
    return [jax.ShapeDtypeStruct((count, part, width), BF16) for count in counts]


def down_gradient(side, act_pieces, depth, acts, back, arrived=None):
    part = acts[0].shape[2]
    width = back.shape[1]
    add = arrived is not None
    operands = [*acts, back] + ([arrived] if add else [])
    shapes = gradient_shapes(depth, part, width, add)
    return pl.pallas_call(
        functools.partial(down_grad_kernel, side, act_pieces, add),
        out_shape=tuple(shapes),
        in_specs=[VMEM] * len(operands),
        out_specs=tuple([VMEM] * len(shapes)),
        compiler_params=params(20),
        cost_estimate=COST,
        name="down_gradient",
    )(*operands)


def up_gradient(
    side, weight_pieces, act_pieces, depth, weights, slopes, back_t, normed, gain, extra=()
):
    part, width = weights[0].shape[2:]
    add = len(extra) > 0
    operands = [*weights, *slopes, back_t, normed, gain, *extra]
    shapes = gradient_shapes(depth, part, width, add)
    if add:
        shapes.append(jax.ShapeDtypeStruct((8, width), F32))
        scratch = [pltpu.VMEM((1, width), F32)]
    else:
        scratch = []
        shapes.append(jax.ShapeDtypeStruct((1, width), F32))
    return pl.pallas_call(
        functools.partial(up_grad_kernel, side, weight_pieces, act_pieces, add),
        out_shape=tuple(shapes),
        in_specs=[VMEM] * len(operands),
        out_specs=tuple([VMEM] * len(shapes)),
        scratch_shapes=scratch,
        compiler_params=params(24),
        cost_estimate=COST,
        name="up_gradient",
    )(*operands)


def merge_kernel(x_ref, y_ref, x_later_ref, y_later_ref, *refs):
    x_out, y_out = refs[-2:]
    half = y_later_ref.shape[0]
    x_out[...] = (x_later_ref[...].astype(F32) + y_ref[:half].astype(F32)).astype(BF16)
    y_out[...] = (y_later_ref[...].astype(F32) + x_ref[:half].astype(F32)).astype(BF16)


def merge(x, y, x_later, y_later, *after):
    return pl.pallas_call(
        merge_kernel,
        out_shape=tuple(jax.ShapeDtypeStruct(a.shape, BF16) for a in (x_later, y_later)),
        in_specs=[VMEM] * 4 + [ANY] * len(after),
        out_specs=(VMEM, VMEM),
        compiler_params=params(16),
        cost_estimate=COST,
        name="merge",
    )(x, y, x_later, y_later, *after)


def total_kernel(own_ref, x_ref, y_ref, x_late_ref, y_late_ref, *refs):
    outs = refs[-own_ref.shape[0]:]
    half = y_late_ref.shape[0]
    for index, out in enumerate(outs):
        total = own_ref[index].astype(F32)
        if index < half:
            total += x_ref[half + index].astype(F32) + y_late_ref[index].astype(F32)
        else:
            total += y_ref[index].astype(F32) + x_late_ref[index - half].astype(F32)
        out[...] = total.astype(BF16)


def totals(own, x, y, x_late, y_late, *after):
    count, part, width = own.shape
    return pl.pallas_call(
        total_kernel,
        out_shape=tuple([jax.ShapeDtypeStruct((part, width), BF16)] * count),
        in_specs=[VMEM] * 5 + [ANY] * len(after),
        out_specs=tuple([VMEM] * count),
        compiler_params=params(16),
        cost_estimate=COST,
        name="totals",
    )(own, x, y, x_late, y_late, *after)


def collect_kernel(count, *refs):
    outs = refs[count:]
    part, width = refs[0].shape
    total = refs[0][...].astype(F32)
    for ref in refs[1:count]:
        total = total + ref[...].astype(F32)
    if len(outs) == 1:
        outs[0][...] = total.astype(BF16)
        return
    vector_ref, other_ref, short_ref, long_ref, held_ref = outs[0], outs[1], *outs[-3:]
    short_ref[pl.ds(0, part), :] = total.astype(BF16)
    rest = vector_ref[0:3, :]
    held_ref[...] = jnp.zeros_like(held_ref)
    for index in range(3):
        piece = rest.astype(BF16).astype(F32)
        held_ref[3 * index:3 * index + 3, :] = piece
        rest = rest - piece
    short_ref[pl.ds(part, 16), :] = held_ref[...].astype(BF16)
    long_ref[pl.ds(0, part + 16), :] = short_ref[...]
    long_ref[pl.ds(part + 16, part), :] = other_ref[...]


def collect(parts, vector=None, other=None, after=()):
    part, width = parts[0].shape
    operands = list(parts)
    if vector is None:
        counts = (part,)
        scratch = []
    else:
        operands += [vector, other]
        counts = (part + 16, 2 * part + 16)
        scratch = [pltpu.VMEM((16, width), F32)]
    return pl.pallas_call(
        functools.partial(collect_kernel, len(parts)),
        out_shape=tuple(jax.ShapeDtypeStruct((rows, width), BF16) for rows in counts),
        in_specs=[VMEM] * len(operands) + [ANY] * len(after),
        out_specs=tuple([VMEM] * len(counts)),
        scratch_shapes=scratch,
        compiler_params=params(16),
        cost_estimate=COST,
        name="collect",
    )(*operands, *after)


def place_kernel(part, tokens, group_ref, *refs):
    ups, downs = refs[:4], refs[4:8]
    up_ref, down_ref, gain_ref, scale_ref, loss_ref, held_ref = refs[8:]
    group = group_ref[0]
    vectors = []
    for index, (up, down) in enumerate(zip(ups, downs)):
        first = pl.multiple_of(jnp.bitwise_xor(group, index) * part, part)
        held_ref[pl.ds(first, part), :] = up[pl.ds(0, part), :].astype(F32)
        start = down.shape[0] - part
        down_ref[pl.ds(first, part), :] = down[pl.ds(start, part), :].astype(F32)
        rows = up[pl.ds(part, 16), :].astype(F32)
        vectors.append((rows[0:3] + rows[3:6]) + rows[6:9])
    up_ref[...] = held_ref[...].T
    vector = (vectors[0] + vectors[1]) + (vectors[2] + vectors[3])
    gain_ref[...] = vector[0:1]
    scale_ref[...] = vector[1:2]
    loss_ref[...] = vector[2:3, 0:1] * (1.0 / tokens)


def place_quarters(group, ups, downs, part, tokens):
    width = ups[0].shape[1]
    shapes = [
        jax.ShapeDtypeStruct((width, 4 * part), F32),
        jax.ShapeDtypeStruct((4 * part, width), F32),
        jax.ShapeDtypeStruct((1, width), F32),
        jax.ShapeDtypeStruct((1, width), F32),
        jax.ShapeDtypeStruct((1, 1), F32),
    ]
    return pl.pallas_call(
        functools.partial(place_kernel, part, tokens),
        out_shape=tuple(shapes),
        in_specs=[SMEM] + [VMEM] * 8,
        out_specs=tuple([VMEM] * len(shapes)),
        scratch_shapes=[pltpu.VMEM((4 * part, width), F32)],
        compiler_params=params(16),
        cost_estimate=COST,
        name="place",
    )(group, *ups, *downs)


def shards_square(
    image_tokens,
    tile_lists,
    opacity,
    tile_counts,
    ray_pixel,
    block_owner,
    gaussian_features,
    layer_norm_gain,
    layer_scale,
    up_weight,
    down_weight,
):
    ray_count = lax.axis_size("ray")
    group_count = lax.axis_size("grp")
    depth = ray_count // 2
    group = lax.axis_index("grp").reshape(1)
    me = lax.axis_index("ray").reshape(1)
    rows, width = image_tokens.shape
    part = down_weight.shape[0] // group_count

    def beside(array, flip):
        return lax.ppermute(array, "grp", [(g, g ^ flip) for g in range(group_count)])

    def partner(array, flip=1):
        return lax.ppermute(array, "ray", [(r, r ^ flip) for r in range(ray_count)])

    def along(array, shift):
        pairs = [(r, (r + 2 * shift) % ray_count) for r in range(ray_count)]
        return lax.ppermute(array, "ray", pairs)

    mine = own_quarter(group, up_weight, down_weight, part)
    arrivals = [along(mine, -shift) for shift in range(1, depth)]
    rendered, rendered_other = render(
        ray_count, True, me, block_owner, tile_lists, opacity, tile_counts.reshape(1, rows),
        ray_pixel, gaussian_features,
    )
    half = depth // 2
    low = pack(arrivals[:half - 1], rendered)
    lows = [low] + [beside(low, flip) for flip in (1, 2, 3)]
    high = pack(arrivals[half - 1:], low)
    highs = [high] + [beside(high, flip) for flip in (1, 2, 3)]
    blocks = mix(rendered, partner(tie(rendered_other, low)), high)
    targets = [blocks[0]] + [along(blocks[shift], shift) for shift in range(1, depth)]
    early = pack([own_rows(group, up_weight, down_weight)] + lows, high)
    early_other = partner(early)
    tokens, normed, normed_t = prepare_tokens(
        ray_count, True, me, block_owner, ray_pixel, image_tokens,
        layer_norm_gain.reshape(1, width),
    )
    act_early, slope_early, mixed = forward(normed_t, [early], [early_other])
    late = pack(highs, mixed, *targets[1:-1])
    late_other = partner(late)
    act_late, slope_late, back, back_t, small = forward(
        normed_t, [late], [late_other], mixed,
        (tokens, layer_scale.reshape(1, width), *targets),
    )
    acts, slopes = (act_early, act_late), (slope_early, slope_late)
    weights = ((early, late), (early_other, late_other))
    count = half - 1
    pieces = tuple(
        ((0, q, 1), (0, 4 + q * count, count), (1, q * (depth - half), depth - half))
        for q in range(4)
    )
    gain = jnp.zeros((1, width), F32)
    (down_other,) = down_gradient(1, pieces, depth, acts, back)
    down_arrived = partner(down_other)
    up_other, gain = up_gradient(
        1, pieces, pieces, depth, weights[1], slopes, back_t, normed, gain
    )
    up_arrived = partner(up_other)
    down_sums = down_gradient(0, pieces, depth, acts, back, down_arrived)
    *up_sums, vector = up_gradient(
        0, pieces, pieces, depth, weights[0], slopes, back_t, normed, gain,
        (up_arrived, layer_norm_gain.reshape(1, width), small),
    )
    vector = vector + partner(vector)
    vector = vector + partner(vector, 2)

    def first_step(to_x, to_y, x_later, y_later, *after):
        from_x, from_y = beside(to_x, 1), beside(to_y, 2)
        return from_x, from_y, merge(from_x, from_y, x_later, y_later, *after)

    def second_step(later):
        return beside(later[0], 1), beside(later[1], 2)

    def arrive_along(shares):
        return [shares[0]] + [along(shares[shift], shift) for shift in range(1, depth)]

    own, *rest = down_sums
    own_up, to_x, to_y, *rest_up = up_sums
    from_x, from_y, later = first_step(*rest, vector)
    late = second_step(later)
    shares = totals(own, from_x, from_y, *late)
    (down_total,) = collect(arrive_along(shares))
    down_x, down_y = beside(down_total, 1), beside(down_total, 2)
    flip = 4
    while flip < ray_count:
        vector = vector + partner(vector, flip)
        flip *= 2
    from_x, from_y, later = first_step(to_x, to_y, *rest_up)
    shares = totals(own_up, from_x, from_y, *second_step(later), vector)
    short, long = collect(arrive_along(shares), vector, down_total, (down_x, down_y))
    up_x, up_y, both = beside(short, 1), beside(short, 2), beside(long, 3)
    grad_up, grad_down, gain, scale, loss = place_quarters(
        group, (short, up_x, up_y, both), (down_total, down_x, down_y, both), part,
        rows * ray_count * group_count,
    )
    return (grad_up, grad_down, gain.reshape(width), scale.reshape(width), loss.reshape(()))


def shards(*operands):
    ray_count, group_count = lax.axis_size("ray"), lax.axis_size("grp")
    hidden = operands[-1].shape[0]
    square = group_count == 4 and ray_count in (8, 16) and hidden % (16 * group_count) == 0
    return (shards_square if square else shards_general)(*operands)


def solution(mesh):
    return jax.shard_map(
        shards,
        mesh=mesh,
        in_specs=(
            P(("grp", "ray"), None),
            P(None, ("grp", "ray")),
            P(None, ("grp", "ray")),
            P(("grp", "ray")),
            P("grp", None),
            P("grp", None),
            P(("grp", "ray"), None),
            P(),
            P(),
            P(None, "ray"),
            P("ray", None),
        ),
        out_specs=(P(None, "ray"), P("ray", None), P(), P(), P()),
        check_vma=False,
    )
```

```python
import functools

import jax
import jax.numpy as jnp
from jax import lax
from jax.experimental import pallas as pl
from jax.experimental.pallas import tpu as pltpu
from jax.sharding import PartitionSpec as P

STABILITY_EPSILON = 1e-06
F32 = jnp.float32
BF16 = jnp.bfloat16
MIB = 1024 * 1024
COST = pl.CostEstimate(flops=1 << 20, bytes_accessed=1 << 16, transcendentals=0)
LONG = pl.CostEstimate(flops=10**10, bytes_accessed=1 << 20, transcendentals=0)
SMEM = pl.BlockSpec(memory_space=pltpu.SMEM)
VMEM = pl.BlockSpec(memory_space=pltpu.VMEM)
ANY = pl.BlockSpec(memory_space=pl.ANY)


def params(mib=48, **more):
    return pltpu.CompilerParams(vmem_limit_bytes=mib * MIB, **more)


def dot_nn(a, b):
    return lax.dot_general(a, b, (((1,), (0,)), ((), ())), preferred_element_type=F32)


def dot_tn(a, b):
    return lax.dot_general(a, b, (((0,), (0,)), ((), ())), preferred_element_type=F32)


def dot_nt(a, b):
    return lax.dot_general(a, b, (((1,), (1,)), ((), ())), preferred_element_type=F32)


def owner_of(pixels, owner_ref, rows, count):
    block = lax.div(pixels, jnp.int32(rows))
    owner = jnp.zeros_like(pixels)
    for slot in range(count):
        owner = jnp.where(block == slot, owner_ref[0:1, slot:slot + 1], owner)
    return owner


def earlier(rows):
    before = lax.broadcasted_iota(jnp.int32, (rows, rows), 0)
    after = lax.broadcasted_iota(jnp.int32, (rows, rows), 1)
    return jnp.where(before < after, 1.0, 0.0).astype(BF16)


HBM = pl.BlockSpec(memory_space=pltpu.HBM)


def fetch(copies, sems):
    started = [
        pltpu.make_async_copy(source, target, sems.at[index])
        for index, (source, target) in enumerate(copies)
    ]
    for copy in started:
        copy.start()

    def wait(*numbers):
        for number in numbers:
            started[number].wait()

    return wait


def render_kernel(
    ray_count, relative, me_ref, owner_hbm, lists_hbm, opacity_hbm, counts_hbm, pixels_hbm,
    features_hbm, *refs,
):
    outs = refs[:-10]
    owner_ref, ids_ref, opacity_ref, counts_ref, mine_ref, features_ref = refs[-10:-4]
    share_ref, table_ref, send_ref, sems = refs[-4:]
    depth, rays = lists_hbm.shape
    gauss = features_hbm.shape[0]
    width = features_hbm.shape[1]
    me = me_ref[0]
    own_pixels = pixels_hbm.at[:, pl.ds(pl.multiple_of(me * rays, rays), rays)]
    wait = fetch(
        [
            (lists_hbm, ids_ref), (opacity_hbm, opacity_ref), (counts_hbm, counts_ref),
            (owner_hbm, owner_ref), (own_pixels, mine_ref), (features_hbm, features_ref),
        ],
        sems,
    )
    wait(0, 1, 2)
    ids_ref[...] = ids_ref[...] - me * gauss
    passing = jnp.ones((1, rays), F32)
    counts = counts_ref[...]
    for level in range(depth):
        alpha = opacity_ref[pl.ds(level, 1), :]
        share_ref[pl.ds(level, 1), :] = jnp.where(level < counts, alpha * passing, 0.0)
        passing = passing * (1.0 - alpha)

    tile = 256
    lanes = 128
    columns = rays // lanes

    @pl.loop(0, (gauss // tile) * columns)
    def _(step):
        first = pl.multiple_of(lax.div(step, columns) * tile, tile)
        lane = pl.multiple_of(lax.rem(step, columns) * lanes, lanes)
        number = (lax.broadcasted_iota(jnp.int32, (tile, lanes), 0) + first).astype(jnp.int16)
        total = jnp.zeros((tile, lanes), BF16)
        for level in range(depth):
            ident = jnp.broadcast_to(ids_ref[pl.ds(level, 1), pl.ds(lane, lanes)], (16, lanes))
            share = jnp.broadcast_to(share_ref[pl.ds(level, 1), pl.ds(lane, lanes)], (16, lanes))
            ident = jnp.concatenate([ident.astype(jnp.int16)] * (tile // 16), axis=0)
            share = jnp.concatenate([share.astype(BF16)] * (tile // 16), axis=0)
            total = total + jnp.where(ident == number, share, jnp.zeros_like(share))
        table_ref[pl.ds(first, tile), pl.ds(lane, lanes)] = total

    wait(3, 4, 5)
    owner = owner_of(mine_ref[...], owner_ref, rays, ray_count)
    padded = -(-ray_count // 16) * 16
    member = (lax.broadcasted_iota(jnp.int32, (padded, rays), 0) == owner)
    ranks = dot_nn(member.astype(F32).astype(BF16), earlier(rays))
    rank = jnp.sum(jnp.where(member, ranks, 0.0), axis=0, keepdims=True).astype(jnp.int32)
    if relative:
        chips = ray_count // 2
        shift = lax.div(owner, jnp.int32(2)) - lax.div(me, jnp.int32(2))
        shift = jnp.where(shift < 0, shift + chips, shift)
        flip = jnp.where(lax.rem(owner, jnp.int32(2)) == lax.rem(me, jnp.int32(2)), 0, 1)
        block = 2 * shift + flip
    else:
        block = owner
    slot = block * (rays // ray_count) + rank
    send_ref[...] = (
        (lax.broadcasted_iota(jnp.int32, (rays, rays), 0) == slot).astype(F32).astype(BF16)
    )

    piece = 256
    span = rays // len(outs)

    @pl.loop(0, width // piece)
    def _(step):
        cols = pl.ds(pl.multiple_of(step * piece, piece), piece)
        rendered = dot_tn(table_ref[...], features_ref[:, cols]).astype(BF16)
        ordered = dot_nn(send_ref[...], rendered).astype(BF16)
        for index, out in enumerate(outs):
            rows = ordered[index * span:(index + 1) * span]
            out[:, :, cols] = rows.reshape(*out.shape[:2], piece)


def render(ray_count, relative, me, owner, lists, opacity, counts, pixels, features):
    depth, rays = lists.shape
    gauss, width = features.shape
    parts = ray_count // 2 if relative else 1
    shape = jax.ShapeDtypeStruct((ray_count // parts, rays // ray_count, width), BF16)
    return pl.pallas_call(
        functools.partial(render_kernel, ray_count, relative),
        out_shape=(shape,) * parts,
        in_specs=[SMEM] + [HBM] * 6,
        out_specs=(VMEM,) * parts,
        scratch_shapes=[
            pltpu.VMEM(owner.shape, jnp.int32),
            pltpu.VMEM((depth, rays), jnp.int32),
            pltpu.VMEM((depth, rays), F32),
            pltpu.VMEM((1, rays), jnp.int32),
            pltpu.VMEM((1, rays), jnp.int32),
            pltpu.VMEM((gauss, width), BF16),
            pltpu.VMEM((depth, rays), F32),
            pltpu.VMEM((gauss, rays), BF16),
            pltpu.VMEM((rays, rays), BF16),
            pltpu.SemaphoreType.DMA((6,)),
        ],
        compiler_params=params(20),
        cost_estimate=COST,
        name="render",
    )(me, owner, lists, opacity, counts, pixels, features)


def tokens_kernel(
    ray_count, relative, me_ref, owner_hbm, pixels_hbm, tokens_hbm, gain_hbm,
    *refs,
):
    tokens_out, normed_out, normed_t_out = refs[-11:-8]
    owner_ref, pixels_ref, tokens_ref, gain_ref, order_ref, rank_ref, place_ref, sems = refs[-8:]
    rows, width = tokens_hbm.shape
    me = me_ref[0]
    each = rows // ray_count
    wait = fetch(
        [
            (owner_hbm, owner_ref), (pixels_hbm, pixels_ref), (gain_hbm, gain_ref),
            (tokens_hbm, tokens_ref),
        ],
        sems,
    )
    wait(0, 1)
    pixels = jnp.concatenate(
        [pixels_ref[:, sender * rows:(sender + 1) * rows] for sender in range(ray_count)], axis=0
    )
    mine = owner_of(pixels, owner_ref, rows, ray_count) == me
    place_ref[...] = lax.rem(pixels, jnp.int32(rows)).astype(F32)
    member = jnp.where(mine, 1.0, 0.0)
    padded = -(-ray_count // 16) * 16
    if padded > ray_count:
        spread = jnp.concatenate([member, jnp.zeros((padded - ray_count, rows), F32)], axis=0)
    else:
        spread = member
    ranks = dot_nn(spread.astype(BF16), earlier(rows))
    rank_ref[...] = jnp.where(mine, ranks[:ray_count], -1.0)
    chips = ray_count // 2
    for index in range(ray_count):
        if relative:
            chip = lax.rem(lax.div(me, jnp.int32(2)) + (chips - index // 2), jnp.int32(chips))
            sender = 2 * chip + jnp.bitwise_xor(lax.rem(me, jnp.int32(2)), index % 2)
        else:
            sender = index
        rank = rank_ref[pl.ds(sender, 1), :].astype(jnp.int32)
        hit = lax.broadcasted_iota(jnp.int32, (each, rows), 0) == rank
        at = jnp.sum(
            jnp.where(hit, place_ref[pl.ds(sender, 1), :], 0.0), axis=1, keepdims=True
        )
        here = lax.broadcasted_iota(jnp.int32, (each, rows), 1) == at.astype(jnp.int32)
        order_ref[pl.ds(index * each, each), :] = here.astype(F32).astype(BF16)
    wait(2, 3)
    half = min(128, rows)
    gain = gain_ref[...]

    @pl.loop(0, rows // half)
    def _(step):
        span = pl.ds(pl.multiple_of(step * half, half), half)
        values = dot_nn(order_ref[span, :], tokens_ref[...])
        tokens_out[span, :] = values.astype(BF16)
        centered = values - jnp.mean(values, axis=-1, keepdims=True)
        variance = jnp.mean(centered * centered, axis=-1, keepdims=True)
        xhat = centered * lax.rsqrt(variance + STABILITY_EPSILON)
        normed = (xhat * gain).astype(BF16)
        normed_out[span, :] = normed
        normed_t_out[:, span] = normed.T


def prepare_tokens(ray_count, relative, me, owner, pixels, tokens, gain, after=()):
    rows, width = tokens.shape
    return pl.pallas_call(
        functools.partial(tokens_kernel, ray_count, relative),
        out_shape=(
            jax.ShapeDtypeStruct((rows, width), BF16),
            jax.ShapeDtypeStruct((rows, width), BF16),
            jax.ShapeDtypeStruct((width, rows), BF16),
        ),
        in_specs=[SMEM] + [HBM] * 4 + [ANY] * len(after),
        out_specs=(VMEM, VMEM, VMEM),
        scratch_shapes=[
            pltpu.VMEM(owner.shape, jnp.int32),
            pltpu.VMEM(pixels.shape, jnp.int32),
            pltpu.VMEM((rows, width), BF16),
            pltpu.VMEM((1, width), F32),
            pltpu.VMEM((rows, rows), BF16),
            pltpu.VMEM((ray_count, rows), F32),
            pltpu.VMEM((ray_count, rows), F32),
            pltpu.SemaphoreType.DMA((4,)),
        ],
        compiler_params=params(20),
        cost_estimate=COST,
        name="tokens",
    )(me, owner, pixels, tokens, gain, *after)


def up_kernel(normed_ref, up_ref, act_ref, slope_ref):
    parts, _, part_rows, width = up_ref.shape
    up = up_ref[...].reshape(parts * part_rows, width)
    rows = normed_ref.shape[0]
    piece = min(128, rows)

    @pl.loop(0, rows // piece)
    def _(step):
        span = pl.ds(pl.multiple_of(step * piece, piece), piece)
        hidden = dot_nn(normed_ref[span, :], up)
        phi = 0.5 * (1.0 + lax.erf(hidden * (0.5 ** 0.5)))
        density = jnp.exp(-0.5 * hidden * hidden) * ((2.0 * jnp.pi) ** -0.5)
        act_ref[span, :] = (hidden * phi).astype(BF16)
        slope_ref[span, :] = (phi + hidden * density).astype(slope_ref.dtype)


def project_up(normed, up):
    rows, width = normed.shape
    parts, chunks, part_rows, chunk = up.shape
    return pl.pallas_call(
        up_kernel,
        grid=(chunks,),
        out_shape=(
            jax.ShapeDtypeStruct((rows, chunks * chunk), BF16),
            jax.ShapeDtypeStruct((rows, chunks * chunk), F32),
        ),
        in_specs=[
            pl.BlockSpec((rows, width), lambda j: (0, 0)),
            pl.BlockSpec((parts, 1, part_rows, chunk), lambda j: (0, j, 0, 0)),
        ],
        out_specs=(
            pl.BlockSpec((rows, chunk), lambda j: (0, j)),
            pl.BlockSpec((rows, chunk), lambda j: (0, j)),
        ),
        compiler_params=params(dimension_semantics=("arbitrary",)),
        cost_estimate=COST,
        name="up",
    )(normed, up)


def down_kernel(
    chunks, act_ref, down_ref, tokens_ref, target_ref, scale_ref,
    grad_ref, back_ref, small_ref, mixed_ref,
):
    step = pl.program_id(0)
    rows, width = tokens_ref.shape
    act = act_ref[...]

    @pl.when(step < chunks)
    def _():
        parts, _, part_rows, _ = down_ref.shape
        part = dot_nn(act, down_ref[...].reshape(parts * part_rows, width))

        @pl.when(step == 0)
        def _():
            mixed_ref[...] = part

        @pl.when(step > 0)
        def _():
            mixed_ref[...] += part

    @pl.when(step == chunks - 1)
    def _():
        scale = scale_ref[...]
        small_ref[...] = jnp.zeros_like(small_ref)
        piece = min(64, rows)

        @pl.loop(0, rows // piece)
        def _(index):
            span = pl.ds(pl.multiple_of(index * piece, piece), piece)
            mixed = mixed_ref[span, :]
            out = tokens_ref[span, :].astype(F32) + scale * mixed
            goal = target_ref[span, :].astype(F32)
            out_norm = jnp.sqrt(jnp.sum(out * out, axis=-1, keepdims=True) + STABILITY_EPSILON)
            goal_norm = jnp.sqrt(jnp.sum(goal * goal, axis=-1, keepdims=True) + STABILITY_EPSILON)
            norms = out_norm * goal_norm
            cosine = jnp.sum(out * goal, axis=-1, keepdims=True) / norms
            upstream = (cosine / (out_norm * out_norm)) * out - goal * (1.0 / norms)
            back_ref[span, :] = (upstream * scale).astype(BF16)
            small_ref[0:1, :] += jnp.sum(upstream * mixed, axis=0, keepdims=True)
            loss = jnp.sum(1.0 - cosine, axis=0, keepdims=True)
            small_ref[1:2, :] += jnp.broadcast_to(loss, (1, width))

    @pl.when(step >= chunks)
    def _():
        grad = dot_tn(act, back_ref[...])
        grad_ref[...] = grad.astype(BF16).reshape(grad_ref.shape)


def project_down(act, down, tokens, target, scale):
    rows, width = tokens.shape
    parts, chunks, part_rows, _ = down.shape
    chunk = parts * part_rows
    return pl.pallas_call(
        functools.partial(down_kernel, chunks),
        grid=(2 * chunks,),
        out_shape=(
            jax.ShapeDtypeStruct(down.shape, BF16),
            jax.ShapeDtypeStruct((rows, width), BF16),
            jax.ShapeDtypeStruct((8, width), F32),
        ),
        in_specs=[
            pl.BlockSpec((rows, chunk), lambda j: (0, lax.rem(j, chunks))),
            pl.BlockSpec(
                (parts, 1, part_rows, width), lambda j: (0, jnp.minimum(j, chunks - 1), 0, 0)
            ),
            pl.BlockSpec((rows, width), lambda j: (0, 0)),
            pl.BlockSpec((rows, width), lambda j: (0, 0)),
            pl.BlockSpec((1, width), lambda j: (0, 0)),
        ],
        out_specs=(
            pl.BlockSpec(
                (parts, 1, part_rows, width), lambda j: (0, jnp.maximum(j - chunks, 0), 0, 0)
            ),
            pl.BlockSpec((rows, width), lambda j: (0, 0)),
            pl.BlockSpec((8, width), lambda j: (0, 0)),
        ),
        scratch_shapes=[pltpu.VMEM((rows, width), F32)],
        compiler_params=params(dimension_semantics=("arbitrary",)),
        cost_estimate=COST,
        name="down",
    )(act, down, tokens, target, scale)


def back_kernel(back_ref, down_ref, slope_ref, normed_t_ref, up_ref, gain_ref, grad_ref, sum_ref):
    step = pl.program_id(0)
    parts, _, part_rows, width = down_ref.shape
    chunk = parts * part_rows
    rows = back_ref.shape[0]
    back_act = dot_nt(back_ref[...], down_ref[...].reshape(chunk, width))
    back_hidden = (back_act * slope_ref[...]).astype(BF16)
    up_parts, _, up_rows, _ = up_ref.shape

    @pl.when(step == 0)
    def _():
        sum_ref[...] = jnp.zeros_like(sum_ref)

    grad = dot_nn(normed_t_ref[...], back_hidden)
    grad_ref[...] = grad.astype(BF16).reshape(grad_ref.shape)
    up = up_ref[...].reshape(up_parts * up_rows, chunk).astype(F32)
    sum_ref[...] += jnp.sum(grad * up, axis=1, keepdims=True) / gain_ref[...]


def back_up(back, down, slope, normed_t, up, gain):
    width, rows = normed_t.shape
    parts, chunks, part_rows, _ = down.shape
    chunk = parts * part_rows
    up_parts, _, up_rows, _ = up.shape
    return pl.pallas_call(
        back_kernel,
        grid=(chunks,),
        out_shape=(
            jax.ShapeDtypeStruct(up.shape, BF16),
            jax.ShapeDtypeStruct((width, 1), F32),
        ),
        in_specs=[
            pl.BlockSpec((rows, width), lambda j: (0, 0)),
            pl.BlockSpec((parts, 1, part_rows, width), lambda j: (0, j, 0, 0)),
            pl.BlockSpec((rows, chunk), lambda j: (0, j)),
            pl.BlockSpec((width, rows), lambda j: (0, 0)),
            pl.BlockSpec((up_parts, 1, up_rows, chunk), lambda j: (0, j, 0, 0)),
            pl.BlockSpec((width, 1), lambda j: (0, 0)),
        ],
        out_specs=(
            pl.BlockSpec((up_parts, 1, up_rows, chunk), lambda j: (0, j, 0, 0)),
            pl.BlockSpec((width, 1), lambda j: (0, 0)),
        ),
        compiler_params=params(dimension_semantics=("arbitrary",)),
        cost_estimate=COST,
        name="back",
    )(back, down, slope, normed_t, up, gain)


def gather_weight(weight, parts, group, group_count, ray_count):
    rows, cols = weight.shape
    if parts == 1:
        whole = lax.all_gather(weight, "ray", axis=0, tiled=True)
    else:
        part = lax.dynamic_slice_in_dim(weight, group * (rows // parts), rows // parts, 0)
        whole = lax.all_gather(part, ("grp", "ray"), axis=0, tiled=True)
    return whole.reshape(parts, ray_count, rows // parts, cols)


def reduce_gradient(grad):
    parts, ray_count, part_rows, cols = grad.shape
    flat = grad.reshape(parts * ray_count * part_rows, cols)
    if parts == 1:
        share = lax.psum_scatter(flat, "ray", scatter_dimension=0, tiled=True)
        return lax.psum(share.astype(F32), "grp")
    share = lax.psum_scatter(flat, "grp", scatter_dimension=0, tiled=True)
    share = lax.psum_scatter(share, "ray", scatter_dimension=0, tiled=True)
    return lax.all_gather(share, "grp", axis=0, tiled=True).astype(F32)


def shards_general(
    image_tokens,
    tile_lists,
    opacity,
    tile_counts,
    ray_pixel,
    block_owner,
    gaussian_features,
    layer_norm_gain,
    layer_scale,
    up_weight,
    down_weight,
):
    ray_count = lax.axis_size("ray")
    group_count = lax.axis_size("grp")
    group = lax.axis_index("grp")
    me = lax.axis_index("ray").reshape(1)
    rows, width = image_tokens.shape
    up_parts = group_count if up_weight.shape[0] % (16 * group_count) == 0 else 1
    down_parts = group_count if down_weight.shape[0] % (16 * group_count) == 0 else 1
    up = gather_weight(up_weight, up_parts, group, group_count, ray_count)
    down = gather_weight(down_weight, down_parts, group, group_count, ray_count)
    rendered = render(
        ray_count, False, me, block_owner, tile_lists, opacity, tile_counts.reshape(1, rows),
        ray_pixel, gaussian_features,
    )
    rendered = rendered[0].reshape(rows, width)
    target = lax.all_to_all(rendered, "ray", split_axis=0, concat_axis=0, tiled=True)
    tokens, normed, normed_t = prepare_tokens(
        ray_count, False, me, block_owner, ray_pixel, image_tokens,
        layer_norm_gain.reshape(1, width),
    )
    act, slope = project_up(normed, up)
    grad_down, back, small = project_down(act, down, tokens, target, layer_scale.reshape(1, width))
    grad_up, gain_sum = back_up(back, down, slope, normed_t, up, layer_norm_gain.reshape(width, 1))
    grad_down = reduce_gradient(grad_down)
    grad_up = reduce_gradient(grad_up)
    sums = jnp.concatenate([gain_sum.reshape(1, width), small[:2]], axis=0)
    sums = lax.psum(sums, ("grp", "ray"))
    loss = sums[2, 0] / (rows * ray_count * group_count)
    return (grad_up, grad_down, sums[0], sums[1], loss)


def quarter_kernel(group_ref, up_hbm, down_hbm, out_ref, up_ref, turned_ref, sems):
    part = out_ref.shape[1]
    lanes = up_ref.shape[1]
    start = pl.multiple_of(group_ref[0] * part, part)
    lane = pl.multiple_of(lax.div(start, jnp.int32(lanes)) * lanes, lanes)
    wait = fetch(
        [
            (up_hbm.at[:, pl.ds(lane, lanes)], up_ref),
            (down_hbm.at[pl.ds(start, part), :], out_ref.at[1]),
        ],
        sems,
    )
    wait(0)
    turned_ref[...] = up_ref[...].T
    out_ref[0] = turned_ref[pl.ds(pl.multiple_of(start - lane, part), part), :]
    wait(1)


def own_quarter(group, up, down, part):
    width, chunk = up.shape
    lanes = max(128, part)
    return pl.pallas_call(
        quarter_kernel,
        out_shape=jax.ShapeDtypeStruct((2, part, width), BF16),
        in_specs=[SMEM, HBM, HBM],
        out_specs=VMEM,
        scratch_shapes=[
            pltpu.VMEM((width, lanes), BF16),
            pltpu.VMEM((lanes, width), BF16),
            pltpu.SemaphoreType.DMA((2,)),
        ],
        compiler_params=params(16),
        cost_estimate=LONG,
        name="quarter",
    )(group, up, down)


def own_rows_kernel(group_ref, up_ref, down_ref, out_ref, turned_ref):
    part = out_ref.shape[2]
    turned_ref[...] = up_ref[...].T
    for index in range(4):
        quarter = jnp.bitwise_xor(group_ref[0], index)
        span = pl.ds(pl.multiple_of(quarter * part, part), part)
        out_ref[index, 0] = turned_ref[span, :]
        out_ref[index, 1] = down_ref[span, :]


def own_rows(group, up, down):
    width, chunk = up.shape
    return pl.pallas_call(
        own_rows_kernel,
        out_shape=jax.ShapeDtypeStruct((4, 2, chunk // 4, width), BF16),
        in_specs=[SMEM, VMEM, VMEM],
        out_specs=VMEM,
        scratch_shapes=[pltpu.VMEM((chunk, width), BF16)],
        compiler_params=params(16),
        cost_estimate=COST,
        name="own_rows",
    )(group, up, down)


def finish_rows(tokens, mixed, goal, scale):
    out = tokens + scale * mixed
    out_norm = jnp.sqrt(jnp.sum(out * out, axis=-1, keepdims=True) + STABILITY_EPSILON)
    goal_norm = jnp.sqrt(jnp.sum(goal * goal, axis=-1, keepdims=True) + STABILITY_EPSILON)
    norms = out_norm * goal_norm
    cosine = jnp.sum(out * goal, axis=-1, keepdims=True) / norms
    upstream = (cosine / (out_norm * out_norm)) * out - goal * (1.0 / norms)
    return upstream, 1.0 - cosine


def forward_kernel(first, blocks, sides, skipped, *refs):
    last = blocks > 0
    refs = list(refs[skipped:])
    normed_t_ref = refs.pop(0)
    own, other = refs[:sides], refs[sides:2 * sides]
    del refs[:2 * sides]
    mixed_in = None if first else refs.pop(0)
    if last:
        tokens_ref, scale_ref = refs[:2]
        targets, passed_ref = refs[2:2 + blocks], refs[2 + blocks]
        del refs[:3 + blocks]
    act_ref, slope_ref = refs[:2]
    del refs[:2]
    width, rows = normed_t_ref.shape
    part = act_ref.shape[2]
    part_sum = None
    downs = []
    for side, group in enumerate((own, other)):
        start = 0
        for ref in group:
            count = ref.shape[0]
            hiddens = dot_nn(ref[:, 0].reshape(count * part, width), normed_t_ref[...])
            for index in range(count):
                hidden = hiddens[index * part:(index + 1) * part]
                phi = 0.5 * (1.0 + lax.erf(hidden * (0.5 ** 0.5)))
                density = jnp.exp(-0.5 * hidden * hidden) * ((2.0 * jnp.pi) ** -0.5)
                act_ref[side, start + index] = (hidden * phi).astype(BF16)
                slope_ref[side, start + index] = phi + hidden * density
            downs.append(ref[:, 1].reshape(count * part, width))
            start += count
    if sides > 1 or last:
        act = act_ref[...].reshape(2 * start * part, rows)
        part_sum = dot_tn(act, jnp.concatenate(downs, axis=0))
    else:
        for side, down in enumerate(downs):
            term = dot_tn(act_ref[side].reshape(start * part, rows), down)
            part_sum = term if part_sum is None else part_sum + term
    if not last:
        mixed_out = refs[0]
        mixed_out[...] = part_sum if first else mixed_in[...] + part_sum
        return
    back_ref, back_t_ref, small_ref, mixed_ref = refs
    mixed_ref[...] = mixed_in[...] + part_sum
    scale = scale_ref[...]
    small_ref[...] = jnp.zeros_like(small_ref)
    piece = rows // blocks
    for index, target_ref in enumerate(targets):
        span = pl.ds(index * piece, piece)
        mixed = mixed_ref[span, :]
        goal = jnp.concatenate([target_ref[0], passed_ref[index]], axis=0).astype(F32)
        upstream, loss = finish_rows(tokens_ref[span, :].astype(F32), mixed, goal, scale)
        back = (upstream * scale).astype(BF16)
        back_ref[span, :] = back
        back_t_ref[:, span] = back.T
        small_ref[0:1, :] += jnp.sum(upstream * mixed, axis=0, keepdims=True)
        small_ref[1:2, :] += jnp.broadcast_to(jnp.sum(loss, axis=0, keepdims=True), (1, width))


def forward(normed_t, own, other, mixed=None, finish=None, after=()):
    width, rows = normed_t.shape
    part = own[0].shape[2]
    total = sum(array.shape[0] for array in own)
    first, last = mixed is None, finish is not None
    blocks = len(finish) - 3 if last else 0
    operands = [*after, normed_t, *own, *other]
    if not first:
        operands.append(mixed)
    if last:
        operands.extend(finish)
    piece = (2, total, part, rows)
    shapes = [jax.ShapeDtypeStruct(piece, BF16), jax.ShapeDtypeStruct(piece, F32)]
    scratch = []
    if last:
        shapes += [
            jax.ShapeDtypeStruct((rows, width), BF16),
            jax.ShapeDtypeStruct((width, rows), BF16),
            jax.ShapeDtypeStruct((8, width), F32),
        ]
        scratch = [pltpu.VMEM((rows, width), F32)]
    else:
        shapes += [jax.ShapeDtypeStruct((rows, width), F32)]
    return pl.pallas_call(
        functools.partial(forward_kernel, first, blocks, len(own), len(after)),
        out_shape=tuple(shapes),
        in_specs=[ANY] * len(after) + [VMEM] * (len(operands) - len(after)),
        out_specs=tuple([VMEM] * len(shapes)),
        scratch_shapes=scratch,
        compiler_params=params(32),
        cost_estimate=COST,
        name="forward",
    )(*operands)


def pack_kernel(counts, *refs):
    out_ref = refs[-1]
    start = 0
    for count, ref in zip(counts, refs):
        out_ref[start:start + count] = ref[...].reshape(count, *out_ref.shape[1:])
        start += count


def pack(pieces, *after):
    counts = [1 if piece.ndim == 3 else piece.shape[0] for piece in pieces]
    return pl.pallas_call(
        functools.partial(pack_kernel, counts),
        out_shape=jax.ShapeDtypeStruct((sum(counts), *pieces[0].shape[-3:]), BF16),
        in_specs=[VMEM] * len(pieces) + [ANY] * len(after),
        out_specs=VMEM,
        compiler_params=params(16),
        cost_estimate=COST,
        name="pack",
    )(*pieces, *after)


def turn_kernel(y_ref, x_ref, a_ref, b_ref):
    count = a_ref.shape[0]
    a_ref[...] = y_ref[:count]
    b_ref[...] = x_ref[count:]


def turn(y, x):
    count = y.shape[0]
    first = count // 2
    return pl.pallas_call(
        turn_kernel,
        out_shape=(
            jax.ShapeDtypeStruct((first, *y.shape[1:]), BF16),
            jax.ShapeDtypeStruct((count - first, *y.shape[1:]), BF16),
        ),
        in_specs=[VMEM] * 2,
        out_specs=(VMEM, VMEM),
        compiler_params=params(16),
        cost_estimate=COST,
        name="turn",
    )(y, x)


def tie_kernel(*refs):
    pass


def tie(array, *after):
    return pl.pallas_call(
        tie_kernel,
        out_shape=jax.ShapeDtypeStruct(array.shape, array.dtype),
        in_specs=[ANY] * (1 + len(after)),
        out_specs=ANY,
        input_output_aliases={0: 0},
        compiler_params=params(4),
        cost_estimate=COST,
        name="tie",
    )(array, *after)


def seconds_kernel(*refs):
    for index, ref in enumerate(refs[:-1]):
        refs[-1][index] = ref[1]


def seconds(blocks):
    count, (_, each, width) = len(blocks), blocks[0].shape
    return pl.pallas_call(
        seconds_kernel,
        out_shape=jax.ShapeDtypeStruct((count, each, width), BF16),
        in_specs=[VMEM] * count,
        out_specs=VMEM,
        compiler_params=params(16),
        cost_estimate=COST,
        name="seconds",
    )(*blocks)


def joined(refs, pieces, pick):
    values = [pick(refs[which], start, count) for which, start, count in pieces]
    flat = [value.reshape(-1, value.shape[-1]) for value in values]
    return flat[0] if len(flat) == 1 else jnp.concatenate(flat, axis=0)


def put(quarter, value, outs):
    own_ref, x_ref, y_ref, x_later_ref, y_later_ref = outs
    value = value.astype(BF16).reshape(own_ref.shape)
    half = x_ref.shape[0] // 2
    if quarter == 0:
        own_ref[...] = value
    elif quarter == 1:
        x_ref[half:] = value[:half]
        x_later_ref[...] = value[half:]
    elif quarter == 2:
        y_ref[half:] = value[half:]
        y_later_ref[...] = value[:half]
    else:
        x_ref[:half] = value[:half]
        y_ref[:half] = value[half:]


def emit(quarter, value, arrived, outs):
    if arrived is None:
        outs[0][quarter] = value.astype(BF16).reshape(outs[0].shape[1:])
    else:
        put(quarter, value + arrived[quarter].reshape(value.shape).astype(F32), outs)


def down_grad_kernel(side, act_pieces, add, *refs):
    acts, back_ref = refs[:3], refs[3]
    arrived = refs[4] if add else None
    outs = refs[5:] if add else refs[4:]
    for quarter in (3, 1, 2, 0):
        act = joined(acts, act_pieces[quarter], lambda ref, a, n: ref[side, a:a + n])
        emit(quarter, dot_nn(act, back_ref[...]), arrived, outs)


def up_grad_kernel(side, weight_pieces, act_pieces, add, *refs):
    weights, slopes = refs[:3], refs[3:6]
    back_t_ref, normed_ref, gain_in = refs[6:9]
    if add:
        arrived, scale_ref, small_ref = refs[9:12]
        outs, vector_ref, gain_ref = refs[12:-2], refs[-2], refs[-1]
    else:
        arrived = None
        outs, gain_ref = refs[9:-1], refs[-1]
    gain_ref[...] = gain_in[...]
    for quarter in (3, 1, 2, 0):
        pieces = weight_pieces[quarter]
        slope = joined(slopes, act_pieces[quarter], lambda ref, a, n: ref[side, a:a + n])
        back_act = dot_nn(joined(weights, pieces, lambda ref, a, n: ref[a:a + n, 1]), back_t_ref[...])
        back_hidden = (back_act * slope).astype(BF16)
        grad = dot_nn(back_hidden, normed_ref[...])
        up = joined(weights, pieces, lambda ref, a, n: ref[a:a + n, 0]).astype(F32)
        gain_ref[...] += jnp.sum(grad * up, axis=0, keepdims=True)
        emit(quarter, grad, arrived, outs)
    if add:
        vector_ref[0:1, :] = gain_ref[...] / scale_ref[...]
        vector_ref[1:3, :] = small_ref[0:2, :]
        vector_ref[3:8, :] = jnp.zeros((5, gain_ref.shape[1]), F32)


def gradient_shapes(depth, part, width, add):
    if not add:
        return [jax.ShapeDtypeStruct((4, depth, part, width), BF16)]
    counts = (depth, depth, depth, depth - depth // 2, depth // 2)
    return [jax.ShapeDtypeStruct((count, part, width), BF16) for count in counts]


def down_gradient(side, act_pieces, depth, acts, back, arrived=None):
    part = acts[0].shape[2]
    width = back.shape[1]
    add = arrived is not None
    operands = [*acts, back] + ([arrived] if add else [])
    shapes = gradient_shapes(depth, part, width, add)
    return pl.pallas_call(
        functools.partial(down_grad_kernel, side, act_pieces, add),
        out_shape=tuple(shapes),
        in_specs=[VMEM] * len(operands),
        out_specs=tuple([VMEM] * len(shapes)),
        compiler_params=params(20),
        cost_estimate=COST,
        name="down_gradient",
    )(*operands)


def up_gradient(
    side, weight_pieces, act_pieces, depth, weights, slopes, back_t, normed, gain, extra=()
):
    part, width = weights[0].shape[2:]
    add = len(extra) > 0
    operands = [*weights, *slopes, back_t, normed, gain, *extra]
    shapes = gradient_shapes(depth, part, width, add)
    if add:
        shapes.append(jax.ShapeDtypeStruct((8, width), F32))
        scratch = [pltpu.VMEM((1, width), F32)]
    else:
        scratch = []
        shapes.append(jax.ShapeDtypeStruct((1, width), F32))
    return pl.pallas_call(
        functools.partial(up_grad_kernel, side, weight_pieces, act_pieces, add),
        out_shape=tuple(shapes),
        in_specs=[VMEM] * len(operands),
        out_specs=tuple([VMEM] * len(shapes)),
        scratch_shapes=scratch,
        compiler_params=params(24),
        cost_estimate=COST,
        name="up_gradient",
    )(*operands)


def merge_kernel(x_ref, y_ref, x_later_ref, y_later_ref, *refs):
    x_out, y_out = refs[-2:]
    half = y_later_ref.shape[0]
    x_out[...] = (x_later_ref[...].astype(F32) + y_ref[:half].astype(F32)).astype(BF16)
    y_out[...] = (y_later_ref[...].astype(F32) + x_ref[:half].astype(F32)).astype(BF16)


def merge(x, y, x_later, y_later, *after):
    return pl.pallas_call(
        merge_kernel,
        out_shape=tuple(jax.ShapeDtypeStruct(a.shape, BF16) for a in (x_later, y_later)),
        in_specs=[VMEM] * 4 + [ANY] * len(after),
        out_specs=(VMEM, VMEM),
        compiler_params=params(16),
        cost_estimate=COST,
        name="merge",
    )(x, y, x_later, y_later, *after)


def total_kernel(own_ref, x_ref, y_ref, x_late_ref, y_late_ref, *refs):
    outs = refs[-own_ref.shape[0]:]
    half = y_late_ref.shape[0]
    for index, out in enumerate(outs):
        total = own_ref[index].astype(F32)
        if index < half:
            total += x_ref[half + index].astype(F32) + y_late_ref[index].astype(F32)
        else:
            total += y_ref[index].astype(F32) + x_late_ref[index - half].astype(F32)
        out[...] = total.astype(BF16)


def totals(own, x, y, x_late, y_late, *after):
    count, part, width = own.shape
    return pl.pallas_call(
        total_kernel,
        out_shape=tuple([jax.ShapeDtypeStruct((part, width), BF16)] * count),
        in_specs=[VMEM] * 5 + [ANY] * len(after),
        out_specs=tuple([VMEM] * count),
        compiler_params=params(16),
        cost_estimate=COST,
        name="totals",
    )(own, x, y, x_late, y_late, *after)


def collect_kernel(count, *refs):
    outs = refs[count:]
    part, width = refs[0].shape
    total = refs[0][...].astype(F32)
    for ref in refs[1:count]:
        total = total + ref[...].astype(F32)
    if len(outs) == 1:
        outs[0][...] = total.astype(BF16)
        return
    vector_ref, other_ref, short_ref, long_ref, held_ref = outs[0], outs[1], *outs[-3:]
    short_ref[pl.ds(0, part), :] = total.astype(BF16)
    rest = vector_ref[0:3, :]
    held_ref[...] = jnp.zeros_like(held_ref)
    for index in range(3):
        piece = rest.astype(BF16).astype(F32)
        held_ref[3 * index:3 * index + 3, :] = piece
        rest = rest - piece
    short_ref[pl.ds(part, 16), :] = held_ref[...].astype(BF16)
    long_ref[pl.ds(0, part + 16), :] = short_ref[...]
    long_ref[pl.ds(part + 16, part), :] = other_ref[...]


def collect(parts, vector=None, other=None, after=()):
    part, width = parts[0].shape
    operands = list(parts)
    if vector is None:
        counts = (part,)
        scratch = []
    else:
        operands += [vector, other]
        counts = (part + 16, 2 * part + 16)
        scratch = [pltpu.VMEM((16, width), F32)]
    return pl.pallas_call(
        functools.partial(collect_kernel, len(parts)),
        out_shape=tuple(jax.ShapeDtypeStruct((rows, width), BF16) for rows in counts),
        in_specs=[VMEM] * len(operands) + [ANY] * len(after),
        out_specs=tuple([VMEM] * len(counts)),
        scratch_shapes=scratch,
        compiler_params=params(16),
        cost_estimate=COST,
        name="collect",
    )(*operands, *after)


def place_kernel(part, tokens, group_ref, *refs):
    ups, downs = refs[:4], refs[4:8]
    up_ref, down_ref, gain_ref, scale_ref, loss_ref, held_ref = refs[8:]
    group = group_ref[0]
    vectors = []
    for index, (up, down) in enumerate(zip(ups, downs)):
        first = pl.multiple_of(jnp.bitwise_xor(group, index) * part, part)
        held_ref[pl.ds(first, part), :] = up[pl.ds(0, part), :].astype(F32)
        start = down.shape[0] - part
        down_ref[pl.ds(first, part), :] = down[pl.ds(start, part), :].astype(F32)
        rows = up[pl.ds(part, 16), :].astype(F32)
        vectors.append((rows[0:3] + rows[3:6]) + rows[6:9])
    up_ref[...] = held_ref[...].T
    vector = (vectors[0] + vectors[1]) + (vectors[2] + vectors[3])
    gain_ref[...] = vector[0:1]
    scale_ref[...] = vector[1:2]
    loss_ref[...] = vector[2:3, 0:1] * (1.0 / tokens)


def place_quarters(group, ups, downs, part, tokens):
    width = ups[0].shape[1]
    shapes = [
        jax.ShapeDtypeStruct((width, 4 * part), F32),
        jax.ShapeDtypeStruct((4 * part, width), F32),
        jax.ShapeDtypeStruct((1, width), F32),
        jax.ShapeDtypeStruct((1, width), F32),
        jax.ShapeDtypeStruct((1, 1), F32),
    ]
    return pl.pallas_call(
        functools.partial(place_kernel, part, tokens),
        out_shape=tuple(shapes),
        in_specs=[SMEM] + [VMEM] * 8,
        out_specs=tuple([VMEM] * len(shapes)),
        scratch_shapes=[pltpu.VMEM((4 * part, width), F32)],
        compiler_params=params(16),
        cost_estimate=COST,
        name="place",
    )(group, *ups, *downs)


def shards_square(
    image_tokens,
    tile_lists,
    opacity,
    tile_counts,
    ray_pixel,
    block_owner,
    gaussian_features,
    layer_norm_gain,
    layer_scale,
    up_weight,
    down_weight,
):
    ray_count = lax.axis_size("ray")
    group_count = lax.axis_size("grp")
    depth = ray_count // 2
    group = lax.axis_index("grp").reshape(1)
    me = lax.axis_index("ray").reshape(1)
    rows, width = image_tokens.shape
    part = down_weight.shape[0] // group_count

    def beside(array, flip):
        return lax.ppermute(array, "grp", [(g, g ^ flip) for g in range(group_count)])

    def partner(array, flip=1):
        return lax.ppermute(array, "ray", [(r, r ^ flip) for r in range(ray_count)])

    def along(array, shift):
        pairs = [(r, (r + 2 * shift) % ray_count) for r in range(ray_count)]
        return lax.ppermute(array, "ray", pairs)

    mine = own_quarter(group, up_weight, down_weight, part)
    arrivals = [along(mine, -shift) for shift in range(1, depth)]
    rendered = render(
        ray_count, True, me, block_owner, tile_lists, opacity, tile_counts.reshape(1, rows),
        ray_pixel, gaussian_features,
    )
    half = depth // 2
    low = pack(arrivals[:half - 1], rendered[0])
    x_low, y_low = beside(low, 1), beside(low, 2)
    high = pack(arrivals[half - 1:], low)
    x_high, y_high = beside(high, 1), beside(high, 2)
    y_low = tie(y_low, high)
    d_low = beside(y_low, 1)
    targets = [rendered[0]] + [along(rendered[shift], shift) for shift in range(1, depth)]
    early = pack([own_rows(group, up_weight, down_weight), low, x_low, y_low], high)
    early_other = partner(early)
    tokens, normed, normed_t = prepare_tokens(
        ray_count, True, me, block_owner, ray_pixel, image_tokens,
        layer_norm_gain.reshape(1, width),
    )
    act_early, slope_early, mixed = forward(normed_t, [early], [early_other])
    late = pack([d_low, high, x_high, y_high], mixed, targets[half])
    late_other = partner(late)
    passed_x, passed_y = turn(y_high, x_high)
    d_high = [beside(passed_x, 1), beside(passed_y, 2)]
    act_late, slope_late, mixed = forward(normed_t, [late], [late_other], mixed)
    rest = [target for shift, target in enumerate(targets) if shift not in (0, half)]
    last = pack(d_high, mixed, *rest)
    last_other = partner(last)
    act_last, slope_last, back, back_t, small = forward(
        normed_t, [last], [last_other], mixed,
        (tokens, layer_scale.reshape(1, width), *targets, partner(seconds(targets))),
    )
    acts, slopes = (act_early, act_late, act_last), (slope_early, slope_late, slope_last)
    weights = ((early, late, last), (early_other, late_other, last_other))
    count = half - 1
    rest = depth - half
    pieces = tuple(
        ((0, q, 1), (0, 4 + q * count, count), (1, count + q * rest, rest)) for q in range(3)
    ) + (((0, 3, 1), (1, 0, count), (2, 0, rest)),)
    gain = jnp.zeros((1, width), F32)
    (down_other,) = down_gradient(1, pieces, depth, acts, back)
    down_arrived = partner(down_other)
    up_other, gain = up_gradient(
        1, pieces, pieces, depth, weights[1], slopes, back_t, normed, gain
    )
    up_arrived = partner(up_other)
    down_sums = down_gradient(0, pieces, depth, acts, back, down_arrived)
    *up_sums, vector = up_gradient(
        0, pieces, pieces, depth, weights[0], slopes, back_t, normed, gain,
        (up_arrived, layer_norm_gain.reshape(1, width), small),
    )
    vector = vector + partner(vector)
    vector = vector + partner(vector, 2)

    def first_step(to_x, to_y, x_later, y_later, *after):
        from_x, from_y = beside(to_x, 1), beside(to_y, 2)
        return from_x, from_y, merge(from_x, from_y, x_later, y_later, *after)

    def second_step(later):
        return beside(later[0], 1), beside(later[1], 2)

    def arrive_along(shares):
        return [shares[0]] + [along(shares[shift], shift) for shift in range(1, depth)]

    own, *rest = down_sums
    own_up, to_x, to_y, *rest_up = up_sums
    from_x, from_y, later = first_step(*rest, vector)
    late = second_step(later)
    shares = totals(own, from_x, from_y, *late)
    (down_total,) = collect(arrive_along(shares))
    down_x, down_y = beside(down_total, 1), beside(down_total, 2)
    flip = 4
    while flip < ray_count:
        vector = vector + partner(vector, flip)
        flip *= 2
    from_x, from_y, later = first_step(to_x, to_y, *rest_up)
    shares = totals(own_up, from_x, from_y, *second_step(later), vector)
    short, long = collect(arrive_along(shares), vector, down_total, (down_x, down_y))
    up_x, up_y, both = beside(short, 1), beside(short, 2), beside(long, 3)
    grad_up, grad_down, gain, scale, loss = place_quarters(
        group, (short, up_x, up_y, both), (down_total, down_x, down_y, both), part,
        rows * ray_count * group_count,
    )
    return (grad_up, grad_down, gain.reshape(width), scale.reshape(width), loss.reshape(()))


def shards(*operands):
    ray_count, group_count = lax.axis_size("ray"), lax.axis_size("grp")
    hidden = operands[-1].shape[0]
    square = group_count == 4 and ray_count in (8, 16) and hidden % (16 * group_count) == 0
    return (shards_square if square else shards_general)(*operands)


def solution(mesh):
    return jax.shard_map(
        shards,
        mesh=mesh,
        in_specs=(
            P(("grp", "ray"), None),
            P(None, ("grp", "ray")),
            P(None, ("grp", "ray")),
            P(("grp", "ray")),
            P("grp", None),
            P("grp", None),
            P(("grp", "ray"), None),
            P(),
            P(),
            P(None, "ray"),
            P("ray", None),
        ),
        out_specs=(P(None, "ray"), P("ray", None), P(), P(), P()),
        check_vma=False,
    )
```

```python
import functools

import jax
import jax.numpy as jnp
from jax import lax
from jax.experimental import pallas as pl
from jax.experimental.pallas import tpu as pltpu
from jax.sharding import PartitionSpec as P

STABILITY_EPSILON = 1e-06
F32 = jnp.float32
BF16 = jnp.bfloat16
MIB = 1024 * 1024
COST = pl.CostEstimate(flops=1 << 20, bytes_accessed=1 << 16, transcendentals=0)
LONG = pl.CostEstimate(flops=10**10, bytes_accessed=1 << 20, transcendentals=0)
SMEM = pl.BlockSpec(memory_space=pltpu.SMEM)
VMEM = pl.BlockSpec(memory_space=pltpu.VMEM)
ANY = pl.BlockSpec(memory_space=pl.ANY)


def params(mib=48, **more):
    return pltpu.CompilerParams(vmem_limit_bytes=mib * MIB, **more)


def dot_nn(a, b):
    return lax.dot_general(a, b, (((1,), (0,)), ((), ())), preferred_element_type=F32)


def dot_tn(a, b):
    return lax.dot_general(a, b, (((0,), (0,)), ((), ())), preferred_element_type=F32)


def dot_nt(a, b):
    return lax.dot_general(a, b, (((1,), (1,)), ((), ())), preferred_element_type=F32)


def owner_of(pixels, owner_ref, rows, count):
    block = lax.div(pixels, jnp.int32(rows))
    owner = jnp.zeros_like(pixels)
    for slot in range(count):
        owner = jnp.where(block == slot, owner_ref[0:1, slot:slot + 1], owner)
    return owner


def earlier(rows):
    before = lax.broadcasted_iota(jnp.int32, (rows, rows), 0)
    after = lax.broadcasted_iota(jnp.int32, (rows, rows), 1)
    return jnp.where(before < after, 1.0, 0.0).astype(BF16)


HBM = pl.BlockSpec(memory_space=pltpu.HBM)


def fetch(copies, sems):
    started = [
        pltpu.make_async_copy(source, target, sems.at[index])
        for index, (source, target) in enumerate(copies)
    ]
    for copy in started:
        copy.start()

    def wait(*numbers):
        for number in numbers:
            started[number].wait()

    return wait


def render_kernel(
    ray_count, relative, me_ref, owner_hbm, lists_hbm, opacity_hbm, counts_hbm, pixels_hbm,
    features_hbm, *refs,
):
    outs = refs[:-10]
    owner_ref, ids_ref, opacity_ref, counts_ref, mine_ref, features_ref = refs[-10:-4]
    share_ref, table_ref, send_ref, sems = refs[-4:]
    depth, rays = lists_hbm.shape
    gauss = features_hbm.shape[0]
    width = features_hbm.shape[1]
    me = me_ref[0]
    own_pixels = pixels_hbm.at[:, pl.ds(pl.multiple_of(me * rays, rays), rays)]
    wait = fetch(
        [
            (lists_hbm, ids_ref), (opacity_hbm, opacity_ref), (counts_hbm, counts_ref),
            (owner_hbm, owner_ref), (own_pixels, mine_ref), (features_hbm, features_ref),
        ],
        sems,
    )
    wait(0, 1, 2)
    ids_ref[...] = ids_ref[...] - me * gauss
    passing = jnp.ones((1, rays), F32)
    counts = counts_ref[...]
    for level in range(depth):
        alpha = opacity_ref[pl.ds(level, 1), :]
        share_ref[pl.ds(level, 1), :] = jnp.where(level < counts, alpha * passing, 0.0)
        passing = passing * (1.0 - alpha)

    tile = 256
    lanes = 128
    columns = rays // lanes

    @pl.loop(0, (gauss // tile) * columns)
    def _(step):
        first = pl.multiple_of(lax.div(step, columns) * tile, tile)
        lane = pl.multiple_of(lax.rem(step, columns) * lanes, lanes)
        number = (lax.broadcasted_iota(jnp.int32, (tile, lanes), 0) + first).astype(jnp.int16)
        total = jnp.zeros((tile, lanes), BF16)
        for level in range(depth):
            ident = jnp.broadcast_to(ids_ref[pl.ds(level, 1), pl.ds(lane, lanes)], (16, lanes))
            share = jnp.broadcast_to(share_ref[pl.ds(level, 1), pl.ds(lane, lanes)], (16, lanes))
            ident = jnp.concatenate([ident.astype(jnp.int16)] * (tile // 16), axis=0)
            share = jnp.concatenate([share.astype(BF16)] * (tile // 16), axis=0)
            total = total + jnp.where(ident == number, share, jnp.zeros_like(share))
        table_ref[pl.ds(first, tile), pl.ds(lane, lanes)] = total

    wait(3, 4, 5)
    owner = owner_of(mine_ref[...], owner_ref, rays, ray_count)
    padded = -(-ray_count // 16) * 16
    member = (lax.broadcasted_iota(jnp.int32, (padded, rays), 0) == owner)
    ranks = dot_nn(member.astype(F32).astype(BF16), earlier(rays))
    rank = jnp.sum(jnp.where(member, ranks, 0.0), axis=0, keepdims=True).astype(jnp.int32)
    if relative:
        chips = ray_count // 2
        shift = lax.div(owner, jnp.int32(2)) - lax.div(me, jnp.int32(2))
        shift = jnp.where(shift < 0, shift + chips, shift)
        flip = jnp.where(lax.rem(owner, jnp.int32(2)) == lax.rem(me, jnp.int32(2)), 0, 1)
        block = 2 * shift + flip
    else:
        block = owner
    slot = block * (rays // ray_count) + rank
    send_ref[...] = (
        (lax.broadcasted_iota(jnp.int32, (rays, rays), 0) == slot).astype(F32).astype(BF16)
    )

    piece = 256
    span = rays // len(outs)

    @pl.loop(0, width // piece)
    def _(step):
        cols = pl.ds(pl.multiple_of(step * piece, piece), piece)
        rendered = dot_tn(table_ref[...], features_ref[:, cols]).astype(BF16)
        ordered = dot_nn(send_ref[...], rendered).astype(BF16)
        for index, out in enumerate(outs):
            rows = ordered[index * span:(index + 1) * span]
            out[:, :, cols] = rows.reshape(*out.shape[:2], piece)


def render(ray_count, relative, me, owner, lists, opacity, counts, pixels, features):
    depth, rays = lists.shape
    gauss, width = features.shape
    parts = ray_count // 2 if relative else 1
    shape = jax.ShapeDtypeStruct((ray_count // parts, rays // ray_count, width), BF16)
    return pl.pallas_call(
        functools.partial(render_kernel, ray_count, relative),
        out_shape=(shape,) * parts,
        in_specs=[SMEM] + [HBM] * 6,
        out_specs=(VMEM,) * parts,
        scratch_shapes=[
            pltpu.VMEM(owner.shape, jnp.int32),
            pltpu.VMEM((depth, rays), jnp.int32),
            pltpu.VMEM((depth, rays), F32),
            pltpu.VMEM((1, rays), jnp.int32),
            pltpu.VMEM((1, rays), jnp.int32),
            pltpu.VMEM((gauss, width), BF16),
            pltpu.VMEM((depth, rays), F32),
            pltpu.VMEM((gauss, rays), BF16),
            pltpu.VMEM((rays, rays), BF16),
            pltpu.SemaphoreType.DMA((6,)),
        ],
        compiler_params=params(20),
        cost_estimate=COST,
        name="render",
    )(me, owner, lists, opacity, counts, pixels, features)


def tokens_kernel(
    ray_count, relative, me_ref, owner_hbm, pixels_hbm, tokens_hbm, gain_hbm,
    *refs,
):
    tokens_out, normed_out, normed_t_out = refs[-11:-8]
    owner_ref, pixels_ref, tokens_ref, gain_ref, order_ref, rank_ref, place_ref, sems = refs[-8:]
    rows, width = tokens_hbm.shape
    me = me_ref[0]
    each = rows // ray_count
    wait = fetch(
        [
            (owner_hbm, owner_ref), (pixels_hbm, pixels_ref), (gain_hbm, gain_ref),
            (tokens_hbm, tokens_ref),
        ],
        sems,
    )
    wait(0, 1)
    pixels = jnp.concatenate(
        [pixels_ref[:, sender * rows:(sender + 1) * rows] for sender in range(ray_count)], axis=0
    )
    mine = owner_of(pixels, owner_ref, rows, ray_count) == me
    place_ref[...] = lax.rem(pixels, jnp.int32(rows)).astype(F32)
    member = jnp.where(mine, 1.0, 0.0)
    padded = -(-ray_count // 16) * 16
    if padded > ray_count:
        spread = jnp.concatenate([member, jnp.zeros((padded - ray_count, rows), F32)], axis=0)
    else:
        spread = member
    ranks = dot_nn(spread.astype(BF16), earlier(rows))
    rank_ref[...] = jnp.where(mine, ranks[:ray_count], -1.0)
    chips = ray_count // 2
    for index in range(ray_count):
        if relative:
            chip = lax.rem(lax.div(me, jnp.int32(2)) + (chips - index // 2), jnp.int32(chips))
            sender = 2 * chip + jnp.bitwise_xor(lax.rem(me, jnp.int32(2)), index % 2)
        else:
            sender = index
        rank = rank_ref[pl.ds(sender, 1), :].astype(jnp.int32)
        hit = lax.broadcasted_iota(jnp.int32, (each, rows), 0) == rank
        at = jnp.sum(
            jnp.where(hit, place_ref[pl.ds(sender, 1), :], 0.0), axis=1, keepdims=True
        )
        here = lax.broadcasted_iota(jnp.int32, (each, rows), 1) == at.astype(jnp.int32)
        order_ref[pl.ds(index * each, each), :] = here.astype(F32).astype(BF16)
    wait(2, 3)
    half = min(128, rows)
    gain = gain_ref[...]

    @pl.loop(0, rows // half)
    def _(step):
        span = pl.ds(pl.multiple_of(step * half, half), half)
        values = dot_nn(order_ref[span, :], tokens_ref[...])
        tokens_out[span, :] = values.astype(BF16)
        centered = values - jnp.mean(values, axis=-1, keepdims=True)
        variance = jnp.mean(centered * centered, axis=-1, keepdims=True)
        xhat = centered * lax.rsqrt(variance + STABILITY_EPSILON)
        normed = (xhat * gain).astype(BF16)
        normed_out[span, :] = normed
        normed_t_out[:, span] = normed.T


def prepare_tokens(ray_count, relative, me, owner, pixels, tokens, gain, after=()):
    rows, width = tokens.shape
    return pl.pallas_call(
        functools.partial(tokens_kernel, ray_count, relative),
        out_shape=(
            jax.ShapeDtypeStruct((rows, width), BF16),
            jax.ShapeDtypeStruct((rows, width), BF16),
            jax.ShapeDtypeStruct((width, rows), BF16),
        ),
        in_specs=[SMEM] + [HBM] * 4 + [ANY] * len(after),
        out_specs=(VMEM, VMEM, VMEM),
        scratch_shapes=[
            pltpu.VMEM(owner.shape, jnp.int32),
            pltpu.VMEM(pixels.shape, jnp.int32),
            pltpu.VMEM((rows, width), BF16),
            pltpu.VMEM((1, width), F32),
            pltpu.VMEM((rows, rows), BF16),
            pltpu.VMEM((ray_count, rows), F32),
            pltpu.VMEM((ray_count, rows), F32),
            pltpu.SemaphoreType.DMA((4,)),
        ],
        compiler_params=params(20),
        cost_estimate=COST,
        name="tokens",
    )(me, owner, pixels, tokens, gain, *after)


def up_kernel(normed_ref, up_ref, act_ref, slope_ref):
    parts, _, part_rows, width = up_ref.shape
    up = up_ref[...].reshape(parts * part_rows, width)
    rows = normed_ref.shape[0]
    piece = min(128, rows)

    @pl.loop(0, rows // piece)
    def _(step):
        span = pl.ds(pl.multiple_of(step * piece, piece), piece)
        hidden = dot_nn(normed_ref[span, :], up)
        phi = 0.5 * (1.0 + lax.erf(hidden * (0.5 ** 0.5)))
        density = jnp.exp(-0.5 * hidden * hidden) * ((2.0 * jnp.pi) ** -0.5)
        act_ref[span, :] = (hidden * phi).astype(BF16)
        slope_ref[span, :] = (phi + hidden * density).astype(slope_ref.dtype)


def project_up(normed, up):
    rows, width = normed.shape
    parts, chunks, part_rows, chunk = up.shape
    return pl.pallas_call(
        up_kernel,
        grid=(chunks,),
        out_shape=(
            jax.ShapeDtypeStruct((rows, chunks * chunk), BF16),
            jax.ShapeDtypeStruct((rows, chunks * chunk), F32),
        ),
        in_specs=[
            pl.BlockSpec((rows, width), lambda j: (0, 0)),
            pl.BlockSpec((parts, 1, part_rows, chunk), lambda j: (0, j, 0, 0)),
        ],
        out_specs=(
            pl.BlockSpec((rows, chunk), lambda j: (0, j)),
            pl.BlockSpec((rows, chunk), lambda j: (0, j)),
        ),
        compiler_params=params(dimension_semantics=("arbitrary",)),
        cost_estimate=COST,
        name="up",
    )(normed, up)


def down_kernel(
    chunks, act_ref, down_ref, tokens_ref, target_ref, scale_ref,
    grad_ref, back_ref, small_ref, mixed_ref,
):
    step = pl.program_id(0)
    rows, width = tokens_ref.shape
    act = act_ref[...]

    @pl.when(step < chunks)
    def _():
        parts, _, part_rows, _ = down_ref.shape
        part = dot_nn(act, down_ref[...].reshape(parts * part_rows, width))

        @pl.when(step == 0)
        def _():
            mixed_ref[...] = part

        @pl.when(step > 0)
        def _():
            mixed_ref[...] += part

    @pl.when(step == chunks - 1)
    def _():
        scale = scale_ref[...]
        small_ref[...] = jnp.zeros_like(small_ref)
        piece = min(64, rows)

        @pl.loop(0, rows // piece)
        def _(index):
            span = pl.ds(pl.multiple_of(index * piece, piece), piece)
            mixed = mixed_ref[span, :]
            out = tokens_ref[span, :].astype(F32) + scale * mixed
            goal = target_ref[span, :].astype(F32)
            out_norm = jnp.sqrt(jnp.sum(out * out, axis=-1, keepdims=True) + STABILITY_EPSILON)
            goal_norm = jnp.sqrt(jnp.sum(goal * goal, axis=-1, keepdims=True) + STABILITY_EPSILON)
            norms = out_norm * goal_norm
            cosine = jnp.sum(out * goal, axis=-1, keepdims=True) / norms
            upstream = (cosine / (out_norm * out_norm)) * out - goal * (1.0 / norms)
            back_ref[span, :] = (upstream * scale).astype(BF16)
            small_ref[0:1, :] += jnp.sum(upstream * mixed, axis=0, keepdims=True)
            loss = jnp.sum(1.0 - cosine, axis=0, keepdims=True)
            small_ref[1:2, :] += jnp.broadcast_to(loss, (1, width))

    @pl.when(step >= chunks)
    def _():
        grad = dot_tn(act, back_ref[...])
        grad_ref[...] = grad.astype(BF16).reshape(grad_ref.shape)


def project_down(act, down, tokens, target, scale):
    rows, width = tokens.shape
    parts, chunks, part_rows, _ = down.shape
    chunk = parts * part_rows
    return pl.pallas_call(
        functools.partial(down_kernel, chunks),
        grid=(2 * chunks,),
        out_shape=(
            jax.ShapeDtypeStruct(down.shape, BF16),
            jax.ShapeDtypeStruct((rows, width), BF16),
            jax.ShapeDtypeStruct((8, width), F32),
        ),
        in_specs=[
            pl.BlockSpec((rows, chunk), lambda j: (0, lax.rem(j, chunks))),
            pl.BlockSpec(
                (parts, 1, part_rows, width), lambda j: (0, jnp.minimum(j, chunks - 1), 0, 0)
            ),
            pl.BlockSpec((rows, width), lambda j: (0, 0)),
            pl.BlockSpec((rows, width), lambda j: (0, 0)),
            pl.BlockSpec((1, width), lambda j: (0, 0)),
        ],
        out_specs=(
            pl.BlockSpec(
                (parts, 1, part_rows, width), lambda j: (0, jnp.maximum(j - chunks, 0), 0, 0)
            ),
            pl.BlockSpec((rows, width), lambda j: (0, 0)),
            pl.BlockSpec((8, width), lambda j: (0, 0)),
        ),
        scratch_shapes=[pltpu.VMEM((rows, width), F32)],
        compiler_params=params(dimension_semantics=("arbitrary",)),
        cost_estimate=COST,
        name="down",
    )(act, down, tokens, target, scale)


def back_kernel(back_ref, down_ref, slope_ref, normed_t_ref, up_ref, gain_ref, grad_ref, sum_ref):
    step = pl.program_id(0)
    parts, _, part_rows, width = down_ref.shape
    chunk = parts * part_rows
    rows = back_ref.shape[0]
    back_act = dot_nt(back_ref[...], down_ref[...].reshape(chunk, width))
    back_hidden = (back_act * slope_ref[...]).astype(BF16)
    up_parts, _, up_rows, _ = up_ref.shape

    @pl.when(step == 0)
    def _():
        sum_ref[...] = jnp.zeros_like(sum_ref)

    grad = dot_nn(normed_t_ref[...], back_hidden)
    grad_ref[...] = grad.astype(BF16).reshape(grad_ref.shape)
    up = up_ref[...].reshape(up_parts * up_rows, chunk).astype(F32)
    sum_ref[...] += jnp.sum(grad * up, axis=1, keepdims=True) / gain_ref[...]


def back_up(back, down, slope, normed_t, up, gain):
    width, rows = normed_t.shape
    parts, chunks, part_rows, _ = down.shape
    chunk = parts * part_rows
    up_parts, _, up_rows, _ = up.shape
    return pl.pallas_call(
        back_kernel,
        grid=(chunks,),
        out_shape=(
            jax.ShapeDtypeStruct(up.shape, BF16),
            jax.ShapeDtypeStruct((width, 1), F32),
        ),
        in_specs=[
            pl.BlockSpec((rows, width), lambda j: (0, 0)),
            pl.BlockSpec((parts, 1, part_rows, width), lambda j: (0, j, 0, 0)),
            pl.BlockSpec((rows, chunk), lambda j: (0, j)),
            pl.BlockSpec((width, rows), lambda j: (0, 0)),
            pl.BlockSpec((up_parts, 1, up_rows, chunk), lambda j: (0, j, 0, 0)),
            pl.BlockSpec((width, 1), lambda j: (0, 0)),
        ],
        out_specs=(
            pl.BlockSpec((up_parts, 1, up_rows, chunk), lambda j: (0, j, 0, 0)),
            pl.BlockSpec((width, 1), lambda j: (0, 0)),
        ),
        compiler_params=params(dimension_semantics=("arbitrary",)),
        cost_estimate=COST,
        name="back",
    )(back, down, slope, normed_t, up, gain)


def gather_weight(weight, parts, group, group_count, ray_count):
    rows, cols = weight.shape
    if parts == 1:
        whole = lax.all_gather(weight, "ray", axis=0, tiled=True)
    else:
        part = lax.dynamic_slice_in_dim(weight, group * (rows // parts), rows // parts, 0)
        whole = lax.all_gather(part, ("grp", "ray"), axis=0, tiled=True)
    return whole.reshape(parts, ray_count, rows // parts, cols)


def reduce_gradient(grad):
    parts, ray_count, part_rows, cols = grad.shape
    flat = grad.reshape(parts * ray_count * part_rows, cols)
    if parts == 1:
        share = lax.psum_scatter(flat, "ray", scatter_dimension=0, tiled=True)
        return lax.psum(share.astype(F32), "grp")
    share = lax.psum_scatter(flat, "grp", scatter_dimension=0, tiled=True)
    share = lax.psum_scatter(share, "ray", scatter_dimension=0, tiled=True)
    return lax.all_gather(share, "grp", axis=0, tiled=True).astype(F32)


def shards_general(
    image_tokens,
    tile_lists,
    opacity,
    tile_counts,
    ray_pixel,
    block_owner,
    gaussian_features,
    layer_norm_gain,
    layer_scale,
    up_weight,
    down_weight,
):
    ray_count = lax.axis_size("ray")
    group_count = lax.axis_size("grp")
    group = lax.axis_index("grp")
    me = lax.axis_index("ray").reshape(1)
    rows, width = image_tokens.shape
    up_parts = group_count if up_weight.shape[0] % (16 * group_count) == 0 else 1
    down_parts = group_count if down_weight.shape[0] % (16 * group_count) == 0 else 1
    up = gather_weight(up_weight, up_parts, group, group_count, ray_count)
    down = gather_weight(down_weight, down_parts, group, group_count, ray_count)
    rendered = render(
        ray_count, False, me, block_owner, tile_lists, opacity, tile_counts.reshape(1, rows),
        ray_pixel, gaussian_features,
    )
    rendered = rendered[0].reshape(rows, width)
    target = lax.all_to_all(rendered, "ray", split_axis=0, concat_axis=0, tiled=True)
    tokens, normed, normed_t = prepare_tokens(
        ray_count, False, me, block_owner, ray_pixel, image_tokens,
        layer_norm_gain.reshape(1, width),
    )
    act, slope = project_up(normed, up)
    grad_down, back, small = project_down(act, down, tokens, target, layer_scale.reshape(1, width))
    grad_up, gain_sum = back_up(back, down, slope, normed_t, up, layer_norm_gain.reshape(width, 1))
    grad_down = reduce_gradient(grad_down)
    grad_up = reduce_gradient(grad_up)
    sums = jnp.concatenate([gain_sum.reshape(1, width), small[:2]], axis=0)
    sums = lax.psum(sums, ("grp", "ray"))
    loss = sums[2, 0] / (rows * ray_count * group_count)
    return (grad_up, grad_down, sums[0], sums[1], loss)


def quarter_kernel(group_ref, up_hbm, down_hbm, out_ref, up_ref, turned_ref, sems):
    part = out_ref.shape[1]
    lanes = up_ref.shape[1]
    start = pl.multiple_of(group_ref[0] * part, part)
    lane = pl.multiple_of(lax.div(start, jnp.int32(lanes)) * lanes, lanes)
    wait = fetch(
        [
            (up_hbm.at[:, pl.ds(lane, lanes)], up_ref),
            (down_hbm.at[pl.ds(start, part), :], out_ref.at[1]),
        ],
        sems,
    )
    wait(0)
    turned_ref[...] = up_ref[...].T
    out_ref[0] = turned_ref[pl.ds(pl.multiple_of(start - lane, part), part), :]
    wait(1)


def own_quarter(group, up, down, part):
    width, chunk = up.shape
    lanes = max(128, part)
    return pl.pallas_call(
        quarter_kernel,
        out_shape=jax.ShapeDtypeStruct((2, part, width), BF16),
        in_specs=[SMEM, HBM, HBM],
        out_specs=VMEM,
        scratch_shapes=[
            pltpu.VMEM((width, lanes), BF16),
            pltpu.VMEM((lanes, width), BF16),
            pltpu.SemaphoreType.DMA((2,)),
        ],
        compiler_params=params(16),
        cost_estimate=LONG,
        name="quarter",
    )(group, up, down)


def own_rows_kernel(group_ref, up_ref, down_ref, out_ref, turned_ref):
    part = out_ref.shape[2]
    turned_ref[...] = up_ref[...].T
    for index in range(4):
        quarter = jnp.bitwise_xor(group_ref[0], index)
        span = pl.ds(pl.multiple_of(quarter * part, part), part)
        out_ref[index, 0] = turned_ref[span, :]
        out_ref[index, 1] = down_ref[span, :]


def own_rows(group, up, down):
    width, chunk = up.shape
    return pl.pallas_call(
        own_rows_kernel,
        out_shape=jax.ShapeDtypeStruct((4, 2, chunk // 4, width), BF16),
        in_specs=[SMEM, VMEM, VMEM],
        out_specs=VMEM,
        scratch_shapes=[pltpu.VMEM((chunk, width), BF16)],
        compiler_params=params(16),
        cost_estimate=COST,
        name="own_rows",
    )(group, up, down)


def finish_rows(tokens, mixed, goal, scale):
    out = tokens + scale * mixed
    out_norm = jnp.sqrt(jnp.sum(out * out, axis=-1, keepdims=True) + STABILITY_EPSILON)
    goal_norm = jnp.sqrt(jnp.sum(goal * goal, axis=-1, keepdims=True) + STABILITY_EPSILON)
    norms = out_norm * goal_norm
    cosine = jnp.sum(out * goal, axis=-1, keepdims=True) / norms
    upstream = (cosine / (out_norm * out_norm)) * out - goal * (1.0 / norms)
    return upstream, 1.0 - cosine


def forward_kernel(first, blocks, sides, skipped, *refs):
    last = blocks > 0
    refs = list(refs[skipped:])
    normed_t_ref = refs.pop(0)
    own, other = refs[:sides], refs[sides:2 * sides]
    del refs[:2 * sides]
    mixed_in = None if first else refs.pop(0)
    if last:
        tokens_ref, scale_ref = refs[:2]
        targets, passed_ref = refs[2:2 + blocks], refs[2 + blocks]
        del refs[:3 + blocks]
    act_ref, slope_ref = refs[:2]
    del refs[:2]
    width, rows = normed_t_ref.shape
    part = act_ref.shape[2]
    part_sum = None
    downs = []
    for side, group in enumerate((own, other)):
        start = 0
        for ref in group:
            count = ref.shape[0]
            hiddens = dot_nn(ref[:, 0].reshape(count * part, width), normed_t_ref[...])
            for index in range(count):
                hidden = hiddens[index * part:(index + 1) * part]
                phi = 0.5 * (1.0 + lax.erf(hidden * (0.5 ** 0.5)))
                density = jnp.exp(-0.5 * hidden * hidden) * ((2.0 * jnp.pi) ** -0.5)
                act_ref[side, start + index] = (hidden * phi).astype(BF16)
                slope_ref[side, start + index] = phi + hidden * density
            downs.append(ref[:, 1].reshape(count * part, width))
            start += count
    if sides > 1 or last:
        act = act_ref[...].reshape(2 * start * part, rows)
        part_sum = dot_tn(act, jnp.concatenate(downs, axis=0))
    else:
        for side, down in enumerate(downs):
            term = dot_tn(act_ref[side].reshape(start * part, rows), down)
            part_sum = term if part_sum is None else part_sum + term
    if not last:
        mixed_out = refs[0]
        mixed_out[...] = part_sum if first else mixed_in[...] + part_sum
        return
    back_ref, back_t_ref, small_ref, mixed_ref = refs
    mixed_ref[...] = mixed_in[...] + part_sum
    scale = scale_ref[...]
    small_ref[...] = jnp.zeros_like(small_ref)
    piece = rows // blocks
    for index, target_ref in enumerate(targets):
        span = pl.ds(index * piece, piece)
        mixed = mixed_ref[span, :]
        goal = jnp.concatenate([target_ref[0], passed_ref[index]], axis=0).astype(F32)
        upstream, loss = finish_rows(tokens_ref[span, :].astype(F32), mixed, goal, scale)
        back = (upstream * scale).astype(BF16)
        back_ref[span, :] = back
        back_t_ref[:, span] = back.T
        small_ref[0:1, :] += jnp.sum(upstream * mixed, axis=0, keepdims=True)
        small_ref[1:2, :] += jnp.broadcast_to(jnp.sum(loss, axis=0, keepdims=True), (1, width))


def forward(normed_t, own, other, mixed=None, finish=None, after=()):
    width, rows = normed_t.shape
    part = own[0].shape[2]
    total = sum(array.shape[0] for array in own)
    first, last = mixed is None, finish is not None
    blocks = len(finish) - 3 if last else 0
    operands = [*after, normed_t, *own, *other]
    if not first:
        operands.append(mixed)
    if last:
        operands.extend(finish)
    piece = (2, total, part, rows)
    shapes = [jax.ShapeDtypeStruct(piece, BF16), jax.ShapeDtypeStruct(piece, F32)]
    scratch = []
    if last:
        shapes += [
            jax.ShapeDtypeStruct((rows, width), BF16),
            jax.ShapeDtypeStruct((width, rows), BF16),
            jax.ShapeDtypeStruct((8, width), F32),
        ]
        scratch = [pltpu.VMEM((rows, width), F32)]
    else:
        shapes += [jax.ShapeDtypeStruct((rows, width), F32)]
    return pl.pallas_call(
        functools.partial(forward_kernel, first, blocks, len(own), len(after)),
        out_shape=tuple(shapes),
        in_specs=[ANY] * len(after) + [VMEM] * (len(operands) - len(after)),
        out_specs=tuple([VMEM] * len(shapes)),
        scratch_shapes=scratch,
        compiler_params=params(32),
        cost_estimate=COST,
        name="forward",
    )(*operands)


def pack_kernel(counts, *refs):
    out_ref = refs[-1]
    start = 0
    for count, ref in zip(counts, refs):
        out_ref[start:start + count] = ref[...].reshape(count, *out_ref.shape[1:])
        start += count


def pack(pieces, *after):
    counts = [1 if piece.ndim == 3 else piece.shape[0] for piece in pieces]
    return pl.pallas_call(
        functools.partial(pack_kernel, counts),
        out_shape=jax.ShapeDtypeStruct((sum(counts), *pieces[0].shape[-3:]), BF16),
        in_specs=[VMEM] * len(pieces) + [ANY] * len(after),
        out_specs=VMEM,
        compiler_params=params(16),
        cost_estimate=COST,
        name="pack",
    )(*pieces, *after)


def turn_kernel(y_ref, x_ref, a_ref, b_ref):
    count = a_ref.shape[0]
    a_ref[...] = y_ref[:count]
    b_ref[...] = x_ref[count:]


def turn(y, x):
    count = y.shape[0]
    first = count // 2
    return pl.pallas_call(
        turn_kernel,
        out_shape=(
            jax.ShapeDtypeStruct((first, *y.shape[1:]), BF16),
            jax.ShapeDtypeStruct((count - first, *y.shape[1:]), BF16),
        ),
        in_specs=[VMEM] * 2,
        out_specs=(VMEM, VMEM),
        compiler_params=params(16),
        cost_estimate=COST,
        name="turn",
    )(y, x)


def tie_kernel(*refs):
    pass


def tie(array, *after):
    return pl.pallas_call(
        tie_kernel,
        out_shape=jax.ShapeDtypeStruct(array.shape, array.dtype),
        in_specs=[ANY] * (1 + len(after)),
        out_specs=ANY,
        input_output_aliases={0: 0},
        compiler_params=params(4),
        cost_estimate=COST,
        name="tie",
    )(array, *after)


def seconds_kernel(*refs):
    for index, ref in enumerate(refs[:-1]):
        refs[-1][index] = ref[1]


def seconds(blocks):
    count, (_, each, width) = len(blocks), blocks[0].shape
    return pl.pallas_call(
        seconds_kernel,
        out_shape=jax.ShapeDtypeStruct((count, each, width), BF16),
        in_specs=[VMEM] * count,
        out_specs=VMEM,
        compiler_params=params(16),
        cost_estimate=COST,
        name="seconds",
    )(*blocks)


def joined(refs, pieces, pick):
    values = [pick(refs[which], start, count) for which, start, count in pieces]
    flat = [value.reshape(-1, value.shape[-1]) for value in values]
    return flat[0] if len(flat) == 1 else jnp.concatenate(flat, axis=0)


def put(quarter, value, outs):
    own_ref, x_ref, y_ref, x_later_ref, y_later_ref = outs
    value = value.astype(BF16).reshape(own_ref.shape)
    half = x_ref.shape[0] // 2
    if quarter == 0:
        own_ref[...] = value
    elif quarter == 1:
        x_ref[half:] = value[:half]
        x_later_ref[...] = value[half:]
    elif quarter == 2:
        y_ref[half:] = value[half:]
        y_later_ref[...] = value[:half]
    else:
        x_ref[:half] = value[:half]
        y_ref[:half] = value[half:]


def emit(quarter, value, arrived, outs):
    if arrived is None:
        outs[0][quarter] = value.astype(BF16).reshape(outs[0].shape[1:])
    else:
        put(quarter, value + arrived[quarter].reshape(value.shape).astype(F32), outs)


def down_grad_kernel(side, act_pieces, add, *refs):
    acts, back_ref = refs[:2], refs[2]
    arrived = refs[3] if add else None
    outs = refs[4:] if add else refs[3:]
    for quarter in (3, 1, 2, 0):
        act = joined(acts, act_pieces[quarter], lambda ref, a, n: ref[side, a:a + n])
        emit(quarter, dot_nn(act, back_ref[...]), arrived, outs)


def up_grad_kernel(side, weight_pieces, act_pieces, add, *refs):
    weights, slopes = refs[:2], refs[2:4]
    back_t_ref, normed_ref, gain_in = refs[4:7]
    if add:
        arrived, scale_ref, small_ref = refs[7:10]
        outs, vector_ref, gain_ref = refs[10:-2], refs[-2], refs[-1]
    else:
        arrived = None
        outs, gain_ref = refs[7:-1], refs[-1]
    gain_ref[...] = gain_in[...]
    for quarter in (3, 1, 2, 0):
        pieces = weight_pieces[quarter]
        slope = joined(slopes, act_pieces[quarter], lambda ref, a, n: ref[side, a:a + n])
        back_act = dot_nn(joined(weights, pieces, lambda ref, a, n: ref[a:a + n, 1]), back_t_ref[...])
        back_hidden = (back_act * slope).astype(BF16)
        grad = dot_nn(back_hidden, normed_ref[...])
        up = joined(weights, pieces, lambda ref, a, n: ref[a:a + n, 0]).astype(F32)
        gain_ref[...] += jnp.sum(grad * up, axis=0, keepdims=True)
        emit(quarter, grad, arrived, outs)
    if add:
        vector_ref[0:1, :] = gain_ref[...] / scale_ref[...]
        vector_ref[1:3, :] = small_ref[0:2, :]
        vector_ref[3:8, :] = jnp.zeros((5, gain_ref.shape[1]), F32)


def gradient_shapes(depth, part, width, add):
    if not add:
        return [jax.ShapeDtypeStruct((4, depth, part, width), BF16)]
    counts = (depth, depth, depth, depth - depth // 2, depth // 2)
    return [jax.ShapeDtypeStruct((count, part, width), BF16) for count in counts]


def down_gradient(side, act_pieces, depth, acts, back, arrived=None):
    part = acts[0].shape[2]
    width = back.shape[1]
    add = arrived is not None
    operands = [*acts, back] + ([arrived] if add else [])
    shapes = gradient_shapes(depth, part, width, add)
    return pl.pallas_call(
        functools.partial(down_grad_kernel, side, act_pieces, add),
        out_shape=tuple(shapes),
        in_specs=[VMEM] * len(operands),
        out_specs=tuple([VMEM] * len(shapes)),
        compiler_params=params(20),
        cost_estimate=COST,
        name="down_gradient",
    )(*operands)


def up_gradient(
    side, weight_pieces, act_pieces, depth, weights, slopes, back_t, normed, gain, extra=()
):
    part, width = weights[0].shape[2:]
    add = len(extra) > 0
    operands = [*weights, *slopes, back_t, normed, gain, *extra]
    shapes = gradient_shapes(depth, part, width, add)
    if add:
        shapes.append(jax.ShapeDtypeStruct((8, width), F32))
        scratch = [pltpu.VMEM((1, width), F32)]
    else:
        scratch = []
        shapes.append(jax.ShapeDtypeStruct((1, width), F32))
    return pl.pallas_call(
        functools.partial(up_grad_kernel, side, weight_pieces, act_pieces, add),
        out_shape=tuple(shapes),
        in_specs=[VMEM] * len(operands),
        out_specs=tuple([VMEM] * len(shapes)),
        scratch_shapes=scratch,
        compiler_params=params(24),
        cost_estimate=COST,
        name="up_gradient",
    )(*operands)


def merge_kernel(x_ref, y_ref, x_later_ref, y_later_ref, *refs):
    x_out, y_out = refs[-2:]
    half = y_later_ref.shape[0]
    x_out[...] = (x_later_ref[...].astype(F32) + y_ref[:half].astype(F32)).astype(BF16)
    y_out[...] = (y_later_ref[...].astype(F32) + x_ref[:half].astype(F32)).astype(BF16)


def merge(x, y, x_later, y_later, *after):
    return pl.pallas_call(
        merge_kernel,
        out_shape=tuple(jax.ShapeDtypeStruct(a.shape, BF16) for a in (x_later, y_later)),
        in_specs=[VMEM] * 4 + [ANY] * len(after),
        out_specs=(VMEM, VMEM),
        compiler_params=params(16),
        cost_estimate=COST,
        name="merge",
    )(x, y, x_later, y_later, *after)


def total_kernel(own_ref, x_ref, y_ref, x_late_ref, y_late_ref, *refs):
    outs = refs[-own_ref.shape[0]:]
    half = y_late_ref.shape[0]
    for index, out in enumerate(outs):
        total = own_ref[index].astype(F32)
        if index < half:
            total += x_ref[half + index].astype(F32) + y_late_ref[index].astype(F32)
        else:
            total += y_ref[index].astype(F32) + x_late_ref[index - half].astype(F32)
        out[...] = total.astype(BF16)


def totals(own, x, y, x_late, y_late, *after):
    count, part, width = own.shape
    return pl.pallas_call(
        total_kernel,
        out_shape=tuple([jax.ShapeDtypeStruct((part, width), BF16)] * count),
        in_specs=[VMEM] * 5 + [ANY] * len(after),
        out_specs=tuple([VMEM] * count),
        compiler_params=params(16),
        cost_estimate=COST,
        name="totals",
    )(own, x, y, x_late, y_late, *after)


def collect_kernel(count, *refs):
    outs = refs[count:]
    part, width = refs[0].shape
    total = refs[0][...].astype(F32)
    for ref in refs[1:count]:
        total = total + ref[...].astype(F32)
    if len(outs) == 1:
        outs[0][...] = total.astype(BF16)
        return
    vector_ref, other_ref, short_ref, long_ref, held_ref = outs[0], outs[1], *outs[-3:]
    short_ref[pl.ds(0, part), :] = total.astype(BF16)
    rest = vector_ref[0:3, :]
    held_ref[...] = jnp.zeros_like(held_ref)
    for index in range(3):
        piece = rest.astype(BF16).astype(F32)
        held_ref[3 * index:3 * index + 3, :] = piece
        rest = rest - piece
    short_ref[pl.ds(part, 16), :] = held_ref[...].astype(BF16)
    long_ref[pl.ds(0, part + 16), :] = short_ref[...]
    long_ref[pl.ds(part + 16, part), :] = other_ref[...]


def collect(parts, vector=None, other=None, after=()):
    part, width = parts[0].shape
    operands = list(parts)
    if vector is None:
        counts = (part,)
        scratch = []
    else:
        operands += [vector, other]
        counts = (part + 16, 2 * part + 16)
        scratch = [pltpu.VMEM((16, width), F32)]
    return pl.pallas_call(
        functools.partial(collect_kernel, len(parts)),
        out_shape=tuple(jax.ShapeDtypeStruct((rows, width), BF16) for rows in counts),
        in_specs=[VMEM] * len(operands) + [ANY] * len(after),
        out_specs=tuple([VMEM] * len(counts)),
        scratch_shapes=scratch,
        compiler_params=params(16),
        cost_estimate=COST,
        name="collect",
    )(*operands, *after)


def place_kernel(part, tokens, group_ref, *refs):
    ups, downs = refs[:4], refs[4:8]
    up_ref, down_ref, gain_ref, scale_ref, loss_ref, held_ref = refs[8:]
    group = group_ref[0]
    vectors = []
    for index, (up, down) in enumerate(zip(ups, downs)):
        first = pl.multiple_of(jnp.bitwise_xor(group, index) * part, part)
        held_ref[pl.ds(first, part), :] = up[pl.ds(0, part), :].astype(F32)
        start = down.shape[0] - part
        down_ref[pl.ds(first, part), :] = down[pl.ds(start, part), :].astype(F32)
        rows = up[pl.ds(part, 16), :].astype(F32)
        vectors.append((rows[0:3] + rows[3:6]) + rows[6:9])
    up_ref[...] = held_ref[...].T
    vector = (vectors[0] + vectors[1]) + (vectors[2] + vectors[3])
    gain_ref[...] = vector[0:1]
    scale_ref[...] = vector[1:2]
    loss_ref[...] = vector[2:3, 0:1] * (1.0 / tokens)


def place_quarters(group, ups, downs, part, tokens):
    width = ups[0].shape[1]
    shapes = [
        jax.ShapeDtypeStruct((width, 4 * part), F32),
        jax.ShapeDtypeStruct((4 * part, width), F32),
        jax.ShapeDtypeStruct((1, width), F32),
        jax.ShapeDtypeStruct((1, width), F32),
        jax.ShapeDtypeStruct((1, 1), F32),
    ]
    return pl.pallas_call(
        functools.partial(place_kernel, part, tokens),
        out_shape=tuple(shapes),
        in_specs=[SMEM] + [VMEM] * 8,
        out_specs=tuple([VMEM] * len(shapes)),
        scratch_shapes=[pltpu.VMEM((4 * part, width), F32)],
        compiler_params=params(16),
        cost_estimate=COST,
        name="place",
    )(group, *ups, *downs)


def shards_square(
    image_tokens,
    tile_lists,
    opacity,
    tile_counts,
    ray_pixel,
    block_owner,
    gaussian_features,
    layer_norm_gain,
    layer_scale,
    up_weight,
    down_weight,
):
    ray_count = lax.axis_size("ray")
    group_count = lax.axis_size("grp")
    depth = ray_count // 2
    group = lax.axis_index("grp").reshape(1)
    me = lax.axis_index("ray").reshape(1)
    rows, width = image_tokens.shape
    part = down_weight.shape[0] // group_count

    def beside(array, flip):
        return lax.ppermute(array, "grp", [(g, g ^ flip) for g in range(group_count)])

    def partner(array, flip=1):
        return lax.ppermute(array, "ray", [(r, r ^ flip) for r in range(ray_count)])

    def along(array, shift):
        pairs = [(r, (r + 2 * shift) % ray_count) for r in range(ray_count)]
        return lax.ppermute(array, "ray", pairs)

    mine = own_quarter(group, up_weight, down_weight, part)
    arrivals = [along(mine, -shift) for shift in range(1, depth)]
    rendered = render(
        ray_count, True, me, block_owner, tile_lists, opacity, tile_counts.reshape(1, rows),
        ray_pixel, gaussian_features,
    )
    half = depth // 2
    low = pack(arrivals[:half - 1], rendered[0])
    x_low, y_low = beside(low, 1), beside(low, 2)
    high = pack(arrivals[half - 1:], low)
    high = tie(high, x_low, y_low)
    x_high, y_high = beside(high, 1), beside(high, 2)
    targets = [rendered[0]] + [along(rendered[shift], shift) for shift in range(1, depth)]
    tokens, normed, normed_t = prepare_tokens(
        ray_count, True, me, block_owner, ray_pixel, image_tokens,
        layer_norm_gain.reshape(1, width),
    )
    most = pack(
        [own_rows(group, up_weight, down_weight), low, x_low, y_low, high, x_high, y_high],
        targets[half],
    )
    most_other = partner(most)
    d_low, d_high = beside(y_low, 1), beside(x_high, 2)
    act_most, slope_most, mixed = forward(normed_t, [most], [most_other])
    late = [target for shift, target in enumerate(targets) if shift not in (0, half)]
    last = pack([d_low, d_high], mixed, *late)
    last_other = partner(last)
    act_last, slope_last, back, back_t, small = forward(
        normed_t, [last], [last_other], mixed,
        (tokens, layer_scale.reshape(1, width), *targets, partner(seconds(targets))),
    )
    acts, slopes = (act_most, act_last), (slope_most, slope_last)
    weights = ((most, last), (most_other, last_other))
    count, rest = half - 1, depth - half
    start = 4 + 3 * count
    pieces = tuple(
        ((0, q, 1), (0, 4 + q * count, count), (0, start + q * rest, rest)) for q in range(3)
    ) + (((0, 3, 1), (1, 0, depth - 1)),)
    gain = jnp.zeros((1, width), F32)
    (down_other,) = down_gradient(1, pieces, depth, acts, back)
    down_arrived = partner(down_other)
    up_other, gain = up_gradient(
        1, pieces, pieces, depth, weights[1], slopes, back_t, normed, gain
    )
    up_arrived = partner(up_other)
    down_sums = down_gradient(0, pieces, depth, acts, back, down_arrived)
    *up_sums, vector = up_gradient(
        0, pieces, pieces, depth, weights[0], slopes, back_t, normed, gain,
        (up_arrived, layer_norm_gain.reshape(1, width), small),
    )
    vector = vector + partner(vector)

    def first_step(to_x, to_y, x_later, y_later, *after):
        from_x, from_y = beside(to_x, 1), beside(to_y, 2)
        return from_x, from_y, merge(from_x, from_y, x_later, y_later, *after)

    def second_step(later):
        return beside(later[0], 1), beside(later[1], 2)

    def arrive_along(shares):
        return [shares[0]] + [along(shares[shift], shift) for shift in range(1, depth)]

    own, *rest = down_sums
    own_up, to_x, to_y, *rest_up = up_sums
    from_x, from_y, later = first_step(*rest, vector)
    late = second_step(later)
    shares = totals(own, from_x, from_y, *late)
    (down_total,) = collect(arrive_along(shares))
    down_x, down_y = beside(down_total, 1), beside(down_total, 2)
    vector = vector + partner(vector, 2)
    to_x, to_y = tie(to_x, *later), tie(to_y, *later)
    from_x, from_y, later = first_step(to_x, to_y, *rest_up, vector)
    flip = 4
    while flip < ray_count:
        vector = vector + partner(vector, flip)
        flip *= 2
    shares = totals(own_up, from_x, from_y, *second_step(later), vector)
    short, long = collect(arrive_along(shares), vector, down_total, (down_x, down_y))
    up_x, up_y, both = beside(short, 1), beside(short, 2), beside(long, 3)
    grad_up, grad_down, gain, scale, loss = place_quarters(
        group, (short, up_x, up_y, both), (down_total, down_x, down_y, both), part,
        rows * ray_count * group_count,
    )
    return (grad_up, grad_down, gain.reshape(width), scale.reshape(width), loss.reshape(()))


def shards(*operands):
    ray_count, group_count = lax.axis_size("ray"), lax.axis_size("grp")
    hidden = operands[-1].shape[0]
    square = group_count == 4 and ray_count in (8, 16) and hidden % (16 * group_count) == 0
    return (shards_square if square else shards_general)(*operands)


def solution(mesh):
    return jax.shard_map(
        shards,
        mesh=mesh,
        in_specs=(
            P(("grp", "ray"), None),
            P(None, ("grp", "ray")),
            P(None, ("grp", "ray")),
            P(("grp", "ray")),
            P("grp", None),
            P("grp", None),
            P(("grp", "ray"), None),
            P(),
            P(),
            P(None, "ray"),
            P("ray", None),
        ),
        out_specs=(P(None, "ray"), P("ray", None), P(), P(), P()),
        check_vma=False,
    )
```

```python
import functools

import jax
import jax.numpy as jnp
from jax import lax
from jax.experimental import pallas as pl
from jax.experimental.pallas import tpu as pltpu
from jax.sharding import PartitionSpec as P

STABILITY_EPSILON = 1e-06
F32 = jnp.float32
BF16 = jnp.bfloat16
MIB = 1024 * 1024
COST = pl.CostEstimate(flops=1 << 20, bytes_accessed=1 << 16, transcendentals=0)
LONG = pl.CostEstimate(flops=10**10, bytes_accessed=1 << 20, transcendentals=0)
SMEM = pl.BlockSpec(memory_space=pltpu.SMEM)
VMEM = pl.BlockSpec(memory_space=pltpu.VMEM)
ANY = pl.BlockSpec(memory_space=pl.ANY)


def params(mib=48, **more):
    return pltpu.CompilerParams(vmem_limit_bytes=mib * MIB, **more)


def dot_nn(a, b):
    return lax.dot_general(a, b, (((1,), (0,)), ((), ())), preferred_element_type=F32)


def dot_tn(a, b):
    return lax.dot_general(a, b, (((0,), (0,)), ((), ())), preferred_element_type=F32)


def dot_nt(a, b):
    return lax.dot_general(a, b, (((1,), (1,)), ((), ())), preferred_element_type=F32)


def owner_of(pixels, owner_ref, rows, count):
    block = lax.div(pixels, jnp.int32(rows))
    owner = jnp.zeros_like(pixels)
    for slot in range(count):
        owner = jnp.where(block == slot, owner_ref[0:1, slot:slot + 1], owner)
    return owner


def earlier(rows):
    before = lax.broadcasted_iota(jnp.int32, (rows, rows), 0)
    after = lax.broadcasted_iota(jnp.int32, (rows, rows), 1)
    return jnp.where(before < after, 1.0, 0.0).astype(BF16)


HBM = pl.BlockSpec(memory_space=pltpu.HBM)


def fetch(copies, sems):
    started = [
        pltpu.make_async_copy(source, target, sems.at[index])
        for index, (source, target) in enumerate(copies)
    ]
    for copy in started:
        copy.start()

    def wait(*numbers):
        for number in numbers:
            started[number].wait()

    return wait


def render_kernel(
    ray_count, relative, me_ref, owner_hbm, lists_hbm, opacity_hbm, counts_hbm, pixels_hbm,
    features_hbm, *refs,
):
    outs = refs[:-10]
    owner_ref, ids_ref, opacity_ref, counts_ref, mine_ref, features_ref = refs[-10:-4]
    share_ref, table_ref, send_ref, sems = refs[-4:]
    depth, rays = lists_hbm.shape
    gauss = features_hbm.shape[0]
    width = features_hbm.shape[1]
    me = me_ref[0]
    own_pixels = pixels_hbm.at[:, pl.ds(pl.multiple_of(me * rays, rays), rays)]
    wait = fetch(
        [
            (lists_hbm, ids_ref), (opacity_hbm, opacity_ref), (counts_hbm, counts_ref),
            (owner_hbm, owner_ref), (own_pixels, mine_ref), (features_hbm, features_ref),
        ],
        sems,
    )
    wait(0, 1, 2)
    ids_ref[...] = ids_ref[...] - me * gauss
    passing = jnp.ones((1, rays), F32)
    counts = counts_ref[...]
    for level in range(depth):
        alpha = opacity_ref[pl.ds(level, 1), :]
        share_ref[pl.ds(level, 1), :] = jnp.where(level < counts, alpha * passing, 0.0)
        passing = passing * (1.0 - alpha)

    tile = 256
    lanes = 128
    columns = rays // lanes

    @pl.loop(0, (gauss // tile) * columns)
    def _(step):
        first = pl.multiple_of(lax.div(step, columns) * tile, tile)
        lane = pl.multiple_of(lax.rem(step, columns) * lanes, lanes)
        number = (lax.broadcasted_iota(jnp.int32, (tile, lanes), 0) + first).astype(jnp.int16)
        total = jnp.zeros((tile, lanes), BF16)
        for level in range(depth):
            ident = jnp.broadcast_to(ids_ref[pl.ds(level, 1), pl.ds(lane, lanes)], (16, lanes))
            share = jnp.broadcast_to(share_ref[pl.ds(level, 1), pl.ds(lane, lanes)], (16, lanes))
            ident = jnp.concatenate([ident.astype(jnp.int16)] * (tile // 16), axis=0)
            share = jnp.concatenate([share.astype(BF16)] * (tile // 16), axis=0)
            total = total + jnp.where(ident == number, share, jnp.zeros_like(share))
        table_ref[pl.ds(first, tile), pl.ds(lane, lanes)] = total

    wait(3, 4, 5)
    owner = owner_of(mine_ref[...], owner_ref, rays, ray_count)
    padded = -(-ray_count // 16) * 16
    member = (lax.broadcasted_iota(jnp.int32, (padded, rays), 0) == owner)
    ranks = dot_nn(member.astype(F32).astype(BF16), earlier(rays))
    rank = jnp.sum(jnp.where(member, ranks, 0.0), axis=0, keepdims=True).astype(jnp.int32)
    if relative:
        chips = ray_count // 2
        shift = lax.div(owner, jnp.int32(2)) - lax.div(me, jnp.int32(2))
        shift = jnp.where(shift < 0, shift + chips, shift)
        flip = jnp.where(lax.rem(owner, jnp.int32(2)) == lax.rem(me, jnp.int32(2)), 0, 1)
        block = 2 * shift + flip
    else:
        block = owner
    slot = block * (rays // ray_count) + rank
    send_ref[...] = (
        (lax.broadcasted_iota(jnp.int32, (rays, rays), 0) == slot).astype(F32).astype(BF16)
    )

    piece = 256
    span = rays // len(outs)

    @pl.loop(0, width // piece)
    def _(step):
        cols = pl.ds(pl.multiple_of(step * piece, piece), piece)
        rendered = dot_tn(table_ref[...], features_ref[:, cols]).astype(BF16)
        ordered = dot_nn(send_ref[...], rendered).astype(BF16)
        for index, out in enumerate(outs):
            rows = ordered[index * span:(index + 1) * span]
            out[:, :, cols] = rows.reshape(*out.shape[:2], piece)


def render(ray_count, relative, me, owner, lists, opacity, counts, pixels, features):
    depth, rays = lists.shape
    gauss, width = features.shape
    parts = ray_count // 2 if relative else 1
    shape = jax.ShapeDtypeStruct((ray_count // parts, rays // ray_count, width), BF16)
    return pl.pallas_call(
        functools.partial(render_kernel, ray_count, relative),
        out_shape=(shape,) * parts,
        in_specs=[SMEM] + [HBM] * 6,
        out_specs=(VMEM,) * parts,
        scratch_shapes=[
            pltpu.VMEM(owner.shape, jnp.int32),
            pltpu.VMEM((depth, rays), jnp.int32),
            pltpu.VMEM((depth, rays), F32),
            pltpu.VMEM((1, rays), jnp.int32),
            pltpu.VMEM((1, rays), jnp.int32),
            pltpu.VMEM((gauss, width), BF16),
            pltpu.VMEM((depth, rays), F32),
            pltpu.VMEM((gauss, rays), BF16),
            pltpu.VMEM((rays, rays), BF16),
            pltpu.SemaphoreType.DMA((6,)),
        ],
        compiler_params=params(20),
        cost_estimate=COST,
        name="render",
    )(me, owner, lists, opacity, counts, pixels, features)


def tokens_kernel(
    ray_count, relative, me_ref, owner_hbm, pixels_hbm, tokens_hbm, gain_hbm,
    *refs,
):
    tokens_out, normed_out, normed_t_out = refs[-11:-8]
    owner_ref, pixels_ref, tokens_ref, gain_ref, order_ref, rank_ref, place_ref, sems = refs[-8:]
    rows, width = tokens_hbm.shape
    me = me_ref[0]
    each = rows // ray_count
    wait = fetch(
        [
            (owner_hbm, owner_ref), (pixels_hbm, pixels_ref), (gain_hbm, gain_ref),
            (tokens_hbm, tokens_ref),
        ],
        sems,
    )
    wait(0, 1)
    pixels = jnp.concatenate(
        [pixels_ref[:, sender * rows:(sender + 1) * rows] for sender in range(ray_count)], axis=0
    )
    mine = owner_of(pixels, owner_ref, rows, ray_count) == me
    place_ref[...] = lax.rem(pixels, jnp.int32(rows)).astype(F32)
    member = jnp.where(mine, 1.0, 0.0)
    padded = -(-ray_count // 16) * 16
    if padded > ray_count:
        spread = jnp.concatenate([member, jnp.zeros((padded - ray_count, rows), F32)], axis=0)
    else:
        spread = member
    ranks = dot_nn(spread.astype(BF16), earlier(rows))
    rank_ref[...] = jnp.where(mine, ranks[:ray_count], -1.0)
    chips = ray_count // 2
    for index in range(ray_count):
        if relative:
            chip = lax.rem(lax.div(me, jnp.int32(2)) + (chips - index // 2), jnp.int32(chips))
            sender = 2 * chip + jnp.bitwise_xor(lax.rem(me, jnp.int32(2)), index % 2)
        else:
            sender = index
        rank = rank_ref[pl.ds(sender, 1), :].astype(jnp.int32)
        hit = lax.broadcasted_iota(jnp.int32, (each, rows), 0) == rank
        at = jnp.sum(
            jnp.where(hit, place_ref[pl.ds(sender, 1), :], 0.0), axis=1, keepdims=True
        )
        here = lax.broadcasted_iota(jnp.int32, (each, rows), 1) == at.astype(jnp.int32)
        order_ref[pl.ds(index * each, each), :] = here.astype(F32).astype(BF16)
    wait(2, 3)
    half = min(128, rows)
    gain = gain_ref[...]

    @pl.loop(0, rows // half)
    def _(step):
        span = pl.ds(pl.multiple_of(step * half, half), half)
        values = dot_nn(order_ref[span, :], tokens_ref[...])
        tokens_out[span, :] = values.astype(BF16)
        centered = values - jnp.mean(values, axis=-1, keepdims=True)
        variance = jnp.mean(centered * centered, axis=-1, keepdims=True)
        xhat = centered * lax.rsqrt(variance + STABILITY_EPSILON)
        normed = (xhat * gain).astype(BF16)
        normed_out[span, :] = normed
        normed_t_out[:, span] = normed.T


def prepare_tokens(ray_count, relative, me, owner, pixels, tokens, gain, after=()):
    rows, width = tokens.shape
    return pl.pallas_call(
        functools.partial(tokens_kernel, ray_count, relative),
        out_shape=(
            jax.ShapeDtypeStruct((rows, width), BF16),
            jax.ShapeDtypeStruct((rows, width), BF16),
            jax.ShapeDtypeStruct((width, rows), BF16),
        ),
        in_specs=[SMEM] + [HBM] * 4 + [ANY] * len(after),
        out_specs=(VMEM, VMEM, VMEM),
        scratch_shapes=[
            pltpu.VMEM(owner.shape, jnp.int32),
            pltpu.VMEM(pixels.shape, jnp.int32),
            pltpu.VMEM((rows, width), BF16),
            pltpu.VMEM((1, width), F32),
            pltpu.VMEM((rows, rows), BF16),
            pltpu.VMEM((ray_count, rows), F32),
            pltpu.VMEM((ray_count, rows), F32),
            pltpu.SemaphoreType.DMA((4,)),
        ],
        compiler_params=params(20),
        cost_estimate=COST,
        name="tokens",
    )(me, owner, pixels, tokens, gain, *after)


def up_kernel(normed_ref, up_ref, act_ref, slope_ref):
    parts, _, part_rows, width = up_ref.shape
    up = up_ref[...].reshape(parts * part_rows, width)
    rows = normed_ref.shape[0]
    piece = min(128, rows)

    @pl.loop(0, rows // piece)
    def _(step):
        span = pl.ds(pl.multiple_of(step * piece, piece), piece)
        hidden = dot_nn(normed_ref[span, :], up)
        phi = 0.5 * (1.0 + lax.erf(hidden * (0.5 ** 0.5)))
        density = jnp.exp(-0.5 * hidden * hidden) * ((2.0 * jnp.pi) ** -0.5)
        act_ref[span, :] = (hidden * phi).astype(BF16)
        slope_ref[span, :] = (phi + hidden * density).astype(slope_ref.dtype)


def project_up(normed, up):
    rows, width = normed.shape
    parts, chunks, part_rows, chunk = up.shape
    return pl.pallas_call(
        up_kernel,
        grid=(chunks,),
        out_shape=(
            jax.ShapeDtypeStruct((rows, chunks * chunk), BF16),
            jax.ShapeDtypeStruct((rows, chunks * chunk), F32),
        ),
        in_specs=[
            pl.BlockSpec((rows, width), lambda j: (0, 0)),
            pl.BlockSpec((parts, 1, part_rows, chunk), lambda j: (0, j, 0, 0)),
        ],
        out_specs=(
            pl.BlockSpec((rows, chunk), lambda j: (0, j)),
            pl.BlockSpec((rows, chunk), lambda j: (0, j)),
        ),
        compiler_params=params(dimension_semantics=("arbitrary",)),
        cost_estimate=COST,
        name="up",
    )(normed, up)


def down_kernel(
    chunks, act_ref, down_ref, tokens_ref, target_ref, scale_ref,
    grad_ref, back_ref, small_ref, mixed_ref,
):
    step = pl.program_id(0)
    rows, width = tokens_ref.shape
    act = act_ref[...]

    @pl.when(step < chunks)
    def _():
        parts, _, part_rows, _ = down_ref.shape
        part = dot_nn(act, down_ref[...].reshape(parts * part_rows, width))

        @pl.when(step == 0)
        def _():
            mixed_ref[...] = part

        @pl.when(step > 0)
        def _():
            mixed_ref[...] += part

    @pl.when(step == chunks - 1)
    def _():
        scale = scale_ref[...]
        small_ref[...] = jnp.zeros_like(small_ref)
        piece = min(64, rows)

        @pl.loop(0, rows // piece)
        def _(index):
            span = pl.ds(pl.multiple_of(index * piece, piece), piece)
            mixed = mixed_ref[span, :]
            out = tokens_ref[span, :].astype(F32) + scale * mixed
            goal = target_ref[span, :].astype(F32)
            out_norm = jnp.sqrt(jnp.sum(out * out, axis=-1, keepdims=True) + STABILITY_EPSILON)
            goal_norm = jnp.sqrt(jnp.sum(goal * goal, axis=-1, keepdims=True) + STABILITY_EPSILON)
            norms = out_norm * goal_norm
            cosine = jnp.sum(out * goal, axis=-1, keepdims=True) / norms
            upstream = (cosine / (out_norm * out_norm)) * out - goal * (1.0 / norms)
            back_ref[span, :] = (upstream * scale).astype(BF16)
            small_ref[0:1, :] += jnp.sum(upstream * mixed, axis=0, keepdims=True)
            loss = jnp.sum(1.0 - cosine, axis=0, keepdims=True)
            small_ref[1:2, :] += jnp.broadcast_to(loss, (1, width))

    @pl.when(step >= chunks)
    def _():
        grad = dot_tn(act, back_ref[...])
        grad_ref[...] = grad.astype(BF16).reshape(grad_ref.shape)


def project_down(act, down, tokens, target, scale):
    rows, width = tokens.shape
    parts, chunks, part_rows, _ = down.shape
    chunk = parts * part_rows
    return pl.pallas_call(
        functools.partial(down_kernel, chunks),
        grid=(2 * chunks,),
        out_shape=(
            jax.ShapeDtypeStruct(down.shape, BF16),
            jax.ShapeDtypeStruct((rows, width), BF16),
            jax.ShapeDtypeStruct((8, width), F32),
        ),
        in_specs=[
            pl.BlockSpec((rows, chunk), lambda j: (0, lax.rem(j, chunks))),
            pl.BlockSpec(
                (parts, 1, part_rows, width), lambda j: (0, jnp.minimum(j, chunks - 1), 0, 0)
            ),
            pl.BlockSpec((rows, width), lambda j: (0, 0)),
            pl.BlockSpec((rows, width), lambda j: (0, 0)),
            pl.BlockSpec((1, width), lambda j: (0, 0)),
        ],
        out_specs=(
            pl.BlockSpec(
                (parts, 1, part_rows, width), lambda j: (0, jnp.maximum(j - chunks, 0), 0, 0)
            ),
            pl.BlockSpec((rows, width), lambda j: (0, 0)),
            pl.BlockSpec((8, width), lambda j: (0, 0)),
        ),
        scratch_shapes=[pltpu.VMEM((rows, width), F32)],
        compiler_params=params(dimension_semantics=("arbitrary",)),
        cost_estimate=COST,
        name="down",
    )(act, down, tokens, target, scale)


def back_kernel(back_ref, down_ref, slope_ref, normed_t_ref, up_ref, gain_ref, grad_ref, sum_ref):
    step = pl.program_id(0)
    parts, _, part_rows, width = down_ref.shape
    chunk = parts * part_rows
    rows = back_ref.shape[0]
    back_act = dot_nt(back_ref[...], down_ref[...].reshape(chunk, width))
    back_hidden = (back_act * slope_ref[...]).astype(BF16)
    up_parts, _, up_rows, _ = up_ref.shape

    @pl.when(step == 0)
    def _():
        sum_ref[...] = jnp.zeros_like(sum_ref)

    grad = dot_nn(normed_t_ref[...], back_hidden)
    grad_ref[...] = grad.astype(BF16).reshape(grad_ref.shape)
    up = up_ref[...].reshape(up_parts * up_rows, chunk).astype(F32)
    sum_ref[...] += jnp.sum(grad * up, axis=1, keepdims=True) / gain_ref[...]


def back_up(back, down, slope, normed_t, up, gain):
    width, rows = normed_t.shape
    parts, chunks, part_rows, _ = down.shape
    chunk = parts * part_rows
    up_parts, _, up_rows, _ = up.shape
    return pl.pallas_call(
        back_kernel,
        grid=(chunks,),
        out_shape=(
            jax.ShapeDtypeStruct(up.shape, BF16),
            jax.ShapeDtypeStruct((width, 1), F32),
        ),
        in_specs=[
            pl.BlockSpec((rows, width), lambda j: (0, 0)),
            pl.BlockSpec((parts, 1, part_rows, width), lambda j: (0, j, 0, 0)),
            pl.BlockSpec((rows, chunk), lambda j: (0, j)),
            pl.BlockSpec((width, rows), lambda j: (0, 0)),
            pl.BlockSpec((up_parts, 1, up_rows, chunk), lambda j: (0, j, 0, 0)),
            pl.BlockSpec((width, 1), lambda j: (0, 0)),
        ],
        out_specs=(
            pl.BlockSpec((up_parts, 1, up_rows, chunk), lambda j: (0, j, 0, 0)),
            pl.BlockSpec((width, 1), lambda j: (0, 0)),
        ),
        compiler_params=params(dimension_semantics=("arbitrary",)),
        cost_estimate=COST,
        name="back",
    )(back, down, slope, normed_t, up, gain)


def gather_weight(weight, parts, group, group_count, ray_count):
    rows, cols = weight.shape
    if parts == 1:
        whole = lax.all_gather(weight, "ray", axis=0, tiled=True)
    else:
        part = lax.dynamic_slice_in_dim(weight, group * (rows // parts), rows // parts, 0)
        whole = lax.all_gather(part, ("grp", "ray"), axis=0, tiled=True)
    return whole.reshape(parts, ray_count, rows // parts, cols)


def reduce_gradient(grad):
    parts, ray_count, part_rows, cols = grad.shape
    flat = grad.reshape(parts * ray_count * part_rows, cols)
    if parts == 1:
        share = lax.psum_scatter(flat, "ray", scatter_dimension=0, tiled=True)
        return lax.psum(share.astype(F32), "grp")
    share = lax.psum_scatter(flat, "grp", scatter_dimension=0, tiled=True)
    share = lax.psum_scatter(share, "ray", scatter_dimension=0, tiled=True)
    return lax.all_gather(share, "grp", axis=0, tiled=True).astype(F32)


def shards_general(
    image_tokens,
    tile_lists,
    opacity,
    tile_counts,
    ray_pixel,
    block_owner,
    gaussian_features,
    layer_norm_gain,
    layer_scale,
    up_weight,
    down_weight,
):
    ray_count = lax.axis_size("ray")
    group_count = lax.axis_size("grp")
    group = lax.axis_index("grp")
    me = lax.axis_index("ray").reshape(1)
    rows, width = image_tokens.shape
    up_parts = group_count if up_weight.shape[0] % (16 * group_count) == 0 else 1
    down_parts = group_count if down_weight.shape[0] % (16 * group_count) == 0 else 1
    up = gather_weight(up_weight, up_parts, group, group_count, ray_count)
    down = gather_weight(down_weight, down_parts, group, group_count, ray_count)
    rendered = render(
        ray_count, False, me, block_owner, tile_lists, opacity, tile_counts.reshape(1, rows),
        ray_pixel, gaussian_features,
    )
    rendered = rendered[0].reshape(rows, width)
    target = lax.all_to_all(rendered, "ray", split_axis=0, concat_axis=0, tiled=True)
    tokens, normed, normed_t = prepare_tokens(
        ray_count, False, me, block_owner, ray_pixel, image_tokens,
        layer_norm_gain.reshape(1, width),
    )
    act, slope = project_up(normed, up)
    grad_down, back, small = project_down(act, down, tokens, target, layer_scale.reshape(1, width))
    grad_up, gain_sum = back_up(back, down, slope, normed_t, up, layer_norm_gain.reshape(width, 1))
    grad_down = reduce_gradient(grad_down)
    grad_up = reduce_gradient(grad_up)
    sums = jnp.concatenate([gain_sum.reshape(1, width), small[:2]], axis=0)
    sums = lax.psum(sums, ("grp", "ray"))
    loss = sums[2, 0] / (rows * ray_count * group_count)
    return (grad_up, grad_down, sums[0], sums[1], loss)


def quarter_kernel(group_ref, up_hbm, down_hbm, out_ref, up_ref, turned_ref, sems):
    part = out_ref.shape[1]
    lanes = up_ref.shape[1]
    start = pl.multiple_of(group_ref[0] * part, part)
    lane = pl.multiple_of(lax.div(start, jnp.int32(lanes)) * lanes, lanes)
    wait = fetch(
        [
            (up_hbm.at[:, pl.ds(lane, lanes)], up_ref),
            (down_hbm.at[pl.ds(start, part), :], out_ref.at[1]),
        ],
        sems,
    )
    wait(0)
    turned_ref[...] = up_ref[...].T
    out_ref[0] = turned_ref[pl.ds(pl.multiple_of(start - lane, part), part), :]
    wait(1)


def own_quarter(group, up, down, part):
    width, chunk = up.shape
    lanes = max(128, part)
    return pl.pallas_call(
        quarter_kernel,
        out_shape=jax.ShapeDtypeStruct((2, part, width), BF16),
        in_specs=[SMEM, HBM, HBM],
        out_specs=VMEM,
        scratch_shapes=[
            pltpu.VMEM((width, lanes), BF16),
            pltpu.VMEM((lanes, width), BF16),
            pltpu.SemaphoreType.DMA((2,)),
        ],
        compiler_params=params(16),
        cost_estimate=LONG,
        name="quarter",
    )(group, up, down)


def own_rows_kernel(group_ref, up_ref, down_ref, out_ref, turned_ref):
    part = out_ref.shape[2]
    turned_ref[...] = up_ref[...].T
    for index in range(4):
        quarter = jnp.bitwise_xor(group_ref[0], index)
        span = pl.ds(pl.multiple_of(quarter * part, part), part)
        out_ref[index, 0] = turned_ref[span, :]
        out_ref[index, 1] = down_ref[span, :]


def own_rows(group, up, down):
    width, chunk = up.shape
    return pl.pallas_call(
        own_rows_kernel,
        out_shape=jax.ShapeDtypeStruct((4, 2, chunk // 4, width), BF16),
        in_specs=[SMEM, VMEM, VMEM],
        out_specs=VMEM,
        scratch_shapes=[pltpu.VMEM((chunk, width), BF16)],
        compiler_params=params(16),
        cost_estimate=COST,
        name="own_rows",
    )(group, up, down)


def finish_rows(tokens, mixed, goal, scale):
    out = tokens + scale * mixed
    out_norm = jnp.sqrt(jnp.sum(out * out, axis=-1, keepdims=True) + STABILITY_EPSILON)
    goal_norm = jnp.sqrt(jnp.sum(goal * goal, axis=-1, keepdims=True) + STABILITY_EPSILON)
    norms = out_norm * goal_norm
    cosine = jnp.sum(out * goal, axis=-1, keepdims=True) / norms
    upstream = (cosine / (out_norm * out_norm)) * out - goal * (1.0 / norms)
    return upstream, 1.0 - cosine


def forward_kernel(first, blocks, sides, skipped, *refs):
    last = blocks > 0
    refs = list(refs[skipped:])
    normed_t_ref = refs.pop(0)
    own, other = refs[:sides], refs[sides:2 * sides]
    del refs[:2 * sides]
    mixed_in = None if first else refs.pop(0)
    if last:
        tokens_ref, scale_ref = refs[:2]
        targets, passed_ref = refs[2:2 + blocks], refs[2 + blocks]
        del refs[:3 + blocks]
    act_ref, slope_ref = refs[:2]
    del refs[:2]
    width, rows = normed_t_ref.shape
    part = act_ref.shape[2]
    part_sum = None
    downs = []
    for side, group in enumerate((own, other)):
        start = 0
        for ref in group:
            count = ref.shape[0]
            hiddens = dot_nn(ref[:, 0].reshape(count * part, width), normed_t_ref[...])
            for index in range(count):
                hidden = hiddens[index * part:(index + 1) * part]
                phi = 0.5 * (1.0 + lax.erf(hidden * (0.5 ** 0.5)))
                density = jnp.exp(-0.5 * hidden * hidden) * ((2.0 * jnp.pi) ** -0.5)
                act_ref[side, start + index] = (hidden * phi).astype(BF16)
                slope_ref[side, start + index] = phi + hidden * density
            downs.append(ref[:, 1].reshape(count * part, width))
            start += count
    if sides > 1 or last:
        act = act_ref[...].reshape(2 * start * part, rows)
        part_sum = dot_tn(act, jnp.concatenate(downs, axis=0))
    else:
        for side, down in enumerate(downs):
            term = dot_tn(act_ref[side].reshape(start * part, rows), down)
            part_sum = term if part_sum is None else part_sum + term
    if not last:
        mixed_out = refs[0]
        mixed_out[...] = part_sum if first else mixed_in[...] + part_sum
        return
    back_ref, back_t_ref, small_ref, mixed_ref = refs
    mixed_ref[...] = mixed_in[...] + part_sum
    scale = scale_ref[...]
    small_ref[...] = jnp.zeros_like(small_ref)
    piece = rows // blocks
    for index, target_ref in enumerate(targets):
        span = pl.ds(index * piece, piece)
        mixed = mixed_ref[span, :]
        goal = jnp.concatenate([target_ref[0], passed_ref[index]], axis=0).astype(F32)
        upstream, loss = finish_rows(tokens_ref[span, :].astype(F32), mixed, goal, scale)
        back = (upstream * scale).astype(BF16)
        back_ref[span, :] = back
        back_t_ref[:, span] = back.T
        small_ref[0:1, :] += jnp.sum(upstream * mixed, axis=0, keepdims=True)
        small_ref[1:2, :] += jnp.broadcast_to(jnp.sum(loss, axis=0, keepdims=True), (1, width))


def forward(normed_t, own, other, mixed=None, finish=None, after=()):
    width, rows = normed_t.shape
    part = own[0].shape[2]
    total = sum(array.shape[0] for array in own)
    first, last = mixed is None, finish is not None
    blocks = len(finish) - 3 if last else 0
    operands = [*after, normed_t, *own, *other]
    if not first:
        operands.append(mixed)
    if last:
        operands.extend(finish)
    piece = (2, total, part, rows)
    shapes = [jax.ShapeDtypeStruct(piece, BF16), jax.ShapeDtypeStruct(piece, F32)]
    scratch = []
    if last:
        shapes += [
            jax.ShapeDtypeStruct((rows, width), BF16),
            jax.ShapeDtypeStruct((width, rows), BF16),
            jax.ShapeDtypeStruct((8, width), F32),
        ]
        scratch = [pltpu.VMEM((rows, width), F32)]
    else:
        shapes += [jax.ShapeDtypeStruct((rows, width), F32)]
    return pl.pallas_call(
        functools.partial(forward_kernel, first, blocks, len(own), len(after)),
        out_shape=tuple(shapes),
        in_specs=[ANY] * len(after) + [VMEM] * (len(operands) - len(after)),
        out_specs=tuple([VMEM] * len(shapes)),
        scratch_shapes=scratch,
        compiler_params=params(32),
        cost_estimate=COST,
        name="forward",
    )(*operands)


def pack_kernel(counts, *refs):
    out_ref = refs[-1]
    start = 0
    for count, ref in zip(counts, refs):
        out_ref[start:start + count] = ref[...].reshape(count, *out_ref.shape[1:])
        start += count


def pack(pieces, *after):
    counts = [1 if piece.ndim == 3 else piece.shape[0] for piece in pieces]
    return pl.pallas_call(
        functools.partial(pack_kernel, counts),
        out_shape=jax.ShapeDtypeStruct((sum(counts), *pieces[0].shape[-3:]), BF16),
        in_specs=[VMEM] * len(pieces) + [ANY] * len(after),
        out_specs=VMEM,
        compiler_params=params(16),
        cost_estimate=COST,
        name="pack",
    )(*pieces, *after)


def turn_kernel(y_ref, x_ref, a_ref, b_ref):
    count = a_ref.shape[0]
    a_ref[...] = y_ref[:count]
    b_ref[...] = x_ref[count:]


def turn(y, x):
    count = y.shape[0]
    first = count // 2
    return pl.pallas_call(
        turn_kernel,
        out_shape=(
            jax.ShapeDtypeStruct((first, *y.shape[1:]), BF16),
            jax.ShapeDtypeStruct((count - first, *y.shape[1:]), BF16),
        ),
        in_specs=[VMEM] * 2,
        out_specs=(VMEM, VMEM),
        compiler_params=params(16),
        cost_estimate=COST,
        name="turn",
    )(y, x)


def tie_kernel(*refs):
    pass


def tie(array, *after):
    return pl.pallas_call(
        tie_kernel,
        out_shape=jax.ShapeDtypeStruct(array.shape, array.dtype),
        in_specs=[ANY] * (1 + len(after)),
        out_specs=ANY,
        input_output_aliases={0: 0},
        compiler_params=params(4),
        cost_estimate=COST,
        name="tie",
    )(array, *after)


def seconds_kernel(*refs):
    for index, ref in enumerate(refs[:-1]):
        refs[-1][index] = ref[1]


def seconds(blocks):
    count, (_, each, width) = len(blocks), blocks[0].shape
    return pl.pallas_call(
        seconds_kernel,
        out_shape=jax.ShapeDtypeStruct((count, each, width), BF16),
        in_specs=[VMEM] * count,
        out_specs=VMEM,
        compiler_params=params(16),
        cost_estimate=COST,
        name="seconds",
    )(*blocks)


def joined(refs, pieces, pick):
    values = [pick(refs[which], start, count) for which, start, count in pieces]
    flat = [value.reshape(-1, value.shape[-1]) for value in values]
    return flat[0] if len(flat) == 1 else jnp.concatenate(flat, axis=0)


def put(quarter, value, outs):
    own_ref, x_ref, y_ref, x_later_ref, y_later_ref = outs
    value = value.astype(BF16).reshape(own_ref.shape)
    half = x_ref.shape[0] // 2
    if quarter == 0:
        own_ref[...] = value
    elif quarter == 1:
        x_ref[half:] = value[:half]
        x_later_ref[...] = value[half:]
    elif quarter == 2:
        y_ref[half:] = value[half:]
        y_later_ref[...] = value[:half]
    else:
        x_ref[:half] = value[:half]
        y_ref[:half] = value[half:]


def emit(quarter, value, arrived, outs):
    if arrived is None:
        outs[0][quarter] = value.astype(BF16).reshape(outs[0].shape[1:])
    else:
        put(quarter, value + arrived[quarter].reshape(value.shape).astype(F32), outs)


def down_grad_kernel(side, act_pieces, add, *refs):
    acts, back_ref = refs[:2], refs[2]
    arrived = refs[3] if add else None
    outs = refs[4:] if add else refs[3:]
    for quarter in (3, 1, 2, 0):
        act = joined(acts, act_pieces[quarter], lambda ref, a, n: ref[side, a:a + n])
        emit(quarter, dot_nn(act, back_ref[...]), arrived, outs)


def up_grad_kernel(side, weight_pieces, act_pieces, add, *refs):
    weights, slopes = refs[:2], refs[2:4]
    back_t_ref, normed_ref, gain_in = refs[4:7]
    if add:
        arrived, scale_ref, small_ref = refs[7:10]
        outs, vector_ref, gain_ref = refs[10:-2], refs[-2], refs[-1]
    else:
        arrived = None
        outs, gain_ref = refs[7:-1], refs[-1]
    gain_ref[...] = gain_in[...]
    for quarter in (3, 1, 2, 0):
        pieces = weight_pieces[quarter]
        slope = joined(slopes, act_pieces[quarter], lambda ref, a, n: ref[side, a:a + n])
        back_act = dot_nn(joined(weights, pieces, lambda ref, a, n: ref[a:a + n, 1]), back_t_ref[...])
        back_hidden = (back_act * slope).astype(BF16)
        grad = dot_nn(back_hidden, normed_ref[...])
        up = joined(weights, pieces, lambda ref, a, n: ref[a:a + n, 0]).astype(F32)
        gain_ref[...] += jnp.sum(grad * up, axis=0, keepdims=True)
        emit(quarter, grad, arrived, outs)
    if add:
        vector_ref[0:1, :] = gain_ref[...] / scale_ref[...]
        vector_ref[1:3, :] = small_ref[0:2, :]
        vector_ref[3:8, :] = jnp.zeros((5, gain_ref.shape[1]), F32)


def gradient_shapes(depth, part, width, add):
    if not add:
        return [jax.ShapeDtypeStruct((4, depth, part, width), BF16)]
    counts = (depth, depth, depth, depth - depth // 2, depth // 2)
    return [jax.ShapeDtypeStruct((count, part, width), BF16) for count in counts]


def down_gradient(side, act_pieces, depth, acts, back, arrived=None):
    part = acts[0].shape[2]
    width = back.shape[1]
    add = arrived is not None
    operands = [*acts, back] + ([arrived] if add else [])
    shapes = gradient_shapes(depth, part, width, add)
    return pl.pallas_call(
        functools.partial(down_grad_kernel, side, act_pieces, add),
        out_shape=tuple(shapes),
        in_specs=[VMEM] * len(operands),
        out_specs=tuple([VMEM] * len(shapes)),
        compiler_params=params(20),
        cost_estimate=COST,
        name="down_gradient",
    )(*operands)


def up_gradient(
    side, weight_pieces, act_pieces, depth, weights, slopes, back_t, normed, gain, extra=()
):
    part, width = weights[0].shape[2:]
    add = len(extra) > 0
    operands = [*weights, *slopes, back_t, normed, gain, *extra]
    shapes = gradient_shapes(depth, part, width, add)
    if add:
        shapes.append(jax.ShapeDtypeStruct((8, width), F32))
        scratch = [pltpu.VMEM((1, width), F32)]
    else:
        scratch = []
        shapes.append(jax.ShapeDtypeStruct((1, width), F32))
    return pl.pallas_call(
        functools.partial(up_grad_kernel, side, weight_pieces, act_pieces, add),
        out_shape=tuple(shapes),
        in_specs=[VMEM] * len(operands),
        out_specs=tuple([VMEM] * len(shapes)),
        scratch_shapes=scratch,
        compiler_params=params(24),
        cost_estimate=COST,
        name="up_gradient",
    )(*operands)


def merge_kernel(x_ref, y_ref, x_later_ref, y_later_ref, *refs):
    x_out, y_out = refs[-2:]
    half = y_later_ref.shape[0]
    x_out[...] = (x_later_ref[...].astype(F32) + y_ref[:half].astype(F32)).astype(BF16)
    y_out[...] = (y_later_ref[...].astype(F32) + x_ref[:half].astype(F32)).astype(BF16)


def merge(x, y, x_later, y_later, *after):
    return pl.pallas_call(
        merge_kernel,
        out_shape=tuple(jax.ShapeDtypeStruct(a.shape, BF16) for a in (x_later, y_later)),
        in_specs=[VMEM] * 4 + [ANY] * len(after),
        out_specs=(VMEM, VMEM),
        compiler_params=params(16),
        cost_estimate=COST,
        name="merge",
    )(x, y, x_later, y_later, *after)


def total_kernel(own_ref, x_ref, y_ref, x_late_ref, y_late_ref, *refs):
    outs = refs[-own_ref.shape[0]:]
    half = y_late_ref.shape[0]
    for index, out in enumerate(outs):
        total = own_ref[index].astype(F32)
        if index < half:
            total += x_ref[half + index].astype(F32) + y_late_ref[index].astype(F32)
        else:
            total += y_ref[index].astype(F32) + x_late_ref[index - half].astype(F32)
        out[...] = total.astype(BF16)


def totals(own, x, y, x_late, y_late, *after):
    count, part, width = own.shape
    return pl.pallas_call(
        total_kernel,
        out_shape=tuple([jax.ShapeDtypeStruct((part, width), BF16)] * count),
        in_specs=[VMEM] * 5 + [ANY] * len(after),
        out_specs=tuple([VMEM] * count),
        compiler_params=params(16),
        cost_estimate=COST,
        name="totals",
    )(own, x, y, x_late, y_late, *after)


def collect_kernel(count, *refs):
    total = refs[0][...].astype(F32)
    for ref in refs[1:count]:
        total = total + ref[...].astype(F32)
    refs[-1][...] = total.astype(BF16)


def collect(parts, *after):
    return pl.pallas_call(
        functools.partial(collect_kernel, len(parts)),
        out_shape=jax.ShapeDtypeStruct(parts[0].shape, BF16),
        in_specs=[VMEM] * len(parts) + [ANY] * len(after),
        out_specs=VMEM,
        compiler_params=params(16),
        cost_estimate=COST,
        name="collect",
    )(*parts, *after)


def join_kernel(total_ref, vector_ref, other_ref, *refs):
    short_ref, long_ref, held_ref = refs[-3:]
    part = total_ref.shape[0]
    short_ref[pl.ds(0, part), :] = total_ref[...]
    rest = vector_ref[0:3, :]
    held_ref[...] = jnp.zeros_like(held_ref)
    for index in range(3):
        piece = rest.astype(BF16).astype(F32)
        held_ref[3 * index:3 * index + 3, :] = piece
        rest = rest - piece
    short_ref[pl.ds(part, 16), :] = held_ref[...].astype(BF16)
    long_ref[pl.ds(0, part + 16), :] = short_ref[...]
    long_ref[pl.ds(part + 16, part), :] = other_ref[...]


def join(total, vector, other, *after):
    part, width = total.shape
    return pl.pallas_call(
        join_kernel,
        out_shape=tuple(
            jax.ShapeDtypeStruct((rows, width), BF16) for rows in (part + 16, 2 * part + 16)
        ),
        in_specs=[VMEM] * 3 + [ANY] * len(after),
        out_specs=(VMEM, VMEM),
        scratch_shapes=[pltpu.VMEM((16, width), F32)],
        compiler_params=params(16),
        cost_estimate=COST,
        name="join",
    )(total, vector, other, *after)


def place_kernel(part, tokens, group_ref, *refs):
    ups, downs = refs[:4], refs[4:8]
    up_ref, down_ref, gain_ref, scale_ref, loss_ref, held_ref = refs[8:]
    group = group_ref[0]
    vectors = []
    for index, (up, down) in enumerate(zip(ups, downs)):
        first = pl.multiple_of(jnp.bitwise_xor(group, index) * part, part)
        held_ref[pl.ds(first, part), :] = up[pl.ds(0, part), :].astype(F32)
        start = down.shape[0] - part
        down_ref[pl.ds(first, part), :] = down[pl.ds(start, part), :].astype(F32)
        rows = up[pl.ds(part, 16), :].astype(F32)
        vectors.append((rows[0:3] + rows[3:6]) + rows[6:9])
    up_ref[...] = held_ref[...].T
    vector = (vectors[0] + vectors[1]) + (vectors[2] + vectors[3])
    gain_ref[...] = vector[0:1]
    scale_ref[...] = vector[1:2]
    loss_ref[...] = vector[2:3, 0:1] * (1.0 / tokens)


def place_quarters(group, ups, downs, part, tokens):
    width = ups[0].shape[1]
    shapes = [
        jax.ShapeDtypeStruct((width, 4 * part), F32),
        jax.ShapeDtypeStruct((4 * part, width), F32),
        jax.ShapeDtypeStruct((1, width), F32),
        jax.ShapeDtypeStruct((1, width), F32),
        jax.ShapeDtypeStruct((1, 1), F32),
    ]
    return pl.pallas_call(
        functools.partial(place_kernel, part, tokens),
        out_shape=tuple(shapes),
        in_specs=[SMEM] + [VMEM] * 8,
        out_specs=tuple([VMEM] * len(shapes)),
        scratch_shapes=[pltpu.VMEM((4 * part, width), F32)],
        compiler_params=params(16),
        cost_estimate=COST,
        name="place",
    )(group, *ups, *downs)


def shards_square(
    image_tokens,
    tile_lists,
    opacity,
    tile_counts,
    ray_pixel,
    block_owner,
    gaussian_features,
    layer_norm_gain,
    layer_scale,
    up_weight,
    down_weight,
):
    ray_count = lax.axis_size("ray")
    group_count = lax.axis_size("grp")
    depth = ray_count // 2
    group = lax.axis_index("grp").reshape(1)
    me = lax.axis_index("ray").reshape(1)
    rows, width = image_tokens.shape
    part = down_weight.shape[0] // group_count

    def beside(array, flip):
        return lax.ppermute(array, "grp", [(g, g ^ flip) for g in range(group_count)])

    def partner(array, flip=1):
        return lax.ppermute(array, "ray", [(r, r ^ flip) for r in range(ray_count)])

    def along(array, shift):
        pairs = [(r, (r + 2 * shift) % ray_count) for r in range(ray_count)]
        return lax.ppermute(array, "ray", pairs)

    mine = own_quarter(group, up_weight, down_weight, part)
    arrivals = [along(mine, -shift) for shift in range(1, depth)]
    rendered = render(
        ray_count, True, me, block_owner, tile_lists, opacity, tile_counts.reshape(1, rows),
        ray_pixel, gaussian_features,
    )
    half = depth // 2
    low = pack(arrivals[:half - 1], rendered[0])
    x_low, y_low = beside(low, 1), beside(low, 2)
    high = pack(arrivals[half - 1:], low)
    high = tie(high, x_low, y_low)
    x_high, y_high = beside(high, 1), beside(high, 2)
    targets = [rendered[0]] + [along(rendered[shift], shift) for shift in range(1, depth)]
    tokens, normed, normed_t = prepare_tokens(
        ray_count, True, me, block_owner, ray_pixel, image_tokens,
        layer_norm_gain.reshape(1, width),
    )
    most = pack(
        [own_rows(group, up_weight, down_weight), low, x_low, y_low, high, x_high, y_high],
        targets[half],
    )
    most_other = partner(most)
    d_low, d_high = beside(y_low, 1), beside(x_high, 2)
    act_most, slope_most, mixed = forward(normed_t, [most], [most_other])
    late = [target for shift, target in enumerate(targets) if shift not in (0, half)]
    last = pack([d_low, d_high], mixed, *late)
    last_other = partner(last)
    act_last, slope_last, back, back_t, small = forward(
        normed_t, [last], [last_other], mixed,
        (tokens, layer_scale.reshape(1, width), *targets, partner(seconds(targets))),
    )
    acts, slopes = (act_most, act_last), (slope_most, slope_last)
    weights = ((most, last), (most_other, last_other))
    count, rest = half - 1, depth - half
    start = 4 + 3 * count
    pieces = tuple(
        ((0, q, 1), (0, 4 + q * count, count), (0, start + q * rest, rest)) for q in range(3)
    ) + (((0, 3, 1), (1, 0, depth - 1)),)
    gain = jnp.zeros((1, width), F32)
    (down_other,) = down_gradient(1, pieces, depth, acts, back)
    down_arrived = partner(down_other)
    up_other, gain = up_gradient(
        1, pieces, pieces, depth, weights[1], slopes, back_t, normed, gain
    )
    up_arrived = partner(up_other)
    down_sums = down_gradient(0, pieces, depth, acts, back, down_arrived)
    *up_sums, vector = up_gradient(
        0, pieces, pieces, depth, weights[0], slopes, back_t, normed, gain,
        (up_arrived, layer_norm_gain.reshape(1, width), small),
    )
    vector = vector + partner(vector)

    def first_step(to_x, to_y, x_later, y_later, *after):
        from_x, from_y = beside(to_x, 1), beside(to_y, 2)
        return from_x, from_y, merge(from_x, from_y, x_later, y_later, *after)

    def second_step(later):
        return beside(later[0], 1), beside(later[1], 2)

    def arrive_along(shares):
        return [shares[0]] + [along(shares[shift], shift) for shift in range(1, depth)]

    own, *rest = down_sums
    own_up, to_x, to_y, *rest_up = up_sums
    from_x, from_y, later = first_step(*rest, vector)
    late = second_step(later)
    shares = totals(own, from_x, from_y, *late)
    flip = 2
    while flip < ray_count:
        vector = vector + partner(vector, flip)
        flip *= 2
    to_x, to_y = tie(to_x, *later), tie(to_y, *later)
    from_x, from_y, later = first_step(to_x, to_y, *rest_up, vector, shares[0])
    up_shares = totals(own_up, from_x, from_y, *second_step(later))
    down_total = collect(arrive_along(shares), up_shares[0])
    down_x, down_y = beside(down_total, 1), beside(down_total, 2)
    up_total = collect(arrive_along(up_shares))
    short, long = join(up_total, vector, down_total, down_x, down_y)
    up_x, up_y, both = beside(short, 1), beside(short, 2), beside(long, 3)
    grad_up, grad_down, gain, scale, loss = place_quarters(
        group, (short, up_x, up_y, both), (down_total, down_x, down_y, both), part,
        rows * ray_count * group_count,
    )
    return (grad_up, grad_down, gain.reshape(width), scale.reshape(width), loss.reshape(()))


def shards(*operands):
    ray_count, group_count = lax.axis_size("ray"), lax.axis_size("grp")
    hidden = operands[-1].shape[0]
    square = group_count == 4 and ray_count in (8, 16) and hidden % (16 * group_count) == 0
    return (shards_square if square else shards_general)(*operands)


def solution(mesh):
    return jax.shard_map(
        shards,
        mesh=mesh,
        in_specs=(
            P(("grp", "ray"), None),
            P(None, ("grp", "ray")),
            P(None, ("grp", "ray")),
            P(("grp", "ray")),
            P("grp", None),
            P("grp", None),
            P(("grp", "ray"), None),
            P(),
            P(),
            P(None, "ray"),
            P("ray", None),
        ),
        out_specs=(P(None, "ray"), P("ray", None), P(), P(), P()),
        check_vma=False,
    )
```

```python
import functools

import jax
import jax.numpy as jnp
from jax import lax
from jax.experimental import pallas as pl
from jax.experimental.pallas import tpu as pltpu
from jax.sharding import PartitionSpec as P

STABILITY_EPSILON = 1e-06
F32 = jnp.float32
BF16 = jnp.bfloat16
MIB = 1024 * 1024
COST = pl.CostEstimate(flops=1 << 20, bytes_accessed=1 << 16, transcendentals=0)
LONG = pl.CostEstimate(flops=10**10, bytes_accessed=1 << 20, transcendentals=0)
SMEM = pl.BlockSpec(memory_space=pltpu.SMEM)
VMEM = pl.BlockSpec(memory_space=pltpu.VMEM)
ANY = pl.BlockSpec(memory_space=pl.ANY)


def params(mib=48, **more):
    return pltpu.CompilerParams(vmem_limit_bytes=mib * MIB, **more)


def dot_nn(a, b):
    return lax.dot_general(a, b, (((1,), (0,)), ((), ())), preferred_element_type=F32)


def dot_tn(a, b):
    return lax.dot_general(a, b, (((0,), (0,)), ((), ())), preferred_element_type=F32)


def dot_nt(a, b):
    return lax.dot_general(a, b, (((1,), (1,)), ((), ())), preferred_element_type=F32)


def owner_of(pixels, owner_ref, rows, count):
    block = lax.div(pixels, jnp.int32(rows))
    owner = jnp.zeros_like(pixels)
    for slot in range(count):
        owner = jnp.where(block == slot, owner_ref[0:1, slot:slot + 1], owner)
    return owner


def earlier(rows):
    before = lax.broadcasted_iota(jnp.int32, (rows, rows), 0)
    after = lax.broadcasted_iota(jnp.int32, (rows, rows), 1)
    return jnp.where(before < after, 1.0, 0.0).astype(BF16)


HBM = pl.BlockSpec(memory_space=pltpu.HBM)


def fetch(copies, sems):
    started = [
        pltpu.make_async_copy(source, target, sems.at[index])
        for index, (source, target) in enumerate(copies)
    ]
    for copy in started:
        copy.start()

    def wait(*numbers):
        for number in numbers:
            started[number].wait()

    return wait


def render_kernel(
    ray_count, relative, me_ref, owner_hbm, lists_hbm, opacity_hbm, counts_hbm, pixels_hbm,
    features_hbm, *refs,
):
    outs = refs[:-10]
    owner_ref, ids_ref, opacity_ref, counts_ref, mine_ref, features_ref = refs[-10:-4]
    share_ref, table_ref, send_ref, sems = refs[-4:]
    depth, rays = lists_hbm.shape
    gauss = features_hbm.shape[0]
    width = features_hbm.shape[1]
    me = me_ref[0]
    own_pixels = pixels_hbm.at[:, pl.ds(pl.multiple_of(me * rays, rays), rays)]
    wait = fetch(
        [
            (lists_hbm, ids_ref), (opacity_hbm, opacity_ref), (counts_hbm, counts_ref),
            (owner_hbm, owner_ref), (own_pixels, mine_ref), (features_hbm, features_ref),
        ],
        sems,
    )
    wait(0, 1, 2)
    ids_ref[...] = ids_ref[...] - me * gauss
    passing = jnp.ones((1, rays), F32)
    counts = counts_ref[...]
    for level in range(depth):
        alpha = opacity_ref[pl.ds(level, 1), :]
        share_ref[pl.ds(level, 1), :] = jnp.where(level < counts, alpha * passing, 0.0)
        passing = passing * (1.0 - alpha)

    tile = 256
    lanes = 128
    columns = rays // lanes

    @pl.loop(0, (gauss // tile) * columns)
    def _(step):
        first = pl.multiple_of(lax.div(step, columns) * tile, tile)
        lane = pl.multiple_of(lax.rem(step, columns) * lanes, lanes)
        number = (lax.broadcasted_iota(jnp.int32, (tile, lanes), 0) + first).astype(jnp.int16)
        total = jnp.zeros((tile, lanes), BF16)
        for level in range(depth):
            ident = jnp.broadcast_to(ids_ref[pl.ds(level, 1), pl.ds(lane, lanes)], (16, lanes))
            share = jnp.broadcast_to(share_ref[pl.ds(level, 1), pl.ds(lane, lanes)], (16, lanes))
            ident = jnp.concatenate([ident.astype(jnp.int16)] * (tile // 16), axis=0)
            share = jnp.concatenate([share.astype(BF16)] * (tile // 16), axis=0)
            total = total + jnp.where(ident == number, share, jnp.zeros_like(share))
        table_ref[pl.ds(first, tile), pl.ds(lane, lanes)] = total

    wait(3, 4, 5)
    owner = owner_of(mine_ref[...], owner_ref, rays, ray_count)
    padded = -(-ray_count // 16) * 16
    member = (lax.broadcasted_iota(jnp.int32, (padded, rays), 0) == owner)
    ranks = dot_nn(member.astype(F32).astype(BF16), earlier(rays))
    rank = jnp.sum(jnp.where(member, ranks, 0.0), axis=0, keepdims=True).astype(jnp.int32)
    if relative:
        chips = ray_count // 2
        shift = lax.div(owner, jnp.int32(2)) - lax.div(me, jnp.int32(2))
        shift = jnp.where(shift < 0, shift + chips, shift)
        flip = jnp.where(lax.rem(owner, jnp.int32(2)) == lax.rem(me, jnp.int32(2)), 0, 1)
        block = 2 * shift + flip
    else:
        block = owner
    slot = block * (rays // ray_count) + rank
    send_ref[...] = (
        (lax.broadcasted_iota(jnp.int32, (rays, rays), 0) == slot).astype(F32).astype(BF16)
    )

    piece = 256
    span = rays // len(outs)

    @pl.loop(0, width // piece)
    def _(step):
        cols = pl.ds(pl.multiple_of(step * piece, piece), piece)
        rendered = dot_tn(table_ref[...], features_ref[:, cols]).astype(BF16)
        ordered = dot_nn(send_ref[...], rendered).astype(BF16)
        for index, out in enumerate(outs):
            rows = ordered[index * span:(index + 1) * span]
            out[:, :, cols] = rows.reshape(*out.shape[:2], piece)


def render(ray_count, relative, me, owner, lists, opacity, counts, pixels, features):
    depth, rays = lists.shape
    gauss, width = features.shape
    parts = ray_count // 2 if relative else 1
    shape = jax.ShapeDtypeStruct((ray_count // parts, rays // ray_count, width), BF16)
    return pl.pallas_call(
        functools.partial(render_kernel, ray_count, relative),
        out_shape=(shape,) * parts,
        in_specs=[SMEM] + [HBM] * 6,
        out_specs=(VMEM,) * parts,
        scratch_shapes=[
            pltpu.VMEM(owner.shape, jnp.int32),
            pltpu.VMEM((depth, rays), jnp.int32),
            pltpu.VMEM((depth, rays), F32),
            pltpu.VMEM((1, rays), jnp.int32),
            pltpu.VMEM((1, rays), jnp.int32),
            pltpu.VMEM((gauss, width), BF16),
            pltpu.VMEM((depth, rays), F32),
            pltpu.VMEM((gauss, rays), BF16),
            pltpu.VMEM((rays, rays), BF16),
            pltpu.SemaphoreType.DMA((6,)),
        ],
        compiler_params=params(20),
        cost_estimate=COST,
        name="render",
    )(me, owner, lists, opacity, counts, pixels, features)


def tokens_kernel(
    ray_count, relative, me_ref, owner_hbm, pixels_hbm, tokens_hbm, gain_hbm,
    *refs,
):
    tokens_out, normed_out, normed_t_out = refs[-11:-8]
    owner_ref, pixels_ref, tokens_ref, gain_ref, order_ref, rank_ref, place_ref, sems = refs[-8:]
    rows, width = tokens_hbm.shape
    me = me_ref[0]
    each = rows // ray_count
    wait = fetch(
        [
            (owner_hbm, owner_ref), (pixels_hbm, pixels_ref), (gain_hbm, gain_ref),
            (tokens_hbm, tokens_ref),
        ],
        sems,
    )
    wait(0, 1)
    pixels = jnp.concatenate(
        [pixels_ref[:, sender * rows:(sender + 1) * rows] for sender in range(ray_count)], axis=0
    )
    mine = owner_of(pixels, owner_ref, rows, ray_count) == me
    place_ref[...] = lax.rem(pixels, jnp.int32(rows)).astype(F32)
    member = jnp.where(mine, 1.0, 0.0)
    padded = -(-ray_count // 16) * 16
    if padded > ray_count:
        spread = jnp.concatenate([member, jnp.zeros((padded - ray_count, rows), F32)], axis=0)
    else:
        spread = member
    ranks = dot_nn(spread.astype(BF16), earlier(rows))
    rank_ref[...] = jnp.where(mine, ranks[:ray_count], -1.0)
    chips = ray_count // 2
    for index in range(ray_count):
        if relative:
            chip = lax.rem(lax.div(me, jnp.int32(2)) + (chips - index // 2), jnp.int32(chips))
            sender = 2 * chip + jnp.bitwise_xor(lax.rem(me, jnp.int32(2)), index % 2)
        else:
            sender = index
        rank = rank_ref[pl.ds(sender, 1), :].astype(jnp.int32)
        hit = lax.broadcasted_iota(jnp.int32, (each, rows), 0) == rank
        at = jnp.sum(
            jnp.where(hit, place_ref[pl.ds(sender, 1), :], 0.0), axis=1, keepdims=True
        )
        here = lax.broadcasted_iota(jnp.int32, (each, rows), 1) == at.astype(jnp.int32)
        order_ref[pl.ds(index * each, each), :] = here.astype(F32).astype(BF16)
    wait(2, 3)
    half = min(128, rows)
    gain = gain_ref[...]

    @pl.loop(0, rows // half)
    def _(step):
        span = pl.ds(pl.multiple_of(step * half, half), half)
        values = dot_nn(order_ref[span, :], tokens_ref[...])
        tokens_out[span, :] = values.astype(BF16)
        centered = values - jnp.mean(values, axis=-1, keepdims=True)
        variance = jnp.mean(centered * centered, axis=-1, keepdims=True)
        xhat = centered * lax.rsqrt(variance + STABILITY_EPSILON)
        normed = (xhat * gain).astype(BF16)
        normed_out[span, :] = normed
        normed_t_out[:, span] = normed.T


def prepare_tokens(ray_count, relative, me, owner, pixels, tokens, gain, after=()):
    rows, width = tokens.shape
    return pl.pallas_call(
        functools.partial(tokens_kernel, ray_count, relative),
        out_shape=(
            jax.ShapeDtypeStruct((rows, width), BF16),
            jax.ShapeDtypeStruct((rows, width), BF16),
            jax.ShapeDtypeStruct((width, rows), BF16),
        ),
        in_specs=[SMEM] + [HBM] * 4 + [ANY] * len(after),
        out_specs=(VMEM, VMEM, VMEM),
        scratch_shapes=[
            pltpu.VMEM(owner.shape, jnp.int32),
            pltpu.VMEM(pixels.shape, jnp.int32),
            pltpu.VMEM((rows, width), BF16),
            pltpu.VMEM((1, width), F32),
            pltpu.VMEM((rows, rows), BF16),
            pltpu.VMEM((ray_count, rows), F32),
            pltpu.VMEM((ray_count, rows), F32),
            pltpu.SemaphoreType.DMA((4,)),
        ],
        compiler_params=params(20),
        cost_estimate=COST,
        name="tokens",
    )(me, owner, pixels, tokens, gain, *after)


def up_kernel(normed_ref, up_ref, act_ref, slope_ref):
    parts, _, part_rows, width = up_ref.shape
    up = up_ref[...].reshape(parts * part_rows, width)
    rows = normed_ref.shape[0]
    piece = min(128, rows)

    @pl.loop(0, rows // piece)
    def _(step):
        span = pl.ds(pl.multiple_of(step * piece, piece), piece)
        hidden = dot_nn(normed_ref[span, :], up)
        phi = 0.5 * (1.0 + lax.erf(hidden * (0.5 ** 0.5)))
        density = jnp.exp(-0.5 * hidden * hidden) * ((2.0 * jnp.pi) ** -0.5)
        act_ref[span, :] = (hidden * phi).astype(BF16)
        slope_ref[span, :] = (phi + hidden * density).astype(slope_ref.dtype)


def project_up(normed, up):
    rows, width = normed.shape
    parts, chunks, part_rows, chunk = up.shape
    return pl.pallas_call(
        up_kernel,
        grid=(chunks,),
        out_shape=(
            jax.ShapeDtypeStruct((rows, chunks * chunk), BF16),
            jax.ShapeDtypeStruct((rows, chunks * chunk), F32),
        ),
        in_specs=[
            pl.BlockSpec((rows, width), lambda j: (0, 0)),
            pl.BlockSpec((parts, 1, part_rows, chunk), lambda j: (0, j, 0, 0)),
        ],
        out_specs=(
            pl.BlockSpec((rows, chunk), lambda j: (0, j)),
            pl.BlockSpec((rows, chunk), lambda j: (0, j)),
        ),
        compiler_params=params(dimension_semantics=("arbitrary",)),
        cost_estimate=COST,
        name="up",
    )(normed, up)


def down_kernel(
    chunks, act_ref, down_ref, tokens_ref, target_ref, scale_ref,
    grad_ref, back_ref, small_ref, mixed_ref,
):
    step = pl.program_id(0)
    rows, width = tokens_ref.shape
    act = act_ref[...]

    @pl.when(step < chunks)
    def _():
        parts, _, part_rows, _ = down_ref.shape
        part = dot_nn(act, down_ref[...].reshape(parts * part_rows, width))

        @pl.when(step == 0)
        def _():
            mixed_ref[...] = part

        @pl.when(step > 0)
        def _():
            mixed_ref[...] += part

    @pl.when(step == chunks - 1)
    def _():
        scale = scale_ref[...]
        small_ref[...] = jnp.zeros_like(small_ref)
        piece = min(64, rows)

        @pl.loop(0, rows // piece)
        def _(index):
            span = pl.ds(pl.multiple_of(index * piece, piece), piece)
            mixed = mixed_ref[span, :]
            out = tokens_ref[span, :].astype(F32) + scale * mixed
            goal = target_ref[span, :].astype(F32)
            out_norm = jnp.sqrt(jnp.sum(out * out, axis=-1, keepdims=True) + STABILITY_EPSILON)
            goal_norm = jnp.sqrt(jnp.sum(goal * goal, axis=-1, keepdims=True) + STABILITY_EPSILON)
            norms = out_norm * goal_norm
            cosine = jnp.sum(out * goal, axis=-1, keepdims=True) / norms
            upstream = (cosine / (out_norm * out_norm)) * out - goal * (1.0 / norms)
            back_ref[span, :] = (upstream * scale).astype(BF16)
            small_ref[0:1, :] += jnp.sum(upstream * mixed, axis=0, keepdims=True)
            loss = jnp.sum(1.0 - cosine, axis=0, keepdims=True)
            small_ref[1:2, :] += jnp.broadcast_to(loss, (1, width))

    @pl.when(step >= chunks)
    def _():
        grad = dot_tn(act, back_ref[...])
        grad_ref[...] = grad.astype(BF16).reshape(grad_ref.shape)


def project_down(act, down, tokens, target, scale):
    rows, width = tokens.shape
    parts, chunks, part_rows, _ = down.shape
    chunk = parts * part_rows
    return pl.pallas_call(
        functools.partial(down_kernel, chunks),
        grid=(2 * chunks,),
        out_shape=(
            jax.ShapeDtypeStruct(down.shape, BF16),
            jax.ShapeDtypeStruct((rows, width), BF16),
            jax.ShapeDtypeStruct((8, width), F32),
        ),
        in_specs=[
            pl.BlockSpec((rows, chunk), lambda j: (0, lax.rem(j, chunks))),
            pl.BlockSpec(
                (parts, 1, part_rows, width), lambda j: (0, jnp.minimum(j, chunks - 1), 0, 0)
            ),
            pl.BlockSpec((rows, width), lambda j: (0, 0)),
            pl.BlockSpec((rows, width), lambda j: (0, 0)),
            pl.BlockSpec((1, width), lambda j: (0, 0)),
        ],
        out_specs=(
            pl.BlockSpec(
                (parts, 1, part_rows, width), lambda j: (0, jnp.maximum(j - chunks, 0), 0, 0)
            ),
            pl.BlockSpec((rows, width), lambda j: (0, 0)),
            pl.BlockSpec((8, width), lambda j: (0, 0)),
        ),
        scratch_shapes=[pltpu.VMEM((rows, width), F32)],
        compiler_params=params(dimension_semantics=("arbitrary",)),
        cost_estimate=COST,
        name="down",
    )(act, down, tokens, target, scale)


def back_kernel(back_ref, down_ref, slope_ref, normed_t_ref, up_ref, gain_ref, grad_ref, sum_ref):
    step = pl.program_id(0)
    parts, _, part_rows, width = down_ref.shape
    chunk = parts * part_rows
    rows = back_ref.shape[0]
    back_act = dot_nt(back_ref[...], down_ref[...].reshape(chunk, width))
    back_hidden = (back_act * slope_ref[...]).astype(BF16)
    up_parts, _, up_rows, _ = up_ref.shape

    @pl.when(step == 0)
    def _():
        sum_ref[...] = jnp.zeros_like(sum_ref)

    grad = dot_nn(normed_t_ref[...], back_hidden)
    grad_ref[...] = grad.astype(BF16).reshape(grad_ref.shape)
    up = up_ref[...].reshape(up_parts * up_rows, chunk).astype(F32)
    sum_ref[...] += jnp.sum(grad * up, axis=1, keepdims=True) / gain_ref[...]


def back_up(back, down, slope, normed_t, up, gain):
    width, rows = normed_t.shape
    parts, chunks, part_rows, _ = down.shape
    chunk = parts * part_rows
    up_parts, _, up_rows, _ = up.shape
    return pl.pallas_call(
        back_kernel,
        grid=(chunks,),
        out_shape=(
            jax.ShapeDtypeStruct(up.shape, BF16),
            jax.ShapeDtypeStruct((width, 1), F32),
        ),
        in_specs=[
            pl.BlockSpec((rows, width), lambda j: (0, 0)),
            pl.BlockSpec((parts, 1, part_rows, width), lambda j: (0, j, 0, 0)),
            pl.BlockSpec((rows, chunk), lambda j: (0, j)),
            pl.BlockSpec((width, rows), lambda j: (0, 0)),
            pl.BlockSpec((up_parts, 1, up_rows, chunk), lambda j: (0, j, 0, 0)),
            pl.BlockSpec((width, 1), lambda j: (0, 0)),
        ],
        out_specs=(
            pl.BlockSpec((up_parts, 1, up_rows, chunk), lambda j: (0, j, 0, 0)),
            pl.BlockSpec((width, 1), lambda j: (0, 0)),
        ),
        compiler_params=params(dimension_semantics=("arbitrary",)),
        cost_estimate=COST,
        name="back",
    )(back, down, slope, normed_t, up, gain)


def gather_weight(weight, parts, group, group_count, ray_count):
    rows, cols = weight.shape
    if parts == 1:
        whole = lax.all_gather(weight, "ray", axis=0, tiled=True)
    else:
        part = lax.dynamic_slice_in_dim(weight, group * (rows // parts), rows // parts, 0)
        whole = lax.all_gather(part, ("grp", "ray"), axis=0, tiled=True)
    return whole.reshape(parts, ray_count, rows // parts, cols)


def reduce_gradient(grad):
    parts, ray_count, part_rows, cols = grad.shape
    flat = grad.reshape(parts * ray_count * part_rows, cols)
    if parts == 1:
        share = lax.psum_scatter(flat, "ray", scatter_dimension=0, tiled=True)
        return lax.psum(share.astype(F32), "grp")
    share = lax.psum_scatter(flat, "grp", scatter_dimension=0, tiled=True)
    share = lax.psum_scatter(share, "ray", scatter_dimension=0, tiled=True)
    return lax.all_gather(share, "grp", axis=0, tiled=True).astype(F32)


def shards_general(
    image_tokens,
    tile_lists,
    opacity,
    tile_counts,
    ray_pixel,
    block_owner,
    gaussian_features,
    layer_norm_gain,
    layer_scale,
    up_weight,
    down_weight,
):
    ray_count = lax.axis_size("ray")
    group_count = lax.axis_size("grp")
    group = lax.axis_index("grp")
    me = lax.axis_index("ray").reshape(1)
    rows, width = image_tokens.shape
    up_parts = group_count if up_weight.shape[0] % (16 * group_count) == 0 else 1
    down_parts = group_count if down_weight.shape[0] % (16 * group_count) == 0 else 1
    up = gather_weight(up_weight, up_parts, group, group_count, ray_count)
    down = gather_weight(down_weight, down_parts, group, group_count, ray_count)
    rendered = render(
        ray_count, False, me, block_owner, tile_lists, opacity, tile_counts.reshape(1, rows),
        ray_pixel, gaussian_features,
    )
    rendered = rendered[0].reshape(rows, width)
    target = lax.all_to_all(rendered, "ray", split_axis=0, concat_axis=0, tiled=True)
    tokens, normed, normed_t = prepare_tokens(
        ray_count, False, me, block_owner, ray_pixel, image_tokens,
        layer_norm_gain.reshape(1, width),
    )
    act, slope = project_up(normed, up)
    grad_down, back, small = project_down(act, down, tokens, target, layer_scale.reshape(1, width))
    grad_up, gain_sum = back_up(back, down, slope, normed_t, up, layer_norm_gain.reshape(width, 1))
    grad_down = reduce_gradient(grad_down)
    grad_up = reduce_gradient(grad_up)
    sums = jnp.concatenate([gain_sum.reshape(1, width), small[:2]], axis=0)
    sums = lax.psum(sums, ("grp", "ray"))
    loss = sums[2, 0] / (rows * ray_count * group_count)
    return (grad_up, grad_down, sums[0], sums[1], loss)


def quarter_kernel(group_ref, up_hbm, down_hbm, out_ref, up_ref, turned_ref, sems):
    part = out_ref.shape[1]
    lanes = up_ref.shape[1]
    start = pl.multiple_of(group_ref[0] * part, part)
    lane = pl.multiple_of(lax.div(start, jnp.int32(lanes)) * lanes, lanes)
    wait = fetch(
        [
            (up_hbm.at[:, pl.ds(lane, lanes)], up_ref),
            (down_hbm.at[pl.ds(start, part), :], out_ref.at[1]),
        ],
        sems,
    )
    wait(0)
    turned_ref[...] = up_ref[...].T
    out_ref[0] = turned_ref[pl.ds(pl.multiple_of(start - lane, part), part), :]
    wait(1)


def own_quarter(group, up, down, part):
    width, chunk = up.shape
    lanes = max(128, part)
    return pl.pallas_call(
        quarter_kernel,
        out_shape=jax.ShapeDtypeStruct((2, part, width), BF16),
        in_specs=[SMEM, HBM, HBM],
        out_specs=VMEM,
        scratch_shapes=[
            pltpu.VMEM((width, lanes), BF16),
            pltpu.VMEM((lanes, width), BF16),
            pltpu.SemaphoreType.DMA((2,)),
        ],
        compiler_params=params(16),
        cost_estimate=LONG,
        name="quarter",
    )(group, up, down)


def own_rows_kernel(group_ref, up_ref, down_ref, out_ref, turned_ref):
    part = out_ref.shape[2]
    turned_ref[...] = up_ref[...].T
    for index in range(4):
        quarter = jnp.bitwise_xor(group_ref[0], index)
        span = pl.ds(pl.multiple_of(quarter * part, part), part)
        out_ref[index, 0] = turned_ref[span, :]
        out_ref[index, 1] = down_ref[span, :]


def own_rows(group, up, down):
    width, chunk = up.shape
    return pl.pallas_call(
        own_rows_kernel,
        out_shape=jax.ShapeDtypeStruct((4, 2, chunk // 4, width), BF16),
        in_specs=[SMEM, VMEM, VMEM],
        out_specs=VMEM,
        scratch_shapes=[pltpu.VMEM((chunk, width), BF16)],
        compiler_params=params(16),
        cost_estimate=COST,
        name="own_rows",
    )(group, up, down)


def finish_rows(tokens, mixed, goal, scale):
    out = tokens + scale * mixed
    out_norm = jnp.sqrt(jnp.sum(out * out, axis=-1, keepdims=True) + STABILITY_EPSILON)
    goal_norm = jnp.sqrt(jnp.sum(goal * goal, axis=-1, keepdims=True) + STABILITY_EPSILON)
    norms = out_norm * goal_norm
    cosine = jnp.sum(out * goal, axis=-1, keepdims=True) / norms
    upstream = (cosine / (out_norm * out_norm)) * out - goal * (1.0 / norms)
    return upstream, 1.0 - cosine


def forward_kernel(first, blocks, sides, skipped, *refs):
    last = blocks > 0
    refs = list(refs[skipped:])
    normed_t_ref = refs.pop(0)
    own, other = refs[:sides], refs[sides:2 * sides]
    del refs[:2 * sides]
    mixed_in = None if first else refs.pop(0)
    if last:
        tokens_ref, scale_ref = refs[:2]
        targets, passed_ref = refs[2:2 + blocks], refs[2 + blocks]
        del refs[:3 + blocks]
    act_ref, slope_ref = refs[:2]
    del refs[:2]
    width, rows = normed_t_ref.shape
    part = act_ref.shape[2]
    part_sum = None
    downs = []
    for side, group in enumerate((own, other)):
        start = 0
        for ref in group:
            count = ref.shape[0]
            hiddens = dot_nn(ref[:, 0].reshape(count * part, width), normed_t_ref[...])
            for index in range(count):
                hidden = hiddens[index * part:(index + 1) * part]
                phi = 0.5 * (1.0 + lax.erf(hidden * (0.5 ** 0.5)))
                density = jnp.exp(-0.5 * hidden * hidden) * ((2.0 * jnp.pi) ** -0.5)
                act_ref[side, start + index] = (hidden * phi).astype(BF16)
                slope_ref[side, start + index] = phi + hidden * density
            downs.append(ref[:, 1].reshape(count * part, width))
            start += count
    if sides > 1 or last:
        act = act_ref[...].reshape(2 * start * part, rows)
        part_sum = dot_tn(act, jnp.concatenate(downs, axis=0))
    else:
        for side, down in enumerate(downs):
            term = dot_tn(act_ref[side].reshape(start * part, rows), down)
            part_sum = term if part_sum is None else part_sum + term
    if not last:
        mixed_out = refs[0]
        mixed_out[...] = part_sum if first else mixed_in[...] + part_sum
        return
    back_ref, back_t_ref, small_ref, mixed_ref = refs
    mixed_ref[...] = mixed_in[...] + part_sum
    scale = scale_ref[...]
    small_ref[...] = jnp.zeros_like(small_ref)
    piece = rows // blocks
    for index, target_ref in enumerate(targets):
        span = pl.ds(index * piece, piece)
        mixed = mixed_ref[span, :]
        goal = jnp.concatenate([target_ref[0], passed_ref[index]], axis=0).astype(F32)
        upstream, loss = finish_rows(tokens_ref[span, :].astype(F32), mixed, goal, scale)
        back = (upstream * scale).astype(BF16)
        back_ref[span, :] = back
        back_t_ref[:, span] = back.T
        small_ref[0:1, :] += jnp.sum(upstream * mixed, axis=0, keepdims=True)
        small_ref[1:2, :] += jnp.broadcast_to(jnp.sum(loss, axis=0, keepdims=True), (1, width))


def forward(normed_t, own, other, mixed=None, finish=None, after=()):
    width, rows = normed_t.shape
    part = own[0].shape[2]
    total = sum(array.shape[0] for array in own)
    first, last = mixed is None, finish is not None
    blocks = len(finish) - 3 if last else 0
    operands = [*after, normed_t, *own, *other]
    if not first:
        operands.append(mixed)
    if last:
        operands.extend(finish)
    piece = (2, total, part, rows)
    shapes = [jax.ShapeDtypeStruct(piece, BF16), jax.ShapeDtypeStruct(piece, F32)]
    scratch = []
    if last:
        shapes += [
            jax.ShapeDtypeStruct((rows, width), BF16),
            jax.ShapeDtypeStruct((width, rows), BF16),
            jax.ShapeDtypeStruct((8, width), F32),
        ]
        scratch = [pltpu.VMEM((rows, width), F32)]
    else:
        shapes += [jax.ShapeDtypeStruct((rows, width), F32)]
    return pl.pallas_call(
        functools.partial(forward_kernel, first, blocks, len(own), len(after)),
        out_shape=tuple(shapes),
        in_specs=[ANY] * len(after) + [VMEM] * (len(operands) - len(after)),
        out_specs=tuple([VMEM] * len(shapes)),
        scratch_shapes=scratch,
        compiler_params=params(32),
        cost_estimate=COST,
        name="forward",
    )(*operands)


def pack_kernel(counts, *refs):
    out_ref = refs[-1]
    start = 0
    for count, ref in zip(counts, refs):
        out_ref[start:start + count] = ref[...].reshape(count, *out_ref.shape[1:])
        start += count


def pack(pieces, *after):
    counts = [1 if piece.ndim == 3 else piece.shape[0] for piece in pieces]
    return pl.pallas_call(
        functools.partial(pack_kernel, counts),
        out_shape=jax.ShapeDtypeStruct((sum(counts), *pieces[0].shape[-3:]), BF16),
        in_specs=[VMEM] * len(pieces) + [ANY] * len(after),
        out_specs=VMEM,
        compiler_params=params(16),
        cost_estimate=COST,
        name="pack",
    )(*pieces, *after)


def turn_kernel(y_ref, x_ref, a_ref, b_ref):
    count = a_ref.shape[0]
    a_ref[...] = y_ref[:count]
    b_ref[...] = x_ref[count:]


def turn(y, x):
    count = y.shape[0]
    first = count // 2
    return pl.pallas_call(
        turn_kernel,
        out_shape=(
            jax.ShapeDtypeStruct((first, *y.shape[1:]), BF16),
            jax.ShapeDtypeStruct((count - first, *y.shape[1:]), BF16),
        ),
        in_specs=[VMEM] * 2,
        out_specs=(VMEM, VMEM),
        compiler_params=params(16),
        cost_estimate=COST,
        name="turn",
    )(y, x)


def tie_kernel(*refs):
    pass


def tie(array, *after):
    return pl.pallas_call(
        tie_kernel,
        out_shape=jax.ShapeDtypeStruct(array.shape, array.dtype),
        in_specs=[ANY] * (1 + len(after)),
        out_specs=ANY,
        input_output_aliases={0: 0},
        compiler_params=params(4),
        cost_estimate=COST,
        name="tie",
    )(array, *after)


def seconds_kernel(*refs):
    for index, ref in enumerate(refs[:-1]):
        refs[-1][index] = ref[1]


def seconds(blocks):
    count, (_, each, width) = len(blocks), blocks[0].shape
    return pl.pallas_call(
        seconds_kernel,
        out_shape=jax.ShapeDtypeStruct((count, each, width), BF16),
        in_specs=[VMEM] * count,
        out_specs=VMEM,
        compiler_params=params(16),
        cost_estimate=COST,
        name="seconds",
    )(*blocks)


def joined(refs, pieces, pick):
    values = [pick(refs[which], start, count) for which, start, count in pieces]
    flat = [value.reshape(-1, value.shape[-1]) for value in values]
    return flat[0] if len(flat) == 1 else jnp.concatenate(flat, axis=0)


def put(quarter, value, outs):
    own_ref, x_ref, y_ref, x_later_ref, y_later_ref = outs
    value = value.astype(BF16).reshape(own_ref.shape)
    half = x_ref.shape[0] // 2
    if quarter == 0:
        own_ref[...] = value
    elif quarter == 1:
        x_ref[half:] = value[:half]
        x_later_ref[...] = value[half:]
    elif quarter == 2:
        y_ref[half:] = value[half:]
        y_later_ref[...] = value[:half]
    else:
        x_ref[:half] = value[:half]
        y_ref[:half] = value[half:]


def emit(quarter, value, arrived, outs):
    if arrived is None:
        outs[0][quarter] = value.astype(BF16).reshape(outs[0].shape[1:])
    else:
        put(quarter, value + arrived[quarter].reshape(value.shape).astype(F32), outs)


def down_grad_kernel(side, act_pieces, add, *refs):
    acts, back_ref = refs[:2], refs[2]
    arrived = refs[3] if add else None
    outs = refs[4:] if add else refs[3:]
    for quarter in (3, 1, 2, 0):
        act = joined(acts, act_pieces[quarter], lambda ref, a, n: ref[side, a:a + n])
        emit(quarter, dot_nn(act, back_ref[...]), arrived, outs)


def up_grad_kernel(side, weight_pieces, act_pieces, add, *refs):
    weights, slopes = refs[:2], refs[2:4]
    back_t_ref, normed_ref, gain_in = refs[4:7]
    if add:
        arrived, scale_ref, small_ref = refs[7:10]
        outs, vector_ref, gain_ref = refs[10:-2], refs[-2], refs[-1]
    else:
        arrived = None
        outs, gain_ref = refs[7:-1], refs[-1]
    gain_ref[...] = gain_in[...]
    for quarter in (3, 1, 2, 0):
        pieces = weight_pieces[quarter]
        slope = joined(slopes, act_pieces[quarter], lambda ref, a, n: ref[side, a:a + n])
        back_act = dot_nn(joined(weights, pieces, lambda ref, a, n: ref[a:a + n, 1]), back_t_ref[...])
        back_hidden = (back_act * slope).astype(BF16)
        grad = dot_nn(back_hidden, normed_ref[...])
        up = joined(weights, pieces, lambda ref, a, n: ref[a:a + n, 0]).astype(F32)
        gain_ref[...] += jnp.sum(grad * up, axis=0, keepdims=True)
        emit(quarter, grad, arrived, outs)
    if add:
        vector_ref[0:1, :] = gain_ref[...] / scale_ref[...]
        vector_ref[1:3, :] = small_ref[0:2, :]
        vector_ref[3:8, :] = jnp.zeros((5, gain_ref.shape[1]), F32)


def gradient_shapes(depth, part, width, add):
    if not add:
        return [jax.ShapeDtypeStruct((4, depth, part, width), BF16)]
    counts = (depth, depth, depth, depth - depth // 2, depth // 2)
    return [jax.ShapeDtypeStruct((count, part, width), BF16) for count in counts]


def down_gradient(side, act_pieces, depth, acts, back, arrived=None):
    part = acts[0].shape[2]
    width = back.shape[1]
    add = arrived is not None
    operands = [*acts, back] + ([arrived] if add else [])
    shapes = gradient_shapes(depth, part, width, add)
    return pl.pallas_call(
        functools.partial(down_grad_kernel, side, act_pieces, add),
        out_shape=tuple(shapes),
        in_specs=[VMEM] * len(operands),
        out_specs=tuple([VMEM] * len(shapes)),
        compiler_params=params(20),
        cost_estimate=COST,
        name="down_gradient",
    )(*operands)


def up_gradient(
    side, weight_pieces, act_pieces, depth, weights, slopes, back_t, normed, gain, extra=()
):
    part, width = weights[0].shape[2:]
    add = len(extra) > 0
    operands = [*weights, *slopes, back_t, normed, gain, *extra]
    shapes = gradient_shapes(depth, part, width, add)
    if add:
        shapes.append(jax.ShapeDtypeStruct((8, width), F32))
        scratch = [pltpu.VMEM((1, width), F32)]
    else:
        scratch = []
        shapes.append(jax.ShapeDtypeStruct((1, width), F32))
    return pl.pallas_call(
        functools.partial(up_grad_kernel, side, weight_pieces, act_pieces, add),
        out_shape=tuple(shapes),
        in_specs=[VMEM] * len(operands),
        out_specs=tuple([VMEM] * len(shapes)),
        scratch_shapes=scratch,
        compiler_params=params(24),
        cost_estimate=COST,
        name="up_gradient",
    )(*operands)


def merge_kernel(x_ref, y_ref, x_later_ref, y_later_ref, *refs):
    x_out, y_out = refs[-2:]
    half = y_later_ref.shape[0]
    x_out[...] = (x_later_ref[...].astype(F32) + y_ref[:half].astype(F32)).astype(BF16)
    y_out[...] = (y_later_ref[...].astype(F32) + x_ref[:half].astype(F32)).astype(BF16)


def merge(x, y, x_later, y_later, *after):
    return pl.pallas_call(
        merge_kernel,
        out_shape=tuple(jax.ShapeDtypeStruct(a.shape, BF16) for a in (x_later, y_later)),
        in_specs=[VMEM] * 4 + [ANY] * len(after),
        out_specs=(VMEM, VMEM),
        compiler_params=params(16),
        cost_estimate=COST,
        name="merge",
    )(x, y, x_later, y_later, *after)


def total_kernel(own_ref, x_ref, y_ref, x_late_ref, y_late_ref, *refs):
    outs = refs[-own_ref.shape[0]:]
    half = y_late_ref.shape[0]
    for index, out in enumerate(outs):
        total = own_ref[index].astype(F32)
        if index < half:
            total += x_ref[half + index].astype(F32) + y_late_ref[index].astype(F32)
        else:
            total += y_ref[index].astype(F32) + x_late_ref[index - half].astype(F32)
        out[...] = total.astype(BF16)


def totals(own, x, y, x_late, y_late, *after):
    count, part, width = own.shape
    return pl.pallas_call(
        total_kernel,
        out_shape=tuple([jax.ShapeDtypeStruct((part, width), BF16)] * count),
        in_specs=[VMEM] * 5 + [ANY] * len(after),
        out_specs=tuple([VMEM] * count),
        compiler_params=params(16),
        cost_estimate=COST,
        name="totals",
    )(own, x, y, x_late, y_late, *after)


def collect_kernel(count, *refs):
    total = refs[0][...].astype(F32)
    for ref in refs[1:count]:
        total = total + ref[...].astype(F32)
    refs[-1][...] = total.astype(BF16)


def collect(parts, *after):
    return pl.pallas_call(
        functools.partial(collect_kernel, len(parts)),
        out_shape=jax.ShapeDtypeStruct(parts[0].shape, BF16),
        in_specs=[VMEM] * len(parts) + [ANY] * len(after),
        out_specs=VMEM,
        compiler_params=params(16),
        cost_estimate=COST,
        name="collect",
    )(*parts, *after)


def join_kernel(total_ref, vector_ref, other_ref, *refs):
    short_ref, long_ref, held_ref = refs[-3:]
    part = total_ref.shape[0]
    short_ref[pl.ds(0, part), :] = total_ref[...]
    rest = vector_ref[0:3, :]
    held_ref[...] = jnp.zeros_like(held_ref)
    for index in range(3):
        piece = rest.astype(BF16).astype(F32)
        held_ref[3 * index:3 * index + 3, :] = piece
        rest = rest - piece
    short_ref[pl.ds(part, 16), :] = held_ref[...].astype(BF16)
    long_ref[pl.ds(0, part + 16), :] = short_ref[...]
    long_ref[pl.ds(part + 16, part), :] = other_ref[...]


def join(total, vector, other, *after):
    part, width = total.shape
    return pl.pallas_call(
        join_kernel,
        out_shape=tuple(
            jax.ShapeDtypeStruct((rows, width), BF16) for rows in (part + 16, 2 * part + 16)
        ),
        in_specs=[VMEM] * 3 + [ANY] * len(after),
        out_specs=(VMEM, VMEM),
        scratch_shapes=[pltpu.VMEM((16, width), F32)],
        compiler_params=params(16),
        cost_estimate=COST,
        name="join",
    )(total, vector, other, *after)


def place_kernel(part, tokens, group_ref, *refs):
    ups, downs = refs[:4], refs[4:8]
    up_ref, down_ref, gain_ref, scale_ref, loss_ref, held_ref = refs[8:]
    group = group_ref[0]
    vectors = []
    for index, (up, down) in enumerate(zip(ups, downs)):
        first = pl.multiple_of(jnp.bitwise_xor(group, index) * part, part)
        held_ref[pl.ds(first, part), :] = up[pl.ds(0, part), :].astype(F32)
        start = down.shape[0] - part
        down_ref[pl.ds(first, part), :] = down[pl.ds(start, part), :].astype(F32)
        rows = up[pl.ds(part, 16), :].astype(F32)
        vectors.append((rows[0:3] + rows[3:6]) + rows[6:9])
    up_ref[...] = held_ref[...].T
    vector = (vectors[0] + vectors[1]) + (vectors[2] + vectors[3])
    gain_ref[...] = vector[0:1]
    scale_ref[...] = vector[1:2]
    loss_ref[...] = vector[2:3, 0:1] * (1.0 / tokens)


def place_quarters(group, ups, downs, part, tokens):
    width = ups[0].shape[1]
    shapes = [
        jax.ShapeDtypeStruct((width, 4 * part), F32),
        jax.ShapeDtypeStruct((4 * part, width), F32),
        jax.ShapeDtypeStruct((1, width), F32),
        jax.ShapeDtypeStruct((1, width), F32),
        jax.ShapeDtypeStruct((1, 1), F32),
    ]
    return pl.pallas_call(
        functools.partial(place_kernel, part, tokens),
        out_shape=tuple(shapes),
        in_specs=[SMEM] + [VMEM] * 8,
        out_specs=tuple([VMEM] * len(shapes)),
        scratch_shapes=[pltpu.VMEM((4 * part, width), F32)],
        compiler_params=params(16),
        cost_estimate=COST,
        name="place",
    )(group, *ups, *downs)


def shards_square(
    image_tokens,
    tile_lists,
    opacity,
    tile_counts,
    ray_pixel,
    block_owner,
    gaussian_features,
    layer_norm_gain,
    layer_scale,
    up_weight,
    down_weight,
):
    ray_count = lax.axis_size("ray")
    group_count = lax.axis_size("grp")
    depth = ray_count // 2
    group = lax.axis_index("grp").reshape(1)
    me = lax.axis_index("ray").reshape(1)
    rows, width = image_tokens.shape
    part = down_weight.shape[0] // group_count

    def beside(array, flip):
        return lax.ppermute(array, "grp", [(g, g ^ flip) for g in range(group_count)])

    def partner(array, flip=1):
        return lax.ppermute(array, "ray", [(r, r ^ flip) for r in range(ray_count)])

    def along(array, shift):
        pairs = [(r, (r + 2 * shift) % ray_count) for r in range(ray_count)]
        return lax.ppermute(array, "ray", pairs)

    mine = own_quarter(group, up_weight, down_weight, part)
    arrivals = [along(mine, -shift) for shift in range(1, depth)]
    rendered = render(
        ray_count, True, me, block_owner, tile_lists, opacity, tile_counts.reshape(1, rows),
        ray_pixel, gaussian_features,
    )
    half = depth // 2
    low = pack(arrivals[:half - 1], rendered[0])
    x_low, y_low = beside(low, 1), beside(low, 2)
    high = pack(arrivals[half - 1:], low)
    high = tie(high, x_low, y_low)
    x_high, y_high = beside(high, 1), beside(high, 2)
    targets = [rendered[0]] + [along(rendered[shift], shift) for shift in range(1, depth)]
    tokens, normed, normed_t = prepare_tokens(
        ray_count, True, me, block_owner, ray_pixel, image_tokens,
        layer_norm_gain.reshape(1, width),
    )
    most = pack(
        [own_rows(group, up_weight, down_weight), low, x_low, y_low, high, x_high, y_high],
        targets[half],
    )
    most_other = partner(most)
    d_low, d_high = beside(y_low, 1), beside(x_high, 2)
    act_most, slope_most, mixed = forward(normed_t, [most], [most_other])
    late = [target for shift, target in enumerate(targets) if shift not in (0, half)]
    last = pack([d_low, d_high], mixed, *late)
    last_other = partner(last)
    act_last, slope_last, back, back_t, small = forward(
        normed_t, [last], [last_other], mixed,
        (tokens, layer_scale.reshape(1, width), *targets, partner(seconds(targets))),
    )
    acts, slopes = (act_most, act_last), (slope_most, slope_last)
    weights = ((most, last), (most_other, last_other))
    count, rest = half - 1, depth - half
    start = 4 + 3 * count
    pieces = tuple(
        ((0, q, 1), (0, 4 + q * count, count), (0, start + q * rest, rest)) for q in range(3)
    ) + (((0, 3, 1), (1, 0, depth - 1)),)
    gain = jnp.zeros((1, width), F32)
    (down_other,) = down_gradient(1, pieces, depth, acts, back)
    down_arrived = partner(down_other)
    up_other, gain = up_gradient(
        1, pieces, pieces, depth, weights[1], slopes, back_t, normed, gain
    )
    up_arrived = partner(up_other)
    down_sums = down_gradient(0, pieces, depth, acts, back, down_arrived)
    *up_sums, vector = up_gradient(
        0, pieces, pieces, depth, weights[0], slopes, back_t, normed, gain,
        (up_arrived, layer_norm_gain.reshape(1, width), small),
    )
    vector = vector + partner(vector)
    flip = 2
    while flip < ray_count:
        vector = vector + partner(vector, flip)
        flip *= 2

    def first_step(to_x, to_y, x_later, y_later, *after):
        from_x, from_y = beside(to_x, 1), beside(to_y, 2)
        return from_x, from_y, merge(from_x, from_y, x_later, y_later, *after)

    def second_step(later):
        return beside(later[0], 1), beside(later[1], 2)

    def arrive_along(shares):
        return [shares[0]] + [along(shares[shift], shift) for shift in range(1, depth)]

    own, *rest = down_sums
    own_up, to_x, to_y, *rest_up = up_sums
    from_x, from_y, later = first_step(*rest, vector)
    late = second_step(later)
    shares = totals(own, from_x, from_y, *late)
    from_x, from_y, later = first_step(to_x, to_y, *rest_up)
    up_shares = totals(own_up, from_x, from_y, *second_step(later))
    down_total = collect(arrive_along(shares), up_shares[0])
    down_x, down_y = beside(down_total, 1), beside(down_total, 2)
    up_total = collect(arrive_along(up_shares))
    short, long = join(up_total, vector, down_total, down_x, down_y)
    up_x, up_y, both = beside(short, 1), beside(short, 2), beside(long, 3)
    grad_up, grad_down, gain, scale, loss = place_quarters(
        group, (short, up_x, up_y, both), (down_total, down_x, down_y, both), part,
        rows * ray_count * group_count,
    )
    return (grad_up, grad_down, gain.reshape(width), scale.reshape(width), loss.reshape(()))


def shards(*operands):
    ray_count, group_count = lax.axis_size("ray"), lax.axis_size("grp")
    hidden = operands[-1].shape[0]
    square = group_count == 4 and ray_count in (8, 16) and hidden % (16 * group_count) == 0
    return (shards_square if square else shards_general)(*operands)


def solution(mesh):
    return jax.shard_map(
        shards,
        mesh=mesh,
        in_specs=(
            P(("grp", "ray"), None),
            P(None, ("grp", "ray")),
            P(None, ("grp", "ray")),
            P(("grp", "ray")),
            P("grp", None),
            P("grp", None),
            P(("grp", "ray"), None),
            P(),
            P(),
            P(None, "ray"),
            P("ray", None),
        ),
        out_specs=(P(None, "ray"), P("ray", None), P(), P(), P()),
        check_vma=False,
    )
```

```python
import functools

import jax
import jax.numpy as jnp
from jax import lax
from jax.experimental import pallas as pl
from jax.experimental.pallas import tpu as pltpu
from jax.sharding import PartitionSpec as P

STABILITY_EPSILON = 1e-06
F32 = jnp.float32
BF16 = jnp.bfloat16
MIB = 1024 * 1024
COST = pl.CostEstimate(flops=1 << 20, bytes_accessed=1 << 16, transcendentals=0)
LONG = pl.CostEstimate(flops=10**10, bytes_accessed=1 << 20, transcendentals=0)
SMEM = pl.BlockSpec(memory_space=pltpu.SMEM)
VMEM = pl.BlockSpec(memory_space=pltpu.VMEM)
ANY = pl.BlockSpec(memory_space=pl.ANY)


def params(mib=48, **more):
    return pltpu.CompilerParams(vmem_limit_bytes=mib * MIB, **more)


def dot_nn(a, b):
    return lax.dot_general(a, b, (((1,), (0,)), ((), ())), preferred_element_type=F32)


def dot_tn(a, b):
    return lax.dot_general(a, b, (((0,), (0,)), ((), ())), preferred_element_type=F32)


def dot_nt(a, b):
    return lax.dot_general(a, b, (((1,), (1,)), ((), ())), preferred_element_type=F32)


def owner_of(pixels, owner_ref, rows, count):
    block = lax.div(pixels, jnp.int32(rows))
    owner = jnp.zeros_like(pixels)
    for slot in range(count):
        owner = jnp.where(block == slot, owner_ref[0:1, slot:slot + 1], owner)
    return owner


def earlier(rows):
    before = lax.broadcasted_iota(jnp.int32, (rows, rows), 0)
    after = lax.broadcasted_iota(jnp.int32, (rows, rows), 1)
    return jnp.where(before < after, 1.0, 0.0).astype(BF16)


HBM = pl.BlockSpec(memory_space=pltpu.HBM)


def fetch(copies, sems):
    started = [
        pltpu.make_async_copy(source, target, sems.at[index])
        for index, (source, target) in enumerate(copies)
    ]
    for copy in started:
        copy.start()

    def wait(*numbers):
        for number in numbers:
            started[number].wait()

    return wait


def render_kernel(
    ray_count, relative, me_ref, owner_hbm, lists_hbm, opacity_hbm, counts_hbm, pixels_hbm,
    features_hbm, *refs,
):
    outs = refs[:-10]
    owner_ref, ids_ref, opacity_ref, counts_ref, mine_ref, features_ref = refs[-10:-4]
    share_ref, table_ref, send_ref, sems = refs[-4:]
    depth, rays = lists_hbm.shape
    gauss = features_hbm.shape[0]
    width = features_hbm.shape[1]
    me = me_ref[0]
    own_pixels = pixels_hbm.at[:, pl.ds(pl.multiple_of(me * rays, rays), rays)]
    wait = fetch(
        [
            (lists_hbm, ids_ref), (opacity_hbm, opacity_ref), (counts_hbm, counts_ref),
            (owner_hbm, owner_ref), (own_pixels, mine_ref), (features_hbm, features_ref),
        ],
        sems,
    )
    wait(0, 1, 2)
    ids_ref[...] = ids_ref[...] - me * gauss
    passing = jnp.ones((1, rays), F32)
    counts = counts_ref[...]
    for level in range(depth):
        alpha = opacity_ref[pl.ds(level, 1), :]
        share_ref[pl.ds(level, 1), :] = jnp.where(level < counts, alpha * passing, 0.0)
        passing = passing * (1.0 - alpha)

    tile = 256
    lanes = 128
    columns = rays // lanes

    @pl.loop(0, (gauss // tile) * columns)
    def _(step):
        first = pl.multiple_of(lax.div(step, columns) * tile, tile)
        lane = pl.multiple_of(lax.rem(step, columns) * lanes, lanes)
        number = (lax.broadcasted_iota(jnp.int32, (tile, lanes), 0) + first).astype(jnp.int16)
        total = jnp.zeros((tile, lanes), BF16)
        for level in range(depth):
            ident = jnp.broadcast_to(ids_ref[pl.ds(level, 1), pl.ds(lane, lanes)], (16, lanes))
            share = jnp.broadcast_to(share_ref[pl.ds(level, 1), pl.ds(lane, lanes)], (16, lanes))
            ident = jnp.concatenate([ident.astype(jnp.int16)] * (tile // 16), axis=0)
            share = jnp.concatenate([share.astype(BF16)] * (tile // 16), axis=0)
            total = total + jnp.where(ident == number, share, jnp.zeros_like(share))
        table_ref[pl.ds(first, tile), pl.ds(lane, lanes)] = total

    wait(3, 4, 5)
    owner = owner_of(mine_ref[...], owner_ref, rays, ray_count)
    padded = -(-ray_count // 16) * 16
    member = (lax.broadcasted_iota(jnp.int32, (padded, rays), 0) == owner)
    ranks = dot_nn(member.astype(F32).astype(BF16), earlier(rays))
    rank = jnp.sum(jnp.where(member, ranks, 0.0), axis=0, keepdims=True).astype(jnp.int32)
    if relative:
        chips = ray_count // 2
        shift = lax.div(owner, jnp.int32(2)) - lax.div(me, jnp.int32(2))
        shift = jnp.where(shift < 0, shift + chips, shift)
        flip = jnp.where(lax.rem(owner, jnp.int32(2)) == lax.rem(me, jnp.int32(2)), 0, 1)
        block = 2 * shift + flip
    else:
        block = owner
    slot = block * (rays // ray_count) + rank
    send_ref[...] = (
        (lax.broadcasted_iota(jnp.int32, (rays, rays), 0) == slot).astype(F32).astype(BF16)
    )

    piece = 256
    span = rays // len(outs)

    @pl.loop(0, width // piece)
    def _(step):
        cols = pl.ds(pl.multiple_of(step * piece, piece), piece)
        rendered = dot_tn(table_ref[...], features_ref[:, cols]).astype(BF16)
        ordered = dot_nn(send_ref[...], rendered).astype(BF16)
        for index, out in enumerate(outs):
            rows = ordered[index * span:(index + 1) * span]
            out[:, :, cols] = rows.reshape(*out.shape[:2], piece)


def render(ray_count, relative, me, owner, lists, opacity, counts, pixels, features):
    depth, rays = lists.shape
    gauss, width = features.shape
    parts = ray_count // 2 if relative else 1
    shape = jax.ShapeDtypeStruct((ray_count // parts, rays // ray_count, width), BF16)
    return pl.pallas_call(
        functools.partial(render_kernel, ray_count, relative),
        out_shape=(shape,) * parts,
        in_specs=[SMEM] + [HBM] * 6,
        out_specs=(VMEM,) * parts,
        scratch_shapes=[
            pltpu.VMEM(owner.shape, jnp.int32),
            pltpu.VMEM((depth, rays), jnp.int32),
            pltpu.VMEM((depth, rays), F32),
            pltpu.VMEM((1, rays), jnp.int32),
            pltpu.VMEM((1, rays), jnp.int32),
            pltpu.VMEM((gauss, width), BF16),
            pltpu.VMEM((depth, rays), F32),
            pltpu.VMEM((gauss, rays), BF16),
            pltpu.VMEM((rays, rays), BF16),
            pltpu.SemaphoreType.DMA((6,)),
        ],
        compiler_params=params(20),
        cost_estimate=COST,
        name="render",
    )(me, owner, lists, opacity, counts, pixels, features)


def tokens_kernel(
    ray_count, relative, me_ref, owner_hbm, pixels_hbm, tokens_hbm, gain_hbm,
    *refs,
):
    tokens_out, normed_out, normed_t_out = refs[-11:-8]
    owner_ref, pixels_ref, tokens_ref, gain_ref, order_ref, rank_ref, place_ref, sems = refs[-8:]
    rows, width = tokens_hbm.shape
    me = me_ref[0]
    each = rows // ray_count
    wait = fetch(
        [
            (owner_hbm, owner_ref), (pixels_hbm, pixels_ref), (gain_hbm, gain_ref),
            (tokens_hbm, tokens_ref),
        ],
        sems,
    )
    wait(0, 1)
    pixels = jnp.concatenate(
        [pixels_ref[:, sender * rows:(sender + 1) * rows] for sender in range(ray_count)], axis=0
    )
    mine = owner_of(pixels, owner_ref, rows, ray_count) == me
    place_ref[...] = lax.rem(pixels, jnp.int32(rows)).astype(F32)
    member = jnp.where(mine, 1.0, 0.0)
    padded = -(-ray_count // 16) * 16
    if padded > ray_count:
        spread = jnp.concatenate([member, jnp.zeros((padded - ray_count, rows), F32)], axis=0)
    else:
        spread = member
    ranks = dot_nn(spread.astype(BF16), earlier(rows))
    rank_ref[...] = jnp.where(mine, ranks[:ray_count], -1.0)
    chips = ray_count // 2
    for index in range(ray_count):
        if relative:
            chip = lax.rem(lax.div(me, jnp.int32(2)) + (chips - index // 2), jnp.int32(chips))
            sender = 2 * chip + jnp.bitwise_xor(lax.rem(me, jnp.int32(2)), index % 2)
        else:
            sender = index
        rank = rank_ref[pl.ds(sender, 1), :].astype(jnp.int32)
        hit = lax.broadcasted_iota(jnp.int32, (each, rows), 0) == rank
        at = jnp.sum(
            jnp.where(hit, place_ref[pl.ds(sender, 1), :], 0.0), axis=1, keepdims=True
        )
        here = lax.broadcasted_iota(jnp.int32, (each, rows), 1) == at.astype(jnp.int32)
        order_ref[pl.ds(index * each, each), :] = here.astype(F32).astype(BF16)
    wait(2, 3)
    half = min(128, rows)
    gain = gain_ref[...]

    @pl.loop(0, rows // half)
    def _(step):
        span = pl.ds(pl.multiple_of(step * half, half), half)
        values = dot_nn(order_ref[span, :], tokens_ref[...])
        tokens_out[span, :] = values.astype(BF16)
        centered = values - jnp.mean(values, axis=-1, keepdims=True)
        variance = jnp.mean(centered * centered, axis=-1, keepdims=True)
        xhat = centered * lax.rsqrt(variance + STABILITY_EPSILON)
        normed = (xhat * gain).astype(BF16)
        normed_out[span, :] = normed
        normed_t_out[:, span] = normed.T


def prepare_tokens(ray_count, relative, me, owner, pixels, tokens, gain, after=()):
    rows, width = tokens.shape
    return pl.pallas_call(
        functools.partial(tokens_kernel, ray_count, relative),
        out_shape=(
            jax.ShapeDtypeStruct((rows, width), BF16),
            jax.ShapeDtypeStruct((rows, width), BF16),
            jax.ShapeDtypeStruct((width, rows), BF16),
        ),
        in_specs=[SMEM] + [HBM] * 4 + [ANY] * len(after),
        out_specs=(VMEM, VMEM, VMEM),
        scratch_shapes=[
            pltpu.VMEM(owner.shape, jnp.int32),
            pltpu.VMEM(pixels.shape, jnp.int32),
            pltpu.VMEM((rows, width), BF16),
            pltpu.VMEM((1, width), F32),
            pltpu.VMEM((rows, rows), BF16),
            pltpu.VMEM((ray_count, rows), F32),
            pltpu.VMEM((ray_count, rows), F32),
            pltpu.SemaphoreType.DMA((4,)),
        ],
        compiler_params=params(20),
        cost_estimate=COST,
        name="tokens",
    )(me, owner, pixels, tokens, gain, *after)


def up_kernel(normed_ref, up_ref, act_ref, slope_ref):
    parts, _, part_rows, width = up_ref.shape
    up = up_ref[...].reshape(parts * part_rows, width)
    rows = normed_ref.shape[0]
    piece = min(128, rows)

    @pl.loop(0, rows // piece)
    def _(step):
        span = pl.ds(pl.multiple_of(step * piece, piece), piece)
        hidden = dot_nn(normed_ref[span, :], up)
        phi = 0.5 * (1.0 + lax.erf(hidden * (0.5 ** 0.5)))
        density = jnp.exp(-0.5 * hidden * hidden) * ((2.0 * jnp.pi) ** -0.5)
        act_ref[span, :] = (hidden * phi).astype(BF16)
        slope_ref[span, :] = (phi + hidden * density).astype(slope_ref.dtype)


def project_up(normed, up):
    rows, width = normed.shape
    parts, chunks, part_rows, chunk = up.shape
    return pl.pallas_call(
        up_kernel,
        grid=(chunks,),
        out_shape=(
            jax.ShapeDtypeStruct((rows, chunks * chunk), BF16),
            jax.ShapeDtypeStruct((rows, chunks * chunk), F32),
        ),
        in_specs=[
            pl.BlockSpec((rows, width), lambda j: (0, 0)),
            pl.BlockSpec((parts, 1, part_rows, chunk), lambda j: (0, j, 0, 0)),
        ],
        out_specs=(
            pl.BlockSpec((rows, chunk), lambda j: (0, j)),
            pl.BlockSpec((rows, chunk), lambda j: (0, j)),
        ),
        compiler_params=params(dimension_semantics=("arbitrary",)),
        cost_estimate=COST,
        name="up",
    )(normed, up)


def down_kernel(
    chunks, act_ref, down_ref, tokens_ref, target_ref, scale_ref,
    grad_ref, back_ref, small_ref, mixed_ref,
):
    step = pl.program_id(0)
    rows, width = tokens_ref.shape
    act = act_ref[...]

    @pl.when(step < chunks)
    def _():
        parts, _, part_rows, _ = down_ref.shape
        part = dot_nn(act, down_ref[...].reshape(parts * part_rows, width))

        @pl.when(step == 0)
        def _():
            mixed_ref[...] = part

        @pl.when(step > 0)
        def _():
            mixed_ref[...] += part

    @pl.when(step == chunks - 1)
    def _():
        scale = scale_ref[...]
        small_ref[...] = jnp.zeros_like(small_ref)
        piece = min(64, rows)

        @pl.loop(0, rows // piece)
        def _(index):
            span = pl.ds(pl.multiple_of(index * piece, piece), piece)
            mixed = mixed_ref[span, :]
            out = tokens_ref[span, :].astype(F32) + scale * mixed
            goal = target_ref[span, :].astype(F32)
            out_norm = jnp.sqrt(jnp.sum(out * out, axis=-1, keepdims=True) + STABILITY_EPSILON)
            goal_norm = jnp.sqrt(jnp.sum(goal * goal, axis=-1, keepdims=True) + STABILITY_EPSILON)
            norms = out_norm * goal_norm
            cosine = jnp.sum(out * goal, axis=-1, keepdims=True) / norms
            upstream = (cosine / (out_norm * out_norm)) * out - goal * (1.0 / norms)
            back_ref[span, :] = (upstream * scale).astype(BF16)
            small_ref[0:1, :] += jnp.sum(upstream * mixed, axis=0, keepdims=True)
            loss = jnp.sum(1.0 - cosine, axis=0, keepdims=True)
            small_ref[1:2, :] += jnp.broadcast_to(loss, (1, width))

    @pl.when(step >= chunks)
    def _():
        grad = dot_tn(act, back_ref[...])
        grad_ref[...] = grad.astype(BF16).reshape(grad_ref.shape)


def project_down(act, down, tokens, target, scale):
    rows, width = tokens.shape
    parts, chunks, part_rows, _ = down.shape
    chunk = parts * part_rows
    return pl.pallas_call(
        functools.partial(down_kernel, chunks),
        grid=(2 * chunks,),
        out_shape=(
            jax.ShapeDtypeStruct(down.shape, BF16),
            jax.ShapeDtypeStruct((rows, width), BF16),
            jax.ShapeDtypeStruct((8, width), F32),
        ),
        in_specs=[
            pl.BlockSpec((rows, chunk), lambda j: (0, lax.rem(j, chunks))),
            pl.BlockSpec(
                (parts, 1, part_rows, width), lambda j: (0, jnp.minimum(j, chunks - 1), 0, 0)
            ),
            pl.BlockSpec((rows, width), lambda j: (0, 0)),
            pl.BlockSpec((rows, width), lambda j: (0, 0)),
            pl.BlockSpec((1, width), lambda j: (0, 0)),
        ],
        out_specs=(
            pl.BlockSpec(
                (parts, 1, part_rows, width), lambda j: (0, jnp.maximum(j - chunks, 0), 0, 0)
            ),
            pl.BlockSpec((rows, width), lambda j: (0, 0)),
            pl.BlockSpec((8, width), lambda j: (0, 0)),
        ),
        scratch_shapes=[pltpu.VMEM((rows, width), F32)],
        compiler_params=params(dimension_semantics=("arbitrary",)),
        cost_estimate=COST,
        name="down",
    )(act, down, tokens, target, scale)


def back_kernel(back_ref, down_ref, slope_ref, normed_t_ref, up_ref, gain_ref, grad_ref, sum_ref):
    step = pl.program_id(0)
    parts, _, part_rows, width = down_ref.shape
    chunk = parts * part_rows
    rows = back_ref.shape[0]
    back_act = dot_nt(back_ref[...], down_ref[...].reshape(chunk, width))
    back_hidden = (back_act * slope_ref[...]).astype(BF16)
    up_parts, _, up_rows, _ = up_ref.shape

    @pl.when(step == 0)
    def _():
        sum_ref[...] = jnp.zeros_like(sum_ref)

    grad = dot_nn(normed_t_ref[...], back_hidden)
    grad_ref[...] = grad.astype(BF16).reshape(grad_ref.shape)
    up = up_ref[...].reshape(up_parts * up_rows, chunk).astype(F32)
    sum_ref[...] += jnp.sum(grad * up, axis=1, keepdims=True) / gain_ref[...]


def back_up(back, down, slope, normed_t, up, gain):
    width, rows = normed_t.shape
    parts, chunks, part_rows, _ = down.shape
    chunk = parts * part_rows
    up_parts, _, up_rows, _ = up.shape
    return pl.pallas_call(
        back_kernel,
        grid=(chunks,),
        out_shape=(
            jax.ShapeDtypeStruct(up.shape, BF16),
            jax.ShapeDtypeStruct((width, 1), F32),
        ),
        in_specs=[
            pl.BlockSpec((rows, width), lambda j: (0, 0)),
            pl.BlockSpec((parts, 1, part_rows, width), lambda j: (0, j, 0, 0)),
            pl.BlockSpec((rows, chunk), lambda j: (0, j)),
            pl.BlockSpec((width, rows), lambda j: (0, 0)),
            pl.BlockSpec((up_parts, 1, up_rows, chunk), lambda j: (0, j, 0, 0)),
            pl.BlockSpec((width, 1), lambda j: (0, 0)),
        ],
        out_specs=(
            pl.BlockSpec((up_parts, 1, up_rows, chunk), lambda j: (0, j, 0, 0)),
            pl.BlockSpec((width, 1), lambda j: (0, 0)),
        ),
        compiler_params=params(dimension_semantics=("arbitrary",)),
        cost_estimate=COST,
        name="back",
    )(back, down, slope, normed_t, up, gain)


def gather_weight(weight, parts, group, group_count, ray_count):
    rows, cols = weight.shape
    if parts == 1:
        whole = lax.all_gather(weight, "ray", axis=0, tiled=True)
    else:
        part = lax.dynamic_slice_in_dim(weight, group * (rows // parts), rows // parts, 0)
        whole = lax.all_gather(part, ("grp", "ray"), axis=0, tiled=True)
    return whole.reshape(parts, ray_count, rows // parts, cols)


def reduce_gradient(grad):
    parts, ray_count, part_rows, cols = grad.shape
    flat = grad.reshape(parts * ray_count * part_rows, cols)
    if parts == 1:
        share = lax.psum_scatter(flat, "ray", scatter_dimension=0, tiled=True)
        return lax.psum(share.astype(F32), "grp")
    share = lax.psum_scatter(flat, "grp", scatter_dimension=0, tiled=True)
    share = lax.psum_scatter(share, "ray", scatter_dimension=0, tiled=True)
    return lax.all_gather(share, "grp", axis=0, tiled=True).astype(F32)


def shards_general(
    image_tokens,
    tile_lists,
    opacity,
    tile_counts,
    ray_pixel,
    block_owner,
    gaussian_features,
    layer_norm_gain,
    layer_scale,
    up_weight,
    down_weight,
):
    ray_count = lax.axis_size("ray")
    group_count = lax.axis_size("grp")
    group = lax.axis_index("grp")
    me = lax.axis_index("ray").reshape(1)
    rows, width = image_tokens.shape
    up_parts = group_count if up_weight.shape[0] % (16 * group_count) == 0 else 1
    down_parts = group_count if down_weight.shape[0] % (16 * group_count) == 0 else 1
    up = gather_weight(up_weight, up_parts, group, group_count, ray_count)
    down = gather_weight(down_weight, down_parts, group, group_count, ray_count)
    rendered = render(
        ray_count, False, me, block_owner, tile_lists, opacity, tile_counts.reshape(1, rows),
        ray_pixel, gaussian_features,
    )
    rendered = rendered[0].reshape(rows, width)
    target = lax.all_to_all(rendered, "ray", split_axis=0, concat_axis=0, tiled=True)
    tokens, normed, normed_t = prepare_tokens(
        ray_count, False, me, block_owner, ray_pixel, image_tokens,
        layer_norm_gain.reshape(1, width),
    )
    act, slope = project_up(normed, up)
    grad_down, back, small = project_down(act, down, tokens, target, layer_scale.reshape(1, width))
    grad_up, gain_sum = back_up(back, down, slope, normed_t, up, layer_norm_gain.reshape(width, 1))
    grad_down = reduce_gradient(grad_down)
    grad_up = reduce_gradient(grad_up)
    sums = jnp.concatenate([gain_sum.reshape(1, width), small[:2]], axis=0)
    sums = lax.psum(sums, ("grp", "ray"))
    loss = sums[2, 0] / (rows * ray_count * group_count)
    return (grad_up, grad_down, sums[0], sums[1], loss)


def quarter_kernel(group_ref, up_hbm, down_hbm, out_ref, up_ref, turned_ref, sems):
    part = out_ref.shape[1]
    lanes = up_ref.shape[1]
    start = pl.multiple_of(group_ref[0] * part, part)
    lane = pl.multiple_of(lax.div(start, jnp.int32(lanes)) * lanes, lanes)
    wait = fetch(
        [
            (up_hbm.at[:, pl.ds(lane, lanes)], up_ref),
            (down_hbm.at[pl.ds(start, part), :], out_ref.at[1]),
        ],
        sems,
    )
    wait(0)
    turned_ref[...] = up_ref[...].T
    out_ref[0] = turned_ref[pl.ds(pl.multiple_of(start - lane, part), part), :]
    wait(1)


def own_quarter(group, up, down, part):
    width, chunk = up.shape
    lanes = max(128, part)
    return pl.pallas_call(
        quarter_kernel,
        out_shape=jax.ShapeDtypeStruct((2, part, width), BF16),
        in_specs=[SMEM, HBM, HBM],
        out_specs=VMEM,
        scratch_shapes=[
            pltpu.VMEM((width, lanes), BF16),
            pltpu.VMEM((lanes, width), BF16),
            pltpu.SemaphoreType.DMA((2,)),
        ],
        compiler_params=params(16),
        cost_estimate=LONG,
        name="quarter",
    )(group, up, down)


def own_rows_kernel(group_ref, up_ref, down_ref, out_ref, turned_ref):
    part = out_ref.shape[2]
    turned_ref[...] = up_ref[...].T
    for index in range(4):
        quarter = jnp.bitwise_xor(group_ref[0], index)
        span = pl.ds(pl.multiple_of(quarter * part, part), part)
        out_ref[index, 0] = turned_ref[span, :]
        out_ref[index, 1] = down_ref[span, :]


def own_rows(group, up, down):
    width, chunk = up.shape
    return pl.pallas_call(
        own_rows_kernel,
        out_shape=jax.ShapeDtypeStruct((4, 2, chunk // 4, width), BF16),
        in_specs=[SMEM, VMEM, VMEM],
        out_specs=VMEM,
        scratch_shapes=[pltpu.VMEM((chunk, width), BF16)],
        compiler_params=params(16),
        cost_estimate=COST,
        name="own_rows",
    )(group, up, down)


def finish_rows(tokens, mixed, goal, scale):
    out = tokens + scale * mixed
    out_norm = jnp.sqrt(jnp.sum(out * out, axis=-1, keepdims=True) + STABILITY_EPSILON)
    goal_norm = jnp.sqrt(jnp.sum(goal * goal, axis=-1, keepdims=True) + STABILITY_EPSILON)
    norms = out_norm * goal_norm
    cosine = jnp.sum(out * goal, axis=-1, keepdims=True) / norms
    upstream = (cosine / (out_norm * out_norm)) * out - goal * (1.0 / norms)
    return upstream, 1.0 - cosine


def forward_kernel(first, blocks, sides, skipped, *refs):
    last = blocks > 0
    refs = list(refs[skipped:])
    normed_t_ref = refs.pop(0)
    own, other = refs[:sides], refs[sides:2 * sides]
    del refs[:2 * sides]
    mixed_in = None if first else refs.pop(0)
    if last:
        tokens_ref, scale_ref = refs[:2]
        targets, passed_ref = refs[2:2 + blocks], refs[2 + blocks]
        del refs[:3 + blocks]
    act_ref, slope_ref = refs[:2]
    del refs[:2]
    width, rows = normed_t_ref.shape
    part = act_ref.shape[2]
    part_sum = None
    downs = []
    for side, group in enumerate((own, other)):
        start = 0
        for ref in group:
            count = ref.shape[0]
            hiddens = dot_nn(ref[:, 0].reshape(count * part, width), normed_t_ref[...])
            for index in range(count):
                hidden = hiddens[index * part:(index + 1) * part]
                phi = 0.5 * (1.0 + lax.erf(hidden * (0.5 ** 0.5)))
                density = jnp.exp(-0.5 * hidden * hidden) * ((2.0 * jnp.pi) ** -0.5)
                act_ref[side, start + index] = (hidden * phi).astype(BF16)
                slope_ref[side, start + index] = phi + hidden * density
            downs.append(ref[:, 1].reshape(count * part, width))
            start += count
    if sides > 1 or last:
        act = act_ref[...].reshape(2 * start * part, rows)
        part_sum = dot_tn(act, jnp.concatenate(downs, axis=0))
    else:
        for side, down in enumerate(downs):
            term = dot_tn(act_ref[side].reshape(start * part, rows), down)
            part_sum = term if part_sum is None else part_sum + term
    if not last:
        mixed_out = refs[0]
        mixed_out[...] = part_sum if first else mixed_in[...] + part_sum
        return
    back_ref, back_t_ref, small_ref, mixed_ref = refs
    mixed_ref[...] = mixed_in[...] + part_sum
    scale = scale_ref[...]
    small_ref[...] = jnp.zeros_like(small_ref)
    piece = rows // blocks
    for index, target_ref in enumerate(targets):
        span = pl.ds(index * piece, piece)
        mixed = mixed_ref[span, :]
        goal = jnp.concatenate([target_ref[0], passed_ref[index]], axis=0).astype(F32)
        upstream, loss = finish_rows(tokens_ref[span, :].astype(F32), mixed, goal, scale)
        back = (upstream * scale).astype(BF16)
        back_ref[span, :] = back
        back_t_ref[:, span] = back.T
        small_ref[0:1, :] += jnp.sum(upstream * mixed, axis=0, keepdims=True)
        small_ref[1:2, :] += jnp.broadcast_to(jnp.sum(loss, axis=0, keepdims=True), (1, width))


def forward(normed_t, own, other, mixed=None, finish=None, after=()):
    width, rows = normed_t.shape
    part = own[0].shape[2]
    total = sum(array.shape[0] for array in own)
    first, last = mixed is None, finish is not None
    blocks = len(finish) - 3 if last else 0
    operands = [*after, normed_t, *own, *other]
    if not first:
        operands.append(mixed)
    if last:
        operands.extend(finish)
    piece = (2, total, part, rows)
    shapes = [jax.ShapeDtypeStruct(piece, BF16), jax.ShapeDtypeStruct(piece, F32)]
    scratch = []
    if last:
        shapes += [
            jax.ShapeDtypeStruct((rows, width), BF16),
            jax.ShapeDtypeStruct((width, rows), BF16),
            jax.ShapeDtypeStruct((8, width), F32),
        ]
        scratch = [pltpu.VMEM((rows, width), F32)]
    else:
        shapes += [jax.ShapeDtypeStruct((rows, width), F32)]
    return pl.pallas_call(
        functools.partial(forward_kernel, first, blocks, len(own), len(after)),
        out_shape=tuple(shapes),
        in_specs=[ANY] * len(after) + [VMEM] * (len(operands) - len(after)),
        out_specs=tuple([VMEM] * len(shapes)),
        scratch_shapes=scratch,
        compiler_params=params(32),
        cost_estimate=COST,
        name="forward",
    )(*operands)


def pack_kernel(counts, *refs):
    out_ref = refs[-1]
    start = 0
    for count, ref in zip(counts, refs):
        out_ref[start:start + count] = ref[...].reshape(count, *out_ref.shape[1:])
        start += count


def pack(pieces, *after):
    counts = [1 if piece.ndim == 3 else piece.shape[0] for piece in pieces]
    return pl.pallas_call(
        functools.partial(pack_kernel, counts),
        out_shape=jax.ShapeDtypeStruct((sum(counts), *pieces[0].shape[-3:]), BF16),
        in_specs=[VMEM] * len(pieces) + [ANY] * len(after),
        out_specs=VMEM,
        compiler_params=params(16),
        cost_estimate=COST,
        name="pack",
    )(*pieces, *after)


def turn_kernel(y_ref, x_ref, a_ref, b_ref):
    count = a_ref.shape[0]
    a_ref[...] = y_ref[:count]
    b_ref[...] = x_ref[count:]


def turn(y, x):
    count = y.shape[0]
    first = count // 2
    return pl.pallas_call(
        turn_kernel,
        out_shape=(
            jax.ShapeDtypeStruct((first, *y.shape[1:]), BF16),
            jax.ShapeDtypeStruct((count - first, *y.shape[1:]), BF16),
        ),
        in_specs=[VMEM] * 2,
        out_specs=(VMEM, VMEM),
        compiler_params=params(16),
        cost_estimate=COST,
        name="turn",
    )(y, x)


def tie_kernel(*refs):
    pass


def tie(array, *after):
    return pl.pallas_call(
        tie_kernel,
        out_shape=jax.ShapeDtypeStruct(array.shape, array.dtype),
        in_specs=[ANY] * (1 + len(after)),
        out_specs=ANY,
        input_output_aliases={0: 0},
        compiler_params=params(4),
        cost_estimate=COST,
        name="tie",
    )(array, *after)


def seconds_kernel(*refs):
    for index, ref in enumerate(refs[:-1]):
        refs[-1][index] = ref[1]


def seconds(blocks):
    count, (_, each, width) = len(blocks), blocks[0].shape
    return pl.pallas_call(
        seconds_kernel,
        out_shape=jax.ShapeDtypeStruct((count, each, width), BF16),
        in_specs=[VMEM] * count,
        out_specs=VMEM,
        compiler_params=params(16),
        cost_estimate=COST,
        name="seconds",
    )(*blocks)


def joined(refs, pieces, pick):
    values = [pick(refs[which], start, count) for which, start, count in pieces]
    flat = [value.reshape(-1, value.shape[-1]) for value in values]
    return flat[0] if len(flat) == 1 else jnp.concatenate(flat, axis=0)


def put(quarter, value, outs):
    own_ref, x_ref, y_ref, x_later_ref, y_later_ref = outs
    value = value.astype(BF16).reshape(own_ref.shape)
    half = x_ref.shape[0] // 2
    if quarter == 0:
        own_ref[...] = value
    elif quarter == 1:
        x_ref[half:] = value[:half]
        x_later_ref[...] = value[half:]
    elif quarter == 2:
        y_ref[half:] = value[half:]
        y_later_ref[...] = value[:half]
    else:
        x_ref[:half] = value[:half]
        y_ref[:half] = value[half:]


def emit(quarter, value, arrived, outs):
    if arrived is None:
        outs[0][quarter] = value.astype(BF16).reshape(outs[0].shape[1:])
    else:
        put(quarter, value + arrived[quarter].reshape(value.shape).astype(F32), outs)


def down_grad_kernel(side, act_pieces, add, *refs):
    acts, back_ref = refs[:2], refs[2]
    arrived = refs[3] if add else None
    outs = refs[4:] if add else refs[3:]
    for quarter in (3, 1, 2, 0):
        act = joined(acts, act_pieces[quarter], lambda ref, a, n: ref[side, a:a + n])
        emit(quarter, dot_nn(act, back_ref[...]), arrived, outs)


def up_grad_kernel(side, weight_pieces, act_pieces, add, *refs):
    weights, slopes = refs[:2], refs[2:4]
    back_t_ref, normed_ref, gain_in = refs[4:7]
    if add:
        arrived, scale_ref, small_ref = refs[7:10]
        outs, vector_ref, gain_ref = refs[10:-2], refs[-2], refs[-1]
    else:
        arrived = None
        outs, gain_ref = refs[7:-1], refs[-1]
    gain_ref[...] = gain_in[...]
    for quarter in (3, 1, 2, 0):
        pieces = weight_pieces[quarter]
        slope = joined(slopes, act_pieces[quarter], lambda ref, a, n: ref[side, a:a + n])
        back_act = dot_nn(joined(weights, pieces, lambda ref, a, n: ref[a:a + n, 1]), back_t_ref[...])
        back_hidden = (back_act * slope).astype(BF16)
        grad = dot_nn(back_hidden, normed_ref[...])
        up = joined(weights, pieces, lambda ref, a, n: ref[a:a + n, 0]).astype(F32)
        gain_ref[...] += jnp.sum(grad * up, axis=0, keepdims=True)
        emit(quarter, grad, arrived, outs)
    if add:
        vector_ref[0:1, :] = gain_ref[...] / scale_ref[...]
        vector_ref[1:3, :] = small_ref[0:2, :]
        vector_ref[3:8, :] = jnp.zeros((5, gain_ref.shape[1]), F32)


def gradient_shapes(depth, part, width, add):
    if not add:
        return [jax.ShapeDtypeStruct((4, depth, part, width), BF16)]
    counts = (depth, depth, depth, depth - depth // 2, depth // 2)
    return [jax.ShapeDtypeStruct((count, part, width), BF16) for count in counts]


def down_gradient(side, act_pieces, depth, acts, back, arrived=None):
    part = acts[0].shape[2]
    width = back.shape[1]
    add = arrived is not None
    operands = [*acts, back] + ([arrived] if add else [])
    shapes = gradient_shapes(depth, part, width, add)
    return pl.pallas_call(
        functools.partial(down_grad_kernel, side, act_pieces, add),
        out_shape=tuple(shapes),
        in_specs=[VMEM] * len(operands),
        out_specs=tuple([VMEM] * len(shapes)),
        compiler_params=params(20),
        cost_estimate=COST,
        name="down_gradient",
    )(*operands)


def up_gradient(
    side, weight_pieces, act_pieces, depth, weights, slopes, back_t, normed, gain, extra=()
):
    part, width = weights[0].shape[2:]
    add = len(extra) > 0
    operands = [*weights, *slopes, back_t, normed, gain, *extra]
    shapes = gradient_shapes(depth, part, width, add)
    if add:
        shapes.append(jax.ShapeDtypeStruct((8, width), F32))
        scratch = [pltpu.VMEM((1, width), F32)]
    else:
        scratch = []
        shapes.append(jax.ShapeDtypeStruct((1, width), F32))
    return pl.pallas_call(
        functools.partial(up_grad_kernel, side, weight_pieces, act_pieces, add),
        out_shape=tuple(shapes),
        in_specs=[VMEM] * len(operands),
        out_specs=tuple([VMEM] * len(shapes)),
        scratch_shapes=scratch,
        compiler_params=params(24),
        cost_estimate=COST,
        name="up_gradient",
    )(*operands)


def merge_kernel(x_ref, y_ref, x_later_ref, y_later_ref, *refs):
    x_out, y_out = refs[-2:]
    half = y_later_ref.shape[0]
    x_out[...] = (x_later_ref[...].astype(F32) + y_ref[:half].astype(F32)).astype(BF16)
    y_out[...] = (y_later_ref[...].astype(F32) + x_ref[:half].astype(F32)).astype(BF16)


def merge(x, y, x_later, y_later, *after):
    return pl.pallas_call(
        merge_kernel,
        out_shape=tuple(jax.ShapeDtypeStruct(a.shape, BF16) for a in (x_later, y_later)),
        in_specs=[VMEM] * 4 + [ANY] * len(after),
        out_specs=(VMEM, VMEM),
        compiler_params=params(16),
        cost_estimate=COST,
        name="merge",
    )(x, y, x_later, y_later, *after)


def total_kernel(own_ref, x_ref, y_ref, x_late_ref, y_late_ref, *refs):
    outs = refs[-own_ref.shape[0]:]
    half = y_late_ref.shape[0]
    for index, out in enumerate(outs):
        total = own_ref[index].astype(F32)
        if index < half:
            total += x_ref[half + index].astype(F32) + y_late_ref[index].astype(F32)
        else:
            total += y_ref[index].astype(F32) + x_late_ref[index - half].astype(F32)
        out[...] = total.astype(BF16)


def totals(own, x, y, x_late, y_late, *after):
    count, part, width = own.shape
    return pl.pallas_call(
        total_kernel,
        out_shape=tuple([jax.ShapeDtypeStruct((part, width), BF16)] * count),
        in_specs=[VMEM] * 5 + [ANY] * len(after),
        out_specs=tuple([VMEM] * count),
        compiler_params=params(16),
        cost_estimate=COST,
        name="totals",
    )(own, x, y, x_late, y_late, *after)


def collect_kernel(count, *refs):
    total = refs[0][...].astype(F32)
    for ref in refs[1:count]:
        total = total + ref[...].astype(F32)
    refs[-1][...] = total.astype(BF16)


def collect(parts, *after):
    return pl.pallas_call(
        functools.partial(collect_kernel, len(parts)),
        out_shape=jax.ShapeDtypeStruct(parts[0].shape, BF16),
        in_specs=[VMEM] * len(parts) + [ANY] * len(after),
        out_specs=VMEM,
        compiler_params=params(16),
        cost_estimate=COST,
        name="collect",
    )(*parts, *after)


def join_kernel(total_ref, vector_ref, other_ref, *refs):
    short_ref, long_ref, held_ref = refs[-3:]
    part = total_ref.shape[0]
    short_ref[pl.ds(0, part), :] = total_ref[...]
    rest = vector_ref[0:3, :]
    held_ref[...] = jnp.zeros_like(held_ref)
    for index in range(3):
        piece = rest.astype(BF16).astype(F32)
        held_ref[3 * index:3 * index + 3, :] = piece
        rest = rest - piece
    short_ref[pl.ds(part, 16), :] = held_ref[...].astype(BF16)
    long_ref[pl.ds(0, part + 16), :] = short_ref[...]
    long_ref[pl.ds(part + 16, part), :] = other_ref[...]


def join(total, vector, other, *after):
    part, width = total.shape
    return pl.pallas_call(
        join_kernel,
        out_shape=tuple(
            jax.ShapeDtypeStruct((rows, width), BF16) for rows in (part + 16, 2 * part + 16)
        ),
        in_specs=[VMEM] * 3 + [ANY] * len(after),
        out_specs=(VMEM, VMEM),
        scratch_shapes=[pltpu.VMEM((16, width), F32)],
        compiler_params=params(16),
        cost_estimate=COST,
        name="join",
    )(total, vector, other, *after)


def place_kernel(part, tokens, group_ref, *refs):
    ups, downs = refs[:4], refs[4:8]
    up_ref, down_ref, gain_ref, scale_ref, loss_ref, held_ref = refs[8:]
    group = group_ref[0]
    vectors = []
    for index, (up, down) in enumerate(zip(ups, downs)):
        first = pl.multiple_of(jnp.bitwise_xor(group, index) * part, part)
        held_ref[pl.ds(first, part), :] = up[pl.ds(0, part), :].astype(F32)
        start = down.shape[0] - part
        down_ref[pl.ds(first, part), :] = down[pl.ds(start, part), :].astype(F32)
        rows = up[pl.ds(part, 16), :].astype(F32)
        vectors.append((rows[0:3] + rows[3:6]) + rows[6:9])
    up_ref[...] = held_ref[...].T
    vector = (vectors[0] + vectors[1]) + (vectors[2] + vectors[3])
    gain_ref[...] = vector[0:1]
    scale_ref[...] = vector[1:2]
    loss_ref[...] = vector[2:3, 0:1] * (1.0 / tokens)


def place_quarters(group, ups, downs, part, tokens):
    width = ups[0].shape[1]
    shapes = [
        jax.ShapeDtypeStruct((width, 4 * part), F32),
        jax.ShapeDtypeStruct((4 * part, width), F32),
        jax.ShapeDtypeStruct((1, width), F32),
        jax.ShapeDtypeStruct((1, width), F32),
        jax.ShapeDtypeStruct((1, 1), F32),
    ]
    return pl.pallas_call(
        functools.partial(place_kernel, part, tokens),
        out_shape=tuple(shapes),
        in_specs=[SMEM] + [VMEM] * 8,
        out_specs=tuple([VMEM] * len(shapes)),
        scratch_shapes=[pltpu.VMEM((4 * part, width), F32)],
        compiler_params=params(16),
        cost_estimate=COST,
        name="place",
    )(group, *ups, *downs)


def shards_square(
    image_tokens,
    tile_lists,
    opacity,
    tile_counts,
    ray_pixel,
    block_owner,
    gaussian_features,
    layer_norm_gain,
    layer_scale,
    up_weight,
    down_weight,
):
    ray_count = lax.axis_size("ray")
    group_count = lax.axis_size("grp")
    depth = ray_count // 2
    group = lax.axis_index("grp").reshape(1)
    me = lax.axis_index("ray").reshape(1)
    rows, width = image_tokens.shape
    part = down_weight.shape[0] // group_count

    def beside(array, flip):
        return lax.ppermute(array, "grp", [(g, g ^ flip) for g in range(group_count)])

    def partner(array, flip=1):
        return lax.ppermute(array, "ray", [(r, r ^ flip) for r in range(ray_count)])

    def along(array, shift):
        pairs = [(r, (r + 2 * shift) % ray_count) for r in range(ray_count)]
        return lax.ppermute(array, "ray", pairs)

    mine = own_quarter(group, up_weight, down_weight, part)
    arrivals = [along(mine, -shift) for shift in range(1, depth)]
    rendered = render(
        ray_count, True, me, block_owner, tile_lists, opacity, tile_counts.reshape(1, rows),
        ray_pixel, gaussian_features,
    )
    half = depth // 2
    low = pack(arrivals[:half - 1], rendered[0])
    x_low, y_low = beside(low, 1), beside(low, 2)
    high, x_high, y_high, last_sent = [], [], [], (x_low, y_low)
    for arrival in arrivals[half - 1:]:
        arrival = tie(arrival, *last_sent)
        last_sent = (arrival,)
        high.append(arrival)
        x_high.append(beside(arrival, 1))
        y_high.append(beside(arrival, 2))
    targets = [rendered[0]] + [along(rendered[shift], shift) for shift in range(1, depth)]
    tokens, normed, normed_t = prepare_tokens(
        ray_count, True, me, block_owner, ray_pixel, image_tokens,
        layer_norm_gain.reshape(1, width),
    )
    most = pack(
        [own_rows(group, up_weight, down_weight), low, x_low, y_low, *high, *x_high, *y_high],
        targets[half], normed,
    )
    most_other = partner(most)
    d_low, d_high = beside(y_low, 1), beside(pack(x_high), 2)
    act_most, slope_most, mixed = forward(normed_t, [most], [most_other])
    late = [target for shift, target in enumerate(targets) if shift not in (0, half)]
    last = pack([d_low, d_high], mixed, *late)
    last_other = partner(last)
    act_last, slope_last, back, back_t, small = forward(
        normed_t, [last], [last_other], mixed,
        (tokens, layer_scale.reshape(1, width), *targets, partner(seconds(targets))),
    )
    acts, slopes = (act_most, act_last), (slope_most, slope_last)
    weights = ((most, last), (most_other, last_other))
    count, rest = half - 1, depth - half
    start = 4 + 3 * count
    pieces = tuple(
        ((0, q, 1), (0, 4 + q * count, count), (0, start + q * rest, rest)) for q in range(3)
    ) + (((0, 3, 1), (1, 0, depth - 1)),)
    gain = jnp.zeros((1, width), F32)
    (down_other,) = down_gradient(1, pieces, depth, acts, back)
    down_arrived = partner(down_other)
    up_other, gain = up_gradient(
        1, pieces, pieces, depth, weights[1], slopes, back_t, normed, gain
    )
    up_arrived = partner(up_other)
    down_sums = down_gradient(0, pieces, depth, acts, back, down_arrived)
    *up_sums, vector = up_gradient(
        0, pieces, pieces, depth, weights[0], slopes, back_t, normed, gain,
        (up_arrived, layer_norm_gain.reshape(1, width), small),
    )
    vector = vector + partner(vector)
    flip = 2
    while flip < ray_count:
        vector = vector + partner(vector, flip)
        flip *= 2

    def first_step(to_x, to_y, x_later, y_later, *after):
        from_x, from_y = beside(to_x, 1), beside(to_y, 2)
        return from_x, from_y, merge(from_x, from_y, x_later, y_later, *after)

    def second_step(later):
        return beside(later[0], 1), beside(later[1], 2)

    def arrive_along(shares):
        return [shares[0]] + [along(shares[shift], shift) for shift in range(1, depth)]

    own, *rest = down_sums
    own_up, to_x, to_y, *rest_up = up_sums
    from_x, from_y, later = first_step(*rest, vector)
    late = second_step(later)
    shares = totals(own, from_x, from_y, *late)
    from_x, from_y, later = first_step(to_x, to_y, *rest_up)
    up_shares = totals(own_up, from_x, from_y, *second_step(later))
    down_total = collect(arrive_along(shares), up_shares[0])
    down_x, down_y = beside(down_total, 1), beside(down_total, 2)
    up_total = collect(arrive_along(up_shares))
    short, long = join(up_total, vector, down_total, down_x, down_y)
    up_x, up_y, both = beside(short, 1), beside(short, 2), beside(long, 3)
    grad_up, grad_down, gain, scale, loss = place_quarters(
        group, (short, up_x, up_y, both), (down_total, down_x, down_y, both), part,
        rows * ray_count * group_count,
    )
    return (grad_up, grad_down, gain.reshape(width), scale.reshape(width), loss.reshape(()))


def shards(*operands):
    ray_count, group_count = lax.axis_size("ray"), lax.axis_size("grp")
    hidden = operands[-1].shape[0]
    square = group_count == 4 and ray_count in (8, 16) and hidden % (16 * group_count) == 0
    return (shards_square if square else shards_general)(*operands)


def solution(mesh):
    return jax.shard_map(
        shards,
        mesh=mesh,
        in_specs=(
            P(("grp", "ray"), None),
            P(None, ("grp", "ray")),
            P(None, ("grp", "ray")),
            P(("grp", "ray")),
            P("grp", None),
            P("grp", None),
            P(("grp", "ray"), None),
            P(),
            P(),
            P(None, "ray"),
            P("ray", None),
        ),
        out_specs=(P(None, "ray"), P("ray", None), P(), P(), P()),
        check_vma=False,
    )
```

```python
import functools

import jax
import jax.numpy as jnp
from jax import lax
from jax.experimental import pallas as pl
from jax.experimental.pallas import tpu as pltpu
from jax.sharding import PartitionSpec as P

STABILITY_EPSILON = 1e-06
F32 = jnp.float32
BF16 = jnp.bfloat16
MIB = 1024 * 1024
COST = pl.CostEstimate(flops=1 << 20, bytes_accessed=1 << 16, transcendentals=0)
LONG = pl.CostEstimate(flops=10**10, bytes_accessed=1 << 20, transcendentals=0)
SMEM = pl.BlockSpec(memory_space=pltpu.SMEM)
VMEM = pl.BlockSpec(memory_space=pltpu.VMEM)
ANY = pl.BlockSpec(memory_space=pl.ANY)


def params(mib=48, **more):
    return pltpu.CompilerParams(vmem_limit_bytes=mib * MIB, **more)


def dot_nn(a, b):
    return lax.dot_general(a, b, (((1,), (0,)), ((), ())), preferred_element_type=F32)


def dot_tn(a, b):
    return lax.dot_general(a, b, (((0,), (0,)), ((), ())), preferred_element_type=F32)


def dot_nt(a, b):
    return lax.dot_general(a, b, (((1,), (1,)), ((), ())), preferred_element_type=F32)


def owner_of(pixels, owner_ref, rows, count):
    block = lax.div(pixels, jnp.int32(rows))
    owner = jnp.zeros_like(pixels)
    for slot in range(count):
        owner = jnp.where(block == slot, owner_ref[0:1, slot:slot + 1], owner)
    return owner


def earlier(rows):
    before = lax.broadcasted_iota(jnp.int32, (rows, rows), 0)
    after = lax.broadcasted_iota(jnp.int32, (rows, rows), 1)
    return jnp.where(before < after, 1.0, 0.0).astype(BF16)


HBM = pl.BlockSpec(memory_space=pltpu.HBM)


def fetch(copies, sems):
    started = [
        pltpu.make_async_copy(source, target, sems.at[index])
        for index, (source, target) in enumerate(copies)
    ]
    for copy in started:
        copy.start()

    def wait(*numbers):
        for number in numbers:
            started[number].wait()

    return wait


def render_kernel(
    ray_count, relative, me_ref, owner_hbm, lists_hbm, opacity_hbm, counts_hbm, pixels_hbm,
    features_hbm, *refs,
):
    outs = refs[:-10]
    owner_ref, ids_ref, opacity_ref, counts_ref, mine_ref, features_ref = refs[-10:-4]
    share_ref, table_ref, send_ref, sems = refs[-4:]
    depth, rays = lists_hbm.shape
    gauss = features_hbm.shape[0]
    width = features_hbm.shape[1]
    me = me_ref[0]
    own_pixels = pixels_hbm.at[:, pl.ds(pl.multiple_of(me * rays, rays), rays)]
    wait = fetch(
        [
            (lists_hbm, ids_ref), (opacity_hbm, opacity_ref), (counts_hbm, counts_ref),
            (owner_hbm, owner_ref), (own_pixels, mine_ref), (features_hbm, features_ref),
        ],
        sems,
    )
    wait(0, 1, 2)
    ids_ref[...] = ids_ref[...] - me * gauss
    passing = jnp.ones((1, rays), F32)
    counts = counts_ref[...]
    for level in range(depth):
        alpha = opacity_ref[pl.ds(level, 1), :]
        share_ref[pl.ds(level, 1), :] = jnp.where(level < counts, alpha * passing, 0.0)
        passing = passing * (1.0 - alpha)

    tile = 256
    lanes = 128
    columns = rays // lanes

    @pl.loop(0, (gauss // tile) * columns)
    def _(step):
        first = pl.multiple_of(lax.div(step, columns) * tile, tile)
        lane = pl.multiple_of(lax.rem(step, columns) * lanes, lanes)
        number = (lax.broadcasted_iota(jnp.int32, (tile, lanes), 0) + first).astype(jnp.int16)
        total = jnp.zeros((tile, lanes), BF16)
        for level in range(depth):
            ident = jnp.broadcast_to(ids_ref[pl.ds(level, 1), pl.ds(lane, lanes)], (16, lanes))
            share = jnp.broadcast_to(share_ref[pl.ds(level, 1), pl.ds(lane, lanes)], (16, lanes))
            ident = jnp.concatenate([ident.astype(jnp.int16)] * (tile // 16), axis=0)
            share = jnp.concatenate([share.astype(BF16)] * (tile // 16), axis=0)
            total = total + jnp.where(ident == number, share, jnp.zeros_like(share))
        table_ref[pl.ds(first, tile), pl.ds(lane, lanes)] = total

    wait(3, 4, 5)
    owner = owner_of(mine_ref[...], owner_ref, rays, ray_count)
    padded = -(-ray_count // 16) * 16
    member = (lax.broadcasted_iota(jnp.int32, (padded, rays), 0) == owner)
    ranks = dot_nn(member.astype(F32).astype(BF16), earlier(rays))
    rank = jnp.sum(jnp.where(member, ranks, 0.0), axis=0, keepdims=True).astype(jnp.int32)
    if relative:
        chips = ray_count // 2
        shift = lax.div(owner, jnp.int32(2)) - lax.div(me, jnp.int32(2))
        shift = jnp.where(shift < 0, shift + chips, shift)
        flip = jnp.where(lax.rem(owner, jnp.int32(2)) == lax.rem(me, jnp.int32(2)), 0, 1)
        block = 2 * shift + flip
    else:
        block = owner
    slot = block * (rays // ray_count) + rank
    send_ref[...] = (
        (lax.broadcasted_iota(jnp.int32, (rays, rays), 0) == slot).astype(F32).astype(BF16)
    )

    piece = 256
    span = rays // len(outs)

    @pl.loop(0, width // piece)
    def _(step):
        cols = pl.ds(pl.multiple_of(step * piece, piece), piece)
        rendered = dot_tn(table_ref[...], features_ref[:, cols]).astype(BF16)
        ordered = dot_nn(send_ref[...], rendered).astype(BF16)
        for index, out in enumerate(outs):
            rows = ordered[index * span:(index + 1) * span]
            out[:, :, cols] = rows.reshape(*out.shape[:2], piece)


def render(ray_count, relative, me, owner, lists, opacity, counts, pixels, features):
    depth, rays = lists.shape
    gauss, width = features.shape
    parts = ray_count // 2 if relative else 1
    shape = jax.ShapeDtypeStruct((ray_count // parts, rays // ray_count, width), BF16)
    return pl.pallas_call(
        functools.partial(render_kernel, ray_count, relative),
        out_shape=(shape,) * parts,
        in_specs=[SMEM] + [HBM] * 6,
        out_specs=(VMEM,) * parts,
        scratch_shapes=[
            pltpu.VMEM(owner.shape, jnp.int32),
            pltpu.VMEM((depth, rays), jnp.int32),
            pltpu.VMEM((depth, rays), F32),
            pltpu.VMEM((1, rays), jnp.int32),
            pltpu.VMEM((1, rays), jnp.int32),
            pltpu.VMEM((gauss, width), BF16),
            pltpu.VMEM((depth, rays), F32),
            pltpu.VMEM((gauss, rays), BF16),
            pltpu.VMEM((rays, rays), BF16),
            pltpu.SemaphoreType.DMA((6,)),
        ],
        compiler_params=params(20),
        cost_estimate=COST,
        name="render",
    )(me, owner, lists, opacity, counts, pixels, features)


def tokens_kernel(
    ray_count, relative, me_ref, owner_hbm, pixels_hbm, tokens_hbm, gain_hbm,
    *refs,
):
    tokens_out, normed_out, normed_t_out = refs[-11:-8]
    owner_ref, pixels_ref, tokens_ref, gain_ref, order_ref, rank_ref, place_ref, sems = refs[-8:]
    rows, width = tokens_hbm.shape
    me = me_ref[0]
    each = rows // ray_count
    wait = fetch(
        [
            (owner_hbm, owner_ref), (pixels_hbm, pixels_ref), (gain_hbm, gain_ref),
            (tokens_hbm, tokens_ref),
        ],
        sems,
    )
    wait(0, 1)
    pixels = jnp.concatenate(
        [pixels_ref[:, sender * rows:(sender + 1) * rows] for sender in range(ray_count)], axis=0
    )
    mine = owner_of(pixels, owner_ref, rows, ray_count) == me
    place_ref[...] = lax.rem(pixels, jnp.int32(rows)).astype(F32)
    member = jnp.where(mine, 1.0, 0.0)
    padded = -(-ray_count // 16) * 16
    if padded > ray_count:
        spread = jnp.concatenate([member, jnp.zeros((padded - ray_count, rows), F32)], axis=0)
    else:
        spread = member
    ranks = dot_nn(spread.astype(BF16), earlier(rows))
    rank_ref[...] = jnp.where(mine, ranks[:ray_count], -1.0)
    chips = ray_count // 2
    for index in range(ray_count):
        if relative:
            chip = lax.rem(lax.div(me, jnp.int32(2)) + (chips - index // 2), jnp.int32(chips))
            sender = 2 * chip + jnp.bitwise_xor(lax.rem(me, jnp.int32(2)), index % 2)
        else:
            sender = index
        rank = rank_ref[pl.ds(sender, 1), :].astype(jnp.int32)
        hit = lax.broadcasted_iota(jnp.int32, (each, rows), 0) == rank
        at = jnp.sum(
            jnp.where(hit, place_ref[pl.ds(sender, 1), :], 0.0), axis=1, keepdims=True
        )
        here = lax.broadcasted_iota(jnp.int32, (each, rows), 1) == at.astype(jnp.int32)
        order_ref[pl.ds(index * each, each), :] = here.astype(F32).astype(BF16)
    wait(2, 3)
    half = min(128, rows)
    gain = gain_ref[...]

    @pl.loop(0, rows // half)
    def _(step):
        span = pl.ds(pl.multiple_of(step * half, half), half)
        values = dot_nn(order_ref[span, :], tokens_ref[...])
        tokens_out[span, :] = values.astype(BF16)
        centered = values - jnp.mean(values, axis=-1, keepdims=True)
        variance = jnp.mean(centered * centered, axis=-1, keepdims=True)
        xhat = centered * lax.rsqrt(variance + STABILITY_EPSILON)
        normed = (xhat * gain).astype(BF16)
        normed_out[span, :] = normed
        normed_t_out[:, span] = normed.T


def prepare_tokens(ray_count, relative, me, owner, pixels, tokens, gain, after=()):
    rows, width = tokens.shape
    return pl.pallas_call(
        functools.partial(tokens_kernel, ray_count, relative),
        out_shape=(
            jax.ShapeDtypeStruct((rows, width), BF16),
            jax.ShapeDtypeStruct((rows, width), BF16),
            jax.ShapeDtypeStruct((width, rows), BF16),
        ),
        in_specs=[SMEM] + [HBM] * 4 + [ANY] * len(after),
        out_specs=(VMEM, VMEM, VMEM),
        scratch_shapes=[
            pltpu.VMEM(owner.shape, jnp.int32),
            pltpu.VMEM(pixels.shape, jnp.int32),
            pltpu.VMEM((rows, width), BF16),
            pltpu.VMEM((1, width), F32),
            pltpu.VMEM((rows, rows), BF16),
            pltpu.VMEM((ray_count, rows), F32),
            pltpu.VMEM((ray_count, rows), F32),
            pltpu.SemaphoreType.DMA((4,)),
        ],
        compiler_params=params(20),
        cost_estimate=COST,
        name="tokens",
    )(me, owner, pixels, tokens, gain, *after)


def up_kernel(normed_ref, up_ref, act_ref, slope_ref):
    parts, _, part_rows, width = up_ref.shape
    up = up_ref[...].reshape(parts * part_rows, width)
    rows = normed_ref.shape[0]
    piece = min(128, rows)

    @pl.loop(0, rows // piece)
    def _(step):
        span = pl.ds(pl.multiple_of(step * piece, piece), piece)
        hidden = dot_nn(normed_ref[span, :], up)
        phi = 0.5 * (1.0 + lax.erf(hidden * (0.5 ** 0.5)))
        density = jnp.exp(-0.5 * hidden * hidden) * ((2.0 * jnp.pi) ** -0.5)
        act_ref[span, :] = (hidden * phi).astype(BF16)
        slope_ref[span, :] = (phi + hidden * density).astype(slope_ref.dtype)


def project_up(normed, up):
    rows, width = normed.shape
    parts, chunks, part_rows, chunk = up.shape
    return pl.pallas_call(
        up_kernel,
        grid=(chunks,),
        out_shape=(
            jax.ShapeDtypeStruct((rows, chunks * chunk), BF16),
            jax.ShapeDtypeStruct((rows, chunks * chunk), F32),
        ),
        in_specs=[
            pl.BlockSpec((rows, width), lambda j: (0, 0)),
            pl.BlockSpec((parts, 1, part_rows, chunk), lambda j: (0, j, 0, 0)),
        ],
        out_specs=(
            pl.BlockSpec((rows, chunk), lambda j: (0, j)),
            pl.BlockSpec((rows, chunk), lambda j: (0, j)),
        ),
        compiler_params=params(dimension_semantics=("arbitrary",)),
        cost_estimate=COST,
        name="up",
    )(normed, up)


def down_kernel(
    chunks, act_ref, down_ref, tokens_ref, target_ref, scale_ref,
    grad_ref, back_ref, small_ref, mixed_ref,
):
    step = pl.program_id(0)
    rows, width = tokens_ref.shape
    act = act_ref[...]

    @pl.when(step < chunks)
    def _():
        parts, _, part_rows, _ = down_ref.shape
        part = dot_nn(act, down_ref[...].reshape(parts * part_rows, width))

        @pl.when(step == 0)
        def _():
            mixed_ref[...] = part

        @pl.when(step > 0)
        def _():
            mixed_ref[...] += part

    @pl.when(step == chunks - 1)
    def _():
        scale = scale_ref[...]
        small_ref[...] = jnp.zeros_like(small_ref)
        piece = min(64, rows)

        @pl.loop(0, rows // piece)
        def _(index):
            span = pl.ds(pl.multiple_of(index * piece, piece), piece)
            mixed = mixed_ref[span, :]
            out = tokens_ref[span, :].astype(F32) + scale * mixed
            goal = target_ref[span, :].astype(F32)
            out_norm = jnp.sqrt(jnp.sum(out * out, axis=-1, keepdims=True) + STABILITY_EPSILON)
            goal_norm = jnp.sqrt(jnp.sum(goal * goal, axis=-1, keepdims=True) + STABILITY_EPSILON)
            norms = out_norm * goal_norm
            cosine = jnp.sum(out * goal, axis=-1, keepdims=True) / norms
            upstream = (cosine / (out_norm * out_norm)) * out - goal * (1.0 / norms)
            back_ref[span, :] = (upstream * scale).astype(BF16)
            small_ref[0:1, :] += jnp.sum(upstream * mixed, axis=0, keepdims=True)
            loss = jnp.sum(1.0 - cosine, axis=0, keepdims=True)
            small_ref[1:2, :] += jnp.broadcast_to(loss, (1, width))

    @pl.when(step >= chunks)
    def _():
        grad = dot_tn(act, back_ref[...])
        grad_ref[...] = grad.astype(BF16).reshape(grad_ref.shape)


def project_down(act, down, tokens, target, scale):
    rows, width = tokens.shape
    parts, chunks, part_rows, _ = down.shape
    chunk = parts * part_rows
    return pl.pallas_call(
        functools.partial(down_kernel, chunks),
        grid=(2 * chunks,),
        out_shape=(
            jax.ShapeDtypeStruct(down.shape, BF16),
            jax.ShapeDtypeStruct((rows, width), BF16),
            jax.ShapeDtypeStruct((8, width), F32),
        ),
        in_specs=[
            pl.BlockSpec((rows, chunk), lambda j: (0, lax.rem(j, chunks))),
            pl.BlockSpec(
                (parts, 1, part_rows, width), lambda j: (0, jnp.minimum(j, chunks - 1), 0, 0)
            ),
            pl.BlockSpec((rows, width), lambda j: (0, 0)),
            pl.BlockSpec((rows, width), lambda j: (0, 0)),
            pl.BlockSpec((1, width), lambda j: (0, 0)),
        ],
        out_specs=(
            pl.BlockSpec(
                (parts, 1, part_rows, width), lambda j: (0, jnp.maximum(j - chunks, 0), 0, 0)
            ),
            pl.BlockSpec((rows, width), lambda j: (0, 0)),
            pl.BlockSpec((8, width), lambda j: (0, 0)),
        ),
        scratch_shapes=[pltpu.VMEM((rows, width), F32)],
        compiler_params=params(dimension_semantics=("arbitrary",)),
        cost_estimate=COST,
        name="down",
    )(act, down, tokens, target, scale)


def back_kernel(back_ref, down_ref, slope_ref, normed_t_ref, up_ref, gain_ref, grad_ref, sum_ref):
    step = pl.program_id(0)
    parts, _, part_rows, width = down_ref.shape
    chunk = parts * part_rows
    rows = back_ref.shape[0]
    back_act = dot_nt(back_ref[...], down_ref[...].reshape(chunk, width))
    back_hidden = (back_act * slope_ref[...]).astype(BF16)
    up_parts, _, up_rows, _ = up_ref.shape

    @pl.when(step == 0)
    def _():
        sum_ref[...] = jnp.zeros_like(sum_ref)

    grad = dot_nn(normed_t_ref[...], back_hidden)
    grad_ref[...] = grad.astype(BF16).reshape(grad_ref.shape)
    up = up_ref[...].reshape(up_parts * up_rows, chunk).astype(F32)
    sum_ref[...] += jnp.sum(grad * up, axis=1, keepdims=True) / gain_ref[...]


def back_up(back, down, slope, normed_t, up, gain):
    width, rows = normed_t.shape
    parts, chunks, part_rows, _ = down.shape
    chunk = parts * part_rows
    up_parts, _, up_rows, _ = up.shape
    return pl.pallas_call(
        back_kernel,
        grid=(chunks,),
        out_shape=(
            jax.ShapeDtypeStruct(up.shape, BF16),
            jax.ShapeDtypeStruct((width, 1), F32),
        ),
        in_specs=[
            pl.BlockSpec((rows, width), lambda j: (0, 0)),
            pl.BlockSpec((parts, 1, part_rows, width), lambda j: (0, j, 0, 0)),
            pl.BlockSpec((rows, chunk), lambda j: (0, j)),
            pl.BlockSpec((width, rows), lambda j: (0, 0)),
            pl.BlockSpec((up_parts, 1, up_rows, chunk), lambda j: (0, j, 0, 0)),
            pl.BlockSpec((width, 1), lambda j: (0, 0)),
        ],
        out_specs=(
            pl.BlockSpec((up_parts, 1, up_rows, chunk), lambda j: (0, j, 0, 0)),
            pl.BlockSpec((width, 1), lambda j: (0, 0)),
        ),
        compiler_params=params(dimension_semantics=("arbitrary",)),
        cost_estimate=COST,
        name="back",
    )(back, down, slope, normed_t, up, gain)


def gather_weight(weight, parts, group, group_count, ray_count):
    rows, cols = weight.shape
    if parts == 1:
        whole = lax.all_gather(weight, "ray", axis=0, tiled=True)
    else:
        part = lax.dynamic_slice_in_dim(weight, group * (rows // parts), rows // parts, 0)
        whole = lax.all_gather(part, ("grp", "ray"), axis=0, tiled=True)
    return whole.reshape(parts, ray_count, rows // parts, cols)


def reduce_gradient(grad):
    parts, ray_count, part_rows, cols = grad.shape
    flat = grad.reshape(parts * ray_count * part_rows, cols)
    if parts == 1:
        share = lax.psum_scatter(flat, "ray", scatter_dimension=0, tiled=True)
        return lax.psum(share.astype(F32), "grp")
    share = lax.psum_scatter(flat, "grp", scatter_dimension=0, tiled=True)
    share = lax.psum_scatter(share, "ray", scatter_dimension=0, tiled=True)
    return lax.all_gather(share, "grp", axis=0, tiled=True).astype(F32)


def shards_general(
    image_tokens,
    tile_lists,
    opacity,
    tile_counts,
    ray_pixel,
    block_owner,
    gaussian_features,
    layer_norm_gain,
    layer_scale,
    up_weight,
    down_weight,
):
    ray_count = lax.axis_size("ray")
    group_count = lax.axis_size("grp")
    group = lax.axis_index("grp")
    me = lax.axis_index("ray").reshape(1)
    rows, width = image_tokens.shape
    up_parts = group_count if up_weight.shape[0] % (16 * group_count) == 0 else 1
    down_parts = group_count if down_weight.shape[0] % (16 * group_count) == 0 else 1
    up = gather_weight(up_weight, up_parts, group, group_count, ray_count)
    down = gather_weight(down_weight, down_parts, group, group_count, ray_count)
    rendered = render(
        ray_count, False, me, block_owner, tile_lists, opacity, tile_counts.reshape(1, rows),
        ray_pixel, gaussian_features,
    )
    rendered = rendered[0].reshape(rows, width)
    target = lax.all_to_all(rendered, "ray", split_axis=0, concat_axis=0, tiled=True)
    tokens, normed, normed_t = prepare_tokens(
        ray_count, False, me, block_owner, ray_pixel, image_tokens,
        layer_norm_gain.reshape(1, width),
    )
    act, slope = project_up(normed, up)
    grad_down, back, small = project_down(act, down, tokens, target, layer_scale.reshape(1, width))
    grad_up, gain_sum = back_up(back, down, slope, normed_t, up, layer_norm_gain.reshape(width, 1))
    grad_down = reduce_gradient(grad_down)
    grad_up = reduce_gradient(grad_up)
    sums = jnp.concatenate([gain_sum.reshape(1, width), small[:2]], axis=0)
    sums = lax.psum(sums, ("grp", "ray"))
    loss = sums[2, 0] / (rows * ray_count * group_count)
    return (grad_up, grad_down, sums[0], sums[1], loss)


def quarter_kernel(group_ref, up_hbm, down_hbm, out_ref, up_ref, turned_ref, sems):
    part = out_ref.shape[1]
    lanes = up_ref.shape[1]
    start = pl.multiple_of(group_ref[0] * part, part)
    lane = pl.multiple_of(lax.div(start, jnp.int32(lanes)) * lanes, lanes)
    wait = fetch(
        [
            (up_hbm.at[:, pl.ds(lane, lanes)], up_ref),
            (down_hbm.at[pl.ds(start, part), :], out_ref.at[1]),
        ],
        sems,
    )
    wait(0)
    turned_ref[...] = up_ref[...].T
    out_ref[0] = turned_ref[pl.ds(pl.multiple_of(start - lane, part), part), :]
    wait(1)


def own_quarter(group, up, down, part):
    width, chunk = up.shape
    lanes = max(128, part)
    return pl.pallas_call(
        quarter_kernel,
        out_shape=jax.ShapeDtypeStruct((2, part, width), BF16),
        in_specs=[SMEM, HBM, HBM],
        out_specs=VMEM,
        scratch_shapes=[
            pltpu.VMEM((width, lanes), BF16),
            pltpu.VMEM((lanes, width), BF16),
            pltpu.SemaphoreType.DMA((2,)),
        ],
        compiler_params=params(16),
        cost_estimate=LONG,
        name="quarter",
    )(group, up, down)


def own_rows_kernel(group_ref, up_ref, down_ref, out_ref, turned_ref):
    part = out_ref.shape[2]
    turned_ref[...] = up_ref[...].T
    for index in range(4):
        quarter = jnp.bitwise_xor(group_ref[0], index)
        span = pl.ds(pl.multiple_of(quarter * part, part), part)
        out_ref[index, 0] = turned_ref[span, :]
        out_ref[index, 1] = down_ref[span, :]


def own_rows(group, up, down):
    width, chunk = up.shape
    return pl.pallas_call(
        own_rows_kernel,
        out_shape=jax.ShapeDtypeStruct((4, 2, chunk // 4, width), BF16),
        in_specs=[SMEM, VMEM, VMEM],
        out_specs=VMEM,
        scratch_shapes=[pltpu.VMEM((chunk, width), BF16)],
        compiler_params=params(16),
        cost_estimate=COST,
        name="own_rows",
    )(group, up, down)


def finish_rows(tokens, mixed, goal, scale):
    out = tokens + scale * mixed
    out_norm = jnp.sqrt(jnp.sum(out * out, axis=-1, keepdims=True) + STABILITY_EPSILON)
    goal_norm = jnp.sqrt(jnp.sum(goal * goal, axis=-1, keepdims=True) + STABILITY_EPSILON)
    norms = out_norm * goal_norm
    cosine = jnp.sum(out * goal, axis=-1, keepdims=True) / norms
    upstream = (cosine / (out_norm * out_norm)) * out - goal * (1.0 / norms)
    return upstream, 1.0 - cosine


def forward_kernel(first, blocks, sides, skipped, *refs):
    last = blocks > 0
    refs = list(refs[skipped:])
    normed_t_ref = refs.pop(0)
    own, other = refs[:sides], refs[sides:2 * sides]
    del refs[:2 * sides]
    mixed_in = None if first else refs.pop(0)
    if last:
        tokens_ref, scale_ref = refs[:2]
        targets, passed_ref = refs[2:2 + blocks], refs[2 + blocks]
        del refs[:3 + blocks]
    act_ref, slope_ref = refs[:2]
    del refs[:2]
    width, rows = normed_t_ref.shape
    part = act_ref.shape[2]
    part_sum = None
    downs = []
    for side, group in enumerate((own, other)):
        start = 0
        for ref in group:
            count = ref.shape[0]
            hiddens = dot_nn(ref[:, 0].reshape(count * part, width), normed_t_ref[...])
            for index in range(count):
                hidden = hiddens[index * part:(index + 1) * part]
                phi = 0.5 * (1.0 + lax.erf(hidden * (0.5 ** 0.5)))
                density = jnp.exp(-0.5 * hidden * hidden) * ((2.0 * jnp.pi) ** -0.5)
                act_ref[side, start + index] = (hidden * phi).astype(BF16)
                slope_ref[side, start + index] = phi + hidden * density
            downs.append(ref[:, 1].reshape(count * part, width))
            start += count
    if sides > 1 or last:
        act = act_ref[...].reshape(2 * start * part, rows)
        part_sum = dot_tn(act, jnp.concatenate(downs, axis=0))
    else:
        for side, down in enumerate(downs):
            term = dot_tn(act_ref[side].reshape(start * part, rows), down)
            part_sum = term if part_sum is None else part_sum + term
    if not last:
        mixed_out = refs[0]
        mixed_out[...] = part_sum if first else mixed_in[...] + part_sum
        return
    back_ref, back_t_ref, small_ref, mixed_ref = refs
    mixed_ref[...] = mixed_in[...] + part_sum
    scale = scale_ref[...]
    small_ref[...] = jnp.zeros_like(small_ref)
    piece = rows // blocks
    for index, target_ref in enumerate(targets):
        span = pl.ds(index * piece, piece)
        mixed = mixed_ref[span, :]
        goal = jnp.concatenate([target_ref[0], passed_ref[index]], axis=0).astype(F32)
        upstream, loss = finish_rows(tokens_ref[span, :].astype(F32), mixed, goal, scale)
        back = (upstream * scale).astype(BF16)
        back_ref[span, :] = back
        back_t_ref[:, span] = back.T
        small_ref[0:1, :] += jnp.sum(upstream * mixed, axis=0, keepdims=True)
        small_ref[1:2, :] += jnp.broadcast_to(jnp.sum(loss, axis=0, keepdims=True), (1, width))


def forward(normed_t, own, other, mixed=None, finish=None, after=()):
    width, rows = normed_t.shape
    part = own[0].shape[2]
    total = sum(array.shape[0] for array in own)
    first, last = mixed is None, finish is not None
    blocks = len(finish) - 3 if last else 0
    operands = [*after, normed_t, *own, *other]
    if not first:
        operands.append(mixed)
    if last:
        operands.extend(finish)
    piece = (2, total, part, rows)
    shapes = [jax.ShapeDtypeStruct(piece, BF16), jax.ShapeDtypeStruct(piece, F32)]
    scratch = []
    if last:
        shapes += [
            jax.ShapeDtypeStruct((rows, width), BF16),
            jax.ShapeDtypeStruct((width, rows), BF16),
            jax.ShapeDtypeStruct((8, width), F32),
        ]
        scratch = [pltpu.VMEM((rows, width), F32)]
    else:
        shapes += [jax.ShapeDtypeStruct((rows, width), F32)]
    return pl.pallas_call(
        functools.partial(forward_kernel, first, blocks, len(own), len(after)),
        out_shape=tuple(shapes),
        in_specs=[ANY] * len(after) + [VMEM] * (len(operands) - len(after)),
        out_specs=tuple([VMEM] * len(shapes)),
        scratch_shapes=scratch,
        compiler_params=params(32),
        cost_estimate=COST,
        name="forward",
    )(*operands)


def pack_kernel(counts, *refs):
    out_ref = refs[-1]
    start = 0
    for count, ref in zip(counts, refs):
        out_ref[start:start + count] = ref[...].reshape(count, *out_ref.shape[1:])
        start += count


def pack(pieces, *after):
    counts = [1 if piece.ndim == 3 else piece.shape[0] for piece in pieces]
    return pl.pallas_call(
        functools.partial(pack_kernel, counts),
        out_shape=jax.ShapeDtypeStruct((sum(counts), *pieces[0].shape[-3:]), BF16),
        in_specs=[VMEM] * len(pieces) + [ANY] * len(after),
        out_specs=VMEM,
        compiler_params=params(16),
        cost_estimate=COST,
        name="pack",
    )(*pieces, *after)


def turn_kernel(y_ref, x_ref, a_ref, b_ref):
    count = a_ref.shape[0]
    a_ref[...] = y_ref[:count]
    b_ref[...] = x_ref[count:]


def turn(y, x):
    count = y.shape[0]
    first = count // 2
    return pl.pallas_call(
        turn_kernel,
        out_shape=(
            jax.ShapeDtypeStruct((first, *y.shape[1:]), BF16),
            jax.ShapeDtypeStruct((count - first, *y.shape[1:]), BF16),
        ),
        in_specs=[VMEM] * 2,
        out_specs=(VMEM, VMEM),
        compiler_params=params(16),
        cost_estimate=COST,
        name="turn",
    )(y, x)


def tie_kernel(*refs):
    pass


def tie(array, *after):
    return pl.pallas_call(
        tie_kernel,
        out_shape=jax.ShapeDtypeStruct(array.shape, array.dtype),
        in_specs=[ANY] * (1 + len(after)),
        out_specs=ANY,
        input_output_aliases={0: 0},
        compiler_params=params(4),
        cost_estimate=COST,
        name="tie",
    )(array, *after)


def seconds_kernel(*refs):
    for index, ref in enumerate(refs[:-1]):
        refs[-1][index] = ref[1]


def seconds(blocks):
    count, (_, each, width) = len(blocks), blocks[0].shape
    return pl.pallas_call(
        seconds_kernel,
        out_shape=jax.ShapeDtypeStruct((count, each, width), BF16),
        in_specs=[VMEM] * count,
        out_specs=VMEM,
        compiler_params=params(16),
        cost_estimate=COST,
        name="seconds",
    )(*blocks)


def joined(refs, pieces, pick):
    values = [pick(refs[which], start, count) for which, start, count in pieces]
    flat = [value.reshape(-1, value.shape[-1]) for value in values]
    return flat[0] if len(flat) == 1 else jnp.concatenate(flat, axis=0)


def put(quarter, value, outs):
    own_ref, x_ref, y_ref, x_later_ref, y_later_ref = outs
    value = value.astype(BF16).reshape(own_ref.shape)
    half = x_ref.shape[0] // 2
    if quarter == 0:
        own_ref[...] = value
    elif quarter == 1:
        x_ref[half:] = value[:half]
        x_later_ref[...] = value[half:]
    elif quarter == 2:
        y_ref[half:] = value[half:]
        y_later_ref[...] = value[:half]
    else:
        x_ref[:half] = value[:half]
        y_ref[:half] = value[half:]


def emit(quarter, value, arrived, outs):
    if arrived is None:
        outs[0][quarter] = value.astype(BF16).reshape(outs[0].shape[1:])
    else:
        put(quarter, value + arrived[quarter].reshape(value.shape).astype(F32), outs)


def down_grad_kernel(side, act_pieces, add, *refs):
    acts, back_ref = refs[:2], refs[2]
    arrived = refs[3] if add else None
    outs = refs[4:] if add else refs[3:]
    for quarter in (3, 1, 2, 0):
        act = joined(acts, act_pieces[quarter], lambda ref, a, n: ref[side, a:a + n])
        emit(quarter, dot_nn(act, back_ref[...]), arrived, outs)


def up_grad_kernel(side, weight_pieces, act_pieces, add, *refs):
    weights, slopes = refs[:2], refs[2:4]
    back_t_ref, normed_ref, gain_in = refs[4:7]
    if add:
        arrived, scale_ref, small_ref = refs[7:10]
        outs, vector_ref, gain_ref = refs[10:-2], refs[-2], refs[-1]
    else:
        arrived = None
        outs, gain_ref = refs[7:-1], refs[-1]
    gain_ref[...] = gain_in[...]
    for quarter in (3, 1, 2, 0):
        pieces = weight_pieces[quarter]
        slope = joined(slopes, act_pieces[quarter], lambda ref, a, n: ref[side, a:a + n])
        back_act = dot_nn(joined(weights, pieces, lambda ref, a, n: ref[a:a + n, 1]), back_t_ref[...])
        back_hidden = (back_act * slope).astype(BF16)
        grad = dot_nn(back_hidden, normed_ref[...])
        up = joined(weights, pieces, lambda ref, a, n: ref[a:a + n, 0]).astype(F32)
        gain_ref[...] += jnp.sum(grad * up, axis=0, keepdims=True)
        emit(quarter, grad, arrived, outs)
    if add:
        vector_ref[0:1, :] = gain_ref[...] / scale_ref[...]
        vector_ref[1:3, :] = small_ref[0:2, :]
        vector_ref[3:8, :] = jnp.zeros((5, gain_ref.shape[1]), F32)


def gradient_shapes(depth, part, width, add):
    if not add:
        return [jax.ShapeDtypeStruct((4, depth, part, width), BF16)]
    counts = (depth, depth, depth, depth - depth // 2, depth // 2)
    return [jax.ShapeDtypeStruct((count, part, width), BF16) for count in counts]


def down_gradient(side, act_pieces, depth, acts, back, arrived=None):
    part = acts[0].shape[2]
    width = back.shape[1]
    add = arrived is not None
    operands = [*acts, back] + ([arrived] if add else [])
    shapes = gradient_shapes(depth, part, width, add)
    return pl.pallas_call(
        functools.partial(down_grad_kernel, side, act_pieces, add),
        out_shape=tuple(shapes),
        in_specs=[VMEM] * len(operands),
        out_specs=tuple([VMEM] * len(shapes)),
        compiler_params=params(20),
        cost_estimate=COST,
        name="down_gradient",
    )(*operands)


def up_gradient(
    side, weight_pieces, act_pieces, depth, weights, slopes, back_t, normed, gain, extra=()
):
    part, width = weights[0].shape[2:]
    add = len(extra) > 0
    operands = [*weights, *slopes, back_t, normed, gain, *extra]
    shapes = gradient_shapes(depth, part, width, add)
    if add:
        shapes.append(jax.ShapeDtypeStruct((8, width), F32))
        scratch = [pltpu.VMEM((1, width), F32)]
    else:
        scratch = []
        shapes.append(jax.ShapeDtypeStruct((1, width), F32))
    return pl.pallas_call(
        functools.partial(up_grad_kernel, side, weight_pieces, act_pieces, add),
        out_shape=tuple(shapes),
        in_specs=[VMEM] * len(operands),
        out_specs=tuple([VMEM] * len(shapes)),
        scratch_shapes=scratch,
        compiler_params=params(24),
        cost_estimate=COST,
        name="up_gradient",
    )(*operands)


def merge_kernel(x_ref, y_ref, x_later_ref, y_later_ref, *refs):
    x_out, y_out = refs[-2:]
    half = y_later_ref.shape[0]
    x_out[...] = (x_later_ref[...].astype(F32) + y_ref[:half].astype(F32)).astype(BF16)
    y_out[...] = (y_later_ref[...].astype(F32) + x_ref[:half].astype(F32)).astype(BF16)


def merge(x, y, x_later, y_later, *after):
    return pl.pallas_call(
        merge_kernel,
        out_shape=tuple(jax.ShapeDtypeStruct(a.shape, BF16) for a in (x_later, y_later)),
        in_specs=[VMEM] * 4 + [ANY] * len(after),
        out_specs=(VMEM, VMEM),
        compiler_params=params(16),
        cost_estimate=COST,
        name="merge",
    )(x, y, x_later, y_later, *after)


def total_kernel(own_ref, x_ref, y_ref, x_late_ref, y_late_ref, *refs):
    outs = refs[-own_ref.shape[0]:]
    half = y_late_ref.shape[0]
    for index, out in enumerate(outs):
        total = own_ref[index].astype(F32)
        if index < half:
            total += x_ref[half + index].astype(F32) + y_late_ref[index].astype(F32)
        else:
            total += y_ref[index].astype(F32) + x_late_ref[index - half].astype(F32)
        out[...] = total.astype(BF16)


def totals(own, x, y, x_late, y_late, *after):
    count, part, width = own.shape
    return pl.pallas_call(
        total_kernel,
        out_shape=tuple([jax.ShapeDtypeStruct((part, width), BF16)] * count),
        in_specs=[VMEM] * 5 + [ANY] * len(after),
        out_specs=tuple([VMEM] * count),
        compiler_params=params(16),
        cost_estimate=COST,
        name="totals",
    )(own, x, y, x_late, y_late, *after)


def collect_kernel(count, *refs):
    total = refs[0][...].astype(F32)
    for ref in refs[1:count]:
        total = total + ref[...].astype(F32)
    refs[-1][...] = total.astype(BF16)


def collect(parts, *after):
    return pl.pallas_call(
        functools.partial(collect_kernel, len(parts)),
        out_shape=jax.ShapeDtypeStruct(parts[0].shape, BF16),
        in_specs=[VMEM] * len(parts) + [ANY] * len(after),
        out_specs=VMEM,
        compiler_params=params(16),
        cost_estimate=COST,
        name="collect",
    )(*parts, *after)


def join_kernel(total_ref, vector_ref, other_ref, *refs):
    short_ref, long_ref, held_ref = refs[-3:]
    part = total_ref.shape[0]
    short_ref[pl.ds(0, part), :] = total_ref[...]
    rest = vector_ref[0:3, :]
    held_ref[...] = jnp.zeros_like(held_ref)
    for index in range(3):
        piece = rest.astype(BF16).astype(F32)
        held_ref[3 * index:3 * index + 3, :] = piece
        rest = rest - piece
    short_ref[pl.ds(part, 16), :] = held_ref[...].astype(BF16)
    long_ref[pl.ds(0, part + 16), :] = short_ref[...]
    long_ref[pl.ds(part + 16, part), :] = other_ref[...]


def join(total, vector, other, *after):
    part, width = total.shape
    return pl.pallas_call(
        join_kernel,
        out_shape=tuple(
            jax.ShapeDtypeStruct((rows, width), BF16) for rows in (part + 16, 2 * part + 16)
        ),
        in_specs=[VMEM] * 3 + [ANY] * len(after),
        out_specs=(VMEM, VMEM),
        scratch_shapes=[pltpu.VMEM((16, width), F32)],
        compiler_params=params(16),
        cost_estimate=COST,
        name="join",
    )(total, vector, other, *after)


def place_kernel(part, tokens, group_ref, *refs):
    ups, downs = refs[:4], refs[4:8]
    up_ref, down_ref, gain_ref, scale_ref, loss_ref, held_ref = refs[8:]
    group = group_ref[0]
    vectors = []
    for index, (up, down) in enumerate(zip(ups, downs)):
        first = pl.multiple_of(jnp.bitwise_xor(group, index) * part, part)
        held_ref[pl.ds(first, part), :] = up[pl.ds(0, part), :].astype(F32)
        start = down.shape[0] - part
        down_ref[pl.ds(first, part), :] = down[pl.ds(start, part), :].astype(F32)
        rows = up[pl.ds(part, 16), :].astype(F32)
        vectors.append((rows[0:3] + rows[3:6]) + rows[6:9])
    up_ref[...] = held_ref[...].T
    vector = (vectors[0] + vectors[1]) + (vectors[2] + vectors[3])
    gain_ref[...] = vector[0:1]
    scale_ref[...] = vector[1:2]
    loss_ref[...] = vector[2:3, 0:1] * (1.0 / tokens)


def place_quarters(group, ups, downs, part, tokens):
    width = ups[0].shape[1]
    shapes = [
        jax.ShapeDtypeStruct((width, 4 * part), F32),
        jax.ShapeDtypeStruct((4 * part, width), F32),
        jax.ShapeDtypeStruct((1, width), F32),
        jax.ShapeDtypeStruct((1, width), F32),
        jax.ShapeDtypeStruct((1, 1), F32),
    ]
    return pl.pallas_call(
        functools.partial(place_kernel, part, tokens),
        out_shape=tuple(shapes),
        in_specs=[SMEM] + [VMEM] * 8,
        out_specs=tuple([VMEM] * len(shapes)),
        scratch_shapes=[pltpu.VMEM((4 * part, width), F32)],
        compiler_params=params(16),
        cost_estimate=COST,
        name="place",
    )(group, *ups, *downs)


def shards_square(
    image_tokens,
    tile_lists,
    opacity,
    tile_counts,
    ray_pixel,
    block_owner,
    gaussian_features,
    layer_norm_gain,
    layer_scale,
    up_weight,
    down_weight,
):
    ray_count = lax.axis_size("ray")
    group_count = lax.axis_size("grp")
    depth = ray_count // 2
    group = lax.axis_index("grp").reshape(1)
    me = lax.axis_index("ray").reshape(1)
    rows, width = image_tokens.shape
    part = down_weight.shape[0] // group_count

    def beside(array, flip):
        return lax.ppermute(array, "grp", [(g, g ^ flip) for g in range(group_count)])

    def partner(array, flip=1):
        return lax.ppermute(array, "ray", [(r, r ^ flip) for r in range(ray_count)])

    def along(array, shift):
        pairs = [(r, (r + 2 * shift) % ray_count) for r in range(ray_count)]
        return lax.ppermute(array, "ray", pairs)

    mine = own_quarter(group, up_weight, down_weight, part)
    arrivals = [along(mine, -shift) for shift in range(1, depth)]
    rendered = render(
        ray_count, True, me, block_owner, tile_lists, opacity, tile_counts.reshape(1, rows),
        ray_pixel, gaussian_features,
    )
    half = depth // 2
    low = pack(arrivals[:half - 1], rendered[0])
    x_low, y_low = beside(low, 1), beside(low, 2)
    high = pack(arrivals[half - 1:], low)
    high = tie(high, x_low, y_low)
    x_high, y_high = beside(high, 1), beside(high, 2)
    targets = [rendered[0]] + [along(rendered[shift], shift) for shift in range(1, depth)]
    tokens, normed, normed_t = prepare_tokens(
        ray_count, True, me, block_owner, ray_pixel, image_tokens,
        layer_norm_gain.reshape(1, width),
    )
    most = pack(
        [own_rows(group, up_weight, down_weight), low, x_low, y_low, high, x_high, y_high],
        normed, targets[1], *targets[half + 1:],
    )
    most_other = partner(most)
    d_low, d_high = beside(y_low, 1), beside(x_high, 2)
    act_most, slope_most, mixed = forward(normed_t, [most], [most_other])
    late = targets[2:half + 1]
    last = pack([d_low, d_high], mixed, *late)
    last_other = partner(last)
    act_last, slope_last, back, back_t, small = forward(
        normed_t, [last], [last_other], mixed,
        (tokens, layer_scale.reshape(1, width), *targets, partner(seconds(targets))),
    )
    acts, slopes = (act_most, act_last), (slope_most, slope_last)
    weights = ((most, last), (most_other, last_other))
    count, rest = half - 1, depth - half
    start = 4 + 3 * count
    pieces = tuple(
        ((0, q, 1), (0, 4 + q * count, count), (0, start + q * rest, rest)) for q in range(3)
    ) + (((0, 3, 1), (1, 0, depth - 1)),)
    gain = jnp.zeros((1, width), F32)
    (down_other,) = down_gradient(1, pieces, depth, acts, back)
    down_arrived = partner(down_other)
    up_other, gain = up_gradient(
        1, pieces, pieces, depth, weights[1], slopes, back_t, normed, gain
    )
    up_arrived = partner(up_other)
    down_sums = down_gradient(0, pieces, depth, acts, back, down_arrived)
    *up_sums, vector = up_gradient(
        0, pieces, pieces, depth, weights[0], slopes, back_t, normed, gain,
        (up_arrived, layer_norm_gain.reshape(1, width), small),
    )
    vector = vector + partner(vector)
    flip = 2
    while flip < ray_count:
        vector = vector + partner(vector, flip)
        flip *= 2

    def first_step(to_x, to_y, x_later, y_later, *after):
        from_x, from_y = beside(to_x, 1), beside(to_y, 2)
        return from_x, from_y, merge(from_x, from_y, x_later, y_later, *after)

    def second_step(later):
        return beside(later[0], 1), beside(later[1], 2)

    def arrive_along(shares):
        return [shares[0]] + [along(shares[shift], shift) for shift in range(1, depth)]

    own, *rest = down_sums
    own_up, to_x, to_y, *rest_up = up_sums
    from_x, from_y, later = first_step(*rest, vector)
    late = second_step(later)
    shares = totals(own, from_x, from_y, *late)
    from_x, from_y, later = first_step(to_x, to_y, *rest_up)
    up_shares = totals(own_up, from_x, from_y, *second_step(later))
    down_total = collect(arrive_along(shares), up_shares[0])
    down_x, down_y = beside(down_total, 1), beside(down_total, 2)
    up_total = collect(arrive_along(up_shares))
    short, long = join(up_total, vector, down_total, down_x, down_y)
    up_x, up_y, both = beside(short, 1), beside(short, 2), beside(long, 3)
    grad_up, grad_down, gain, scale, loss = place_quarters(
        group, (short, up_x, up_y, both), (down_total, down_x, down_y, both), part,
        rows * ray_count * group_count,
    )
    return (grad_up, grad_down, gain.reshape(width), scale.reshape(width), loss.reshape(()))


def shards(*operands):
    ray_count, group_count = lax.axis_size("ray"), lax.axis_size("grp")
    hidden = operands[-1].shape[0]
    square = group_count == 4 and ray_count in (8, 16) and hidden % (16 * group_count) == 0
    return (shards_square if square else shards_general)(*operands)


def solution(mesh):
    return jax.shard_map(
        shards,
        mesh=mesh,
        in_specs=(
            P(("grp", "ray"), None),
            P(None, ("grp", "ray")),
            P(None, ("grp", "ray")),
            P(("grp", "ray")),
            P("grp", None),
            P("grp", None),
            P(("grp", "ray"), None),
            P(),
            P(),
            P(None, "ray"),
            P("ray", None),
        ),
        out_specs=(P(None, "ray"), P("ray", None), P(), P(), P()),
        check_vma=False,
    )
```

```python
import functools

import jax
import jax.numpy as jnp
from jax import lax
from jax.experimental import pallas as pl
from jax.experimental.pallas import tpu as pltpu
from jax.sharding import PartitionSpec as P

STABILITY_EPSILON = 1e-06
F32 = jnp.float32
BF16 = jnp.bfloat16
MIB = 1024 * 1024
COST = pl.CostEstimate(flops=1 << 20, bytes_accessed=1 << 16, transcendentals=0)
LONG = pl.CostEstimate(flops=10**10, bytes_accessed=1 << 20, transcendentals=0)
SMEM = pl.BlockSpec(memory_space=pltpu.SMEM)
VMEM = pl.BlockSpec(memory_space=pltpu.VMEM)
ANY = pl.BlockSpec(memory_space=pl.ANY)


def params(mib=48, **more):
    return pltpu.CompilerParams(vmem_limit_bytes=mib * MIB, **more)


def dot_nn(a, b):
    return lax.dot_general(a, b, (((1,), (0,)), ((), ())), preferred_element_type=F32)


def dot_tn(a, b):
    return lax.dot_general(a, b, (((0,), (0,)), ((), ())), preferred_element_type=F32)


def dot_nt(a, b):
    return lax.dot_general(a, b, (((1,), (1,)), ((), ())), preferred_element_type=F32)


def owner_of(pixels, owner_ref, rows, count):
    block = lax.div(pixels, jnp.int32(rows))
    owner = jnp.zeros_like(pixels)
    for slot in range(count):
        owner = jnp.where(block == slot, owner_ref[0:1, slot:slot + 1], owner)
    return owner


def earlier(rows):
    before = lax.broadcasted_iota(jnp.int32, (rows, rows), 0)
    after = lax.broadcasted_iota(jnp.int32, (rows, rows), 1)
    return jnp.where(before < after, 1.0, 0.0).astype(BF16)


HBM = pl.BlockSpec(memory_space=pltpu.HBM)


def fetch(copies, sems):
    started = [
        pltpu.make_async_copy(source, target, sems.at[index])
        for index, (source, target) in enumerate(copies)
    ]
    for copy in started:
        copy.start()

    def wait(*numbers):
        for number in numbers:
            started[number].wait()

    return wait


def render_kernel(
    ray_count, relative, me_ref, owner_hbm, lists_hbm, opacity_hbm, counts_hbm, pixels_hbm,
    features_hbm, *refs,
):
    outs = refs[:-10]
    owner_ref, ids_ref, opacity_ref, counts_ref, mine_ref, features_ref = refs[-10:-4]
    share_ref, table_ref, send_ref, sems = refs[-4:]
    depth, rays = lists_hbm.shape
    gauss = features_hbm.shape[0]
    width = features_hbm.shape[1]
    me = me_ref[0]
    own_pixels = pixels_hbm.at[:, pl.ds(pl.multiple_of(me * rays, rays), rays)]
    wait = fetch(
        [
            (lists_hbm, ids_ref), (opacity_hbm, opacity_ref), (counts_hbm, counts_ref),
            (owner_hbm, owner_ref), (own_pixels, mine_ref), (features_hbm, features_ref),
        ],
        sems,
    )
    wait(0, 1, 2)
    ids_ref[...] = ids_ref[...] - me * gauss
    passing = jnp.ones((1, rays), F32)
    counts = counts_ref[...]
    for level in range(depth):
        alpha = opacity_ref[pl.ds(level, 1), :]
        share_ref[pl.ds(level, 1), :] = jnp.where(level < counts, alpha * passing, 0.0)
        passing = passing * (1.0 - alpha)

    tile = 256
    lanes = 128
    columns = rays // lanes

    @pl.loop(0, (gauss // tile) * columns)
    def _(step):
        first = pl.multiple_of(lax.div(step, columns) * tile, tile)
        lane = pl.multiple_of(lax.rem(step, columns) * lanes, lanes)
        number = (lax.broadcasted_iota(jnp.int32, (tile, lanes), 0) + first).astype(jnp.int16)
        total = jnp.zeros((tile, lanes), BF16)
        for level in range(depth):
            ident = jnp.broadcast_to(ids_ref[pl.ds(level, 1), pl.ds(lane, lanes)], (16, lanes))
            share = jnp.broadcast_to(share_ref[pl.ds(level, 1), pl.ds(lane, lanes)], (16, lanes))
            ident = jnp.concatenate([ident.astype(jnp.int16)] * (tile // 16), axis=0)
            share = jnp.concatenate([share.astype(BF16)] * (tile // 16), axis=0)
            total = total + jnp.where(ident == number, share, jnp.zeros_like(share))
        table_ref[pl.ds(first, tile), pl.ds(lane, lanes)] = total

    wait(3, 4, 5)
    owner = owner_of(mine_ref[...], owner_ref, rays, ray_count)
    padded = -(-ray_count // 16) * 16
    member = (lax.broadcasted_iota(jnp.int32, (padded, rays), 0) == owner)
    ranks = dot_nn(member.astype(F32).astype(BF16), earlier(rays))
    rank = jnp.sum(jnp.where(member, ranks, 0.0), axis=0, keepdims=True).astype(jnp.int32)
    if relative:
        chips = ray_count // 2
        shift = lax.div(owner, jnp.int32(2)) - lax.div(me, jnp.int32(2))
        shift = jnp.where(shift < 0, shift + chips, shift)
        flip = jnp.where(lax.rem(owner, jnp.int32(2)) == lax.rem(me, jnp.int32(2)), 0, 1)
        block = 2 * shift + flip
    else:
        block = owner
    slot = block * (rays // ray_count) + rank
    send_ref[...] = (
        (lax.broadcasted_iota(jnp.int32, (rays, rays), 0) == slot).astype(F32).astype(BF16)
    )

    piece = 256
    span = rays // len(outs)

    @pl.loop(0, width // piece)
    def _(step):
        cols = pl.ds(pl.multiple_of(step * piece, piece), piece)
        rendered = dot_tn(table_ref[...], features_ref[:, cols]).astype(BF16)
        ordered = dot_nn(send_ref[...], rendered).astype(BF16)
        for index, out in enumerate(outs):
            rows = ordered[index * span:(index + 1) * span]
            out[:, :, cols] = rows.reshape(*out.shape[:2], piece)


def render(ray_count, relative, me, owner, lists, opacity, counts, pixels, features):
    depth, rays = lists.shape
    gauss, width = features.shape
    parts = ray_count // 2 if relative else 1
    shape = jax.ShapeDtypeStruct((ray_count // parts, rays // ray_count, width), BF16)
    return pl.pallas_call(
        functools.partial(render_kernel, ray_count, relative),
        out_shape=(shape,) * parts,
        in_specs=[SMEM] + [HBM] * 6,
        out_specs=(VMEM,) * parts,
        scratch_shapes=[
            pltpu.VMEM(owner.shape, jnp.int32),
            pltpu.VMEM((depth, rays), jnp.int32),
            pltpu.VMEM((depth, rays), F32),
            pltpu.VMEM((1, rays), jnp.int32),
            pltpu.VMEM((1, rays), jnp.int32),
            pltpu.VMEM((gauss, width), BF16),
            pltpu.VMEM((depth, rays), F32),
            pltpu.VMEM((gauss, rays), BF16),
            pltpu.VMEM((rays, rays), BF16),
            pltpu.SemaphoreType.DMA((6,)),
        ],
        compiler_params=params(20),
        cost_estimate=COST,
        name="render",
    )(me, owner, lists, opacity, counts, pixels, features)


def tokens_kernel(
    ray_count, relative, me_ref, owner_hbm, pixels_hbm, tokens_hbm, gain_hbm,
    *refs,
):
    tokens_out, normed_out, normed_t_out = refs[-11:-8]
    owner_ref, pixels_ref, tokens_ref, gain_ref, order_ref, rank_ref, place_ref, sems = refs[-8:]
    rows, width = tokens_hbm.shape
    me = me_ref[0]
    each = rows // ray_count
    wait = fetch(
        [
            (owner_hbm, owner_ref), (pixels_hbm, pixels_ref), (gain_hbm, gain_ref),
            (tokens_hbm, tokens_ref),
        ],
        sems,
    )
    wait(0, 1)
    pixels = jnp.concatenate(
        [pixels_ref[:, sender * rows:(sender + 1) * rows] for sender in range(ray_count)], axis=0
    )
    mine = owner_of(pixels, owner_ref, rows, ray_count) == me
    place_ref[...] = lax.rem(pixels, jnp.int32(rows)).astype(F32)
    member = jnp.where(mine, 1.0, 0.0)
    padded = -(-ray_count // 16) * 16
    if padded > ray_count:
        spread = jnp.concatenate([member, jnp.zeros((padded - ray_count, rows), F32)], axis=0)
    else:
        spread = member
    ranks = dot_nn(spread.astype(BF16), earlier(rows))
    rank_ref[...] = jnp.where(mine, ranks[:ray_count], -1.0)
    chips = ray_count // 2
    for index in range(ray_count):
        if relative:
            chip = lax.rem(lax.div(me, jnp.int32(2)) + (chips - index // 2), jnp.int32(chips))
            sender = 2 * chip + jnp.bitwise_xor(lax.rem(me, jnp.int32(2)), index % 2)
        else:
            sender = index
        rank = rank_ref[pl.ds(sender, 1), :].astype(jnp.int32)
        hit = lax.broadcasted_iota(jnp.int32, (each, rows), 0) == rank
        at = jnp.sum(
            jnp.where(hit, place_ref[pl.ds(sender, 1), :], 0.0), axis=1, keepdims=True
        )
        here = lax.broadcasted_iota(jnp.int32, (each, rows), 1) == at.astype(jnp.int32)
        order_ref[pl.ds(index * each, each), :] = here.astype(F32).astype(BF16)
    wait(2, 3)
    half = min(128, rows)
    gain = gain_ref[...]

    @pl.loop(0, rows // half)
    def _(step):
        span = pl.ds(pl.multiple_of(step * half, half), half)
        values = dot_nn(order_ref[span, :], tokens_ref[...])
        tokens_out[span, :] = values.astype(BF16)
        centered = values - jnp.mean(values, axis=-1, keepdims=True)
        variance = jnp.mean(centered * centered, axis=-1, keepdims=True)
        xhat = centered * lax.rsqrt(variance + STABILITY_EPSILON)
        normed = (xhat * gain).astype(BF16)
        normed_out[span, :] = normed
        normed_t_out[:, span] = normed.T


def prepare_tokens(ray_count, relative, me, owner, pixels, tokens, gain, after=()):
    rows, width = tokens.shape
    return pl.pallas_call(
        functools.partial(tokens_kernel, ray_count, relative),
        out_shape=(
            jax.ShapeDtypeStruct((rows, width), BF16),
            jax.ShapeDtypeStruct((rows, width), BF16),
            jax.ShapeDtypeStruct((width, rows), BF16),
        ),
        in_specs=[SMEM] + [HBM] * 4 + [ANY] * len(after),
        out_specs=(VMEM, VMEM, VMEM),
        scratch_shapes=[
            pltpu.VMEM(owner.shape, jnp.int32),
            pltpu.VMEM(pixels.shape, jnp.int32),
            pltpu.VMEM((rows, width), BF16),
            pltpu.VMEM((1, width), F32),
            pltpu.VMEM((rows, rows), BF16),
            pltpu.VMEM((ray_count, rows), F32),
            pltpu.VMEM((ray_count, rows), F32),
            pltpu.SemaphoreType.DMA((4,)),
        ],
        compiler_params=params(20),
        cost_estimate=COST,
        name="tokens",
    )(me, owner, pixels, tokens, gain, *after)


def up_kernel(normed_ref, up_ref, act_ref, slope_ref):
    parts, _, part_rows, width = up_ref.shape
    up = up_ref[...].reshape(parts * part_rows, width)
    rows = normed_ref.shape[0]
    piece = min(128, rows)

    @pl.loop(0, rows // piece)
    def _(step):
        span = pl.ds(pl.multiple_of(step * piece, piece), piece)
        hidden = dot_nn(normed_ref[span, :], up)
        phi = 0.5 * (1.0 + lax.erf(hidden * (0.5 ** 0.5)))
        density = jnp.exp(-0.5 * hidden * hidden) * ((2.0 * jnp.pi) ** -0.5)
        act_ref[span, :] = (hidden * phi).astype(BF16)
        slope_ref[span, :] = (phi + hidden * density).astype(slope_ref.dtype)


def project_up(normed, up):
    rows, width = normed.shape
    parts, chunks, part_rows, chunk = up.shape
    return pl.pallas_call(
        up_kernel,
        grid=(chunks,),
        out_shape=(
            jax.ShapeDtypeStruct((rows, chunks * chunk), BF16),
            jax.ShapeDtypeStruct((rows, chunks * chunk), F32),
        ),
        in_specs=[
            pl.BlockSpec((rows, width), lambda j: (0, 0)),
            pl.BlockSpec((parts, 1, part_rows, chunk), lambda j: (0, j, 0, 0)),
        ],
        out_specs=(
            pl.BlockSpec((rows, chunk), lambda j: (0, j)),
            pl.BlockSpec((rows, chunk), lambda j: (0, j)),
        ),
        compiler_params=params(dimension_semantics=("arbitrary",)),
        cost_estimate=COST,
        name="up",
    )(normed, up)


def down_kernel(
    chunks, act_ref, down_ref, tokens_ref, target_ref, scale_ref,
    grad_ref, back_ref, small_ref, mixed_ref,
):
    step = pl.program_id(0)
    rows, width = tokens_ref.shape
    act = act_ref[...]

    @pl.when(step < chunks)
    def _():
        parts, _, part_rows, _ = down_ref.shape
        part = dot_nn(act, down_ref[...].reshape(parts * part_rows, width))

        @pl.when(step == 0)
        def _():
            mixed_ref[...] = part

        @pl.when(step > 0)
        def _():
            mixed_ref[...] += part

    @pl.when(step == chunks - 1)
    def _():
        scale = scale_ref[...]
        small_ref[...] = jnp.zeros_like(small_ref)
        piece = min(64, rows)

        @pl.loop(0, rows // piece)
        def _(index):
            span = pl.ds(pl.multiple_of(index * piece, piece), piece)
            mixed = mixed_ref[span, :]
            out = tokens_ref[span, :].astype(F32) + scale * mixed
            goal = target_ref[span, :].astype(F32)
            out_norm = jnp.sqrt(jnp.sum(out * out, axis=-1, keepdims=True) + STABILITY_EPSILON)
            goal_norm = jnp.sqrt(jnp.sum(goal * goal, axis=-1, keepdims=True) + STABILITY_EPSILON)
            norms = out_norm * goal_norm
            cosine = jnp.sum(out * goal, axis=-1, keepdims=True) / norms
            upstream = (cosine / (out_norm * out_norm)) * out - goal * (1.0 / norms)
            back_ref[span, :] = (upstream * scale).astype(BF16)
            small_ref[0:1, :] += jnp.sum(upstream * mixed, axis=0, keepdims=True)
            loss = jnp.sum(1.0 - cosine, axis=0, keepdims=True)
            small_ref[1:2, :] += jnp.broadcast_to(loss, (1, width))

    @pl.when(step >= chunks)
    def _():
        grad = dot_tn(act, back_ref[...])
        grad_ref[...] = grad.astype(BF16).reshape(grad_ref.shape)


def project_down(act, down, tokens, target, scale):
    rows, width = tokens.shape
    parts, chunks, part_rows, _ = down.shape
    chunk = parts * part_rows
    return pl.pallas_call(
        functools.partial(down_kernel, chunks),
        grid=(2 * chunks,),
        out_shape=(
            jax.ShapeDtypeStruct(down.shape, BF16),
            jax.ShapeDtypeStruct((rows, width), BF16),
            jax.ShapeDtypeStruct((8, width), F32),
        ),
        in_specs=[
            pl.BlockSpec((rows, chunk), lambda j: (0, lax.rem(j, chunks))),
            pl.BlockSpec(
                (parts, 1, part_rows, width), lambda j: (0, jnp.minimum(j, chunks - 1), 0, 0)
            ),
            pl.BlockSpec((rows, width), lambda j: (0, 0)),
            pl.BlockSpec((rows, width), lambda j: (0, 0)),
            pl.BlockSpec((1, width), lambda j: (0, 0)),
        ],
        out_specs=(
            pl.BlockSpec(
                (parts, 1, part_rows, width), lambda j: (0, jnp.maximum(j - chunks, 0), 0, 0)
            ),
            pl.BlockSpec((rows, width), lambda j: (0, 0)),
            pl.BlockSpec((8, width), lambda j: (0, 0)),
        ),
        scratch_shapes=[pltpu.VMEM((rows, width), F32)],
        compiler_params=params(dimension_semantics=("arbitrary",)),
        cost_estimate=COST,
        name="down",
    )(act, down, tokens, target, scale)


def back_kernel(back_ref, down_ref, slope_ref, normed_t_ref, up_ref, gain_ref, grad_ref, sum_ref):
    step = pl.program_id(0)
    parts, _, part_rows, width = down_ref.shape
    chunk = parts * part_rows
    rows = back_ref.shape[0]
    back_act = dot_nt(back_ref[...], down_ref[...].reshape(chunk, width))
    back_hidden = (back_act * slope_ref[...]).astype(BF16)
    up_parts, _, up_rows, _ = up_ref.shape

    @pl.when(step == 0)
    def _():
        sum_ref[...] = jnp.zeros_like(sum_ref)

    grad = dot_nn(normed_t_ref[...], back_hidden)
    grad_ref[...] = grad.astype(BF16).reshape(grad_ref.shape)
    up = up_ref[...].reshape(up_parts * up_rows, chunk).astype(F32)
    sum_ref[...] += jnp.sum(grad * up, axis=1, keepdims=True) / gain_ref[...]


def back_up(back, down, slope, normed_t, up, gain):
    width, rows = normed_t.shape
    parts, chunks, part_rows, _ = down.shape
    chunk = parts * part_rows
    up_parts, _, up_rows, _ = up.shape
    return pl.pallas_call(
        back_kernel,
        grid=(chunks,),
        out_shape=(
            jax.ShapeDtypeStruct(up.shape, BF16),
            jax.ShapeDtypeStruct((width, 1), F32),
        ),
        in_specs=[
            pl.BlockSpec((rows, width), lambda j: (0, 0)),
            pl.BlockSpec((parts, 1, part_rows, width), lambda j: (0, j, 0, 0)),
            pl.BlockSpec((rows, chunk), lambda j: (0, j)),
            pl.BlockSpec((width, rows), lambda j: (0, 0)),
            pl.BlockSpec((up_parts, 1, up_rows, chunk), lambda j: (0, j, 0, 0)),
            pl.BlockSpec((width, 1), lambda j: (0, 0)),
        ],
        out_specs=(
            pl.BlockSpec((up_parts, 1, up_rows, chunk), lambda j: (0, j, 0, 0)),
            pl.BlockSpec((width, 1), lambda j: (0, 0)),
        ),
        compiler_params=params(dimension_semantics=("arbitrary",)),
        cost_estimate=COST,
        name="back",
    )(back, down, slope, normed_t, up, gain)


def gather_weight(weight, parts, group, group_count, ray_count):
    rows, cols = weight.shape
    if parts == 1:
        whole = lax.all_gather(weight, "ray", axis=0, tiled=True)
    else:
        part = lax.dynamic_slice_in_dim(weight, group * (rows // parts), rows // parts, 0)
        whole = lax.all_gather(part, ("grp", "ray"), axis=0, tiled=True)
    return whole.reshape(parts, ray_count, rows // parts, cols)


def reduce_gradient(grad):
    parts, ray_count, part_rows, cols = grad.shape
    flat = grad.reshape(parts * ray_count * part_rows, cols)
    if parts == 1:
        share = lax.psum_scatter(flat, "ray", scatter_dimension=0, tiled=True)
        return lax.psum(share.astype(F32), "grp")
    share = lax.psum_scatter(flat, "grp", scatter_dimension=0, tiled=True)
    share = lax.psum_scatter(share, "ray", scatter_dimension=0, tiled=True)
    return lax.all_gather(share, "grp", axis=0, tiled=True).astype(F32)


def shards_general(
    image_tokens,
    tile_lists,
    opacity,
    tile_counts,
    ray_pixel,
    block_owner,
    gaussian_features,
    layer_norm_gain,
    layer_scale,
    up_weight,
    down_weight,
):
    ray_count = lax.axis_size("ray")
    group_count = lax.axis_size("grp")
    group = lax.axis_index("grp")
    me = lax.axis_index("ray").reshape(1)
    rows, width = image_tokens.shape
    up_parts = group_count if up_weight.shape[0] % (16 * group_count) == 0 else 1
    down_parts = group_count if down_weight.shape[0] % (16 * group_count) == 0 else 1
    up = gather_weight(up_weight, up_parts, group, group_count, ray_count)
    down = gather_weight(down_weight, down_parts, group, group_count, ray_count)
    rendered = render(
        ray_count, False, me, block_owner, tile_lists, opacity, tile_counts.reshape(1, rows),
        ray_pixel, gaussian_features,
    )
    rendered = rendered[0].reshape(rows, width)
    target = lax.all_to_all(rendered, "ray", split_axis=0, concat_axis=0, tiled=True)
    tokens, normed, normed_t = prepare_tokens(
        ray_count, False, me, block_owner, ray_pixel, image_tokens,
        layer_norm_gain.reshape(1, width),
    )
    act, slope = project_up(normed, up)
    grad_down, back, small = project_down(act, down, tokens, target, layer_scale.reshape(1, width))
    grad_up, gain_sum = back_up(back, down, slope, normed_t, up, layer_norm_gain.reshape(width, 1))
    grad_down = reduce_gradient(grad_down)
    grad_up = reduce_gradient(grad_up)
    sums = jnp.concatenate([gain_sum.reshape(1, width), small[:2]], axis=0)
    sums = lax.psum(sums, ("grp", "ray"))
    loss = sums[2, 0] / (rows * ray_count * group_count)
    return (grad_up, grad_down, sums[0], sums[1], loss)


def quarter_kernel(group_ref, up_hbm, down_hbm, out_ref, up_ref, turned_ref, sems):
    part = out_ref.shape[1]
    lanes = up_ref.shape[1]
    start = pl.multiple_of(group_ref[0] * part, part)
    lane = pl.multiple_of(lax.div(start, jnp.int32(lanes)) * lanes, lanes)
    wait = fetch(
        [
            (up_hbm.at[:, pl.ds(lane, lanes)], up_ref),
            (down_hbm.at[pl.ds(start, part), :], out_ref.at[1]),
        ],
        sems,
    )
    wait(0)
    turned_ref[...] = up_ref[...].T
    out_ref[0] = turned_ref[pl.ds(pl.multiple_of(start - lane, part), part), :]
    wait(1)


def own_quarter(group, up, down, part):
    width, chunk = up.shape
    lanes = max(128, part)
    return pl.pallas_call(
        quarter_kernel,
        out_shape=jax.ShapeDtypeStruct((2, part, width), BF16),
        in_specs=[SMEM, HBM, HBM],
        out_specs=VMEM,
        scratch_shapes=[
            pltpu.VMEM((width, lanes), BF16),
            pltpu.VMEM((lanes, width), BF16),
            pltpu.SemaphoreType.DMA((2,)),
        ],
        compiler_params=params(56),
        cost_estimate=LONG,
        name="quarter",
    )(group, up, down)


def own_rows_kernel(group_ref, up_ref, down_ref, out_ref, turned_ref):
    part = out_ref.shape[2]
    turned_ref[...] = up_ref[...].T
    for index in range(4):
        quarter = jnp.bitwise_xor(group_ref[0], index)
        span = pl.ds(pl.multiple_of(quarter * part, part), part)
        out_ref[index, 0] = turned_ref[span, :]
        out_ref[index, 1] = down_ref[span, :]


def own_rows(group, up, down):
    width, chunk = up.shape
    return pl.pallas_call(
        own_rows_kernel,
        out_shape=jax.ShapeDtypeStruct((4, 2, chunk // 4, width), BF16),
        in_specs=[SMEM, VMEM, VMEM],
        out_specs=VMEM,
        scratch_shapes=[pltpu.VMEM((chunk, width), BF16)],
        compiler_params=params(16),
        cost_estimate=COST,
        name="own_rows",
    )(group, up, down)


def finish_rows(tokens, mixed, goal, scale):
    out = tokens + scale * mixed
    out_norm = jnp.sqrt(jnp.sum(out * out, axis=-1, keepdims=True) + STABILITY_EPSILON)
    goal_norm = jnp.sqrt(jnp.sum(goal * goal, axis=-1, keepdims=True) + STABILITY_EPSILON)
    norms = out_norm * goal_norm
    cosine = jnp.sum(out * goal, axis=-1, keepdims=True) / norms
    upstream = (cosine / (out_norm * out_norm)) * out - goal * (1.0 / norms)
    return upstream, 1.0 - cosine


def forward_kernel(first, blocks, sides, skipped, *refs):
    last = blocks > 0
    refs = list(refs[skipped:])
    normed_t_ref = refs.pop(0)
    own, other = refs[:sides], refs[sides:2 * sides]
    del refs[:2 * sides]
    mixed_in = None if first else refs.pop(0)
    if last:
        tokens_ref, scale_ref = refs[:2]
        targets, passed_ref = refs[2:2 + blocks], refs[2 + blocks]
        del refs[:3 + blocks]
    act_ref, slope_ref = refs[:2]
    del refs[:2]
    width, rows = normed_t_ref.shape
    part = act_ref.shape[2]
    part_sum = None
    downs = []
    for side, group in enumerate((own, other)):
        start = 0
        for ref in group:
            count = ref.shape[0]
            hiddens = dot_nn(ref[:, 0].reshape(count * part, width), normed_t_ref[...])
            for index in range(count):
                hidden = hiddens[index * part:(index + 1) * part]
                phi = 0.5 * (1.0 + lax.erf(hidden * (0.5 ** 0.5)))
                density = jnp.exp(-0.5 * hidden * hidden) * ((2.0 * jnp.pi) ** -0.5)
                act_ref[side, start + index] = (hidden * phi).astype(BF16)
                slope_ref[side, start + index] = phi + hidden * density
            downs.append(ref[:, 1].reshape(count * part, width))
            start += count
    if sides > 1 or last:
        act = act_ref[...].reshape(2 * start * part, rows)
        part_sum = dot_tn(act, jnp.concatenate(downs, axis=0))
    else:
        for side, down in enumerate(downs):
            term = dot_tn(act_ref[side].reshape(start * part, rows), down)
            part_sum = term if part_sum is None else part_sum + term
    if not last:
        mixed_out = refs[0]
        mixed_out[...] = part_sum if first else mixed_in[...] + part_sum
        return
    back_ref, back_t_ref, small_ref, mixed_ref = refs
    mixed_ref[...] = mixed_in[...] + part_sum
    scale = scale_ref[...]
    small_ref[...] = jnp.zeros_like(small_ref)
    piece = rows // blocks
    for index, target_ref in enumerate(targets):
        span = pl.ds(index * piece, piece)
        mixed = mixed_ref[span, :]
        goal = jnp.concatenate([target_ref[0], passed_ref[index]], axis=0).astype(F32)
        upstream, loss = finish_rows(tokens_ref[span, :].astype(F32), mixed, goal, scale)
        back = (upstream * scale).astype(BF16)
        back_ref[span, :] = back
        back_t_ref[:, span] = back.T
        small_ref[0:1, :] += jnp.sum(upstream * mixed, axis=0, keepdims=True)
        small_ref[1:2, :] += jnp.broadcast_to(jnp.sum(loss, axis=0, keepdims=True), (1, width))


def forward(normed_t, own, other, mixed=None, finish=None, after=()):
    width, rows = normed_t.shape
    part = own[0].shape[2]
    total = sum(array.shape[0] for array in own)
    first, last = mixed is None, finish is not None
    blocks = len(finish) - 3 if last else 0
    operands = [*after, normed_t, *own, *other]
    if not first:
        operands.append(mixed)
    if last:
        operands.extend(finish)
    piece = (2, total, part, rows)
    shapes = [jax.ShapeDtypeStruct(piece, BF16), jax.ShapeDtypeStruct(piece, F32)]
    scratch = []
    if last:
        shapes += [
            jax.ShapeDtypeStruct((rows, width), BF16),
            jax.ShapeDtypeStruct((width, rows), BF16),
            jax.ShapeDtypeStruct((8, width), F32),
        ]
        scratch = [pltpu.VMEM((rows, width), F32)]
    else:
        shapes += [jax.ShapeDtypeStruct((rows, width), F32)]
    return pl.pallas_call(
        functools.partial(forward_kernel, first, blocks, len(own), len(after)),
        out_shape=tuple(shapes),
        in_specs=[ANY] * len(after) + [VMEM] * (len(operands) - len(after)),
        out_specs=tuple([VMEM] * len(shapes)),
        scratch_shapes=scratch,
        compiler_params=params(32),
        cost_estimate=COST,
        name="forward",
    )(*operands)


def pack_kernel(counts, *refs):
    out_ref = refs[-1]
    start = 0
    for count, ref in zip(counts, refs):
        out_ref[start:start + count] = ref[...].reshape(count, *out_ref.shape[1:])
        start += count


def pack(pieces, *after):
    counts = [1 if piece.ndim == 3 else piece.shape[0] for piece in pieces]
    return pl.pallas_call(
        functools.partial(pack_kernel, counts),
        out_shape=jax.ShapeDtypeStruct((sum(counts), *pieces[0].shape[-3:]), BF16),
        in_specs=[VMEM] * len(pieces) + [ANY] * len(after),
        out_specs=VMEM,
        compiler_params=params(16),
        cost_estimate=COST,
        name="pack",
    )(*pieces, *after)


def turn_kernel(y_ref, x_ref, a_ref, b_ref):
    count = a_ref.shape[0]
    a_ref[...] = y_ref[:count]
    b_ref[...] = x_ref[count:]


def turn(y, x):
    count = y.shape[0]
    first = count // 2
    return pl.pallas_call(
        turn_kernel,
        out_shape=(
            jax.ShapeDtypeStruct((first, *y.shape[1:]), BF16),
            jax.ShapeDtypeStruct((count - first, *y.shape[1:]), BF16),
        ),
        in_specs=[VMEM] * 2,
        out_specs=(VMEM, VMEM),
        compiler_params=params(16),
        cost_estimate=COST,
        name="turn",
    )(y, x)


def tie_kernel(*refs):
    pass


def tie(array, *after):
    return pl.pallas_call(
        tie_kernel,
        out_shape=jax.ShapeDtypeStruct(array.shape, array.dtype),
        in_specs=[ANY] * (1 + len(after)),
        out_specs=ANY,
        input_output_aliases={0: 0},
        compiler_params=params(4),
        cost_estimate=COST,
        name="tie",
    )(array, *after)


def seconds_kernel(*refs):
    for index, ref in enumerate(refs[:-1]):
        refs[-1][index] = ref[1]


def seconds(blocks):
    count, (_, each, width) = len(blocks), blocks[0].shape
    return pl.pallas_call(
        seconds_kernel,
        out_shape=jax.ShapeDtypeStruct((count, each, width), BF16),
        in_specs=[VMEM] * count,
        out_specs=VMEM,
        compiler_params=params(16),
        cost_estimate=COST,
        name="seconds",
    )(*blocks)


def joined(refs, pieces, pick):
    values = [pick(refs[which], start, count) for which, start, count in pieces]
    flat = [value.reshape(-1, value.shape[-1]) for value in values]
    return flat[0] if len(flat) == 1 else jnp.concatenate(flat, axis=0)


def put(quarter, value, outs):
    own_ref, x_ref, y_ref, x_later_ref, y_later_ref = outs
    value = value.astype(BF16).reshape(own_ref.shape)
    half = x_ref.shape[0] // 2
    if quarter == 0:
        own_ref[...] = value
    elif quarter == 1:
        x_ref[half:] = value[:half]
        x_later_ref[...] = value[half:]
    elif quarter == 2:
        y_ref[half:] = value[half:]
        y_later_ref[...] = value[:half]
    else:
        x_ref[:half] = value[:half]
        y_ref[:half] = value[half:]


def emit(quarter, value, arrived, outs):
    if arrived is None:
        outs[0][quarter] = value.astype(BF16).reshape(outs[0].shape[1:])
    else:
        put(quarter, value + arrived[quarter].reshape(value.shape).astype(F32), outs)


def down_grad_kernel(side, act_pieces, add, *refs):
    acts, back_ref = refs[:2], refs[2]
    arrived = refs[3] if add else None
    outs = refs[4:] if add else refs[3:]
    for quarter in (3, 1, 2, 0):
        act = joined(acts, act_pieces[quarter], lambda ref, a, n: ref[side, a:a + n])
        emit(quarter, dot_nn(act, back_ref[...]), arrived, outs)


def up_grad_kernel(side, weight_pieces, act_pieces, add, *refs):
    weights, slopes = refs[:2], refs[2:4]
    back_t_ref, normed_ref, gain_in = refs[4:7]
    if add:
        arrived, scale_ref, small_ref = refs[7:10]
        outs, vector_ref, gain_ref = refs[10:-2], refs[-2], refs[-1]
    else:
        arrived = None
        outs, gain_ref = refs[7:-1], refs[-1]
    gain_ref[...] = gain_in[...]
    for quarter in (3, 1, 2, 0):
        pieces = weight_pieces[quarter]
        slope = joined(slopes, act_pieces[quarter], lambda ref, a, n: ref[side, a:a + n])
        back_act = dot_nn(joined(weights, pieces, lambda ref, a, n: ref[a:a + n, 1]), back_t_ref[...])
        back_hidden = (back_act * slope).astype(BF16)
        grad = dot_nn(back_hidden, normed_ref[...])
        up = joined(weights, pieces, lambda ref, a, n: ref[a:a + n, 0]).astype(F32)
        gain_ref[...] += jnp.sum(grad * up, axis=0, keepdims=True)
        emit(quarter, grad, arrived, outs)
    if add:
        vector_ref[0:1, :] = gain_ref[...] / scale_ref[...]
        vector_ref[1:3, :] = small_ref[0:2, :]
        vector_ref[3:8, :] = jnp.zeros((5, gain_ref.shape[1]), F32)


def gradient_shapes(depth, part, width, add):
    if not add:
        return [jax.ShapeDtypeStruct((4, depth, part, width), BF16)]
    counts = (depth, depth, depth, depth - depth // 2, depth // 2)
    return [jax.ShapeDtypeStruct((count, part, width), BF16) for count in counts]


def down_gradient(side, act_pieces, depth, acts, back, arrived=None):
    part = acts[0].shape[2]
    width = back.shape[1]
    add = arrived is not None
    operands = [*acts, back] + ([arrived] if add else [])
    shapes = gradient_shapes(depth, part, width, add)
    return pl.pallas_call(
        functools.partial(down_grad_kernel, side, act_pieces, add),
        out_shape=tuple(shapes),
        in_specs=[VMEM] * len(operands),
        out_specs=tuple([VMEM] * len(shapes)),
        compiler_params=params(20),
        cost_estimate=COST,
        name="down_gradient",
    )(*operands)


def up_gradient(
    side, weight_pieces, act_pieces, depth, weights, slopes, back_t, normed, gain, extra=()
):
    part, width = weights[0].shape[2:]
    add = len(extra) > 0
    operands = [*weights, *slopes, back_t, normed, gain, *extra]
    shapes = gradient_shapes(depth, part, width, add)
    if add:
        shapes.append(jax.ShapeDtypeStruct((8, width), F32))
        scratch = [pltpu.VMEM((1, width), F32)]
    else:
        scratch = []
        shapes.append(jax.ShapeDtypeStruct((1, width), F32))
    return pl.pallas_call(
        functools.partial(up_grad_kernel, side, weight_pieces, act_pieces, add),
        out_shape=tuple(shapes),
        in_specs=[VMEM] * len(operands),
        out_specs=tuple([VMEM] * len(shapes)),
        scratch_shapes=scratch,
        compiler_params=params(24),
        cost_estimate=COST,
        name="up_gradient",
    )(*operands)


def merge_kernel(x_ref, y_ref, x_later_ref, y_later_ref, *refs):
    x_out, y_out = refs[-2:]
    half = y_later_ref.shape[0]
    x_out[...] = (x_later_ref[...].astype(F32) + y_ref[:half].astype(F32)).astype(BF16)
    y_out[...] = (y_later_ref[...].astype(F32) + x_ref[:half].astype(F32)).astype(BF16)


def merge(x, y, x_later, y_later, *after):
    return pl.pallas_call(
        merge_kernel,
        out_shape=tuple(jax.ShapeDtypeStruct(a.shape, BF16) for a in (x_later, y_later)),
        in_specs=[VMEM] * 4 + [ANY] * len(after),
        out_specs=(VMEM, VMEM),
        compiler_params=params(16),
        cost_estimate=COST,
        name="merge",
    )(x, y, x_later, y_later, *after)


def total_kernel(own_ref, x_ref, y_ref, x_late_ref, y_late_ref, *refs):
    outs = refs[-own_ref.shape[0]:]
    half = y_late_ref.shape[0]
    for index, out in enumerate(outs):
        total = own_ref[index].astype(F32)
        if index < half:
            total += x_ref[half + index].astype(F32) + y_late_ref[index].astype(F32)
        else:
            total += y_ref[index].astype(F32) + x_late_ref[index - half].astype(F32)
        out[...] = total.astype(BF16)


def totals(own, x, y, x_late, y_late, *after):
    count, part, width = own.shape
    return pl.pallas_call(
        total_kernel,
        out_shape=tuple([jax.ShapeDtypeStruct((part, width), BF16)] * count),
        in_specs=[VMEM] * 5 + [ANY] * len(after),
        out_specs=tuple([VMEM] * count),
        compiler_params=params(16),
        cost_estimate=COST,
        name="totals",
    )(own, x, y, x_late, y_late, *after)


def collect_kernel(count, *refs):
    total = refs[0][...].astype(F32)
    for ref in refs[1:count]:
        total = total + ref[...].astype(F32)
    refs[-1][...] = total.astype(BF16)


def collect(parts, *after):
    return pl.pallas_call(
        functools.partial(collect_kernel, len(parts)),
        out_shape=jax.ShapeDtypeStruct(parts[0].shape, BF16),
        in_specs=[VMEM] * len(parts) + [ANY] * len(after),
        out_specs=VMEM,
        compiler_params=params(16),
        cost_estimate=COST,
        name="collect",
    )(*parts, *after)


def join_kernel(total_ref, vector_ref, other_ref, *refs):
    short_ref, long_ref, held_ref = refs[-3:]
    part = total_ref.shape[0]
    short_ref[pl.ds(0, part), :] = total_ref[...]
    rest = vector_ref[0:3, :]
    held_ref[...] = jnp.zeros_like(held_ref)
    for index in range(3):
        piece = rest.astype(BF16).astype(F32)
        held_ref[3 * index:3 * index + 3, :] = piece
        rest = rest - piece
    short_ref[pl.ds(part, 16), :] = held_ref[...].astype(BF16)
    long_ref[pl.ds(0, part + 16), :] = short_ref[...]
    long_ref[pl.ds(part + 16, part), :] = other_ref[...]


def join(total, vector, other, *after):
    part, width = total.shape
    return pl.pallas_call(
        join_kernel,
        out_shape=tuple(
            jax.ShapeDtypeStruct((rows, width), BF16) for rows in (part + 16, 2 * part + 16)
        ),
        in_specs=[VMEM] * 3 + [ANY] * len(after),
        out_specs=(VMEM, VMEM),
        scratch_shapes=[pltpu.VMEM((16, width), F32)],
        compiler_params=params(16),
        cost_estimate=COST,
        name="join",
    )(total, vector, other, *after)


def place_kernel(part, tokens, group_ref, *refs):
    ups, downs = refs[:4], refs[4:8]
    up_ref, down_ref, gain_ref, scale_ref, loss_ref, held_ref = refs[8:]
    group = group_ref[0]
    vectors = []
    for index, (up, down) in enumerate(zip(ups, downs)):
        first = pl.multiple_of(jnp.bitwise_xor(group, index) * part, part)
        held_ref[pl.ds(first, part), :] = up[pl.ds(0, part), :].astype(F32)
        start = down.shape[0] - part
        down_ref[pl.ds(first, part), :] = down[pl.ds(start, part), :].astype(F32)
        rows = up[pl.ds(part, 16), :].astype(F32)
        vectors.append((rows[0:3] + rows[3:6]) + rows[6:9])
    up_ref[...] = held_ref[...].T
    vector = (vectors[0] + vectors[1]) + (vectors[2] + vectors[3])
    gain_ref[...] = vector[0:1]
    scale_ref[...] = vector[1:2]
    loss_ref[...] = vector[2:3, 0:1] * (1.0 / tokens)


def place_quarters(group, ups, downs, part, tokens):
    width = ups[0].shape[1]
    shapes = [
        jax.ShapeDtypeStruct((width, 4 * part), F32),
        jax.ShapeDtypeStruct((4 * part, width), F32),
        jax.ShapeDtypeStruct((1, width), F32),
        jax.ShapeDtypeStruct((1, width), F32),
        jax.ShapeDtypeStruct((1, 1), F32),
    ]
    return pl.pallas_call(
        functools.partial(place_kernel, part, tokens),
        out_shape=tuple(shapes),
        in_specs=[SMEM] + [VMEM] * 8,
        out_specs=tuple([VMEM] * len(shapes)),
        scratch_shapes=[pltpu.VMEM((4 * part, width), F32)],
        compiler_params=params(16),
        cost_estimate=COST,
        name="place",
    )(group, *ups, *downs)


def shards_square(
    image_tokens,
    tile_lists,
    opacity,
    tile_counts,
    ray_pixel,
    block_owner,
    gaussian_features,
    layer_norm_gain,
    layer_scale,
    up_weight,
    down_weight,
):
    ray_count = lax.axis_size("ray")
    group_count = lax.axis_size("grp")
    depth = ray_count // 2
    group = lax.axis_index("grp").reshape(1)
    me = lax.axis_index("ray").reshape(1)
    rows, width = image_tokens.shape
    part = down_weight.shape[0] // group_count

    def beside(array, flip):
        return lax.ppermute(array, "grp", [(g, g ^ flip) for g in range(group_count)])

    def partner(array, flip=1):
        return lax.ppermute(array, "ray", [(r, r ^ flip) for r in range(ray_count)])

    def along(array, shift):
        pairs = [(r, (r + 2 * shift) % ray_count) for r in range(ray_count)]
        return lax.ppermute(array, "ray", pairs)

    mine = own_quarter(group, up_weight, down_weight, part)
    arrivals = [along(mine, -shift) for shift in range(1, depth)]
    rendered = render(
        ray_count, True, me, block_owner, tile_lists, opacity, tile_counts.reshape(1, rows),
        ray_pixel, gaussian_features,
    )
    half = depth // 2
    low = pack(arrivals[:half - 1], rendered[0])
    x_low, y_low = beside(low, 1), beside(low, 2)
    high = pack(arrivals[half - 1:], low)
    high = tie(high, x_low, y_low)
    x_high, y_high = beside(high, 1), beside(high, 2)
    targets = [rendered[0]] + [along(rendered[shift], shift) for shift in range(1, depth)]
    tokens, normed, normed_t = prepare_tokens(
        ray_count, True, me, block_owner, ray_pixel, image_tokens,
        layer_norm_gain.reshape(1, width),
    )
    most = pack(
        [own_rows(group, up_weight, down_weight), low, x_low, y_low, high, x_high, y_high],
        normed, targets[1], *targets[half + 1:],
    )
    most_other = partner(most)
    d_low, d_high = beside(y_low, 1), beside(x_high, 2)
    act_most, slope_most, mixed = forward(normed_t, [most], [most_other])
    late = targets[2:half + 1]
    last = pack([d_low, d_high], mixed, *late)
    last_other = partner(last)
    act_last, slope_last, back, back_t, small = forward(
        normed_t, [last], [last_other], mixed,
        (tokens, layer_scale.reshape(1, width), *targets, partner(seconds(targets))),
    )
    acts, slopes = (act_most, act_last), (slope_most, slope_last)
    weights = ((most, last), (most_other, last_other))
    count, rest = half - 1, depth - half
    start = 4 + 3 * count
    pieces = tuple(
        ((0, q, 1), (0, 4 + q * count, count), (0, start + q * rest, rest)) for q in range(3)
    ) + (((0, 3, 1), (1, 0, depth - 1)),)
    gain = jnp.zeros((1, width), F32)
    (down_other,) = down_gradient(1, pieces, depth, acts, back)
    down_arrived = partner(down_other)
    up_other, gain = up_gradient(
        1, pieces, pieces, depth, weights[1], slopes, back_t, normed, gain
    )
    up_arrived = partner(up_other)
    down_sums = down_gradient(0, pieces, depth, acts, back, down_arrived)
    *up_sums, vector = up_gradient(
        0, pieces, pieces, depth, weights[0], slopes, back_t, normed, gain,
        (up_arrived, layer_norm_gain.reshape(1, width), small),
    )
    vector = vector + partner(vector)
    flip = 2
    while flip < ray_count:
        vector = vector + partner(vector, flip)
        flip *= 2

    def first_step(to_x, to_y, x_later, y_later, *after):
        from_x, from_y = beside(to_x, 1), beside(to_y, 2)
        return from_x, from_y, merge(from_x, from_y, x_later, y_later, *after)

    def second_step(later):
        return beside(later[0], 1), beside(later[1], 2)

    def arrive_along(shares):
        return [shares[0]] + [along(shares[shift], shift) for shift in range(1, depth)]

    own, *rest = down_sums
    own_up, to_x, to_y, *rest_up = up_sums
    from_x, from_y, later = first_step(*rest, vector)
    late = second_step(later)
    shares = totals(own, from_x, from_y, *late)
    from_x, from_y, later = first_step(to_x, to_y, *rest_up)
    up_shares = totals(own_up, from_x, from_y, *second_step(later))
    down_total = collect(arrive_along(shares), up_shares[0])
    down_x, down_y = beside(down_total, 1), beside(down_total, 2)
    up_total = collect(arrive_along(up_shares))
    short, long = join(up_total, vector, down_total, down_x, down_y)
    up_x, up_y, both = beside(short, 1), beside(short, 2), beside(long, 3)
    grad_up, grad_down, gain, scale, loss = place_quarters(
        group, (short, up_x, up_y, both), (down_total, down_x, down_y, both), part,
        rows * ray_count * group_count,
    )
    return (grad_up, grad_down, gain.reshape(width), scale.reshape(width), loss.reshape(()))


def shards(*operands):
    ray_count, group_count = lax.axis_size("ray"), lax.axis_size("grp")
    hidden = operands[-1].shape[0]
    square = group_count == 4 and ray_count in (8, 16) and hidden % (16 * group_count) == 0
    return (shards_square if square else shards_general)(*operands)


def solution(mesh):
    return jax.shard_map(
        shards,
        mesh=mesh,
        in_specs=(
            P(("grp", "ray"), None),
            P(None, ("grp", "ray")),
            P(None, ("grp", "ray")),
            P(("grp", "ray")),
            P("grp", None),
            P("grp", None),
            P(("grp", "ray"), None),
            P(),
            P(),
            P(None, "ray"),
            P("ray", None),
        ),
        out_specs=(P(None, "ray"), P("ray", None), P(), P(), P()),
        check_vma=False,
    )
```

```python
import functools

import jax
import jax.numpy as jnp
from jax import lax
from jax.experimental import pallas as pl
from jax.experimental.pallas import tpu as pltpu
from jax.sharding import PartitionSpec as P

STABILITY_EPSILON = 1e-06
F32 = jnp.float32
BF16 = jnp.bfloat16
MIB = 1024 * 1024
COST = pl.CostEstimate(flops=1 << 20, bytes_accessed=1 << 16, transcendentals=0)
LONG = pl.CostEstimate(flops=10**10, bytes_accessed=1 << 20, transcendentals=0)
SMEM = pl.BlockSpec(memory_space=pltpu.SMEM)
VMEM = pl.BlockSpec(memory_space=pltpu.VMEM)
ANY = pl.BlockSpec(memory_space=pl.ANY)


def params(mib=48, **more):
    return pltpu.CompilerParams(vmem_limit_bytes=mib * MIB, **more)


def dot_nn(a, b):
    return lax.dot_general(a, b, (((1,), (0,)), ((), ())), preferred_element_type=F32)


def dot_tn(a, b):
    return lax.dot_general(a, b, (((0,), (0,)), ((), ())), preferred_element_type=F32)


def dot_nt(a, b):
    return lax.dot_general(a, b, (((1,), (1,)), ((), ())), preferred_element_type=F32)


def owner_of(pixels, owner_ref, rows, count):
    block = lax.div(pixels, jnp.int32(rows))
    owner = jnp.zeros_like(pixels)
    for slot in range(count):
        owner = jnp.where(block == slot, owner_ref[0:1, slot:slot + 1], owner)
    return owner


def earlier(rows):
    before = lax.broadcasted_iota(jnp.int32, (rows, rows), 0)
    after = lax.broadcasted_iota(jnp.int32, (rows, rows), 1)
    return jnp.where(before < after, 1.0, 0.0).astype(BF16)


HBM = pl.BlockSpec(memory_space=pltpu.HBM)


def fetch(copies, sems):
    started = [
        pltpu.make_async_copy(source, target, sems.at[index])
        for index, (source, target) in enumerate(copies)
    ]
    for copy in started:
        copy.start()

    def wait(*numbers):
        for number in numbers:
            started[number].wait()

    return wait


def render_kernel(
    ray_count, relative, me_ref, owner_hbm, lists_hbm, opacity_hbm, counts_hbm, pixels_hbm,
    features_hbm, *refs,
):
    outs = refs[:-10]
    owner_ref, ids_ref, opacity_ref, counts_ref, mine_ref, features_ref = refs[-10:-4]
    share_ref, table_ref, send_ref, sems = refs[-4:]
    depth, rays = lists_hbm.shape
    gauss = features_hbm.shape[0]
    width = features_hbm.shape[1]
    me = me_ref[0]
    own_pixels = pixels_hbm.at[:, pl.ds(pl.multiple_of(me * rays, rays), rays)]
    wait = fetch(
        [
            (lists_hbm, ids_ref), (opacity_hbm, opacity_ref), (counts_hbm, counts_ref),
            (owner_hbm, owner_ref), (own_pixels, mine_ref), (features_hbm, features_ref),
        ],
        sems,
    )
    wait(0, 1, 2)
    ids_ref[...] = ids_ref[...] - me * gauss
    passing = jnp.ones((1, rays), F32)
    counts = counts_ref[...]
    for level in range(depth):
        alpha = opacity_ref[pl.ds(level, 1), :]
        share_ref[pl.ds(level, 1), :] = jnp.where(level < counts, alpha * passing, 0.0)
        passing = passing * (1.0 - alpha)

    tile = 256
    lanes = 128
    columns = rays // lanes

    @pl.loop(0, (gauss // tile) * columns)
    def _(step):
        first = pl.multiple_of(lax.div(step, columns) * tile, tile)
        lane = pl.multiple_of(lax.rem(step, columns) * lanes, lanes)
        number = (lax.broadcasted_iota(jnp.int32, (tile, lanes), 0) + first).astype(jnp.int16)
        total = jnp.zeros((tile, lanes), BF16)
        for level in range(depth):
            ident = jnp.broadcast_to(ids_ref[pl.ds(level, 1), pl.ds(lane, lanes)], (16, lanes))
            share = jnp.broadcast_to(share_ref[pl.ds(level, 1), pl.ds(lane, lanes)], (16, lanes))
            ident = jnp.concatenate([ident.astype(jnp.int16)] * (tile // 16), axis=0)
            share = jnp.concatenate([share.astype(BF16)] * (tile // 16), axis=0)
            total = total + jnp.where(ident == number, share, jnp.zeros_like(share))
        table_ref[pl.ds(first, tile), pl.ds(lane, lanes)] = total

    wait(3, 4, 5)
    owner = owner_of(mine_ref[...], owner_ref, rays, ray_count)
    padded = -(-ray_count // 16) * 16
    member = (lax.broadcasted_iota(jnp.int32, (padded, rays), 0) == owner)
    ranks = dot_nn(member.astype(F32).astype(BF16), earlier(rays))
    rank = jnp.sum(jnp.where(member, ranks, 0.0), axis=0, keepdims=True).astype(jnp.int32)
    if relative:
        chips = ray_count // 2
        shift = lax.div(owner, jnp.int32(2)) - lax.div(me, jnp.int32(2))
        shift = jnp.where(shift < 0, shift + chips, shift)
        flip = jnp.where(lax.rem(owner, jnp.int32(2)) == lax.rem(me, jnp.int32(2)), 0, 1)
        block = 2 * shift + flip
    else:
        block = owner
    slot = block * (rays // ray_count) + rank
    send_ref[...] = (
        (lax.broadcasted_iota(jnp.int32, (rays, rays), 0) == slot).astype(F32).astype(BF16)
    )

    piece = 256
    span = rays // len(outs)

    @pl.loop(0, width // piece)
    def _(step):
        cols = pl.ds(pl.multiple_of(step * piece, piece), piece)
        rendered = dot_tn(table_ref[...], features_ref[:, cols]).astype(BF16)
        ordered = dot_nn(send_ref[...], rendered).astype(BF16)
        for index, out in enumerate(outs):
            rows = ordered[index * span:(index + 1) * span]
            out[:, :, cols] = rows.reshape(*out.shape[:2], piece)


def render(ray_count, relative, me, owner, lists, opacity, counts, pixels, features):
    depth, rays = lists.shape
    gauss, width = features.shape
    parts = ray_count // 2 if relative else 1
    shape = jax.ShapeDtypeStruct((ray_count // parts, rays // ray_count, width), BF16)
    return pl.pallas_call(
        functools.partial(render_kernel, ray_count, relative),
        out_shape=(shape,) * parts,
        in_specs=[SMEM] + [HBM] * 6,
        out_specs=(VMEM,) * parts,
        scratch_shapes=[
            pltpu.VMEM(owner.shape, jnp.int32),
            pltpu.VMEM((depth, rays), jnp.int32),
            pltpu.VMEM((depth, rays), F32),
            pltpu.VMEM((1, rays), jnp.int32),
            pltpu.VMEM((1, rays), jnp.int32),
            pltpu.VMEM((gauss, width), BF16),
            pltpu.VMEM((depth, rays), F32),
            pltpu.VMEM((gauss, rays), BF16),
            pltpu.VMEM((rays, rays), BF16),
            pltpu.SemaphoreType.DMA((6,)),
        ],
        compiler_params=params(20),
        cost_estimate=COST,
        name="render",
    )(me, owner, lists, opacity, counts, pixels, features)


def tokens_kernel(
    ray_count, relative, me_ref, owner_hbm, pixels_hbm, tokens_hbm, gain_hbm,
    *refs,
):
    tokens_out, normed_out, normed_t_out = refs[-11:-8]
    owner_ref, pixels_ref, tokens_ref, gain_ref, order_ref, rank_ref, place_ref, sems = refs[-8:]
    rows, width = tokens_hbm.shape
    me = me_ref[0]
    each = rows // ray_count
    wait = fetch(
        [
            (owner_hbm, owner_ref), (pixels_hbm, pixels_ref), (gain_hbm, gain_ref),
            (tokens_hbm, tokens_ref),
        ],
        sems,
    )
    wait(0, 1)
    pixels = jnp.concatenate(
        [pixels_ref[:, sender * rows:(sender + 1) * rows] for sender in range(ray_count)], axis=0
    )
    mine = owner_of(pixels, owner_ref, rows, ray_count) == me
    place_ref[...] = lax.rem(pixels, jnp.int32(rows)).astype(F32)
    member = jnp.where(mine, 1.0, 0.0)
    padded = -(-ray_count // 16) * 16
    if padded > ray_count:
        spread = jnp.concatenate([member, jnp.zeros((padded - ray_count, rows), F32)], axis=0)
    else:
        spread = member
    ranks = dot_nn(spread.astype(BF16), earlier(rows))
    rank_ref[...] = jnp.where(mine, ranks[:ray_count], -1.0)
    chips = ray_count // 2
    for index in range(ray_count):
        if relative:
            chip = lax.rem(lax.div(me, jnp.int32(2)) + (chips - index // 2), jnp.int32(chips))
            sender = 2 * chip + jnp.bitwise_xor(lax.rem(me, jnp.int32(2)), index % 2)
        else:
            sender = index
        rank = rank_ref[pl.ds(sender, 1), :].astype(jnp.int32)
        hit = lax.broadcasted_iota(jnp.int32, (each, rows), 0) == rank
        at = jnp.sum(
            jnp.where(hit, place_ref[pl.ds(sender, 1), :], 0.0), axis=1, keepdims=True
        )
        here = lax.broadcasted_iota(jnp.int32, (each, rows), 1) == at.astype(jnp.int32)
        order_ref[pl.ds(index * each, each), :] = here.astype(F32).astype(BF16)
    wait(2, 3)
    half = min(128, rows)
    gain = gain_ref[...]

    @pl.loop(0, rows // half)
    def _(step):
        span = pl.ds(pl.multiple_of(step * half, half), half)
        values = dot_nn(order_ref[span, :], tokens_ref[...])
        tokens_out[span, :] = values.astype(BF16)
        centered = values - jnp.mean(values, axis=-1, keepdims=True)
        variance = jnp.mean(centered * centered, axis=-1, keepdims=True)
        xhat = centered * lax.rsqrt(variance + STABILITY_EPSILON)
        normed = (xhat * gain).astype(BF16)
        normed_out[span, :] = normed
        normed_t_out[:, span] = normed.T


def prepare_tokens(ray_count, relative, me, owner, pixels, tokens, gain, after=()):
    rows, width = tokens.shape
    return pl.pallas_call(
        functools.partial(tokens_kernel, ray_count, relative),
        out_shape=(
            jax.ShapeDtypeStruct((rows, width), BF16),
            jax.ShapeDtypeStruct((rows, width), BF16),
            jax.ShapeDtypeStruct((width, rows), BF16),
        ),
        in_specs=[SMEM] + [HBM] * 4 + [ANY] * len(after),
        out_specs=(VMEM, VMEM, VMEM),
        scratch_shapes=[
            pltpu.VMEM(owner.shape, jnp.int32),
            pltpu.VMEM(pixels.shape, jnp.int32),
            pltpu.VMEM((rows, width), BF16),
            pltpu.VMEM((1, width), F32),
            pltpu.VMEM((rows, rows), BF16),
            pltpu.VMEM((ray_count, rows), F32),
            pltpu.VMEM((ray_count, rows), F32),
            pltpu.SemaphoreType.DMA((4,)),
        ],
        compiler_params=params(20),
        cost_estimate=COST,
        name="tokens",
    )(me, owner, pixels, tokens, gain, *after)


def up_kernel(normed_ref, up_ref, act_ref, slope_ref):
    parts, _, part_rows, width = up_ref.shape
    up = up_ref[...].reshape(parts * part_rows, width)
    rows = normed_ref.shape[0]
    piece = min(128, rows)

    @pl.loop(0, rows // piece)
    def _(step):
        span = pl.ds(pl.multiple_of(step * piece, piece), piece)
        hidden = dot_nn(normed_ref[span, :], up)
        phi = 0.5 * (1.0 + lax.erf(hidden * (0.5 ** 0.5)))
        density = jnp.exp(-0.5 * hidden * hidden) * ((2.0 * jnp.pi) ** -0.5)
        act_ref[span, :] = (hidden * phi).astype(BF16)
        slope_ref[span, :] = (phi + hidden * density).astype(slope_ref.dtype)


def project_up(normed, up):
    rows, width = normed.shape
    parts, chunks, part_rows, chunk = up.shape
    return pl.pallas_call(
        up_kernel,
        grid=(chunks,),
        out_shape=(
            jax.ShapeDtypeStruct((rows, chunks * chunk), BF16),
            jax.ShapeDtypeStruct((rows, chunks * chunk), F32),
        ),
        in_specs=[
            pl.BlockSpec((rows, width), lambda j: (0, 0)),
            pl.BlockSpec((parts, 1, part_rows, chunk), lambda j: (0, j, 0, 0)),
        ],
        out_specs=(
            pl.BlockSpec((rows, chunk), lambda j: (0, j)),
            pl.BlockSpec((rows, chunk), lambda j: (0, j)),
        ),
        compiler_params=params(dimension_semantics=("arbitrary",)),
        cost_estimate=COST,
        name="up",
    )(normed, up)


def down_kernel(
    chunks, act_ref, down_ref, tokens_ref, target_ref, scale_ref,
    grad_ref, back_ref, small_ref, mixed_ref,
):
    step = pl.program_id(0)
    rows, width = tokens_ref.shape
    act = act_ref[...]

    @pl.when(step < chunks)
    def _():
        parts, _, part_rows, _ = down_ref.shape
        part = dot_nn(act, down_ref[...].reshape(parts * part_rows, width))

        @pl.when(step == 0)
        def _():
            mixed_ref[...] = part

        @pl.when(step > 0)
        def _():
            mixed_ref[...] += part

    @pl.when(step == chunks - 1)
    def _():
        scale = scale_ref[...]
        small_ref[...] = jnp.zeros_like(small_ref)
        piece = min(64, rows)

        @pl.loop(0, rows // piece)
        def _(index):
            span = pl.ds(pl.multiple_of(index * piece, piece), piece)
            mixed = mixed_ref[span, :]
            out = tokens_ref[span, :].astype(F32) + scale * mixed
            goal = target_ref[span, :].astype(F32)
            out_norm = jnp.sqrt(jnp.sum(out * out, axis=-1, keepdims=True) + STABILITY_EPSILON)
            goal_norm = jnp.sqrt(jnp.sum(goal * goal, axis=-1, keepdims=True) + STABILITY_EPSILON)
            norms = out_norm * goal_norm
            cosine = jnp.sum(out * goal, axis=-1, keepdims=True) / norms
            upstream = (cosine / (out_norm * out_norm)) * out - goal * (1.0 / norms)
            back_ref[span, :] = (upstream * scale).astype(BF16)
            small_ref[0:1, :] += jnp.sum(upstream * mixed, axis=0, keepdims=True)
            loss = jnp.sum(1.0 - cosine, axis=0, keepdims=True)
            small_ref[1:2, :] += jnp.broadcast_to(loss, (1, width))

    @pl.when(step >= chunks)
    def _():
        grad = dot_tn(act, back_ref[...])
        grad_ref[...] = grad.astype(BF16).reshape(grad_ref.shape)


def project_down(act, down, tokens, target, scale):
    rows, width = tokens.shape
    parts, chunks, part_rows, _ = down.shape
    chunk = parts * part_rows
    return pl.pallas_call(
        functools.partial(down_kernel, chunks),
        grid=(2 * chunks,),
        out_shape=(
            jax.ShapeDtypeStruct(down.shape, BF16),
            jax.ShapeDtypeStruct((rows, width), BF16),
            jax.ShapeDtypeStruct((8, width), F32),
        ),
        in_specs=[
            pl.BlockSpec((rows, chunk), lambda j: (0, lax.rem(j, chunks))),
            pl.BlockSpec(
                (parts, 1, part_rows, width), lambda j: (0, jnp.minimum(j, chunks - 1), 0, 0)
            ),
            pl.BlockSpec((rows, width), lambda j: (0, 0)),
            pl.BlockSpec((rows, width), lambda j: (0, 0)),
            pl.BlockSpec((1, width), lambda j: (0, 0)),
        ],
        out_specs=(
            pl.BlockSpec(
                (parts, 1, part_rows, width), lambda j: (0, jnp.maximum(j - chunks, 0), 0, 0)
            ),
            pl.BlockSpec((rows, width), lambda j: (0, 0)),
            pl.BlockSpec((8, width), lambda j: (0, 0)),
        ),
        scratch_shapes=[pltpu.VMEM((rows, width), F32)],
        compiler_params=params(dimension_semantics=("arbitrary",)),
        cost_estimate=COST,
        name="down",
    )(act, down, tokens, target, scale)


def back_kernel(back_ref, down_ref, slope_ref, normed_t_ref, up_ref, gain_ref, grad_ref, sum_ref):
    step = pl.program_id(0)
    parts, _, part_rows, width = down_ref.shape
    chunk = parts * part_rows
    rows = back_ref.shape[0]
    back_act = dot_nt(back_ref[...], down_ref[...].reshape(chunk, width))
    back_hidden = (back_act * slope_ref[...]).astype(BF16)
    up_parts, _, up_rows, _ = up_ref.shape

    @pl.when(step == 0)
    def _():
        sum_ref[...] = jnp.zeros_like(sum_ref)

    grad = dot_nn(normed_t_ref[...], back_hidden)
    grad_ref[...] = grad.astype(BF16).reshape(grad_ref.shape)
    up = up_ref[...].reshape(up_parts * up_rows, chunk).astype(F32)
    sum_ref[...] += jnp.sum(grad * up, axis=1, keepdims=True) / gain_ref[...]


def back_up(back, down, slope, normed_t, up, gain):
    width, rows = normed_t.shape
    parts, chunks, part_rows, _ = down.shape
    chunk = parts * part_rows
    up_parts, _, up_rows, _ = up.shape
    return pl.pallas_call(
        back_kernel,
        grid=(chunks,),
        out_shape=(
            jax.ShapeDtypeStruct(up.shape, BF16),
            jax.ShapeDtypeStruct((width, 1), F32),
        ),
        in_specs=[
            pl.BlockSpec((rows, width), lambda j: (0, 0)),
            pl.BlockSpec((parts, 1, part_rows, width), lambda j: (0, j, 0, 0)),
            pl.BlockSpec((rows, chunk), lambda j: (0, j)),
            pl.BlockSpec((width, rows), lambda j: (0, 0)),
            pl.BlockSpec((up_parts, 1, up_rows, chunk), lambda j: (0, j, 0, 0)),
            pl.BlockSpec((width, 1), lambda j: (0, 0)),
        ],
        out_specs=(
            pl.BlockSpec((up_parts, 1, up_rows, chunk), lambda j: (0, j, 0, 0)),
            pl.BlockSpec((width, 1), lambda j: (0, 0)),
        ),
        compiler_params=params(dimension_semantics=("arbitrary",)),
        cost_estimate=COST,
        name="back",
    )(back, down, slope, normed_t, up, gain)


def gather_weight(weight, parts, group, group_count, ray_count):
    rows, cols = weight.shape
    if parts == 1:
        whole = lax.all_gather(weight, "ray", axis=0, tiled=True)
    else:
        part = lax.dynamic_slice_in_dim(weight, group * (rows // parts), rows // parts, 0)
        whole = lax.all_gather(part, ("grp", "ray"), axis=0, tiled=True)
    return whole.reshape(parts, ray_count, rows // parts, cols)


def reduce_gradient(grad):
    parts, ray_count, part_rows, cols = grad.shape
    flat = grad.reshape(parts * ray_count * part_rows, cols)
    if parts == 1:
        share = lax.psum_scatter(flat, "ray", scatter_dimension=0, tiled=True)
        return lax.psum(share.astype(F32), "grp")
    share = lax.psum_scatter(flat, "grp", scatter_dimension=0, tiled=True)
    share = lax.psum_scatter(share, "ray", scatter_dimension=0, tiled=True)
    return lax.all_gather(share, "grp", axis=0, tiled=True).astype(F32)


def shards_general(
    image_tokens,
    tile_lists,
    opacity,
    tile_counts,
    ray_pixel,
    block_owner,
    gaussian_features,
    layer_norm_gain,
    layer_scale,
    up_weight,
    down_weight,
):
    ray_count = lax.axis_size("ray")
    group_count = lax.axis_size("grp")
    group = lax.axis_index("grp")
    me = lax.axis_index("ray").reshape(1)
    rows, width = image_tokens.shape
    up_parts = group_count if up_weight.shape[0] % (16 * group_count) == 0 else 1
    down_parts = group_count if down_weight.shape[0] % (16 * group_count) == 0 else 1
    up = gather_weight(up_weight, up_parts, group, group_count, ray_count)
    down = gather_weight(down_weight, down_parts, group, group_count, ray_count)
    rendered = render(
        ray_count, False, me, block_owner, tile_lists, opacity, tile_counts.reshape(1, rows),
        ray_pixel, gaussian_features,
    )
    rendered = rendered[0].reshape(rows, width)
    target = lax.all_to_all(rendered, "ray", split_axis=0, concat_axis=0, tiled=True)
    tokens, normed, normed_t = prepare_tokens(
        ray_count, False, me, block_owner, ray_pixel, image_tokens,
        layer_norm_gain.reshape(1, width),
    )
    act, slope = project_up(normed, up)
    grad_down, back, small = project_down(act, down, tokens, target, layer_scale.reshape(1, width))
    grad_up, gain_sum = back_up(back, down, slope, normed_t, up, layer_norm_gain.reshape(width, 1))
    grad_down = reduce_gradient(grad_down)
    grad_up = reduce_gradient(grad_up)
    sums = jnp.concatenate([gain_sum.reshape(1, width), small[:2]], axis=0)
    sums = lax.psum(sums, ("grp", "ray"))
    loss = sums[2, 0] / (rows * ray_count * group_count)
    return (grad_up, grad_down, sums[0], sums[1], loss)


def quarter_kernel(group_ref, up_hbm, down_hbm, out_ref, up_ref, turned_ref, sems):
    part = out_ref.shape[1]
    lanes = up_ref.shape[1]
    start = pl.multiple_of(group_ref[0] * part, part)
    lane = pl.multiple_of(lax.div(start, jnp.int32(lanes)) * lanes, lanes)
    wait = fetch(
        [
            (up_hbm.at[:, pl.ds(lane, lanes)], up_ref),
            (down_hbm.at[pl.ds(start, part), :], out_ref.at[1]),
        ],
        sems,
    )
    wait(0)
    turned_ref[...] = up_ref[...].T
    out_ref[0] = turned_ref[pl.ds(pl.multiple_of(start - lane, part), part), :]
    wait(1)


def own_quarter(group, up, down, part):
    width, chunk = up.shape
    lanes = max(128, part)
    return pl.pallas_call(
        quarter_kernel,
        out_shape=jax.ShapeDtypeStruct((2, part, width), BF16),
        in_specs=[SMEM, HBM, HBM],
        out_specs=VMEM,
        scratch_shapes=[
            pltpu.VMEM((width, lanes), BF16),
            pltpu.VMEM((lanes, width), BF16),
            pltpu.SemaphoreType.DMA((2,)),
        ],
        compiler_params=params(56),
        cost_estimate=LONG,
        name="quarter",
    )(group, up, down)


def own_rows_kernel(group_ref, up_ref, down_ref, out_ref, turned_ref):
    part = out_ref.shape[2]
    turned_ref[...] = up_ref[...].T
    for index in range(4):
        quarter = jnp.bitwise_xor(group_ref[0], index)
        span = pl.ds(pl.multiple_of(quarter * part, part), part)
        out_ref[index, 0] = turned_ref[span, :]
        out_ref[index, 1] = down_ref[span, :]


def own_rows(group, up, down):
    width, chunk = up.shape
    return pl.pallas_call(
        own_rows_kernel,
        out_shape=jax.ShapeDtypeStruct((4, 2, chunk // 4, width), BF16),
        in_specs=[SMEM, VMEM, VMEM],
        out_specs=VMEM,
        scratch_shapes=[pltpu.VMEM((chunk, width), BF16)],
        compiler_params=params(16),
        cost_estimate=COST,
        name="own_rows",
    )(group, up, down)


def finish_rows(tokens, mixed, goal, scale):
    out = tokens + scale * mixed
    out_norm = jnp.sqrt(jnp.sum(out * out, axis=-1, keepdims=True) + STABILITY_EPSILON)
    goal_norm = jnp.sqrt(jnp.sum(goal * goal, axis=-1, keepdims=True) + STABILITY_EPSILON)
    norms = out_norm * goal_norm
    cosine = jnp.sum(out * goal, axis=-1, keepdims=True) / norms
    upstream = (cosine / (out_norm * out_norm)) * out - goal * (1.0 / norms)
    return upstream, 1.0 - cosine


def forward_kernel(first, blocks, sides, skipped, *refs):
    last = blocks > 0
    refs = list(refs[skipped:])
    normed_t_ref = refs.pop(0)
    own, other = refs[:sides], refs[sides:2 * sides]
    del refs[:2 * sides]
    mixed_in = None if first else refs.pop(0)
    if last:
        tokens_ref, scale_ref = refs[:2]
        targets, passed_ref = refs[2:2 + blocks], refs[2 + blocks]
        del refs[:3 + blocks]
    act_ref, slope_ref = refs[:2]
    del refs[:2]
    width, rows = normed_t_ref.shape
    part = act_ref.shape[2]
    part_sum = None
    downs = []
    for side, group in enumerate((own, other)):
        start = 0
        for ref in group:
            count = ref.shape[0]
            hiddens = dot_nn(ref[:, 0].reshape(count * part, width), normed_t_ref[...])
            for index in range(count):
                hidden = hiddens[index * part:(index + 1) * part]
                phi = 0.5 * (1.0 + lax.erf(hidden * (0.5 ** 0.5)))
                density = jnp.exp(-0.5 * hidden * hidden) * ((2.0 * jnp.pi) ** -0.5)
                act_ref[side, start + index] = (hidden * phi).astype(BF16)
                slope_ref[side, start + index] = phi + hidden * density
            downs.append(ref[:, 1].reshape(count * part, width))
            start += count
    if sides > 1 or last:
        act = act_ref[...].reshape(2 * start * part, rows)
        part_sum = dot_tn(act, jnp.concatenate(downs, axis=0))
    else:
        for side, down in enumerate(downs):
            term = dot_tn(act_ref[side].reshape(start * part, rows), down)
            part_sum = term if part_sum is None else part_sum + term
    if not last:
        mixed_out = refs[0]
        mixed_out[...] = part_sum if first else mixed_in[...] + part_sum
        return
    back_ref, back_t_ref, small_ref, mixed_ref = refs
    mixed_ref[...] = mixed_in[...] + part_sum
    scale = scale_ref[...]
    small_ref[...] = jnp.zeros_like(small_ref)
    piece = rows // blocks
    for index, target_ref in enumerate(targets):
        span = pl.ds(index * piece, piece)
        mixed = mixed_ref[span, :]
        goal = jnp.concatenate([target_ref[0], passed_ref[index]], axis=0).astype(F32)
        upstream, loss = finish_rows(tokens_ref[span, :].astype(F32), mixed, goal, scale)
        back = (upstream * scale).astype(BF16)
        back_ref[span, :] = back
        back_t_ref[:, span] = back.T
        small_ref[0:1, :] += jnp.sum(upstream * mixed, axis=0, keepdims=True)
        small_ref[1:2, :] += jnp.broadcast_to(jnp.sum(loss, axis=0, keepdims=True), (1, width))


def forward(normed_t, own, other, mixed=None, finish=None, after=()):
    width, rows = normed_t.shape
    part = own[0].shape[2]
    total = sum(array.shape[0] for array in own)
    first, last = mixed is None, finish is not None
    blocks = len(finish) - 3 if last else 0
    operands = [*after, normed_t, *own, *other]
    if not first:
        operands.append(mixed)
    if last:
        operands.extend(finish)
    piece = (2, total, part, rows)
    shapes = [jax.ShapeDtypeStruct(piece, BF16), jax.ShapeDtypeStruct(piece, F32)]
    scratch = []
    if last:
        shapes += [
            jax.ShapeDtypeStruct((rows, width), BF16),
            jax.ShapeDtypeStruct((width, rows), BF16),
            jax.ShapeDtypeStruct((8, width), F32),
        ]
        scratch = [pltpu.VMEM((rows, width), F32)]
    else:
        shapes += [jax.ShapeDtypeStruct((rows, width), F32)]
    return pl.pallas_call(
        functools.partial(forward_kernel, first, blocks, len(own), len(after)),
        out_shape=tuple(shapes),
        in_specs=[ANY] * len(after) + [VMEM] * (len(operands) - len(after)),
        out_specs=tuple([VMEM] * len(shapes)),
        scratch_shapes=scratch,
        compiler_params=params(32),
        cost_estimate=COST,
        name="forward",
    )(*operands)


def pack_kernel(counts, *refs):
    out_ref = refs[-1]
    start = 0
    for count, ref in zip(counts, refs):
        out_ref[start:start + count] = ref[...].reshape(count, *out_ref.shape[1:])
        start += count


def pack(pieces, *after):
    counts = [1 if piece.ndim == 3 else piece.shape[0] for piece in pieces]
    return pl.pallas_call(
        functools.partial(pack_kernel, counts),
        out_shape=jax.ShapeDtypeStruct((sum(counts), *pieces[0].shape[-3:]), BF16),
        in_specs=[VMEM] * len(pieces) + [ANY] * len(after),
        out_specs=VMEM,
        compiler_params=params(16),
        cost_estimate=COST,
        name="pack",
    )(*pieces, *after)


def turn_kernel(y_ref, x_ref, a_ref, b_ref):
    count = a_ref.shape[0]
    a_ref[...] = y_ref[:count]
    b_ref[...] = x_ref[count:]


def turn(y, x):
    count = y.shape[0]
    first = count // 2
    return pl.pallas_call(
        turn_kernel,
        out_shape=(
            jax.ShapeDtypeStruct((first, *y.shape[1:]), BF16),
            jax.ShapeDtypeStruct((count - first, *y.shape[1:]), BF16),
        ),
        in_specs=[VMEM] * 2,
        out_specs=(VMEM, VMEM),
        compiler_params=params(16),
        cost_estimate=COST,
        name="turn",
    )(y, x)


def tie_kernel(*refs):
    pass


def tie(array, *after):
    return pl.pallas_call(
        tie_kernel,
        out_shape=jax.ShapeDtypeStruct(array.shape, array.dtype),
        in_specs=[ANY] * (1 + len(after)),
        out_specs=ANY,
        input_output_aliases={0: 0},
        compiler_params=params(4),
        cost_estimate=COST,
        name="tie",
    )(array, *after)


def seconds_kernel(*refs):
    for index, ref in enumerate(refs[:-1]):
        refs[-1][index] = ref[1]


def seconds(blocks):
    count, (_, each, width) = len(blocks), blocks[0].shape
    return pl.pallas_call(
        seconds_kernel,
        out_shape=jax.ShapeDtypeStruct((count, each, width), BF16),
        in_specs=[VMEM] * count,
        out_specs=VMEM,
        compiler_params=params(16),
        cost_estimate=COST,
        name="seconds",
    )(*blocks)


def joined(refs, pieces, pick):
    values = [pick(refs[which], start, count) for which, start, count in pieces]
    flat = [value.reshape(-1, value.shape[-1]) for value in values]
    return flat[0] if len(flat) == 1 else jnp.concatenate(flat, axis=0)


def put(quarter, value, outs):
    own_ref, x_ref, y_ref, x_later_ref, y_later_ref = outs
    value = value.astype(BF16).reshape(own_ref.shape)
    half = x_ref.shape[0] // 2
    if quarter == 0:
        own_ref[...] = value
    elif quarter == 1:
        x_ref[half:] = value[:half]
        x_later_ref[...] = value[half:]
    elif quarter == 2:
        y_ref[half:] = value[half:]
        y_later_ref[...] = value[:half]
    else:
        x_ref[:half] = value[:half]
        y_ref[:half] = value[half:]


def emit(quarter, value, arrived, outs):
    if arrived is None:
        outs[0][quarter] = value.astype(BF16).reshape(outs[0].shape[1:])
    else:
        put(quarter, value + arrived[quarter].reshape(value.shape).astype(F32), outs)


def down_grad_kernel(side, act_pieces, add, *refs):
    acts, back_ref = refs[:2], refs[2]
    arrived = refs[3] if add else None
    outs = refs[4:] if add else refs[3:]
    for quarter in (3, 1, 2, 0):
        act = joined(acts, act_pieces[quarter], lambda ref, a, n: ref[side, a:a + n])
        emit(quarter, dot_nn(act, back_ref[...]), arrived, outs)


def up_grad_kernel(side, weight_pieces, act_pieces, add, *refs):
    weights, slopes = refs[:2], refs[2:4]
    back_t_ref, normed_ref, gain_in = refs[4:7]
    if add:
        arrived, scale_ref, small_ref = refs[7:10]
        outs, vector_ref, gain_ref = refs[10:-2], refs[-2], refs[-1]
    else:
        arrived = None
        outs, gain_ref = refs[7:-1], refs[-1]
    gain_ref[...] = gain_in[...]
    for quarter in (3, 1, 2, 0):
        pieces = weight_pieces[quarter]
        slope = joined(slopes, act_pieces[quarter], lambda ref, a, n: ref[side, a:a + n])
        back_act = dot_nn(joined(weights, pieces, lambda ref, a, n: ref[a:a + n, 1]), back_t_ref[...])
        back_hidden = (back_act * slope).astype(BF16)
        grad = dot_nn(back_hidden, normed_ref[...])
        up = joined(weights, pieces, lambda ref, a, n: ref[a:a + n, 0]).astype(F32)
        gain_ref[...] += jnp.sum(grad * up, axis=0, keepdims=True)
        emit(quarter, grad, arrived, outs)
    if add:
        vector_ref[0:1, :] = gain_ref[...] / scale_ref[...]
        vector_ref[1:3, :] = small_ref[0:2, :]
        vector_ref[3:8, :] = jnp.zeros((5, gain_ref.shape[1]), F32)


def gradient_shapes(depth, part, width, add):
    if not add:
        return [jax.ShapeDtypeStruct((4, depth, part, width), BF16)]
    counts = (depth, depth, depth, depth - depth // 2, depth // 2)
    return [jax.ShapeDtypeStruct((count, part, width), BF16) for count in counts]


def down_gradient(side, act_pieces, depth, acts, back, arrived=None):
    part = acts[0].shape[2]
    width = back.shape[1]
    add = arrived is not None
    operands = [*acts, back] + ([arrived] if add else [])
    shapes = gradient_shapes(depth, part, width, add)
    return pl.pallas_call(
        functools.partial(down_grad_kernel, side, act_pieces, add),
        out_shape=tuple(shapes),
        in_specs=[VMEM] * len(operands),
        out_specs=tuple([VMEM] * len(shapes)),
        compiler_params=params(20),
        cost_estimate=COST,
        name="down_gradient",
    )(*operands)


def up_gradient(
    side, weight_pieces, act_pieces, depth, weights, slopes, back_t, normed, gain, extra=()
):
    part, width = weights[0].shape[2:]
    add = len(extra) > 0
    operands = [*weights, *slopes, back_t, normed, gain, *extra]
    shapes = gradient_shapes(depth, part, width, add)
    if add:
        shapes.append(jax.ShapeDtypeStruct((8, width), F32))
        scratch = [pltpu.VMEM((1, width), F32)]
    else:
        scratch = []
        shapes.append(jax.ShapeDtypeStruct((1, width), F32))
    return pl.pallas_call(
        functools.partial(up_grad_kernel, side, weight_pieces, act_pieces, add),
        out_shape=tuple(shapes),
        in_specs=[VMEM] * len(operands),
        out_specs=tuple([VMEM] * len(shapes)),
        scratch_shapes=scratch,
        compiler_params=params(24),
        cost_estimate=COST,
        name="up_gradient",
    )(*operands)


def merge_kernel(x_ref, y_ref, x_later_ref, y_later_ref, *refs):
    x_out, y_out = refs[-2:]
    half = y_later_ref.shape[0]
    x_out[...] = (x_later_ref[...].astype(F32) + y_ref[:half].astype(F32)).astype(BF16)
    y_out[...] = (y_later_ref[...].astype(F32) + x_ref[:half].astype(F32)).astype(BF16)


def merge(x, y, x_later, y_later, *after):
    return pl.pallas_call(
        merge_kernel,
        out_shape=tuple(jax.ShapeDtypeStruct(a.shape, BF16) for a in (x_later, y_later)),
        in_specs=[VMEM] * 4 + [ANY] * len(after),
        out_specs=(VMEM, VMEM),
        compiler_params=params(16),
        cost_estimate=COST,
        name="merge",
    )(x, y, x_later, y_later, *after)


def total_kernel(own_ref, x_ref, y_ref, x_late_ref, y_late_ref, *refs):
    outs = refs[-own_ref.shape[0]:]
    half = y_late_ref.shape[0]
    for index, out in enumerate(outs):
        total = own_ref[index].astype(F32)
        if index < half:
            total += x_ref[half + index].astype(F32) + y_late_ref[index].astype(F32)
        else:
            total += y_ref[index].astype(F32) + x_late_ref[index - half].astype(F32)
        out[...] = total.astype(BF16)


def totals(own, x, y, x_late, y_late, *after):
    count, part, width = own.shape
    return pl.pallas_call(
        total_kernel,
        out_shape=tuple([jax.ShapeDtypeStruct((part, width), BF16)] * count),
        in_specs=[VMEM] * 5 + [ANY] * len(after),
        out_specs=tuple([VMEM] * count),
        compiler_params=params(16),
        cost_estimate=COST,
        name="totals",
    )(own, x, y, x_late, y_late, *after)


def collect_kernel(count, *refs):
    total = refs[0][...].astype(F32)
    for ref in refs[1:count]:
        total = total + ref[...].astype(F32)
    refs[-1][...] = total.astype(BF16)


def collect(parts, *after):
    return pl.pallas_call(
        functools.partial(collect_kernel, len(parts)),
        out_shape=jax.ShapeDtypeStruct(parts[0].shape, BF16),
        in_specs=[VMEM] * len(parts) + [ANY] * len(after),
        out_specs=VMEM,
        compiler_params=params(16),
        cost_estimate=COST,
        name="collect",
    )(*parts, *after)


def join_kernel(total_ref, vector_ref, other_ref, *refs):
    short_ref, long_ref, held_ref = refs[-3:]
    part = total_ref.shape[0]
    short_ref[pl.ds(0, part), :] = total_ref[...]
    rest = vector_ref[0:3, :]
    held_ref[...] = jnp.zeros_like(held_ref)
    for index in range(3):
        piece = rest.astype(BF16).astype(F32)
        held_ref[3 * index:3 * index + 3, :] = piece
        rest = rest - piece
    short_ref[pl.ds(part, 16), :] = held_ref[...].astype(BF16)
    long_ref[pl.ds(0, part + 16), :] = short_ref[...]
    long_ref[pl.ds(part + 16, part), :] = other_ref[...]


def join(total, vector, other, *after):
    part, width = total.shape
    return pl.pallas_call(
        join_kernel,
        out_shape=tuple(
            jax.ShapeDtypeStruct((rows, width), BF16) for rows in (part + 16, 2 * part + 16)
        ),
        in_specs=[VMEM] * 3 + [ANY] * len(after),
        out_specs=(VMEM, VMEM),
        scratch_shapes=[pltpu.VMEM((16, width), F32)],
        compiler_params=params(16),
        cost_estimate=COST,
        name="join",
    )(total, vector, other, *after)


def place_kernel(part, tokens, group_ref, *refs):
    ups, downs = refs[:4], refs[4:8]
    up_ref, down_ref, gain_ref, scale_ref, loss_ref, held_ref = refs[8:]
    group = group_ref[0]
    vectors = []
    for index, (up, down) in enumerate(zip(ups, downs)):
        first = pl.multiple_of(jnp.bitwise_xor(group, index) * part, part)
        held_ref[pl.ds(first, part), :] = up[pl.ds(0, part), :]
        start = down.shape[0] - part
        down_ref[pl.ds(first, part), :] = down[pl.ds(start, part), :].astype(F32)
        rows = up[pl.ds(part, 16), :].astype(F32)
        vectors.append((rows[0:3] + rows[3:6]) + rows[6:9])
    up_ref[...] = held_ref[...].T.astype(F32)
    vector = (vectors[0] + vectors[1]) + (vectors[2] + vectors[3])
    gain_ref[...] = vector[0:1]
    scale_ref[...] = vector[1:2]
    loss_ref[...] = vector[2:3, 0:1] * (1.0 / tokens)


def place_quarters(group, ups, downs, part, tokens):
    width = ups[0].shape[1]
    shapes = [
        jax.ShapeDtypeStruct((width, 4 * part), F32),
        jax.ShapeDtypeStruct((4 * part, width), F32),
        jax.ShapeDtypeStruct((1, width), F32),
        jax.ShapeDtypeStruct((1, width), F32),
        jax.ShapeDtypeStruct((1, 1), F32),
    ]
    return pl.pallas_call(
        functools.partial(place_kernel, part, tokens),
        out_shape=tuple(shapes),
        in_specs=[SMEM] + [VMEM] * 8,
        out_specs=tuple([VMEM] * len(shapes)),
        scratch_shapes=[pltpu.VMEM((4 * part, width), BF16)],
        compiler_params=params(16),
        cost_estimate=COST,
        name="place",
    )(group, *ups, *downs)


def shards_square(
    image_tokens,
    tile_lists,
    opacity,
    tile_counts,
    ray_pixel,
    block_owner,
    gaussian_features,
    layer_norm_gain,
    layer_scale,
    up_weight,
    down_weight,
):
    ray_count = lax.axis_size("ray")
    group_count = lax.axis_size("grp")
    depth = ray_count // 2
    group = lax.axis_index("grp").reshape(1)
    me = lax.axis_index("ray").reshape(1)
    rows, width = image_tokens.shape
    part = down_weight.shape[0] // group_count

    def beside(array, flip):
        return lax.ppermute(array, "grp", [(g, g ^ flip) for g in range(group_count)])

    def partner(array, flip=1):
        return lax.ppermute(array, "ray", [(r, r ^ flip) for r in range(ray_count)])

    def along(array, shift):
        pairs = [(r, (r + 2 * shift) % ray_count) for r in range(ray_count)]
        return lax.ppermute(array, "ray", pairs)

    mine = own_quarter(group, up_weight, down_weight, part)
    arrivals = [along(mine, -shift) for shift in range(1, depth)]
    rendered = render(
        ray_count, True, me, block_owner, tile_lists, opacity, tile_counts.reshape(1, rows),
        ray_pixel, gaussian_features,
    )
    half = depth // 2
    low = pack(arrivals[:half - 1], rendered[0])
    x_low, y_low = beside(low, 1), beside(low, 2)
    high = pack(arrivals[half - 1:], low)
    high = tie(high, x_low, y_low)
    x_high, y_high = beside(high, 1), beside(high, 2)
    targets = [rendered[0]] + [along(rendered[shift], shift) for shift in range(1, depth)]
    tokens, normed, normed_t = prepare_tokens(
        ray_count, True, me, block_owner, ray_pixel, image_tokens,
        layer_norm_gain.reshape(1, width),
    )
    most = pack(
        [own_rows(group, up_weight, down_weight), low, x_low, y_low, high, x_high, y_high],
        normed, targets[half],
    )
    most_other = partner(most)
    d_low, d_high = beside(y_low, 1), beside(x_high, 2)
    act_most, slope_most, mixed = forward(normed_t, [most], [most_other])
    late = targets[1:half] + targets[half + 1:]
    last = pack([d_low, d_high], mixed, *late)
    last_other = partner(last)
    act_last, slope_last, back, back_t, small = forward(
        normed_t, [last], [last_other], mixed,
        (tokens, layer_scale.reshape(1, width), *targets, partner(seconds(targets))),
    )
    acts, slopes = (act_most, act_last), (slope_most, slope_last)
    weights = ((most, last), (most_other, last_other))
    count, rest = half - 1, depth - half
    start = 4 + 3 * count
    pieces = tuple(
        ((0, q, 1), (0, 4 + q * count, count), (0, start + q * rest, rest)) for q in range(3)
    ) + (((0, 3, 1), (1, 0, depth - 1)),)
    gain = jnp.zeros((1, width), F32)
    (down_other,) = down_gradient(1, pieces, depth, acts, back)
    down_arrived = partner(down_other)
    up_other, gain = up_gradient(
        1, pieces, pieces, depth, weights[1], slopes, back_t, normed, gain
    )
    up_arrived = partner(up_other)
    down_sums = down_gradient(0, pieces, depth, acts, back, down_arrived)
    *up_sums, vector = up_gradient(
        0, pieces, pieces, depth, weights[0], slopes, back_t, normed, gain,
        (up_arrived, layer_norm_gain.reshape(1, width), small),
    )
    vector = vector + partner(vector)
    flip = 2
    while flip < ray_count:
        vector = vector + partner(vector, flip)
        flip *= 2

    def first_step(to_x, to_y, x_later, y_later, *after):
        from_x, from_y = beside(to_x, 1), beside(to_y, 2)
        return from_x, from_y, merge(from_x, from_y, x_later, y_later, *after)

    def second_step(later):
        return beside(later[0], 1), beside(later[1], 2)

    def arrive_along(shares):
        return [shares[0]] + [along(shares[shift], shift) for shift in range(1, depth)]

    own, *rest = down_sums
    own_up, to_x, to_y, *rest_up = up_sums
    from_x, from_y, later = first_step(*rest, vector)
    late = second_step(later)
    shares = totals(own, from_x, from_y, *late)
    from_x, from_y, later = first_step(to_x, to_y, *rest_up)
    up_shares = totals(own_up, from_x, from_y, *second_step(later))
    down_total = collect(arrive_along(shares), up_shares[0])
    down_x, down_y = beside(down_total, 1), beside(down_total, 2)
    up_total = collect(arrive_along(up_shares))
    short, long = join(up_total, vector, down_total, down_x, down_y)
    up_x, up_y, both = beside(short, 1), beside(short, 2), beside(long, 3)
    grad_up, grad_down, gain, scale, loss = place_quarters(
        group, (short, up_x, up_y, both), (down_total, down_x, down_y, both), part,
        rows * ray_count * group_count,
    )
    return (grad_up, grad_down, gain.reshape(width), scale.reshape(width), loss.reshape(()))


def shards(*operands):
    ray_count, group_count = lax.axis_size("ray"), lax.axis_size("grp")
    hidden = operands[-1].shape[0]
    square = group_count == 4 and ray_count in (8, 16) and hidden % (16 * group_count) == 0
    return (shards_square if square else shards_general)(*operands)


def solution(mesh):
    return jax.shard_map(
        shards,
        mesh=mesh,
        in_specs=(
            P(("grp", "ray"), None),
            P(None, ("grp", "ray")),
            P(None, ("grp", "ray")),
            P(("grp", "ray")),
            P("grp", None),
            P("grp", None),
            P(("grp", "ray"), None),
            P(),
            P(),
            P(None, "ray"),
            P("ray", None),
        ),
        out_specs=(P(None, "ray"), P("ray", None), P(), P(), P()),
        check_vma=False,
    )
```

```python
import functools

import jax
import jax.numpy as jnp
from jax import lax
from jax.experimental import pallas as pl
from jax.experimental.pallas import tpu as pltpu
from jax.sharding import PartitionSpec as P

STABILITY_EPSILON = 1e-06
F32 = jnp.float32
BF16 = jnp.bfloat16
MIB = 1024 * 1024
COST = pl.CostEstimate(flops=1 << 20, bytes_accessed=1 << 16, transcendentals=0)
LONG = pl.CostEstimate(flops=10**10, bytes_accessed=1 << 20, transcendentals=0)
SMEM = pl.BlockSpec(memory_space=pltpu.SMEM)
VMEM = pl.BlockSpec(memory_space=pltpu.VMEM)
ANY = pl.BlockSpec(memory_space=pl.ANY)


def params(mib=48, **more):
    return pltpu.CompilerParams(vmem_limit_bytes=mib * MIB, **more)


def dot_nn(a, b):
    return lax.dot_general(a, b, (((1,), (0,)), ((), ())), preferred_element_type=F32)


def dot_tn(a, b):
    return lax.dot_general(a, b, (((0,), (0,)), ((), ())), preferred_element_type=F32)


def dot_nt(a, b):
    return lax.dot_general(a, b, (((1,), (1,)), ((), ())), preferred_element_type=F32)


def owner_of(pixels, owner_ref, rows, count):
    block = lax.div(pixels, jnp.int32(rows))
    owner = jnp.zeros_like(pixels)
    for slot in range(count):
        owner = jnp.where(block == slot, owner_ref[0:1, slot:slot + 1], owner)
    return owner


def earlier(rows):
    before = lax.broadcasted_iota(jnp.int32, (rows, rows), 0)
    after = lax.broadcasted_iota(jnp.int32, (rows, rows), 1)
    return jnp.where(before < after, 1.0, 0.0).astype(BF16)


HBM = pl.BlockSpec(memory_space=pltpu.HBM)


def fetch(copies, sems):
    started = [
        pltpu.make_async_copy(source, target, sems.at[index])
        for index, (source, target) in enumerate(copies)
    ]
    for copy in started:
        copy.start()

    def wait(*numbers):
        for number in numbers:
            started[number].wait()

    return wait


def render_kernel(
    ray_count, relative, me_ref, owner_hbm, lists_hbm, opacity_hbm, counts_hbm, pixels_hbm,
    features_hbm, *refs,
):
    outs = refs[:-10]
    owner_ref, ids_ref, opacity_ref, counts_ref, mine_ref, features_ref = refs[-10:-4]
    share_ref, table_ref, send_ref, sems = refs[-4:]
    depth, rays = lists_hbm.shape
    gauss = features_hbm.shape[0]
    width = features_hbm.shape[1]
    me = me_ref[0]
    own_pixels = pixels_hbm.at[:, pl.ds(pl.multiple_of(me * rays, rays), rays)]
    wait = fetch(
        [
            (lists_hbm, ids_ref), (opacity_hbm, opacity_ref), (counts_hbm, counts_ref),
            (owner_hbm, owner_ref), (own_pixels, mine_ref), (features_hbm, features_ref),
        ],
        sems,
    )
    wait(0, 1, 2)
    ids_ref[...] = ids_ref[...] - me * gauss
    passing = jnp.ones((1, rays), F32)
    counts = counts_ref[...]
    for level in range(depth):
        alpha = opacity_ref[pl.ds(level, 1), :]
        share_ref[pl.ds(level, 1), :] = jnp.where(level < counts, alpha * passing, 0.0)
        passing = passing * (1.0 - alpha)

    tile = 256
    lanes = 128
    columns = rays // lanes

    @pl.loop(0, (gauss // tile) * columns)
    def _(step):
        first = pl.multiple_of(lax.div(step, columns) * tile, tile)
        lane = pl.multiple_of(lax.rem(step, columns) * lanes, lanes)
        number = (lax.broadcasted_iota(jnp.int32, (tile, lanes), 0) + first).astype(jnp.int16)
        total = jnp.zeros((tile, lanes), BF16)
        for level in range(depth):
            ident = jnp.broadcast_to(ids_ref[pl.ds(level, 1), pl.ds(lane, lanes)], (16, lanes))
            share = jnp.broadcast_to(share_ref[pl.ds(level, 1), pl.ds(lane, lanes)], (16, lanes))
            ident = jnp.concatenate([ident.astype(jnp.int16)] * (tile // 16), axis=0)
            share = jnp.concatenate([share.astype(BF16)] * (tile // 16), axis=0)
            total = total + jnp.where(ident == number, share, jnp.zeros_like(share))
        table_ref[pl.ds(first, tile), pl.ds(lane, lanes)] = total

    wait(3, 4, 5)
    owner = owner_of(mine_ref[...], owner_ref, rays, ray_count)
    padded = -(-ray_count // 16) * 16
    member = (lax.broadcasted_iota(jnp.int32, (padded, rays), 0) == owner)
    ranks = dot_nn(member.astype(F32).astype(BF16), earlier(rays))
    rank = jnp.sum(jnp.where(member, ranks, 0.0), axis=0, keepdims=True).astype(jnp.int32)
    if relative:
        chips = ray_count // 2
        shift = lax.div(owner, jnp.int32(2)) - lax.div(me, jnp.int32(2))
        shift = jnp.where(shift < 0, shift + chips, shift)
        flip = jnp.where(lax.rem(owner, jnp.int32(2)) == lax.rem(me, jnp.int32(2)), 0, 1)
        block = 2 * shift + flip
    else:
        block = owner
    slot = block * (rays // ray_count) + rank
    send_ref[...] = (
        (lax.broadcasted_iota(jnp.int32, (rays, rays), 0) == slot).astype(F32).astype(BF16)
    )

    piece = 256
    span = rays // len(outs)

    @pl.loop(0, width // piece)
    def _(step):
        cols = pl.ds(pl.multiple_of(step * piece, piece), piece)
        rendered = dot_tn(table_ref[...], features_ref[:, cols]).astype(BF16)
        ordered = dot_nn(send_ref[...], rendered).astype(BF16)
        for index, out in enumerate(outs):
            rows = ordered[index * span:(index + 1) * span]
            out[:, :, cols] = rows.reshape(*out.shape[:2], piece)


def render(ray_count, relative, me, owner, lists, opacity, counts, pixels, features):
    depth, rays = lists.shape
    gauss, width = features.shape
    parts = ray_count // 2 if relative else 1
    shape = jax.ShapeDtypeStruct((ray_count // parts, rays // ray_count, width), BF16)
    return pl.pallas_call(
        functools.partial(render_kernel, ray_count, relative),
        out_shape=(shape,) * parts,
        in_specs=[SMEM] + [HBM] * 6,
        out_specs=(VMEM,) * parts,
        scratch_shapes=[
            pltpu.VMEM(owner.shape, jnp.int32),
            pltpu.VMEM((depth, rays), jnp.int32),
            pltpu.VMEM((depth, rays), F32),
            pltpu.VMEM((1, rays), jnp.int32),
            pltpu.VMEM((1, rays), jnp.int32),
            pltpu.VMEM((gauss, width), BF16),
            pltpu.VMEM((depth, rays), F32),
            pltpu.VMEM((gauss, rays), BF16),
            pltpu.VMEM((rays, rays), BF16),
            pltpu.SemaphoreType.DMA((6,)),
        ],
        compiler_params=params(20),
        cost_estimate=COST,
        name="render",
    )(me, owner, lists, opacity, counts, pixels, features)


def tokens_kernel(
    ray_count, relative, me_ref, owner_hbm, pixels_hbm, tokens_hbm, gain_hbm,
    *refs,
):
    tokens_out, normed_out, normed_t_out = refs[-11:-8]
    owner_ref, pixels_ref, tokens_ref, gain_ref, order_ref, rank_ref, place_ref, sems = refs[-8:]
    rows, width = tokens_hbm.shape
    me = me_ref[0]
    each = rows // ray_count
    wait = fetch(
        [
            (owner_hbm, owner_ref), (pixels_hbm, pixels_ref), (gain_hbm, gain_ref),
            (tokens_hbm, tokens_ref),
        ],
        sems,
    )
    wait(0, 1)
    pixels = jnp.concatenate(
        [pixels_ref[:, sender * rows:(sender + 1) * rows] for sender in range(ray_count)], axis=0
    )
    mine = owner_of(pixels, owner_ref, rows, ray_count) == me
    place_ref[...] = lax.rem(pixels, jnp.int32(rows)).astype(F32)
    member = jnp.where(mine, 1.0, 0.0)
    padded = -(-ray_count // 16) * 16
    if padded > ray_count:
        spread = jnp.concatenate([member, jnp.zeros((padded - ray_count, rows), F32)], axis=0)
    else:
        spread = member
    ranks = dot_nn(spread.astype(BF16), earlier(rows))
    rank_ref[...] = jnp.where(mine, ranks[:ray_count], -1.0)
    chips = ray_count // 2
    for index in range(ray_count):
        if relative:
            chip = lax.rem(lax.div(me, jnp.int32(2)) + (chips - index // 2), jnp.int32(chips))
            sender = 2 * chip + jnp.bitwise_xor(lax.rem(me, jnp.int32(2)), index % 2)
        else:
            sender = index
        rank = rank_ref[pl.ds(sender, 1), :].astype(jnp.int32)
        hit = lax.broadcasted_iota(jnp.int32, (each, rows), 0) == rank
        at = jnp.sum(
            jnp.where(hit, place_ref[pl.ds(sender, 1), :], 0.0), axis=1, keepdims=True
        )
        here = lax.broadcasted_iota(jnp.int32, (each, rows), 1) == at.astype(jnp.int32)
        order_ref[pl.ds(index * each, each), :] = here.astype(F32).astype(BF16)
    wait(2, 3)
    half = min(128, rows)
    gain = gain_ref[...]

    @pl.loop(0, rows // half)
    def _(step):
        span = pl.ds(pl.multiple_of(step * half, half), half)
        values = dot_nn(order_ref[span, :], tokens_ref[...])
        tokens_out[span, :] = values.astype(BF16)
        centered = values - jnp.mean(values, axis=-1, keepdims=True)
        variance = jnp.mean(centered * centered, axis=-1, keepdims=True)
        xhat = centered * lax.rsqrt(variance + STABILITY_EPSILON)
        normed = (xhat * gain).astype(BF16)
        normed_out[span, :] = normed
        normed_t_out[:, span] = normed.T


def prepare_tokens(ray_count, relative, me, owner, pixels, tokens, gain, after=()):
    rows, width = tokens.shape
    return pl.pallas_call(
        functools.partial(tokens_kernel, ray_count, relative),
        out_shape=(
            jax.ShapeDtypeStruct((rows, width), BF16),
            jax.ShapeDtypeStruct((rows, width), BF16),
            jax.ShapeDtypeStruct((width, rows), BF16),
        ),
        in_specs=[SMEM] + [HBM] * 4 + [ANY] * len(after),
        out_specs=(VMEM, VMEM, VMEM),
        scratch_shapes=[
            pltpu.VMEM(owner.shape, jnp.int32),
            pltpu.VMEM(pixels.shape, jnp.int32),
            pltpu.VMEM((rows, width), BF16),
            pltpu.VMEM((1, width), F32),
            pltpu.VMEM((rows, rows), BF16),
            pltpu.VMEM((ray_count, rows), F32),
            pltpu.VMEM((ray_count, rows), F32),
            pltpu.SemaphoreType.DMA((4,)),
        ],
        compiler_params=params(20),
        cost_estimate=COST,
        name="tokens",
    )(me, owner, pixels, tokens, gain, *after)


def up_kernel(normed_ref, up_ref, act_ref, slope_ref):
    parts, _, part_rows, width = up_ref.shape
    up = up_ref[...].reshape(parts * part_rows, width)
    rows = normed_ref.shape[0]
    piece = min(128, rows)

    @pl.loop(0, rows // piece)
    def _(step):
        span = pl.ds(pl.multiple_of(step * piece, piece), piece)
        hidden = dot_nn(normed_ref[span, :], up)
        phi = 0.5 * (1.0 + lax.erf(hidden * (0.5 ** 0.5)))
        density = jnp.exp(-0.5 * hidden * hidden) * ((2.0 * jnp.pi) ** -0.5)
        act_ref[span, :] = (hidden * phi).astype(BF16)
        slope_ref[span, :] = (phi + hidden * density).astype(slope_ref.dtype)


def project_up(normed, up):
    rows, width = normed.shape
    parts, chunks, part_rows, chunk = up.shape
    return pl.pallas_call(
        up_kernel,
        grid=(chunks,),
        out_shape=(
            jax.ShapeDtypeStruct((rows, chunks * chunk), BF16),
            jax.ShapeDtypeStruct((rows, chunks * chunk), F32),
        ),
        in_specs=[
            pl.BlockSpec((rows, width), lambda j: (0, 0)),
            pl.BlockSpec((parts, 1, part_rows, chunk), lambda j: (0, j, 0, 0)),
        ],
        out_specs=(
            pl.BlockSpec((rows, chunk), lambda j: (0, j)),
            pl.BlockSpec((rows, chunk), lambda j: (0, j)),
        ),
        compiler_params=params(dimension_semantics=("arbitrary",)),
        cost_estimate=COST,
        name="up",
    )(normed, up)


def down_kernel(
    chunks, act_ref, down_ref, tokens_ref, target_ref, scale_ref,
    grad_ref, back_ref, small_ref, mixed_ref,
):
    step = pl.program_id(0)
    rows, width = tokens_ref.shape
    act = act_ref[...]

    @pl.when(step < chunks)
    def _():
        parts, _, part_rows, _ = down_ref.shape
        part = dot_nn(act, down_ref[...].reshape(parts * part_rows, width))

        @pl.when(step == 0)
        def _():
            mixed_ref[...] = part

        @pl.when(step > 0)
        def _():
            mixed_ref[...] += part

    @pl.when(step == chunks - 1)
    def _():
        scale = scale_ref[...]
        small_ref[...] = jnp.zeros_like(small_ref)
        piece = min(64, rows)

        @pl.loop(0, rows // piece)
        def _(index):
            span = pl.ds(pl.multiple_of(index * piece, piece), piece)
            mixed = mixed_ref[span, :]
            out = tokens_ref[span, :].astype(F32) + scale * mixed
            goal = target_ref[span, :].astype(F32)
            out_norm = jnp.sqrt(jnp.sum(out * out, axis=-1, keepdims=True) + STABILITY_EPSILON)
            goal_norm = jnp.sqrt(jnp.sum(goal * goal, axis=-1, keepdims=True) + STABILITY_EPSILON)
            norms = out_norm * goal_norm
            cosine = jnp.sum(out * goal, axis=-1, keepdims=True) / norms
            upstream = (cosine / (out_norm * out_norm)) * out - goal * (1.0 / norms)
            back_ref[span, :] = (upstream * scale).astype(BF16)
            small_ref[0:1, :] += jnp.sum(upstream * mixed, axis=0, keepdims=True)
            loss = jnp.sum(1.0 - cosine, axis=0, keepdims=True)
            small_ref[1:2, :] += jnp.broadcast_to(loss, (1, width))

    @pl.when(step >= chunks)
    def _():
        grad = dot_tn(act, back_ref[...])
        grad_ref[...] = grad.astype(BF16).reshape(grad_ref.shape)


def project_down(act, down, tokens, target, scale):
    rows, width = tokens.shape
    parts, chunks, part_rows, _ = down.shape
    chunk = parts * part_rows
    return pl.pallas_call(
        functools.partial(down_kernel, chunks),
        grid=(2 * chunks,),
        out_shape=(
            jax.ShapeDtypeStruct(down.shape, BF16),
            jax.ShapeDtypeStruct((rows, width), BF16),
            jax.ShapeDtypeStruct((8, width), F32),
        ),
        in_specs=[
            pl.BlockSpec((rows, chunk), lambda j: (0, lax.rem(j, chunks))),
            pl.BlockSpec(
                (parts, 1, part_rows, width), lambda j: (0, jnp.minimum(j, chunks - 1), 0, 0)
            ),
            pl.BlockSpec((rows, width), lambda j: (0, 0)),
            pl.BlockSpec((rows, width), lambda j: (0, 0)),
            pl.BlockSpec((1, width), lambda j: (0, 0)),
        ],
        out_specs=(
            pl.BlockSpec(
                (parts, 1, part_rows, width), lambda j: (0, jnp.maximum(j - chunks, 0), 0, 0)
            ),
            pl.BlockSpec((rows, width), lambda j: (0, 0)),
            pl.BlockSpec((8, width), lambda j: (0, 0)),
        ),
        scratch_shapes=[pltpu.VMEM((rows, width), F32)],
        compiler_params=params(dimension_semantics=("arbitrary",)),
        cost_estimate=COST,
        name="down",
    )(act, down, tokens, target, scale)


def back_kernel(back_ref, down_ref, slope_ref, normed_t_ref, up_ref, gain_ref, grad_ref, sum_ref):
    step = pl.program_id(0)
    parts, _, part_rows, width = down_ref.shape
    chunk = parts * part_rows
    rows = back_ref.shape[0]
    back_act = dot_nt(back_ref[...], down_ref[...].reshape(chunk, width))
    back_hidden = (back_act * slope_ref[...]).astype(BF16)
    up_parts, _, up_rows, _ = up_ref.shape

    @pl.when(step == 0)
    def _():
        sum_ref[...] = jnp.zeros_like(sum_ref)

    grad = dot_nn(normed_t_ref[...], back_hidden)
    grad_ref[...] = grad.astype(BF16).reshape(grad_ref.shape)
    up = up_ref[...].reshape(up_parts * up_rows, chunk).astype(F32)
    sum_ref[...] += jnp.sum(grad * up, axis=1, keepdims=True) / gain_ref[...]


def back_up(back, down, slope, normed_t, up, gain):
    width, rows = normed_t.shape
    parts, chunks, part_rows, _ = down.shape
    chunk = parts * part_rows
    up_parts, _, up_rows, _ = up.shape
    return pl.pallas_call(
        back_kernel,
        grid=(chunks,),
        out_shape=(
            jax.ShapeDtypeStruct(up.shape, BF16),
            jax.ShapeDtypeStruct((width, 1), F32),
        ),
        in_specs=[
            pl.BlockSpec((rows, width), lambda j: (0, 0)),
            pl.BlockSpec((parts, 1, part_rows, width), lambda j: (0, j, 0, 0)),
            pl.BlockSpec((rows, chunk), lambda j: (0, j)),
            pl.BlockSpec((width, rows), lambda j: (0, 0)),
            pl.BlockSpec((up_parts, 1, up_rows, chunk), lambda j: (0, j, 0, 0)),
            pl.BlockSpec((width, 1), lambda j: (0, 0)),
        ],
        out_specs=(
            pl.BlockSpec((up_parts, 1, up_rows, chunk), lambda j: (0, j, 0, 0)),
            pl.BlockSpec((width, 1), lambda j: (0, 0)),
        ),
        compiler_params=params(dimension_semantics=("arbitrary",)),
        cost_estimate=COST,
        name="back",
    )(back, down, slope, normed_t, up, gain)


def gather_weight(weight, parts, group, group_count, ray_count):
    rows, cols = weight.shape
    if parts == 1:
        whole = lax.all_gather(weight, "ray", axis=0, tiled=True)
    else:
        part = lax.dynamic_slice_in_dim(weight, group * (rows // parts), rows // parts, 0)
        whole = lax.all_gather(part, ("grp", "ray"), axis=0, tiled=True)
    return whole.reshape(parts, ray_count, rows // parts, cols)


def reduce_gradient(grad):
    parts, ray_count, part_rows, cols = grad.shape
    flat = grad.reshape(parts * ray_count * part_rows, cols)
    if parts == 1:
        share = lax.psum_scatter(flat, "ray", scatter_dimension=0, tiled=True)
        return lax.psum(share.astype(F32), "grp")
    share = lax.psum_scatter(flat, "grp", scatter_dimension=0, tiled=True)
    share = lax.psum_scatter(share, "ray", scatter_dimension=0, tiled=True)
    return lax.all_gather(share, "grp", axis=0, tiled=True).astype(F32)


def shards_general(
    image_tokens,
    tile_lists,
    opacity,
    tile_counts,
    ray_pixel,
    block_owner,
    gaussian_features,
    layer_norm_gain,
    layer_scale,
    up_weight,
    down_weight,
):
    ray_count = lax.axis_size("ray")
    group_count = lax.axis_size("grp")
    group = lax.axis_index("grp")
    me = lax.axis_index("ray").reshape(1)
    rows, width = image_tokens.shape
    up_parts = group_count if up_weight.shape[0] % (16 * group_count) == 0 else 1
    down_parts = group_count if down_weight.shape[0] % (16 * group_count) == 0 else 1
    up = gather_weight(up_weight, up_parts, group, group_count, ray_count)
    down = gather_weight(down_weight, down_parts, group, group_count, ray_count)
    rendered = render(
        ray_count, False, me, block_owner, tile_lists, opacity, tile_counts.reshape(1, rows),
        ray_pixel, gaussian_features,
    )
    rendered = rendered[0].reshape(rows, width)
    target = lax.all_to_all(rendered, "ray", split_axis=0, concat_axis=0, tiled=True)
    tokens, normed, normed_t = prepare_tokens(
        ray_count, False, me, block_owner, ray_pixel, image_tokens,
        layer_norm_gain.reshape(1, width),
    )
    act, slope = project_up(normed, up)
    grad_down, back, small = project_down(act, down, tokens, target, layer_scale.reshape(1, width))
    grad_up, gain_sum = back_up(back, down, slope, normed_t, up, layer_norm_gain.reshape(width, 1))
    grad_down = reduce_gradient(grad_down)
    grad_up = reduce_gradient(grad_up)
    sums = jnp.concatenate([gain_sum.reshape(1, width), small[:2]], axis=0)
    sums = lax.psum(sums, ("grp", "ray"))
    loss = sums[2, 0] / (rows * ray_count * group_count)
    return (grad_up, grad_down, sums[0], sums[1], loss)


def quarter_kernel(group_ref, up_hbm, down_hbm, out_ref, up_ref, turned_ref, sems):
    part = out_ref.shape[1]
    lanes = up_ref.shape[1]
    start = pl.multiple_of(group_ref[0] * part, part)
    lane = pl.multiple_of(lax.div(start, jnp.int32(lanes)) * lanes, lanes)
    wait = fetch(
        [
            (up_hbm.at[:, pl.ds(lane, lanes)], up_ref),
            (down_hbm.at[pl.ds(start, part), :], out_ref.at[1]),
        ],
        sems,
    )
    wait(0)
    turned_ref[...] = up_ref[...].T
    out_ref[0] = turned_ref[pl.ds(pl.multiple_of(start - lane, part), part), :]
    wait(1)


def own_quarter(group, up, down, part):
    width, chunk = up.shape
    lanes = max(128, part)
    return pl.pallas_call(
        quarter_kernel,
        out_shape=jax.ShapeDtypeStruct((2, part, width), BF16),
        in_specs=[SMEM, HBM, HBM],
        out_specs=VMEM,
        scratch_shapes=[
            pltpu.VMEM((width, lanes), BF16),
            pltpu.VMEM((lanes, width), BF16),
            pltpu.SemaphoreType.DMA((2,)),
        ],
        compiler_params=params(56),
        cost_estimate=LONG,
        name="quarter",
    )(group, up, down)


def own_rows_kernel(group_ref, up_ref, down_ref, out_ref, turned_ref):
    part = out_ref.shape[2]
    turned_ref[...] = up_ref[...].T
    for index in range(4):
        quarter = jnp.bitwise_xor(group_ref[0], index)
        span = pl.ds(pl.multiple_of(quarter * part, part), part)
        out_ref[index, 0] = turned_ref[span, :]
        out_ref[index, 1] = down_ref[span, :]


def own_rows(group, up, down):
    width, chunk = up.shape
    return pl.pallas_call(
        own_rows_kernel,
        out_shape=jax.ShapeDtypeStruct((4, 2, chunk // 4, width), BF16),
        in_specs=[SMEM, VMEM, VMEM],
        out_specs=VMEM,
        scratch_shapes=[pltpu.VMEM((chunk, width), BF16)],
        compiler_params=params(16),
        cost_estimate=COST,
        name="own_rows",
    )(group, up, down)


def finish_rows(tokens, mixed, goal, scale):
    out = tokens + scale * mixed
    out_norm = jnp.sqrt(jnp.sum(out * out, axis=-1, keepdims=True) + STABILITY_EPSILON)
    goal_norm = jnp.sqrt(jnp.sum(goal * goal, axis=-1, keepdims=True) + STABILITY_EPSILON)
    norms = out_norm * goal_norm
    cosine = jnp.sum(out * goal, axis=-1, keepdims=True) / norms
    upstream = (cosine / (out_norm * out_norm)) * out - goal * (1.0 / norms)
    return upstream, 1.0 - cosine


def forward_kernel(first, blocks, sides, skipped, *refs):
    last = blocks > 0
    refs = list(refs[skipped:])
    normed_t_ref = refs.pop(0)
    own, other = refs[:sides], refs[sides:2 * sides]
    del refs[:2 * sides]
    mixed_in = None if first else refs.pop(0)
    if last:
        tokens_ref, scale_ref = refs[:2]
        targets, passed_ref = refs[2:2 + blocks], refs[2 + blocks]
        del refs[:3 + blocks]
    act_ref, slope_ref = refs[:2]
    del refs[:2]
    width, rows = normed_t_ref.shape
    part = act_ref.shape[2]
    part_sum = None
    downs = []
    for side, group in enumerate((own, other)):
        start = 0
        for ref in group:
            count = ref.shape[0]
            hiddens = dot_nn(ref[:, 0].reshape(count * part, width), normed_t_ref[...])
            for index in range(count):
                hidden = hiddens[index * part:(index + 1) * part]
                phi = 0.5 * (1.0 + lax.erf(hidden * (0.5 ** 0.5)))
                density = jnp.exp(-0.5 * hidden * hidden) * ((2.0 * jnp.pi) ** -0.5)
                act_ref[side, start + index] = (hidden * phi).astype(BF16)
                slope_ref[side, start + index] = phi + hidden * density
            downs.append(ref[:, 1].reshape(count * part, width))
            start += count
    if sides > 1 or last:
        act = act_ref[...].reshape(2 * start * part, rows)
        part_sum = dot_tn(act, jnp.concatenate(downs, axis=0))
    else:
        for side, down in enumerate(downs):
            term = dot_tn(act_ref[side].reshape(start * part, rows), down)
            part_sum = term if part_sum is None else part_sum + term
    if not last:
        mixed_out = refs[0]
        mixed_out[...] = part_sum if first else mixed_in[...] + part_sum
        return
    back_ref, back_t_ref, small_ref, mixed_ref = refs
    mixed_ref[...] = mixed_in[...] + part_sum
    scale = scale_ref[...]
    small_ref[...] = jnp.zeros_like(small_ref)
    piece = rows // blocks
    for index, target_ref in enumerate(targets):
        span = pl.ds(index * piece, piece)
        mixed = mixed_ref[span, :]
        goal = jnp.concatenate([target_ref[0], passed_ref[index]], axis=0).astype(F32)
        upstream, loss = finish_rows(tokens_ref[span, :].astype(F32), mixed, goal, scale)
        back = (upstream * scale).astype(BF16)
        back_ref[span, :] = back
        back_t_ref[:, span] = back.T
        small_ref[0:1, :] += jnp.sum(upstream * mixed, axis=0, keepdims=True)
        small_ref[1:2, :] += jnp.broadcast_to(jnp.sum(loss, axis=0, keepdims=True), (1, width))


def forward(normed_t, own, other, mixed=None, finish=None, after=()):
    width, rows = normed_t.shape
    part = own[0].shape[2]
    total = sum(array.shape[0] for array in own)
    first, last = mixed is None, finish is not None
    blocks = len(finish) - 3 if last else 0
    operands = [*after, normed_t, *own, *other]
    if not first:
        operands.append(mixed)
    if last:
        operands.extend(finish)
    piece = (2, total, part, rows)
    shapes = [jax.ShapeDtypeStruct(piece, BF16), jax.ShapeDtypeStruct(piece, F32)]
    scratch = []
    if last:
        shapes += [
            jax.ShapeDtypeStruct((rows, width), BF16),
            jax.ShapeDtypeStruct((width, rows), BF16),
            jax.ShapeDtypeStruct((8, width), F32),
        ]
        scratch = [pltpu.VMEM((rows, width), F32)]
    else:
        shapes += [jax.ShapeDtypeStruct((rows, width), F32)]
    return pl.pallas_call(
        functools.partial(forward_kernel, first, blocks, len(own), len(after)),
        out_shape=tuple(shapes),
        in_specs=[ANY] * len(after) + [VMEM] * (len(operands) - len(after)),
        out_specs=tuple([VMEM] * len(shapes)),
        scratch_shapes=scratch,
        compiler_params=params(32),
        cost_estimate=COST,
        name="forward",
    )(*operands)


def pack_kernel(counts, *refs):
    out_ref = refs[-1]
    start = 0
    for count, ref in zip(counts, refs):
        out_ref[start:start + count] = ref[...].reshape(count, *out_ref.shape[1:])
        start += count


def pack(pieces, *after):
    counts = [1 if piece.ndim == 3 else piece.shape[0] for piece in pieces]
    return pl.pallas_call(
        functools.partial(pack_kernel, counts),
        out_shape=jax.ShapeDtypeStruct((sum(counts), *pieces[0].shape[-3:]), BF16),
        in_specs=[VMEM] * len(pieces) + [ANY] * len(after),
        out_specs=VMEM,
        compiler_params=params(16),
        cost_estimate=COST,
        name="pack",
    )(*pieces, *after)


def turn_kernel(y_ref, x_ref, a_ref, b_ref):
    count = a_ref.shape[0]
    a_ref[...] = y_ref[:count]
    b_ref[...] = x_ref[count:]


def turn(y, x):
    count = y.shape[0]
    first = count // 2
    return pl.pallas_call(
        turn_kernel,
        out_shape=(
            jax.ShapeDtypeStruct((first, *y.shape[1:]), BF16),
            jax.ShapeDtypeStruct((count - first, *y.shape[1:]), BF16),
        ),
        in_specs=[VMEM] * 2,
        out_specs=(VMEM, VMEM),
        compiler_params=params(16),
        cost_estimate=COST,
        name="turn",
    )(y, x)


def tie_kernel(*refs):
    pass


def tie(array, *after):
    return pl.pallas_call(
        tie_kernel,
        out_shape=jax.ShapeDtypeStruct(array.shape, array.dtype),
        in_specs=[ANY] * (1 + len(after)),
        out_specs=ANY,
        input_output_aliases={0: 0},
        compiler_params=params(4),
        cost_estimate=COST,
        name="tie",
    )(array, *after)


def seconds_kernel(*refs):
    for index, ref in enumerate(refs[:-1]):
        refs[-1][index] = ref[1]


def seconds(blocks):
    count, (_, each, width) = len(blocks), blocks[0].shape
    return pl.pallas_call(
        seconds_kernel,
        out_shape=jax.ShapeDtypeStruct((count, each, width), BF16),
        in_specs=[VMEM] * count,
        out_specs=VMEM,
        compiler_params=params(16),
        cost_estimate=COST,
        name="seconds",
    )(*blocks)


def joined(refs, pieces, pick):
    values = [pick(refs[which], start, count) for which, start, count in pieces]
    flat = [value.reshape(-1, value.shape[-1]) for value in values]
    return flat[0] if len(flat) == 1 else jnp.concatenate(flat, axis=0)


def put(quarter, value, outs):
    own_ref, x_ref, y_ref, x_later_ref, y_later_ref = outs
    value = value.astype(BF16).reshape(own_ref.shape)
    half = x_ref.shape[0] // 2
    if quarter == 0:
        own_ref[...] = value
    elif quarter == 1:
        x_ref[half:] = value[:half]
        x_later_ref[...] = value[half:]
    elif quarter == 2:
        y_ref[half:] = value[half:]
        y_later_ref[...] = value[:half]
    else:
        x_ref[:half] = value[:half]
        y_ref[:half] = value[half:]


def emit(quarter, value, arrived, outs):
    if arrived is None:
        outs[0][quarter] = value.astype(BF16).reshape(outs[0].shape[1:])
    else:
        put(quarter, value + arrived[quarter].reshape(value.shape).astype(F32), outs)


def down_grad_kernel(side, act_pieces, add, *refs):
    acts, back_ref = refs[:2], refs[2]
    arrived = refs[3] if add else None
    outs = refs[4:] if add else refs[3:]
    for quarter in (3, 1, 2, 0):
        act = joined(acts, act_pieces[quarter], lambda ref, a, n: ref[side, a:a + n])
        emit(quarter, dot_nn(act, back_ref[...]), arrived, outs)


def up_grad_kernel(side, weight_pieces, act_pieces, add, *refs):
    weights, slopes = refs[:2], refs[2:4]
    back_t_ref, normed_ref, gain_in = refs[4:7]
    if add:
        arrived, scale_ref, small_ref = refs[7:10]
        outs, vector_ref, gain_ref = refs[10:-2], refs[-2], refs[-1]
    else:
        arrived = None
        outs, gain_ref = refs[7:-1], refs[-1]
    gain_ref[...] = gain_in[...]
    for quarter in (3, 1, 2, 0):
        pieces = weight_pieces[quarter]
        slope = joined(slopes, act_pieces[quarter], lambda ref, a, n: ref[side, a:a + n])
        back_act = dot_nn(joined(weights, pieces, lambda ref, a, n: ref[a:a + n, 1]), back_t_ref[...])
        back_hidden = (back_act * slope).astype(BF16)
        grad = dot_nn(back_hidden, normed_ref[...])
        up = joined(weights, pieces, lambda ref, a, n: ref[a:a + n, 0]).astype(F32)
        gain_ref[...] += jnp.sum(grad * up, axis=0, keepdims=True)
        emit(quarter, grad, arrived, outs)
    if add:
        vector_ref[0:1, :] = gain_ref[...] / scale_ref[...]
        vector_ref[1:3, :] = small_ref[0:2, :]
        vector_ref[3:8, :] = jnp.zeros((5, gain_ref.shape[1]), F32)


def gradient_shapes(depth, part, width, add):
    if not add:
        return [jax.ShapeDtypeStruct((4, depth, part, width), BF16)]
    counts = (depth, depth, depth, depth - depth // 2, depth // 2)
    return [jax.ShapeDtypeStruct((count, part, width), BF16) for count in counts]


def down_gradient(side, act_pieces, depth, acts, back, arrived=None):
    part = acts[0].shape[2]
    width = back.shape[1]
    add = arrived is not None
    operands = [*acts, back] + ([arrived] if add else [])
    shapes = gradient_shapes(depth, part, width, add)
    return pl.pallas_call(
        functools.partial(down_grad_kernel, side, act_pieces, add),
        out_shape=tuple(shapes),
        in_specs=[VMEM] * len(operands),
        out_specs=tuple([VMEM] * len(shapes)),
        compiler_params=params(20),
        cost_estimate=COST,
        name="down_gradient",
    )(*operands)


def up_gradient(
    side, weight_pieces, act_pieces, depth, weights, slopes, back_t, normed, gain, extra=()
):
    part, width = weights[0].shape[2:]
    add = len(extra) > 0
    operands = [*weights, *slopes, back_t, normed, gain, *extra]
    shapes = gradient_shapes(depth, part, width, add)
    if add:
        shapes.append(jax.ShapeDtypeStruct((8, width), F32))
        scratch = [pltpu.VMEM((1, width), F32)]
    else:
        scratch = []
        shapes.append(jax.ShapeDtypeStruct((1, width), F32))
    return pl.pallas_call(
        functools.partial(up_grad_kernel, side, weight_pieces, act_pieces, add),
        out_shape=tuple(shapes),
        in_specs=[VMEM] * len(operands),
        out_specs=tuple([VMEM] * len(shapes)),
        scratch_shapes=scratch,
        compiler_params=params(24),
        cost_estimate=COST,
        name="up_gradient",
    )(*operands)


def merge_kernel(x_ref, y_ref, x_later_ref, y_later_ref, *refs):
    x_out, y_out = refs[-2:]
    half = y_later_ref.shape[0]
    x_out[...] = (x_later_ref[...].astype(F32) + y_ref[:half].astype(F32)).astype(BF16)
    y_out[...] = (y_later_ref[...].astype(F32) + x_ref[:half].astype(F32)).astype(BF16)


def merge(x, y, x_later, y_later, *after):
    return pl.pallas_call(
        merge_kernel,
        out_shape=tuple(jax.ShapeDtypeStruct(a.shape, BF16) for a in (x_later, y_later)),
        in_specs=[VMEM] * 4 + [ANY] * len(after),
        out_specs=(VMEM, VMEM),
        compiler_params=params(16),
        cost_estimate=COST,
        name="merge",
    )(x, y, x_later, y_later, *after)


def total_kernel(own_ref, x_ref, y_ref, x_late_ref, y_late_ref, *refs):
    outs = refs[-own_ref.shape[0]:]
    half = y_late_ref.shape[0]
    for index, out in enumerate(outs):
        total = own_ref[index].astype(F32)
        if index < half:
            total += x_ref[half + index].astype(F32) + y_late_ref[index].astype(F32)
        else:
            total += y_ref[index].astype(F32) + x_late_ref[index - half].astype(F32)
        out[...] = total.astype(BF16)


def totals(own, x, y, x_late, y_late, *after):
    count, part, width = own.shape
    return pl.pallas_call(
        total_kernel,
        out_shape=tuple([jax.ShapeDtypeStruct((part, width), BF16)] * count),
        in_specs=[VMEM] * 5 + [ANY] * len(after),
        out_specs=tuple([VMEM] * count),
        compiler_params=params(16),
        cost_estimate=COST,
        name="totals",
    )(own, x, y, x_late, y_late, *after)


def collect_kernel(count, *refs):
    total = refs[0][...].astype(F32)
    for ref in refs[1:count]:
        total = total + ref[...].astype(F32)
    refs[-1][...] = total.astype(BF16)


def collect(parts, *after):
    return pl.pallas_call(
        functools.partial(collect_kernel, len(parts)),
        out_shape=jax.ShapeDtypeStruct(parts[0].shape, BF16),
        in_specs=[VMEM] * len(parts) + [ANY] * len(after),
        out_specs=VMEM,
        compiler_params=params(16),
        cost_estimate=COST,
        name="collect",
    )(*parts, *after)


def join_kernel(total_ref, vector_ref, other_ref, *refs):
    short_ref, long_ref, held_ref = refs[-3:]
    part = total_ref.shape[0]
    short_ref[pl.ds(0, part), :] = total_ref[...]
    rest = vector_ref[0:3, :]
    held_ref[...] = jnp.zeros_like(held_ref)
    for index in range(3):
        piece = rest.astype(BF16).astype(F32)
        held_ref[3 * index:3 * index + 3, :] = piece
        rest = rest - piece
    short_ref[pl.ds(part, 16), :] = held_ref[...].astype(BF16)
    long_ref[pl.ds(0, part + 16), :] = short_ref[...]
    long_ref[pl.ds(part + 16, part), :] = other_ref[...]


def join(total, vector, other, *after):
    part, width = total.shape
    return pl.pallas_call(
        join_kernel,
        out_shape=tuple(
            jax.ShapeDtypeStruct((rows, width), BF16) for rows in (part + 16, 2 * part + 16)
        ),
        in_specs=[VMEM] * 3 + [ANY] * len(after),
        out_specs=(VMEM, VMEM),
        scratch_shapes=[pltpu.VMEM((16, width), F32)],
        compiler_params=params(16),
        cost_estimate=COST,
        name="join",
    )(total, vector, other, *after)


def place_kernel(part, tokens, group_ref, *refs):
    ups, downs = refs[:4], refs[4:8]
    up_ref, down_ref, gain_ref, scale_ref, loss_ref, held_ref = refs[8:]
    group = group_ref[0]
    vectors = []
    for index, (up, down) in enumerate(zip(ups, downs)):
        first = pl.multiple_of(jnp.bitwise_xor(group, index) * part, part)
        held_ref[pl.ds(first, part), :] = up[pl.ds(0, part), :]
        start = down.shape[0] - part
        down_ref[pl.ds(first, part), :] = down[pl.ds(start, part), :].astype(F32)
        rows = up[pl.ds(part, 16), :].astype(F32)
        vectors.append((rows[0:3] + rows[3:6]) + rows[6:9])
    up_ref[...] = held_ref[...].T.astype(F32)
    vector = (vectors[0] + vectors[1]) + (vectors[2] + vectors[3])
    gain_ref[...] = vector[0:1]
    scale_ref[...] = vector[1:2]
    loss_ref[...] = vector[2:3, 0:1] * (1.0 / tokens)


def place_quarters(group, ups, downs, part, tokens):
    width = ups[0].shape[1]
    shapes = [
        jax.ShapeDtypeStruct((width, 4 * part), F32),
        jax.ShapeDtypeStruct((4 * part, width), F32),
        jax.ShapeDtypeStruct((1, width), F32),
        jax.ShapeDtypeStruct((1, width), F32),
        jax.ShapeDtypeStruct((1, 1), F32),
    ]
    return pl.pallas_call(
        functools.partial(place_kernel, part, tokens),
        out_shape=tuple(shapes),
        in_specs=[SMEM] + [VMEM] * 8,
        out_specs=tuple([VMEM] * len(shapes)),
        scratch_shapes=[pltpu.VMEM((4 * part, width), BF16)],
        compiler_params=params(16),
        cost_estimate=COST,
        name="place",
    )(group, *ups, *downs)


def shards_square(
    image_tokens,
    tile_lists,
    opacity,
    tile_counts,
    ray_pixel,
    block_owner,
    gaussian_features,
    layer_norm_gain,
    layer_scale,
    up_weight,
    down_weight,
):
    ray_count = lax.axis_size("ray")
    group_count = lax.axis_size("grp")
    depth = ray_count // 2
    group = lax.axis_index("grp").reshape(1)
    me = lax.axis_index("ray").reshape(1)
    rows, width = image_tokens.shape
    part = down_weight.shape[0] // group_count

    def beside(array, flip):
        return lax.ppermute(array, "grp", [(g, g ^ flip) for g in range(group_count)])

    def partner(array, flip=1):
        return lax.ppermute(array, "ray", [(r, r ^ flip) for r in range(ray_count)])

    def along(array, shift):
        pairs = [(r, (r + 2 * shift) % ray_count) for r in range(ray_count)]
        return lax.ppermute(array, "ray", pairs)

    mine = own_quarter(group, up_weight, down_weight, part)
    arrivals = [along(mine, -shift) for shift in range(1, depth)]
    rendered = render(
        ray_count, True, me, block_owner, tile_lists, opacity, tile_counts.reshape(1, rows),
        ray_pixel, gaussian_features,
    )
    half = depth // 2
    low = pack(arrivals[:half - 1], rendered[0])
    x_low, y_low = beside(low, 1), beside(low, 2)
    high = pack(arrivals[half - 1:], low)
    high = tie(high, x_low, y_low)
    x_high, y_high = beside(high, 1), beside(high, 2)
    targets = [rendered[0]] + [along(rendered[shift], shift) for shift in range(1, depth)]
    tokens, normed, normed_t = prepare_tokens(
        ray_count, True, me, block_owner, ray_pixel, image_tokens,
        layer_norm_gain.reshape(1, width),
    )
    most = pack(
        [own_rows(group, up_weight, down_weight), low, x_low, y_low, high, x_high, y_high],
        normed, targets[1], *targets[half + 1:],
    )
    most_other = partner(most)
    d_low, d_high = beside(y_low, 1), beside(x_high, 2)
    act_most, slope_most, mixed = forward(normed_t, [most], [most_other])
    late = targets[2:half + 1]
    last = pack([d_low, d_high], mixed, *late)
    last_other = partner(last)
    act_last, slope_last, back, back_t, small = forward(
        normed_t, [last], [last_other], mixed,
        (tokens, layer_scale.reshape(1, width), *targets, partner(seconds(targets))),
    )
    acts, slopes = (act_most, act_last), (slope_most, slope_last)
    weights = ((most, last), (most_other, last_other))
    count, rest = half - 1, depth - half
    start = 4 + 3 * count
    pieces = tuple(
        ((0, q, 1), (0, 4 + q * count, count), (0, start + q * rest, rest)) for q in range(3)
    ) + (((0, 3, 1), (1, 0, depth - 1)),)
    gain = jnp.zeros((1, width), F32)
    (down_other,) = down_gradient(1, pieces, depth, acts, back)
    down_arrived = partner(down_other)
    up_other, gain = up_gradient(
        1, pieces, pieces, depth, weights[1], slopes, back_t, normed, gain
    )
    up_arrived = partner(up_other)
    down_sums = down_gradient(0, pieces, depth, acts, back, down_arrived)
    *up_sums, vector = up_gradient(
        0, pieces, pieces, depth, weights[0], slopes, back_t, normed, gain,
        (up_arrived, layer_norm_gain.reshape(1, width), small),
    )
    vector = vector + partner(vector)
    flip = 2
    while flip < ray_count:
        vector = vector + partner(vector, flip)
        flip *= 2

    def first_step(to_x, to_y, x_later, y_later, *after):
        from_x, from_y = beside(to_x, 1), beside(to_y, 2)
        return from_x, from_y, merge(from_x, from_y, x_later, y_later, *after)

    def second_step(later):
        return beside(later[0], 1), beside(later[1], 2)

    def arrive_along(shares):
        return [shares[0]] + [along(shares[shift], shift) for shift in range(1, depth)]

    own, *rest = down_sums
    own_up, to_x, to_y, *rest_up = up_sums
    from_x, from_y, later = first_step(*rest, vector)
    late = second_step(later)
    shares = totals(own, from_x, from_y, *late)
    from_x, from_y, later = first_step(to_x, to_y, *rest_up)
    up_shares = totals(own_up, from_x, from_y, *second_step(later))
    down_total = collect(arrive_along(shares), up_shares[0])
    down_x, down_y = beside(down_total, 1), beside(down_total, 2)
    up_total = collect(arrive_along(up_shares))
    short, long = join(up_total, vector, down_total, down_x, down_y)
    up_x, up_y, both = beside(short, 1), beside(short, 2), beside(long, 3)
    grad_up, grad_down, gain, scale, loss = place_quarters(
        group, (short, up_x, up_y, both), (down_total, down_x, down_y, both), part,
        rows * ray_count * group_count,
    )
    return (grad_up, grad_down, gain.reshape(width), scale.reshape(width), loss.reshape(()))


def shards(*operands):
    ray_count, group_count = lax.axis_size("ray"), lax.axis_size("grp")
    hidden = operands[-1].shape[0]
    square = group_count == 4 and ray_count in (8, 16) and hidden % (16 * group_count) == 0
    return (shards_square if square else shards_general)(*operands)


def solution(mesh):
    return jax.shard_map(
        shards,
        mesh=mesh,
        in_specs=(
            P(("grp", "ray"), None),
            P(None, ("grp", "ray")),
            P(None, ("grp", "ray")),
            P(("grp", "ray")),
            P("grp", None),
            P("grp", None),
            P(("grp", "ray"), None),
            P(),
            P(),
            P(None, "ray"),
            P("ray", None),
        ),
        out_specs=(P(None, "ray"), P("ray", None), P(), P(), P()),
        check_vma=False,
    )
```
